32 devices in a mesh: groups: 2 (over y), blk: 4 (over z), chan: 2 (over x), sub: 2 (over core).
Axes of the slice: x: 2, y: 2, z: 4, core: 2. Of those that a mesh axis runs over, the one named last changes fastest.
Arguments:
- pair: bfloat16 [64, 64, 64, 128], P(('groups', 'blk'), 'chan', 'sub'), parts along dimension 0, may hold values from -6 to 6
- block_list: int32 [64, 2], P('groups'), parts along dimension 0, may hold values from 0 to 63
- term_owner: int32 [64, 2], P('groups'), parts along dimension 0, may hold values from 0 to 3, all different within a row; in each aligned block of 8 rows (0 to 7, 8 to 15, ...) at most 4 rows name the same one
- term_slots: int32 [64, 2, 2], P('groups'), parts along dimension 0, may hold values from 0 to 7
- chain_ids: int32 [8192], P('groups'), parts along dimension 0, may hold values from -1 to 1, as said below
- w_in: bfloat16 [2, 128, 640], replicated, may hold values from -0.5 to 0.5
- w_out: bfloat16 [2, 128, 128], replicated, may hold values from -0.5 to 0.5
Outputs:
- updated_pair: bfloat16 [64, 64, 64, 128], P(('groups', 'blk'), 'chan', 'sub'), parts along dimension 0
The draws below stay inside these ranges and needn't reach their ends.
There are 2 independent parts, one for each index of `groups`. The reference program is written for one: setup_inputs(seed, part) draws one part's arguments, and reference() takes and returns one part's arrays. A program takes and returns all parts, laid end to end along the dimension named above; an argument that names none is the same for every part. Nothing has to cross between parts.
Inputs may be any that keep to these rules, and one draw needn't show every extreme that they name: term_owner[s, t] is the blk index of the device that holds both operands of term t of kept block s; the 2 values of a block differ; within the rows of one device (aligned runs of 8 kept blocks) no value stands more than 4 times, and some value stands exactly 4 times. term_slots[s, t, r] is the slot, among the 8 blocks that device holds, of the left (r = 0) or right (r = 1) operand. `block_list`: block coordinates in units of 64 residues. `chain_ids`: padding (-1) fills the last eighth to quarter of the residues; before it, chain 0 is followed by chain 1.
All inputs are finite; a program needn't handle non-finite values.
Results may differ from the reference program's by a relative error of at most 0.009.
Values may be sent and summed in bfloat16 or wider, within the bound.
No kernel may reach another device: no remote copies, remote signals or barrier semaphores. Data moves between devices by JAX's collectives and lax.ppermute only.
A program may use at most 128 MiB of HBM per device.

```python
import math
import jax
import jax.numpy as jnp
import numpy as np
from jax import lax

CHANNELS = 128
HIDDEN_SIZE = 128
BLOCK = 64
TERMS = 2
SLOT_DEV = 8
RESIDUES = 4096
NBLOCKS = 64
KEPT = 32
CAP = 4
N_BLK = 4


def draw_chain_ids(key, part):
    key = jax.random.fold_in(key, 17)
    pad_key, split_key = jax.random.split(key)
    padding = jax.random.randint(pad_key, (), RESIDUES // 8, RESIDUES // 4 + 1)
    live_count = RESIDUES - padding
    boundary = jax.random.randint(split_key, (), live_count // 4, 3 * live_count // 4 + 1)
    positions = jnp.arange(RESIDUES, dtype=jnp.int32)
    chains = jnp.where(positions < boundary, 0, 1)
    return jnp.where(positions >= live_count, -1, chains).astype(jnp.int32)


def set_ends(values, key, low, high):
    extent = values.shape
    place = [jax.random.randint(jax.random.fold_in(key, axis), (), 0, extent[axis]) for axis in range(len(extent))]
    values = values.at[tuple(place)].set(low)
    longest = extent.index(max(extent))
    place[longest] = (place[longest] + 1) % extent[longest]
    return values.at[tuple(place)].set(high)


def steps_of(stream_key, shape, shards, least, high):
    gain = 1.0
    for axis_at, shards_of in shards:
        steps = jax.random.uniform(jax.random.fold_in(jax.random.fold_in(stream_key, 6), axis_at), (shards_of,), jnp.float32, least / len(shards), high / len(shards))
        gain = gain * jnp.repeat(jnp.exp(steps), shape[axis_at] // shards_of).reshape((-1,) + (1,) * (len(shape) - 1 - axis_at))
    return gain


def deal_out(key, own, number, rows, number_of, top, bound, skew):
    order = jax.random.permutation(key, number_of)
    crowded, common = shares(number_of, rows * top, bound, skew, True), shares(number_of, rows * top, bound, skew, False)
    places = jnp.arange(number_of)

    def named(lengths, rotation):
        used = int((lengths > 0).sum())
        fixed = max(1, used // 4)
        moved = fixed + (places - fixed + rotation * (used - fixed)) % max(1, number_of - fixed)
        return jnp.zeros((number_of,), jnp.int32).at[order[jnp.where(places < fixed, places, moved)]].set(jnp.asarray(lengths, jnp.int32))

    lengths = jnp.where(number % 4 == 0, named(crowded, number // 4), named(common, number - number // 4 - 1))
    mixed = jax.random.permutation(jax.random.fold_in(own, 3), number_of)
    donor, sink = mixed[0:number_of // 2 * 2:2], mixed[1:number_of // 2 * 2:2]
    room = jnp.minimum(lengths[donor] - 1, bound - lengths[sink]) // 2
    room = jnp.where((donor == order[0]) | (sink == order[0]) | (lengths[sink] == 0), 0, jnp.maximum(room, 0))
    moved = jax.random.randint(jax.random.fold_in(own, 4), (number_of // 2,), 0, 1 << 20) % (room + 1)
    lengths = lengths.at[donor].add(-moved).at[sink].add(moved)
    items = jnp.searchsorted(jnp.cumsum(lengths), jnp.arange(rows * top), side="right").astype(jnp.int32)
    grid = items.reshape(top, rows).T
    grid = grid[jax.random.permutation(jax.random.fold_in(own, 1), rows)]
    rotation = jax.random.randint(jax.random.fold_in(own, 2), (rows, 1), 0, top)
    return jnp.take_along_axis(grid, (jnp.arange(top)[None, :] + rotation) % top, axis=1)


def shares(amount, total, limit, lean, full):
    weights = [(1 << 20) // math.isqrt(rank ** lean) + 1 for rank in range(1, amount + 1)]
    largest = limit if full else min(limit, max(-(-total // amount), total * weights[0] // sum(weights)))
    least = 1 if total - largest >= amount - 1 else 0
    given, rest = [largest] + [least] * (amount - 1), total - largest - least * (amount - 1)
    while rest > 0:
        free = [i for i in range(1, amount) if given[i] < largest] or [i for i in range(1, amount) if given[i] < limit]
        pool, budget = sum([weights[i] for i in free]), rest
        for i in free:
            more = min(limit - given[i], max(1, budget * weights[i] // pool), rest)
            given[i] = given[i] + more
            rest = rest - more
    return np.array(given)


def normal_values(stream_key, extent, scale, bound, cuts=(), held_as=jnp.bfloat16):
    drawn = scale * jax.random.normal(stream_key, extent, jnp.float32)
    if cuts:
        drawn = drawn * steps_of(stream_key, extent, cuts, -0.22, 0.18)
    return jnp.clip(drawn, -bound, bound).astype(held_as)


def setup_inputs(seed: int = 0, part: int = 0) -> dict:
    key_of = jax.random.split(jax.random.key(seed), 8)
    part_splits = jax.random.split(jax.random.fold_in(key_of[7], part), 8)
    pair = normal_values(part_splits[0], (KEPT, BLOCK, BLOCK, CHANNELS), 1.0, 6.0, ((0, 4), (1, 2), (2, 2)))
    block_list = set_ends(jax.random.randint(part_splits[1], (KEPT, 2), 0, NBLOCKS), jax.random.fold_in(part_splits[1], 1), 0, NBLOCKS - 1).astype(jnp.int32)
    term_owner_keys = jax.random.split(jax.random.fold_in(part_splits[2], 1), KEPT // SLOT_DEV)
    term_owner_turns = jax.random.permutation(jax.random.fold_in(part_splits[2], 3), KEPT // SLOT_DEV)
    term_owner = jax.vmap(lambda own, number: deal_out(jax.random.fold_in(part_splits[2], 2), own, number, SLOT_DEV, N_BLK, TERMS, CAP, 2))(term_owner_keys, term_owner_turns).reshape((KEPT, TERMS))
    term_slots = set_ends(jax.random.randint(part_splits[3], (KEPT, TERMS, 2), 0, SLOT_DEV), jax.random.fold_in(part_splits[3], 1), 0, SLOT_DEV - 1).astype(jnp.int32)
    chain_ids = draw_chain_ids(jax.random.fold_in(jax.random.fold_in(key_of[7], part), 71), part)
    w_in = normal_values(key_of[5], (2, CHANNELS, 4 * HIDDEN_SIZE + CHANNELS), CHANNELS ** -0.5, 0.5)
    w_out = normal_values(key_of[6], (2, HIDDEN_SIZE, CHANNELS), HIDDEN_SIZE ** -0.5, 0.5)
    return dict(pair=pair, block_list=block_list, term_owner=term_owner, term_slots=term_slots, chain_ids=chain_ids, w_in=w_in, w_out=w_out)


norm_epsilon = 1e-05

def layer_norm(values, channel_axis):
    values = values.astype(jnp.float32)
    average = lax.optimization_barrier(jnp.mean(values, axis=channel_axis, keepdims=True))
    centred = values - average
    variance = lax.optimization_barrier(jnp.mean(centred * centred, axis=channel_axis, keepdims=True))
    return centred * lax.rsqrt(variance + norm_epsilon)

def round_trip(values):
    return lax.optimization_barrier(values.astype(jnp.bfloat16)).astype(jnp.float32)

def slot_mask(coords, chain_ids):
    offsets = jnp.arange(BLOCK, dtype=jnp.int32)
    row_alive = (chain_ids[coords[0] * BLOCK + offsets] >= 0).astype(jnp.float32)
    col_alive = (chain_ids[coords[1] * BLOCK + offsets] >= 0).astype(jnp.float32)
    return row_alive[:, None] * col_alive[None, :]

def project_all(current, block_list, chain_ids, weights):

    def one_slot(inputs):
        block_rows, coords = inputs
        pair_mask = slot_mask(coords, chain_ids)[:, :, None]
        normed = layer_norm(block_rows, 2).astype(jnp.bfloat16).reshape(BLOCK * BLOCK, CHANNELS)
        projected = jnp.dot(normed, weights[:, :4 * HIDDEN_SIZE], preferred_element_type=jnp.float32)
        projected = projected.reshape(BLOCK, BLOCK, 4 * HIDDEN_SIZE)
        gate_logit = jnp.dot(normed, weights[:, 4 * HIDDEN_SIZE:], preferred_element_type=jnp.float32)
        gate_logit = gate_logit.reshape(BLOCK, BLOCK, CHANNELS)
        left_part = pair_mask * jax.nn.sigmoid(projected[:, :, HIDDEN_SIZE:2 * HIDDEN_SIZE]) * projected[:, :, :HIDDEN_SIZE]
        right_part = pair_mask * jax.nn.sigmoid(projected[:, :, 3 * HIDDEN_SIZE:]) * projected[:, :, 2 * HIDDEN_SIZE:3 * HIDDEN_SIZE]
        return (left_part.astype(jnp.bfloat16), right_part.astype(jnp.bfloat16), gate_logit)
    return lax.map(one_slot, (current, block_list))

def mix_all(left_all, right_all, sources, incoming):
    midpoint = BLOCK // 2

    def one_output(slot_index):
        summed = jnp.zeros((BLOCK, BLOCK, HIDDEN_SIZE), jnp.float32)
        for term_index in range(TERMS):
            left_part = left_all[sources[slot_index, term_index, 0]].astype(jnp.float32)
            right_part = right_all[sources[slot_index, term_index, 1]].astype(jnp.float32)
            if incoming:
                summed = summed + round_trip(jnp.einsum('kic,kjc->ijc', left_part, right_part))
            else:
                summed = summed + round_trip(jnp.einsum('ikc,jkc->ijc', left_part[:, :midpoint], right_part[:, :midpoint]))
                summed = summed + round_trip(jnp.einsum('ikc,jkc->ijc', left_part[:, midpoint:], right_part[:, midpoint:]))
        return summed.astype(jnp.bfloat16)
    return lax.map(one_output, jnp.arange(KEPT, dtype=jnp.int32))

def finish_all(current, mixture, gate_logit, weights):

    def one_slot(inputs):
        block_rows, mixed_block, gate_block = inputs
        normed = layer_norm(mixed_block, 2).astype(jnp.bfloat16).reshape(BLOCK * BLOCK, HIDDEN_SIZE)
        update = jnp.dot(normed, weights, preferred_element_type=jnp.float32).reshape(BLOCK, BLOCK, CHANNELS)
        return (block_rows.astype(jnp.float32) + jax.nn.sigmoid(gate_block) * update).astype(jnp.bfloat16)
    return lax.map(one_slot, (current, mixture, gate_logit))

def reference(pair, block_list, term_owner, term_slots, chain_ids, w_in, w_out):
    sources = (term_owner[:, :, None] * SLOT_DEV + term_slots).astype(jnp.int32)
    current = pair
    for layer_index, incoming in ((0, False), (1, True)):
        left_all, right_all, gate_logit = project_all(current, block_list, chain_ids, w_in[layer_index])
        mixture = mix_all(left_all, right_all, sources, incoming)
        current = finish_all(current, mixture, gate_logit, w_out[layer_index])
    return current
```

```python
import functools

import jax
import jax.numpy as jnp
from jax import lax
from jax.experimental import pallas as pl
from jax.experimental.pallas import tpu as pltpu
from jax.sharding import PartitionSpec as P

norm_epsilon = 1e-05
vmem_limit = 56 * 1024 * 1024


def sigmoid(values):
    return 0.5 + 0.5 * jnp.tanh(0.5 * values)


def layer_norm(values):
    average = jnp.mean(values, axis=-1, keepdims=True)
    centred = values - average
    variance = jnp.mean(centred * centred, axis=-1, keepdims=True)
    return centred * lax.rsqrt(variance + norm_epsilon)


def dot(a, b):
    return jnp.dot(a, b, preferred_element_type=jnp.float32)


def gated_pair(projected, mask, hidden):
    left = mask * sigmoid(projected[:, hidden : 2 * hidden]) * projected[:, :hidden]
    right = mask * sigmoid(projected[:, 3 * hidden : 4 * hidden]) * projected[:, 2 * hidden : 3 * hidden]
    return left.astype(jnp.bfloat16), right.astype(jnp.bfloat16)


def first_kernel(hidden, row_parts, ids, blocks, pair_ref, row_ref, col_ref, w_ref, gate_ref, left_ref, *rest):
    right_refs, (norm_ref, turned_ref) = rest[:row_parts], rest[row_parts:]
    _, rows, cols, channels = pair_ref.shape
    normed = layer_norm(pair_ref[0].reshape(rows * cols, channels).astype(jnp.float32))
    norm_ref[...] = normed
    gate = sigmoid(dot(normed.astype(jnp.bfloat16), w_ref[:, 4 * hidden :]))
    gate_ref[0] = gate.reshape(rows, cols, channels)
    for col in range(cols):
        turned_ref[col] = norm_ref[pl.ds(col, rows, stride=cols), :].astype(jnp.bfloat16)
    step = max(1, 128 // rows)
    part = rows // row_parts
    for start in range(0, cols, step):
        taken = turned_ref[start : start + step].reshape(step * rows, channels)
        projected = dot(taken, w_ref[:, : 4 * hidden])
        mask = col_ref[0, start : start + step, :][:, None, :] * row_ref[0][None, :, :]
        left, right = gated_pair(projected, mask.reshape(step * rows, -1), hidden)
        left_ref[0, start : start + step] = left.reshape(step, rows, hidden)
        right = right.reshape(step, rows, hidden)
        for p, right_ref in enumerate(right_refs):
            right_ref[0, start : start + step] = right[:, p * part : (p + 1) * part]


def first_operands(ids, blocks, pair, row_alive, col_alive, weights, hidden, row_parts):
    slots, rows, cols, channels = pair.shape
    n_rows = lax.axis_size("chan")
    n_cols = lax.axis_size("sub")
    part = rows // row_parts
    operand = jax.ShapeDtypeStruct((slots, cols, rows, hidden), jnp.bfloat16)
    right = jax.ShapeDtypeStruct((slots, cols, part, hidden), jnp.bfloat16)
    return pl.pallas_call(
        functools.partial(first_kernel, hidden, row_parts),
        grid_spec=pltpu.PrefetchScalarGridSpec(
            num_scalar_prefetch=2,
            grid=(slots,),
            in_specs=[
                pl.BlockSpec((1, rows, cols, channels), lambda s, ids, blocks: (s, 0, 0, 0)),
                pl.BlockSpec(
                    (1, rows, channels),
                    lambda s, ids, blocks: (blocks[2 * (ids[0] * slots + s)] * n_rows + ids[1], 0, 0),
                ),
                pl.BlockSpec(
                    (1, cols, channels),
                    lambda s, ids, blocks: (blocks[2 * (ids[0] * slots + s) + 1] * n_cols + ids[2], 0, 0),
                ),
                pl.BlockSpec(weights.shape, lambda s, ids, blocks: (0, 0)),
            ],
            out_specs=[
                pl.BlockSpec((1, rows, cols, channels), lambda s, ids, blocks: (s, 0, 0, 0)),
                pl.BlockSpec((1, cols, rows, hidden), lambda s, ids, blocks: (s, 0, 0, 0)),
            ]
            + [pl.BlockSpec((1, cols, part, hidden), lambda s, ids, blocks: (s, 0, 0, 0))] * row_parts,
            scratch_shapes=[
                pltpu.VMEM((rows * cols, channels), jnp.float32),
                pltpu.VMEM((cols, rows, channels), jnp.bfloat16),
            ],
        ),
        out_shape=[jax.ShapeDtypeStruct(pair.shape, jnp.float32), operand] + [right] * row_parts,
        compiler_params=pltpu.CompilerParams(vmem_limit_bytes=vmem_limit),
        name="first_operands",
    )(ids, blocks, pair, row_alive, col_alive, weights)


def product_kernel(shift, n_blk, width, capacity, pieces, n_refs, ids, owners, slots, *rest):
    refs = rest[:n_refs]
    out_ref, left_held, right_held, left_wide, right_wide, chosen, sems = rest[n_refs:]
    step = pl.program_id(0)
    turn = lax.rem(step, 2)
    depth, n_i, hidden = left_wide.shape
    n_j = right_wide.shape[1]

    @pl.when(step == 0)
    def _():
        target = lax.rem(ids[0] + shift, n_blk)
        for e in range(2 * capacity):
            chosen[e] = 0

        def scan(e, count):
            at = target * width + e
            here = jnp.logical_and(owners[at] == ids[0], count < capacity)

            @pl.when(here)
            def _():
                chosen[2 * count] = slots[2 * at]
                chosen[2 * count + 1] = slots[2 * at + 1]

            return count + here.astype(jnp.int32)

        lax.fori_loop(0, width, scan, jnp.int32(0))

    def copy(n, term, buffer, source):
        side, _, _, k0, depth_of, i0, size = pieces[n]
        held = (left_held, right_held)[side]
        return pltpu.make_async_copy(
            refs[source].at[chosen[2 * term + side]],
            held.at[buffer, pl.ds(k0, depth_of), pl.ds(i0, size), :],
            sems.at[buffer, n],
        )

    def start(term, buffer):
        for n, (_, on, off, *_) in enumerate(pieces):
            if on == off:
                copy(n, term, buffer, on).start()
            else:

                @pl.when(ids[3] == 1)
                def _(n=n, on=on):
                    copy(n, term, buffer, on).start()

                @pl.when(ids[3] == 0)
                def _(n=n, off=off):
                    copy(n, term, buffer, off).start()

    @pl.when(step == 0)
    def _():
        start(0, 0)

    @pl.when(step + 1 < capacity)
    def _():
        start(step + 1, 1 - turn)

    for n, piece in enumerate(pieces):
        copy(n, step, turn, piece[1]).wait()

    span = 8

    def widen(n, carry):
        at = pl.ds(n * span, span)
        left_wide[at] = left_held[turn, at].astype(jnp.float32)
        right_wide[at] = right_held[turn, at].astype(jnp.float32)
        return carry

    lax.fori_loop(0, depth // span, widen, 0)

    group = min(16, n_i)
    unroll = 4
    for i0 in range(0, n_i, group):

        def body(n, sums):
            for u in range(unroll):
                k = n * unroll + u
                right = right_wide[k]
                sums = tuple(
                    total + jnp.broadcast_to(left_wide[k, pl.ds(i0 + i, 1), :], (n_j, hidden)) * right
                    for i, total in enumerate(sums)
                )
            return sums

        zero = jnp.zeros((n_j, hidden), jnp.float32)
        sums = lax.fori_loop(0, depth // unroll, body, (zero,) * group)
        for i, total in enumerate(sums):
            out_ref[0, i0 + i] = total.astype(jnp.bfloat16)


def term_products(shift, ids, owners, slots, lefts, rights, capacity, width):
    n_blk = lax.axis_size("blk")
    refs, pieces = [], []

    def index_of(array):
        for n, known in enumerate(refs):
            if known is array:
                return n
        refs.append(array)
        return len(refs) - 1

    for side, operands in ((0, lefts), (1, rights)):
        for on, off, k0, i0 in operands:
            pieces.append((side, index_of(on), index_of(off), k0, on.shape[1], i0, on.shape[2]))
    hidden = lefts[0][0].shape[3]
    n_i = max(p[5] + p[6] for p in pieces if p[0] == 0)
    n_j = max(p[5] + p[6] for p in pieces if p[0] == 1)
    depth = max(p[3] + p[4] for p in pieces)
    return pl.pallas_call(
        functools.partial(product_kernel, shift, n_blk, width, capacity, tuple(pieces), len(refs)),
        grid_spec=pltpu.PrefetchScalarGridSpec(
            num_scalar_prefetch=3,
            grid=(capacity,),
            in_specs=[pl.BlockSpec(memory_space=pl.ANY)] * len(refs),
            out_specs=pl.BlockSpec((1, n_i, n_j, hidden), lambda t, *_: (t, 0, 0, 0)),
            scratch_shapes=[
                pltpu.VMEM((2, depth, n_i, hidden), jnp.bfloat16),
                pltpu.VMEM((2, depth, n_j, hidden), jnp.bfloat16),
                pltpu.VMEM((depth, n_i, hidden), jnp.float32),
                pltpu.VMEM((depth, n_j, hidden), jnp.float32),
                pltpu.SMEM((2 * capacity,), jnp.int32),
                pltpu.SemaphoreType.DMA((2, len(pieces))),
            ],
        ),
        out_shape=jax.ShapeDtypeStruct((capacity, n_i, n_j, hidden), jnp.bfloat16),
        compiler_params=pltpu.CompilerParams(vmem_limit_bytes=vmem_limit),
        cost_estimate=pl.CostEstimate(
            flops=2 * capacity * n_i * n_j * depth * hidden * 100,
            bytes_accessed=capacity * (depth * (n_i + n_j) + n_i * n_j) * hidden * 2,
            transcendentals=0,
        ),
        name="term_products",
    )(ids, owners, slots, *refs)


def home_kernel(last, hidden, n_blk, width, capacity, terms, ids, blocks, owners, *rest):
    parts, rest = rest[:n_blk], rest[n_blk:]
    if last:
        cur_ref, gate_ref, w_out_ref = rest[:3]
        rest = rest[3:]
        if len(rest) == 6:
            rest = rest[1:]
        out_ref, held, place, seen, sems = rest
    else:
        cur_ref, gate_ref, w_out_ref, row_ref, col_ref, w_ref = rest[:6]
        out_ref, next_gate_ref, left_ref, right_ref, held, place, seen, sems = rest[6:]
    step = pl.program_id(0)

    @pl.when(step == 0)
    def _():
        for shift in range(n_blk):
            pltpu.make_async_copy(
                parts[shift], held.at[pl.ds(shift * capacity, capacity)], sems.at[shift]
            ).start()
            seen[shift] = 0

        def scan(e, carry):
            owner = owners[ids[0] * width + e]
            shift = lax.rem(ids[0] - owner + n_blk, n_blk)
            count = seen[owner]
            seen[owner] = count + 1
            place[e] = shift * capacity + count
            return carry

        lax.fori_loop(0, width, scan, jnp.int32(0))
        for shift in range(n_blk):
            pltpu.make_async_copy(
                parts[shift], held.at[pl.ds(shift * capacity, capacity)], sems.at[shift]
            ).wait()

    _, rows, cols, channels = cur_ref.shape
    group = max(1, 128 // cols)
    for start in range(0, rows, group):
        at = pl.ds(start, group)
        total = held[place[step * terms], at].astype(jnp.float32)
        for t in range(1, terms):
            total = total + held[place[step * terms + t], at].astype(jnp.float32)
        mixture = total.astype(jnp.bfloat16).astype(jnp.float32).reshape(group * cols, hidden)
        update = dot(layer_norm(mixture).astype(jnp.bfloat16), w_out_ref[...])
        current = cur_ref[0, at].astype(jnp.float32).reshape(group * cols, channels)
        gate = gate_ref[0, at].reshape(group * cols, channels)
        result = (current + gate * update).astype(jnp.bfloat16)
        out_ref[0, at] = result.reshape(group, cols, channels)
        if not last:
            normed = layer_norm(result.astype(jnp.float32)).astype(jnp.bfloat16)
            projected = dot(normed, w_ref[...])
            next_gate_ref[0, at] = sigmoid(projected[:, 4 * hidden :]).reshape(group, cols, channels)
            mask = row_ref[0, start : start + group, :][:, None, :] * col_ref[0][None, :, :]
            left, right = gated_pair(projected, mask.reshape(group * cols, channels), hidden)
            left_ref[0, at] = left.reshape(group, cols, hidden)
            right_ref[0, at] = right.reshape(group, cols, hidden)


def home(parts, ids, blocks, owners, current, gate, w_out, capacity, terms, at, of, masks=None, w_in=None, into=None):
    n_blk = len(parts)
    slots, rows, _, channels = current.shape
    hidden = w_out.shape[0]
    cols = parts[0].shape[2]
    last = masks is None
    width = slots * terms
    n_rows, n_cols = lax.axis_size("chan"), lax.axis_size("sub")
    chunk = (1, rows, cols, channels)

    def chunk_spec(array):
        whole = array.shape[2] != cols
        return pl.BlockSpec(chunk, lambda s, *_: (s, 0, at if whole else 0, 0))

    in_specs = [pl.BlockSpec(memory_space=pl.ANY)] * n_blk + [
        chunk_spec(current),
        chunk_spec(gate),
        pl.BlockSpec(w_out.shape, lambda s, *_: (0, 0)),
    ]
    operands = [*parts, current, gate, w_out]
    aliases = {}
    if last:
        if into is not None:
            aliases = {3 + len(operands): 0}
            operands.append(into)
            in_specs.append(pl.BlockSpec(memory_space=pl.ANY))
        out_shape = [jax.ShapeDtypeStruct((slots, rows, cols * of, channels), jnp.bfloat16)]
        out_specs = [pl.BlockSpec(chunk, lambda s, *_: (s, 0, at, 0))]
    else:
        row_alive, col_alive = masks
        operands += [row_alive, col_alive, w_in]
        in_specs += [
            pl.BlockSpec(
                (1, rows, channels),
                lambda s, ids, blocks, owners: (blocks[2 * (ids[0] * slots + s)] * n_rows + ids[1], 0, 0),
            ),
            pl.BlockSpec(
                (1, cols, channels),
                lambda s, ids, blocks, owners: (blocks[2 * (ids[0] * slots + s) + 1] * n_cols + ids[2], at, 0),
            ),
            pl.BlockSpec(w_in.shape, lambda s, *_: (0, 0)),
        ]
        small = (slots, rows, cols, channels)
        out_shape = [
            jax.ShapeDtypeStruct(small, jnp.bfloat16),
            jax.ShapeDtypeStruct(small, jnp.float32),
            jax.ShapeDtypeStruct(small, jnp.bfloat16),
            jax.ShapeDtypeStruct(small, jnp.bfloat16),
        ]
        out_specs = [pl.BlockSpec(chunk, lambda s, *_: (s, 0, 0, 0))] * 4
    return pl.pallas_call(
        functools.partial(home_kernel, last, hidden, n_blk, width, capacity, terms),
        grid_spec=pltpu.PrefetchScalarGridSpec(
            num_scalar_prefetch=3,
            grid=(slots,),
            in_specs=in_specs,
            out_specs=out_specs,
            scratch_shapes=[
                pltpu.VMEM((n_blk * capacity, rows, cols, hidden), jnp.bfloat16),
                pltpu.SMEM((width,), jnp.int32),
                pltpu.SMEM((n_blk,), jnp.int32),
                pltpu.SemaphoreType.DMA((n_blk,)),
            ],
        ),
        out_shape=out_shape,
        input_output_aliases=aliases,
        compiler_params=pltpu.CompilerParams(vmem_limit_bytes=vmem_limit),
        cost_estimate=pl.CostEstimate(
            flops=2 * slots * rows * cols * channels * 6 * channels * 10,
            bytes_accessed=slots * rows * cols * channels * 16,
            transcendentals=0,
        ),
        name="home",
    )(ids, blocks, owners, *operands)


def exchange_outgoing(left, rights, n_chan, n_sub):
    if n_chan == 2 and n_sub == 2:
        both = ("chan", "sub")
        other_left = lax.ppermute(left, "sub", [(0, 1), (1, 0)])
        lefts = [(other_left, left, 0, 0), (left, other_left, left.shape[1], 0)]
        chunks = []
        for right in rights:
            one = lax.ppermute(right, both, [(0, 2), (3, 1), (1, 0), (2, 3)])
            two = lax.ppermute(right, both, [(1, 2), (2, 1)])
            chunks.append([(one, one, 0, 0), (right, two, right.shape[1], 0)])
        return lefts, chunks
    left = lax.all_gather(left, "sub", axis=1, tiled=True)
    right = jnp.concatenate(rights, axis=2)
    right = lax.all_gather(right, "chan", axis=2, tiled=True)
    right = lax.all_to_all(right, "sub", split_axis=2, concat_axis=1, tiled=True)
    cols = right.shape[2] // 2
    chunks = [right[:, :, :cols], right[:, :, cols:]]
    return [(left, left, 0, 0)], [[(r, r, 0, 0)] for r in chunks]


def exchange_incoming(lefts, rights, n_chan, n_sub):
    if n_chan == 2 and n_sub == 2:
        both = ("chan", "sub")
        left_pieces, chunks = [], []
        at = 0
        for left, right in zip(lefts, rights):
            depth = left.shape[1]
            one = lax.ppermute(left, both, [(1, 3), (2, 0), (0, 1), (3, 2)])
            two = lax.ppermute(one, both, [(0, 1), (3, 2)])
            left_pieces += [(left, one, 0, at), (one, two, depth, at)]
            other = lax.ppermute(right, "chan", [(0, 1), (1, 0)])
            chunks.append([(right, right, 0, 0), (other, other, depth, 0)])
            at += left.shape[2]
        return left_pieces, chunks
    left = lax.all_gather(jnp.concatenate(lefts, axis=2), "chan", axis=1, tiled=True)
    left = lax.all_gather(left, "sub", axis=2, tiled=True)
    size = left.shape[2] // n_chan
    left = lax.dynamic_slice_in_dim(left, lax.axis_index("chan") * size, size, 2)
    gathered = [lax.all_gather(right, "chan", axis=1, tiled=True) for right in rights]
    return [(left, left, 0, 0)], [[(r, r, 0, 0)] for r in gathered]


def per_device(pair, block_list, term_owner, term_slots, chain_ids, w_in, w_out):
    n_blk = lax.axis_size("blk")
    n_chan = lax.axis_size("chan")
    n_sub = lax.axis_size("sub")
    position = lax.axis_index("blk")
    row_group = lax.axis_index("chan")
    col_group = lax.axis_index("sub")
    slots, rows, cols, channels = pair.shape
    hidden = w_out.shape[1]
    terms = term_owner.shape[1]
    width = slots * terms
    capacity = max(2, -(-width // n_blk))
    fast = n_chan == 2 and n_sub == 2
    on_diagonal = (row_group == col_group).astype(jnp.int32)
    ids = jnp.stack([position, row_group, col_group, on_diagonal]).astype(jnp.int32)
    blocks = block_list.reshape(-1)
    owners = term_owner.reshape(-1)
    slot_of = term_slots.reshape(-1)
    alive = (chain_ids >= 0).astype(jnp.float32)

    def spread(size):
        return jnp.broadcast_to(alive.reshape(-1, size, 1), (alive.shape[0] // size, size, channels))

    row_alive, col_alive = spread(rows), spread(cols)
    shifts = [n_blk // 2] + [s for s in range(1, n_blk) if s != n_blk // 2] + [0]

    def all_products(lefts, right):
        parts = [None] * n_blk
        for shift in shifts:
            made = term_products(shift, ids, owners, slot_of, lefts, right, capacity, width)
            if shift:
                pairs = [(p, (p + shift) % n_blk) for p in range(n_blk)]
                made = lax.ppermute(made, "blk", pairs)
            parts[shift] = made
        return parts

    gate, left, *rights = first_operands(
        ids, blocks, pair, row_alive, col_alive, w_in[0], hidden, 2 if fast else 1
    )
    lefts, chunks = exchange_outgoing(left, rights, n_chan, n_sub)
    count = len(chunks)
    made = [all_products(lefts, right) for right in chunks]
    homes = [
        home(parts, ids, blocks, owners, pair, gate, w_out[0], capacity, terms, at, count, (row_alive, col_alive), w_in[1])
        for at, parts in enumerate(made)
    ]
    lefts, chunks = exchange_incoming([h[2] for h in homes], [h[3] for h in homes], n_chan, n_sub)
    made = [all_products(lefts, right) for right in chunks]
    out = None
    for at, parts in enumerate(made):
        (out,) = home(
            parts, ids, blocks, owners, homes[at][0], homes[at][1], w_out[1], capacity, terms, at, count, into=out
        )
    return out


def solution(mesh):
    in_specs = (
        P(("groups", "blk"), "chan", "sub", None),
        P("groups", None),
        P("groups", None),
        P("groups", None, None),
        P("groups"),
        P(),
        P(),
    )
    out_specs = P(("groups", "blk"), "chan", "sub", None)
    return jax.shard_map(
        per_device, mesh=mesh, in_specs=in_specs, out_specs=out_specs, check_vma=False
    )
```

```python
import functools

import jax
import jax.numpy as jnp
from jax import lax
from jax.experimental import pallas as pl
from jax.experimental.pallas import tpu as pltpu
from jax.sharding import PartitionSpec as P

norm_epsilon = 1e-05
vmem_limit = 56 * 1024 * 1024


def sigmoid(values):
    return 0.5 + 0.5 * jnp.tanh(0.5 * values)


def layer_norm(values):
    size = values.shape[1]
    ones = jnp.ones((2 * size, size), jnp.bfloat16)
    centred = values.astype(jnp.float32) - dot(values, ones[:size]) * (1.0 / size)
    squares = centred * centred
    high = squares.astype(jnp.bfloat16)
    low = (squares - high.astype(jnp.float32)).astype(jnp.bfloat16)
    variance = dot(jnp.concatenate([high, low], axis=1), ones) * (1.0 / size)
    return centred * lax.rsqrt(variance + norm_epsilon)


def alive_rows(chain_ref, start, size):
    lanes = chain_ref.shape[1]
    line = chain_ref[pl.ds(start // lanes, 1), :] >= 0
    spot = lax.broadcasted_iota(jnp.int32, (size, lanes), 0) + lax.rem(start, lanes)
    pick = jnp.logical_and(lax.broadcasted_iota(jnp.int32, (size, lanes), 1) == spot, line)
    return dot(pick.astype(jnp.float32).astype(jnp.bfloat16), jnp.ones((lanes, lanes), jnp.bfloat16))


def dot(a, b):
    return jnp.dot(a, b, preferred_element_type=jnp.float32)


def gated_pair(projected, mask, hidden):
    left = mask * sigmoid(projected[:, hidden : 2 * hidden]) * projected[:, :hidden]
    right = mask * sigmoid(projected[:, 3 * hidden : 4 * hidden]) * projected[:, 2 * hidden : 3 * hidden]
    return left.astype(jnp.bfloat16), right.astype(jnp.bfloat16)


def first_kernel(hidden, row_parts, n_chan, n_sub, ids, blocks, pair_ref, chain_ref, w_ref, gate_ref, left_ref, *rest):
    right_refs, (norm_ref, turned_ref) = rest[:row_parts], rest[row_parts:]
    slots = pl.num_programs(0)
    _, rows, cols, channels = pair_ref.shape
    block = ids[0] * slots + pl.program_id(0)
    row_alive = alive_rows(chain_ref, (blocks[0, block] * n_chan + ids[1]) * rows, rows)
    col_alive = alive_rows(chain_ref, (blocks[1, block] * n_sub + ids[2]) * cols, cols)
    group = max(1, 256 // cols)
    for start in range(0, rows, group):
        at = pl.ds(start, group)
        normed = layer_norm(pair_ref[0, at].reshape(group * cols, channels))
        norm_ref[pl.ds(start * cols, group * cols), :] = normed
        gate = sigmoid(dot(normed.astype(jnp.bfloat16), w_ref[0, :, 4 * hidden :]))
        gate_ref[0, at] = gate.reshape(group, cols, channels)
    for col in range(cols):
        turned_ref[col] = norm_ref[pl.ds(col, rows, stride=cols), :].astype(jnp.bfloat16)
    step = max(1, 128 // rows)
    part = rows // row_parts
    for start in range(0, cols, step):
        taken = turned_ref[start : start + step].reshape(step * rows, channels)
        projected = dot(taken, w_ref[0, :, : 4 * hidden])
        mask = col_alive[start : start + step][:, None, :] * row_alive[None, :, :]
        left, right = gated_pair(projected, mask.reshape(step * rows, -1), hidden)
        left_ref[0, start : start + step] = left.reshape(step, rows, hidden)
        right = right.reshape(step, rows, hidden)
        for p, right_ref in enumerate(right_refs):
            right_ref[0, start : start + step] = right[:, p * part : (p + 1) * part]


def first_operands(ids, blocks, pair, chains, w_in, hidden, row_parts):
    slots, rows, cols, channels = pair.shape
    part = rows // row_parts
    operand = jax.ShapeDtypeStruct((slots, cols, rows, hidden), jnp.bfloat16)
    right = jax.ShapeDtypeStruct((slots, cols, part, hidden), jnp.bfloat16)
    return pl.pallas_call(
        functools.partial(first_kernel, hidden, row_parts, lax.axis_size("chan"), lax.axis_size("sub")),
        grid_spec=pltpu.PrefetchScalarGridSpec(
            num_scalar_prefetch=2,
            grid=(slots,),
            in_specs=[
                pl.BlockSpec((1, rows, cols, channels), lambda s, *_: (s, 0, 0, 0)),
                pl.BlockSpec(chains.shape, lambda s, *_: (0, 0)),
                pl.BlockSpec((1,) + w_in.shape[1:], lambda s, *_: (0, 0, 0)),
            ],
            out_specs=[
                pl.BlockSpec((1, rows, cols, channels), lambda s, *_: (s, 0, 0, 0)),
                pl.BlockSpec((1, cols, rows, hidden), lambda s, *_: (s, 0, 0, 0)),
            ]
            + [pl.BlockSpec((1, cols, part, hidden), lambda s, *_: (s, 0, 0, 0))] * row_parts,
            scratch_shapes=[
                pltpu.VMEM((rows * cols, channels), jnp.float32),
                pltpu.VMEM((cols, rows, channels), jnp.bfloat16),
            ],
        ),
        out_shape=[jax.ShapeDtypeStruct(pair.shape, jnp.float32), operand] + [right] * row_parts,
        compiler_params=pltpu.CompilerParams(vmem_limit_bytes=vmem_limit),
        name="first_operands",
    )(ids, blocks, pair, chains, w_in)


def product_kernel(shift, n_blk, slots_dev, terms, capacity, pieces, n_refs, ids, owners, slots, *rest):
    refs = rest[:n_refs]
    out_ref, left_held, right_held, right_wide, chosen, sems = rest[n_refs:]
    step = pl.program_id(0)
    turn = lax.rem(step, 2)
    _, depth, n_i, hidden = left_held.shape
    n_j = right_wide.shape[1]

    @pl.when(step == 0)
    def _():
        target = lax.rem(ids[0] + shift, n_blk)
        for e in range(2 * capacity):
            chosen[e] = 0

        def scan(e, count):
            block, term = target * slots_dev + e // terms, lax.rem(e, terms)
            here = jnp.logical_and(owners[term, block] == ids[0], count < capacity)

            @pl.when(here)
            def _():
                chosen[2 * count] = slots[term, 0, block]
                chosen[2 * count + 1] = slots[term, 1, block]

            return count + here.astype(jnp.int32)

        lax.fori_loop(0, slots_dev * terms, scan, jnp.int32(0))

    def copy(n, term, buffer, source):
        side, _, _, k0, depth_of, i0, size = pieces[n]
        held = (left_held, right_held)[side]
        return pltpu.make_async_copy(
            refs[source].at[chosen[2 * term + side]],
            held.at[buffer, pl.ds(k0, depth_of), pl.ds(i0, size), :],
            sems.at[buffer, n],
        )

    def start(term, buffer):
        for n, (_, on, off, *_) in enumerate(pieces):
            if on == off:
                copy(n, term, buffer, on).start()
            else:

                @pl.when(ids[3] == 1)
                def _(n=n, on=on):
                    copy(n, term, buffer, on).start()

                @pl.when(ids[3] == 0)
                def _(n=n, off=off):
                    copy(n, term, buffer, off).start()

    @pl.when(step == 0)
    def _():
        start(0, 0)

    @pl.when(step + 1 < capacity)
    def _():
        start(step + 1, 1 - turn)

    for n, piece in enumerate(pieces):
        copy(n, step, turn, piece[1]).wait()

    span = 8

    def widen(n, carry):
        at = pl.ds(n * span, span)
        right_wide[at] = right_held[turn, at].astype(jnp.float32)
        return carry

    lax.fori_loop(0, depth // span, widen, 0)

    group = min(8, n_j)
    unroll = 4
    for j0 in range(0, n_j, group):

        def body(n, sums):
            for u in range(unroll):
                k = n * unroll + u
                left = left_held[turn, k].astype(jnp.float32).reshape(n_i // 8, 8, hidden)
                sums = tuple(
                    total + left * right_wide[k, pl.ds(j0 + j, 8, stride=0), :][None]
                    for j, total in enumerate(sums)
                )
            return sums

        zero = jnp.zeros((n_i // 8, 8, hidden), jnp.float32)
        sums = lax.fori_loop(0, depth // unroll, body, (zero,) * group)
        for j, total in enumerate(sums):
            out_ref[0, j0 + j] = total.reshape(n_i, hidden).astype(jnp.bfloat16)


def term_products(shift, ids, owners, slots, lefts, rights, capacity, slots_dev, terms):
    n_blk = lax.axis_size("blk")
    refs, pieces = [], []

    def index_of(array):
        for n, known in enumerate(refs):
            if known is array:
                return n
        refs.append(array)
        return len(refs) - 1

    for side, operands in ((0, lefts), (1, rights)):
        for on, off, k0, i0 in operands:
            pieces.append((side, index_of(on), index_of(off), k0, on.shape[1], i0, on.shape[2]))
    hidden = lefts[0][0].shape[3]
    n_i = max(p[5] + p[6] for p in pieces if p[0] == 0)
    n_j = max(p[5] + p[6] for p in pieces if p[0] == 1)
    depth = max(p[3] + p[4] for p in pieces)
    return pl.pallas_call(
        functools.partial(
            product_kernel, shift, n_blk, slots_dev, terms, capacity, tuple(pieces), len(refs)
        ),
        grid_spec=pltpu.PrefetchScalarGridSpec(
            num_scalar_prefetch=3,
            grid=(capacity,),
            in_specs=[pl.BlockSpec(memory_space=pl.ANY)] * len(refs),
            out_specs=pl.BlockSpec((1, n_j, n_i, hidden), lambda t, *_: (t, 0, 0, 0)),
            scratch_shapes=[
                pltpu.VMEM((2, depth, n_i, hidden), jnp.bfloat16),
                pltpu.VMEM((2, depth, n_j, hidden), jnp.bfloat16),
                pltpu.VMEM((depth, n_j, hidden), jnp.float32),
                pltpu.SMEM((2 * capacity,), jnp.int32),
                pltpu.SemaphoreType.DMA((2, len(pieces))),
            ],
        ),
        out_shape=jax.ShapeDtypeStruct((capacity, n_j, n_i, hidden), jnp.bfloat16),
        compiler_params=pltpu.CompilerParams(vmem_limit_bytes=vmem_limit),
        cost_estimate=pl.CostEstimate(
            flops=2 * capacity * n_i * n_j * depth * hidden * 100,
            bytes_accessed=capacity * (depth * (n_i + n_j) + n_i * n_j) * hidden * 2,
            transcendentals=0,
        ),
        name="term_products",
    )(ids, owners, slots, *refs)


def home_kernel(last, hidden, n_blk, n_chan, n_sub, at, of, slots_dev, terms, capacity, ids, blocks, owners, *rest):
    parts, rest = rest[:n_blk], rest[n_blk:]
    scratch, rest = rest[-5:], rest[:-5]
    held, turned, place, seen, sems = scratch
    cur_ref, gate_ref, w_out_ref = rest[:3]
    if last:
        out_ref = rest[-1]
    else:
        chain_ref, w_ref, out_ref, next_gate_ref, left_ref, right_ref = rest[3:]
    step = pl.program_id(0)
    _, rows, cols, channels = cur_ref.shape

    def arrival(shift):
        return pltpu.make_async_copy(parts[shift], held.at[pl.ds(shift * capacity, capacity)], sems.at[shift])

    @pl.when(step == 0)
    def _():
        for shift in range(n_blk):
            arrival(shift).start()
            seen[shift] = 0

        def scan(e, carry):
            owner = owners[lax.rem(e, terms), ids[0] * slots_dev + e // terms]
            shift = lax.rem(ids[0] - owner + n_blk, n_blk)
            count = seen[owner]
            seen[owner] = count + 1
            place[e] = shift * capacity + count
            return carry

        lax.fori_loop(0, slots_dev * terms, scan, jnp.int32(0))
        for shift in range(n_blk):
            arrival(shift).wait()

    if not last:
        block = ids[0] * slots_dev + step
        row_alive = alive_rows(chain_ref, (blocks[0, block] * n_chan + ids[1]) * rows, rows)
        col_alive = alive_rows(chain_ref, ((blocks[1, block] * n_sub + ids[2]) * of + at) * cols, cols)
    span = max(1, 128 // rows)
    for start in range(0, cols, span):
        taken = pl.ds(start, span)
        total = held[place[step * terms], taken].astype(jnp.float32)
        for t in range(1, terms):
            total = total + held[place[step * terms + t], taken].astype(jnp.float32)
        rounded = total.astype(jnp.bfloat16).astype(jnp.float32)
        turned[pl.ds(start * rows, span * rows), :] = rounded.reshape(span * rows, hidden)
    group = min(rows, max(1, 256 // cols))
    for start in range(0, rows, group):
        taken = pl.ds(start, group)
        mixture = jnp.concatenate(
            [turned[pl.ds(row, cols, stride=rows), :].astype(jnp.bfloat16) for row in range(start, start + group)]
        )
        update = dot(layer_norm(mixture).astype(jnp.bfloat16), w_out_ref[0])
        current = cur_ref[0, taken].astype(jnp.float32).reshape(group * cols, channels)
        gate = gate_ref[0, taken].reshape(group * cols, channels)
        result = (current + gate * update).astype(jnp.bfloat16)
        out_ref[0, taken] = result.reshape(group, cols, channels)
        if not last:
            normed = layer_norm(result).astype(jnp.bfloat16)
            projected = dot(normed, w_ref[0])
            next_gate_ref[0, taken] = sigmoid(projected[:, 4 * hidden :]).reshape(group, cols, channels)
            mask = row_alive[start : start + group][:, None, :] * col_alive[None, :, :]
            left, right = gated_pair(projected, mask.reshape(group * cols, channels), hidden)
            left_ref[0, taken] = left.reshape(group, cols, hidden)
            right_ref[0, taken] = right.reshape(group, cols, hidden)


def home(layer, parts, ids, blocks, owners, current, gate, w_out, capacity, terms, at, of, chains, w_in, last, into=None):
    n_blk = len(parts)
    slots, rows, _, channels = current.shape
    hidden = w_out.shape[1]
    cols = parts[0].shape[1]
    chunk = (1, rows, cols, channels)

    def chunk_spec(array):
        whole = array.shape[2] != cols
        return pl.BlockSpec(chunk, lambda s, *_: (s, 0, at if whole else 0, 0))

    def layer_spec(array, index):
        return pl.BlockSpec((1,) + array.shape[1:], lambda s, *_: (index, 0, 0))

    in_specs = [pl.BlockSpec(memory_space=pl.ANY)] * n_blk + [
        chunk_spec(current),
        chunk_spec(gate),
        layer_spec(w_out, layer),
    ]
    operands = [*parts, current, gate, w_out]
    aliases = {}
    if last:
        if into is not None:
            aliases = {3 + len(operands): 0}
            operands.append(into)
            in_specs.append(pl.BlockSpec(memory_space=pl.ANY))
        out_shape = [jax.ShapeDtypeStruct((slots, rows, cols * of, channels), jnp.bfloat16)]
        out_specs = [pl.BlockSpec(chunk, lambda s, *_: (s, 0, at, 0))]
    else:
        operands += [chains, w_in]
        in_specs += [pl.BlockSpec(chains.shape, lambda s, *_: (0, 0)), layer_spec(w_in, layer + 1)]
        small = (slots, rows, cols, channels)
        out_shape = [jax.ShapeDtypeStruct(small, t) for t in (jnp.bfloat16, jnp.float32, jnp.bfloat16, jnp.bfloat16)]
        out_specs = [pl.BlockSpec(chunk, lambda s, *_: (s, 0, 0, 0))] * 4
    return pl.pallas_call(
        functools.partial(
            home_kernel, last, hidden, n_blk, lax.axis_size("chan"), lax.axis_size("sub"), at, of, slots, terms, capacity
        ),
        grid_spec=pltpu.PrefetchScalarGridSpec(
            num_scalar_prefetch=3,
            grid=(slots,),
            in_specs=in_specs,
            out_specs=out_specs,
            scratch_shapes=[
                pltpu.VMEM((n_blk * capacity, cols, rows, hidden), jnp.bfloat16),
                pltpu.VMEM((rows * cols, hidden), jnp.float32),
                pltpu.SMEM((slots * terms,), jnp.int32),
                pltpu.SMEM((n_blk,), jnp.int32),
                pltpu.SemaphoreType.DMA((n_blk,)),
            ],
        ),
        out_shape=out_shape,
        input_output_aliases=aliases,
        compiler_params=pltpu.CompilerParams(vmem_limit_bytes=vmem_limit),
        cost_estimate=pl.CostEstimate(
            flops=2 * slots * rows * cols * channels * 6 * channels * 10,
            bytes_accessed=slots * rows * cols * channels * 16,
            transcendentals=0,
        ),
        name="home",
    )(ids, blocks, owners, *operands)


def exchange_outgoing(left, rights, n_chan, n_sub):
    if n_chan == 2 and n_sub == 2:
        both = ("chan", "sub")
        other_left = lax.ppermute(left, "sub", [(0, 1), (1, 0)])
        lefts = [(other_left, left, 0, 0), (left, other_left, left.shape[1], 0)]
        chunks = []
        for right in rights:
            if chunks:
                (one, *_), (_, two, *_) = chunks[-1]
                right, *_ = lax.optimization_barrier((right, one, two))
            one = lax.ppermute(right, both, [(0, 2), (3, 1), (1, 0), (2, 3)])
            two = lax.ppermute(right, both, [(1, 2), (2, 1)])
            chunks.append([(one, one, 0, 0), (right, two, right.shape[1], 0)])
        return lefts, chunks
    left = lax.all_gather(left, "sub", axis=1, tiled=True)
    right = jnp.concatenate(rights, axis=2)
    right = lax.all_gather(right, "chan", axis=2, tiled=True)
    right = lax.all_to_all(right, "sub", split_axis=2, concat_axis=1, tiled=True)
    cols = right.shape[2] // 2
    chunks = [right[:, :, :cols], right[:, :, cols:]]
    return [(left, left, 0, 0)], [[(r, r, 0, 0)] for r in chunks]


def exchange_incoming(lefts, rights, n_chan, n_sub):
    if n_chan == 2 and n_sub == 2:
        both = ("chan", "sub")
        left_pieces, chunks = [], []
        at = 0
        for left, right in zip(lefts, rights):
            depth = left.shape[1]
            one = lax.ppermute(left, both, [(1, 3), (2, 0), (0, 1), (3, 2)])
            two = lax.ppermute(one, both, [(0, 1), (3, 2)])
            left_pieces += [(left, one, 0, at), (one, two, depth, at)]
            other = lax.ppermute(right, "chan", [(0, 1), (1, 0)])
            chunks.append([(right, right, 0, 0), (other, other, depth, 0)])
            at += left.shape[2]
        return left_pieces, chunks
    left = lax.all_gather(jnp.concatenate(lefts, axis=2), "chan", axis=1, tiled=True)
    left = lax.all_gather(left, "sub", axis=2, tiled=True)
    size = left.shape[2] // n_chan
    left = lax.dynamic_slice_in_dim(left, lax.axis_index("chan") * size, size, 2)
    gathered = [lax.all_gather(right, "chan", axis=1, tiled=True) for right in rights]
    return [(left, left, 0, 0)], [[(r, r, 0, 0)] for r in gathered]


def per_device(pair, block_list, term_owner, term_slots, chain_ids, w_in, w_out):
    n_blk = lax.axis_size("blk")
    n_chan = lax.axis_size("chan")
    n_sub = lax.axis_size("sub")
    position = lax.axis_index("blk")
    row_group = lax.axis_index("chan")
    col_group = lax.axis_index("sub")
    slots, rows, cols, channels = pair.shape
    hidden = w_out.shape[1]
    terms = term_owner.shape[1]
    capacity = max(2, -(-slots * terms // n_blk))
    fast = n_chan == 2 and n_sub == 2
    on_diagonal = (row_group == col_group).astype(jnp.int32)
    ids = jnp.stack([position, row_group, col_group, on_diagonal]).astype(jnp.int32)
    blocks = block_list.T
    owners = term_owner.T
    slot_of = jnp.transpose(term_slots, (1, 2, 0))
    chains = chain_ids.reshape(-1, 128)
    shifts = [n_blk // 2] + [s for s in range(1, n_blk) if s != n_blk // 2] + [0]

    def all_products(lefts, right):
        parts = [None] * n_blk
        for shift in shifts:
            made = term_products(shift, ids, owners, slot_of, lefts, right, capacity, slots, terms)
            if shift:
                pairs = [(p, (p + shift) % n_blk) for p in range(n_blk)]
                made = lax.ppermute(made, "blk", pairs)
            parts[shift] = made
        return parts

    def at_home(layer, parts, current, gate, at, of, into=None):
        last = layer == w_in.shape[0] - 1
        return home(
            layer, parts, ids, blocks, owners, current, gate, w_out, capacity, terms, at, of, chains, w_in, last, into
        )

    gate, left, *rights = first_operands(ids, blocks, pair, chains, w_in, hidden, 2 if fast else 1)
    lefts, chunks = exchange_outgoing(left, rights, n_chan, n_sub)
    count = len(chunks)
    made = [all_products(lefts, right) for right in chunks]
    homes = [at_home(0, parts, pair, gate, at, count) for at, parts in enumerate(made)]
    lefts, chunks = exchange_incoming([h[2] for h in homes], [h[3] for h in homes], n_chan, n_sub)
    made = [all_products(lefts, right) for right in chunks]
    out = None
    for at, parts in enumerate(made):
        (out,) = at_home(1, parts, homes[at][0], homes[at][1], at, count, into=out)
    return out


def solution(mesh):
    in_specs = (
        P(("groups", "blk"), "chan", "sub", None),
        P("groups", None),
        P("groups", None),
        P("groups", None, None),
        P("groups"),
        P(),
        P(),
    )
    out_specs = P(("groups", "blk"), "chan", "sub", None)
    return jax.shard_map(
        per_device, mesh=mesh, in_specs=in_specs, out_specs=out_specs, check_vma=False
    )
```

```python
import functools

import jax
import jax.numpy as jnp
from jax import lax
from jax.experimental import pallas as pl
from jax.experimental.pallas import tpu as pltpu
from jax.sharding import PartitionSpec as P

norm_epsilon = 1e-05
vmem_limit = 56 * 1024 * 1024


def sigmoid(values):
    return 0.5 + 0.5 * jnp.tanh(0.5 * values)


def layer_norm(values):
    values = values.astype(jnp.float32)
    centred = values - jnp.mean(values, axis=-1, keepdims=True)
    variance = jnp.mean(centred * centred, axis=-1, keepdims=True)
    return centred * lax.rsqrt(variance + norm_epsilon)


def alive_rows(chain_ref, start, size):
    lanes = chain_ref.shape[1]
    line = chain_ref[pl.ds(start // lanes, 1), :] >= 0
    spot = lax.broadcasted_iota(jnp.int32, (size, lanes), 0) + lax.rem(start, lanes)
    pick = jnp.logical_and(lax.broadcasted_iota(jnp.int32, (size, lanes), 1) == spot, line)
    return dot(pick.astype(jnp.float32).astype(jnp.bfloat16), jnp.ones((lanes, lanes), jnp.bfloat16))


def dot(a, b):
    return jnp.dot(a, b, preferred_element_type=jnp.float32)


def gated_pair(projected, mask, hidden):
    left = mask * sigmoid(projected[:, hidden : 2 * hidden]) * projected[:, :hidden]
    right = mask * sigmoid(projected[:, 3 * hidden : 4 * hidden]) * projected[:, 2 * hidden : 3 * hidden]
    return left.astype(jnp.bfloat16), right.astype(jnp.bfloat16)


def first_kernel(hidden, row_parts, n_chan, n_sub, ids, blocks, pair_ref, chain_ref, w_ref, gate_ref, left_ref, *rest):
    right_refs, (norm_ref, turned_ref) = rest[:row_parts], rest[row_parts:]
    slots = pl.num_programs(0)
    _, rows, cols, channels = pair_ref.shape
    block = ids[0] * slots + pl.program_id(0)
    row_alive = alive_rows(chain_ref, (blocks[0, block] * n_chan + ids[1]) * rows, rows)
    col_alive = alive_rows(chain_ref, (blocks[1, block] * n_sub + ids[2]) * cols, cols)
    group = max(1, 256 // cols)
    for start in range(0, rows, group):
        at = pl.ds(start, group)
        normed = layer_norm(pair_ref[0, at].reshape(group * cols, channels))
        norm_ref[pl.ds(start * cols, group * cols), :] = normed
        gate = sigmoid(dot(normed.astype(jnp.bfloat16), w_ref[0, :, 4 * hidden :]))
        gate_ref[0, at] = gate.reshape(group, cols, channels)
    for col in range(cols):
        turned_ref[col] = norm_ref[pl.ds(col, rows, stride=cols), :].astype(jnp.bfloat16)
    step = max(1, 128 // rows)
    part = rows // row_parts
    for start in range(0, cols, step):
        taken = turned_ref[start : start + step].reshape(step * rows, channels)
        projected = dot(taken, w_ref[0, :, : 4 * hidden])
        mask = col_alive[start : start + step][:, None, :] * row_alive[None, :, :]
        left, right = gated_pair(projected, mask.reshape(step * rows, -1), hidden)
        left_ref[0, start : start + step] = left.reshape(step, rows, hidden)
        right = right.reshape(step, rows, hidden)
        for p, right_ref in enumerate(right_refs):
            right_ref[0, start : start + step] = right[:, p * part : (p + 1) * part]


def first_operands(ids, blocks, pair, chains, w_in, hidden, row_parts):
    slots, rows, cols, channels = pair.shape
    part = rows // row_parts
    operand = jax.ShapeDtypeStruct((slots, cols, rows, hidden), jnp.bfloat16)
    right = jax.ShapeDtypeStruct((slots, cols, part, hidden), jnp.bfloat16)
    return pl.pallas_call(
        functools.partial(first_kernel, hidden, row_parts, lax.axis_size("chan"), lax.axis_size("sub")),
        grid_spec=pltpu.PrefetchScalarGridSpec(
            num_scalar_prefetch=2,
            grid=(slots,),
            in_specs=[
                pl.BlockSpec((1, rows, cols, channels), lambda s, *_: (s, 0, 0, 0)),
                pl.BlockSpec(chains.shape, lambda s, *_: (0, 0)),
                pl.BlockSpec((1,) + w_in.shape[1:], lambda s, *_: (0, 0, 0)),
            ],
            out_specs=[
                pl.BlockSpec((1, rows, cols, channels), lambda s, *_: (s, 0, 0, 0)),
                pl.BlockSpec((1, cols, rows, hidden), lambda s, *_: (s, 0, 0, 0)),
            ]
            + [pl.BlockSpec((1, cols, part, hidden), lambda s, *_: (s, 0, 0, 0))] * row_parts,
            scratch_shapes=[
                pltpu.VMEM((rows * cols, channels), jnp.float32),
                pltpu.VMEM((cols, rows, channels), jnp.bfloat16),
            ],
        ),
        out_shape=[jax.ShapeDtypeStruct(pair.shape, jnp.float32), operand] + [right] * row_parts,
        compiler_params=pltpu.CompilerParams(vmem_limit_bytes=vmem_limit),
        name="first_operands",
    )(ids, blocks, pair, chains, w_in)


def product_kernel(shift, n_blk, slots_dev, terms, capacity, pieces, n_refs, ids, owners, slots, *rest):
    refs = rest[:n_refs]
    out_ref, left_held, right_held, right_wide, chosen, sems = rest[n_refs:]
    step = pl.program_id(0)
    turn = lax.rem(step, 2)
    _, depth, n_i, hidden = left_held.shape
    n_j = right_wide.shape[1]

    @pl.when(step == 0)
    def _():
        target = lax.rem(ids[0] + shift, n_blk)
        for e in range(2 * capacity):
            chosen[e] = 0

        def scan(e, count):
            block, term = target * slots_dev + e // terms, lax.rem(e, terms)
            here = jnp.logical_and(owners[term, block] == ids[0], count < capacity)

            @pl.when(here)
            def _():
                chosen[2 * count] = slots[term, 0, block]
                chosen[2 * count + 1] = slots[term, 1, block]

            return count + here.astype(jnp.int32)

        lax.fori_loop(0, slots_dev * terms, scan, jnp.int32(0))

    def copy(n, term, buffer, source):
        side, _, _, k0, depth_of, i0, size = pieces[n]
        held = (left_held, right_held)[side]
        return pltpu.make_async_copy(
            refs[source].at[chosen[2 * term + side]],
            held.at[buffer, pl.ds(k0, depth_of), pl.ds(i0, size), :],
            sems.at[buffer, n],
        )

    def start(term, buffer):
        for n, (_, on, off, *_) in enumerate(pieces):
            if on == off:
                copy(n, term, buffer, on).start()
            else:

                @pl.when(ids[3] == 1)
                def _(n=n, on=on):
                    copy(n, term, buffer, on).start()

                @pl.when(ids[3] == 0)
                def _(n=n, off=off):
                    copy(n, term, buffer, off).start()

    @pl.when(step == 0)
    def _():
        start(0, 0)

    @pl.when(step + 1 < capacity)
    def _():
        start(step + 1, 1 - turn)

    for n, piece in enumerate(pieces):
        copy(n, step, turn, piece[1]).wait()

    span = 8

    def widen(n, carry):
        at = pl.ds(n * span, span)
        right_wide[at] = right_held[turn, at].astype(jnp.float32)
        return carry

    lax.fori_loop(0, depth // span, widen, 0)

    group = min(8, n_j)
    unroll = 4
    for j0 in range(0, n_j, group):

        def body(n, sums):
            for u in range(unroll):
                k = n * unroll + u
                left = left_held[turn, k].astype(jnp.float32).reshape(n_i // 8, 8, hidden)
                sums = tuple(
                    total + left * right_wide[k, pl.ds(j0 + j, 8, stride=0), :][None]
                    for j, total in enumerate(sums)
                )
            return sums

        zero = jnp.zeros((n_i // 8, 8, hidden), jnp.float32)
        sums = lax.fori_loop(0, depth // unroll, body, (zero,) * group)
        for j, total in enumerate(sums):
            out_ref[0, j0 + j] = total.reshape(n_i, hidden).astype(jnp.bfloat16)


def term_products(shift, ids, owners, slots, lefts, rights, capacity, slots_dev, terms):
    n_blk = lax.axis_size("blk")
    refs, pieces = [], []

    def index_of(array):
        for n, known in enumerate(refs):
            if known is array:
                return n
        refs.append(array)
        return len(refs) - 1

    for side, operands in ((0, lefts), (1, rights)):
        for on, off, k0, i0 in operands:
            pieces.append((side, index_of(on), index_of(off), k0, on.shape[1], i0, on.shape[2]))
    hidden = lefts[0][0].shape[3]
    n_i = max(p[5] + p[6] for p in pieces if p[0] == 0)
    n_j = max(p[5] + p[6] for p in pieces if p[0] == 1)
    depth = max(p[3] + p[4] for p in pieces)
    return pl.pallas_call(
        functools.partial(
            product_kernel, shift, n_blk, slots_dev, terms, capacity, tuple(pieces), len(refs)
        ),
        grid_spec=pltpu.PrefetchScalarGridSpec(
            num_scalar_prefetch=3,
            grid=(capacity,),
            in_specs=[pl.BlockSpec(memory_space=pl.ANY)] * len(refs),
            out_specs=pl.BlockSpec((1, n_j, n_i, hidden), lambda t, *_: (t, 0, 0, 0)),
            scratch_shapes=[
                pltpu.VMEM((2, depth, n_i, hidden), jnp.bfloat16),
                pltpu.VMEM((2, depth, n_j, hidden), jnp.bfloat16),
                pltpu.VMEM((depth, n_j, hidden), jnp.float32),
                pltpu.SMEM((2 * capacity,), jnp.int32),
                pltpu.SemaphoreType.DMA((2, len(pieces))),
            ],
        ),
        out_shape=jax.ShapeDtypeStruct((capacity, n_j, n_i, hidden), jnp.bfloat16),
        compiler_params=pltpu.CompilerParams(vmem_limit_bytes=vmem_limit),
        cost_estimate=pl.CostEstimate(
            flops=2 * capacity * n_i * n_j * depth * hidden * 100,
            bytes_accessed=capacity * (depth * (n_i + n_j) + n_i * n_j) * hidden * 2,
            transcendentals=0,
        ),
        name="term_products",
    )(ids, owners, slots, *refs)


def home_kernel(last, hidden, n_blk, n_chan, n_sub, at, of, slots_dev, terms, capacity, ids, blocks, owners, *rest):
    parts, rest = rest[:n_blk], rest[n_blk:]
    scratch, rest = rest[-5:], rest[:-5]
    held, turned, place, seen, sems = scratch
    cur_ref, gate_ref, w_out_ref = rest[:3]
    if last:
        out_ref = rest[-1]
    else:
        chain_ref, w_ref, out_ref, next_gate_ref, left_ref, right_ref = rest[3:]
    step = pl.program_id(0)
    _, rows, cols, channels = cur_ref.shape

    def arrival(shift):
        return pltpu.make_async_copy(parts[shift], held.at[pl.ds(shift * capacity, capacity)], sems.at[shift])

    @pl.when(step == 0)
    def _():
        for shift in range(n_blk):
            arrival(shift).start()
            seen[shift] = 0

        def scan(e, carry):
            owner = owners[lax.rem(e, terms), ids[0] * slots_dev + e // terms]
            shift = lax.rem(ids[0] - owner + n_blk, n_blk)
            count = seen[owner]
            seen[owner] = count + 1
            place[e] = shift * capacity + count
            return carry

        lax.fori_loop(0, slots_dev * terms, scan, jnp.int32(0))
        for shift in range(n_blk):
            arrival(shift).wait()

    if not last:
        block = ids[0] * slots_dev + step
        row_alive = alive_rows(chain_ref, (blocks[0, block] * n_chan + ids[1]) * rows, rows)
        col_alive = alive_rows(chain_ref, ((blocks[1, block] * n_sub + ids[2]) * of + at) * cols, cols)
    span = max(1, 128 // rows)
    for start in range(0, cols, span):
        taken = pl.ds(start, span)
        total = held[place[step * terms], taken].astype(jnp.float32)
        for t in range(1, terms):
            total = total + held[place[step * terms + t], taken].astype(jnp.float32)
        rounded = total.astype(jnp.bfloat16).astype(jnp.float32)
        turned[pl.ds(start * rows, span * rows), :] = rounded.reshape(span * rows, hidden)
    group = min(rows, max(1, 256 // cols))
    for start in range(0, rows, group):
        taken = pl.ds(start, group)
        mixture = jnp.concatenate(
            [turned[pl.ds(row, cols, stride=rows), :].astype(jnp.bfloat16) for row in range(start, start + group)]
        )
        update = dot(layer_norm(mixture).astype(jnp.bfloat16), w_out_ref[0])
        current = cur_ref[0, taken].astype(jnp.float32).reshape(group * cols, channels)
        gate = gate_ref[0, taken].reshape(group * cols, channels)
        result = (current + gate * update).astype(jnp.bfloat16)
        out_ref[0, taken] = result.reshape(group, cols, channels)
        if not last:
            normed = layer_norm(result).astype(jnp.bfloat16)
            projected = dot(normed, w_ref[0])
            next_gate_ref[0, taken] = sigmoid(projected[:, 4 * hidden :]).reshape(group, cols, channels)
            mask = row_alive[start : start + group][:, None, :] * col_alive[None, :, :]
            left, right = gated_pair(projected, mask.reshape(group * cols, channels), hidden)
            left_ref[0, taken] = left.reshape(group, cols, hidden)
            right_ref[0, taken] = right.reshape(group, cols, hidden)


def home(layer, parts, ids, blocks, owners, current, gate, w_out, capacity, terms, at, of, chains, w_in, last, into=None):
    n_blk = len(parts)
    slots, rows, _, channels = current.shape
    hidden = w_out.shape[1]
    cols = parts[0].shape[1]
    chunk = (1, rows, cols, channels)

    def chunk_spec(array):
        whole = array.shape[2] != cols
        return pl.BlockSpec(chunk, lambda s, *_: (s, 0, at if whole else 0, 0))

    def layer_spec(array, index):
        return pl.BlockSpec((1,) + array.shape[1:], lambda s, *_: (index, 0, 0))

    in_specs = [pl.BlockSpec(memory_space=pl.ANY)] * n_blk + [
        chunk_spec(current),
        chunk_spec(gate),
        layer_spec(w_out, layer),
    ]
    operands = [*parts, current, gate, w_out]
    aliases = {}
    if last:
        if into is not None:
            aliases = {3 + len(operands): 0}
            operands.append(into)
            in_specs.append(pl.BlockSpec(memory_space=pl.ANY))
        out_shape = [jax.ShapeDtypeStruct((slots, rows, cols * of, channels), jnp.bfloat16)]
        out_specs = [pl.BlockSpec(chunk, lambda s, *_: (s, 0, at, 0))]
    else:
        operands += [chains, w_in]
        in_specs += [pl.BlockSpec(chains.shape, lambda s, *_: (0, 0)), layer_spec(w_in, layer + 1)]
        small = (slots, rows, cols, channels)
        out_shape = [jax.ShapeDtypeStruct(small, t) for t in (jnp.bfloat16, jnp.float32, jnp.bfloat16, jnp.bfloat16)]
        out_specs = [pl.BlockSpec(chunk, lambda s, *_: (s, 0, 0, 0))] * 4
    return pl.pallas_call(
        functools.partial(
            home_kernel, last, hidden, n_blk, lax.axis_size("chan"), lax.axis_size("sub"), at, of, slots, terms, capacity
        ),
        grid_spec=pltpu.PrefetchScalarGridSpec(
            num_scalar_prefetch=3,
            grid=(slots,),
            in_specs=in_specs,
            out_specs=out_specs,
            scratch_shapes=[
                pltpu.VMEM((n_blk * capacity, cols, rows, hidden), jnp.bfloat16),
                pltpu.VMEM((rows * cols, hidden), jnp.float32),
                pltpu.SMEM((slots * terms,), jnp.int32),
                pltpu.SMEM((n_blk,), jnp.int32),
                pltpu.SemaphoreType.DMA((n_blk,)),
            ],
        ),
        out_shape=out_shape,
        input_output_aliases=aliases,
        compiler_params=pltpu.CompilerParams(vmem_limit_bytes=vmem_limit),
        cost_estimate=pl.CostEstimate(
            flops=2 * slots * rows * cols * channels * 6 * channels * 10,
            bytes_accessed=slots * rows * cols * channels * 16,
            transcendentals=0,
        ),
        name="home",
    )(ids, blocks, owners, *operands)


def exchange_outgoing(left, rights, n_chan, n_sub):
    if n_chan == 2 and n_sub == 2:
        both = ("chan", "sub")
        other_left = lax.ppermute(left, "sub", [(0, 1), (1, 0)])
        lefts = [(other_left, left, 0, 0), (left, other_left, left.shape[1], 0)]
        chunks = []
        for right in rights:
            if chunks:
                (one, *_), (_, two, *_) = chunks[-1]
                right, *_ = lax.optimization_barrier((right, one, two))
            one = lax.ppermute(right, both, [(0, 2), (3, 1), (1, 0), (2, 3)])
            two = lax.ppermute(right, both, [(1, 2), (2, 1)])
            chunks.append([(one, one, 0, 0), (right, two, right.shape[1], 0)])
        return lefts, chunks
    left = lax.all_gather(left, "sub", axis=1, tiled=True)
    right = jnp.concatenate(rights, axis=2)
    right = lax.all_gather(right, "chan", axis=2, tiled=True)
    right = lax.all_to_all(right, "sub", split_axis=2, concat_axis=1, tiled=True)
    cols = right.shape[2] // 2
    chunks = [right[:, :, :cols], right[:, :, cols:]]
    return [(left, left, 0, 0)], [[(r, r, 0, 0)] for r in chunks]


def exchange_incoming(lefts, rights, n_chan, n_sub):
    if n_chan == 2 and n_sub == 2:
        both = ("chan", "sub")
        left_pieces, chunks = [], []
        at = 0
        for left, right in zip(lefts, rights):
            depth = left.shape[1]
            one = lax.ppermute(left, both, [(1, 3), (2, 0), (0, 1), (3, 2)])
            two = lax.ppermute(one, both, [(0, 1), (3, 2)])
            left_pieces += [(left, one, 0, at), (one, two, depth, at)]
            other = lax.ppermute(right, "chan", [(0, 1), (1, 0)])
            chunks.append([(right, right, 0, 0), (other, other, depth, 0)])
            at += left.shape[2]
        return left_pieces, chunks
    left = lax.all_gather(jnp.concatenate(lefts, axis=2), "chan", axis=1, tiled=True)
    left = lax.all_gather(left, "sub", axis=2, tiled=True)
    size = left.shape[2] // n_chan
    left = lax.dynamic_slice_in_dim(left, lax.axis_index("chan") * size, size, 2)
    gathered = [lax.all_gather(right, "chan", axis=1, tiled=True) for right in rights]
    return [(left, left, 0, 0)], [[(r, r, 0, 0)] for r in gathered]


def lane_group(shape, size):
    return lax.broadcasted_iota(jnp.int32, shape, 1) // size


def spread_weights(w_ref, wide_ref, hidden, size):
    parts = hidden // size
    for kind in range(4):
        weights = w_ref[0, :, kind * hidden : (kind + 1) * hidden].astype(jnp.float32)
        group = lane_group(weights.shape, size)
        for part in range(parts):
            kept = jnp.where(group == part, weights, 0.0)
            for a in range(parts):
                moved = pltpu.roll(kept, ((a - part) % parts) * size, 1) if a != part else kept
                at = (kind * parts + part) * hidden
                wide_ref[a * hidden : (a + 1) * hidden, at : at + hidden] = moved.astype(jnp.bfloat16)


def make_operands(taken, wide_ref, row_alive, k_alive, out_refs, laid, turned):
    rows, size, hidden = taken.shape
    parts, bands = hidden // size, size
    groups = rows // parts
    stacked = jnp.concatenate(
        [jnp.concatenate([taken[g * parts + a] for a in range(parts)], axis=1) for g in range(groups)], axis=0
    )
    mask = (row_alive[:, None, :] * k_alive[None, :, :]).reshape(groups * size, hidden)
    for part in range(parts):
        made = []
        for kind in range(4):
            at = (kind * parts + part) * hidden
            made.append(dot(stacked, wide_ref[:, at : at + hidden]))
        for side in range(2):
            value = mask * sigmoid(made[2 * side + 1]) * made[2 * side]
            laid[side, :, part * size : (part + 1) * size, :] = value.reshape(groups, size, hidden)
    for side in range(2):
        for g in range(groups):
            block = laid[side, g].T
            for a in range(parts):
                turned[side, pl.ds(g * parts + a, bands, stride=rows), :] = block[a * bands : (a + 1) * bands]
        start = 0
        for ref in out_refs[side]:
            count = ref.shape[1]
            value = turned[side, start * rows : (start + count) * rows].astype(jnp.bfloat16)
            ref[0] = value.reshape(count, rows, hidden)
            start += count


def alive_groups(chain_ref, start, rows, parts):
    lanes = chain_ref.shape[1]
    groups = rows // parts
    line = chain_ref[pl.ds(start // lanes, 1), :] >= 0
    row = lax.broadcasted_iota(jnp.int32, (groups, lanes), 1) - lax.rem(start, lanes)
    group = lax.broadcasted_iota(jnp.int32, (groups, lanes), 0)
    pick = jnp.logical_and(jnp.logical_and(row >= group * parts, row < (group + 1) * parts), line)
    fold = lax.rem(lax.broadcasted_iota(jnp.int32, (lanes, lanes), 0), parts) == lane_group(
        (lanes, lanes), lanes // parts
    )
    return dot(pick.astype(jnp.float32).astype(jnp.bfloat16), fold.astype(jnp.float32).astype(jnp.bfloat16))


def open_kernel(hidden, chunks, n_chan, n_sub, ids, blocks, pair_ref, chain_ref, w_ref, gate_ref, *rest):
    left_refs, right_refs = rest[:chunks], rest[chunks : 2 * chunks]
    wide, laid, turned = rest[2 * chunks :]
    slots = pl.num_programs(0)
    step = pl.program_id(0)
    _, rows, cols, channels = pair_ref.shape
    block = ids[0] * slots + step

    @pl.when(step == 0)
    def _():
        spread_weights(w_ref, wide, hidden, cols)

    normed = layer_norm(pair_ref[0].reshape(rows * cols, channels)).astype(jnp.bfloat16)
    gate = sigmoid(dot(normed, w_ref[0, :, 4 * hidden :]))
    gate_ref[0] = gate.reshape(rows, cols, channels)
    row_alive = alive_groups(chain_ref, (blocks[0, block] * n_chan + ids[1]) * rows, rows, hidden // cols)
    k_alive = alive_rows(chain_ref, (blocks[1, block] * n_sub + ids[2]) * cols, cols)
    taken = normed.reshape(rows, cols, channels)
    make_operands(taken, wide, row_alive, k_alive, (left_refs, right_refs), laid, turned)


def operand_scratch(rows, size, hidden):
    parts = hidden // size
    return [
        pltpu.VMEM((parts * hidden, 4 * parts * hidden), jnp.bfloat16),
        pltpu.VMEM((2, rows // parts, parts * size, hidden), jnp.float32),
        pltpu.VMEM((2, size * rows, hidden), jnp.float32),
    ]


def open_operands(ids, blocks, pair, chains, w_in, hidden, bands):
    slots, rows, cols, channels = pair.shape
    operands = [jax.ShapeDtypeStruct((slots, count, rows, hidden), jnp.bfloat16) for count in bands] * 2
    out = pl.pallas_call(
        functools.partial(open_kernel, hidden, len(bands), lax.axis_size("chan"), lax.axis_size("sub")),
        grid_spec=pltpu.PrefetchScalarGridSpec(
            num_scalar_prefetch=2,
            grid=(slots,),
            in_specs=[
                pl.BlockSpec((1, rows, cols, channels), lambda s, *_: (s, 0, 0, 0)),
                pl.BlockSpec(chains.shape, lambda s, *_: (0, 0)),
                pl.BlockSpec((1,) + w_in.shape[1:], lambda s, *_: (0, 0, 0)),
            ],
            out_specs=[pl.BlockSpec((1, rows, cols, channels), lambda s, *_: (s, 0, 0, 0))]
            + [pl.BlockSpec((1,) + o.shape[1:], lambda s, *_: (s, 0, 0, 0)) for o in operands],
            scratch_shapes=operand_scratch(rows, cols, hidden),
        ),
        out_shape=[jax.ShapeDtypeStruct(pair.shape, jnp.float32)] + operands,
        compiler_params=pltpu.CompilerParams(vmem_limit_bytes=vmem_limit),
        name="open_operands",
    )(ids, blocks, pair, chains, w_in)
    return out[0], out[1 : 1 + len(bands)], out[1 + len(bands) :]


def banded_kernel(shift, n_blk, slots_dev, terms, capacity, pieces, n_refs, size, ids, owners, slots, *rest):
    refs = rest[:n_refs]
    out_ref, left_held, right_held, chosen, sems = rest[n_refs:]
    step = pl.program_id(0)
    turn = lax.rem(step, 2)
    _, halves, bands, rows, hidden = left_held.shape
    cols = right_held.shape[3]
    parts = hidden // size

    @pl.when(step == 0)
    def _():
        target = lax.rem(ids[0] + shift, n_blk)
        for e in range(2 * capacity):
            chosen[e] = 0

        def scan(e, count):
            block, term = target * slots_dev + e // terms, lax.rem(e, terms)
            here = jnp.logical_and(owners[term, block] == ids[0], count < capacity)

            @pl.when(here)
            def _():
                chosen[2 * count] = slots[term, 0, block]
                chosen[2 * count + 1] = slots[term, 1, block]

            return count + here.astype(jnp.int32)

        lax.fori_loop(0, slots_dev * terms, scan, jnp.int32(0))

    def copy(n, term, buffer, source):
        side, half, *_ = pieces[n]
        held = (left_held, right_held)[side]
        return pltpu.make_async_copy(
            refs[source].at[chosen[2 * term + side]], held.at[buffer, half], sems.at[buffer, n]
        )

    def start(term, buffer):
        for n, (_, _, on, off) in enumerate(pieces):
            if on == off:
                copy(n, term, buffer, on).start()
            else:

                @pl.when(ids[3] == 1)
                def _(n=n, on=on):
                    copy(n, term, buffer, on).start()

                @pl.when(ids[3] == 0)
                def _(n=n, off=off):
                    copy(n, term, buffer, off).start()

    @pl.when(step == 0)
    def _():
        start(0, 0)

    @pl.when(step + 1 < capacity)
    def _():
        start(step + 1, 1 - turn)

    for n, piece in enumerate(pieces):
        copy(n, step, turn, piece[2]).wait()

    group = lax.rem(lane_group((cols, halves * hidden), size), parts)
    for band in range(bands):
        left = jnp.concatenate([left_held[turn, h, band] for h in range(halves)], axis=1)
        right = jnp.concatenate([right_held[turn, h, band] for h in range(halves)], axis=1)
        apart = jnp.concatenate(
            [jnp.where(group == part, right, jnp.zeros_like(right)) for part in range(parts)], axis=0
        )
        made = lax.dot_general(left, apart, (((1,), (1,)), ((), ())), preferred_element_type=jnp.float32)
        out_ref[0, band] = made.astype(jnp.bfloat16)


def banded_products(shift, ids, owners, slots, lefts, rights, capacity, slots_dev, terms, size):
    n_blk = lax.axis_size("blk")
    refs, pieces = [], []

    def index_of(array):
        for n, known in enumerate(refs):
            if known is array:
                return n
        refs.append(array)
        return len(refs) - 1

    for side, operands in ((0, lefts), (1, rights)):
        for half, (on, off) in enumerate(operands):
            pieces.append((side, half, index_of(on), index_of(off)))
    _, bands, rows, hidden = lefts[0][0].shape
    cols = rights[0][0].shape[2]
    return pl.pallas_call(
        functools.partial(
            banded_kernel, shift, n_blk, slots_dev, terms, capacity, tuple(pieces), len(refs), size
        ),
        grid_spec=pltpu.PrefetchScalarGridSpec(
            num_scalar_prefetch=3,
            grid=(capacity,),
            in_specs=[pl.BlockSpec(memory_space=pl.ANY)] * len(refs),
            out_specs=pl.BlockSpec((1, bands, rows, hidden), lambda t, *_: (t, 0, 0, 0)),
            scratch_shapes=[
                pltpu.VMEM((2, len(lefts), bands, rows, hidden), jnp.bfloat16),
                pltpu.VMEM((2, len(rights), bands, cols, hidden), jnp.bfloat16),
                pltpu.SMEM((2 * capacity,), jnp.int32),
                pltpu.SemaphoreType.DMA((2, len(pieces))),
            ],
        ),
        out_shape=jax.ShapeDtypeStruct((capacity, bands, rows, hidden), jnp.bfloat16),
        compiler_params=pltpu.CompilerParams(vmem_limit_bytes=vmem_limit),
        cost_estimate=pl.CostEstimate(
            flops=2 * capacity * bands * rows * hidden * hidden * len(lefts) * 50,
            bytes_accessed=capacity * bands * rows * hidden * 2 * 5,
            transcendentals=0,
        ),
        name="banded_products",
    )(ids, owners, slots, *refs)


def close_kernel(last, n_parts, n_blk, n_chan, n_sub, slots_dev, terms, capacity, ids, blocks, owners, *rest):
    chunks = n_parts // n_blk
    arrived, rest = rest[:n_parts], rest[n_parts:]
    cur_ref, gate_ref, w_out_ref = rest[:3]
    if last:
        out_ref, held, summed, wide_out, place, seen, sems = rest[3:]
    else:
        chain_ref, w_ref, out_ref, next_gate_ref = rest[3:7]
        left_refs, right_refs = rest[7 : 7 + chunks], rest[7 + chunks : 7 + 2 * chunks]
        held, summed, wide_out, place, seen, sems, norm_ref, wide, laid, turned = rest[7 + 2 * chunks :]
    step = pl.program_id(0)
    _, rows, cols, channels = cur_ref.shape
    _, bands, _, hidden = held.shape
    parts, size = hidden // bands, bands

    def arrival(n):
        at = sum(arrived[m * n_blk].shape[1] for m in range(n // n_blk))
        count = arrived[n].shape[1]
        target = held.at[pl.ds(n % n_blk * capacity, capacity), pl.ds(at, count)]
        return pltpu.make_async_copy(arrived[n], target, sems.at[n])

    @pl.when(step == 0)
    def _():
        for n in range(n_parts):
            arrival(n).start()
        for shift in range(n_blk):
            seen[shift] = 0

        def scan(e, carry):
            owner = owners[lax.rem(e, terms), ids[0] * slots_dev + e // terms]
            shift = lax.rem(ids[0] - owner + n_blk, n_blk)
            count = seen[owner]
            seen[owner] = count + 1
            place[e] = shift * capacity + count
            return carry

        lax.fori_loop(0, slots_dev * terms, scan, jnp.int32(0))
        wide_out[...] = jnp.zeros_like(wide_out)
        for part in range(parts):
            for a in range(parts):
                at = (part * parts + a) * bands
                wide_out[at : at + bands, a * channels : (a + 1) * channels] = w_out_ref[
                    0, part * bands : (part + 1) * bands, :
                ]
        if not last:
            spread_weights(w_ref, wide, hidden, rows)
        for n in range(n_parts):
            arrival(n).wait()

    span = 4
    for band in range(0, bands, span):
        taken = pl.ds(band, span)
        total = held[place[step * terms], taken].astype(jnp.float32)
        for t in range(1, terms):
            total = total + held[place[step * terms + t], taken].astype(jnp.float32)
        rounded = total.astype(jnp.bfloat16).astype(jnp.float32)
        summed[pl.ds(band * rows, span * rows), :] = rounded.reshape(span * rows, hidden)
    groups = rows // parts
    pieces = []
    for g in range(groups):
        block = jnp.concatenate([summed[pl.ds(g * parts + a, bands, stride=rows), :] for a in range(parts)]).T
        pieces.append(jnp.concatenate([block[p * cols : (p + 1) * cols] for p in range(parts)], axis=1))
    mixture = jnp.concatenate(pieces)
    together = (lane_group((hidden, hidden), size) == lax.broadcasted_iota(jnp.int32, (hidden, hidden), 0) // size)
    together = together.astype(jnp.float32).astype(jnp.bfloat16)
    average = dot(mixture.astype(jnp.bfloat16), jnp.concatenate([together] * parts)) * (1.0 / hidden)
    centred = [mixture[:, p * hidden : (p + 1) * hidden] - average for p in range(parts)]
    squares = sum(c * c for c in centred)
    high = squares.astype(jnp.bfloat16)
    low = (squares - high.astype(jnp.float32)).astype(jnp.bfloat16)
    variance = dot(jnp.concatenate([high, low], axis=1), jnp.concatenate([together] * 2)) * (1.0 / hidden)
    scale = lax.rsqrt(variance + norm_epsilon)
    normed = jnp.concatenate([(c * scale).astype(jnp.bfloat16) for c in centred], axis=1)
    update = dot(normed, wide_out[...])
    for g in range(groups):
        taken = pl.ds(g * parts, parts)
        change = jnp.concatenate(
            [update[g * cols : (g + 1) * cols, a * channels : (a + 1) * channels] for a in range(parts)]
        )
        gate = gate_ref[0, taken].reshape(parts * cols, channels)
        current = cur_ref[0, taken].astype(jnp.float32).reshape(parts * cols, channels)
        result = (current + gate * change).astype(jnp.bfloat16)
        out_ref[0, taken] = result.reshape(parts, cols, channels)
        if not last:
            norm = layer_norm(result)
            norm_ref[pl.ds(g * parts * cols, parts * cols), :] = norm
            next_gate = sigmoid(dot(norm.astype(jnp.bfloat16), w_ref[0, :, 4 * hidden :]))
            next_gate_ref[0, taken] = next_gate.reshape(parts, cols, channels)
    if not last:
        block = ids[0] * slots_dev + step
        k_alive = alive_rows(chain_ref, (blocks[0, block] * n_chan + ids[1]) * rows, rows)
        col_alive = alive_groups(chain_ref, (blocks[1, block] * n_sub + ids[2]) * cols, cols, parts)
        taken = jnp.stack([norm_ref[pl.ds(col, rows, stride=cols), :].astype(jnp.bfloat16) for col in range(cols)])
        make_operands(taken, wide, col_alive, k_alive, (left_refs, right_refs), laid, turned)


def close_layer(layer, arrived, ids, blocks, owners, current, gate, w_out, capacity, terms, chains, w_in, last, bands):
    n_blk = len(arrived[0])
    flat = [part for chunk in arrived for part in chunk]
    slots, rows, cols, channels = current.shape
    hidden = w_out.shape[1]
    whole = pl.BlockSpec((1, rows, cols, channels), lambda s, *_: (s, 0, 0, 0))

    def layer_spec(array, index):
        return pl.BlockSpec((1,) + array.shape[1:], lambda s, *_: (index, 0, 0))

    in_specs = [pl.BlockSpec(memory_space=pl.ANY)] * len(flat) + [whole, whole, layer_spec(w_out, layer)]
    operands = [*flat, current, gate, w_out]
    out_shape = [jax.ShapeDtypeStruct(current.shape, jnp.bfloat16)]
    out_specs = [whole]
    scratch = [
        pltpu.VMEM((n_blk * capacity, sum(bands), rows, hidden), jnp.bfloat16),
        pltpu.VMEM((sum(bands) * rows, hidden), jnp.float32),
        pltpu.VMEM((hidden // cols * hidden, hidden // cols * channels), jnp.bfloat16),
        pltpu.SMEM((slots * terms,), jnp.int32),
        pltpu.SMEM((n_blk,), jnp.int32),
        pltpu.SemaphoreType.DMA((len(flat),)),
    ]
    if not last:
        operands += [chains, w_in]
        in_specs += [pl.BlockSpec(chains.shape, lambda s, *_: (0, 0)), layer_spec(w_in, layer + 1)]
        made = [jax.ShapeDtypeStruct((slots, count, cols, hidden), jnp.bfloat16) for count in bands] * 2
        out_shape += [jax.ShapeDtypeStruct(current.shape, jnp.float32)] + made
        out_specs += [whole] + [pl.BlockSpec((1,) + o.shape[1:], lambda s, *_: (s, 0, 0, 0)) for o in made]
        scratch += [pltpu.VMEM((rows * cols, channels), jnp.float32)] + operand_scratch(cols, rows, hidden)
    out = pl.pallas_call(
        functools.partial(
            close_kernel, last, len(flat), n_blk, lax.axis_size("chan"), lax.axis_size("sub"), slots, terms, capacity
        ),
        grid_spec=pltpu.PrefetchScalarGridSpec(
            num_scalar_prefetch=3, grid=(slots,), in_specs=in_specs, out_specs=out_specs, scratch_shapes=scratch
        ),
        out_shape=out_shape,
        compiler_params=pltpu.CompilerParams(vmem_limit_bytes=vmem_limit),
        name="close_layer",
    )(ids, blocks, owners, *operands)
    if last:
        return out[0]
    return out[0], out[1], out[2 : 2 + len(bands)], out[2 + len(bands) :]


def after(value, *others):
    return lax.optimization_barrier((value, *others))[0]


def exchange_bands_outgoing(lefts, rights):
    both = ("chan", "sub")
    made = []
    for left, right in zip(lefts, rights):
        if made:
            (_, other_left), *_ = made[-1][0]
            _, (_, two) = made[-1][1]
            right = after(right, two)
        other_left = lax.ppermute(left, "sub", [(0, 1), (1, 0)])
        one = lax.ppermute(right, both, [(0, 2), (3, 1), (1, 0), (2, 3)])
        two = lax.ppermute(right, both, [(1, 2), (2, 1)])
        made.append(([(other_left, left), (left, other_left)], [(one, one), (right, two)]))
    return made


def exchange_bands_incoming(lefts, rights):
    both = ("chan", "sub")
    made = []
    for left, right in zip(lefts, rights):
        if made:
            right, left = lax.optimization_barrier((right, left, made[-1][1][1][0]))[:2]
        one = lax.ppermute(left, both, [(1, 3), (2, 0), (0, 1), (3, 2)])
        two = lax.ppermute(one, both, [(0, 1), (3, 2)])
        other = lax.ppermute(right, "chan", [(0, 1), (1, 0)])
        made.append(([(left, one), (one, two)], [(right, right), (other, other)]))
    return made


def banded(pair, ids, blocks, owners, slot_of, chains, w_in, w_out, capacity, terms, n_blk):
    slots, rows, cols, channels = pair.shape
    hidden = w_out.shape[1]
    shifts = [n_blk // 2] + [s for s in range(1, n_blk) if s != n_blk // 2] + [0]
    layers = w_in.shape[0]
    current = pair
    for layer in range(layers):
        bands = [cols // 2, cols // 2]
        if layer == 0:
            gate, lefts, rights = open_operands(ids, blocks, pair, chains, w_in, hidden, bands)
        exchange = exchange_bands_incoming if layer % 2 else exchange_bands_outgoing
        arrived = []
        for left, right in exchange(lefts, rights):
            parts = [None] * n_blk
            for shift in shifts:
                made = banded_products(shift, ids, owners, slot_of, left, right, capacity, slots, terms, cols)
                if shift:
                    made = lax.ppermute(made, "blk", [(p, (p + shift) % n_blk) for p in range(n_blk)])
                parts[shift] = made
            arrived.append(parts)
        last = layer == layers - 1
        out = close_layer(
            layer, arrived, ids, blocks, owners, current, gate, w_out, capacity, terms, chains, w_in, last, bands
        )
        if last:
            return out
        current, gate, lefts, rights = out


def per_device(pair, block_list, term_owner, term_slots, chain_ids, w_in, w_out):
    n_blk = lax.axis_size("blk")
    n_chan = lax.axis_size("chan")
    n_sub = lax.axis_size("sub")
    position = lax.axis_index("blk")
    row_group = lax.axis_index("chan")
    col_group = lax.axis_index("sub")
    slots, rows, cols, channels = pair.shape
    hidden = w_out.shape[1]
    terms = term_owner.shape[1]
    capacity = max(2, -(-slots * terms // n_blk))
    fast = n_chan == 2 and n_sub == 2
    on_diagonal = (row_group == col_group).astype(jnp.int32)
    ids = jnp.stack([position, row_group, col_group, on_diagonal]).astype(jnp.int32)
    blocks = block_list.T
    owners = term_owner.T
    slot_of = jnp.transpose(term_slots, (1, 2, 0))
    chains = chain_ids.reshape(-1, 128)
    if fast and rows == cols and channels == hidden == 128 and hidden % cols == 0:
        return banded(pair, ids, blocks, owners, slot_of, chains, w_in, w_out, capacity, terms, n_blk)
    shifts = [n_blk // 2] + [s for s in range(1, n_blk) if s != n_blk // 2] + [0]

    def all_products(lefts, right):
        parts = [None] * n_blk
        for shift in shifts:
            made = term_products(shift, ids, owners, slot_of, lefts, right, capacity, slots, terms)
            if shift:
                pairs = [(p, (p + shift) % n_blk) for p in range(n_blk)]
                made = lax.ppermute(made, "blk", pairs)
            parts[shift] = made
        return parts

    def at_home(layer, parts, current, gate, at, of, into=None):
        last = layer == w_in.shape[0] - 1
        return home(
            layer, parts, ids, blocks, owners, current, gate, w_out, capacity, terms, at, of, chains, w_in, last, into
        )

    gate, left, *rights = first_operands(ids, blocks, pair, chains, w_in, hidden, 2 if fast else 1)
    lefts, chunks = exchange_outgoing(left, rights, n_chan, n_sub)
    count = len(chunks)
    made = [all_products(lefts, right) for right in chunks]
    homes = [at_home(0, parts, pair, gate, at, count) for at, parts in enumerate(made)]
    lefts, chunks = exchange_incoming([h[2] for h in homes], [h[3] for h in homes], n_chan, n_sub)
    made = [all_products(lefts, right) for right in chunks]
    out = None
    for at, parts in enumerate(made):
        (out,) = at_home(1, parts, homes[at][0], homes[at][1], at, count, into=out)
    return out


def solution(mesh):
    in_specs = (
        P(("groups", "blk"), "chan", "sub", None),
        P("groups", None),
        P("groups", None),
        P("groups", None, None),
        P("groups"),
        P(),
        P(),
    )
    out_specs = P(("groups", "blk"), "chan", "sub", None)
    return jax.shard_map(
        per_device, mesh=mesh, in_specs=in_specs, out_specs=out_specs, check_vma=False
    )
```

```python
import functools

import jax
import jax.numpy as jnp
from jax import lax
from jax.experimental import pallas as pl
from jax.experimental.pallas import tpu as pltpu
from jax.sharding import PartitionSpec as P

norm_epsilon = 1e-05
vmem_limit = 56 * 1024 * 1024


def sigmoid(values):
    return 0.5 + 0.5 * jnp.tanh(0.5 * values)


def layer_norm(values):
    values = values.astype(jnp.float32)
    centred = values - jnp.mean(values, axis=-1, keepdims=True)
    variance = jnp.mean(centred * centred, axis=-1, keepdims=True)
    return centred * lax.rsqrt(variance + norm_epsilon)


def alive_rows(chain_ref, start, size):
    lanes = chain_ref.shape[1]
    line = chain_ref[pl.ds(start // lanes, 1), :] >= 0
    spot = lax.broadcasted_iota(jnp.int32, (size, lanes), 0) + lax.rem(start, lanes)
    pick = jnp.logical_and(lax.broadcasted_iota(jnp.int32, (size, lanes), 1) == spot, line)
    return dot(pick.astype(jnp.float32).astype(jnp.bfloat16), jnp.ones((lanes, lanes), jnp.bfloat16))


def dot(a, b):
    return jnp.dot(a, b, preferred_element_type=jnp.float32)


def gated_pair(projected, mask, hidden):
    left = mask * sigmoid(projected[:, hidden : 2 * hidden]) * projected[:, :hidden]
    right = mask * sigmoid(projected[:, 3 * hidden : 4 * hidden]) * projected[:, 2 * hidden : 3 * hidden]
    return left.astype(jnp.bfloat16), right.astype(jnp.bfloat16)


def first_kernel(hidden, row_parts, n_chan, n_sub, ids, blocks, pair_ref, chain_ref, w_ref, gate_ref, left_ref, *rest):
    right_refs, (norm_ref, turned_ref) = rest[:row_parts], rest[row_parts:]
    slots = pl.num_programs(0)
    _, rows, cols, channels = pair_ref.shape
    block = ids[0] * slots + pl.program_id(0)
    row_alive = alive_rows(chain_ref, (blocks[0, block] * n_chan + ids[1]) * rows, rows)
    col_alive = alive_rows(chain_ref, (blocks[1, block] * n_sub + ids[2]) * cols, cols)
    group = max(1, 256 // cols)
    for start in range(0, rows, group):
        at = pl.ds(start, group)
        normed = layer_norm(pair_ref[0, at].reshape(group * cols, channels))
        norm_ref[pl.ds(start * cols, group * cols), :] = normed
        gate = sigmoid(dot(normed.astype(jnp.bfloat16), w_ref[0, :, 4 * hidden :]))
        gate_ref[0, at] = gate.reshape(group, cols, channels)
    for col in range(cols):
        turned_ref[col] = norm_ref[pl.ds(col, rows, stride=cols), :].astype(jnp.bfloat16)
    step = max(1, 128 // rows)
    part = rows // row_parts
    for start in range(0, cols, step):
        taken = turned_ref[start : start + step].reshape(step * rows, channels)
        projected = dot(taken, w_ref[0, :, : 4 * hidden])
        mask = col_alive[start : start + step][:, None, :] * row_alive[None, :, :]
        left, right = gated_pair(projected, mask.reshape(step * rows, -1), hidden)
        left_ref[0, start : start + step] = left.reshape(step, rows, hidden)
        right = right.reshape(step, rows, hidden)
        for p, right_ref in enumerate(right_refs):
            right_ref[0, start : start + step] = right[:, p * part : (p + 1) * part]


def first_operands(ids, blocks, pair, chains, w_in, hidden, row_parts):
    slots, rows, cols, channels = pair.shape
    part = rows // row_parts
    operand = jax.ShapeDtypeStruct((slots, cols, rows, hidden), jnp.bfloat16)
    right = jax.ShapeDtypeStruct((slots, cols, part, hidden), jnp.bfloat16)
    return pl.pallas_call(
        functools.partial(first_kernel, hidden, row_parts, lax.axis_size("chan"), lax.axis_size("sub")),
        grid_spec=pltpu.PrefetchScalarGridSpec(
            num_scalar_prefetch=2,
            grid=(slots,),
            in_specs=[
                pl.BlockSpec((1, rows, cols, channels), lambda s, *_: (s, 0, 0, 0)),
                pl.BlockSpec(chains.shape, lambda s, *_: (0, 0)),
                pl.BlockSpec((1,) + w_in.shape[1:], lambda s, *_: (0, 0, 0)),
            ],
            out_specs=[
                pl.BlockSpec((1, rows, cols, channels), lambda s, *_: (s, 0, 0, 0)),
                pl.BlockSpec((1, cols, rows, hidden), lambda s, *_: (s, 0, 0, 0)),
            ]
            + [pl.BlockSpec((1, cols, part, hidden), lambda s, *_: (s, 0, 0, 0))] * row_parts,
            scratch_shapes=[
                pltpu.VMEM((rows * cols, channels), jnp.float32),
                pltpu.VMEM((cols, rows, channels), jnp.bfloat16),
            ],
        ),
        out_shape=[jax.ShapeDtypeStruct(pair.shape, jnp.float32), operand] + [right] * row_parts,
        compiler_params=pltpu.CompilerParams(vmem_limit_bytes=vmem_limit),
        name="first_operands",
    )(ids, blocks, pair, chains, w_in)


def product_kernel(shift, n_blk, slots_dev, terms, capacity, pieces, n_refs, ids, owners, slots, *rest):
    refs = rest[:n_refs]
    out_ref, left_held, right_held, right_wide, chosen, sems = rest[n_refs:]
    step = pl.program_id(0)
    turn = lax.rem(step, 2)
    _, depth, n_i, hidden = left_held.shape
    n_j = right_wide.shape[1]

    @pl.when(step == 0)
    def _():
        target = lax.rem(ids[0] + shift, n_blk)
        for e in range(2 * capacity):
            chosen[e] = 0

        def scan(e, count):
            block, term = target * slots_dev + e // terms, lax.rem(e, terms)
            here = jnp.logical_and(owners[term, block] == ids[0], count < capacity)

            @pl.when(here)
            def _():
                chosen[2 * count] = slots[term, 0, block]
                chosen[2 * count + 1] = slots[term, 1, block]

            return count + here.astype(jnp.int32)

        lax.fori_loop(0, slots_dev * terms, scan, jnp.int32(0))

    def copy(n, term, buffer, source):
        side, _, _, k0, depth_of, i0, size = pieces[n]
        held = (left_held, right_held)[side]
        return pltpu.make_async_copy(
            refs[source].at[chosen[2 * term + side]],
            held.at[buffer, pl.ds(k0, depth_of), pl.ds(i0, size), :],
            sems.at[buffer, n],
        )

    def start(term, buffer):
        for n, (_, on, off, *_) in enumerate(pieces):
            if on == off:
                copy(n, term, buffer, on).start()
            else:

                @pl.when(ids[3] == 1)
                def _(n=n, on=on):
                    copy(n, term, buffer, on).start()

                @pl.when(ids[3] == 0)
                def _(n=n, off=off):
                    copy(n, term, buffer, off).start()

    @pl.when(step == 0)
    def _():
        start(0, 0)

    @pl.when(step + 1 < capacity)
    def _():
        start(step + 1, 1 - turn)

    for n, piece in enumerate(pieces):
        copy(n, step, turn, piece[1]).wait()

    span = 8

    def widen(n, carry):
        at = pl.ds(n * span, span)
        right_wide[at] = right_held[turn, at].astype(jnp.float32)
        return carry

    lax.fori_loop(0, depth // span, widen, 0)

    group = min(8, n_j)
    unroll = 4
    for j0 in range(0, n_j, group):

        def body(n, sums):
            for u in range(unroll):
                k = n * unroll + u
                left = left_held[turn, k].astype(jnp.float32).reshape(n_i // 8, 8, hidden)
                sums = tuple(
                    total + left * right_wide[k, pl.ds(j0 + j, 8, stride=0), :][None]
                    for j, total in enumerate(sums)
                )
            return sums

        zero = jnp.zeros((n_i // 8, 8, hidden), jnp.float32)
        sums = lax.fori_loop(0, depth // unroll, body, (zero,) * group)
        for j, total in enumerate(sums):
            out_ref[0, j0 + j] = total.reshape(n_i, hidden).astype(jnp.bfloat16)


def term_products(shift, ids, owners, slots, lefts, rights, capacity, slots_dev, terms):
    n_blk = lax.axis_size("blk")
    refs, pieces = [], []

    def index_of(array):
        for n, known in enumerate(refs):
            if known is array:
                return n
        refs.append(array)
        return len(refs) - 1

    for side, operands in ((0, lefts), (1, rights)):
        for on, off, k0, i0 in operands:
            pieces.append((side, index_of(on), index_of(off), k0, on.shape[1], i0, on.shape[2]))
    hidden = lefts[0][0].shape[3]
    n_i = max(p[5] + p[6] for p in pieces if p[0] == 0)
    n_j = max(p[5] + p[6] for p in pieces if p[0] == 1)
    depth = max(p[3] + p[4] for p in pieces)
    return pl.pallas_call(
        functools.partial(
            product_kernel, shift, n_blk, slots_dev, terms, capacity, tuple(pieces), len(refs)
        ),
        grid_spec=pltpu.PrefetchScalarGridSpec(
            num_scalar_prefetch=3,
            grid=(capacity,),
            in_specs=[pl.BlockSpec(memory_space=pl.ANY)] * len(refs),
            out_specs=pl.BlockSpec((1, n_j, n_i, hidden), lambda t, *_: (t, 0, 0, 0)),
            scratch_shapes=[
                pltpu.VMEM((2, depth, n_i, hidden), jnp.bfloat16),
                pltpu.VMEM((2, depth, n_j, hidden), jnp.bfloat16),
                pltpu.VMEM((depth, n_j, hidden), jnp.float32),
                pltpu.SMEM((2 * capacity,), jnp.int32),
                pltpu.SemaphoreType.DMA((2, len(pieces))),
            ],
        ),
        out_shape=jax.ShapeDtypeStruct((capacity, n_j, n_i, hidden), jnp.bfloat16),
        compiler_params=pltpu.CompilerParams(vmem_limit_bytes=vmem_limit),
        cost_estimate=pl.CostEstimate(
            flops=2 * capacity * n_i * n_j * depth * hidden * 100,
            bytes_accessed=capacity * (depth * (n_i + n_j) + n_i * n_j) * hidden * 2,
            transcendentals=0,
        ),
        name="term_products",
    )(ids, owners, slots, *refs)


def home_kernel(last, hidden, n_blk, n_chan, n_sub, at, of, slots_dev, terms, capacity, ids, blocks, owners, *rest):
    parts, rest = rest[:n_blk], rest[n_blk:]
    scratch, rest = rest[-5:], rest[:-5]
    held, turned, place, seen, sems = scratch
    cur_ref, gate_ref, w_out_ref = rest[:3]
    if last:
        out_ref = rest[-1]
    else:
        chain_ref, w_ref, out_ref, next_gate_ref, left_ref, right_ref = rest[3:]
    step = pl.program_id(0)
    _, rows, cols, channels = cur_ref.shape

    def arrival(shift):
        return pltpu.make_async_copy(parts[shift], held.at[pl.ds(shift * capacity, capacity)], sems.at[shift])

    @pl.when(step == 0)
    def _():
        for shift in range(n_blk):
            arrival(shift).start()
            seen[shift] = 0

        def scan(e, carry):
            owner = owners[lax.rem(e, terms), ids[0] * slots_dev + e // terms]
            shift = lax.rem(ids[0] - owner + n_blk, n_blk)
            count = seen[owner]
            seen[owner] = count + 1
            place[e] = shift * capacity + count
            return carry

        lax.fori_loop(0, slots_dev * terms, scan, jnp.int32(0))
        for shift in range(n_blk):
            arrival(shift).wait()

    if not last:
        block = ids[0] * slots_dev + step
        row_alive = alive_rows(chain_ref, (blocks[0, block] * n_chan + ids[1]) * rows, rows)
        col_alive = alive_rows(chain_ref, ((blocks[1, block] * n_sub + ids[2]) * of + at) * cols, cols)
    span = max(1, 128 // rows)
    for start in range(0, cols, span):
        taken = pl.ds(start, span)
        total = held[place[step * terms], taken].astype(jnp.float32)
        for t in range(1, terms):
            total = total + held[place[step * terms + t], taken].astype(jnp.float32)
        rounded = total.astype(jnp.bfloat16).astype(jnp.float32)
        turned[pl.ds(start * rows, span * rows), :] = rounded.reshape(span * rows, hidden)
    group = min(rows, max(1, 256 // cols))
    for start in range(0, rows, group):
        taken = pl.ds(start, group)
        mixture = jnp.concatenate(
            [turned[pl.ds(row, cols, stride=rows), :].astype(jnp.bfloat16) for row in range(start, start + group)]
        )
        update = dot(layer_norm(mixture).astype(jnp.bfloat16), w_out_ref[0])
        current = cur_ref[0, taken].astype(jnp.float32).reshape(group * cols, channels)
        gate = gate_ref[0, taken].reshape(group * cols, channels)
        result = (current + gate * update).astype(jnp.bfloat16)
        out_ref[0, taken] = result.reshape(group, cols, channels)
        if not last:
            normed = layer_norm(result).astype(jnp.bfloat16)
            projected = dot(normed, w_ref[0])
            next_gate_ref[0, taken] = sigmoid(projected[:, 4 * hidden :]).reshape(group, cols, channels)
            mask = row_alive[start : start + group][:, None, :] * col_alive[None, :, :]
            left, right = gated_pair(projected, mask.reshape(group * cols, channels), hidden)
            left_ref[0, taken] = left.reshape(group, cols, hidden)
            right_ref[0, taken] = right.reshape(group, cols, hidden)


def home(layer, parts, ids, blocks, owners, current, gate, w_out, capacity, terms, at, of, chains, w_in, last, into=None):
    n_blk = len(parts)
    slots, rows, _, channels = current.shape
    hidden = w_out.shape[1]
    cols = parts[0].shape[1]
    chunk = (1, rows, cols, channels)

    def chunk_spec(array):
        whole = array.shape[2] != cols
        return pl.BlockSpec(chunk, lambda s, *_: (s, 0, at if whole else 0, 0))

    def layer_spec(array, index):
        return pl.BlockSpec((1,) + array.shape[1:], lambda s, *_: (index, 0, 0))

    in_specs = [pl.BlockSpec(memory_space=pl.ANY)] * n_blk + [
        chunk_spec(current),
        chunk_spec(gate),
        layer_spec(w_out, layer),
    ]
    operands = [*parts, current, gate, w_out]
    aliases = {}
    if last:
        if into is not None:
            aliases = {3 + len(operands): 0}
            operands.append(into)
            in_specs.append(pl.BlockSpec(memory_space=pl.ANY))
        out_shape = [jax.ShapeDtypeStruct((slots, rows, cols * of, channels), jnp.bfloat16)]
        out_specs = [pl.BlockSpec(chunk, lambda s, *_: (s, 0, at, 0))]
    else:
        operands += [chains, w_in]
        in_specs += [pl.BlockSpec(chains.shape, lambda s, *_: (0, 0)), layer_spec(w_in, layer + 1)]
        small = (slots, rows, cols, channels)
        out_shape = [jax.ShapeDtypeStruct(small, t) for t in (jnp.bfloat16, jnp.float32, jnp.bfloat16, jnp.bfloat16)]
        out_specs = [pl.BlockSpec(chunk, lambda s, *_: (s, 0, 0, 0))] * 4
    return pl.pallas_call(
        functools.partial(
            home_kernel, last, hidden, n_blk, lax.axis_size("chan"), lax.axis_size("sub"), at, of, slots, terms, capacity
        ),
        grid_spec=pltpu.PrefetchScalarGridSpec(
            num_scalar_prefetch=3,
            grid=(slots,),
            in_specs=in_specs,
            out_specs=out_specs,
            scratch_shapes=[
                pltpu.VMEM((n_blk * capacity, cols, rows, hidden), jnp.bfloat16),
                pltpu.VMEM((rows * cols, hidden), jnp.float32),
                pltpu.SMEM((slots * terms,), jnp.int32),
                pltpu.SMEM((n_blk,), jnp.int32),
                pltpu.SemaphoreType.DMA((n_blk,)),
            ],
        ),
        out_shape=out_shape,
        input_output_aliases=aliases,
        compiler_params=pltpu.CompilerParams(vmem_limit_bytes=vmem_limit),
        cost_estimate=pl.CostEstimate(
            flops=2 * slots * rows * cols * channels * 6 * channels * 10,
            bytes_accessed=slots * rows * cols * channels * 16,
            transcendentals=0,
        ),
        name="home",
    )(ids, blocks, owners, *operands)


def exchange_outgoing(left, rights, n_chan, n_sub):
    if n_chan == 2 and n_sub == 2:
        both = ("chan", "sub")
        other_left = lax.ppermute(left, "sub", [(0, 1), (1, 0)])
        lefts = [(other_left, left, 0, 0), (left, other_left, left.shape[1], 0)]
        chunks = []
        for right in rights:
            if chunks:
                (one, *_), (_, two, *_) = chunks[-1]
                right, *_ = lax.optimization_barrier((right, one, two))
            one = lax.ppermute(right, both, [(0, 2), (3, 1), (1, 0), (2, 3)])
            two = lax.ppermute(right, both, [(1, 2), (2, 1)])
            chunks.append([(one, one, 0, 0), (right, two, right.shape[1], 0)])
        return lefts, chunks
    left = lax.all_gather(left, "sub", axis=1, tiled=True)
    right = jnp.concatenate(rights, axis=2)
    right = lax.all_gather(right, "chan", axis=2, tiled=True)
    right = lax.all_to_all(right, "sub", split_axis=2, concat_axis=1, tiled=True)
    cols = right.shape[2] // 2
    chunks = [right[:, :, :cols], right[:, :, cols:]]
    return [(left, left, 0, 0)], [[(r, r, 0, 0)] for r in chunks]


def exchange_incoming(lefts, rights, n_chan, n_sub):
    if n_chan == 2 and n_sub == 2:
        both = ("chan", "sub")
        left_pieces, chunks = [], []
        at = 0
        for left, right in zip(lefts, rights):
            depth = left.shape[1]
            one = lax.ppermute(left, both, [(1, 3), (2, 0), (0, 1), (3, 2)])
            two = lax.ppermute(one, both, [(0, 1), (3, 2)])
            left_pieces += [(left, one, 0, at), (one, two, depth, at)]
            other = lax.ppermute(right, "chan", [(0, 1), (1, 0)])
            chunks.append([(right, right, 0, 0), (other, other, depth, 0)])
            at += left.shape[2]
        return left_pieces, chunks
    left = lax.all_gather(jnp.concatenate(lefts, axis=2), "chan", axis=1, tiled=True)
    left = lax.all_gather(left, "sub", axis=2, tiled=True)
    size = left.shape[2] // n_chan
    left = lax.dynamic_slice_in_dim(left, lax.axis_index("chan") * size, size, 2)
    gathered = [lax.all_gather(right, "chan", axis=1, tiled=True) for right in rights]
    return [(left, left, 0, 0)], [[(r, r, 0, 0)] for r in gathered]


def lane_group(shape, size):
    return lax.broadcasted_iota(jnp.int32, shape, 1) // size


def spread_weights(w_ref, wide_ref, hidden, size):
    parts = hidden // size
    for side in range(2):
        for kind in range(2):
            start = (2 * side + kind) * hidden
            weights = w_ref[0, :, start : start + hidden].astype(jnp.float32)
            group = lane_group(weights.shape, size)
            for part in range(parts):
                kept = jnp.where(group == part, weights, 0.0)
                at = ((side * parts + part) * 2 + kind) * hidden
                for a in range(parts):
                    moved = pltpu.roll(kept, ((a - part) % parts) * size, 1) if a != part else kept
                    wide_ref[a * hidden : (a + 1) * hidden, at : at + hidden] = moved.astype(jnp.bfloat16)


def swap_matrix(half):
    shape = (half * half, half * half)
    to, of = lax.broadcasted_iota(jnp.int32, shape, 0), lax.broadcasted_iota(jnp.int32, shape, 1)
    same = jnp.logical_and(to // half == lax.rem(of, half), lax.rem(to, half) == of // half)
    return same.astype(jnp.float32).astype(jnp.bfloat16)


def swapped(values, swap_ref):
    half, _, lanes = values.shape
    moved = dot(swap_ref[...], values.reshape(half * half, lanes))
    return moved.astype(jnp.bfloat16).reshape(half, half, lanes)


def turn(taken, turned, swap_ref):
    half = 16
    for x in range(0, taken.shape[0], half):
        for y in range(0, taken.shape[1], half):
            turned[y : y + half, x : x + half] = swapped(taken[x : x + half, y : y + half], swap_ref)


def make_operand(side, taken, row_alive, inner_alive, wide_ref, out_refs, laid, swap_ref):
    rows, size, hidden = taken.shape
    parts, bands, half = hidden // size, size, 16
    groups = rows // parts
    stacked = jnp.concatenate(
        [jnp.concatenate([taken[g * parts + a] for a in range(parts)], axis=1) for g in range(groups)], axis=0
    )
    mask = (row_alive[:, None, :] * inner_alive[None, :, :]).reshape(groups * size, hidden)
    for part in range(parts):
        at = (side * parts + part) * 2 * hidden
        made = dot(stacked, wide_ref[:, at : at + 2 * hidden])
        value = mask * sigmoid(made[:, hidden:]) * made[:, :hidden]
        laid[side, :, part * size : (part + 1) * size, :] = value.astype(jnp.bfloat16).reshape(groups, size, hidden)
    blocks = [laid[side, g].T for g in range(groups)]
    starts = [sum(ref.shape[1] for ref in out_refs[:n]) for n in range(len(out_refs))]
    for first in range(0, bands, half):
        for row in range(0, rows, half):
            tiles = []
            for r in range(row, row + half):
                at = r % parts * bands + first
                tiles.append(blocks[r // parts][at : at + half])
            moved = swapped(jnp.stack(tiles), swap_ref)
            for start, ref in zip(starts, out_refs):
                low, high = max(start, first), min(start + ref.shape[1], first + half)
                if low < high:
                    ref[0, low - start : high - start, row : row + half] = moved[low - first : high - first]


def alive_groups(chain_ref, start, rows, parts):
    lanes = chain_ref.shape[1]
    groups = rows // parts
    line = chain_ref[pl.ds(start // lanes, 1), :] >= 0
    row = lax.broadcasted_iota(jnp.int32, (groups, lanes), 1) - lax.rem(start, lanes)
    group = lax.broadcasted_iota(jnp.int32, (groups, lanes), 0)
    pick = jnp.logical_and(jnp.logical_and(row >= group * parts, row < (group + 1) * parts), line)
    fold = lax.rem(lax.broadcasted_iota(jnp.int32, (lanes, lanes), 0), parts) == lane_group(
        (lanes, lanes), lanes // parts
    )
    return dot(pick.astype(jnp.float32).astype(jnp.bfloat16), fold.astype(jnp.float32).astype(jnp.bfloat16))


def open_layer(layer, natural, chain_ref, row_start, col_start, w_ref, left_refs, right_refs, wide, laid, turned, swap):
    rows, cols, hidden = natural.shape
    parts = hidden // rows
    turn(natural, turned, swap)
    row_mask = alive_groups(chain_ref, row_start, rows, parts), alive_rows(chain_ref, col_start, cols)
    col_mask = alive_groups(chain_ref, col_start, cols, parts), alive_rows(chain_ref, row_start, rows)
    for side, refs in ((0, left_refs), (1, right_refs)):
        if side == layer % 2:
            make_operand(side, natural, *row_mask, wide, refs, laid, swap)
        else:
            make_operand(side, turned[...], *col_mask, wide, refs, laid, swap)


def open_kernel(hidden, chunks, n_chan, n_sub, ids, blocks, pair_ref, chain_ref, w_ref, gate_ref, *rest):
    left_refs, right_refs = rest[:chunks], rest[chunks : 2 * chunks]
    wide, laid, turned, swap = rest[2 * chunks :]
    slots = pl.num_programs(0)
    step = pl.program_id(0)
    _, rows, cols, channels = pair_ref.shape
    block = ids[0] * slots + step

    @pl.when(step == 0)
    def _():
        spread_weights(w_ref, wide, hidden, cols)
        swap[...] = swap_matrix(16)

    normed = layer_norm(pair_ref[0].reshape(rows * cols, channels)).astype(jnp.bfloat16)
    gate = sigmoid(dot(normed, w_ref[0, :, 4 * hidden :]))
    gate_ref[0] = gate.reshape(rows, cols, channels)
    row_start, col_start = (blocks[0, block] * n_chan + ids[1]) * rows, (blocks[1, block] * n_sub + ids[2]) * cols
    natural = normed.reshape(rows, cols, channels)
    open_layer(0, natural, chain_ref, row_start, col_start, w_ref, left_refs, right_refs, wide, laid, turned, swap)


def operand_scratch(rows, size, hidden):
    parts = hidden // size
    return [
        pltpu.VMEM((parts * hidden, 4 * parts * hidden), jnp.bfloat16),
        pltpu.VMEM((2, rows // parts, parts * size, hidden), jnp.bfloat16),
        pltpu.VMEM((size, rows, hidden), jnp.bfloat16),
        pltpu.VMEM((256, 256), jnp.bfloat16),
    ]


def open_operands(ids, blocks, pair, chains, w_in, hidden, bands):
    slots, rows, cols, channels = pair.shape
    operands = [jax.ShapeDtypeStruct((slots, count, rows, hidden), jnp.bfloat16) for count in bands] * 2
    out = pl.pallas_call(
        functools.partial(open_kernel, hidden, len(bands), lax.axis_size("chan"), lax.axis_size("sub")),
        grid_spec=pltpu.PrefetchScalarGridSpec(
            num_scalar_prefetch=2,
            grid=(slots,),
            in_specs=[
                pl.BlockSpec((1, rows, cols, channels), lambda s, *_: (s, 0, 0, 0)),
                pl.BlockSpec(chains.shape, lambda s, *_: (0, 0)),
                pl.BlockSpec((1,) + w_in.shape[1:], lambda s, *_: (0, 0, 0)),
            ],
            out_specs=[pl.BlockSpec((1, rows, cols, channels), lambda s, *_: (s, 0, 0, 0))]
            + [pl.BlockSpec((1,) + o.shape[1:], lambda s, *_: (s, 0, 0, 0)) for o in operands],
            scratch_shapes=operand_scratch(rows, cols, hidden),
        ),
        out_shape=[jax.ShapeDtypeStruct(pair.shape, jnp.float32)] + operands,
        compiler_params=pltpu.CompilerParams(vmem_limit_bytes=vmem_limit),
        name="open_operands",
    )(ids, blocks, pair, chains, w_in)
    return out[0], out[1 : 1 + len(bands)], out[1 + len(bands) :]


def banded_kernel(shift, n_blk, slots_dev, terms, capacity, pieces, n_refs, size, ids, owners, slots, *rest):
    refs = rest[:n_refs]
    out_ref, left_held, right_held, chosen, sems = rest[n_refs:]
    step = pl.program_id(0)
    turn = lax.rem(step, 2)
    _, halves, bands, rows, hidden = left_held.shape
    parts = hidden // size

    @pl.when(step == 0)
    def _():
        target = lax.rem(ids[0] + shift, n_blk)
        for e in range(2 * capacity):
            chosen[e] = 0

        def scan(e, count):
            block, term = target * slots_dev + e // terms, lax.rem(e, terms)
            here = jnp.logical_and(owners[term, block] == ids[0], count < capacity)

            @pl.when(here)
            def _():
                chosen[2 * count] = slots[term, 0, block]
                chosen[2 * count + 1] = slots[term, 1, block]

            return count + here.astype(jnp.int32)

        lax.fori_loop(0, slots_dev * terms, scan, jnp.int32(0))

    def copy(n, term, buffer, source):
        side, half, *_ = pieces[n]
        held = (left_held, right_held)[side]
        return pltpu.make_async_copy(
            refs[source].at[chosen[2 * term + side]], held.at[buffer, half], sems.at[buffer, n]
        )

    def start(term, buffer):
        for n, (_, _, on, off) in enumerate(pieces):
            if on == off:
                copy(n, term, buffer, on).start()
            else:

                @pl.when(ids[3] == 1)
                def _(n=n, on=on):
                    copy(n, term, buffer, on).start()

                @pl.when(ids[3] == 0)
                def _(n=n, off=off):
                    copy(n, term, buffer, off).start()

    @pl.when(step == 0)
    def _():
        start(0, 0)

    @pl.when(step + 1 < capacity)
    def _():
        start(step + 1, 1 - turn)

    for n, piece in enumerate(pieces):
        copy(n, step, turn, piece[2]).wait()

    group = lane_group((size, hidden), size)
    for band in range(bands):
        left = jnp.concatenate([left_held[turn, h, band] for h in range(halves)], axis=1)
        apart = []
        for h in range(halves):
            right = right_held[turn, h, band]
            apart += [jnp.where(group == part, right, jnp.zeros_like(right)) for part in range(parts)]
        out_ref[0, band] = dot(left, jnp.concatenate(apart, axis=0)).astype(jnp.bfloat16)


def banded_products(shift, ids, owners, slots, lefts, rights, capacity, slots_dev, terms, size):
    n_blk = lax.axis_size("blk")
    refs, pieces = [], []

    def index_of(array):
        for n, known in enumerate(refs):
            if known is array:
                return n
        refs.append(array)
        return len(refs) - 1

    for side, operands in ((0, lefts), (1, rights)):
        for half, (on, off) in enumerate(operands):
            pieces.append((side, half, index_of(on), index_of(off)))
    _, bands, rows, hidden = lefts[0][0].shape
    return pl.pallas_call(
        functools.partial(
            banded_kernel, shift, n_blk, slots_dev, terms, capacity, tuple(pieces), len(refs), size
        ),
        grid_spec=pltpu.PrefetchScalarGridSpec(
            num_scalar_prefetch=3,
            grid=(capacity,),
            in_specs=[pl.BlockSpec(memory_space=pl.ANY)] * len(refs),
            out_specs=pl.BlockSpec((1, bands, rows, hidden), lambda t, *_: (t, 0, 0, 0)),
            scratch_shapes=[
                pltpu.VMEM((2, len(lefts), bands, rows, hidden), jnp.bfloat16),
                pltpu.VMEM((2, len(rights), bands, size, hidden), jnp.bfloat16),
                pltpu.SMEM((2 * capacity,), jnp.int32),
                pltpu.SemaphoreType.DMA((2, len(pieces))),
            ],
        ),
        out_shape=jax.ShapeDtypeStruct((capacity, bands, rows, hidden), jnp.bfloat16),
        compiler_params=pltpu.CompilerParams(vmem_limit_bytes=vmem_limit),
        cost_estimate=pl.CostEstimate(
            flops=2 * capacity * bands * rows * hidden * hidden * len(lefts) * 50,
            bytes_accessed=capacity * bands * rows * hidden * 2 * 5,
            transcendentals=0,
        ),
        name="banded_products",
    )(ids, owners, slots, *refs)


def close_kernel(layer, last, n_parts, n_blk, n_chan, n_sub, slots_dev, terms, capacity, ids, blocks, owners, *rest):
    chunks = n_parts // n_blk
    arrived, rest = rest[:n_parts], rest[n_parts:]
    cur_ref, gate_ref, w_out_ref = rest[:3]
    if last:
        out_ref, held, wide_out, place, seen, sems, swap = rest[3:]
    else:
        chain_ref, w_ref, out_ref, next_gate_ref = rest[3:7]
        left_refs, right_refs = rest[7 : 7 + chunks], rest[7 + chunks : 7 + 2 * chunks]
        held, wide_out, place, seen, sems, norm_ref, wide, laid, turned, swap = rest[7 + 2 * chunks :]
    step = pl.program_id(0)
    _, rows, cols, channels = cur_ref.shape
    _, bands, _, hidden = held.shape
    parts, size = hidden // bands, bands

    def arrival(n):
        at = sum(arrived[m * n_blk].shape[1] for m in range(n // n_blk))
        count = arrived[n].shape[1]
        target = held.at[pl.ds(n % n_blk * capacity, capacity), pl.ds(at, count)]
        return pltpu.make_async_copy(arrived[n], target, sems.at[n])

    @pl.when(step == 0)
    def _():
        for n in range(n_parts):
            arrival(n).start()
        for shift in range(n_blk):
            seen[shift] = 0

        def scan(e, carry):
            owner = owners[lax.rem(e, terms), ids[0] * slots_dev + e // terms]
            shift = lax.rem(ids[0] - owner + n_blk, n_blk)
            count = seen[owner]
            seen[owner] = count + 1
            place[e] = shift * capacity + count
            return carry

        lax.fori_loop(0, slots_dev * terms, scan, jnp.int32(0))
        wide_out[...] = jnp.zeros_like(wide_out)
        for part in range(parts):
            for a in range(parts):
                at = (part * parts + a) * bands
                wide_out[at : at + bands, a * channels : (a + 1) * channels] = w_out_ref[
                    0, part * bands : (part + 1) * bands, :
                ]
        swap[...] = swap_matrix(16)
        if not last:
            spread_weights(w_ref, wide, hidden, rows)
        for n in range(n_parts):
            arrival(n).wait()

    half = 16
    by_row = [[] for _ in range(rows)]
    for row in range(0, rows, half):
        for band in range(0, bands, half):
            taken = pl.ds(band, half), pl.ds(row, half)
            total = held[(place[step * terms], *taken)].astype(jnp.float32)
            for t in range(1, terms):
                total = total + held[(place[step * terms + t], *taken)].astype(jnp.float32)
            moved = swapped(total.astype(jnp.bfloat16), swap)
            for r in range(half):
                by_row[row + r].append(moved[r])
    groups = rows // parts
    pieces = []
    for g in range(groups):
        block = jnp.concatenate([x for a in range(parts) for x in by_row[g * parts + a]]).T
        pieces.append(jnp.concatenate([block[p * cols : (p + 1) * cols] for p in range(parts)], axis=1))
    mixture = jnp.concatenate(pieces)
    together = (lane_group((hidden, hidden), size) == lax.broadcasted_iota(jnp.int32, (hidden, hidden), 0) // size)
    together = together.astype(jnp.float32).astype(jnp.bfloat16)
    average = dot(mixture, jnp.concatenate([together] * parts)) * (1.0 / hidden)
    centred = [mixture[:, p * hidden : (p + 1) * hidden].astype(jnp.float32) - average for p in range(parts)]
    squares = sum(c * c for c in centred)
    high = squares.astype(jnp.bfloat16)
    low = (squares - high.astype(jnp.float32)).astype(jnp.bfloat16)
    variance = dot(jnp.concatenate([high, low], axis=1), jnp.concatenate([together] * 2)) * (1.0 / hidden)
    scale = lax.rsqrt(variance + norm_epsilon)
    normed = jnp.concatenate([(c * scale).astype(jnp.bfloat16) for c in centred], axis=1)
    update = dot(normed, wide_out[...])
    for g in range(groups):
        taken = pl.ds(g * parts, parts)
        change = jnp.concatenate(
            [update[g * cols : (g + 1) * cols, a * channels : (a + 1) * channels] for a in range(parts)]
        )
        gate = gate_ref[0, taken].reshape(parts * cols, channels)
        current = cur_ref[0, taken].astype(jnp.float32).reshape(parts * cols, channels)
        result = (current + gate * change).astype(jnp.bfloat16)
        out_ref[0, taken] = result.reshape(parts, cols, channels)
        if not last:
            norm = layer_norm(result).astype(jnp.bfloat16)
            norm_ref[taken] = norm.reshape(parts, cols, channels)
            next_gate = sigmoid(dot(norm, w_ref[0, :, 4 * hidden :]))
            next_gate_ref[0, taken] = next_gate.reshape(parts, cols, channels)
    if not last:
        block = ids[0] * slots_dev + step
        starts = (blocks[0, block] * n_chan + ids[1]) * rows, (blocks[1, block] * n_sub + ids[2]) * cols
        open_layer(
            layer + 1, norm_ref[...], chain_ref, *starts, w_ref, left_refs, right_refs, wide, laid, turned, swap
        )


def close_layer(layer, arrived, ids, blocks, owners, current, gate, w_out, capacity, terms, chains, w_in, last, bands):
    n_blk = len(arrived[0])
    flat = [part for chunk in arrived for part in chunk]
    slots, rows, cols, channels = current.shape
    hidden = w_out.shape[1]
    whole = pl.BlockSpec((1, rows, cols, channels), lambda s, *_: (s, 0, 0, 0))

    def layer_spec(array, index):
        return pl.BlockSpec((1,) + array.shape[1:], lambda s, *_: (index, 0, 0))

    in_specs = [pl.BlockSpec(memory_space=pl.ANY)] * len(flat) + [whole, whole, layer_spec(w_out, layer)]
    operands = [*flat, current, gate, w_out]
    out_shape = [jax.ShapeDtypeStruct(current.shape, jnp.bfloat16)]
    out_specs = [whole]
    scratch = [
        pltpu.VMEM((n_blk * capacity, sum(bands), rows, hidden), jnp.bfloat16),
        pltpu.VMEM((hidden // cols * hidden, hidden // cols * channels), jnp.bfloat16),
        pltpu.SMEM((slots * terms,), jnp.int32),
        pltpu.SMEM((n_blk,), jnp.int32),
        pltpu.SemaphoreType.DMA((len(flat),)),
    ]
    if not last:
        operands += [chains, w_in]
        in_specs += [pl.BlockSpec(chains.shape, lambda s, *_: (0, 0)), layer_spec(w_in, layer + 1)]
        made = [jax.ShapeDtypeStruct((slots, count, cols, hidden), jnp.bfloat16) for count in bands] * 2
        out_shape += [jax.ShapeDtypeStruct(current.shape, jnp.float32)] + made
        out_specs += [whole] + [pl.BlockSpec((1,) + o.shape[1:], lambda s, *_: (s, 0, 0, 0)) for o in made]
        scratch += [pltpu.VMEM((rows, cols, channels), jnp.bfloat16)] + operand_scratch(cols, rows, hidden)
    else:
        scratch += [pltpu.VMEM((256, 256), jnp.bfloat16)]
    out = pl.pallas_call(
        functools.partial(
            close_kernel, layer, last, len(flat), n_blk, lax.axis_size("chan"), lax.axis_size("sub"), slots, terms, capacity
        ),
        grid_spec=pltpu.PrefetchScalarGridSpec(
            num_scalar_prefetch=3, grid=(slots,), in_specs=in_specs, out_specs=out_specs, scratch_shapes=scratch
        ),
        out_shape=out_shape,
        compiler_params=pltpu.CompilerParams(vmem_limit_bytes=vmem_limit),
        name="close_layer",
    )(ids, blocks, owners, *operands)
    if last:
        return out[0]
    return out[0], out[1], out[2 : 2 + len(bands)], out[2 + len(bands) :]


def after(value, *others):
    return lax.optimization_barrier((value, *others))[0]


def exchange_bands_outgoing(lefts, rights):
    both = ("chan", "sub")
    made = []
    for left, right in zip(lefts, rights):
        if made:
            (_, other_left), *_ = made[-1][0]
            _, (_, two) = made[-1][1]
            right = after(right, two)
        other_left = lax.ppermute(left, "sub", [(0, 1), (1, 0)])
        one = lax.ppermute(right, both, [(0, 2), (3, 1), (1, 0), (2, 3)])
        two = lax.ppermute(right, both, [(1, 2), (2, 1)])
        made.append(([(other_left, left), (left, other_left)], [(one, one), (right, two)]))
    return made


def exchange_bands_incoming(lefts, rights):
    both = ("chan", "sub")
    made = []
    for left, right in zip(lefts, rights):
        if made:
            right, left = lax.optimization_barrier((right, left, made[-1][1][1][0]))[:2]
        one = lax.ppermute(left, both, [(1, 3), (2, 0), (0, 1), (3, 2)])
        two = lax.ppermute(one, both, [(0, 1), (3, 2)])
        other = lax.ppermute(right, "chan", [(0, 1), (1, 0)])
        made.append(([(left, one), (one, two)], [(right, right), (other, other)]))
    return made


def banded(pair, ids, blocks, owners, slot_of, chains, w_in, w_out, capacity, terms, n_blk):
    slots, rows, cols, channels = pair.shape
    hidden = w_out.shape[1]
    shifts = [n_blk // 2] + [s for s in range(1, n_blk) if s != n_blk // 2] + [0]
    layers = w_in.shape[0]
    current = pair
    for layer in range(layers):
        bands = [cols // 4, cols // 4, cols // 2]
        if layer == 0:
            gate, lefts, rights = open_operands(ids, blocks, pair, chains, w_in, hidden, bands)
        exchange = exchange_bands_incoming if layer % 2 else exchange_bands_outgoing
        arrived = []
        for left, right in exchange(lefts, rights):
            parts = [None] * n_blk
            for shift in shifts:
                made = banded_products(shift, ids, owners, slot_of, left, right, capacity, slots, terms, cols)
                if shift:
                    made = lax.ppermute(made, "blk", [(p, (p + shift) % n_blk) for p in range(n_blk)])
                parts[shift] = made
            arrived.append(parts)
        last = layer == layers - 1
        out = close_layer(
            layer, arrived, ids, blocks, owners, current, gate, w_out, capacity, terms, chains, w_in, last, bands
        )
        if last:
            return out
        current, gate, lefts, rights = out


def per_device(pair, block_list, term_owner, term_slots, chain_ids, w_in, w_out):
    n_blk = lax.axis_size("blk")
    n_chan = lax.axis_size("chan")
    n_sub = lax.axis_size("sub")
    position = lax.axis_index("blk")
    row_group = lax.axis_index("chan")
    col_group = lax.axis_index("sub")
    slots, rows, cols, channels = pair.shape
    hidden = w_out.shape[1]
    terms = term_owner.shape[1]
    capacity = max(2, -(-slots * terms // n_blk))
    fast = n_chan == 2 and n_sub == 2
    on_diagonal = (row_group == col_group).astype(jnp.int32)
    ids = jnp.stack([position, row_group, col_group, on_diagonal]).astype(jnp.int32)
    blocks = block_list.T
    owners = term_owner.T
    slot_of = jnp.transpose(term_slots, (1, 2, 0))
    chains = chain_ids.reshape(-1, 128)
    if fast and rows == cols == 32 and channels == hidden == 128:
        return banded(pair, ids, blocks, owners, slot_of, chains, w_in, w_out, capacity, terms, n_blk)
    shifts = [n_blk // 2] + [s for s in range(1, n_blk) if s != n_blk // 2] + [0]

    def all_products(lefts, right):
        parts = [None] * n_blk
        for shift in shifts:
            made = term_products(shift, ids, owners, slot_of, lefts, right, capacity, slots, terms)
            if shift:
                pairs = [(p, (p + shift) % n_blk) for p in range(n_blk)]
                made = lax.ppermute(made, "blk", pairs)
            parts[shift] = made
        return parts

    def at_home(layer, parts, current, gate, at, of, into=None):
        last = layer == w_in.shape[0] - 1
        return home(
            layer, parts, ids, blocks, owners, current, gate, w_out, capacity, terms, at, of, chains, w_in, last, into
        )

    gate, left, *rights = first_operands(ids, blocks, pair, chains, w_in, hidden, 2 if fast else 1)
    lefts, chunks = exchange_outgoing(left, rights, n_chan, n_sub)
    count = len(chunks)
    made = [all_products(lefts, right) for right in chunks]
    homes = [at_home(0, parts, pair, gate, at, count) for at, parts in enumerate(made)]
    lefts, chunks = exchange_incoming([h[2] for h in homes], [h[3] for h in homes], n_chan, n_sub)
    made = [all_products(lefts, right) for right in chunks]
    out = None
    for at, parts in enumerate(made):
        (out,) = at_home(1, parts, homes[at][0], homes[at][1], at, count, into=out)
    return out


def solution(mesh):
    in_specs = (
        P(("groups", "blk"), "chan", "sub", None),
        P("groups", None),
        P("groups", None),
        P("groups", None, None),
        P("groups"),
        P(),
        P(),
    )
    out_specs = P(("groups", "blk"), "chan", "sub", None)
    return jax.shard_map(
        per_device, mesh=mesh, in_specs=in_specs, out_specs=out_specs, check_vma=False
    )
```

```python
import functools

import jax
import jax.numpy as jnp
from jax import lax
from jax.experimental import pallas as pl
from jax.experimental.pallas import tpu as pltpu
from jax.sharding import PartitionSpec as P

norm_epsilon = 1e-05
vmem_limit = 56 * 1024 * 1024


def sigmoid(values):
    return 0.5 + 0.5 * jnp.tanh(0.5 * values)


def layer_norm(values):
    values = values.astype(jnp.float32)
    centred = values - jnp.mean(values, axis=-1, keepdims=True)
    variance = jnp.mean(centred * centred, axis=-1, keepdims=True)
    return centred * lax.rsqrt(variance + norm_epsilon)


def alive_rows(chain_ref, start, size):
    lanes = chain_ref.shape[1]
    line = chain_ref[pl.ds(start // lanes, 1), :] >= 0
    spot = lax.broadcasted_iota(jnp.int32, (size, lanes), 0) + lax.rem(start, lanes)
    pick = jnp.logical_and(lax.broadcasted_iota(jnp.int32, (size, lanes), 1) == spot, line)
    return dot(pick.astype(jnp.float32).astype(jnp.bfloat16), jnp.ones((lanes, lanes), jnp.bfloat16))


def dot(a, b):
    return jnp.dot(a, b, preferred_element_type=jnp.float32)


def gated_pair(projected, mask, hidden):
    left = mask * sigmoid(projected[:, hidden : 2 * hidden]) * projected[:, :hidden]
    right = mask * sigmoid(projected[:, 3 * hidden : 4 * hidden]) * projected[:, 2 * hidden : 3 * hidden]
    return left.astype(jnp.bfloat16), right.astype(jnp.bfloat16)


def first_kernel(hidden, row_parts, n_chan, n_sub, ids, blocks, pair_ref, chain_ref, w_ref, gate_ref, left_ref, *rest):
    right_refs, (norm_ref, turned_ref) = rest[:row_parts], rest[row_parts:]
    slots = pl.num_programs(0)
    _, rows, cols, channels = pair_ref.shape
    block = ids[0] * slots + pl.program_id(0)
    row_alive = alive_rows(chain_ref, (blocks[0, block] * n_chan + ids[1]) * rows, rows)
    col_alive = alive_rows(chain_ref, (blocks[1, block] * n_sub + ids[2]) * cols, cols)
    group = max(1, 256 // cols)
    for start in range(0, rows, group):
        at = pl.ds(start, group)
        normed = layer_norm(pair_ref[0, at].reshape(group * cols, channels))
        norm_ref[pl.ds(start * cols, group * cols), :] = normed
        gate = sigmoid(dot(normed.astype(jnp.bfloat16), w_ref[0, :, 4 * hidden :]))
        gate_ref[0, at] = gate.reshape(group, cols, channels)
    for col in range(cols):
        turned_ref[col] = norm_ref[pl.ds(col, rows, stride=cols), :].astype(jnp.bfloat16)
    step = max(1, 128 // rows)
    part = rows // row_parts
    for start in range(0, cols, step):
        taken = turned_ref[start : start + step].reshape(step * rows, channels)
        projected = dot(taken, w_ref[0, :, : 4 * hidden])
        mask = col_alive[start : start + step][:, None, :] * row_alive[None, :, :]
        left, right = gated_pair(projected, mask.reshape(step * rows, -1), hidden)
        left_ref[0, start : start + step] = left.reshape(step, rows, hidden)
        right = right.reshape(step, rows, hidden)
        for p, right_ref in enumerate(right_refs):
            right_ref[0, start : start + step] = right[:, p * part : (p + 1) * part]


def first_operands(ids, blocks, pair, chains, w_in, hidden, row_parts):
    slots, rows, cols, channels = pair.shape
    part = rows // row_parts
    operand = jax.ShapeDtypeStruct((slots, cols, rows, hidden), jnp.bfloat16)
    right = jax.ShapeDtypeStruct((slots, cols, part, hidden), jnp.bfloat16)
    return pl.pallas_call(
        functools.partial(first_kernel, hidden, row_parts, lax.axis_size("chan"), lax.axis_size("sub")),
        grid_spec=pltpu.PrefetchScalarGridSpec(
            num_scalar_prefetch=2,
            grid=(slots,),
            in_specs=[
                pl.BlockSpec((1, rows, cols, channels), lambda s, *_: (s, 0, 0, 0)),
                pl.BlockSpec(chains.shape, lambda s, *_: (0, 0)),
                pl.BlockSpec((1,) + w_in.shape[1:], lambda s, *_: (0, 0, 0)),
            ],
            out_specs=[
                pl.BlockSpec((1, rows, cols, channels), lambda s, *_: (s, 0, 0, 0)),
                pl.BlockSpec((1, cols, rows, hidden), lambda s, *_: (s, 0, 0, 0)),
            ]
            + [pl.BlockSpec((1, cols, part, hidden), lambda s, *_: (s, 0, 0, 0))] * row_parts,
            scratch_shapes=[
                pltpu.VMEM((rows * cols, channels), jnp.float32),
                pltpu.VMEM((cols, rows, channels), jnp.bfloat16),
            ],
        ),
        out_shape=[jax.ShapeDtypeStruct(pair.shape, jnp.float32), operand] + [right] * row_parts,
        compiler_params=pltpu.CompilerParams(vmem_limit_bytes=vmem_limit),
        name="first_operands",
    )(ids, blocks, pair, chains, w_in)


def product_kernel(shift, n_blk, slots_dev, terms, capacity, pieces, n_refs, ids, owners, slots, *rest):
    refs = rest[:n_refs]
    out_ref, left_held, right_held, right_wide, chosen, sems = rest[n_refs:]
    step = pl.program_id(0)
    turn = lax.rem(step, 2)
    _, depth, n_i, hidden = left_held.shape
    n_j = right_wide.shape[1]

    @pl.when(step == 0)
    def _():
        target = lax.rem(ids[0] + shift, n_blk)
        for e in range(2 * capacity):
            chosen[e] = 0

        def scan(e, count):
            block, term = target * slots_dev + e // terms, lax.rem(e, terms)
            here = jnp.logical_and(owners[term, block] == ids[0], count < capacity)

            @pl.when(here)
            def _():
                chosen[2 * count] = slots[term, 0, block]
                chosen[2 * count + 1] = slots[term, 1, block]

            return count + here.astype(jnp.int32)

        lax.fori_loop(0, slots_dev * terms, scan, jnp.int32(0))

    def copy(n, term, buffer, source):
        side, _, _, k0, depth_of, i0, size = pieces[n]
        held = (left_held, right_held)[side]
        return pltpu.make_async_copy(
            refs[source].at[chosen[2 * term + side]],
            held.at[buffer, pl.ds(k0, depth_of), pl.ds(i0, size), :],
            sems.at[buffer, n],
        )

    def start(term, buffer):
        for n, (_, on, off, *_) in enumerate(pieces):
            if on == off:
                copy(n, term, buffer, on).start()
            else:

                @pl.when(ids[3] == 1)
                def _(n=n, on=on):
                    copy(n, term, buffer, on).start()

                @pl.when(ids[3] == 0)
                def _(n=n, off=off):
                    copy(n, term, buffer, off).start()

    @pl.when(step == 0)
    def _():
        start(0, 0)

    @pl.when(step + 1 < capacity)
    def _():
        start(step + 1, 1 - turn)

    for n, piece in enumerate(pieces):
        copy(n, step, turn, piece[1]).wait()

    span = 8

    def widen(n, carry):
        at = pl.ds(n * span, span)
        right_wide[at] = right_held[turn, at].astype(jnp.float32)
        return carry

    lax.fori_loop(0, depth // span, widen, 0)

    group = min(8, n_j)
    unroll = 4
    for j0 in range(0, n_j, group):

        def body(n, sums):
            for u in range(unroll):
                k = n * unroll + u
                left = left_held[turn, k].astype(jnp.float32).reshape(n_i // 8, 8, hidden)
                sums = tuple(
                    total + left * right_wide[k, pl.ds(j0 + j, 8, stride=0), :][None]
                    for j, total in enumerate(sums)
                )
            return sums

        zero = jnp.zeros((n_i // 8, 8, hidden), jnp.float32)
        sums = lax.fori_loop(0, depth // unroll, body, (zero,) * group)
        for j, total in enumerate(sums):
            out_ref[0, j0 + j] = total.reshape(n_i, hidden).astype(jnp.bfloat16)


def term_products(shift, ids, owners, slots, lefts, rights, capacity, slots_dev, terms):
    n_blk = lax.axis_size("blk")
    refs, pieces = [], []

    def index_of(array):
        for n, known in enumerate(refs):
            if known is array:
                return n
        refs.append(array)
        return len(refs) - 1

    for side, operands in ((0, lefts), (1, rights)):
        for on, off, k0, i0 in operands:
            pieces.append((side, index_of(on), index_of(off), k0, on.shape[1], i0, on.shape[2]))
    hidden = lefts[0][0].shape[3]
    n_i = max(p[5] + p[6] for p in pieces if p[0] == 0)
    n_j = max(p[5] + p[6] for p in pieces if p[0] == 1)
    depth = max(p[3] + p[4] for p in pieces)
    return pl.pallas_call(
        functools.partial(
            product_kernel, shift, n_blk, slots_dev, terms, capacity, tuple(pieces), len(refs)
        ),
        grid_spec=pltpu.PrefetchScalarGridSpec(
            num_scalar_prefetch=3,
            grid=(capacity,),
            in_specs=[pl.BlockSpec(memory_space=pl.ANY)] * len(refs),
            out_specs=pl.BlockSpec((1, n_j, n_i, hidden), lambda t, *_: (t, 0, 0, 0)),
            scratch_shapes=[
                pltpu.VMEM((2, depth, n_i, hidden), jnp.bfloat16),
                pltpu.VMEM((2, depth, n_j, hidden), jnp.bfloat16),
                pltpu.VMEM((depth, n_j, hidden), jnp.float32),
                pltpu.SMEM((2 * capacity,), jnp.int32),
                pltpu.SemaphoreType.DMA((2, len(pieces))),
            ],
        ),
        out_shape=jax.ShapeDtypeStruct((capacity, n_j, n_i, hidden), jnp.bfloat16),
        compiler_params=pltpu.CompilerParams(vmem_limit_bytes=vmem_limit),
        cost_estimate=pl.CostEstimate(
            flops=2 * capacity * n_i * n_j * depth * hidden * 100,
            bytes_accessed=capacity * (depth * (n_i + n_j) + n_i * n_j) * hidden * 2,
            transcendentals=0,
        ),
        name="term_products",
    )(ids, owners, slots, *refs)


def home_kernel(last, hidden, n_blk, n_chan, n_sub, at, of, slots_dev, terms, capacity, ids, blocks, owners, *rest):
    parts, rest = rest[:n_blk], rest[n_blk:]
    scratch, rest = rest[-5:], rest[:-5]
    held, turned, place, seen, sems = scratch
    cur_ref, gate_ref, w_out_ref = rest[:3]
    if last:
        out_ref = rest[-1]
    else:
        chain_ref, w_ref, out_ref, next_gate_ref, left_ref, right_ref = rest[3:]
    step = pl.program_id(0)
    _, rows, cols, channels = cur_ref.shape

    def arrival(shift):
        return pltpu.make_async_copy(parts[shift], held.at[pl.ds(shift * capacity, capacity)], sems.at[shift])

    @pl.when(step == 0)
    def _():
        for shift in range(n_blk):
            arrival(shift).start()
            seen[shift] = 0

        def scan(e, carry):
            owner = owners[lax.rem(e, terms), ids[0] * slots_dev + e // terms]
            shift = lax.rem(ids[0] - owner + n_blk, n_blk)
            count = seen[owner]
            seen[owner] = count + 1
            place[e] = shift * capacity + count
            return carry

        lax.fori_loop(0, slots_dev * terms, scan, jnp.int32(0))
        for shift in range(n_blk):
            arrival(shift).wait()

    if not last:
        block = ids[0] * slots_dev + step
        row_alive = alive_rows(chain_ref, (blocks[0, block] * n_chan + ids[1]) * rows, rows)
        col_alive = alive_rows(chain_ref, ((blocks[1, block] * n_sub + ids[2]) * of + at) * cols, cols)
    span = max(1, 128 // rows)
    for start in range(0, cols, span):
        taken = pl.ds(start, span)
        total = held[place[step * terms], taken].astype(jnp.float32)
        for t in range(1, terms):
            total = total + held[place[step * terms + t], taken].astype(jnp.float32)
        rounded = total.astype(jnp.bfloat16).astype(jnp.float32)
        turned[pl.ds(start * rows, span * rows), :] = rounded.reshape(span * rows, hidden)
    group = min(rows, max(1, 256 // cols))
    for start in range(0, rows, group):
        taken = pl.ds(start, group)
        mixture = jnp.concatenate(
            [turned[pl.ds(row, cols, stride=rows), :].astype(jnp.bfloat16) for row in range(start, start + group)]
        )
        update = dot(layer_norm(mixture).astype(jnp.bfloat16), w_out_ref[0])
        current = cur_ref[0, taken].astype(jnp.float32).reshape(group * cols, channels)
        gate = gate_ref[0, taken].reshape(group * cols, channels)
        result = (current + gate * update).astype(jnp.bfloat16)
        out_ref[0, taken] = result.reshape(group, cols, channels)
        if not last:
            normed = layer_norm(result).astype(jnp.bfloat16)
            projected = dot(normed, w_ref[0])
            next_gate_ref[0, taken] = sigmoid(projected[:, 4 * hidden :]).reshape(group, cols, channels)
            mask = row_alive[start : start + group][:, None, :] * col_alive[None, :, :]
            left, right = gated_pair(projected, mask.reshape(group * cols, channels), hidden)
            left_ref[0, taken] = left.reshape(group, cols, hidden)
            right_ref[0, taken] = right.reshape(group, cols, hidden)


def home(layer, parts, ids, blocks, owners, current, gate, w_out, capacity, terms, at, of, chains, w_in, last, into=None):
    n_blk = len(parts)
    slots, rows, _, channels = current.shape
    hidden = w_out.shape[1]
    cols = parts[0].shape[1]
    chunk = (1, rows, cols, channels)

    def chunk_spec(array):
        whole = array.shape[2] != cols
        return pl.BlockSpec(chunk, lambda s, *_: (s, 0, at if whole else 0, 0))

    def layer_spec(array, index):
        return pl.BlockSpec((1,) + array.shape[1:], lambda s, *_: (index, 0, 0))

    in_specs = [pl.BlockSpec(memory_space=pl.ANY)] * n_blk + [
        chunk_spec(current),
        chunk_spec(gate),
        layer_spec(w_out, layer),
    ]
    operands = [*parts, current, gate, w_out]
    aliases = {}
    if last:
        if into is not None:
            aliases = {3 + len(operands): 0}
            operands.append(into)
            in_specs.append(pl.BlockSpec(memory_space=pl.ANY))
        out_shape = [jax.ShapeDtypeStruct((slots, rows, cols * of, channels), jnp.bfloat16)]
        out_specs = [pl.BlockSpec(chunk, lambda s, *_: (s, 0, at, 0))]
    else:
        operands += [chains, w_in]
        in_specs += [pl.BlockSpec(chains.shape, lambda s, *_: (0, 0)), layer_spec(w_in, layer + 1)]
        small = (slots, rows, cols, channels)
        out_shape = [jax.ShapeDtypeStruct(small, t) for t in (jnp.bfloat16, jnp.float32, jnp.bfloat16, jnp.bfloat16)]
        out_specs = [pl.BlockSpec(chunk, lambda s, *_: (s, 0, 0, 0))] * 4
    return pl.pallas_call(
        functools.partial(
            home_kernel, last, hidden, n_blk, lax.axis_size("chan"), lax.axis_size("sub"), at, of, slots, terms, capacity
        ),
        grid_spec=pltpu.PrefetchScalarGridSpec(
            num_scalar_prefetch=3,
            grid=(slots,),
            in_specs=in_specs,
            out_specs=out_specs,
            scratch_shapes=[
                pltpu.VMEM((n_blk * capacity, cols, rows, hidden), jnp.bfloat16),
                pltpu.VMEM((rows * cols, hidden), jnp.float32),
                pltpu.SMEM((slots * terms,), jnp.int32),
                pltpu.SMEM((n_blk,), jnp.int32),
                pltpu.SemaphoreType.DMA((n_blk,)),
            ],
        ),
        out_shape=out_shape,
        input_output_aliases=aliases,
        compiler_params=pltpu.CompilerParams(vmem_limit_bytes=vmem_limit),
        cost_estimate=pl.CostEstimate(
            flops=2 * slots * rows * cols * channels * 6 * channels * 10,
            bytes_accessed=slots * rows * cols * channels * 16,
            transcendentals=0,
        ),
        name="home",
    )(ids, blocks, owners, *operands)


def exchange_outgoing(left, rights, n_chan, n_sub):
    if n_chan == 2 and n_sub == 2:
        both = ("chan", "sub")
        other_left = lax.ppermute(left, "sub", [(0, 1), (1, 0)])
        lefts = [(other_left, left, 0, 0), (left, other_left, left.shape[1], 0)]
        chunks = []
        for right in rights:
            if chunks:
                (one, *_), (_, two, *_) = chunks[-1]
                right, *_ = lax.optimization_barrier((right, one, two))
            one = lax.ppermute(right, both, [(0, 2), (3, 1), (1, 0), (2, 3)])
            two = lax.ppermute(right, both, [(1, 2), (2, 1)])
            chunks.append([(one, one, 0, 0), (right, two, right.shape[1], 0)])
        return lefts, chunks
    left = lax.all_gather(left, "sub", axis=1, tiled=True)
    right = jnp.concatenate(rights, axis=2)
    right = lax.all_gather(right, "chan", axis=2, tiled=True)
    right = lax.all_to_all(right, "sub", split_axis=2, concat_axis=1, tiled=True)
    cols = right.shape[2] // 2
    chunks = [right[:, :, :cols], right[:, :, cols:]]
    return [(left, left, 0, 0)], [[(r, r, 0, 0)] for r in chunks]


def exchange_incoming(lefts, rights, n_chan, n_sub):
    if n_chan == 2 and n_sub == 2:
        both = ("chan", "sub")
        left_pieces, chunks = [], []
        at = 0
        for left, right in zip(lefts, rights):
            depth = left.shape[1]
            one = lax.ppermute(left, both, [(1, 3), (2, 0), (0, 1), (3, 2)])
            two = lax.ppermute(one, both, [(0, 1), (3, 2)])
            left_pieces += [(left, one, 0, at), (one, two, depth, at)]
            other = lax.ppermute(right, "chan", [(0, 1), (1, 0)])
            chunks.append([(right, right, 0, 0), (other, other, depth, 0)])
            at += left.shape[2]
        return left_pieces, chunks
    left = lax.all_gather(jnp.concatenate(lefts, axis=2), "chan", axis=1, tiled=True)
    left = lax.all_gather(left, "sub", axis=2, tiled=True)
    size = left.shape[2] // n_chan
    left = lax.dynamic_slice_in_dim(left, lax.axis_index("chan") * size, size, 2)
    gathered = [lax.all_gather(right, "chan", axis=1, tiled=True) for right in rights]
    return [(left, left, 0, 0)], [[(r, r, 0, 0)] for r in gathered]


def lane_group(shape, size):
    return lax.broadcasted_iota(jnp.int32, shape, 1) // size


def spread_weights(w_ref, wide_ref, hidden, size):
    parts = hidden // size
    for side in range(2):
        for kind in range(2):
            start = (2 * side + kind) * hidden
            weights = w_ref[0, :, start : start + hidden].astype(jnp.float32)
            group = lane_group(weights.shape, size)
            for part in range(parts):
                kept = jnp.where(group == part, weights, 0.0)
                at = ((side * parts + part) * 2 + kind) * hidden
                for a in range(parts):
                    moved = pltpu.roll(kept, ((a - part) % parts) * size, 1) if a != part else kept
                    wide_ref[a * hidden : (a + 1) * hidden, at : at + hidden] = moved.astype(jnp.bfloat16)


def swap_matrix(half):
    shape = (half * half, half * half)
    to, of = lax.broadcasted_iota(jnp.int32, shape, 0), lax.broadcasted_iota(jnp.int32, shape, 1)
    same = jnp.logical_and(to // half == lax.rem(of, half), lax.rem(to, half) == of // half)
    return same.astype(jnp.float32).astype(jnp.bfloat16)


def swapped(values, swap_ref):
    half, _, lanes = values.shape
    moved = dot(swap_ref[...], values.reshape(half * half, lanes))
    return moved.astype(jnp.bfloat16).reshape(half, half, lanes)


def turn(taken, turned, swap_ref):
    half = 16
    for x in range(0, taken.shape[0], half):
        for y in range(0, taken.shape[1], half):
            turned[y : y + half, x : x + half] = swapped(taken[x : x + half, y : y + half], swap_ref)


def make_operand(side, taken, row_alive, inner_alive, wide_ref, out_refs, laid, swap_ref):
    rows, size, hidden = taken.shape
    parts, bands, half = hidden // size, size, 16
    groups = rows // parts
    stacked = jnp.concatenate(
        [jnp.concatenate([taken[g * parts + a] for a in range(parts)], axis=1) for g in range(groups)], axis=0
    )
    mask = (row_alive[:, None, :] * inner_alive[None, :, :]).reshape(groups * size, hidden)
    for part in range(parts):
        at = (side * parts + part) * 2 * hidden
        made = dot(stacked, wide_ref[:, at : at + 2 * hidden])
        value = mask * sigmoid(made[:, hidden:]) * made[:, :hidden]
        laid[side, :, part * size : (part + 1) * size, :] = value.astype(jnp.bfloat16).reshape(groups, size, hidden)
    blocks = [laid[side, g].T for g in range(groups)]
    starts = [sum(ref.shape[1] for ref in out_refs[:n]) for n in range(len(out_refs))]
    for first in range(0, bands, half):
        for row in range(0, rows, half):
            tiles = []
            for r in range(row, row + half):
                at = r % parts * bands + first
                tiles.append(blocks[r // parts][at : at + half])
            moved = swapped(jnp.stack(tiles), swap_ref)
            for start, ref in zip(starts, out_refs):
                low, high = max(start, first), min(start + ref.shape[1], first + half)
                if low < high:
                    ref[0, low - start : high - start, row : row + half] = moved[low - first : high - first]


def alive_groups(chain_ref, start, rows, parts):
    lanes = chain_ref.shape[1]
    groups = rows // parts
    line = chain_ref[pl.ds(start // lanes, 1), :] >= 0
    row = lax.broadcasted_iota(jnp.int32, (groups, lanes), 1) - lax.rem(start, lanes)
    group = lax.broadcasted_iota(jnp.int32, (groups, lanes), 0)
    pick = jnp.logical_and(jnp.logical_and(row >= group * parts, row < (group + 1) * parts), line)
    fold = lax.rem(lax.broadcasted_iota(jnp.int32, (lanes, lanes), 0), parts) == lane_group(
        (lanes, lanes), lanes // parts
    )
    return dot(pick.astype(jnp.float32).astype(jnp.bfloat16), fold.astype(jnp.float32).astype(jnp.bfloat16))


def open_layer(layer, natural, chain_ref, row_start, col_start, w_ref, left_refs, right_refs, wide, laid, turned, swap):
    rows, cols, hidden = natural.shape
    parts = hidden // rows
    turn(natural, turned, swap)
    row_mask = alive_groups(chain_ref, row_start, rows, parts), alive_rows(chain_ref, col_start, cols)
    col_mask = alive_groups(chain_ref, col_start, cols, parts), alive_rows(chain_ref, row_start, rows)
    for side, refs in ((0, left_refs), (1, right_refs)):
        if side == layer % 2:
            make_operand(side, natural, *row_mask, wide, refs, laid, swap)
        else:
            make_operand(side, turned[...], *col_mask, wide, refs, laid, swap)


def open_kernel(hidden, chunks, n_chan, n_sub, ids, blocks, pair_ref, chain_ref, w_ref, gate_ref, *rest):
    left_refs, right_refs = rest[:chunks], rest[chunks : 2 * chunks]
    norm_ref, wide, laid, turned, swap = rest[2 * chunks :]
    slots = pl.num_programs(0)
    step = pl.program_id(0)
    _, rows, cols, channels = pair_ref.shape
    block = ids[0] * slots + step

    @pl.when(step == 0)
    def _():
        spread_weights(w_ref, wide, hidden, cols)
        swap[...] = swap_matrix(16)

    group = hidden // cols
    for start in range(0, rows, group):
        at = pl.ds(start, group)
        normed = layer_norm(pair_ref[0, at].reshape(group * cols, channels)).astype(jnp.bfloat16)
        gate = sigmoid(dot(normed, w_ref[0, :, 4 * hidden :]))
        gate_ref[0, at] = gate.reshape(group, cols, channels)
        norm_ref[at] = normed.reshape(group, cols, channels)
    row_start, col_start = (blocks[0, block] * n_chan + ids[1]) * rows, (blocks[1, block] * n_sub + ids[2]) * cols
    open_layer(0, norm_ref[...], chain_ref, row_start, col_start, w_ref, left_refs, right_refs, wide, laid, turned, swap)


def operand_scratch(rows, size, hidden):
    parts = hidden // size
    return [
        pltpu.VMEM((parts * hidden, 4 * parts * hidden), jnp.bfloat16),
        pltpu.VMEM((2, rows // parts, parts * size, hidden), jnp.bfloat16),
        pltpu.VMEM((size, rows, hidden), jnp.bfloat16),
        pltpu.VMEM((256, 256), jnp.bfloat16),
    ]


def open_operands(ids, blocks, pair, chains, w_in, hidden, bands):
    slots, rows, cols, channels = pair.shape
    operands = [jax.ShapeDtypeStruct((slots, count, rows, hidden), jnp.bfloat16) for count in bands] * 2
    out = pl.pallas_call(
        functools.partial(open_kernel, hidden, len(bands), lax.axis_size("chan"), lax.axis_size("sub")),
        grid_spec=pltpu.PrefetchScalarGridSpec(
            num_scalar_prefetch=2,
            grid=(slots,),
            in_specs=[
                pl.BlockSpec((1, rows, cols, channels), lambda s, *_: (s, 0, 0, 0)),
                pl.BlockSpec(chains.shape, lambda s, *_: (0, 0)),
                pl.BlockSpec((1,) + w_in.shape[1:], lambda s, *_: (0, 0, 0)),
            ],
            out_specs=[pl.BlockSpec((1, rows, cols, channels), lambda s, *_: (s, 0, 0, 0))]
            + [pl.BlockSpec((1,) + o.shape[1:], lambda s, *_: (s, 0, 0, 0)) for o in operands],
            scratch_shapes=[pltpu.VMEM((rows, cols, channels), jnp.bfloat16)] + operand_scratch(rows, cols, hidden),
        ),
        out_shape=[jax.ShapeDtypeStruct(pair.shape, jnp.float32)] + operands,
        compiler_params=pltpu.CompilerParams(vmem_limit_bytes=vmem_limit),
        name="open_operands",
    )(ids, blocks, pair, chains, w_in)
    return out[0], out[1 : 1 + len(bands)], out[1 + len(bands) :]


def banded_kernel(shifts, n_blk, slots_dev, terms, capacity, pieces, n_refs, size, ids, owners, slots, *rest):
    refs, rest = rest[:n_refs], rest[n_refs:]
    out_refs, (left_held, right_held, chosen, sems) = rest[: len(shifts)], rest[len(shifts) :]
    step = pl.program_id(0)
    _, halves, bands, rows, hidden = left_held.shape
    parts = hidden // size
    count = len(shifts) * capacity

    def copy(n, term, source):
        side, half, *_ = pieces[n]
        held = (left_held, right_held)[side]
        return pltpu.make_async_copy(refs[source].at[chosen[2 * term + side]], held.at[term, half], sems.at[term, n])

    def start(term):
        for n, (_, _, on, off) in enumerate(pieces):
            if on == off:
                copy(n, term, on).start()
            else:

                @pl.when(ids[3] == 1)
                def _(n=n, on=on):
                    copy(n, term, on).start()

                @pl.when(ids[3] == 0)
                def _(n=n, off=off):
                    copy(n, term, off).start()

    @pl.when(step == 0)
    def _():
        for e in range(2 * count):
            chosen[e] = 0
        for n, shift in enumerate(shifts):
            target = lax.rem(ids[0] + shift, n_blk)

            def scan(e, found):
                block, term = target * slots_dev + e // terms, lax.rem(e, terms)
                here = jnp.logical_and(owners[term, block] == ids[0], found < capacity)

                @pl.when(here)
                def _():
                    chosen[2 * (n * capacity + found)] = slots[term, 0, block]
                    chosen[2 * (n * capacity + found) + 1] = slots[term, 1, block]

                return found + here.astype(jnp.int32)

            lax.fori_loop(0, slots_dev * terms, scan, jnp.int32(0))
        for term in range(count):
            start(term)

    for n, piece in enumerate(pieces):
        copy(n, step, piece[2]).wait()

    for n, out_ref in enumerate(out_refs):

        @pl.when(step // capacity == n)
        def _(out_ref=out_ref):
            group = lane_group((size, hidden), size)
            for band in range(bands):
                left = jnp.concatenate([left_held[step, h, band] for h in range(halves)], axis=1)
                apart = []
                for h in range(halves):
                    right = right_held[step, h, band]
                    apart += [jnp.where(group == part, right, jnp.zeros_like(right)) for part in range(parts)]
                out_ref[0, band] = dot(left, jnp.concatenate(apart, axis=0)).astype(jnp.bfloat16)


def banded_products(shifts, ids, owners, slots, lefts, rights, capacity, slots_dev, terms, size):
    n_blk = lax.axis_size("blk")
    refs, pieces = [], []

    def index_of(array):
        for n, known in enumerate(refs):
            if known is array:
                return n
        refs.append(array)
        return len(refs) - 1

    for side, operands in ((0, lefts), (1, rights)):
        for half, (on, off) in enumerate(operands):
            pieces.append((side, half, index_of(on), index_of(off)))
    _, bands, rows, hidden = lefts[0][0].shape
    count = len(shifts) * capacity

    def out_spec(n):
        return pl.BlockSpec(
            (1, bands, rows, hidden), lambda t, *_: (jnp.clip(t - n * capacity, 0, capacity - 1), 0, 0, 0)
        )

    return pl.pallas_call(
        functools.partial(
            banded_kernel, shifts, n_blk, slots_dev, terms, capacity, tuple(pieces), len(refs), size
        ),
        grid_spec=pltpu.PrefetchScalarGridSpec(
            num_scalar_prefetch=3,
            grid=(count,),
            in_specs=[pl.BlockSpec(memory_space=pl.ANY)] * len(refs),
            out_specs=[out_spec(n) for n in range(len(shifts))],
            scratch_shapes=[
                pltpu.VMEM((count, len(lefts), bands, rows, hidden), jnp.bfloat16),
                pltpu.VMEM((count, len(rights), bands, size, hidden), jnp.bfloat16),
                pltpu.SMEM((2 * count,), jnp.int32),
                pltpu.SemaphoreType.DMA((count, len(pieces))),
            ],
        ),
        out_shape=[jax.ShapeDtypeStruct((capacity, bands, rows, hidden), jnp.bfloat16)] * len(shifts),
        compiler_params=pltpu.CompilerParams(vmem_limit_bytes=vmem_limit),
        cost_estimate=pl.CostEstimate(
            flops=2 * count * bands * rows * hidden * hidden * len(lefts), bytes_accessed=1, transcendentals=0
        ),
        name="banded_products",
    )(ids, owners, slots, *refs)


def close_kernel(layer, last, n_parts, n_blk, n_chan, n_sub, slots_dev, terms, capacity, ids, blocks, owners, *rest):
    chunks = n_parts // n_blk
    arrived, rest = rest[:n_parts], rest[n_parts:]
    cur_ref, gate_ref, w_out_ref = rest[:3]
    if last:
        out_ref, held, wide_out, place, seen, sems, swap = rest[3:]
    else:
        chain_ref, w_ref, out_ref, next_gate_ref = rest[3:7]
        left_refs, right_refs = rest[7 : 7 + chunks], rest[7 + chunks : 7 + 2 * chunks]
        held, wide_out, place, seen, sems, norm_ref, wide, laid, turned, swap = rest[7 + 2 * chunks :]
    step = pl.program_id(0)
    _, rows, cols, channels = cur_ref.shape
    _, bands, _, hidden = held.shape
    parts, size = hidden // bands, bands

    def arrival(n):
        at = sum(arrived[m * n_blk].shape[1] for m in range(n // n_blk))
        count = arrived[n].shape[1]
        target = held.at[pl.ds(n % n_blk * capacity, capacity), pl.ds(at, count)]
        return pltpu.make_async_copy(arrived[n], target, sems.at[n])

    @pl.when(step == 0)
    def _():
        for n in range(n_parts):
            arrival(n).start()
        for shift in range(n_blk):
            seen[shift] = 0

        def scan(e, carry):
            owner = owners[lax.rem(e, terms), ids[0] * slots_dev + e // terms]
            shift = lax.rem(ids[0] - owner + n_blk, n_blk)
            count = seen[owner]
            seen[owner] = count + 1
            place[e] = shift * capacity + count
            return carry

        lax.fori_loop(0, slots_dev * terms, scan, jnp.int32(0))
        wide_out[...] = jnp.zeros_like(wide_out)
        for part in range(parts):
            for a in range(parts):
                at = (part * parts + a) * bands
                wide_out[at : at + bands, a * channels : (a + 1) * channels] = w_out_ref[
                    0, part * bands : (part + 1) * bands, :
                ]
        swap[...] = swap_matrix(16)
        if not last:
            spread_weights(w_ref, wide, hidden, rows)
        for n in range(n_parts):
            arrival(n).wait()

    half = 16
    by_row = [[] for _ in range(rows)]
    for row in range(0, rows, half):
        for band in range(0, bands, half):
            taken = pl.ds(band, half), pl.ds(row, half)
            total = held[(place[step * terms], *taken)].astype(jnp.float32)
            for t in range(1, terms):
                total = total + held[(place[step * terms + t], *taken)].astype(jnp.float32)
            moved = swapped(total.astype(jnp.bfloat16), swap)
            for r in range(half):
                by_row[row + r].append(moved[r])
    groups = rows // parts
    pieces = []
    for g in range(groups):
        block = jnp.concatenate([x for a in range(parts) for x in by_row[g * parts + a]]).T
        pieces.append(jnp.concatenate([block[p * cols : (p + 1) * cols] for p in range(parts)], axis=1))
    mixture = jnp.concatenate(pieces)
    together = (lane_group((hidden, hidden), size) == lax.broadcasted_iota(jnp.int32, (hidden, hidden), 0) // size)
    together = together.astype(jnp.float32).astype(jnp.bfloat16)
    average = dot(mixture, jnp.concatenate([together] * parts)) * (1.0 / hidden)
    centred = [mixture[:, p * hidden : (p + 1) * hidden].astype(jnp.float32) - average for p in range(parts)]
    squares = sum(c * c for c in centred)
    high = squares.astype(jnp.bfloat16)
    low = (squares - high.astype(jnp.float32)).astype(jnp.bfloat16)
    variance = dot(jnp.concatenate([high, low], axis=1), jnp.concatenate([together] * 2)) * (1.0 / hidden)
    scale = lax.rsqrt(variance + norm_epsilon)
    normed = jnp.concatenate([(c * scale).astype(jnp.bfloat16) for c in centred], axis=1)
    update = dot(normed, wide_out[...])
    for g in range(groups):
        taken = pl.ds(g * parts, parts)
        change = jnp.concatenate(
            [update[g * cols : (g + 1) * cols, a * channels : (a + 1) * channels] for a in range(parts)]
        )
        gate = gate_ref[0, taken].reshape(parts * cols, channels)
        current = cur_ref[0, taken].astype(jnp.float32).reshape(parts * cols, channels)
        result = (current + gate * change).astype(jnp.bfloat16)
        out_ref[0, taken] = result.reshape(parts, cols, channels)
        if not last:
            norm = layer_norm(result).astype(jnp.bfloat16)
            norm_ref[taken] = norm.reshape(parts, cols, channels)
            next_gate = sigmoid(dot(norm, w_ref[0, :, 4 * hidden :]))
            next_gate_ref[0, taken] = next_gate.reshape(parts, cols, channels)
    if not last:
        block = ids[0] * slots_dev + step
        starts = (blocks[0, block] * n_chan + ids[1]) * rows, (blocks[1, block] * n_sub + ids[2]) * cols
        open_layer(
            layer + 1, norm_ref[...], chain_ref, *starts, w_ref, left_refs, right_refs, wide, laid, turned, swap
        )


def close_layer(layer, arrived, ids, blocks, owners, current, gate, w_out, capacity, terms, chains, w_in, last, bands):
    n_blk = len(arrived[0])
    flat = [part for chunk in arrived for part in chunk]
    slots, rows, cols, channels = current.shape
    hidden = w_out.shape[1]
    whole = pl.BlockSpec((1, rows, cols, channels), lambda s, *_: (s, 0, 0, 0))

    def layer_spec(array, index):
        return pl.BlockSpec((1,) + array.shape[1:], lambda s, *_: (index, 0, 0))

    in_specs = [pl.BlockSpec(memory_space=pl.ANY)] * len(flat) + [whole, whole, layer_spec(w_out, layer)]
    operands = [*flat, current, gate, w_out]
    out_shape = [jax.ShapeDtypeStruct(current.shape, jnp.bfloat16)]
    out_specs = [whole]
    scratch = [
        pltpu.VMEM((n_blk * capacity, sum(bands[layer]), rows, hidden), jnp.bfloat16),
        pltpu.VMEM((hidden // cols * hidden, hidden // cols * channels), jnp.bfloat16),
        pltpu.SMEM((slots * terms,), jnp.int32),
        pltpu.SMEM((n_blk,), jnp.int32),
        pltpu.SemaphoreType.DMA((len(flat),)),
    ]
    if not last:
        operands += [chains, w_in]
        in_specs += [pl.BlockSpec(chains.shape, lambda s, *_: (0, 0)), layer_spec(w_in, layer + 1)]
        bands = bands[layer + 1]
        made = [jax.ShapeDtypeStruct((slots, count, cols, hidden), jnp.bfloat16) for count in bands] * 2
        out_shape += [jax.ShapeDtypeStruct(current.shape, jnp.float32)] + made
        out_specs += [whole] + [pl.BlockSpec((1,) + o.shape[1:], lambda s, *_: (s, 0, 0, 0)) for o in made]
        scratch += [pltpu.VMEM((rows, cols, channels), jnp.bfloat16)] + operand_scratch(cols, rows, hidden)
    else:
        scratch += [pltpu.VMEM((256, 256), jnp.bfloat16)]
    out = pl.pallas_call(
        functools.partial(
            close_kernel, layer, last, len(flat), n_blk, lax.axis_size("chan"), lax.axis_size("sub"), slots, terms, capacity
        ),
        grid_spec=pltpu.PrefetchScalarGridSpec(
            num_scalar_prefetch=3, grid=(slots,), in_specs=in_specs, out_specs=out_specs, scratch_shapes=scratch
        ),
        out_shape=out_shape,
        compiler_params=pltpu.CompilerParams(vmem_limit_bytes=vmem_limit),
        name="close_layer",
    )(ids, blocks, owners, *operands)
    if last:
        return out[0]
    return out[0], out[1], out[2 : 2 + len(bands)], out[2 + len(bands) :]


def after(value, *others):
    return lax.optimization_barrier((value, *others))[0]


def exchange_bands_outgoing(lefts, rights):
    both = ("chan", "sub")
    made = []
    for left, right in zip(lefts, rights):
        if made:
            (before, _), _ = made[-1][0]
            (one, _), (_, two) = made[-1][1]
            left, right = lax.optimization_barrier((left, right, before, one, two))[:2]
        other_left = lax.ppermute(left, "sub", [(0, 1), (1, 0)])
        one = lax.ppermute(right, both, [(0, 2), (3, 1), (1, 0), (2, 3)])
        two = lax.ppermute(right, both, [(1, 2), (2, 1)])
        made.append(([(other_left, left), (left, other_left)], [(one, one), (right, two)]))
    return made


def exchange_bands_incoming(lefts, rights):
    both = ("chan", "sub")
    made = []
    for left, right in zip(lefts, rights):
        if made:
            before, other = made[-1][0][1][1], made[-1][1][1][0]
            left, right = lax.optimization_barrier((left, right, before, other))[:2]
        one = lax.ppermute(left, both, [(1, 3), (2, 0), (0, 1), (3, 2)])
        two = lax.ppermute(one, both, [(0, 1), (3, 2)])
        other = lax.ppermute(right, "chan", [(0, 1), (1, 0)])
        made.append(([(left, one), (one, two)], [(right, right), (other, other)]))
    return made


def banded(pair, ids, blocks, owners, slot_of, chains, w_in, w_out, capacity, terms, n_blk):
    slots, rows, cols, channels = pair.shape
    hidden = w_out.shape[1]
    far = n_blk // 2
    calls = [[far], [s for s in range(1, n_blk) if s != far] + [0]]
    layers = w_in.shape[0]
    current = pair
    bands = [[12, 20], [14, 18]]
    for layer in range(layers):
        if layer == 0:
            gate, lefts, rights = open_operands(ids, blocks, pair, chains, w_in, hidden, bands[0])
        exchange = exchange_bands_incoming if layer % 2 else exchange_bands_outgoing
        arrived, last_made = [], None
        for left, right in exchange(lefts, rights):
            parts = [None] * n_blk
            for shifts in calls:
                if last_made is not None:
                    ids = after(ids, last_made)
                made = banded_products(shifts, ids, owners, slot_of, left, right, capacity, slots, terms, cols)
                last_made = made[-1]
                for shift, part in zip(shifts, made):
                    if shift:
                        if arrived:
                            part = after(part, arrived[-1][shift])
                        part = lax.ppermute(part, "blk", [(p, (p + shift) % n_blk) for p in range(n_blk)])
                    parts[shift] = part
            arrived.append(parts)
        last = layer == layers - 1
        out = close_layer(
            layer, arrived, ids, blocks, owners, current, gate, w_out, capacity, terms, chains, w_in, last, bands
        )
        if last:
            return out
        current, gate, lefts, rights = out


def per_device(pair, block_list, term_owner, term_slots, chain_ids, w_in, w_out):
    n_blk = lax.axis_size("blk")
    n_chan = lax.axis_size("chan")
    n_sub = lax.axis_size("sub")
    position = lax.axis_index("blk")
    row_group = lax.axis_index("chan")
    col_group = lax.axis_index("sub")
    slots, rows, cols, channels = pair.shape
    hidden = w_out.shape[1]
    terms = term_owner.shape[1]
    capacity = max(2, -(-slots * terms // n_blk))
    fast = n_chan == 2 and n_sub == 2
    on_diagonal = (row_group == col_group).astype(jnp.int32)
    ids = jnp.stack([position, row_group, col_group, on_diagonal]).astype(jnp.int32)
    blocks = block_list.T
    owners = term_owner.T
    slot_of = jnp.transpose(term_slots, (1, 2, 0))
    chains = chain_ids.reshape(-1, 128)
    if fast and rows == cols == 32 and channels == hidden == 128:
        return banded(pair, ids, blocks, owners, slot_of, chains, w_in, w_out, capacity, terms, n_blk)
    shifts = [n_blk // 2] + [s for s in range(1, n_blk) if s != n_blk // 2] + [0]

    def all_products(lefts, right):
        parts = [None] * n_blk
        for shift in shifts:
            made = term_products(shift, ids, owners, slot_of, lefts, right, capacity, slots, terms)
            if shift:
                pairs = [(p, (p + shift) % n_blk) for p in range(n_blk)]
                made = lax.ppermute(made, "blk", pairs)
            parts[shift] = made
        return parts

    def at_home(layer, parts, current, gate, at, of, into=None):
        last = layer == w_in.shape[0] - 1
        return home(
            layer, parts, ids, blocks, owners, current, gate, w_out, capacity, terms, at, of, chains, w_in, last, into
        )

    gate, left, *rights = first_operands(ids, blocks, pair, chains, w_in, hidden, 2 if fast else 1)
    lefts, chunks = exchange_outgoing(left, rights, n_chan, n_sub)
    count = len(chunks)
    made = [all_products(lefts, right) for right in chunks]
    homes = [at_home(0, parts, pair, gate, at, count) for at, parts in enumerate(made)]
    lefts, chunks = exchange_incoming([h[2] for h in homes], [h[3] for h in homes], n_chan, n_sub)
    made = [all_products(lefts, right) for right in chunks]
    out = None
    for at, parts in enumerate(made):
        (out,) = at_home(1, parts, homes[at][0], homes[at][1], at, count, into=out)
    return out


def solution(mesh):
    in_specs = (
        P(("groups", "blk"), "chan", "sub", None),
        P("groups", None),
        P("groups", None),
        P("groups", None, None),
        P("groups"),
        P(),
        P(),
    )
    out_specs = P(("groups", "blk"), "chan", "sub", None)
    return jax.shard_map(
        per_device, mesh=mesh, in_specs=in_specs, out_specs=out_specs, check_vma=False
    )
```

```python
import functools

import jax
import jax.numpy as jnp
from jax import lax
from jax.experimental import pallas as pl
from jax.experimental.pallas import tpu as pltpu
from jax.sharding import PartitionSpec as P

norm_epsilon = 1e-05
vmem_limit = 56 * 1024 * 1024


def sigmoid(values):
    return 0.5 + 0.5 * jnp.tanh(0.5 * values)


def layer_norm(values):
    values = values.astype(jnp.float32)
    centred = values - jnp.mean(values, axis=-1, keepdims=True)
    variance = jnp.mean(centred * centred, axis=-1, keepdims=True)
    return centred * lax.rsqrt(variance + norm_epsilon)


def alive_rows(chain_ref, start, size):
    lanes = chain_ref.shape[1]
    line = chain_ref[pl.ds(start // lanes, 1), :] >= 0
    spot = lax.broadcasted_iota(jnp.int32, (size, lanes), 0) + lax.rem(start, lanes)
    pick = jnp.logical_and(lax.broadcasted_iota(jnp.int32, (size, lanes), 1) == spot, line)
    return dot(pick.astype(jnp.float32).astype(jnp.bfloat16), jnp.ones((lanes, lanes), jnp.bfloat16))


def dot(a, b):
    return jnp.dot(a, b, preferred_element_type=jnp.float32)


def gated_pair(projected, mask, hidden):
    left = mask * sigmoid(projected[:, hidden : 2 * hidden]) * projected[:, :hidden]
    right = mask * sigmoid(projected[:, 3 * hidden : 4 * hidden]) * projected[:, 2 * hidden : 3 * hidden]
    return left.astype(jnp.bfloat16), right.astype(jnp.bfloat16)


def first_kernel(hidden, row_parts, n_chan, n_sub, ids, blocks, pair_ref, chain_ref, w_ref, gate_ref, left_ref, *rest):
    right_refs, (norm_ref, turned_ref) = rest[:row_parts], rest[row_parts:]
    slots = pl.num_programs(0)
    _, rows, cols, channels = pair_ref.shape
    block = ids[0] * slots + pl.program_id(0)
    row_alive = alive_rows(chain_ref, (blocks[0, block] * n_chan + ids[1]) * rows, rows)
    col_alive = alive_rows(chain_ref, (blocks[1, block] * n_sub + ids[2]) * cols, cols)
    group = max(1, 256 // cols)
    for start in range(0, rows, group):
        at = pl.ds(start, group)
        normed = layer_norm(pair_ref[0, at].reshape(group * cols, channels))
        norm_ref[pl.ds(start * cols, group * cols), :] = normed
        gate = sigmoid(dot(normed.astype(jnp.bfloat16), w_ref[0, :, 4 * hidden :]))
        gate_ref[0, at] = gate.reshape(group, cols, channels)
    for col in range(cols):
        turned_ref[col] = norm_ref[pl.ds(col, rows, stride=cols), :].astype(jnp.bfloat16)
    step = max(1, 128 // rows)
    part = rows // row_parts
    for start in range(0, cols, step):
        taken = turned_ref[start : start + step].reshape(step * rows, channels)
        projected = dot(taken, w_ref[0, :, : 4 * hidden])
        mask = col_alive[start : start + step][:, None, :] * row_alive[None, :, :]
        left, right = gated_pair(projected, mask.reshape(step * rows, -1), hidden)
        left_ref[0, start : start + step] = left.reshape(step, rows, hidden)
        right = right.reshape(step, rows, hidden)
        for p, right_ref in enumerate(right_refs):
            right_ref[0, start : start + step] = right[:, p * part : (p + 1) * part]


def first_operands(ids, blocks, pair, chains, w_in, hidden, row_parts):
    slots, rows, cols, channels = pair.shape
    part = rows // row_parts
    operand = jax.ShapeDtypeStruct((slots, cols, rows, hidden), jnp.bfloat16)
    right = jax.ShapeDtypeStruct((slots, cols, part, hidden), jnp.bfloat16)
    return pl.pallas_call(
        functools.partial(first_kernel, hidden, row_parts, lax.axis_size("chan"), lax.axis_size("sub")),
        grid_spec=pltpu.PrefetchScalarGridSpec(
            num_scalar_prefetch=2,
            grid=(slots,),
            in_specs=[
                pl.BlockSpec((1, rows, cols, channels), lambda s, *_: (s, 0, 0, 0)),
                pl.BlockSpec(chains.shape, lambda s, *_: (0, 0)),
                pl.BlockSpec((1,) + w_in.shape[1:], lambda s, *_: (0, 0, 0)),
            ],
            out_specs=[
                pl.BlockSpec((1, rows, cols, channels), lambda s, *_: (s, 0, 0, 0)),
                pl.BlockSpec((1, cols, rows, hidden), lambda s, *_: (s, 0, 0, 0)),
            ]
            + [pl.BlockSpec((1, cols, part, hidden), lambda s, *_: (s, 0, 0, 0))] * row_parts,
            scratch_shapes=[
                pltpu.VMEM((rows * cols, channels), jnp.float32),
                pltpu.VMEM((cols, rows, channels), jnp.bfloat16),
            ],
        ),
        out_shape=[jax.ShapeDtypeStruct(pair.shape, jnp.float32), operand] + [right] * row_parts,
        compiler_params=pltpu.CompilerParams(vmem_limit_bytes=vmem_limit),
        name="first_operands",
    )(ids, blocks, pair, chains, w_in)


def product_kernel(shift, n_blk, slots_dev, terms, capacity, pieces, n_refs, ids, owners, slots, *rest):
    refs = rest[:n_refs]
    out_ref, left_held, right_held, right_wide, chosen, sems = rest[n_refs:]
    step = pl.program_id(0)
    turn = lax.rem(step, 2)
    _, depth, n_i, hidden = left_held.shape
    n_j = right_wide.shape[1]

    @pl.when(step == 0)
    def _():
        target = lax.rem(ids[0] + shift, n_blk)
        for e in range(2 * capacity):
            chosen[e] = 0

        def scan(e, count):
            block, term = target * slots_dev + e // terms, lax.rem(e, terms)
            here = jnp.logical_and(owners[term, block] == ids[0], count < capacity)

            @pl.when(here)
            def _():
                chosen[2 * count] = slots[term, 0, block]
                chosen[2 * count + 1] = slots[term, 1, block]

            return count + here.astype(jnp.int32)

        lax.fori_loop(0, slots_dev * terms, scan, jnp.int32(0))

    def copy(n, term, buffer, source):
        side, _, _, k0, depth_of, i0, size = pieces[n]
        held = (left_held, right_held)[side]
        return pltpu.make_async_copy(
            refs[source].at[chosen[2 * term + side]],
            held.at[buffer, pl.ds(k0, depth_of), pl.ds(i0, size), :],
            sems.at[buffer, n],
        )

    def start(term, buffer):
        for n, (_, on, off, *_) in enumerate(pieces):
            if on == off:
                copy(n, term, buffer, on).start()
            else:

                @pl.when(ids[3] == 1)
                def _(n=n, on=on):
                    copy(n, term, buffer, on).start()

                @pl.when(ids[3] == 0)
                def _(n=n, off=off):
                    copy(n, term, buffer, off).start()

    @pl.when(step == 0)
    def _():
        start(0, 0)

    @pl.when(step + 1 < capacity)
    def _():
        start(step + 1, 1 - turn)

    for n, piece in enumerate(pieces):
        copy(n, step, turn, piece[1]).wait()

    span = 8

    def widen(n, carry):
        at = pl.ds(n * span, span)
        right_wide[at] = right_held[turn, at].astype(jnp.float32)
        return carry

    lax.fori_loop(0, depth // span, widen, 0)

    group = min(8, n_j)
    unroll = 4
    for j0 in range(0, n_j, group):

        def body(n, sums):
            for u in range(unroll):
                k = n * unroll + u
                left = left_held[turn, k].astype(jnp.float32).reshape(n_i // 8, 8, hidden)
                sums = tuple(
                    total + left * right_wide[k, pl.ds(j0 + j, 8, stride=0), :][None]
                    for j, total in enumerate(sums)
                )
            return sums

        zero = jnp.zeros((n_i // 8, 8, hidden), jnp.float32)
        sums = lax.fori_loop(0, depth // unroll, body, (zero,) * group)
        for j, total in enumerate(sums):
            out_ref[0, j0 + j] = total.reshape(n_i, hidden).astype(jnp.bfloat16)


def term_products(shift, ids, owners, slots, lefts, rights, capacity, slots_dev, terms):
    n_blk = lax.axis_size("blk")
    refs, pieces = [], []

    def index_of(array):
        for n, known in enumerate(refs):
            if known is array:
                return n
        refs.append(array)
        return len(refs) - 1

    for side, operands in ((0, lefts), (1, rights)):
        for on, off, k0, i0 in operands:
            pieces.append((side, index_of(on), index_of(off), k0, on.shape[1], i0, on.shape[2]))
    hidden = lefts[0][0].shape[3]
    n_i = max(p[5] + p[6] for p in pieces if p[0] == 0)
    n_j = max(p[5] + p[6] for p in pieces if p[0] == 1)
    depth = max(p[3] + p[4] for p in pieces)
    return pl.pallas_call(
        functools.partial(
            product_kernel, shift, n_blk, slots_dev, terms, capacity, tuple(pieces), len(refs)
        ),
        grid_spec=pltpu.PrefetchScalarGridSpec(
            num_scalar_prefetch=3,
            grid=(capacity,),
            in_specs=[pl.BlockSpec(memory_space=pl.ANY)] * len(refs),
            out_specs=pl.BlockSpec((1, n_j, n_i, hidden), lambda t, *_: (t, 0, 0, 0)),
            scratch_shapes=[
                pltpu.VMEM((2, depth, n_i, hidden), jnp.bfloat16),
                pltpu.VMEM((2, depth, n_j, hidden), jnp.bfloat16),
                pltpu.VMEM((depth, n_j, hidden), jnp.float32),
                pltpu.SMEM((2 * capacity,), jnp.int32),
                pltpu.SemaphoreType.DMA((2, len(pieces))),
            ],
        ),
        out_shape=jax.ShapeDtypeStruct((capacity, n_j, n_i, hidden), jnp.bfloat16),
        compiler_params=pltpu.CompilerParams(vmem_limit_bytes=vmem_limit),
        cost_estimate=pl.CostEstimate(
            flops=2 * capacity * n_i * n_j * depth * hidden * 100,
            bytes_accessed=capacity * (depth * (n_i + n_j) + n_i * n_j) * hidden * 2,
            transcendentals=0,
        ),
        name="term_products",
    )(ids, owners, slots, *refs)


def home_kernel(last, hidden, n_blk, n_chan, n_sub, at, of, slots_dev, terms, capacity, ids, blocks, owners, *rest):
    parts, rest = rest[:n_blk], rest[n_blk:]
    scratch, rest = rest[-5:], rest[:-5]
    held, turned, place, seen, sems = scratch
    cur_ref, gate_ref, w_out_ref = rest[:3]
    if last:
        out_ref = rest[-1]
    else:
        chain_ref, w_ref, out_ref, next_gate_ref, left_ref, right_ref = rest[3:]
    step = pl.program_id(0)
    _, rows, cols, channels = cur_ref.shape

    def arrival(shift):
        return pltpu.make_async_copy(parts[shift], held.at[pl.ds(shift * capacity, capacity)], sems.at[shift])

    @pl.when(step == 0)
    def _():
        for shift in range(n_blk):
            arrival(shift).start()
            seen[shift] = 0

        def scan(e, carry):
            owner = owners[lax.rem(e, terms), ids[0] * slots_dev + e // terms]
            shift = lax.rem(ids[0] - owner + n_blk, n_blk)
            count = seen[owner]
            seen[owner] = count + 1
            place[e] = shift * capacity + count
            return carry

        lax.fori_loop(0, slots_dev * terms, scan, jnp.int32(0))
        for shift in range(n_blk):
            arrival(shift).wait()

    if not last:
        block = ids[0] * slots_dev + step
        row_alive = alive_rows(chain_ref, (blocks[0, block] * n_chan + ids[1]) * rows, rows)
        col_alive = alive_rows(chain_ref, ((blocks[1, block] * n_sub + ids[2]) * of + at) * cols, cols)
    span = max(1, 128 // rows)
    for start in range(0, cols, span):
        taken = pl.ds(start, span)
        total = held[place[step * terms], taken].astype(jnp.float32)
        for t in range(1, terms):
            total = total + held[place[step * terms + t], taken].astype(jnp.float32)
        rounded = total.astype(jnp.bfloat16).astype(jnp.float32)
        turned[pl.ds(start * rows, span * rows), :] = rounded.reshape(span * rows, hidden)
    group = min(rows, max(1, 256 // cols))
    for start in range(0, rows, group):
        taken = pl.ds(start, group)
        mixture = jnp.concatenate(
            [turned[pl.ds(row, cols, stride=rows), :].astype(jnp.bfloat16) for row in range(start, start + group)]
        )
        update = dot(layer_norm(mixture).astype(jnp.bfloat16), w_out_ref[0])
        current = cur_ref[0, taken].astype(jnp.float32).reshape(group * cols, channels)
        gate = gate_ref[0, taken].reshape(group * cols, channels)
        result = (current + gate * update).astype(jnp.bfloat16)
        out_ref[0, taken] = result.reshape(group, cols, channels)
        if not last:
            normed = layer_norm(result).astype(jnp.bfloat16)
            projected = dot(normed, w_ref[0])
            next_gate_ref[0, taken] = sigmoid(projected[:, 4 * hidden :]).reshape(group, cols, channels)
            mask = row_alive[start : start + group][:, None, :] * col_alive[None, :, :]
            left, right = gated_pair(projected, mask.reshape(group * cols, channels), hidden)
            left_ref[0, taken] = left.reshape(group, cols, hidden)
            right_ref[0, taken] = right.reshape(group, cols, hidden)


def home(layer, parts, ids, blocks, owners, current, gate, w_out, capacity, terms, at, of, chains, w_in, last, into=None):
    n_blk = len(parts)
    slots, rows, _, channels = current.shape
    hidden = w_out.shape[1]
    cols = parts[0].shape[1]
    chunk = (1, rows, cols, channels)

    def chunk_spec(array):
        whole = array.shape[2] != cols
        return pl.BlockSpec(chunk, lambda s, *_: (s, 0, at if whole else 0, 0))

    def layer_spec(array, index):
        return pl.BlockSpec((1,) + array.shape[1:], lambda s, *_: (index, 0, 0))

    in_specs = [pl.BlockSpec(memory_space=pl.ANY)] * n_blk + [
        chunk_spec(current),
        chunk_spec(gate),
        layer_spec(w_out, layer),
    ]
    operands = [*parts, current, gate, w_out]
    aliases = {}
    if last:
        if into is not None:
            aliases = {3 + len(operands): 0}
            operands.append(into)
            in_specs.append(pl.BlockSpec(memory_space=pl.ANY))
        out_shape = [jax.ShapeDtypeStruct((slots, rows, cols * of, channels), jnp.bfloat16)]
        out_specs = [pl.BlockSpec(chunk, lambda s, *_: (s, 0, at, 0))]
    else:
        operands += [chains, w_in]
        in_specs += [pl.BlockSpec(chains.shape, lambda s, *_: (0, 0)), layer_spec(w_in, layer + 1)]
        small = (slots, rows, cols, channels)
        out_shape = [jax.ShapeDtypeStruct(small, t) for t in (jnp.bfloat16, jnp.float32, jnp.bfloat16, jnp.bfloat16)]
        out_specs = [pl.BlockSpec(chunk, lambda s, *_: (s, 0, 0, 0))] * 4
    return pl.pallas_call(
        functools.partial(
            home_kernel, last, hidden, n_blk, lax.axis_size("chan"), lax.axis_size("sub"), at, of, slots, terms, capacity
        ),
        grid_spec=pltpu.PrefetchScalarGridSpec(
            num_scalar_prefetch=3,
            grid=(slots,),
            in_specs=in_specs,
            out_specs=out_specs,
            scratch_shapes=[
                pltpu.VMEM((n_blk * capacity, cols, rows, hidden), jnp.bfloat16),
                pltpu.VMEM((rows * cols, hidden), jnp.float32),
                pltpu.SMEM((slots * terms,), jnp.int32),
                pltpu.SMEM((n_blk,), jnp.int32),
                pltpu.SemaphoreType.DMA((n_blk,)),
            ],
        ),
        out_shape=out_shape,
        input_output_aliases=aliases,
        compiler_params=pltpu.CompilerParams(vmem_limit_bytes=vmem_limit),
        cost_estimate=pl.CostEstimate(
            flops=2 * slots * rows * cols * channels * 6 * channels * 10,
            bytes_accessed=slots * rows * cols * channels * 16,
            transcendentals=0,
        ),
        name="home",
    )(ids, blocks, owners, *operands)


def exchange_outgoing(left, rights, n_chan, n_sub):
    if n_chan == 2 and n_sub == 2:
        both = ("chan", "sub")
        other_left = lax.ppermute(left, "sub", [(0, 1), (1, 0)])
        lefts = [(other_left, left, 0, 0), (left, other_left, left.shape[1], 0)]
        chunks = []
        for right in rights:
            if chunks:
                (one, *_), (_, two, *_) = chunks[-1]
                right, *_ = lax.optimization_barrier((right, one, two))
            one = lax.ppermute(right, both, [(0, 2), (3, 1), (1, 0), (2, 3)])
            two = lax.ppermute(right, both, [(1, 2), (2, 1)])
            chunks.append([(one, one, 0, 0), (right, two, right.shape[1], 0)])
        return lefts, chunks
    left = lax.all_gather(left, "sub", axis=1, tiled=True)
    right = jnp.concatenate(rights, axis=2)
    right = lax.all_gather(right, "chan", axis=2, tiled=True)
    right = lax.all_to_all(right, "sub", split_axis=2, concat_axis=1, tiled=True)
    cols = right.shape[2] // 2
    chunks = [right[:, :, :cols], right[:, :, cols:]]
    return [(left, left, 0, 0)], [[(r, r, 0, 0)] for r in chunks]


def exchange_incoming(lefts, rights, n_chan, n_sub):
    if n_chan == 2 and n_sub == 2:
        both = ("chan", "sub")
        left_pieces, chunks = [], []
        at = 0
        for left, right in zip(lefts, rights):
            depth = left.shape[1]
            one = lax.ppermute(left, both, [(1, 3), (2, 0), (0, 1), (3, 2)])
            two = lax.ppermute(one, both, [(0, 1), (3, 2)])
            left_pieces += [(left, one, 0, at), (one, two, depth, at)]
            other = lax.ppermute(right, "chan", [(0, 1), (1, 0)])
            chunks.append([(right, right, 0, 0), (other, other, depth, 0)])
            at += left.shape[2]
        return left_pieces, chunks
    left = lax.all_gather(jnp.concatenate(lefts, axis=2), "chan", axis=1, tiled=True)
    left = lax.all_gather(left, "sub", axis=2, tiled=True)
    size = left.shape[2] // n_chan
    left = lax.dynamic_slice_in_dim(left, lax.axis_index("chan") * size, size, 2)
    gathered = [lax.all_gather(right, "chan", axis=1, tiled=True) for right in rights]
    return [(left, left, 0, 0)], [[(r, r, 0, 0)] for r in gathered]


def lane_group(shape, size):
    return lax.broadcasted_iota(jnp.int32, shape, 1) // size


def exchange_groups(tiles, size):
    tiles = list(tiles)
    lanes = tiles[0].shape[1]
    group = lane_group(tiles[0].shape, size)
    distance = len(tiles) // 2
    while distance:
        low = lax.rem(group // distance, 2) == 0
        for a in range(len(tiles)):
            if not a & distance:
                x, y = tiles[a], tiles[a + distance]
                tiles[a] = jnp.where(low, x, pltpu.roll(y, distance * size, 1))
                tiles[a + distance] = jnp.where(low, pltpu.roll(x, lanes - distance * size, 1), y)
        distance //= 2
    return tiles


def swap_matrix(half):
    shape = (half * half, half * half)
    to, of = lax.broadcasted_iota(jnp.int32, shape, 0), lax.broadcasted_iota(jnp.int32, shape, 1)
    same = jnp.logical_and(to // half == lax.rem(of, half), lax.rem(to, half) == of // half)
    return same.astype(jnp.float32).astype(jnp.bfloat16)


def swapped(values, swap_ref):
    half, _, lanes = values.shape
    moved = dot(swap_ref[...], values.reshape(half * half, lanes))
    return moved.astype(jnp.bfloat16).reshape(half, half, lanes)


def turn(taken, turned, swap_ref):
    half = 16
    for x in range(0, taken.shape[0], half):
        for y in range(0, taken.shape[1], half):
            turned[y : y + half, x : x + half] = swapped(taken[x : x + half, y : y + half], swap_ref)


def make_operand(side, taken, row_alive, inner_alive, w_ref, out_refs, laid, swap_ref):
    rows, size, hidden = taken.shape
    parts, bands, half = hidden // size, size, 16
    groups = rows // parts
    weights = w_ref[0, :, 2 * side * hidden : (2 * side + 2) * hidden]
    step = 2 * parts
    for start in range(0, rows, step):
        made = dot(taken[start : start + step].reshape(step * size, hidden), weights)
        mask = (row_alive[start : start + step, None, :] * inner_alive[None, :, :]).reshape(step * size, hidden)
        value = mask * sigmoid(made[:, hidden:]) * made[:, :hidden]
        for first in range(0, step, parts):
            tiles = [value[(first + a) * size : (first + a + 1) * size] for a in range(parts)]
            for part, tile in enumerate(exchange_groups(tiles, size)):
                at = slice(part * size, (part + 1) * size)
                laid[side, (start + first) // parts, at, :] = tile.astype(jnp.bfloat16)
    blocks = [laid[side, g].T for g in range(groups)]
    starts = [sum(ref.shape[1] for ref in out_refs[:n]) for n in range(len(out_refs))]
    for first in range(0, bands, half):
        for row in range(0, rows, half):
            tiles = []
            for r in range(row, row + half):
                at = r % parts * bands + first
                tiles.append(blocks[r // parts][at : at + half])
            moved = swapped(jnp.stack(tiles), swap_ref)
            for start, ref in zip(starts, out_refs):
                low, high = max(start, first), min(start + ref.shape[1], first + half)
                if low < high:
                    ref[0, low - start : high - start, row : row + half] = moved[low - first : high - first]


def open_layer(layer, natural, chain_ref, row_start, col_start, w_ref, left_refs, right_refs, laid, turned, swap):
    rows, cols, hidden = natural.shape
    turn(natural, turned, swap)
    row_alive, col_alive = alive_rows(chain_ref, row_start, rows), alive_rows(chain_ref, col_start, cols)
    for side, refs in ((0, left_refs), (1, right_refs)):
        if side == layer % 2:
            make_operand(side, natural, row_alive, col_alive, w_ref, refs, laid, swap)
        else:
            make_operand(side, turned[...], col_alive, row_alive, w_ref, refs, laid, swap)


def open_kernel(hidden, chunks, n_chan, n_sub, ids, blocks, pair_ref, chain_ref, w_ref, gate_ref, *rest):
    left_refs, right_refs = rest[:chunks], rest[chunks : 2 * chunks]
    norm_ref, laid, turned, swap = rest[2 * chunks :]
    slots = pl.num_programs(0)
    step = pl.program_id(0)
    _, rows, cols, channels = pair_ref.shape
    block = ids[0] * slots + step

    @pl.when(step == 0)
    def _():
        swap[...] = swap_matrix(16)

    group = hidden // cols
    for start in range(0, rows, group):
        at = pl.ds(start, group)
        normed = layer_norm(pair_ref[0, at].reshape(group * cols, channels)).astype(jnp.bfloat16)
        gate = sigmoid(dot(normed, w_ref[0, :, 4 * hidden :]))
        gate_ref[0, at] = gate.reshape(group, cols, channels)
        norm_ref[at] = normed.reshape(group, cols, channels)
    row_start, col_start = (blocks[0, block] * n_chan + ids[1]) * rows, (blocks[1, block] * n_sub + ids[2]) * cols
    open_layer(0, norm_ref[...], chain_ref, row_start, col_start, w_ref, left_refs, right_refs, laid, turned, swap)


def operand_scratch(rows, size, hidden):
    parts = hidden // size
    return [
        pltpu.VMEM((2, rows // parts, parts * size, hidden), jnp.bfloat16),
        pltpu.VMEM((size, rows, hidden), jnp.bfloat16),
        pltpu.VMEM((256, 256), jnp.bfloat16),
    ]


def open_operands(ids, blocks, pair, chains, w_in, hidden, bands):
    slots, rows, cols, channels = pair.shape
    operands = [jax.ShapeDtypeStruct((slots, count, rows, hidden), jnp.bfloat16) for count in bands] * 2
    out = pl.pallas_call(
        functools.partial(open_kernel, hidden, len(bands), lax.axis_size("chan"), lax.axis_size("sub")),
        grid_spec=pltpu.PrefetchScalarGridSpec(
            num_scalar_prefetch=2,
            grid=(slots,),
            in_specs=[
                pl.BlockSpec((1, rows, cols, channels), lambda s, *_: (s, 0, 0, 0)),
                pl.BlockSpec(chains.shape, lambda s, *_: (0, 0)),
                pl.BlockSpec((1,) + w_in.shape[1:], lambda s, *_: (0, 0, 0)),
            ],
            out_specs=[pl.BlockSpec((1, rows, cols, channels), lambda s, *_: (s, 0, 0, 0))]
            + [pl.BlockSpec((1,) + o.shape[1:], lambda s, *_: (s, 0, 0, 0)) for o in operands],
            scratch_shapes=[pltpu.VMEM((rows, cols, channels), jnp.bfloat16)] + operand_scratch(rows, cols, hidden),
        ),
        out_shape=[jax.ShapeDtypeStruct(pair.shape, jnp.float32)] + operands,
        compiler_params=pltpu.CompilerParams(vmem_limit_bytes=vmem_limit),
        name="open_operands",
    )(ids, blocks, pair, chains, w_in)
    return out[0], out[1 : 1 + len(bands)], out[1 + len(bands) :]


def plan_kernel(n_blk, slots_dev, terms, capacity, ids, owners, slots, chosen, place, seen):
    for e in range(2 * n_blk * capacity):
        chosen[e] = 0
    for shift in range(n_blk):
        seen[shift] = 0
        target = lax.rem(ids[0] + shift, n_blk)

        def scan(e, found):
            block, term = target * slots_dev + e // terms, lax.rem(e, terms)
            here = jnp.logical_and(owners[term, block] == ids[0], found < capacity)

            @pl.when(here)
            def _():
                chosen[2 * (shift * capacity + found)] = slots[term, 0, block]
                chosen[2 * (shift * capacity + found) + 1] = slots[term, 1, block]

            return found + here.astype(jnp.int32)

        lax.fori_loop(0, slots_dev * terms, scan, jnp.int32(0))

    def own(e, carry):
        owner = owners[lax.rem(e, terms), ids[0] * slots_dev + e // terms]
        count = seen[owner]
        seen[owner] = count + 1
        place[e] = lax.rem(ids[0] - owner + n_blk, n_blk) * capacity + count
        return carry

    lax.fori_loop(0, slots_dev * terms, own, jnp.int32(0))


def make_plan(ids, owners, slots, n_blk, slots_dev, terms, capacity):
    scalars = pl.BlockSpec(memory_space=pltpu.SMEM)
    return pl.pallas_call(
        functools.partial(plan_kernel, n_blk, slots_dev, terms, capacity),
        in_specs=[scalars] * 3,
        out_specs=[scalars] * 2,
        out_shape=[
            jax.ShapeDtypeStruct((2 * n_blk * capacity,), jnp.int32),
            jax.ShapeDtypeStruct((slots_dev * terms,), jnp.int32),
        ],
        scratch_shapes=[pltpu.SMEM((n_blk,), jnp.int32)],
        name="make_plan",
    )(ids, owners, slots)


def banded_kernel(shifts, capacity, pieces, n_refs, size, ids, chosen, *rest):
    refs, rest = rest[:n_refs], rest[n_refs:]
    out_refs, (left_held, right_held, out_held, sems, out_sems) = rest[: len(shifts)], rest[len(shifts) :]
    halves, _, bands, rows, hidden = left_held.shape
    parts = hidden // size

    def copy(n, source):
        side, half, *_ = pieces[n]
        return pltpu.make_async_copy(refs[source], (left_held, right_held)[side].at[half], sems.at[n])

    for n, (_, _, on, off) in enumerate(pieces):
        if on == off:
            copy(n, on).start()
        else:

            @pl.when(ids[3] == 1)
            def _(n=n, on=on):
                copy(n, on).start()

            @pl.when(ids[3] == 0)
            def _(n=n, off=off):
                copy(n, off).start()

    for n, piece in enumerate(pieces):
        copy(n, piece[2]).wait()

    def leave(n):
        return pltpu.make_async_copy(out_held.at[pl.ds(n * capacity, capacity)], out_refs[n], out_sems.at[n])

    for n, shift in enumerate(shifts):

        def one(term, carry, n=n, shift=shift):
            at = 2 * (shift * capacity + term)
            left_slot, right_slot = chosen[at], chosen[at + 1]
            group = lane_group((size, hidden), size)
            for band in range(bands):
                left = jnp.concatenate([left_held[h, left_slot, band] for h in range(halves)], axis=1)
                apart = []
                for h in range(halves):
                    right = right_held[h, right_slot, band]
                    apart += [jnp.where(group == part, right, jnp.zeros_like(right)) for part in range(parts)]
                made = dot(left, jnp.concatenate(apart, axis=0))
                out_held[n * capacity + term, band] = made.astype(jnp.bfloat16)
            return carry

        lax.fori_loop(0, capacity, one, 0)
        leave(n).start()
    for n in range(len(shifts)):
        leave(n).wait()


def banded_products(shifts, ids, chosen, lefts, rights, capacity, size):
    refs, pieces = [], []

    def index_of(array):
        for n, known in enumerate(refs):
            if known is array:
                return n
        refs.append(array)
        return len(refs) - 1

    for side, operands in ((0, lefts), (1, rights)):
        for half, (on, off) in enumerate(operands):
            pieces.append((side, half, index_of(on), index_of(off)))
    slots, bands, rows, hidden = lefts[0][0].shape
    count = len(shifts) * capacity
    anywhere = pl.BlockSpec(memory_space=pl.ANY)
    return pl.pallas_call(
        functools.partial(banded_kernel, shifts, capacity, tuple(pieces), len(refs), size),
        grid_spec=pltpu.PrefetchScalarGridSpec(
            num_scalar_prefetch=2,
            grid=(),
            in_specs=[anywhere] * len(refs),
            out_specs=[anywhere] * len(shifts),
            scratch_shapes=[
                pltpu.VMEM((len(lefts), slots, bands, rows, hidden), jnp.bfloat16),
                pltpu.VMEM((len(rights), slots, bands, size, hidden), jnp.bfloat16),
                pltpu.VMEM((count, bands, rows, hidden), jnp.bfloat16),
                pltpu.SemaphoreType.DMA((len(pieces),)),
                pltpu.SemaphoreType.DMA((len(shifts),)),
            ],
        ),
        out_shape=[jax.ShapeDtypeStruct((capacity, bands, rows, hidden), jnp.bfloat16)] * len(shifts),
        compiler_params=pltpu.CompilerParams(vmem_limit_bytes=vmem_limit),
        cost_estimate=pl.CostEstimate(
            flops=2 * count * bands * rows * hidden * hidden * len(lefts), bytes_accessed=1, transcendentals=0
        ),
        name="banded_products",
    )(ids, chosen, *refs)


def close_kernel(layer, last, n_parts, n_blk, n_chan, n_sub, slots_dev, terms, capacity, ids, blocks, place, *rest):
    chunks = n_parts // n_blk
    arrived, rest = rest[:n_parts], rest[n_parts:]
    cur_ref, gate_ref, w_out_ref = rest[:3]
    if last:
        out_ref, held, sems, swap = rest[3:]
    else:
        chain_ref, w_ref, out_ref, next_gate_ref = rest[3:7]
        left_refs, right_refs = rest[7 : 7 + chunks], rest[7 + chunks : 7 + 2 * chunks]
        held, sems, norm_ref, laid, turned, swap = rest[7 + 2 * chunks :]
    step = pl.program_id(0)
    _, rows, cols, channels = cur_ref.shape
    _, bands, _, hidden = held.shape
    parts, size = hidden // bands, bands

    def arrival(n):
        at = sum(arrived[m * n_blk].shape[1] for m in range(n // n_blk))
        count = arrived[n].shape[1]
        target = held.at[pl.ds(n % n_blk * capacity, capacity), pl.ds(at, count)]
        return pltpu.make_async_copy(arrived[n], target, sems.at[n])

    @pl.when(step == 0)
    def _():
        for n in range(n_parts):
            arrival(n).start()
        swap[...] = swap_matrix(16)
        for n in range(n_parts):
            arrival(n).wait()

    half = 16
    by_row = [[] for _ in range(rows)]
    for row in range(0, rows, half):
        for band in range(0, bands, half):
            taken = pl.ds(band, half), pl.ds(row, half)
            total = held[(place[step * terms], *taken)].astype(jnp.float32)
            for t in range(1, terms):
                total = total + held[(place[step * terms + t], *taken)].astype(jnp.float32)
            moved = swapped(total.astype(jnp.bfloat16), swap)
            for r in range(half):
                by_row[row + r].append(moved[r])
    for g in range(rows // parts):
        block = jnp.concatenate([x for a in range(parts) for x in by_row[g * parts + a]]).T
        block = block.astype(jnp.float32)
        tiles = [block[p * cols : (p + 1) * cols] for p in range(parts)]
        mixture = jnp.concatenate(exchange_groups(tiles, size))
        change = dot(layer_norm(mixture).astype(jnp.bfloat16), w_out_ref[0])
        taken = pl.ds(g * parts, parts)
        gate = gate_ref[0, taken].reshape(parts * cols, channels)
        current = cur_ref[0, taken].astype(jnp.float32).reshape(parts * cols, channels)
        result = (current + gate * change).astype(jnp.bfloat16)
        out_ref[0, taken] = result.reshape(parts, cols, channels)
        if not last:
            norm = layer_norm(result).astype(jnp.bfloat16)
            norm_ref[taken] = norm.reshape(parts, cols, channels)
            next_gate = sigmoid(dot(norm, w_ref[0, :, 4 * hidden :]))
            next_gate_ref[0, taken] = next_gate.reshape(parts, cols, channels)
    if not last:
        block = ids[0] * slots_dev + step
        starts = (blocks[0, block] * n_chan + ids[1]) * rows, (blocks[1, block] * n_sub + ids[2]) * cols
        open_layer(layer + 1, norm_ref[...], chain_ref, *starts, w_ref, left_refs, right_refs, laid, turned, swap)


def close_layer(layer, arrived, ids, blocks, place, current, gate, w_out, capacity, terms, chains, w_in, last, bands):
    n_blk = len(arrived[0])
    flat = [part for chunk in arrived for part in chunk]
    slots, rows, cols, channels = current.shape
    hidden = w_out.shape[1]
    whole = pl.BlockSpec((1, rows, cols, channels), lambda s, *_: (s, 0, 0, 0))

    def layer_spec(array, index):
        return pl.BlockSpec((1,) + array.shape[1:], lambda s, *_: (index, 0, 0))

    in_specs = [pl.BlockSpec(memory_space=pl.ANY)] * len(flat) + [whole, whole, layer_spec(w_out, layer)]
    operands = [*flat, current, gate, w_out]
    out_shape = [jax.ShapeDtypeStruct(current.shape, jnp.bfloat16)]
    out_specs = [whole]
    scratch = [
        pltpu.VMEM((n_blk * capacity, sum(bands[layer]), rows, hidden), jnp.bfloat16),
        pltpu.SemaphoreType.DMA((len(flat),)),
    ]
    if not last:
        operands += [chains, w_in]
        in_specs += [pl.BlockSpec(chains.shape, lambda s, *_: (0, 0)), layer_spec(w_in, layer + 1)]
        bands = bands[layer + 1]
        made = [jax.ShapeDtypeStruct((slots, count, cols, hidden), jnp.bfloat16) for count in bands] * 2
        out_shape += [jax.ShapeDtypeStruct(current.shape, jnp.float32)] + made
        out_specs += [whole] + [pl.BlockSpec((1,) + o.shape[1:], lambda s, *_: (s, 0, 0, 0)) for o in made]
        scratch += [pltpu.VMEM((rows, cols, channels), jnp.bfloat16)] + operand_scratch(cols, rows, hidden)
    else:
        scratch += [pltpu.VMEM((256, 256), jnp.bfloat16)]
    out = pl.pallas_call(
        functools.partial(
            close_kernel, layer, last, len(flat), n_blk, lax.axis_size("chan"), lax.axis_size("sub"), slots, terms, capacity
        ),
        grid_spec=pltpu.PrefetchScalarGridSpec(
            num_scalar_prefetch=3, grid=(slots,), in_specs=in_specs, out_specs=out_specs, scratch_shapes=scratch
        ),
        out_shape=out_shape,
        compiler_params=pltpu.CompilerParams(vmem_limit_bytes=vmem_limit),
        name="close_layer",
    )(ids, blocks, place, *operands)
    if last:
        return out[0]
    return out[0], out[1], out[2 : 2 + len(bands)], out[2 + len(bands) :]


def after(value, *others):
    return lax.optimization_barrier((value, *others))[0]


def exchange_bands_outgoing(left, right, before):
    both = ("chan", "sub")
    if before:
        ((other, _), _), ((one, _), (_, two)) = before[0]
        left, right = lax.optimization_barrier((left, right, other, one, two))[:2]
    other = lax.ppermute(left, "sub", [(0, 1), (1, 0)])
    one = lax.ppermute(right, both, [(0, 2), (3, 1), (1, 0), (2, 3)])
    two = lax.ppermute(right, both, [(1, 2), (2, 1)])
    return [(other, left), (left, other)], [(one, one), (right, two)]


def exchange_bands_incoming(left, right, before):
    both = ("chan", "sub")
    if before:
        (_, (_, two)), (_, (other, _)) = before[0]
        left, right = lax.optimization_barrier((left, right, two, other))[:2]
    one = lax.ppermute(left, both, [(1, 3), (2, 0), (0, 1), (3, 2)])
    other = lax.ppermute(right, "chan", [(0, 1), (1, 0)])
    two = lax.ppermute(after(one, before[1]) if before else one, both, [(0, 1), (3, 2)])
    return [(left, one), (one, two)], [(right, right), (other, other)]


def banded(pair, ids, blocks, owners, slot_of, chains, w_in, w_out, capacity, terms, n_blk):
    slots, rows, cols, channels = pair.shape
    hidden = w_out.shape[1]
    far = n_blk // 2
    shifts = [far] + [s for s in range(1, n_blk) if s != far] + [0]
    layers = w_in.shape[0]
    current = pair
    bands = [[12, 20], [14, 18]]
    chosen, place = make_plan(ids, owners, slot_of, n_blk, slots, terms, capacity)
    for layer in range(layers):
        if layer == 0:
            gate, lefts, rights = open_operands(ids, blocks, pair, chains, w_in, hidden, bands[0])
        exchange = exchange_bands_incoming if layer % 2 else exchange_bands_outgoing
        arrived, before = [], None
        for left, right in zip(lefts, rights):
            operands = exchange(left, right, before)
            made = banded_products(shifts, ids, chosen, *operands, capacity, cols)
            parts = [None] * n_blk
            for shift, part in zip(shifts, made):
                if shift:
                    if arrived:
                        part = after(part, arrived[-1][shift])
                    part = lax.ppermute(part, "blk", [(p, (p + shift) % n_blk) for p in range(n_blk)])
                parts[shift] = part
            arrived.append(parts)
            before = operands, parts[far]
        last = layer == layers - 1
        out = close_layer(
            layer, arrived, ids, blocks, place, current, gate, w_out, capacity, terms, chains, w_in, last, bands
        )
        if last:
            return out
        current, gate, lefts, rights = out


def per_device(pair, block_list, term_owner, term_slots, chain_ids, w_in, w_out):
    n_blk = lax.axis_size("blk")
    n_chan = lax.axis_size("chan")
    n_sub = lax.axis_size("sub")
    position = lax.axis_index("blk")
    row_group = lax.axis_index("chan")
    col_group = lax.axis_index("sub")
    slots, rows, cols, channels = pair.shape
    hidden = w_out.shape[1]
    terms = term_owner.shape[1]
    capacity = max(2, -(-slots * terms // n_blk))
    fast = n_chan == 2 and n_sub == 2
    on_diagonal = (row_group == col_group).astype(jnp.int32)
    ids = jnp.stack([position, row_group, col_group, on_diagonal]).astype(jnp.int32)
    blocks = block_list.T
    owners = term_owner.T
    slot_of = jnp.transpose(term_slots, (1, 2, 0))
    chains = chain_ids.reshape(-1, 128)
    if fast and rows == cols == 32 and channels == hidden == 128:
        return banded(pair, ids, blocks, owners, slot_of, chains, w_in, w_out, capacity, terms, n_blk)
    shifts = [n_blk // 2] + [s for s in range(1, n_blk) if s != n_blk // 2] + [0]

    def all_products(lefts, right):
        parts = [None] * n_blk
        for shift in shifts:
            made = term_products(shift, ids, owners, slot_of, lefts, right, capacity, slots, terms)
            if shift:
                pairs = [(p, (p + shift) % n_blk) for p in range(n_blk)]
                made = lax.ppermute(made, "blk", pairs)
            parts[shift] = made
        return parts

    def at_home(layer, parts, current, gate, at, of, into=None):
        last = layer == w_in.shape[0] - 1
        return home(
            layer, parts, ids, blocks, owners, current, gate, w_out, capacity, terms, at, of, chains, w_in, last, into
        )

    gate, left, *rights = first_operands(ids, blocks, pair, chains, w_in, hidden, 2 if fast else 1)
    lefts, chunks = exchange_outgoing(left, rights, n_chan, n_sub)
    count = len(chunks)
    made = [all_products(lefts, right) for right in chunks]
    homes = [at_home(0, parts, pair, gate, at, count) for at, parts in enumerate(made)]
    lefts, chunks = exchange_incoming([h[2] for h in homes], [h[3] for h in homes], n_chan, n_sub)
    made = [all_products(lefts, right) for right in chunks]
    out = None
    for at, parts in enumerate(made):
        (out,) = at_home(1, parts, homes[at][0], homes[at][1], at, count, into=out)
    return out


def solution(mesh):
    in_specs = (
        P(("groups", "blk"), "chan", "sub", None),
        P("groups", None),
        P("groups", None),
        P("groups", None, None),
        P("groups"),
        P(),
        P(),
    )
    out_specs = P(("groups", "blk"), "chan", "sub", None)
    return jax.shard_map(
        per_device, mesh=mesh, in_specs=in_specs, out_specs=out_specs, check_vma=False
    )
```

```python
import functools

import jax
import jax.numpy as jnp
from jax import lax
from jax.experimental import pallas as pl
from jax.experimental.pallas import tpu as pltpu
from jax.sharding import PartitionSpec as P

norm_epsilon = 1e-05
vmem_limit = 56 * 1024 * 1024


def sigmoid(values):
    return 0.5 + 0.5 * jnp.tanh(0.5 * values)


def layer_norm(values):
    values = values.astype(jnp.float32)
    centred = values - jnp.mean(values, axis=-1, keepdims=True)
    variance = jnp.mean(centred * centred, axis=-1, keepdims=True)
    return centred * lax.rsqrt(variance + norm_epsilon)


def alive_rows(chain_ref, start, size):
    lanes = chain_ref.shape[1]
    line = chain_ref[pl.ds(start // lanes, 1), :] >= 0
    spot = lax.broadcasted_iota(jnp.int32, (size, lanes), 0) + lax.rem(start, lanes)
    pick = jnp.logical_and(lax.broadcasted_iota(jnp.int32, (size, lanes), 1) == spot, line)
    return dot(pick.astype(jnp.float32).astype(jnp.bfloat16), jnp.ones((lanes, lanes), jnp.bfloat16))


def dot(a, b):
    return jnp.dot(a, b, preferred_element_type=jnp.float32)


def gated_pair(projected, mask, hidden):
    left = mask * sigmoid(projected[:, hidden : 2 * hidden]) * projected[:, :hidden]
    right = mask * sigmoid(projected[:, 3 * hidden : 4 * hidden]) * projected[:, 2 * hidden : 3 * hidden]
    return left.astype(jnp.bfloat16), right.astype(jnp.bfloat16)


def first_kernel(hidden, row_parts, n_chan, n_sub, ids, blocks, pair_ref, chain_ref, w_ref, gate_ref, left_ref, *rest):
    right_refs, (norm_ref, turned_ref) = rest[:row_parts], rest[row_parts:]
    slots = pl.num_programs(0)
    _, rows, cols, channels = pair_ref.shape
    block = ids[0] * slots + pl.program_id(0)
    row_alive = alive_rows(chain_ref, (blocks[0, block] * n_chan + ids[1]) * rows, rows)
    col_alive = alive_rows(chain_ref, (blocks[1, block] * n_sub + ids[2]) * cols, cols)
    group = max(1, 256 // cols)
    for start in range(0, rows, group):
        at = pl.ds(start, group)
        normed = layer_norm(pair_ref[0, at].reshape(group * cols, channels))
        norm_ref[pl.ds(start * cols, group * cols), :] = normed
        gate = sigmoid(dot(normed.astype(jnp.bfloat16), w_ref[0, :, 4 * hidden :]))
        gate_ref[0, at] = gate.reshape(group, cols, channels)
    for col in range(cols):
        turned_ref[col] = norm_ref[pl.ds(col, rows, stride=cols), :].astype(jnp.bfloat16)
    step = max(1, 128 // rows)
    part = rows // row_parts
    for start in range(0, cols, step):
        taken = turned_ref[start : start + step].reshape(step * rows, channels)
        projected = dot(taken, w_ref[0, :, : 4 * hidden])
        mask = col_alive[start : start + step][:, None, :] * row_alive[None, :, :]
        left, right = gated_pair(projected, mask.reshape(step * rows, -1), hidden)
        left_ref[0, start : start + step] = left.reshape(step, rows, hidden)
        right = right.reshape(step, rows, hidden)
        for p, right_ref in enumerate(right_refs):
            right_ref[0, start : start + step] = right[:, p * part : (p + 1) * part]


def first_operands(ids, blocks, pair, chains, w_in, hidden, row_parts):
    slots, rows, cols, channels = pair.shape
    part = rows // row_parts
    operand = jax.ShapeDtypeStruct((slots, cols, rows, hidden), jnp.bfloat16)
    right = jax.ShapeDtypeStruct((slots, cols, part, hidden), jnp.bfloat16)
    return pl.pallas_call(
        functools.partial(first_kernel, hidden, row_parts, lax.axis_size("chan"), lax.axis_size("sub")),
        grid_spec=pltpu.PrefetchScalarGridSpec(
            num_scalar_prefetch=2,
            grid=(slots,),
            in_specs=[
                pl.BlockSpec((1, rows, cols, channels), lambda s, *_: (s, 0, 0, 0)),
                pl.BlockSpec(chains.shape, lambda s, *_: (0, 0)),
                pl.BlockSpec((1,) + w_in.shape[1:], lambda s, *_: (0, 0, 0)),
            ],
            out_specs=[
                pl.BlockSpec((1, rows, cols, channels), lambda s, *_: (s, 0, 0, 0)),
                pl.BlockSpec((1, cols, rows, hidden), lambda s, *_: (s, 0, 0, 0)),
            ]
            + [pl.BlockSpec((1, cols, part, hidden), lambda s, *_: (s, 0, 0, 0))] * row_parts,
            scratch_shapes=[
                pltpu.VMEM((rows * cols, channels), jnp.float32),
                pltpu.VMEM((cols, rows, channels), jnp.bfloat16),
            ],
        ),
        out_shape=[jax.ShapeDtypeStruct(pair.shape, jnp.float32), operand] + [right] * row_parts,
        compiler_params=pltpu.CompilerParams(vmem_limit_bytes=vmem_limit),
        name="first_operands",
    )(ids, blocks, pair, chains, w_in)


def product_kernel(shift, n_blk, slots_dev, terms, capacity, pieces, n_refs, ids, owners, slots, *rest):
    refs = rest[:n_refs]
    out_ref, left_held, right_held, right_wide, chosen, sems = rest[n_refs:]
    step = pl.program_id(0)
    turn = lax.rem(step, 2)
    _, depth, n_i, hidden = left_held.shape
    n_j = right_wide.shape[1]

    @pl.when(step == 0)
    def _():
        target = lax.rem(ids[0] + shift, n_blk)
        for e in range(2 * capacity):
            chosen[e] = 0

        def scan(e, count):
            block, term = target * slots_dev + e // terms, lax.rem(e, terms)
            here = jnp.logical_and(owners[term, block] == ids[0], count < capacity)

            @pl.when(here)
            def _():
                chosen[2 * count] = slots[term, 0, block]
                chosen[2 * count + 1] = slots[term, 1, block]

            return count + here.astype(jnp.int32)

        lax.fori_loop(0, slots_dev * terms, scan, jnp.int32(0))

    def copy(n, term, buffer, source):
        side, _, _, k0, depth_of, i0, size = pieces[n]
        held = (left_held, right_held)[side]
        return pltpu.make_async_copy(
            refs[source].at[chosen[2 * term + side]],
            held.at[buffer, pl.ds(k0, depth_of), pl.ds(i0, size), :],
            sems.at[buffer, n],
        )

    def start(term, buffer):
        for n, (_, on, off, *_) in enumerate(pieces):
            if on == off:
                copy(n, term, buffer, on).start()
            else:

                @pl.when(ids[3] == 1)
                def _(n=n, on=on):
                    copy(n, term, buffer, on).start()

                @pl.when(ids[3] == 0)
                def _(n=n, off=off):
                    copy(n, term, buffer, off).start()

    @pl.when(step == 0)
    def _():
        start(0, 0)

    @pl.when(step + 1 < capacity)
    def _():
        start(step + 1, 1 - turn)

    for n, piece in enumerate(pieces):
        copy(n, step, turn, piece[1]).wait()

    span = 8

    def widen(n, carry):
        at = pl.ds(n * span, span)
        right_wide[at] = right_held[turn, at].astype(jnp.float32)
        return carry

    lax.fori_loop(0, depth // span, widen, 0)

    group = min(8, n_j)
    unroll = 4
    for j0 in range(0, n_j, group):

        def body(n, sums):
            for u in range(unroll):
                k = n * unroll + u
                left = left_held[turn, k].astype(jnp.float32).reshape(n_i // 8, 8, hidden)
                sums = tuple(
                    total + left * right_wide[k, pl.ds(j0 + j, 8, stride=0), :][None]
                    for j, total in enumerate(sums)
                )
            return sums

        zero = jnp.zeros((n_i // 8, 8, hidden), jnp.float32)
        sums = lax.fori_loop(0, depth // unroll, body, (zero,) * group)
        for j, total in enumerate(sums):
            out_ref[0, j0 + j] = total.reshape(n_i, hidden).astype(jnp.bfloat16)


def term_products(shift, ids, owners, slots, lefts, rights, capacity, slots_dev, terms):
    n_blk = lax.axis_size("blk")
    refs, pieces = [], []

    def index_of(array):
        for n, known in enumerate(refs):
            if known is array:
                return n
        refs.append(array)
        return len(refs) - 1

    for side, operands in ((0, lefts), (1, rights)):
        for on, off, k0, i0 in operands:
            pieces.append((side, index_of(on), index_of(off), k0, on.shape[1], i0, on.shape[2]))
    hidden = lefts[0][0].shape[3]
    n_i = max(p[5] + p[6] for p in pieces if p[0] == 0)
    n_j = max(p[5] + p[6] for p in pieces if p[0] == 1)
    depth = max(p[3] + p[4] for p in pieces)
    return pl.pallas_call(
        functools.partial(
            product_kernel, shift, n_blk, slots_dev, terms, capacity, tuple(pieces), len(refs)
        ),
        grid_spec=pltpu.PrefetchScalarGridSpec(
            num_scalar_prefetch=3,
            grid=(capacity,),
            in_specs=[pl.BlockSpec(memory_space=pl.ANY)] * len(refs),
            out_specs=pl.BlockSpec((1, n_j, n_i, hidden), lambda t, *_: (t, 0, 0, 0)),
            scratch_shapes=[
                pltpu.VMEM((2, depth, n_i, hidden), jnp.bfloat16),
                pltpu.VMEM((2, depth, n_j, hidden), jnp.bfloat16),
                pltpu.VMEM((depth, n_j, hidden), jnp.float32),
                pltpu.SMEM((2 * capacity,), jnp.int32),
                pltpu.SemaphoreType.DMA((2, len(pieces))),
            ],
        ),
        out_shape=jax.ShapeDtypeStruct((capacity, n_j, n_i, hidden), jnp.bfloat16),
        compiler_params=pltpu.CompilerParams(vmem_limit_bytes=vmem_limit),
        cost_estimate=pl.CostEstimate(
            flops=2 * capacity * n_i * n_j * depth * hidden * 100,
            bytes_accessed=capacity * (depth * (n_i + n_j) + n_i * n_j) * hidden * 2,
            transcendentals=0,
        ),
        name="term_products",
    )(ids, owners, slots, *refs)


def home_kernel(last, hidden, n_blk, n_chan, n_sub, at, of, slots_dev, terms, capacity, ids, blocks, owners, *rest):
    parts, rest = rest[:n_blk], rest[n_blk:]
    scratch, rest = rest[-5:], rest[:-5]
    held, turned, place, seen, sems = scratch
    cur_ref, gate_ref, w_out_ref = rest[:3]
    if last:
        out_ref = rest[-1]
    else:
        chain_ref, w_ref, out_ref, next_gate_ref, left_ref, right_ref = rest[3:]
    step = pl.program_id(0)
    _, rows, cols, channels = cur_ref.shape

    def arrival(shift):
        return pltpu.make_async_copy(parts[shift], held.at[pl.ds(shift * capacity, capacity)], sems.at[shift])

    @pl.when(step == 0)
    def _():
        for shift in range(n_blk):
            arrival(shift).start()
            seen[shift] = 0

        def scan(e, carry):
            owner = owners[lax.rem(e, terms), ids[0] * slots_dev + e // terms]
            shift = lax.rem(ids[0] - owner + n_blk, n_blk)
            count = seen[owner]
            seen[owner] = count + 1
            place[e] = shift * capacity + count
            return carry

        lax.fori_loop(0, slots_dev * terms, scan, jnp.int32(0))
        for shift in range(n_blk):
            arrival(shift).wait()

    if not last:
        block = ids[0] * slots_dev + step
        row_alive = alive_rows(chain_ref, (blocks[0, block] * n_chan + ids[1]) * rows, rows)
        col_alive = alive_rows(chain_ref, ((blocks[1, block] * n_sub + ids[2]) * of + at) * cols, cols)
    span = max(1, 128 // rows)
    for start in range(0, cols, span):
        taken = pl.ds(start, span)
        total = held[place[step * terms], taken].astype(jnp.float32)
        for t in range(1, terms):
            total = total + held[place[step * terms + t], taken].astype(jnp.float32)
        rounded = total.astype(jnp.bfloat16).astype(jnp.float32)
        turned[pl.ds(start * rows, span * rows), :] = rounded.reshape(span * rows, hidden)
    group = min(rows, max(1, 256 // cols))
    for start in range(0, rows, group):
        taken = pl.ds(start, group)
        mixture = jnp.concatenate(
            [turned[pl.ds(row, cols, stride=rows), :].astype(jnp.bfloat16) for row in range(start, start + group)]
        )
        update = dot(layer_norm(mixture).astype(jnp.bfloat16), w_out_ref[0])
        current = cur_ref[0, taken].astype(jnp.float32).reshape(group * cols, channels)
        gate = gate_ref[0, taken].reshape(group * cols, channels)
        result = (current + gate * update).astype(jnp.bfloat16)
        out_ref[0, taken] = result.reshape(group, cols, channels)
        if not last:
            normed = layer_norm(result).astype(jnp.bfloat16)
            projected = dot(normed, w_ref[0])
            next_gate_ref[0, taken] = sigmoid(projected[:, 4 * hidden :]).reshape(group, cols, channels)
            mask = row_alive[start : start + group][:, None, :] * col_alive[None, :, :]
            left, right = gated_pair(projected, mask.reshape(group * cols, channels), hidden)
            left_ref[0, taken] = left.reshape(group, cols, hidden)
            right_ref[0, taken] = right.reshape(group, cols, hidden)


def home(layer, parts, ids, blocks, owners, current, gate, w_out, capacity, terms, at, of, chains, w_in, last, into=None):
    n_blk = len(parts)
    slots, rows, _, channels = current.shape
    hidden = w_out.shape[1]
    cols = parts[0].shape[1]
    chunk = (1, rows, cols, channels)

    def chunk_spec(array):
        whole = array.shape[2] != cols
        return pl.BlockSpec(chunk, lambda s, *_: (s, 0, at if whole else 0, 0))

    def layer_spec(array, index):
        return pl.BlockSpec((1,) + array.shape[1:], lambda s, *_: (index, 0, 0))

    in_specs = [pl.BlockSpec(memory_space=pl.ANY)] * n_blk + [
        chunk_spec(current),
        chunk_spec(gate),
        layer_spec(w_out, layer),
    ]
    operands = [*parts, current, gate, w_out]
    aliases = {}
    if last:
        if into is not None:
            aliases = {3 + len(operands): 0}
            operands.append(into)
            in_specs.append(pl.BlockSpec(memory_space=pl.ANY))
        out_shape = [jax.ShapeDtypeStruct((slots, rows, cols * of, channels), jnp.bfloat16)]
        out_specs = [pl.BlockSpec(chunk, lambda s, *_: (s, 0, at, 0))]
    else:
        operands += [chains, w_in]
        in_specs += [pl.BlockSpec(chains.shape, lambda s, *_: (0, 0)), layer_spec(w_in, layer + 1)]
        small = (slots, rows, cols, channels)
        out_shape = [jax.ShapeDtypeStruct(small, t) for t in (jnp.bfloat16, jnp.float32, jnp.bfloat16, jnp.bfloat16)]
        out_specs = [pl.BlockSpec(chunk, lambda s, *_: (s, 0, 0, 0))] * 4
    return pl.pallas_call(
        functools.partial(
            home_kernel, last, hidden, n_blk, lax.axis_size("chan"), lax.axis_size("sub"), at, of, slots, terms, capacity
        ),
        grid_spec=pltpu.PrefetchScalarGridSpec(
            num_scalar_prefetch=3,
            grid=(slots,),
            in_specs=in_specs,
            out_specs=out_specs,
            scratch_shapes=[
                pltpu.VMEM((n_blk * capacity, cols, rows, hidden), jnp.bfloat16),
                pltpu.VMEM((rows * cols, hidden), jnp.float32),
                pltpu.SMEM((slots * terms,), jnp.int32),
                pltpu.SMEM((n_blk,), jnp.int32),
                pltpu.SemaphoreType.DMA((n_blk,)),
            ],
        ),
        out_shape=out_shape,
        input_output_aliases=aliases,
        compiler_params=pltpu.CompilerParams(vmem_limit_bytes=vmem_limit),
        cost_estimate=pl.CostEstimate(
            flops=2 * slots * rows * cols * channels * 6 * channels * 10,
            bytes_accessed=slots * rows * cols * channels * 16,
            transcendentals=0,
        ),
        name="home",
    )(ids, blocks, owners, *operands)


def exchange_outgoing(left, rights, n_chan, n_sub):
    if n_chan == 2 and n_sub == 2:
        both = ("chan", "sub")
        other_left = lax.ppermute(left, "sub", [(0, 1), (1, 0)])
        lefts = [(other_left, left, 0, 0), (left, other_left, left.shape[1], 0)]
        chunks = []
        for right in rights:
            if chunks:
                (one, *_), (_, two, *_) = chunks[-1]
                right, *_ = lax.optimization_barrier((right, one, two))
            one = lax.ppermute(right, both, [(0, 2), (3, 1), (1, 0), (2, 3)])
            two = lax.ppermute(right, both, [(1, 2), (2, 1)])
            chunks.append([(one, one, 0, 0), (right, two, right.shape[1], 0)])
        return lefts, chunks
    left = lax.all_gather(left, "sub", axis=1, tiled=True)
    right = jnp.concatenate(rights, axis=2)
    right = lax.all_gather(right, "chan", axis=2, tiled=True)
    right = lax.all_to_all(right, "sub", split_axis=2, concat_axis=1, tiled=True)
    cols = right.shape[2] // 2
    chunks = [right[:, :, :cols], right[:, :, cols:]]
    return [(left, left, 0, 0)], [[(r, r, 0, 0)] for r in chunks]


def exchange_incoming(lefts, rights, n_chan, n_sub):
    if n_chan == 2 and n_sub == 2:
        both = ("chan", "sub")
        left_pieces, chunks = [], []
        at = 0
        for left, right in zip(lefts, rights):
            depth = left.shape[1]
            one = lax.ppermute(left, both, [(1, 3), (2, 0), (0, 1), (3, 2)])
            two = lax.ppermute(one, both, [(0, 1), (3, 2)])
            left_pieces += [(left, one, 0, at), (one, two, depth, at)]
            other = lax.ppermute(right, "chan", [(0, 1), (1, 0)])
            chunks.append([(right, right, 0, 0), (other, other, depth, 0)])
            at += left.shape[2]
        return left_pieces, chunks
    left = lax.all_gather(jnp.concatenate(lefts, axis=2), "chan", axis=1, tiled=True)
    left = lax.all_gather(left, "sub", axis=2, tiled=True)
    size = left.shape[2] // n_chan
    left = lax.dynamic_slice_in_dim(left, lax.axis_index("chan") * size, size, 2)
    gathered = [lax.all_gather(right, "chan", axis=1, tiled=True) for right in rights]
    return [(left, left, 0, 0)], [[(r, r, 0, 0)] for r in gathered]


def lane_group(shape, size):
    return lax.broadcasted_iota(jnp.int32, shape, 1) // size


def spread_weights(w_ref, wide_ref, hidden, size):
    parts = hidden // size
    for side in range(2):
        for kind in range(2):
            start = (2 * side + kind) * hidden
            weights = w_ref[0, :, start : start + hidden].astype(jnp.float32)
            group = lane_group(weights.shape, size)
            for part in range(parts):
                kept = jnp.where(group == part, weights, 0.0)
                at = ((side * parts + part) * 2 + kind) * hidden
                for a in range(parts):
                    moved = pltpu.roll(kept, ((a - part) % parts) * size, 1) if a != part else kept
                    wide_ref[a * hidden : (a + 1) * hidden, at : at + hidden] = moved.astype(jnp.bfloat16)


def swap_matrix(half):
    shape = (half * half, half * half)
    to, of = lax.broadcasted_iota(jnp.int32, shape, 0), lax.broadcasted_iota(jnp.int32, shape, 1)
    same = jnp.logical_and(to // half == lax.rem(of, half), lax.rem(to, half) == of // half)
    return same.astype(jnp.float32).astype(jnp.bfloat16)


def swapped(values, swap_ref):
    half, _, lanes = values.shape
    moved = dot(swap_ref[...], values.reshape(half * half, lanes))
    return moved.astype(jnp.bfloat16).reshape(half, half, lanes)


def turn(taken, turned, swap_ref):
    half = 16
    for x in range(0, taken.shape[0], half):
        for y in range(0, taken.shape[1], half):
            turned[y : y + half, x : x + half] = swapped(taken[x : x + half, y : y + half], swap_ref)


def make_operand(side, taken, row_alive, inner_alive, wide_ref, out_refs, laid, swap_ref):
    rows, size, hidden = taken.shape
    parts, bands, half = hidden // size, size, 16
    groups = rows // parts
    stacked = jnp.concatenate(
        [jnp.concatenate([taken[g * parts + a] for a in range(parts)], axis=1) for g in range(groups)], axis=0
    )
    mask = (row_alive[:, None, :] * inner_alive[None, :, :]).reshape(groups * size, hidden)
    for part in range(parts):
        at = (side * parts + part) * 2 * hidden
        made = dot(stacked, wide_ref[:, at : at + 2 * hidden])
        value = mask * sigmoid(made[:, hidden:]) * made[:, :hidden]
        laid[side, :, part * size : (part + 1) * size, :] = value.astype(jnp.bfloat16).reshape(groups, size, hidden)
    blocks = [laid[side, g].T for g in range(groups)]
    starts = [sum(ref.shape[1] for ref in out_refs[:n]) for n in range(len(out_refs))]
    for first in range(0, bands, half):
        for row in range(0, rows, half):
            tiles = []
            for r in range(row, row + half):
                at = r % parts * bands + first
                tiles.append(blocks[r // parts][at : at + half])
            moved = swapped(jnp.stack(tiles), swap_ref)
            for start, ref in zip(starts, out_refs):
                low, high = max(start, first), min(start + ref.shape[1], first + half)
                if low < high:
                    ref[0, low - start : high - start, row : row + half] = moved[low - first : high - first]


def alive_groups(chain_ref, start, rows, parts):
    lanes = chain_ref.shape[1]
    groups = rows // parts
    line = chain_ref[pl.ds(start // lanes, 1), :] >= 0
    row = lax.broadcasted_iota(jnp.int32, (groups, lanes), 1) - lax.rem(start, lanes)
    group = lax.broadcasted_iota(jnp.int32, (groups, lanes), 0)
    pick = jnp.logical_and(jnp.logical_and(row >= group * parts, row < (group + 1) * parts), line)
    fold = lax.rem(lax.broadcasted_iota(jnp.int32, (lanes, lanes), 0), parts) == lane_group(
        (lanes, lanes), lanes // parts
    )
    return dot(pick.astype(jnp.float32).astype(jnp.bfloat16), fold.astype(jnp.float32).astype(jnp.bfloat16))


def open_layer(layer, natural, chain_ref, row_start, col_start, w_ref, left_refs, right_refs, wide, laid, turned, swap):
    rows, cols, hidden = natural.shape
    parts = hidden // rows
    turn(natural, turned, swap)
    row_mask = alive_groups(chain_ref, row_start, rows, parts), alive_rows(chain_ref, col_start, cols)
    col_mask = alive_groups(chain_ref, col_start, cols, parts), alive_rows(chain_ref, row_start, rows)
    for side, refs in ((0, left_refs), (1, right_refs)):
        if side == layer % 2:
            make_operand(side, natural, *row_mask, wide, refs, laid, swap)
        else:
            make_operand(side, turned[...], *col_mask, wide, refs, laid, swap)


def open_kernel(hidden, chunks, n_chan, n_sub, base, of, ids, blocks, pair_ref, chain_ref, w_ref, *rest):
    gate_ref, *operand_refs, norm_ref, wide, laid, turned, swap = rest[-(2 * chunks + 6) :]
    step = pl.program_id(0)
    _, rows, cols, channels = pair_ref.shape
    block = ids[0] * of + base + step

    @pl.when(step == 0)
    def _():
        spread_weights(w_ref, wide, hidden, cols)
        swap[...] = swap_matrix(16)

    group = hidden // cols
    for start in range(0, rows, group):
        at = pl.ds(start, group)
        normed = layer_norm(pair_ref[0, at].reshape(group * cols, channels)).astype(jnp.bfloat16)
        gate = sigmoid(dot(normed, w_ref[0, :, 4 * hidden :]))
        gate_ref[0, at] = gate.reshape(group, cols, channels)
        norm_ref[at] = normed.reshape(group, cols, channels)
    starts = (blocks[0, block] * n_chan + ids[1]) * rows, (blocks[1, block] * n_sub + ids[2]) * cols
    lefts, rights = operand_refs[:chunks], operand_refs[chunks:]
    open_layer(0, norm_ref[...], chain_ref, *starts, w_ref, lefts, rights, wide, laid, turned, swap)


def operand_scratch(rows, size, hidden):
    parts = hidden // size
    return [
        pltpu.VMEM((parts * hidden, 4 * parts * hidden), jnp.bfloat16),
        pltpu.VMEM((2, rows // parts, parts * size, hidden), jnp.bfloat16),
        pltpu.VMEM((size, rows, hidden), jnp.bfloat16),
        pltpu.VMEM((256, 256), jnp.bfloat16),
    ]


def operand_outputs(slots, count, rows, hidden, bands):
    kept = [count if n == 0 else slots for n in range(len(bands))] * 2
    return [jax.ShapeDtypeStruct((k, b, rows, hidden), jnp.bfloat16) for k, b in zip(kept, bands * 2)]


def slot_specs(arrays, slots, base):
    def spec(array):
        offset = base if array.shape[0] == slots else 0
        return pl.BlockSpec((1,) + array.shape[1:], lambda s, *_: (s + offset, 0, 0, 0))

    return [spec(a) for a in arrays]


def fill(out_shape, earlier, slots, n_before):
    if earlier is None:
        return [], [], {}
    shared = [n for n, o in enumerate(out_shape) if o.shape[0] == slots]
    specs = [pl.BlockSpec(memory_space=pl.ANY)] * len(shared)
    return [earlier[n] for n in shared], specs, {n_before + k: n for k, n in enumerate(shared)}


def open_operands(ids, blocks, pair, chains, w_in, hidden, bands, base, count, earlier):
    slots, rows, cols, channels = pair.shape
    out_shape = [jax.ShapeDtypeStruct(pair.shape, jnp.float32)] + operand_outputs(slots, count, rows, hidden, bands)
    more, more_specs, aliases = fill(out_shape, earlier, slots, 5)
    return pl.pallas_call(
        functools.partial(open_kernel, hidden, len(bands), lax.axis_size("chan"), lax.axis_size("sub"), base, slots),
        grid_spec=pltpu.PrefetchScalarGridSpec(
            num_scalar_prefetch=2,
            grid=(count,),
            in_specs=slot_specs([pair], slots, base)
            + [
                pl.BlockSpec(chains.shape, lambda s, *_: (0, 0)),
                pl.BlockSpec((1,) + w_in.shape[1:], lambda s, *_: (0, 0, 0)),
            ]
            + more_specs,
            out_specs=slot_specs(out_shape, slots, base),
            scratch_shapes=[pltpu.VMEM((rows, cols, channels), jnp.bfloat16)] + operand_scratch(rows, cols, hidden),
        ),
        out_shape=out_shape,
        input_output_aliases=aliases,
        compiler_params=pltpu.CompilerParams(vmem_limit_bytes=vmem_limit),
        cost_estimate=pl.CostEstimate(flops=1 << 33, bytes_accessed=1 << 20, transcendentals=0),
        name="open_operands",
    )(ids, blocks, pair, chains, w_in, *more)


def plan_kernel(n_blk, slots_dev, terms, capacity, ids, owners, slots, chosen, place, seen):
    for shift in range(n_blk):
        seen[shift] = 0
        target = lax.rem(ids[0] + shift, n_blk)
        for e in range(2 * (capacity + 1)):
            chosen[2 * shift * (capacity + 1) + e] = 0
        found = jnp.int32(0)
        for e in range(slots_dev * terms):
            block, term = target * slots_dev + e // terms, e % terms
            at = 2 * (shift * (capacity + 1) + jnp.minimum(found, capacity))
            chosen[at] = slots[term, 0, block]
            chosen[at + 1] = slots[term, 1, block]
            found = found + (owners[term, block] == ids[0]).astype(jnp.int32)
    for e in range(slots_dev * terms):
        owner = owners[e % terms, ids[0] * slots_dev + e // terms]
        count = seen[owner]
        seen[owner] = count + 1
        place[e] = lax.rem(ids[0] - owner + n_blk, n_blk) * capacity + count


def make_plan(ids, owners, slots, n_blk, slots_dev, terms, capacity):
    scalars = pl.BlockSpec(memory_space=pltpu.SMEM)
    return pl.pallas_call(
        functools.partial(plan_kernel, n_blk, slots_dev, terms, capacity),
        in_specs=[scalars] * 3,
        out_specs=[scalars] * 2,
        out_shape=[
            jax.ShapeDtypeStruct((2 * n_blk * (capacity + 1),), jnp.int32),
            jax.ShapeDtypeStruct((slots_dev * terms,), jnp.int32),
        ],
        scratch_shapes=[pltpu.SMEM((n_blk,), jnp.int32)],
        name="make_plan",
    )(ids, owners, slots)


def banded_kernel(shifts, capacity, pieces, n_refs, size, ids, chosen, *rest):
    refs, rest = rest[:n_refs], rest[n_refs:]
    out_refs, (left_held, right_held, out_held, sems, out_sems) = rest[: len(shifts)], rest[len(shifts) :]
    halves, _, bands, rows, hidden = left_held.shape
    parts = hidden // size

    def copy(n, source):
        side, half, base, *_ = pieces[n]
        target = (left_held, right_held)[side].at[half, pl.ds(base, refs[source].shape[0])]
        return pltpu.make_async_copy(refs[source], target, sems.at[n])

    for n, (*_, on, off) in enumerate(pieces):
        if on == off:
            copy(n, on).start()
        else:

            @pl.when(ids[3] == 1)
            def _(n=n, on=on):
                copy(n, on).start()

            @pl.when(ids[3] == 0)
            def _(n=n, off=off):
                copy(n, off).start()

    for n, piece in enumerate(pieces):
        copy(n, piece[-1]).wait()

    def leave(n):
        return pltpu.make_async_copy(out_held.at[pl.ds(n * capacity, capacity)], out_refs[n], out_sems.at[n])

    for n, shift in enumerate(shifts):

        def one(term, carry, n=n, shift=shift):
            at = 2 * (shift * (capacity + 1) + term)
            left_slot, right_slot = chosen[at], chosen[at + 1]
            group = lane_group((size, hidden), size)
            for band in range(bands):
                left = jnp.concatenate([left_held[h, left_slot, band] for h in range(halves)], axis=1)
                apart = []
                for h in range(halves):
                    right = right_held[h, right_slot, band]
                    apart += [jnp.where(group == part, right, jnp.zeros_like(right)) for part in range(parts)]
                made = dot(left, jnp.concatenate(apart, axis=0))
                out_held[n * capacity + term, band] = made.astype(jnp.bfloat16)
            return carry

        lax.fori_loop(0, capacity, one, 0)
        leave(n).start()
    for n in range(len(shifts)):
        leave(n).wait()


def banded_products(shifts, ids, chosen, operands, capacity, size):
    refs, pieces = [], []

    def index_of(array):
        for n, known in enumerate(refs):
            if known is array:
                return n
        refs.append(array)
        return len(refs) - 1

    slots = 0
    for both in operands:
        for side in range(2):
            for half, (on, off) in enumerate(both[side]):
                pieces.append((side, half, slots, index_of(on), index_of(off)))
        slots += both[0][0][0].shape[0]
    halves = len(operands[0][0])
    _, bands, rows, hidden = operands[0][0][0][0].shape
    count = len(shifts) * capacity
    anywhere = pl.BlockSpec(memory_space=pl.ANY)
    return pl.pallas_call(
        functools.partial(banded_kernel, shifts, capacity, tuple(pieces), len(refs), size),
        grid_spec=pltpu.PrefetchScalarGridSpec(
            num_scalar_prefetch=2,
            grid=(),
            in_specs=[anywhere] * len(refs),
            out_specs=[anywhere] * len(shifts),
            scratch_shapes=[
                pltpu.VMEM((halves, slots, bands, rows, hidden), jnp.bfloat16),
                pltpu.VMEM((halves, slots, bands, size, hidden), jnp.bfloat16),
                pltpu.VMEM((count, bands, rows, hidden), jnp.bfloat16),
                pltpu.SemaphoreType.DMA((len(pieces),)),
                pltpu.SemaphoreType.DMA((len(shifts),)),
            ],
        ),
        out_shape=[jax.ShapeDtypeStruct((capacity, bands, rows, hidden), jnp.bfloat16)] * len(shifts),
        compiler_params=pltpu.CompilerParams(vmem_limit_bytes=vmem_limit),
        cost_estimate=pl.CostEstimate(
            flops=2 * count * bands * rows * hidden * hidden * halves, bytes_accessed=1, transcendentals=0
        ),
        name="banded_products",
    )(ids, chosen, *refs)


def close_kernel(layer, last, n_parts, n_blk, n_chan, n_sub, base, of, terms, capacity, ids, blocks, place, *rest):
    chunks = n_parts // n_blk
    arrived, rest = rest[:n_parts], rest[n_parts:]
    cur_ref, gate_ref, w_out_ref = rest[:3]
    if last:
        out_ref, held, wide_out, sems, swap = rest[3:]
    else:
        chain_ref, w_ref = rest[3:5]
        out_ref, next_gate_ref, *operand_refs, held, wide_out, sems, norm_ref, wide, laid, turned, swap = rest[
            -(2 * chunks + 10) :
        ]
        left_refs, right_refs = operand_refs[:chunks], operand_refs[chunks:]
    step = pl.program_id(0)
    _, rows, cols, channels = cur_ref.shape
    _, bands, _, hidden = held.shape
    parts, size = hidden // bands, bands

    def arrival(n):
        at = sum(arrived[m * n_blk].shape[1] for m in range(n // n_blk))
        count = arrived[n].shape[1]
        target = held.at[pl.ds(n % n_blk * capacity, capacity), pl.ds(at, count)]
        return pltpu.make_async_copy(arrived[n], target, sems.at[n])

    @pl.when(step == 0)
    def _():
        for n in range(n_parts):
            arrival(n).start()
        wide_out[...] = jnp.zeros_like(wide_out)
        for part in range(parts):
            for a in range(parts):
                at = (part * parts + a) * bands
                wide_out[at : at + bands, a * channels : (a + 1) * channels] = w_out_ref[
                    0, part * bands : (part + 1) * bands, :
                ]
        swap[...] = swap_matrix(16)
        if not last:
            spread_weights(w_ref, wide, hidden, rows)
        for n in range(n_parts):
            arrival(n).wait()

    half = 16
    by_row = [[] for _ in range(rows)]
    for row in range(0, rows, half):
        for band in range(0, bands, half):
            taken = pl.ds(band, half), pl.ds(row, half)
            total = held[(place[(base + step) * terms], *taken)].astype(jnp.float32)
            for t in range(1, terms):
                total = total + held[(place[(base + step) * terms + t], *taken)].astype(jnp.float32)
            moved = swapped(total.astype(jnp.bfloat16), swap)
            for r in range(half):
                by_row[row + r].append(moved[r])
    groups = rows // parts
    pieces = []
    for g in range(groups):
        block = jnp.concatenate([x for a in range(parts) for x in by_row[g * parts + a]]).T
        pieces.append(jnp.concatenate([block[p * cols : (p + 1) * cols] for p in range(parts)], axis=1))
    mixture = jnp.concatenate(pieces)
    together = (lane_group((hidden, hidden), size) == lax.broadcasted_iota(jnp.int32, (hidden, hidden), 0) // size)
    together = together.astype(jnp.float32).astype(jnp.bfloat16)
    average = dot(mixture, jnp.concatenate([together] * parts)) * (1.0 / hidden)
    centred = [mixture[:, p * hidden : (p + 1) * hidden].astype(jnp.float32) - average for p in range(parts)]
    squares = sum(c * c for c in centred)
    high = squares.astype(jnp.bfloat16)
    low = (squares - high.astype(jnp.float32)).astype(jnp.bfloat16)
    variance = dot(jnp.concatenate([high, low], axis=1), jnp.concatenate([together] * 2)) * (1.0 / hidden)
    scale = lax.rsqrt(variance + norm_epsilon)
    normed = jnp.concatenate([(c * scale).astype(jnp.bfloat16) for c in centred], axis=1)
    update = dot(normed, wide_out[...])
    for g in range(groups):
        taken = pl.ds(g * parts, parts)
        change = jnp.concatenate(
            [update[g * cols : (g + 1) * cols, a * channels : (a + 1) * channels] for a in range(parts)]
        )
        gate = gate_ref[0, taken].reshape(parts * cols, channels)
        current = cur_ref[0, taken].astype(jnp.float32).reshape(parts * cols, channels)
        result = (current + gate * change).astype(jnp.bfloat16)
        out_ref[0, taken] = result.reshape(parts, cols, channels)
        if not last:
            norm = layer_norm(result).astype(jnp.bfloat16)
            norm_ref[taken] = norm.reshape(parts, cols, channels)
            next_gate = sigmoid(dot(norm, w_ref[0, :, 4 * hidden :]))
            next_gate_ref[0, taken] = next_gate.reshape(parts, cols, channels)
    if not last:
        block = ids[0] * of + base + step
        starts = (blocks[0, block] * n_chan + ids[1]) * rows, (blocks[1, block] * n_sub + ids[2]) * cols
        open_layer(
            layer + 1, norm_ref[...], chain_ref, *starts, w_ref, left_refs, right_refs, wide, laid, turned, swap
        )


def close_layer(
    layer, arrived, ids, blocks, place, current, gate, w_out, capacity, terms, chains, w_in, last, bands, base, count, earlier
):
    n_blk = len(arrived[0])
    flat = [part for chunk in arrived for part in chunk]
    slots, rows, cols, channels = current.shape
    hidden = w_out.shape[1]

    def layer_spec(array, index):
        return pl.BlockSpec((1,) + array.shape[1:], lambda s, *_: (index, 0, 0))

    in_specs = [pl.BlockSpec(memory_space=pl.ANY)] * len(flat)
    in_specs += slot_specs([current, gate], slots, base) + [layer_spec(w_out, layer)]
    operands = [*flat, current, gate, w_out]
    out_shape = [jax.ShapeDtypeStruct(current.shape, jnp.bfloat16)]
    scratch = [
        pltpu.VMEM((n_blk * capacity, sum(bands[layer]), rows, hidden), jnp.bfloat16),
        pltpu.VMEM((hidden // cols * hidden, hidden // cols * channels), jnp.bfloat16),
        pltpu.SemaphoreType.DMA((len(flat),)),
    ]
    if not last:
        operands += [chains, w_in]
        in_specs += [pl.BlockSpec(chains.shape, lambda s, *_: (0, 0)), layer_spec(w_in, layer + 1)]
        out_shape += [jax.ShapeDtypeStruct(current.shape, jnp.float32)]
        out_shape += operand_outputs(slots, count, cols, hidden, bands[layer + 1])
        scratch += [pltpu.VMEM((rows, cols, channels), jnp.bfloat16)] + operand_scratch(cols, rows, hidden)
    else:
        scratch += [pltpu.VMEM((256, 256), jnp.bfloat16)]
    more, more_specs, aliases = fill(out_shape, earlier, slots, 3 + len(operands))
    return pl.pallas_call(
        functools.partial(
            close_kernel,
            *(layer, last, len(flat), n_blk, lax.axis_size("chan"), lax.axis_size("sub"), base, slots, terms, capacity),
        ),
        grid_spec=pltpu.PrefetchScalarGridSpec(
            num_scalar_prefetch=3,
            grid=(count,),
            in_specs=in_specs + more_specs,
            out_specs=slot_specs(out_shape, slots, base),
            scratch_shapes=scratch,
        ),
        out_shape=out_shape,
        input_output_aliases=aliases,
        compiler_params=pltpu.CompilerParams(vmem_limit_bytes=vmem_limit),
        cost_estimate=pl.CostEstimate(flops=1 << 33, bytes_accessed=1 << 20, transcendentals=0),
        name="close_layer",
    )(ids, blocks, place, *operands, *more)


def after(value, *others):
    return lax.optimization_barrier((value, *others))[0]


def exchange_bands_outgoing(left, right, over):
    both = ("chan", "sub")
    other = lax.ppermute(left, "sub", [(0, 1), (1, 0)])
    one = lax.ppermute(right, both, [(0, 2), (3, 1), (1, 0), (2, 3)])
    two = lax.ppermute(right, both, [(1, 2), (2, 1)])
    return [(other, left), (left, other)], [(one, one), (right, two)]


def exchange_bands_incoming(left, right, over):
    both = ("chan", "sub")
    one = lax.ppermute(left, both, [(1, 3), (2, 0), (0, 1), (3, 2)])
    other = lax.ppermute(right, "chan", [(0, 1), (1, 0)])
    two = lax.ppermute(after(one, over), both, [(0, 1), (3, 2)])
    return [(left, one), (one, two)], [(right, right), (other, other)]


def banded(pair, ids, blocks, owners, slot_of, chains, w_in, w_out, capacity, terms, n_blk):
    slots, rows, cols, channels = pair.shape
    hidden = w_out.shape[1]
    far = n_blk // 2
    shifts = [far] + [s for s in range(1, n_blk) if s != far] + [0]
    layers = w_in.shape[0]
    current = pair
    bands = [[12, 20], [14, 18]]
    chosen, place = make_plan(ids, owners, slot_of, n_blk, slots, terms, capacity)
    half = slots // 2
    halves = [(0, half), (half, slots - half)]
    for layer in range(layers):
        count = len(bands[layer])
        if layer == 0:
            calls = [None]
            for base, size in halves:
                calls.append(open_operands(ids, blocks, pair, chains, w_in, hidden, bands[0], base, size, calls[-1]))
            gate = calls[-1][0]
        operands = [call[-2 * count :] for call in calls[1:]]
        exchange = exchange_bands_incoming if layer % 2 else exchange_bands_outgoing
        arrived = []
        for chunk in range(count):
            if chunk == 0:
                exchanged = []
                over = operands[-1][count]
                for left, right in [(o[0], o[count]) for o in operands]:
                    if exchanged and layer % 2:
                        (_, (one, _)), (_, (other, _)) = exchanged[-1]
                        left, right = lax.optimization_barrier((left, right, one, other))[:2]
                    exchanged.append(exchange(left, right, over))
            else:
                left, right = operands[-1][chunk], operands[-1][count + chunk]
                last_of = exchanged[-1]
                left, right = lax.optimization_barrier(
                    (left, right, last_of[0][1][1], last_of[0][0][0], last_of[1][0][1], last_of[1][1][1])
                    + ((made[-1],) if layer % 2 == 0 else ())
                )[:2]
                exchanged = [exchange(left, right, arrived[-1][far])]
            made = banded_products(shifts, ids, chosen, exchanged, capacity, cols)
            parts = [None] * n_blk
            for shift, part in zip(shifts, made):
                if shift:
                    if arrived:
                        part = after(part, arrived[-1][shift])
                    part = lax.ppermute(part, "blk", [(p, (p + shift) % n_blk) for p in range(n_blk)])
                parts[shift] = part
            arrived.append(parts)
        last = layer == layers - 1
        calls = [None]
        for base, size in [(0, slots)] if last else halves:
            calls.append(
                close_layer(
                    *(layer, arrived, ids, blocks, place, current, gate, w_out, capacity, terms, chains, w_in, last),
                    *(bands, base, size, calls[-1]),
                )
            )
        if last:
            return calls[-1][0]
        current, gate = calls[-1][:2]


def per_device(pair, block_list, term_owner, term_slots, chain_ids, w_in, w_out):
    n_blk = lax.axis_size("blk")
    n_chan = lax.axis_size("chan")
    n_sub = lax.axis_size("sub")
    position = lax.axis_index("blk")
    row_group = lax.axis_index("chan")
    col_group = lax.axis_index("sub")
    slots, rows, cols, channels = pair.shape
    hidden = w_out.shape[1]
    terms = term_owner.shape[1]
    capacity = max(2, -(-slots * terms // n_blk))
    fast = n_chan == 2 and n_sub == 2
    on_diagonal = (row_group == col_group).astype(jnp.int32)
    ids = jnp.stack([position, row_group, col_group, on_diagonal]).astype(jnp.int32)
    blocks = block_list.T
    owners = term_owner.T
    slot_of = jnp.transpose(term_slots, (1, 2, 0))
    chains = chain_ids.reshape(-1, 128)
    if fast and rows == cols == 32 and channels == hidden == 128:
        return banded(pair, ids, blocks, owners, slot_of, chains, w_in, w_out, capacity, terms, n_blk)
    shifts = [n_blk // 2] + [s for s in range(1, n_blk) if s != n_blk // 2] + [0]

    def all_products(lefts, right):
        parts = [None] * n_blk
        for shift in shifts:
            made = term_products(shift, ids, owners, slot_of, lefts, right, capacity, slots, terms)
            if shift:
                pairs = [(p, (p + shift) % n_blk) for p in range(n_blk)]
                made = lax.ppermute(made, "blk", pairs)
            parts[shift] = made
        return parts

    def at_home(layer, parts, current, gate, at, of, into=None):
        last = layer == w_in.shape[0] - 1
        return home(
            layer, parts, ids, blocks, owners, current, gate, w_out, capacity, terms, at, of, chains, w_in, last, into
        )

    gate, left, *rights = first_operands(ids, blocks, pair, chains, w_in, hidden, 2 if fast else 1)
    lefts, chunks = exchange_outgoing(left, rights, n_chan, n_sub)
    count = len(chunks)
    made = [all_products(lefts, right) for right in chunks]
    homes = [at_home(0, parts, pair, gate, at, count) for at, parts in enumerate(made)]
    lefts, chunks = exchange_incoming([h[2] for h in homes], [h[3] for h in homes], n_chan, n_sub)
    made = [all_products(lefts, right) for right in chunks]
    out = None
    for at, parts in enumerate(made):
        (out,) = at_home(1, parts, homes[at][0], homes[at][1], at, count, into=out)
    return out


def solution(mesh):
    in_specs = (
        P(("groups", "blk"), "chan", "sub", None),
        P("groups", None),
        P("groups", None),
        P("groups", None, None),
        P("groups"),
        P(),
        P(),
    )
    out_specs = P(("groups", "blk"), "chan", "sub", None)
    return jax.shard_map(
        per_device, mesh=mesh, in_specs=in_specs, out_specs=out_specs, check_vma=False
    )
```

```python
import functools

import jax
import jax.numpy as jnp
from jax import lax
from jax.experimental import pallas as pl
from jax.experimental.pallas import tpu as pltpu
from jax.sharding import PartitionSpec as P

norm_epsilon = 1e-05
mebi = 1024 * 1024
vmem_limit = 56 * mebi


def sigmoid(values):
    return 0.5 + 0.5 * jnp.tanh(0.5 * values)


def layer_norm(values):
    values = values.astype(jnp.float32)
    centred = values - jnp.mean(values, axis=-1, keepdims=True)
    variance = jnp.mean(centred * centred, axis=-1, keepdims=True)
    return centred * lax.rsqrt(variance + norm_epsilon)


def alive_rows(chain_ref, start, size):
    lanes = chain_ref.shape[1]
    line = chain_ref[pl.ds(start // lanes, 1), :] >= 0
    spot = lax.broadcasted_iota(jnp.int32, (size, lanes), 0) + lax.rem(start, lanes)
    pick = jnp.logical_and(lax.broadcasted_iota(jnp.int32, (size, lanes), 1) == spot, line)
    return dot(pick.astype(jnp.float32).astype(jnp.bfloat16), jnp.ones((lanes, lanes), jnp.bfloat16))


def dot(a, b):
    return jnp.dot(a, b, preferred_element_type=jnp.float32)


def gated_pair(projected, mask, hidden):
    left = mask * sigmoid(projected[:, hidden : 2 * hidden]) * projected[:, :hidden]
    right = mask * sigmoid(projected[:, 3 * hidden : 4 * hidden]) * projected[:, 2 * hidden : 3 * hidden]
    return left.astype(jnp.bfloat16), right.astype(jnp.bfloat16)


def first_kernel(hidden, row_parts, n_chan, n_sub, ids, blocks, pair_ref, chain_ref, w_ref, gate_ref, left_ref, *rest):
    right_refs, (norm_ref, turned_ref) = rest[:row_parts], rest[row_parts:]
    slots = pl.num_programs(0)
    _, rows, cols, channels = pair_ref.shape
    block = ids[0] * slots + pl.program_id(0)
    row_alive = alive_rows(chain_ref, (blocks[0, block] * n_chan + ids[1]) * rows, rows)
    col_alive = alive_rows(chain_ref, (blocks[1, block] * n_sub + ids[2]) * cols, cols)
    group = max(1, 256 // cols)
    for start in range(0, rows, group):
        at = pl.ds(start, group)
        normed = layer_norm(pair_ref[0, at].reshape(group * cols, channels))
        norm_ref[pl.ds(start * cols, group * cols), :] = normed
        gate = sigmoid(dot(normed.astype(jnp.bfloat16), w_ref[0, :, 4 * hidden :]))
        gate_ref[0, at] = gate.reshape(group, cols, channels)
    for col in range(cols):
        turned_ref[col] = norm_ref[pl.ds(col, rows, stride=cols), :].astype(jnp.bfloat16)
    step = max(1, 128 // rows)
    part = rows // row_parts
    for start in range(0, cols, step):
        taken = turned_ref[start : start + step].reshape(step * rows, channels)
        projected = dot(taken, w_ref[0, :, : 4 * hidden])
        mask = col_alive[start : start + step][:, None, :] * row_alive[None, :, :]
        left, right = gated_pair(projected, mask.reshape(step * rows, -1), hidden)
        left_ref[0, start : start + step] = left.reshape(step, rows, hidden)
        right = right.reshape(step, rows, hidden)
        for p, right_ref in enumerate(right_refs):
            right_ref[0, start : start + step] = right[:, p * part : (p + 1) * part]


def first_operands(ids, blocks, pair, chains, w_in, hidden, row_parts):
    slots, rows, cols, channels = pair.shape
    part = rows // row_parts
    operand = jax.ShapeDtypeStruct((slots, cols, rows, hidden), jnp.bfloat16)
    right = jax.ShapeDtypeStruct((slots, cols, part, hidden), jnp.bfloat16)
    return pl.pallas_call(
        functools.partial(first_kernel, hidden, row_parts, lax.axis_size("chan"), lax.axis_size("sub")),
        grid_spec=pltpu.PrefetchScalarGridSpec(
            num_scalar_prefetch=2,
            grid=(slots,),
            in_specs=[
                pl.BlockSpec((1, rows, cols, channels), lambda s, *_: (s, 0, 0, 0)),
                pl.BlockSpec(chains.shape, lambda s, *_: (0, 0)),
                pl.BlockSpec((1,) + w_in.shape[1:], lambda s, *_: (0, 0, 0)),
            ],
            out_specs=[
                pl.BlockSpec((1, rows, cols, channels), lambda s, *_: (s, 0, 0, 0)),
                pl.BlockSpec((1, cols, rows, hidden), lambda s, *_: (s, 0, 0, 0)),
            ]
            + [pl.BlockSpec((1, cols, part, hidden), lambda s, *_: (s, 0, 0, 0))] * row_parts,
            scratch_shapes=[
                pltpu.VMEM((rows * cols, channels), jnp.float32),
                pltpu.VMEM((cols, rows, channels), jnp.bfloat16),
            ],
        ),
        out_shape=[jax.ShapeDtypeStruct(pair.shape, jnp.float32), operand] + [right] * row_parts,
        compiler_params=pltpu.CompilerParams(vmem_limit_bytes=vmem_limit),
        name="first_operands",
    )(ids, blocks, pair, chains, w_in)


def product_kernel(shift, n_blk, slots_dev, terms, capacity, pieces, n_refs, ids, owners, slots, *rest):
    refs = rest[:n_refs]
    out_ref, left_held, right_held, right_wide, chosen, sems = rest[n_refs:]
    step = pl.program_id(0)
    turn = lax.rem(step, 2)
    _, depth, n_i, hidden = left_held.shape
    n_j = right_wide.shape[1]

    @pl.when(step == 0)
    def _():
        target = lax.rem(ids[0] + shift, n_blk)
        for e in range(2 * capacity):
            chosen[e] = 0

        def scan(e, count):
            block, term = target * slots_dev + e // terms, lax.rem(e, terms)
            here = jnp.logical_and(owners[term, block] == ids[0], count < capacity)

            @pl.when(here)
            def _():
                chosen[2 * count] = slots[term, 0, block]
                chosen[2 * count + 1] = slots[term, 1, block]

            return count + here.astype(jnp.int32)

        lax.fori_loop(0, slots_dev * terms, scan, jnp.int32(0))

    def copy(n, term, buffer, source):
        side, _, _, k0, depth_of, i0, size = pieces[n]
        held = (left_held, right_held)[side]
        return pltpu.make_async_copy(
            refs[source].at[chosen[2 * term + side]],
            held.at[buffer, pl.ds(k0, depth_of), pl.ds(i0, size), :],
            sems.at[buffer, n],
        )

    def start(term, buffer):
        for n, (_, on, off, *_) in enumerate(pieces):
            if on == off:
                copy(n, term, buffer, on).start()
            else:

                @pl.when(ids[3] == 1)
                def _(n=n, on=on):
                    copy(n, term, buffer, on).start()

                @pl.when(ids[3] == 0)
                def _(n=n, off=off):
                    copy(n, term, buffer, off).start()

    @pl.when(step == 0)
    def _():
        start(0, 0)

    @pl.when(step + 1 < capacity)
    def _():
        start(step + 1, 1 - turn)

    for n, piece in enumerate(pieces):
        copy(n, step, turn, piece[1]).wait()

    span = 8

    def widen(n, carry):
        at = pl.ds(n * span, span)
        right_wide[at] = right_held[turn, at].astype(jnp.float32)
        return carry

    lax.fori_loop(0, depth // span, widen, 0)

    group = min(8, n_j)
    unroll = 4
    for j0 in range(0, n_j, group):

        def body(n, sums):
            for u in range(unroll):
                k = n * unroll + u
                left = left_held[turn, k].astype(jnp.float32).reshape(n_i // 8, 8, hidden)
                sums = tuple(
                    total + left * right_wide[k, pl.ds(j0 + j, 8, stride=0), :][None]
                    for j, total in enumerate(sums)
                )
            return sums

        zero = jnp.zeros((n_i // 8, 8, hidden), jnp.float32)
        sums = lax.fori_loop(0, depth // unroll, body, (zero,) * group)
        for j, total in enumerate(sums):
            out_ref[0, j0 + j] = total.reshape(n_i, hidden).astype(jnp.bfloat16)


def term_products(shift, ids, owners, slots, lefts, rights, capacity, slots_dev, terms):
    n_blk = lax.axis_size("blk")
    refs, pieces = [], []

    def index_of(array):
        for n, known in enumerate(refs):
            if known is array:
                return n
        refs.append(array)
        return len(refs) - 1

    for side, operands in ((0, lefts), (1, rights)):
        for on, off, k0, i0 in operands:
            pieces.append((side, index_of(on), index_of(off), k0, on.shape[1], i0, on.shape[2]))
    hidden = lefts[0][0].shape[3]
    n_i = max(p[5] + p[6] for p in pieces if p[0] == 0)
    n_j = max(p[5] + p[6] for p in pieces if p[0] == 1)
    depth = max(p[3] + p[4] for p in pieces)
    return pl.pallas_call(
        functools.partial(
            product_kernel, shift, n_blk, slots_dev, terms, capacity, tuple(pieces), len(refs)
        ),
        grid_spec=pltpu.PrefetchScalarGridSpec(
            num_scalar_prefetch=3,
            grid=(capacity,),
            in_specs=[pl.BlockSpec(memory_space=pl.ANY)] * len(refs),
            out_specs=pl.BlockSpec((1, n_j, n_i, hidden), lambda t, *_: (t, 0, 0, 0)),
            scratch_shapes=[
                pltpu.VMEM((2, depth, n_i, hidden), jnp.bfloat16),
                pltpu.VMEM((2, depth, n_j, hidden), jnp.bfloat16),
                pltpu.VMEM((depth, n_j, hidden), jnp.float32),
                pltpu.SMEM((2 * capacity,), jnp.int32),
                pltpu.SemaphoreType.DMA((2, len(pieces))),
            ],
        ),
        out_shape=jax.ShapeDtypeStruct((capacity, n_j, n_i, hidden), jnp.bfloat16),
        compiler_params=pltpu.CompilerParams(vmem_limit_bytes=vmem_limit),
        cost_estimate=pl.CostEstimate(
            flops=2 * capacity * n_i * n_j * depth * hidden * 100,
            bytes_accessed=capacity * (depth * (n_i + n_j) + n_i * n_j) * hidden * 2,
            transcendentals=0,
        ),
        name="term_products",
    )(ids, owners, slots, *refs)


def home_kernel(last, hidden, n_blk, n_chan, n_sub, at, of, slots_dev, terms, capacity, ids, blocks, owners, *rest):
    parts, rest = rest[:n_blk], rest[n_blk:]
    scratch, rest = rest[-5:], rest[:-5]
    held, turned, place, seen, sems = scratch
    cur_ref, gate_ref, w_out_ref = rest[:3]
    if last:
        out_ref = rest[-1]
    else:
        chain_ref, w_ref, out_ref, next_gate_ref, left_ref, right_ref = rest[3:]
    step = pl.program_id(0)
    _, rows, cols, channels = cur_ref.shape

    def arrival(shift):
        return pltpu.make_async_copy(parts[shift], held.at[pl.ds(shift * capacity, capacity)], sems.at[shift])

    @pl.when(step == 0)
    def _():
        for shift in range(n_blk):
            arrival(shift).start()
            seen[shift] = 0

        def scan(e, carry):
            owner = owners[lax.rem(e, terms), ids[0] * slots_dev + e // terms]
            shift = lax.rem(ids[0] - owner + n_blk, n_blk)
            count = seen[owner]
            seen[owner] = count + 1
            place[e] = shift * capacity + count
            return carry

        lax.fori_loop(0, slots_dev * terms, scan, jnp.int32(0))
        for shift in range(n_blk):
            arrival(shift).wait()

    if not last:
        block = ids[0] * slots_dev + step
        row_alive = alive_rows(chain_ref, (blocks[0, block] * n_chan + ids[1]) * rows, rows)
        col_alive = alive_rows(chain_ref, ((blocks[1, block] * n_sub + ids[2]) * of + at) * cols, cols)
    span = max(1, 128 // rows)
    for start in range(0, cols, span):
        taken = pl.ds(start, span)
        total = held[place[step * terms], taken].astype(jnp.float32)
        for t in range(1, terms):
            total = total + held[place[step * terms + t], taken].astype(jnp.float32)
        rounded = total.astype(jnp.bfloat16).astype(jnp.float32)
        turned[pl.ds(start * rows, span * rows), :] = rounded.reshape(span * rows, hidden)
    group = min(rows, max(1, 256 // cols))
    for start in range(0, rows, group):
        taken = pl.ds(start, group)
        mixture = jnp.concatenate(
            [turned[pl.ds(row, cols, stride=rows), :].astype(jnp.bfloat16) for row in range(start, start + group)]
        )
        update = dot(layer_norm(mixture).astype(jnp.bfloat16), w_out_ref[0])
        current = cur_ref[0, taken].astype(jnp.float32).reshape(group * cols, channels)
        gate = gate_ref[0, taken].reshape(group * cols, channels)
        result = (current + gate * update).astype(jnp.bfloat16)
        out_ref[0, taken] = result.reshape(group, cols, channels)
        if not last:
            normed = layer_norm(result).astype(jnp.bfloat16)
            projected = dot(normed, w_ref[0])
            next_gate_ref[0, taken] = sigmoid(projected[:, 4 * hidden :]).reshape(group, cols, channels)
            mask = row_alive[start : start + group][:, None, :] * col_alive[None, :, :]
            left, right = gated_pair(projected, mask.reshape(group * cols, channels), hidden)
            left_ref[0, taken] = left.reshape(group, cols, hidden)
            right_ref[0, taken] = right.reshape(group, cols, hidden)


def home(layer, parts, ids, blocks, owners, current, gate, w_out, capacity, terms, at, of, chains, w_in, last, into=None):
    n_blk = len(parts)
    slots, rows, _, channels = current.shape
    hidden = w_out.shape[1]
    cols = parts[0].shape[1]
    chunk = (1, rows, cols, channels)

    def chunk_spec(array):
        whole = array.shape[2] != cols
        return pl.BlockSpec(chunk, lambda s, *_: (s, 0, at if whole else 0, 0))

    def layer_spec(array, index):
        return pl.BlockSpec((1,) + array.shape[1:], lambda s, *_: (index, 0, 0))

    in_specs = [pl.BlockSpec(memory_space=pl.ANY)] * n_blk + [
        chunk_spec(current),
        chunk_spec(gate),
        layer_spec(w_out, layer),
    ]
    operands = [*parts, current, gate, w_out]
    aliases = {}
    if last:
        if into is not None:
            aliases = {3 + len(operands): 0}
            operands.append(into)
            in_specs.append(pl.BlockSpec(memory_space=pl.ANY))
        out_shape = [jax.ShapeDtypeStruct((slots, rows, cols * of, channels), jnp.bfloat16)]
        out_specs = [pl.BlockSpec(chunk, lambda s, *_: (s, 0, at, 0))]
    else:
        operands += [chains, w_in]
        in_specs += [pl.BlockSpec(chains.shape, lambda s, *_: (0, 0)), layer_spec(w_in, layer + 1)]
        small = (slots, rows, cols, channels)
        out_shape = [jax.ShapeDtypeStruct(small, t) for t in (jnp.bfloat16, jnp.float32, jnp.bfloat16, jnp.bfloat16)]
        out_specs = [pl.BlockSpec(chunk, lambda s, *_: (s, 0, 0, 0))] * 4
    return pl.pallas_call(
        functools.partial(
            home_kernel, last, hidden, n_blk, lax.axis_size("chan"), lax.axis_size("sub"), at, of, slots, terms, capacity
        ),
        grid_spec=pltpu.PrefetchScalarGridSpec(
            num_scalar_prefetch=3,
            grid=(slots,),
            in_specs=in_specs,
            out_specs=out_specs,
            scratch_shapes=[
                pltpu.VMEM((n_blk * capacity, cols, rows, hidden), jnp.bfloat16),
                pltpu.VMEM((rows * cols, hidden), jnp.float32),
                pltpu.SMEM((slots * terms,), jnp.int32),
                pltpu.SMEM((n_blk,), jnp.int32),
                pltpu.SemaphoreType.DMA((n_blk,)),
            ],
        ),
        out_shape=out_shape,
        input_output_aliases=aliases,
        compiler_params=pltpu.CompilerParams(vmem_limit_bytes=vmem_limit),
        cost_estimate=pl.CostEstimate(
            flops=2 * slots * rows * cols * channels * 6 * channels * 10,
            bytes_accessed=slots * rows * cols * channels * 16,
            transcendentals=0,
        ),
        name="home",
    )(ids, blocks, owners, *operands)


def exchange_outgoing(left, rights, n_chan, n_sub):
    if n_chan == 2 and n_sub == 2:
        both = ("chan", "sub")
        other_left = lax.ppermute(left, "sub", [(0, 1), (1, 0)])
        lefts = [(other_left, left, 0, 0), (left, other_left, left.shape[1], 0)]
        chunks = []
        for right in rights:
            if chunks:
                (one, *_), (_, two, *_) = chunks[-1]
                right, *_ = lax.optimization_barrier((right, one, two))
            one = lax.ppermute(right, both, [(0, 2), (3, 1), (1, 0), (2, 3)])
            two = lax.ppermute(right, both, [(1, 2), (2, 1)])
            chunks.append([(one, one, 0, 0), (right, two, right.shape[1], 0)])
        return lefts, chunks
    left = lax.all_gather(left, "sub", axis=1, tiled=True)
    right = jnp.concatenate(rights, axis=2)
    right = lax.all_gather(right, "chan", axis=2, tiled=True)
    right = lax.all_to_all(right, "sub", split_axis=2, concat_axis=1, tiled=True)
    cols = right.shape[2] // 2
    chunks = [right[:, :, :cols], right[:, :, cols:]]
    return [(left, left, 0, 0)], [[(r, r, 0, 0)] for r in chunks]


def exchange_incoming(lefts, rights, n_chan, n_sub):
    if n_chan == 2 and n_sub == 2:
        both = ("chan", "sub")
        left_pieces, chunks = [], []
        at = 0
        for left, right in zip(lefts, rights):
            depth = left.shape[1]
            one = lax.ppermute(left, both, [(1, 3), (2, 0), (0, 1), (3, 2)])
            two = lax.ppermute(one, both, [(0, 1), (3, 2)])
            left_pieces += [(left, one, 0, at), (one, two, depth, at)]
            other = lax.ppermute(right, "chan", [(0, 1), (1, 0)])
            chunks.append([(right, right, 0, 0), (other, other, depth, 0)])
            at += left.shape[2]
        return left_pieces, chunks
    left = lax.all_gather(jnp.concatenate(lefts, axis=2), "chan", axis=1, tiled=True)
    left = lax.all_gather(left, "sub", axis=2, tiled=True)
    size = left.shape[2] // n_chan
    left = lax.dynamic_slice_in_dim(left, lax.axis_index("chan") * size, size, 2)
    gathered = [lax.all_gather(right, "chan", axis=1, tiled=True) for right in rights]
    return [(left, left, 0, 0)], [[(r, r, 0, 0)] for r in gathered]


def lane_group(shape, size):
    return lax.broadcasted_iota(jnp.int32, shape, 1) // size


def spread_kernel(size, w_ref, wide_ref):
    hidden = w_ref.shape[1]
    parts = hidden // size
    for side in range(2):
        for kind in range(2):
            start = (2 * side + kind) * hidden
            weights = 0.5 * w_ref[0, :, start : start + hidden].astype(jnp.float32)
            group = lane_group(weights.shape, size)
            for part in range(parts):
                kept = jnp.where(group == part, weights, 0.0)
                at = ((side * parts + part) * 2 + kind) * hidden
                for a in range(parts):
                    moved = pltpu.roll(kept, ((a - part) % parts) * size, 1) if a != part else kept
                    wide_ref[a * hidden : (a + 1) * hidden, at : at + hidden] = moved.astype(jnp.bfloat16)


def spread_weights(w_in, layer, size):
    hidden = w_in.shape[1]
    parts = hidden // size
    shape = (parts * hidden, 4 * parts * hidden)
    return pl.pallas_call(
        functools.partial(spread_kernel, size),
        grid=(1,),
        in_specs=[pl.BlockSpec((1,) + w_in.shape[1:], lambda s: (layer, 0, 0))],
        out_specs=pl.BlockSpec(shape, lambda s: (0, 0)),
        out_shape=jax.ShapeDtypeStruct(shape, jnp.bfloat16),
        compiler_params=pltpu.CompilerParams(vmem_limit_bytes=16 * mebi),
        cost_estimate=pl.CostEstimate(flops=1 << 30, bytes_accessed=1 << 20, transcendentals=0),
        name="spread_weights",
    )(w_in)


def swap_matrix(half):
    shape = (half * half, half * half)
    to, of = lax.broadcasted_iota(jnp.int32, shape, 0), lax.broadcasted_iota(jnp.int32, shape, 1)
    same = jnp.logical_and(to // half == lax.rem(of, half), lax.rem(to, half) == of // half)
    return same.astype(jnp.float32).astype(jnp.bfloat16)


def swapped(values, swap_ref):
    half, _, lanes = values.shape
    moved = dot(swap_ref[...], values.reshape(half * half, lanes))
    return moved.astype(jnp.bfloat16).reshape(half, half, lanes)


def turn(taken, turned, swap_ref):
    half = 16
    for x in range(0, taken.shape[0], half):
        for y in range(0, taken.shape[1], half):
            turned[y : y + half, x : x + half] = swapped(taken[x : x + half, y : y + half], swap_ref)


def make_operand(side, taken, wide_ref, out_refs, laid, swap_ref):
    rows, size, hidden = taken.shape
    parts, bands, half = hidden // size, size, 16
    groups = rows // parts
    stacked = jnp.concatenate(
        [jnp.concatenate([taken[g * parts + a] for a in range(parts)], axis=1) for g in range(groups)], axis=0
    )
    for part in range(parts):
        at = (side * parts + part) * 2 * hidden
        made = dot(stacked, wide_ref[:, at : at + 2 * hidden])
        value = made[:, :hidden] * (1.0 + jnp.tanh(made[:, hidden:]))
        laid[side, :, part * size : (part + 1) * size, :] = value.astype(jnp.bfloat16).reshape(groups, size, hidden)
    blocks = [laid[side, g].T for g in range(groups)]
    starts = [sum(ref.shape[1] for ref in out_refs[:n]) for n in range(len(out_refs))]
    for first in range(0, bands, half):
        for row in range(0, rows, half):
            tiles = []
            for r in range(row, row + half):
                at = r % parts * bands + first
                tiles.append(blocks[r // parts][at : at + half])
            moved = swapped(jnp.stack(tiles), swap_ref)
            for start, ref in zip(starts, out_refs):
                low, high = max(start, first), min(start + ref.shape[1], first + half)
                if low < high:
                    ref[0, low - start : high - start, row : row + half] = moved[low - first : high - first]


def open_layer(layer, natural, left_refs, right_refs, wide, laid, turned, swap):
    turn(natural, turned, swap)
    for side, refs in ((0, left_refs), (1, right_refs)):
        make_operand(side, natural if side == layer % 2 else turned[...], wide, refs, laid, swap)


def norm_and_gate(values, row_alive, col_alive, w_ref, at, norm_ref, gate_ref):
    _, cols, channels = norm_ref.shape
    rows = values.shape[0] // cols
    normed = layer_norm(values)
    gate = sigmoid(dot(normed.astype(jnp.bfloat16), w_ref[0, :, -channels:]))
    gate_ref[0, pl.ds(at, rows)] = gate.reshape(rows, cols, channels)
    mask = row_alive[at : at + rows, None, :] * col_alive[None, :, :]
    norm_ref[pl.ds(at, rows)] = (normed.reshape(rows, cols, channels) * mask).astype(jnp.bfloat16)


def open_kernel(hidden, chunks, n_chan, n_sub, base, of, ids, blocks, pair_ref, chain_ref, w_ref, wide, *rest):
    gate_ref, *operand_refs, norm_ref, laid, turned, swap = rest[-(2 * chunks + 5) :]
    step = pl.program_id(0)
    _, rows, cols, channels = pair_ref.shape
    block = ids[0] * of + base + step

    @pl.when(step == 0)
    def _():
        swap[...] = swap_matrix(16)

    row_alive = alive_rows(chain_ref, (blocks[0, block] * n_chan + ids[1]) * rows, rows)
    col_alive = alive_rows(chain_ref, (blocks[1, block] * n_sub + ids[2]) * cols, cols)
    group = hidden // cols
    for at in range(0, rows, group):
        values = pair_ref[0, pl.ds(at, group)].reshape(group * cols, channels)
        norm_and_gate(values, row_alive, col_alive, w_ref, at, norm_ref, gate_ref)
    open_layer(0, norm_ref[...], operand_refs[:chunks], operand_refs[chunks:], wide, laid, turned, swap)


def operand_scratch(rows, size, hidden):
    parts = hidden // size
    return [
        pltpu.VMEM((2, rows // parts, parts * size, hidden), jnp.bfloat16),
        pltpu.VMEM((size, rows, hidden), jnp.bfloat16),
        pltpu.VMEM((256, 256), jnp.bfloat16),
    ]


def operand_outputs(slots, count, rows, hidden, bands):
    kept = [count if n == 0 else slots for n in range(len(bands))] * 2
    return [jax.ShapeDtypeStruct((k, b, rows, hidden), jnp.bfloat16) for k, b in zip(kept, bands * 2)]


def slot_specs(arrays, slots, base):
    def spec(array):
        offset = base if array.shape[0] == slots else 0
        return pl.BlockSpec((1,) + array.shape[1:], lambda s, *_: (s + offset, 0, 0, 0))

    return [spec(a) for a in arrays]


def fill(out_shape, earlier, slots, n_before):
    if earlier is None:
        return [], [], {}
    shared = [n for n, o in enumerate(out_shape) if o.shape[0] == slots]
    specs = [pl.BlockSpec(memory_space=pl.ANY)] * len(shared)
    return [earlier[n] for n in shared], specs, {n_before + k: n for k, n in enumerate(shared)}


def open_operands(ids, blocks, pair, chains, w_in, wide, hidden, bands, base, count, earlier):
    slots, rows, cols, channels = pair.shape
    out_shape = [jax.ShapeDtypeStruct(pair.shape, jnp.float32)] + operand_outputs(slots, count, rows, hidden, bands)
    more, more_specs, aliases = fill(out_shape, earlier, slots, 6)
    return pl.pallas_call(
        functools.partial(open_kernel, hidden, len(bands), lax.axis_size("chan"), lax.axis_size("sub"), base, slots),
        grid_spec=pltpu.PrefetchScalarGridSpec(
            num_scalar_prefetch=2,
            grid=(count,),
            in_specs=slot_specs([pair], slots, base)
            + [
                pl.BlockSpec(chains.shape, lambda s, *_: (0, 0)),
                pl.BlockSpec((1,) + w_in.shape[1:], lambda s, *_: (0, 0, 0)),
                pl.BlockSpec(wide.shape, lambda s, *_: (0, 0)),
            ]
            + more_specs,
            out_specs=slot_specs(out_shape, slots, base),
            scratch_shapes=[pltpu.VMEM((rows, cols, channels), jnp.bfloat16)] + operand_scratch(rows, cols, hidden),
        ),
        out_shape=out_shape,
        input_output_aliases=aliases,
        compiler_params=pltpu.CompilerParams(vmem_limit_bytes=28 * mebi),
        cost_estimate=pl.CostEstimate(flops=1 << 33, bytes_accessed=1 << 20, transcendentals=0),
        name="open_operands",
    )(ids, blocks, pair, chains, w_in, wide, *more)


def plan_kernel(n_blk, slots_dev, terms, capacity, ids, owners, slots, chosen, place, seen):
    for shift in range(n_blk):
        seen[shift] = 0
        target = lax.rem(ids[0] + shift, n_blk)
        for e in range(2 * (capacity + 1)):
            chosen[2 * shift * (capacity + 1) + e] = 0
        found = jnp.int32(0)
        for e in range(slots_dev * terms):
            block, term = target * slots_dev + e // terms, e % terms
            at = 2 * (shift * (capacity + 1) + jnp.minimum(found, capacity))
            chosen[at] = slots[term, 0, block]
            chosen[at + 1] = slots[term, 1, block]
            found = found + (owners[term, block] == ids[0]).astype(jnp.int32)
    for e in range(slots_dev * terms):
        owner = owners[e % terms, ids[0] * slots_dev + e // terms]
        count = seen[owner]
        seen[owner] = count + 1
        place[e] = lax.rem(ids[0] - owner + n_blk, n_blk) * capacity + count


def make_plan(ids, owners, slots, n_blk, slots_dev, terms, capacity):
    scalars = pl.BlockSpec(memory_space=pltpu.SMEM)
    return pl.pallas_call(
        functools.partial(plan_kernel, n_blk, slots_dev, terms, capacity),
        in_specs=[scalars] * 3,
        out_specs=[scalars] * 2,
        out_shape=[
            jax.ShapeDtypeStruct((2 * n_blk * (capacity + 1),), jnp.int32),
            jax.ShapeDtypeStruct((slots_dev * terms,), jnp.int32),
        ],
        scratch_shapes=[pltpu.SMEM((n_blk,), jnp.int32)],
        name="make_plan",
    )(ids, owners, slots)


def banded_kernel(shifts, capacity, pieces, n_refs, size, ids, chosen, *rest):
    refs, rest = rest[:n_refs], rest[n_refs:]
    out_refs, (left_held, right_held, out_held, sems, out_sems) = rest[: len(shifts)], rest[len(shifts) :]
    halves, _, bands, rows, hidden = left_held.shape
    parts = hidden // size

    def copy(n, source):
        side, half, base, *_ = pieces[n]
        target = (left_held, right_held)[side].at[half, pl.ds(base, refs[source].shape[0])]
        return pltpu.make_async_copy(refs[source], target, sems.at[n])

    for n, (*_, on, off) in enumerate(pieces):
        if on == off:
            copy(n, on).start()
        else:

            @pl.when(ids[3] == 1)
            def _(n=n, on=on):
                copy(n, on).start()

            @pl.when(ids[3] == 0)
            def _(n=n, off=off):
                copy(n, off).start()

    for n, piece in enumerate(pieces):
        copy(n, piece[-1]).wait()

    def leave(n):
        return pltpu.make_async_copy(out_held.at[pl.ds(n * capacity, capacity)], out_refs[n], out_sems.at[n])

    for n, shift in enumerate(shifts):

        def one(term, carry, n=n, shift=shift):
            at = 2 * (shift * (capacity + 1) + term)
            left_slot, right_slot = chosen[at], chosen[at + 1]
            group = lane_group((size, hidden), size)
            for band in range(bands):
                left = jnp.concatenate([left_held[h, left_slot, band] for h in range(halves)], axis=1)
                apart = []
                for h in range(halves):
                    right = right_held[h, right_slot, band]
                    apart += [jnp.where(group == part, right, jnp.zeros_like(right)) for part in range(parts)]
                made = dot(left, jnp.concatenate(apart, axis=0))
                out_held[n * capacity + term, band] = made.astype(jnp.bfloat16)
            return carry

        lax.fori_loop(0, capacity, one, 0)
        leave(n).start()
    for n in range(len(shifts)):
        leave(n).wait()


def banded_products(shifts, ids, chosen, operands, capacity, size):
    refs, pieces = [], []

    def index_of(array):
        for n, known in enumerate(refs):
            if known is array:
                return n
        refs.append(array)
        return len(refs) - 1

    slots = 0
    for both in operands:
        for side in range(2):
            for half, (on, off) in enumerate(both[side]):
                pieces.append((side, half, slots, index_of(on), index_of(off)))
        slots += both[0][0][0].shape[0]
    halves = len(operands[0][0])
    _, bands, rows, hidden = operands[0][0][0][0].shape
    count = len(shifts) * capacity
    anywhere = pl.BlockSpec(memory_space=pl.ANY)
    return pl.pallas_call(
        functools.partial(banded_kernel, shifts, capacity, tuple(pieces), len(refs), size),
        grid_spec=pltpu.PrefetchScalarGridSpec(
            num_scalar_prefetch=2,
            grid=(),
            in_specs=[anywhere] * len(refs),
            out_specs=[anywhere] * len(shifts),
            scratch_shapes=[
                pltpu.VMEM((halves, slots, bands, rows, hidden), jnp.bfloat16),
                pltpu.VMEM((halves, slots, bands, size, hidden), jnp.bfloat16),
                pltpu.VMEM((count, bands, rows, hidden), jnp.bfloat16),
                pltpu.SemaphoreType.DMA((len(pieces),)),
                pltpu.SemaphoreType.DMA((len(shifts),)),
            ],
        ),
        out_shape=[jax.ShapeDtypeStruct((capacity, bands, rows, hidden), jnp.bfloat16)] * len(shifts),
        compiler_params=pltpu.CompilerParams(vmem_limit_bytes=14 * mebi),
        cost_estimate=pl.CostEstimate(
            flops=2 * count * bands * rows * hidden * hidden * halves, bytes_accessed=1, transcendentals=0
        ),
        name="banded_products",
    )(ids, chosen, *refs)


def close_kernel(layer, last, n_parts, n_blk, n_chan, n_sub, base, of, terms, capacity, ids, blocks, place, *rest):
    chunks = n_parts // n_blk
    arrived, rest = rest[:n_parts], rest[n_parts:]
    cur_ref, gate_ref, w_out_ref = rest[:3]
    if last:
        out_ref, held, wide_out, sems, swap = rest[3:]
    else:
        chain_ref, w_ref, wide = rest[3:6]
        out_ref, next_gate_ref, *operand_refs, held, wide_out, sems, norm_ref, laid, turned, swap = rest[
            -(2 * chunks + 9) :
        ]
        left_refs, right_refs = operand_refs[:chunks], operand_refs[chunks:]
    step = pl.program_id(0)
    _, rows, cols, channels = cur_ref.shape
    _, bands, _, hidden = held.shape
    parts, size = hidden // bands, bands

    def arrival(n):
        at = sum(arrived[m * n_blk].shape[1] for m in range(n // n_blk))
        count = arrived[n].shape[1]
        target = held.at[pl.ds(n % n_blk * capacity, capacity), pl.ds(at, count)]
        return pltpu.make_async_copy(arrived[n], target, sems.at[n])

    @pl.when(step == 0)
    def _():
        for n in range(n_parts):
            arrival(n).start()
        wide_out[...] = jnp.zeros_like(wide_out)
        for part in range(parts):
            for a in range(parts):
                at = (part * parts + a) * bands
                wide_out[at : at + bands, a * channels : (a + 1) * channels] = w_out_ref[
                    0, part * bands : (part + 1) * bands, :
                ]
        swap[...] = swap_matrix(16)
        for n in range(n_parts):
            arrival(n).wait()

    if not last:
        block = ids[0] * of + base + step
        row_alive = alive_rows(chain_ref, (blocks[0, block] * n_chan + ids[1]) * rows, rows)
        col_alive = alive_rows(chain_ref, (blocks[1, block] * n_sub + ids[2]) * cols, cols)
    half = 16
    by_row = [[] for _ in range(rows)]
    for row in range(0, rows, half):
        for band in range(0, bands, half):
            taken = pl.ds(band, half), pl.ds(row, half)
            total = held[(place[(base + step) * terms], *taken)].astype(jnp.float32)
            for t in range(1, terms):
                total = total + held[(place[(base + step) * terms + t], *taken)].astype(jnp.float32)
            moved = swapped(total.astype(jnp.bfloat16), swap)
            for r in range(half):
                by_row[row + r].append(moved[r])
    groups = rows // parts
    pieces = []
    for g in range(groups):
        block = jnp.concatenate([x for a in range(parts) for x in by_row[g * parts + a]]).T
        pieces.append(jnp.concatenate([block[p * cols : (p + 1) * cols] for p in range(parts)], axis=1))
    mixture = jnp.concatenate(pieces)
    together = (lane_group((hidden, hidden), size) == lax.broadcasted_iota(jnp.int32, (hidden, hidden), 0) // size)
    together = together.astype(jnp.float32).astype(jnp.bfloat16)
    average = dot(mixture, jnp.concatenate([together] * parts)) * (1.0 / hidden)
    centred = [mixture[:, p * hidden : (p + 1) * hidden].astype(jnp.float32) - average for p in range(parts)]
    squares = sum(c * c for c in centred)
    high = squares.astype(jnp.bfloat16)
    low = (squares - high.astype(jnp.float32)).astype(jnp.bfloat16)
    variance = dot(jnp.concatenate([high, low], axis=1), jnp.concatenate([together] * 2)) * (1.0 / hidden)
    scale = lax.rsqrt(variance + norm_epsilon)
    normed = jnp.concatenate([(c * scale).astype(jnp.bfloat16) for c in centred], axis=1)
    update = dot(normed, wide_out[...])
    for g in range(groups):
        taken = pl.ds(g * parts, parts)
        change = jnp.concatenate(
            [update[g * cols : (g + 1) * cols, a * channels : (a + 1) * channels] for a in range(parts)]
        )
        gate = gate_ref[0, taken].reshape(parts * cols, channels)
        current = cur_ref[0, taken].astype(jnp.float32).reshape(parts * cols, channels)
        result = (current + gate * change).astype(jnp.bfloat16)
        out_ref[0, taken] = result.reshape(parts, cols, channels)
        if not last:
            norm_and_gate(result, row_alive, col_alive, w_ref, g * parts, norm_ref, next_gate_ref)
    if not last:
        open_layer(layer + 1, norm_ref[...], left_refs, right_refs, wide, laid, turned, swap)


def close_layer(
    layer, arrived, ids, blocks, place, current, gate, w_out, capacity, terms, chains, w_in, wide, last, bands, base, count, earlier
):
    n_blk = len(arrived[0])
    flat = [part for chunk in arrived for part in chunk]
    slots, rows, cols, channels = current.shape
    hidden = w_out.shape[1]

    def layer_spec(array, index):
        return pl.BlockSpec((1,) + array.shape[1:], lambda s, *_: (index, 0, 0))

    in_specs = [pl.BlockSpec(memory_space=pl.ANY)] * len(flat)
    in_specs += slot_specs([current, gate], slots, base) + [layer_spec(w_out, layer)]
    operands = [*flat, current, gate, w_out]
    out_shape = [jax.ShapeDtypeStruct(current.shape, jnp.bfloat16)]
    scratch = [
        pltpu.VMEM((n_blk * capacity, sum(bands[layer]), rows, hidden), jnp.bfloat16),
        pltpu.VMEM((hidden // cols * hidden, hidden // cols * channels), jnp.bfloat16),
        pltpu.SemaphoreType.DMA((len(flat),)),
    ]
    if not last:
        operands += [chains, w_in, wide]
        in_specs += [pl.BlockSpec(chains.shape, lambda s, *_: (0, 0)), layer_spec(w_in, layer + 1)]
        in_specs += [pl.BlockSpec(wide.shape, lambda s, *_: (0, 0))]
        out_shape += [jax.ShapeDtypeStruct(current.shape, jnp.float32)]
        out_shape += operand_outputs(slots, count, cols, hidden, bands[layer + 1])
        scratch += [pltpu.VMEM((rows, cols, channels), jnp.bfloat16)] + operand_scratch(cols, rows, hidden)
    else:
        scratch += [pltpu.VMEM((256, 256), jnp.bfloat16)]
    more, more_specs, aliases = fill(out_shape, earlier, slots, 3 + len(operands))
    return pl.pallas_call(
        functools.partial(
            close_kernel,
            *(layer, last, len(flat), n_blk, lax.axis_size("chan"), lax.axis_size("sub"), base, slots, terms, capacity),
        ),
        grid_spec=pltpu.PrefetchScalarGridSpec(
            num_scalar_prefetch=3,
            grid=(count,),
            in_specs=in_specs + more_specs,
            out_specs=slot_specs(out_shape, slots, base),
            scratch_shapes=scratch,
        ),
        out_shape=out_shape,
        input_output_aliases=aliases,
        compiler_params=pltpu.CompilerParams(vmem_limit_bytes=32 * mebi),
        cost_estimate=pl.CostEstimate(flops=1 << 33, bytes_accessed=1 << 20, transcendentals=0),
        name="close_layer",
    )(ids, blocks, place, *operands, *more)


def after(value, *others):
    return lax.optimization_barrier((value, *others))[0]


def exchange_bands_outgoing(left, right, over):
    both = ("chan", "sub")
    other = lax.ppermute(left, "sub", [(0, 1), (1, 0)])
    one = lax.ppermute(right, both, [(0, 2), (3, 1), (1, 0), (2, 3)])
    two = lax.ppermute(right, both, [(1, 2), (2, 1)])
    return [(other, left), (left, other)], [(one, one), (right, two)]


def exchange_bands_incoming(left, right, over):
    both = ("chan", "sub")
    one = lax.ppermute(left, both, [(1, 3), (2, 0), (0, 1), (3, 2)])
    other = lax.ppermute(right, "chan", [(0, 1), (1, 0)])
    two = lax.ppermute(after(one, over), both, [(0, 1), (3, 2)])
    return [(left, one), (one, two)], [(right, right), (other, other)]


def banded(pair, ids, blocks, owners, slot_of, chains, w_in, w_out, capacity, terms, n_blk):
    slots, rows, cols, channels = pair.shape
    hidden = w_out.shape[1]
    far = n_blk // 2
    shifts = [far] + [s for s in range(1, n_blk) if s != far] + [0]
    layers = w_in.shape[0]
    current = pair
    bands = [[12, 20], [14, 18]]
    chosen, place = make_plan(ids, owners, slot_of, n_blk, slots, terms, capacity)
    half = slots // 2
    halves = [(0, half), (half, slots - half)]
    for layer in range(layers):
        count = len(bands[layer])
        if layer == 0:
            calls, wide = [None], spread_weights(w_in, 0, cols)
            for base, size in halves:
                calls.append(open_operands(ids, blocks, pair, chains, w_in, wide, hidden, bands[0], base, size, calls[-1]))
            gate = calls[-1][0]
        operands = [call[-2 * count :] for call in calls[1:]]
        exchange = exchange_bands_incoming if layer % 2 else exchange_bands_outgoing
        arrived = []
        for chunk in range(count):
            if chunk == 0:
                exchanged = []
                over = operands[-1][count]
                for left, right in [(o[0], o[count]) for o in operands]:
                    if exchanged and layer % 2:
                        (_, (one, _)), (_, (other, _)) = exchanged[-1]
                        left, right = lax.optimization_barrier((left, right, one, other))[:2]
                    elif exchanged:
                        ((other, _), _), ((one, _), (_, two)) = exchanged[-1]
                        left, right = lax.optimization_barrier((left, right, other, one, two))[:2]
                    exchanged.append(exchange(left, right, over))
            else:
                left, right = operands[-1][chunk], operands[-1][count + chunk]
                last_of = exchanged[-1]
                left, right = lax.optimization_barrier(
                    (left, right, last_of[0][1][1], last_of[0][0][0], last_of[1][0][1], last_of[1][1][1])
                    + ((made[-1],) if layer % 2 == 0 else ())
                )[:2]
                exchanged = [exchange(left, right, arrived[-1][far])]
            made = banded_products(shifts, ids, chosen, exchanged, capacity, cols)
            parts = [None] * n_blk
            for shift, part in zip(shifts, made):
                if shift:
                    if arrived:
                        part = after(part, arrived[-1][shift])
                    part = lax.ppermute(part, "blk", [(p, (p + shift) % n_blk) for p in range(n_blk)])
                parts[shift] = part
            arrived.append(parts)
        last = layer == layers - 1
        calls = [None]
        if not last:
            wide = spread_weights(after(w_in, made[-1]), layer + 1, cols)
        for base, size in [(0, slots)] if last else halves:
            calls.append(
                close_layer(
                    *(layer, arrived, ids, blocks, place, current, gate, w_out, capacity, terms, chains, w_in, wide, last),
                    *(bands, base, size, calls[-1]),
                )
            )
        if last:
            return calls[-1][0]
        current, gate = calls[-1][:2]


def per_device(pair, block_list, term_owner, term_slots, chain_ids, w_in, w_out):
    n_blk = lax.axis_size("blk")
    n_chan = lax.axis_size("chan")
    n_sub = lax.axis_size("sub")
    position = lax.axis_index("blk")
    row_group = lax.axis_index("chan")
    col_group = lax.axis_index("sub")
    slots, rows, cols, channels = pair.shape
    hidden = w_out.shape[1]
    terms = term_owner.shape[1]
    capacity = max(2, -(-slots * terms // n_blk))
    fast = n_chan == 2 and n_sub == 2
    on_diagonal = (row_group == col_group).astype(jnp.int32)
    ids = jnp.stack([position, row_group, col_group, on_diagonal]).astype(jnp.int32)
    blocks = block_list.T
    owners = term_owner.T
    slot_of = jnp.transpose(term_slots, (1, 2, 0))
    chains = chain_ids.reshape(-1, 128)
    if fast and rows == cols == 32 and channels == hidden == 128:
        return banded(pair, ids, blocks, owners, slot_of, chains, w_in, w_out, capacity, terms, n_blk)
    shifts = [n_blk // 2] + [s for s in range(1, n_blk) if s != n_blk // 2] + [0]

    def all_products(lefts, right):
        parts = [None] * n_blk
        for shift in shifts:
            made = term_products(shift, ids, owners, slot_of, lefts, right, capacity, slots, terms)
            if shift:
                pairs = [(p, (p + shift) % n_blk) for p in range(n_blk)]
                made = lax.ppermute(made, "blk", pairs)
            parts[shift] = made
        return parts

    def at_home(layer, parts, current, gate, at, of, into=None):
        last = layer == w_in.shape[0] - 1
        return home(
            layer, parts, ids, blocks, owners, current, gate, w_out, capacity, terms, at, of, chains, w_in, last, into
        )

    gate, left, *rights = first_operands(ids, blocks, pair, chains, w_in, hidden, 2 if fast else 1)
    lefts, chunks = exchange_outgoing(left, rights, n_chan, n_sub)
    count = len(chunks)
    made = [all_products(lefts, right) for right in chunks]
    homes = [at_home(0, parts, pair, gate, at, count) for at, parts in enumerate(made)]
    lefts, chunks = exchange_incoming([h[2] for h in homes], [h[3] for h in homes], n_chan, n_sub)
    made = [all_products(lefts, right) for right in chunks]
    out = None
    for at, parts in enumerate(made):
        (out,) = at_home(1, parts, homes[at][0], homes[at][1], at, count, into=out)
    return out


def solution(mesh):
    in_specs = (
        P(("groups", "blk"), "chan", "sub", None),
        P("groups", None),
        P("groups", None),
        P("groups", None, None),
        P("groups"),
        P(),
        P(),
    )
    out_specs = P(("groups", "blk"), "chan", "sub", None)
    return jax.shard_map(
        per_device, mesh=mesh, in_specs=in_specs, out_specs=out_specs, check_vma=False
    )
```

```python
import functools

import jax
import jax.numpy as jnp
from jax import lax
from jax.experimental import pallas as pl
from jax.experimental.pallas import tpu as pltpu
from jax.sharding import PartitionSpec as P

norm_epsilon = 1e-05
mebi = 1024 * 1024
vmem_limit = 56 * mebi


def sigmoid(values):
    return 0.5 + 0.5 * jnp.tanh(0.5 * values)


def layer_norm(values):
    values = values.astype(jnp.float32)
    centred = values - jnp.mean(values, axis=-1, keepdims=True)
    variance = jnp.mean(centred * centred, axis=-1, keepdims=True)
    return centred * lax.rsqrt(variance + norm_epsilon)


def alive_rows(chain_ref, start, size):
    lanes = chain_ref.shape[1]
    line = chain_ref[pl.ds(start // lanes, 1), :] >= 0
    spot = lax.broadcasted_iota(jnp.int32, (size, lanes), 0) + lax.rem(start, lanes)
    pick = jnp.logical_and(lax.broadcasted_iota(jnp.int32, (size, lanes), 1) == spot, line)
    return dot(pick.astype(jnp.float32).astype(jnp.bfloat16), jnp.ones((lanes, lanes), jnp.bfloat16))


def dot(a, b):
    return jnp.dot(a, b, preferred_element_type=jnp.float32)


def gated_pair(projected, mask, hidden):
    left = mask * sigmoid(projected[:, hidden : 2 * hidden]) * projected[:, :hidden]
    right = mask * sigmoid(projected[:, 3 * hidden : 4 * hidden]) * projected[:, 2 * hidden : 3 * hidden]
    return left.astype(jnp.bfloat16), right.astype(jnp.bfloat16)


def first_kernel(hidden, row_parts, n_chan, n_sub, ids, blocks, pair_ref, chain_ref, w_ref, gate_ref, left_ref, *rest):
    right_refs, (norm_ref, turned_ref) = rest[:row_parts], rest[row_parts:]
    slots = pl.num_programs(0)
    _, rows, cols, channels = pair_ref.shape
    block = ids[0] * slots + pl.program_id(0)
    row_alive = alive_rows(chain_ref, (blocks[0, block] * n_chan + ids[1]) * rows, rows)
    col_alive = alive_rows(chain_ref, (blocks[1, block] * n_sub + ids[2]) * cols, cols)
    group = max(1, 256 // cols)
    for start in range(0, rows, group):
        at = pl.ds(start, group)
        normed = layer_norm(pair_ref[0, at].reshape(group * cols, channels))
        norm_ref[pl.ds(start * cols, group * cols), :] = normed
        gate = sigmoid(dot(normed.astype(jnp.bfloat16), w_ref[0, :, 4 * hidden :]))
        gate_ref[0, at] = gate.reshape(group, cols, channels)
    for col in range(cols):
        turned_ref[col] = norm_ref[pl.ds(col, rows, stride=cols), :].astype(jnp.bfloat16)
    step = max(1, 128 // rows)
    part = rows // row_parts
    for start in range(0, cols, step):
        taken = turned_ref[start : start + step].reshape(step * rows, channels)
        projected = dot(taken, w_ref[0, :, : 4 * hidden])
        mask = col_alive[start : start + step][:, None, :] * row_alive[None, :, :]
        left, right = gated_pair(projected, mask.reshape(step * rows, -1), hidden)
        left_ref[0, start : start + step] = left.reshape(step, rows, hidden)
        right = right.reshape(step, rows, hidden)
        for p, right_ref in enumerate(right_refs):
            right_ref[0, start : start + step] = right[:, p * part : (p + 1) * part]


def first_operands(ids, blocks, pair, chains, w_in, hidden, row_parts):
    slots, rows, cols, channels = pair.shape
    part = rows // row_parts
    operand = jax.ShapeDtypeStruct((slots, cols, rows, hidden), jnp.bfloat16)
    right = jax.ShapeDtypeStruct((slots, cols, part, hidden), jnp.bfloat16)
    return pl.pallas_call(
        functools.partial(first_kernel, hidden, row_parts, lax.axis_size("chan"), lax.axis_size("sub")),
        grid_spec=pltpu.PrefetchScalarGridSpec(
            num_scalar_prefetch=2,
            grid=(slots,),
            in_specs=[
                pl.BlockSpec((1, rows, cols, channels), lambda s, *_: (s, 0, 0, 0)),
                pl.BlockSpec(chains.shape, lambda s, *_: (0, 0)),
                pl.BlockSpec((1,) + w_in.shape[1:], lambda s, *_: (0, 0, 0)),
            ],
            out_specs=[
                pl.BlockSpec((1, rows, cols, channels), lambda s, *_: (s, 0, 0, 0)),
                pl.BlockSpec((1, cols, rows, hidden), lambda s, *_: (s, 0, 0, 0)),
            ]
            + [pl.BlockSpec((1, cols, part, hidden), lambda s, *_: (s, 0, 0, 0))] * row_parts,
            scratch_shapes=[
                pltpu.VMEM((rows * cols, channels), jnp.float32),
                pltpu.VMEM((cols, rows, channels), jnp.bfloat16),
            ],
        ),
        out_shape=[jax.ShapeDtypeStruct(pair.shape, jnp.float32), operand] + [right] * row_parts,
        compiler_params=pltpu.CompilerParams(vmem_limit_bytes=vmem_limit),
        name="first_operands",
    )(ids, blocks, pair, chains, w_in)


def product_kernel(shift, n_blk, slots_dev, terms, capacity, pieces, n_refs, ids, owners, slots, *rest):
    refs = rest[:n_refs]
    out_ref, left_held, right_held, right_wide, chosen, sems = rest[n_refs:]
    step = pl.program_id(0)
    turn = lax.rem(step, 2)
    _, depth, n_i, hidden = left_held.shape
    n_j = right_wide.shape[1]

    @pl.when(step == 0)
    def _():
        target = lax.rem(ids[0] + shift, n_blk)
        for e in range(2 * capacity):
            chosen[e] = 0

        def scan(e, count):
            block, term = target * slots_dev + e // terms, lax.rem(e, terms)
            here = jnp.logical_and(owners[term, block] == ids[0], count < capacity)

            @pl.when(here)
            def _():
                chosen[2 * count] = slots[term, 0, block]
                chosen[2 * count + 1] = slots[term, 1, block]

            return count + here.astype(jnp.int32)

        lax.fori_loop(0, slots_dev * terms, scan, jnp.int32(0))

    def copy(n, term, buffer, source):
        side, _, _, k0, depth_of, i0, size = pieces[n]
        held = (left_held, right_held)[side]
        return pltpu.make_async_copy(
            refs[source].at[chosen[2 * term + side]],
            held.at[buffer, pl.ds(k0, depth_of), pl.ds(i0, size), :],
            sems.at[buffer, n],
        )

    def start(term, buffer):
        for n, (_, on, off, *_) in enumerate(pieces):
            if on == off:
                copy(n, term, buffer, on).start()
            else:

                @pl.when(ids[3] == 1)
                def _(n=n, on=on):
                    copy(n, term, buffer, on).start()

                @pl.when(ids[3] == 0)
                def _(n=n, off=off):
                    copy(n, term, buffer, off).start()

    @pl.when(step == 0)
    def _():
        start(0, 0)

    @pl.when(step + 1 < capacity)
    def _():
        start(step + 1, 1 - turn)

    for n, piece in enumerate(pieces):
        copy(n, step, turn, piece[1]).wait()

    span = 8

    def widen(n, carry):
        at = pl.ds(n * span, span)
        right_wide[at] = right_held[turn, at].astype(jnp.float32)
        return carry

    lax.fori_loop(0, depth // span, widen, 0)

    group = min(8, n_j)
    unroll = 4
    for j0 in range(0, n_j, group):

        def body(n, sums):
            for u in range(unroll):
                k = n * unroll + u
                left = left_held[turn, k].astype(jnp.float32).reshape(n_i // 8, 8, hidden)
                sums = tuple(
                    total + left * right_wide[k, pl.ds(j0 + j, 8, stride=0), :][None]
                    for j, total in enumerate(sums)
                )
            return sums

        zero = jnp.zeros((n_i // 8, 8, hidden), jnp.float32)
        sums = lax.fori_loop(0, depth // unroll, body, (zero,) * group)
        for j, total in enumerate(sums):
            out_ref[0, j0 + j] = total.reshape(n_i, hidden).astype(jnp.bfloat16)


def term_products(shift, ids, owners, slots, lefts, rights, capacity, slots_dev, terms):
    n_blk = lax.axis_size("blk")
    refs, pieces = [], []

    def index_of(array):
        for n, known in enumerate(refs):
            if known is array:
                return n
        refs.append(array)
        return len(refs) - 1

    for side, operands in ((0, lefts), (1, rights)):
        for on, off, k0, i0 in operands:
            pieces.append((side, index_of(on), index_of(off), k0, on.shape[1], i0, on.shape[2]))
    hidden = lefts[0][0].shape[3]
    n_i = max(p[5] + p[6] for p in pieces if p[0] == 0)
    n_j = max(p[5] + p[6] for p in pieces if p[0] == 1)
    depth = max(p[3] + p[4] for p in pieces)
    return pl.pallas_call(
        functools.partial(
            product_kernel, shift, n_blk, slots_dev, terms, capacity, tuple(pieces), len(refs)
        ),
        grid_spec=pltpu.PrefetchScalarGridSpec(
            num_scalar_prefetch=3,
            grid=(capacity,),
            in_specs=[pl.BlockSpec(memory_space=pl.ANY)] * len(refs),
            out_specs=pl.BlockSpec((1, n_j, n_i, hidden), lambda t, *_: (t, 0, 0, 0)),
            scratch_shapes=[
                pltpu.VMEM((2, depth, n_i, hidden), jnp.bfloat16),
                pltpu.VMEM((2, depth, n_j, hidden), jnp.bfloat16),
                pltpu.VMEM((depth, n_j, hidden), jnp.float32),
                pltpu.SMEM((2 * capacity,), jnp.int32),
                pltpu.SemaphoreType.DMA((2, len(pieces))),
            ],
        ),
        out_shape=jax.ShapeDtypeStruct((capacity, n_j, n_i, hidden), jnp.bfloat16),
        compiler_params=pltpu.CompilerParams(vmem_limit_bytes=vmem_limit),
        cost_estimate=pl.CostEstimate(
            flops=2 * capacity * n_i * n_j * depth * hidden * 100,
            bytes_accessed=capacity * (depth * (n_i + n_j) + n_i * n_j) * hidden * 2,
            transcendentals=0,
        ),
        name="term_products",
    )(ids, owners, slots, *refs)


def home_kernel(last, hidden, n_blk, n_chan, n_sub, at, of, slots_dev, terms, capacity, ids, blocks, owners, *rest):
    parts, rest = rest[:n_blk], rest[n_blk:]
    scratch, rest = rest[-5:], rest[:-5]
    held, turned, place, seen, sems = scratch
    cur_ref, gate_ref, w_out_ref = rest[:3]
    if last:
        out_ref = rest[-1]
    else:
        chain_ref, w_ref, out_ref, next_gate_ref, left_ref, right_ref = rest[3:]
    step = pl.program_id(0)
    _, rows, cols, channels = cur_ref.shape

    def arrival(shift):
        return pltpu.make_async_copy(parts[shift], held.at[pl.ds(shift * capacity, capacity)], sems.at[shift])

    @pl.when(step == 0)
    def _():
        for shift in range(n_blk):
            arrival(shift).start()
            seen[shift] = 0

        def scan(e, carry):
            owner = owners[lax.rem(e, terms), ids[0] * slots_dev + e // terms]
            shift = lax.rem(ids[0] - owner + n_blk, n_blk)
            count = seen[owner]
            seen[owner] = count + 1
            place[e] = shift * capacity + count
            return carry

        lax.fori_loop(0, slots_dev * terms, scan, jnp.int32(0))
        for shift in range(n_blk):
            arrival(shift).wait()

    if not last:
        block = ids[0] * slots_dev + step
        row_alive = alive_rows(chain_ref, (blocks[0, block] * n_chan + ids[1]) * rows, rows)
        col_alive = alive_rows(chain_ref, ((blocks[1, block] * n_sub + ids[2]) * of + at) * cols, cols)
    span = max(1, 128 // rows)
    for start in range(0, cols, span):
        taken = pl.ds(start, span)
        total = held[place[step * terms], taken].astype(jnp.float32)
        for t in range(1, terms):
            total = total + held[place[step * terms + t], taken].astype(jnp.float32)
        rounded = total.astype(jnp.bfloat16).astype(jnp.float32)
        turned[pl.ds(start * rows, span * rows), :] = rounded.reshape(span * rows, hidden)
    group = min(rows, max(1, 256 // cols))
    for start in range(0, rows, group):
        taken = pl.ds(start, group)
        mixture = jnp.concatenate(
            [turned[pl.ds(row, cols, stride=rows), :].astype(jnp.bfloat16) for row in range(start, start + group)]
        )
        update = dot(layer_norm(mixture).astype(jnp.bfloat16), w_out_ref[0])
        current = cur_ref[0, taken].astype(jnp.float32).reshape(group * cols, channels)
        gate = gate_ref[0, taken].reshape(group * cols, channels)
        result = (current + gate * update).astype(jnp.bfloat16)
        out_ref[0, taken] = result.reshape(group, cols, channels)
        if not last:
            normed = layer_norm(result).astype(jnp.bfloat16)
            projected = dot(normed, w_ref[0])
            next_gate_ref[0, taken] = sigmoid(projected[:, 4 * hidden :]).reshape(group, cols, channels)
            mask = row_alive[start : start + group][:, None, :] * col_alive[None, :, :]
            left, right = gated_pair(projected, mask.reshape(group * cols, channels), hidden)
            left_ref[0, taken] = left.reshape(group, cols, hidden)
            right_ref[0, taken] = right.reshape(group, cols, hidden)


def home(layer, parts, ids, blocks, owners, current, gate, w_out, capacity, terms, at, of, chains, w_in, last, into=None):
    n_blk = len(parts)
    slots, rows, _, channels = current.shape
    hidden = w_out.shape[1]
    cols = parts[0].shape[1]
    chunk = (1, rows, cols, channels)

    def chunk_spec(array):
        whole = array.shape[2] != cols
        return pl.BlockSpec(chunk, lambda s, *_: (s, 0, at if whole else 0, 0))

    def layer_spec(array, index):
        return pl.BlockSpec((1,) + array.shape[1:], lambda s, *_: (index, 0, 0))

    in_specs = [pl.BlockSpec(memory_space=pl.ANY)] * n_blk + [
        chunk_spec(current),
        chunk_spec(gate),
        layer_spec(w_out, layer),
    ]
    operands = [*parts, current, gate, w_out]
    aliases = {}
    if last:
        if into is not None:
            aliases = {3 + len(operands): 0}
            operands.append(into)
            in_specs.append(pl.BlockSpec(memory_space=pl.ANY))
        out_shape = [jax.ShapeDtypeStruct((slots, rows, cols * of, channels), jnp.bfloat16)]
        out_specs = [pl.BlockSpec(chunk, lambda s, *_: (s, 0, at, 0))]
    else:
        operands += [chains, w_in]
        in_specs += [pl.BlockSpec(chains.shape, lambda s, *_: (0, 0)), layer_spec(w_in, layer + 1)]
        small = (slots, rows, cols, channels)
        out_shape = [jax.ShapeDtypeStruct(small, t) for t in (jnp.bfloat16, jnp.float32, jnp.bfloat16, jnp.bfloat16)]
        out_specs = [pl.BlockSpec(chunk, lambda s, *_: (s, 0, 0, 0))] * 4
    return pl.pallas_call(
        functools.partial(
            home_kernel, last, hidden, n_blk, lax.axis_size("chan"), lax.axis_size("sub"), at, of, slots, terms, capacity
        ),
        grid_spec=pltpu.PrefetchScalarGridSpec(
            num_scalar_prefetch=3,
            grid=(slots,),
            in_specs=in_specs,
            out_specs=out_specs,
            scratch_shapes=[
                pltpu.VMEM((n_blk * capacity, cols, rows, hidden), jnp.bfloat16),
                pltpu.VMEM((rows * cols, hidden), jnp.float32),
                pltpu.SMEM((slots * terms,), jnp.int32),
                pltpu.SMEM((n_blk,), jnp.int32),
                pltpu.SemaphoreType.DMA((n_blk,)),
            ],
        ),
        out_shape=out_shape,
        input_output_aliases=aliases,
        compiler_params=pltpu.CompilerParams(vmem_limit_bytes=vmem_limit),
        cost_estimate=pl.CostEstimate(
            flops=2 * slots * rows * cols * channels * 6 * channels * 10,
            bytes_accessed=slots * rows * cols * channels * 16,
            transcendentals=0,
        ),
        name="home",
    )(ids, blocks, owners, *operands)


def exchange_outgoing(left, rights, n_chan, n_sub):
    if n_chan == 2 and n_sub == 2:
        both = ("chan", "sub")
        other_left = lax.ppermute(left, "sub", [(0, 1), (1, 0)])
        lefts = [(other_left, left, 0, 0), (left, other_left, left.shape[1], 0)]
        chunks = []
        for right in rights:
            if chunks:
                (one, *_), (_, two, *_) = chunks[-1]
                right, *_ = lax.optimization_barrier((right, one, two))
            one = lax.ppermute(right, both, [(0, 2), (3, 1), (1, 0), (2, 3)])
            two = lax.ppermute(right, both, [(1, 2), (2, 1)])
            chunks.append([(one, one, 0, 0), (right, two, right.shape[1], 0)])
        return lefts, chunks
    left = lax.all_gather(left, "sub", axis=1, tiled=True)
    right = jnp.concatenate(rights, axis=2)
    right = lax.all_gather(right, "chan", axis=2, tiled=True)
    right = lax.all_to_all(right, "sub", split_axis=2, concat_axis=1, tiled=True)
    cols = right.shape[2] // 2
    chunks = [right[:, :, :cols], right[:, :, cols:]]
    return [(left, left, 0, 0)], [[(r, r, 0, 0)] for r in chunks]


def exchange_incoming(lefts, rights, n_chan, n_sub):
    if n_chan == 2 and n_sub == 2:
        both = ("chan", "sub")
        left_pieces, chunks = [], []
        at = 0
        for left, right in zip(lefts, rights):
            depth = left.shape[1]
            one = lax.ppermute(left, both, [(1, 3), (2, 0), (0, 1), (3, 2)])
            two = lax.ppermute(one, both, [(0, 1), (3, 2)])
            left_pieces += [(left, one, 0, at), (one, two, depth, at)]
            other = lax.ppermute(right, "chan", [(0, 1), (1, 0)])
            chunks.append([(right, right, 0, 0), (other, other, depth, 0)])
            at += left.shape[2]
        return left_pieces, chunks
    left = lax.all_gather(jnp.concatenate(lefts, axis=2), "chan", axis=1, tiled=True)
    left = lax.all_gather(left, "sub", axis=2, tiled=True)
    size = left.shape[2] // n_chan
    left = lax.dynamic_slice_in_dim(left, lax.axis_index("chan") * size, size, 2)
    gathered = [lax.all_gather(right, "chan", axis=1, tiled=True) for right in rights]
    return [(left, left, 0, 0)], [[(r, r, 0, 0)] for r in gathered]


def lane_group(shape, size):
    return lax.broadcasted_iota(jnp.int32, shape, 1) // size


def spread_kernel(size, w_ref, wide_ref):
    hidden = w_ref.shape[1]
    parts = hidden // size
    for side in range(2):
        for kind in range(2):
            start = (2 * side + kind) * hidden
            weights = 0.5 * w_ref[0, :, start : start + hidden].astype(jnp.float32)
            group = lane_group(weights.shape, size)
            for part in range(parts):
                kept = jnp.where(group == part, weights, 0.0)
                at = ((side * parts + part) * 2 + kind) * hidden
                for a in range(parts):
                    moved = pltpu.roll(kept, ((a - part) % parts) * size, 1) if a != part else kept
                    wide_ref[a * hidden : (a + 1) * hidden, at : at + hidden] = moved.astype(jnp.bfloat16)


def spread_weights(w_in, layer, size):
    hidden = w_in.shape[1]
    parts = hidden // size
    shape = (parts * hidden, 4 * parts * hidden)
    return pl.pallas_call(
        functools.partial(spread_kernel, size),
        grid=(1,),
        in_specs=[pl.BlockSpec((1,) + w_in.shape[1:], lambda s: (layer, 0, 0))],
        out_specs=pl.BlockSpec(shape, lambda s: (0, 0)),
        out_shape=jax.ShapeDtypeStruct(shape, jnp.bfloat16),
        compiler_params=pltpu.CompilerParams(vmem_limit_bytes=16 * mebi),
        cost_estimate=pl.CostEstimate(flops=1 << 30, bytes_accessed=1 << 20, transcendentals=0),
        name="spread_weights",
    )(w_in)


def swap_matrix(half):
    shape = (half * half, half * half)
    to, of = lax.broadcasted_iota(jnp.int32, shape, 0), lax.broadcasted_iota(jnp.int32, shape, 1)
    same = jnp.logical_and(to // half == lax.rem(of, half), lax.rem(to, half) == of // half)
    return same.astype(jnp.float32).astype(jnp.bfloat16)


def swapped(values, swap_ref):
    half, _, lanes = values.shape
    moved = dot(swap_ref[...], values.reshape(half * half, lanes))
    return moved.astype(jnp.bfloat16).reshape(half, half, lanes)


def turn(taken, turned, swap_ref):
    half = 16
    for x in range(0, taken.shape[0], half):
        for y in range(0, taken.shape[1], half):
            turned[y : y + half, x : x + half] = swapped(taken[x : x + half, y : y + half], swap_ref)


def make_operand(side, taken, wide_ref, out_refs, laid, swap_ref):
    rows, size, hidden = taken.shape
    parts, bands, half = hidden // size, size, 16
    groups = rows // parts
    stacked = jnp.concatenate(
        [jnp.concatenate([taken[g * parts + a] for a in range(parts)], axis=1) for g in range(groups)], axis=0
    )
    for part in range(parts):
        at = (side * parts + part) * 2 * hidden
        made = dot(stacked, wide_ref[:, at : at + 2 * hidden])
        value = made[:, :hidden] * (1.0 + jnp.tanh(made[:, hidden:]))
        laid[side, :, part * size : (part + 1) * size, :] = value.astype(jnp.bfloat16).reshape(groups, size, hidden)
    blocks = [laid[side, g].T for g in range(groups)]
    starts = [sum(ref.shape[1] for ref in out_refs[:n]) for n in range(len(out_refs))]
    for first in range(0, bands, half):
        for row in range(0, rows, half):
            tiles = []
            for r in range(row, row + half):
                at = r % parts * bands + first
                tiles.append(blocks[r // parts][at : at + half])
            moved = swapped(jnp.stack(tiles), swap_ref)
            for start, ref in zip(starts, out_refs):
                low, high = max(start, first), min(start + ref.shape[1], first + half)
                if low < high:
                    ref[0, low - start : high - start, row : row + half] = moved[low - first : high - first]


def open_layer(layer, natural, left_refs, right_refs, wide, laid, turned, swap):
    turn(natural, turned, swap)
    for side, refs in ((0, left_refs), (1, right_refs)):
        make_operand(side, natural if side == layer % 2 else turned[...], wide, refs, laid, swap)


def norm_and_gate(values, row_alive, col_alive, w_ref, at, norm_ref, gate_ref):
    _, cols, channels = norm_ref.shape
    rows = values.shape[0] // cols
    normed = layer_norm(values)
    gate = sigmoid(dot(normed.astype(jnp.bfloat16), w_ref[0, :, -channels:]))
    gate_ref[0, pl.ds(at, rows)] = gate.reshape(rows, cols, channels)
    mask = row_alive[at : at + rows, None, :] * col_alive[None, :, :]
    norm_ref[pl.ds(at, rows)] = (normed.reshape(rows, cols, channels) * mask).astype(jnp.bfloat16)


def open_kernel(hidden, chunks, n_chan, n_sub, base, of, ids, blocks, pair_ref, chain_ref, w_ref, wide, *rest):
    gate_ref, *operand_refs, norm_ref, laid, turned, swap = rest[-(2 * chunks + 5) :]
    step = pl.program_id(0)
    _, rows, cols, channels = pair_ref.shape
    block = ids[0] * of + base + step

    @pl.when(step == 0)
    def _():
        swap[...] = swap_matrix(16)

    row_alive = alive_rows(chain_ref, (blocks[0, block] * n_chan + ids[1]) * rows, rows)
    col_alive = alive_rows(chain_ref, (blocks[1, block] * n_sub + ids[2]) * cols, cols)
    group = hidden // cols
    for at in range(0, rows, group):
        values = pair_ref[0, pl.ds(at, group)].reshape(group * cols, channels)
        norm_and_gate(values, row_alive, col_alive, w_ref, at, norm_ref, gate_ref)
    open_layer(0, norm_ref[...], operand_refs[:chunks], operand_refs[chunks:], wide, laid, turned, swap)


def operand_scratch(rows, size, hidden):
    parts = hidden // size
    return [
        pltpu.VMEM((2, rows // parts, parts * size, hidden), jnp.bfloat16),
        pltpu.VMEM((size, rows, hidden), jnp.bfloat16),
        pltpu.VMEM((256, 256), jnp.bfloat16),
    ]


def operand_outputs(slots, count, rows, hidden, bands):
    kept = [count if n == 0 else slots for n in range(len(bands))] * 2
    return [jax.ShapeDtypeStruct((k, b, rows, hidden), jnp.bfloat16) for k, b in zip(kept, bands * 2)]


def slot_specs(arrays, slots, base):
    def spec(array):
        offset = base if array.shape[0] == slots else 0
        return pl.BlockSpec((1,) + array.shape[1:], lambda s, *_: (s + offset, 0, 0, 0))

    return [spec(a) for a in arrays]


def fill(out_shape, earlier, slots, n_before):
    if earlier is None:
        return [], [], {}
    shared = [n for n, o in enumerate(out_shape) if o.shape[0] == slots]
    specs = [pl.BlockSpec(memory_space=pl.ANY)] * len(shared)
    return [earlier[n] for n in shared], specs, {n_before + k: n for k, n in enumerate(shared)}


def open_operands(ids, blocks, pair, chains, w_in, wide, hidden, bands, base, count, earlier):
    slots, rows, cols, channels = pair.shape
    out_shape = [jax.ShapeDtypeStruct(pair.shape, jnp.float32)] + operand_outputs(slots, count, rows, hidden, bands)
    more, more_specs, aliases = fill(out_shape, earlier, slots, 6)
    return pl.pallas_call(
        functools.partial(open_kernel, hidden, len(bands), lax.axis_size("chan"), lax.axis_size("sub"), base, slots),
        grid_spec=pltpu.PrefetchScalarGridSpec(
            num_scalar_prefetch=2,
            grid=(count,),
            in_specs=slot_specs([pair], slots, base)
            + [
                pl.BlockSpec(chains.shape, lambda s, *_: (0, 0)),
                pl.BlockSpec((1,) + w_in.shape[1:], lambda s, *_: (0, 0, 0)),
                pl.BlockSpec(wide.shape, lambda s, *_: (0, 0)),
            ]
            + more_specs,
            out_specs=slot_specs(out_shape, slots, base),
            scratch_shapes=[pltpu.VMEM((rows, cols, channels), jnp.bfloat16)] + operand_scratch(rows, cols, hidden),
        ),
        out_shape=out_shape,
        input_output_aliases=aliases,
        compiler_params=pltpu.CompilerParams(vmem_limit_bytes=28 * mebi),
        cost_estimate=pl.CostEstimate(flops=1 << 33, bytes_accessed=1 << 20, transcendentals=0),
        name="open_operands",
    )(ids, blocks, pair, chains, w_in, wide, *more)


def plan_kernel(n_blk, slots_dev, terms, capacity, ids, owners, slots, chosen, place, seen):
    for shift in range(n_blk):
        seen[shift] = 0
        target = lax.rem(ids[0] + shift, n_blk)
        for e in range(2 * (capacity + 1)):
            chosen[2 * shift * (capacity + 1) + e] = 0
        found = jnp.int32(0)
        for e in range(slots_dev * terms):
            block, term = target * slots_dev + e // terms, e % terms
            at = 2 * (shift * (capacity + 1) + jnp.minimum(found, capacity))
            chosen[at] = slots[term, 0, block]
            chosen[at + 1] = slots[term, 1, block]
            found = found + (owners[term, block] == ids[0]).astype(jnp.int32)
    for e in range(slots_dev * terms):
        owner = owners[e % terms, ids[0] * slots_dev + e // terms]
        count = seen[owner]
        seen[owner] = count + 1
        place[e] = lax.rem(ids[0] - owner + n_blk, n_blk) * capacity + count


def make_plan(ids, owners, slots, n_blk, slots_dev, terms, capacity):
    scalars = pl.BlockSpec(memory_space=pltpu.SMEM)
    return pl.pallas_call(
        functools.partial(plan_kernel, n_blk, slots_dev, terms, capacity),
        in_specs=[scalars] * 3,
        out_specs=[scalars] * 2,
        out_shape=[
            jax.ShapeDtypeStruct((2 * n_blk * (capacity + 1),), jnp.int32),
            jax.ShapeDtypeStruct((slots_dev * terms,), jnp.int32),
        ],
        scratch_shapes=[pltpu.SMEM((n_blk,), jnp.int32)],
        compiler_params=pltpu.CompilerParams(vmem_limit_bytes=mebi),
        name="make_plan",
    )(ids, owners, slots)


def banded_kernel(shifts, capacity, pieces, n_refs, size, ids, chosen, *rest):
    refs, rest = rest[:n_refs], rest[n_refs:]
    out_refs, (left_held, right_held, out_held, sems, out_sems) = rest[: len(shifts)], rest[len(shifts) :]
    halves, _, bands, rows, hidden = left_held.shape
    parts = hidden // size
    at_once = 2 if capacity % 2 == 0 else 1

    def copy(n, source):
        side, half, base, *_ = pieces[n]
        target = (left_held, right_held)[side].at[half, pl.ds(base, refs[source].shape[0])]
        return pltpu.make_async_copy(refs[source], target, sems.at[n])

    for n, (*_, on, off) in enumerate(pieces):
        if on == off:
            copy(n, on).start()
        else:

            @pl.when(ids[3] == 1)
            def _(n=n, on=on):
                copy(n, on).start()

            @pl.when(ids[3] == 0)
            def _(n=n, off=off):
                copy(n, off).start()

    for n, piece in enumerate(pieces):
        copy(n, piece[-1]).wait()

    def leave(n):
        return pltpu.make_async_copy(out_held.at[pl.ds(n * capacity, capacity)], out_refs[n], out_sems.at[n])

    for n, shift in enumerate(shifts):

        def one(turn, carry, n=n, shift=shift):
            group = lane_group((size, hidden), size)
            for term in [turn * at_once + t for t in range(at_once)]:
                at = 2 * (shift * (capacity + 1) + term)
                left_slot, right_slot = chosen[at], chosen[at + 1]
                for band in range(bands):
                    left = jnp.concatenate([left_held[h, left_slot, band] for h in range(halves)], axis=1)
                    apart = []
                    for h in range(halves):
                        right = right_held[h, right_slot, band]
                        apart += [jnp.where(group == part, right, jnp.zeros_like(right)) for part in range(parts)]
                    made = dot(left, jnp.concatenate(apart, axis=0))
                    out_held[n * capacity + term, band] = made.astype(jnp.bfloat16)
            return carry

        lax.fori_loop(0, capacity // at_once, one, 0)
        leave(n).start()
    for n in range(len(shifts)):
        leave(n).wait()


def banded_products(shifts, ids, chosen, operands, capacity, size):
    refs, pieces = [], []

    def index_of(array):
        for n, known in enumerate(refs):
            if known is array:
                return n
        refs.append(array)
        return len(refs) - 1

    slots = 0
    for both in operands:
        for side in range(2):
            for half, (on, off) in enumerate(both[side]):
                pieces.append((side, half, slots, index_of(on), index_of(off)))
        slots += both[0][0][0].shape[0]
    halves = len(operands[0][0])
    _, bands, rows, hidden = operands[0][0][0][0].shape
    count = len(shifts) * capacity
    anywhere = pl.BlockSpec(memory_space=pl.ANY)
    return pl.pallas_call(
        functools.partial(banded_kernel, shifts, capacity, tuple(pieces), len(refs), size),
        grid_spec=pltpu.PrefetchScalarGridSpec(
            num_scalar_prefetch=2,
            grid=(),
            in_specs=[anywhere] * len(refs),
            out_specs=[anywhere] * len(shifts),
            scratch_shapes=[
                pltpu.VMEM((halves, slots, bands, rows, hidden), jnp.bfloat16),
                pltpu.VMEM((halves, slots, bands, size, hidden), jnp.bfloat16),
                pltpu.VMEM((count, bands, rows, hidden), jnp.bfloat16),
                pltpu.SemaphoreType.DMA((len(pieces),)),
                pltpu.SemaphoreType.DMA((len(shifts),)),
            ],
        ),
        out_shape=[jax.ShapeDtypeStruct((capacity, bands, rows, hidden), jnp.bfloat16)] * len(shifts),
        compiler_params=pltpu.CompilerParams(vmem_limit_bytes=14 * mebi),
        cost_estimate=pl.CostEstimate(
            flops=2 * count * bands * rows * hidden * hidden * halves, bytes_accessed=1, transcendentals=0
        ),
        name="banded_products",
    )(ids, chosen, *refs)


def close_kernel(layer, last, n_parts, n_blk, n_chan, n_sub, base, of, terms, capacity, ids, blocks, place, *rest):
    chunks = n_parts // n_blk
    arrived, rest = rest[:n_parts], rest[n_parts:]
    cur_ref, gate_ref, w_out_ref = rest[:3]
    if last:
        out_ref, held, wide_out, sems, swap = rest[3:]
    else:
        chain_ref, w_ref, wide = rest[3:6]
        out_ref, next_gate_ref, *operand_refs, held, wide_out, sems, norm_ref, laid, turned, swap = rest[
            -(2 * chunks + 9) :
        ]
        left_refs, right_refs = operand_refs[:chunks], operand_refs[chunks:]
    step = pl.program_id(0)
    _, rows, cols, channels = cur_ref.shape
    _, bands, _, hidden = held.shape
    parts, size = hidden // bands, bands

    def arrival(n):
        at = sum(arrived[m * n_blk].shape[1] for m in range(n // n_blk))
        count = arrived[n].shape[1]
        target = held.at[pl.ds(n % n_blk * capacity, capacity), pl.ds(at, count)]
        return pltpu.make_async_copy(arrived[n], target, sems.at[n])

    @pl.when(step == 0)
    def _():
        for n in range(n_parts):
            arrival(n).start()
        wide_out[...] = jnp.zeros_like(wide_out)
        for part in range(parts):
            for a in range(parts):
                at = (part * parts + a) * bands
                wide_out[at : at + bands, a * channels : (a + 1) * channels] = w_out_ref[
                    0, part * bands : (part + 1) * bands, :
                ]
        swap[...] = swap_matrix(16)
        for n in range(n_parts):
            arrival(n).wait()

    if not last:
        block = ids[0] * of + base + step
        row_alive = alive_rows(chain_ref, (blocks[0, block] * n_chan + ids[1]) * rows, rows)
        col_alive = alive_rows(chain_ref, (blocks[1, block] * n_sub + ids[2]) * cols, cols)
    half = 16
    by_row = [[] for _ in range(rows)]
    for row in range(0, rows, half):
        for band in range(0, bands, half):
            taken = pl.ds(band, half), pl.ds(row, half)
            total = held[(place[(base + step) * terms], *taken)].astype(jnp.float32)
            for t in range(1, terms):
                total = total + held[(place[(base + step) * terms + t], *taken)].astype(jnp.float32)
            moved = swapped(total.astype(jnp.bfloat16), swap)
            for r in range(half):
                by_row[row + r].append(moved[r])
    groups = rows // parts
    pieces = []
    for g in range(groups):
        block = jnp.concatenate([x for a in range(parts) for x in by_row[g * parts + a]]).T
        pieces.append(jnp.concatenate([block[p * cols : (p + 1) * cols] for p in range(parts)], axis=1))
    mixture = jnp.concatenate(pieces)
    together = (lane_group((hidden, hidden), size) == lax.broadcasted_iota(jnp.int32, (hidden, hidden), 0) // size)
    together = together.astype(jnp.float32).astype(jnp.bfloat16)
    average = dot(mixture, jnp.concatenate([together] * parts)) * (1.0 / hidden)
    centred = [mixture[:, p * hidden : (p + 1) * hidden].astype(jnp.float32) - average for p in range(parts)]
    squares = sum(c * c for c in centred)
    high = squares.astype(jnp.bfloat16)
    low = (squares - high.astype(jnp.float32)).astype(jnp.bfloat16)
    variance = dot(jnp.concatenate([high, low], axis=1), jnp.concatenate([together] * 2)) * (1.0 / hidden)
    scale = lax.rsqrt(variance + norm_epsilon)
    normed = jnp.concatenate([(c * scale).astype(jnp.bfloat16) for c in centred], axis=1)
    update = dot(normed, wide_out[...])
    for g in range(groups):
        taken = pl.ds(g * parts, parts)
        change = jnp.concatenate(
            [update[g * cols : (g + 1) * cols, a * channels : (a + 1) * channels] for a in range(parts)]
        )
        gate = gate_ref[0, taken].reshape(parts * cols, channels)
        current = cur_ref[0, taken].astype(jnp.float32).reshape(parts * cols, channels)
        result = (current + gate * change).astype(jnp.bfloat16)
        out_ref[0, taken] = result.reshape(parts, cols, channels)
        if not last:
            norm_and_gate(result, row_alive, col_alive, w_ref, g * parts, norm_ref, next_gate_ref)
    if not last:
        open_layer(layer + 1, norm_ref[...], left_refs, right_refs, wide, laid, turned, swap)


def close_layer(
    layer, arrived, ids, blocks, place, current, gate, w_out, capacity, terms, chains, w_in, wide, last, bands, base, count, earlier
):
    n_blk = len(arrived[0])
    flat = [part for chunk in arrived for part in chunk]
    slots, rows, cols, channels = current.shape
    hidden = w_out.shape[1]

    def layer_spec(array, index):
        return pl.BlockSpec((1,) + array.shape[1:], lambda s, *_: (index, 0, 0))

    in_specs = [pl.BlockSpec(memory_space=pl.ANY)] * len(flat)
    in_specs += slot_specs([current, gate], slots, base) + [layer_spec(w_out, layer)]
    operands = [*flat, current, gate, w_out]
    out_shape = [jax.ShapeDtypeStruct(current.shape, jnp.bfloat16)]
    scratch = [
        pltpu.VMEM((n_blk * capacity, sum(bands[layer]), rows, hidden), jnp.bfloat16),
        pltpu.VMEM((hidden // cols * hidden, hidden // cols * channels), jnp.bfloat16),
        pltpu.SemaphoreType.DMA((len(flat),)),
    ]
    if not last:
        operands += [chains, w_in, wide]
        in_specs += [pl.BlockSpec(chains.shape, lambda s, *_: (0, 0)), layer_spec(w_in, layer + 1)]
        in_specs += [pl.BlockSpec(wide.shape, lambda s, *_: (0, 0))]
        out_shape += [jax.ShapeDtypeStruct(current.shape, jnp.float32)]
        out_shape += operand_outputs(slots, count, cols, hidden, bands[layer + 1])
        scratch += [pltpu.VMEM((rows, cols, channels), jnp.bfloat16)] + operand_scratch(cols, rows, hidden)
    else:
        scratch += [pltpu.VMEM((256, 256), jnp.bfloat16)]
    more, more_specs, aliases = fill(out_shape, earlier, slots, 3 + len(operands))
    return pl.pallas_call(
        functools.partial(
            close_kernel,
            *(layer, last, len(flat), n_blk, lax.axis_size("chan"), lax.axis_size("sub"), base, slots, terms, capacity),
        ),
        grid_spec=pltpu.PrefetchScalarGridSpec(
            num_scalar_prefetch=3,
            grid=(count,),
            in_specs=in_specs + more_specs,
            out_specs=slot_specs(out_shape, slots, base),
            scratch_shapes=scratch,
        ),
        out_shape=out_shape,
        input_output_aliases=aliases,
        compiler_params=pltpu.CompilerParams(vmem_limit_bytes=32 * mebi),
        cost_estimate=pl.CostEstimate(flops=1 << 33, bytes_accessed=1 << 20, transcendentals=0),
        name="close_layer",
    )(ids, blocks, place, *operands, *more)


def after(value, *others):
    return lax.optimization_barrier((value, *others))[0]


def exchange_bands_outgoing(left, right, over):
    both = ("chan", "sub")
    other = lax.ppermute(left, "sub", [(0, 1), (1, 0)])
    one = lax.ppermute(right, both, [(0, 2), (3, 1), (1, 0), (2, 3)])
    two = lax.ppermute(right, both, [(1, 2), (2, 1)])
    return [(other, left), (left, other)], [(one, one), (right, two)]


def exchange_bands_incoming(left, right, over):
    both = ("chan", "sub")
    one = lax.ppermute(left, both, [(1, 3), (2, 0), (0, 1), (3, 2)])
    other = lax.ppermute(right, "chan", [(0, 1), (1, 0)])
    two = lax.ppermute(after(one, over), both, [(0, 1), (3, 2)])
    return [(left, one), (one, two)], [(right, right), (other, other)]


def banded(pair, ids, blocks, owners, slot_of, chains, w_in, w_out, capacity, terms, n_blk):
    slots, rows, cols, channels = pair.shape
    hidden = w_out.shape[1]
    far = n_blk // 2
    shifts = [far] + [s for s in range(1, n_blk) if s != far] + [0]
    layers = w_in.shape[0]
    current = pair
    bands = [[12, 20], [14, 18]]
    chosen, place = make_plan(ids, owners, slot_of, n_blk, slots, terms, capacity)
    half = slots // 2
    halves = [(0, half), (half, slots - half)]
    for layer in range(layers):
        count = len(bands[layer])
        if layer == 0:
            calls, wide = [None], spread_weights(w_in, 0, cols)
            for base, size in halves:
                calls.append(open_operands(ids, blocks, pair, chains, w_in, wide, hidden, bands[0], base, size, calls[-1]))
            gate = calls[-1][0]
        operands = [call[-2 * count :] for call in calls[1:]]
        exchange = exchange_bands_incoming if layer % 2 else exchange_bands_outgoing
        arrived = []
        for chunk in range(count):
            if chunk == 0:
                exchanged = []
                over = operands[-1][count]
                for left, right in [(o[0], o[count]) for o in operands]:
                    if exchanged and layer % 2:
                        (_, (one, _)), (_, (other, _)) = exchanged[-1]
                        left, right = lax.optimization_barrier((left, right, one, other))[:2]
                    elif exchanged:
                        ((other, _), _), ((one, _), (_, two)) = exchanged[-1]
                        left, right = lax.optimization_barrier((left, right, other, one, two))[:2]
                    exchanged.append(exchange(left, right, over))
            else:
                left, right = operands[-1][chunk], operands[-1][count + chunk]
                if layer % 2:
                    (_, (_, two)), (_, (other, _)) = exchanged[-1]
                    left, right = lax.optimization_barrier((left, right, two, other))[:2]
                else:
                    ((other, _), _), ((one, _), (_, two)) = exchanged[-1]
                    left = after(left, other)
                    right = after(right, one, two, made[-1])
                exchanged = [exchange(left, right, arrived[-1][far])]
            made = banded_products(shifts, ids, chosen, exchanged, capacity, cols)
            parts = [None] * n_blk
            for shift, part in zip(shifts, made):
                if shift:
                    if arrived:
                        part = after(part, arrived[-1][shift])
                    part = lax.ppermute(part, "blk", [(p, (p + shift) % n_blk) for p in range(n_blk)])
                parts[shift] = part
            arrived.append(parts)
        last = layer == layers - 1
        calls = [None]
        if not last:
            wide = spread_weights(after(w_in, made[-1]), layer + 1, cols)
        for base, size in [(0, slots)] if last else halves:
            calls.append(
                close_layer(
                    *(layer, arrived, ids, blocks, place, current, gate, w_out, capacity, terms, chains, w_in, wide, last),
                    *(bands, base, size, calls[-1]),
                )
            )
        if last:
            return calls[-1][0]
        current, gate = calls[-1][:2]


def per_device(pair, block_list, term_owner, term_slots, chain_ids, w_in, w_out):
    n_blk = lax.axis_size("blk")
    n_chan = lax.axis_size("chan")
    n_sub = lax.axis_size("sub")
    position = lax.axis_index("blk")
    row_group = lax.axis_index("chan")
    col_group = lax.axis_index("sub")
    slots, rows, cols, channels = pair.shape
    hidden = w_out.shape[1]
    terms = term_owner.shape[1]
    capacity = max(2, -(-slots * terms // n_blk))
    fast = n_chan == 2 and n_sub == 2
    on_diagonal = (row_group == col_group).astype(jnp.int32)
    ids = jnp.stack([position, row_group, col_group, on_diagonal]).astype(jnp.int32)
    blocks = block_list.T
    owners = term_owner.T
    slot_of = jnp.transpose(term_slots, (1, 2, 0))
    chains = chain_ids.reshape(-1, 128)
    if fast and rows == cols == 32 and channels == hidden == 128:
        return banded(pair, ids, blocks, owners, slot_of, chains, w_in, w_out, capacity, terms, n_blk)
    shifts = [n_blk // 2] + [s for s in range(1, n_blk) if s != n_blk // 2] + [0]

    def all_products(lefts, right):
        parts = [None] * n_blk
        for shift in shifts:
            made = term_products(shift, ids, owners, slot_of, lefts, right, capacity, slots, terms)
            if shift:
                pairs = [(p, (p + shift) % n_blk) for p in range(n_blk)]
                made = lax.ppermute(made, "blk", pairs)
            parts[shift] = made
        return parts

    def at_home(layer, parts, current, gate, at, of, into=None):
        last = layer == w_in.shape[0] - 1
        return home(
            layer, parts, ids, blocks, owners, current, gate, w_out, capacity, terms, at, of, chains, w_in, last, into
        )

    gate, left, *rights = first_operands(ids, blocks, pair, chains, w_in, hidden, 2 if fast else 1)
    lefts, chunks = exchange_outgoing(left, rights, n_chan, n_sub)
    count = len(chunks)
    made = [all_products(lefts, right) for right in chunks]
    homes = [at_home(0, parts, pair, gate, at, count) for at, parts in enumerate(made)]
    lefts, chunks = exchange_incoming([h[2] for h in homes], [h[3] for h in homes], n_chan, n_sub)
    made = [all_products(lefts, right) for right in chunks]
    out = None
    for at, parts in enumerate(made):
        (out,) = at_home(1, parts, homes[at][0], homes[at][1], at, count, into=out)
    return out


def solution(mesh):
    in_specs = (
        P(("groups", "blk"), "chan", "sub", None),
        P("groups", None),
        P("groups", None),
        P("groups", None, None),
        P("groups"),
        P(),
        P(),
    )
    out_specs = P(("groups", "blk"), "chan", "sub", None)
    return jax.shard_map(
        per_device, mesh=mesh, in_specs=in_specs, out_specs=out_specs, check_vma=False
    )
```

```python
import functools

import jax
import jax.numpy as jnp
from jax import lax
from jax.experimental import pallas as pl
from jax.experimental.pallas import tpu as pltpu
from jax.sharding import PartitionSpec as P

norm_epsilon = 1e-05
mebi = 1024 * 1024
vmem_limit = 56 * mebi


def sigmoid(values):
    return 0.5 + 0.5 * jnp.tanh(0.5 * values)


def layer_norm(values):
    values = values.astype(jnp.float32)
    centred = values - jnp.mean(values, axis=-1, keepdims=True)
    variance = jnp.mean(centred * centred, axis=-1, keepdims=True)
    return centred * lax.rsqrt(variance + norm_epsilon)


def alive_rows(chain_ref, start, size):
    lanes = chain_ref.shape[1]
    line = chain_ref[pl.ds(start // lanes, 1), :] >= 0
    spot = lax.broadcasted_iota(jnp.int32, (size, lanes), 0) + lax.rem(start, lanes)
    pick = jnp.logical_and(lax.broadcasted_iota(jnp.int32, (size, lanes), 1) == spot, line)
    return dot(pick.astype(jnp.float32).astype(jnp.bfloat16), jnp.ones((lanes, lanes), jnp.bfloat16))


def dot(a, b):
    return jnp.dot(a, b, preferred_element_type=jnp.float32)


def gated_pair(projected, mask, hidden):
    left = mask * sigmoid(projected[:, hidden : 2 * hidden]) * projected[:, :hidden]
    right = mask * sigmoid(projected[:, 3 * hidden : 4 * hidden]) * projected[:, 2 * hidden : 3 * hidden]
    return left.astype(jnp.bfloat16), right.astype(jnp.bfloat16)


def first_kernel(hidden, row_parts, n_chan, n_sub, ids, blocks, pair_ref, chain_ref, w_ref, gate_ref, left_ref, *rest):
    right_refs, (norm_ref, turned_ref) = rest[:row_parts], rest[row_parts:]
    slots = pl.num_programs(0)
    _, rows, cols, channels = pair_ref.shape
    block = ids[0] * slots + pl.program_id(0)
    row_alive = alive_rows(chain_ref, (blocks[0, block] * n_chan + ids[1]) * rows, rows)
    col_alive = alive_rows(chain_ref, (blocks[1, block] * n_sub + ids[2]) * cols, cols)
    group = max(1, 256 // cols)
    for start in range(0, rows, group):
        at = pl.ds(start, group)
        normed = layer_norm(pair_ref[0, at].reshape(group * cols, channels))
        norm_ref[pl.ds(start * cols, group * cols), :] = normed
        gate = sigmoid(dot(normed.astype(jnp.bfloat16), w_ref[0, :, 4 * hidden :]))
        gate_ref[0, at] = gate.reshape(group, cols, channels)
    for col in range(cols):
        turned_ref[col] = norm_ref[pl.ds(col, rows, stride=cols), :].astype(jnp.bfloat16)
    step = max(1, 128 // rows)
    part = rows // row_parts
    for start in range(0, cols, step):
        taken = turned_ref[start : start + step].reshape(step * rows, channels)
        projected = dot(taken, w_ref[0, :, : 4 * hidden])
        mask = col_alive[start : start + step][:, None, :] * row_alive[None, :, :]
        left, right = gated_pair(projected, mask.reshape(step * rows, -1), hidden)
        left_ref[0, start : start + step] = left.reshape(step, rows, hidden)
        right = right.reshape(step, rows, hidden)
        for p, right_ref in enumerate(right_refs):
            right_ref[0, start : start + step] = right[:, p * part : (p + 1) * part]


def first_operands(ids, blocks, pair, chains, w_in, hidden, row_parts):
    slots, rows, cols, channels = pair.shape
    part = rows // row_parts
    operand = jax.ShapeDtypeStruct((slots, cols, rows, hidden), jnp.bfloat16)
    right = jax.ShapeDtypeStruct((slots, cols, part, hidden), jnp.bfloat16)
    return pl.pallas_call(
        functools.partial(first_kernel, hidden, row_parts, lax.axis_size("chan"), lax.axis_size("sub")),
        grid_spec=pltpu.PrefetchScalarGridSpec(
            num_scalar_prefetch=2,
            grid=(slots,),
            in_specs=[
                pl.BlockSpec((1, rows, cols, channels), lambda s, *_: (s, 0, 0, 0)),
                pl.BlockSpec(chains.shape, lambda s, *_: (0, 0)),
                pl.BlockSpec((1,) + w_in.shape[1:], lambda s, *_: (0, 0, 0)),
            ],
            out_specs=[
                pl.BlockSpec((1, rows, cols, channels), lambda s, *_: (s, 0, 0, 0)),
                pl.BlockSpec((1, cols, rows, hidden), lambda s, *_: (s, 0, 0, 0)),
            ]
            + [pl.BlockSpec((1, cols, part, hidden), lambda s, *_: (s, 0, 0, 0))] * row_parts,
            scratch_shapes=[
                pltpu.VMEM((rows * cols, channels), jnp.float32),
                pltpu.VMEM((cols, rows, channels), jnp.bfloat16),
            ],
        ),
        out_shape=[jax.ShapeDtypeStruct(pair.shape, jnp.float32), operand] + [right] * row_parts,
        compiler_params=pltpu.CompilerParams(vmem_limit_bytes=vmem_limit),
        name="first_operands",
    )(ids, blocks, pair, chains, w_in)


def product_kernel(shift, n_blk, slots_dev, terms, capacity, pieces, n_refs, ids, owners, slots, *rest):
    refs = rest[:n_refs]
    out_ref, left_held, right_held, right_wide, chosen, sems = rest[n_refs:]
    step = pl.program_id(0)
    turn = lax.rem(step, 2)
    _, depth, n_i, hidden = left_held.shape
    n_j = right_wide.shape[1]

    @pl.when(step == 0)
    def _():
        target = lax.rem(ids[0] + shift, n_blk)
        for e in range(2 * capacity):
            chosen[e] = 0

        def scan(e, count):
            block, term = target * slots_dev + e // terms, lax.rem(e, terms)
            here = jnp.logical_and(owners[term, block] == ids[0], count < capacity)

            @pl.when(here)
            def _():
                chosen[2 * count] = slots[term, 0, block]
                chosen[2 * count + 1] = slots[term, 1, block]

            return count + here.astype(jnp.int32)

        lax.fori_loop(0, slots_dev * terms, scan, jnp.int32(0))

    def copy(n, term, buffer, source):
        side, _, _, k0, depth_of, i0, size = pieces[n]
        held = (left_held, right_held)[side]
        return pltpu.make_async_copy(
            refs[source].at[chosen[2 * term + side]],
            held.at[buffer, pl.ds(k0, depth_of), pl.ds(i0, size), :],
            sems.at[buffer, n],
        )

    def start(term, buffer):
        for n, (_, on, off, *_) in enumerate(pieces):
            if on == off:
                copy(n, term, buffer, on).start()
            else:

                @pl.when(ids[3] == 1)
                def _(n=n, on=on):
                    copy(n, term, buffer, on).start()

                @pl.when(ids[3] == 0)
                def _(n=n, off=off):
                    copy(n, term, buffer, off).start()

    @pl.when(step == 0)
    def _():
        start(0, 0)

    @pl.when(step + 1 < capacity)
    def _():
        start(step + 1, 1 - turn)

    for n, piece in enumerate(pieces):
        copy(n, step, turn, piece[1]).wait()

    span = 8

    def widen(n, carry):
        at = pl.ds(n * span, span)
        right_wide[at] = right_held[turn, at].astype(jnp.float32)
        return carry

    lax.fori_loop(0, depth // span, widen, 0)

    group = min(8, n_j)
    unroll = 4
    for j0 in range(0, n_j, group):

        def body(n, sums):
            for u in range(unroll):
                k = n * unroll + u
                left = left_held[turn, k].astype(jnp.float32).reshape(n_i // 8, 8, hidden)
                sums = tuple(
                    total + left * right_wide[k, pl.ds(j0 + j, 8, stride=0), :][None]
                    for j, total in enumerate(sums)
                )
            return sums

        zero = jnp.zeros((n_i // 8, 8, hidden), jnp.float32)
        sums = lax.fori_loop(0, depth // unroll, body, (zero,) * group)
        for j, total in enumerate(sums):
            out_ref[0, j0 + j] = total.reshape(n_i, hidden).astype(jnp.bfloat16)


def term_products(shift, ids, owners, slots, lefts, rights, capacity, slots_dev, terms):
    n_blk = lax.axis_size("blk")
    refs, pieces = [], []

    def index_of(array):
        for n, known in enumerate(refs):
            if known is array:
                return n
        refs.append(array)
        return len(refs) - 1

    for side, operands in ((0, lefts), (1, rights)):
        for on, off, k0, i0 in operands:
            pieces.append((side, index_of(on), index_of(off), k0, on.shape[1], i0, on.shape[2]))
    hidden = lefts[0][0].shape[3]
    n_i = max(p[5] + p[6] for p in pieces if p[0] == 0)
    n_j = max(p[5] + p[6] for p in pieces if p[0] == 1)
    depth = max(p[3] + p[4] for p in pieces)
    return pl.pallas_call(
        functools.partial(
            product_kernel, shift, n_blk, slots_dev, terms, capacity, tuple(pieces), len(refs)
        ),
        grid_spec=pltpu.PrefetchScalarGridSpec(
            num_scalar_prefetch=3,
            grid=(capacity,),
            in_specs=[pl.BlockSpec(memory_space=pl.ANY)] * len(refs),
            out_specs=pl.BlockSpec((1, n_j, n_i, hidden), lambda t, *_: (t, 0, 0, 0)),
            scratch_shapes=[
                pltpu.VMEM((2, depth, n_i, hidden), jnp.bfloat16),
                pltpu.VMEM((2, depth, n_j, hidden), jnp.bfloat16),
                pltpu.VMEM((depth, n_j, hidden), jnp.float32),
                pltpu.SMEM((2 * capacity,), jnp.int32),
                pltpu.SemaphoreType.DMA((2, len(pieces))),
            ],
        ),
        out_shape=jax.ShapeDtypeStruct((capacity, n_j, n_i, hidden), jnp.bfloat16),
        compiler_params=pltpu.CompilerParams(vmem_limit_bytes=vmem_limit),
        cost_estimate=pl.CostEstimate(
            flops=2 * capacity * n_i * n_j * depth * hidden * 100,
            bytes_accessed=capacity * (depth * (n_i + n_j) + n_i * n_j) * hidden * 2,
            transcendentals=0,
        ),
        name="term_products",
    )(ids, owners, slots, *refs)


def home_kernel(last, hidden, n_blk, n_chan, n_sub, at, of, slots_dev, terms, capacity, ids, blocks, owners, *rest):
    parts, rest = rest[:n_blk], rest[n_blk:]
    scratch, rest = rest[-5:], rest[:-5]
    held, turned, place, seen, sems = scratch
    cur_ref, gate_ref, w_out_ref = rest[:3]
    if last:
        out_ref = rest[-1]
    else:
        chain_ref, w_ref, out_ref, next_gate_ref, left_ref, right_ref = rest[3:]
    step = pl.program_id(0)
    _, rows, cols, channels = cur_ref.shape

    def arrival(shift):
        return pltpu.make_async_copy(parts[shift], held.at[pl.ds(shift * capacity, capacity)], sems.at[shift])

    @pl.when(step == 0)
    def _():
        for shift in range(n_blk):
            arrival(shift).start()
            seen[shift] = 0

        def scan(e, carry):
            owner = owners[lax.rem(e, terms), ids[0] * slots_dev + e // terms]
            shift = lax.rem(ids[0] - owner + n_blk, n_blk)
            count = seen[owner]
            seen[owner] = count + 1
            place[e] = shift * capacity + count
            return carry

        lax.fori_loop(0, slots_dev * terms, scan, jnp.int32(0))
        for shift in range(n_blk):
            arrival(shift).wait()

    if not last:
        block = ids[0] * slots_dev + step
        row_alive = alive_rows(chain_ref, (blocks[0, block] * n_chan + ids[1]) * rows, rows)
        col_alive = alive_rows(chain_ref, ((blocks[1, block] * n_sub + ids[2]) * of + at) * cols, cols)
    span = max(1, 128 // rows)
    for start in range(0, cols, span):
        taken = pl.ds(start, span)
        total = held[place[step * terms], taken].astype(jnp.float32)
        for t in range(1, terms):
            total = total + held[place[step * terms + t], taken].astype(jnp.float32)
        rounded = total.astype(jnp.bfloat16).astype(jnp.float32)
        turned[pl.ds(start * rows, span * rows), :] = rounded.reshape(span * rows, hidden)
    group = min(rows, max(1, 256 // cols))
    for start in range(0, rows, group):
        taken = pl.ds(start, group)
        mixture = jnp.concatenate(
            [turned[pl.ds(row, cols, stride=rows), :].astype(jnp.bfloat16) for row in range(start, start + group)]
        )
        update = dot(layer_norm(mixture).astype(jnp.bfloat16), w_out_ref[0])
        current = cur_ref[0, taken].astype(jnp.float32).reshape(group * cols, channels)
        gate = gate_ref[0, taken].reshape(group * cols, channels)
        result = (current + gate * update).astype(jnp.bfloat16)
        out_ref[0, taken] = result.reshape(group, cols, channels)
        if not last:
            normed = layer_norm(result).astype(jnp.bfloat16)
            projected = dot(normed, w_ref[0])
            next_gate_ref[0, taken] = sigmoid(projected[:, 4 * hidden :]).reshape(group, cols, channels)
            mask = row_alive[start : start + group][:, None, :] * col_alive[None, :, :]
            left, right = gated_pair(projected, mask.reshape(group * cols, channels), hidden)
            left_ref[0, taken] = left.reshape(group, cols, hidden)
            right_ref[0, taken] = right.reshape(group, cols, hidden)


def home(layer, parts, ids, blocks, owners, current, gate, w_out, capacity, terms, at, of, chains, w_in, last, into=None):
    n_blk = len(parts)
    slots, rows, _, channels = current.shape
    hidden = w_out.shape[1]
    cols = parts[0].shape[1]
    chunk = (1, rows, cols, channels)

    def chunk_spec(array):
        whole = array.shape[2] != cols
        return pl.BlockSpec(chunk, lambda s, *_: (s, 0, at if whole else 0, 0))

    def layer_spec(array, index):
        return pl.BlockSpec((1,) + array.shape[1:], lambda s, *_: (index, 0, 0))

    in_specs = [pl.BlockSpec(memory_space=pl.ANY)] * n_blk + [
        chunk_spec(current),
        chunk_spec(gate),
        layer_spec(w_out, layer),
    ]
    operands = [*parts, current, gate, w_out]
    aliases = {}
    if last:
        if into is not None:
            aliases = {3 + len(operands): 0}
            operands.append(into)
            in_specs.append(pl.BlockSpec(memory_space=pl.ANY))
        out_shape = [jax.ShapeDtypeStruct((slots, rows, cols * of, channels), jnp.bfloat16)]
        out_specs = [pl.BlockSpec(chunk, lambda s, *_: (s, 0, at, 0))]
    else:
        operands += [chains, w_in]
        in_specs += [pl.BlockSpec(chains.shape, lambda s, *_: (0, 0)), layer_spec(w_in, layer + 1)]
        small = (slots, rows, cols, channels)
        out_shape = [jax.ShapeDtypeStruct(small, t) for t in (jnp.bfloat16, jnp.float32, jnp.bfloat16, jnp.bfloat16)]
        out_specs = [pl.BlockSpec(chunk, lambda s, *_: (s, 0, 0, 0))] * 4
    return pl.pallas_call(
        functools.partial(
            home_kernel, last, hidden, n_blk, lax.axis_size("chan"), lax.axis_size("sub"), at, of, slots, terms, capacity
        ),
        grid_spec=pltpu.PrefetchScalarGridSpec(
            num_scalar_prefetch=3,
            grid=(slots,),
            in_specs=in_specs,
            out_specs=out_specs,
            scratch_shapes=[
                pltpu.VMEM((n_blk * capacity, cols, rows, hidden), jnp.bfloat16),
                pltpu.VMEM((rows * cols, hidden), jnp.float32),
                pltpu.SMEM((slots * terms,), jnp.int32),
                pltpu.SMEM((n_blk,), jnp.int32),
                pltpu.SemaphoreType.DMA((n_blk,)),
            ],
        ),
        out_shape=out_shape,
        input_output_aliases=aliases,
        compiler_params=pltpu.CompilerParams(vmem_limit_bytes=vmem_limit),
        cost_estimate=pl.CostEstimate(
            flops=2 * slots * rows * cols * channels * 6 * channels * 10,
            bytes_accessed=slots * rows * cols * channels * 16,
            transcendentals=0,
        ),
        name="home",
    )(ids, blocks, owners, *operands)


def exchange_outgoing(left, rights, n_chan, n_sub):
    if n_chan == 2 and n_sub == 2:
        both = ("chan", "sub")
        other_left = lax.ppermute(left, "sub", [(0, 1), (1, 0)])
        lefts = [(other_left, left, 0, 0), (left, other_left, left.shape[1], 0)]
        chunks = []
        for right in rights:
            if chunks:
                (one, *_), (_, two, *_) = chunks[-1]
                right, *_ = lax.optimization_barrier((right, one, two))
            one = lax.ppermute(right, both, [(0, 2), (3, 1), (1, 0), (2, 3)])
            two = lax.ppermute(right, both, [(1, 2), (2, 1)])
            chunks.append([(one, one, 0, 0), (right, two, right.shape[1], 0)])
        return lefts, chunks
    left = lax.all_gather(left, "sub", axis=1, tiled=True)
    right = jnp.concatenate(rights, axis=2)
    right = lax.all_gather(right, "chan", axis=2, tiled=True)
    right = lax.all_to_all(right, "sub", split_axis=2, concat_axis=1, tiled=True)
    cols = right.shape[2] // 2
    chunks = [right[:, :, :cols], right[:, :, cols:]]
    return [(left, left, 0, 0)], [[(r, r, 0, 0)] for r in chunks]


def exchange_incoming(lefts, rights, n_chan, n_sub):
    if n_chan == 2 and n_sub == 2:
        both = ("chan", "sub")
        left_pieces, chunks = [], []
        at = 0
        for left, right in zip(lefts, rights):
            depth = left.shape[1]
            one = lax.ppermute(left, both, [(1, 3), (2, 0), (0, 1), (3, 2)])
            two = lax.ppermute(one, both, [(0, 1), (3, 2)])
            left_pieces += [(left, one, 0, at), (one, two, depth, at)]
            other = lax.ppermute(right, "chan", [(0, 1), (1, 0)])
            chunks.append([(right, right, 0, 0), (other, other, depth, 0)])
            at += left.shape[2]
        return left_pieces, chunks
    left = lax.all_gather(jnp.concatenate(lefts, axis=2), "chan", axis=1, tiled=True)
    left = lax.all_gather(left, "sub", axis=2, tiled=True)
    size = left.shape[2] // n_chan
    left = lax.dynamic_slice_in_dim(left, lax.axis_index("chan") * size, size, 2)
    gathered = [lax.all_gather(right, "chan", axis=1, tiled=True) for right in rights]
    return [(left, left, 0, 0)], [[(r, r, 0, 0)] for r in gathered]


def lane_group(shape, size):
    return lax.broadcasted_iota(jnp.int32, shape, 1) // size


def spread_kernel(size, w_ref, wide_ref):
    hidden = w_ref.shape[1]
    parts = hidden // size
    for side in range(2):
        for kind in range(2):
            start = (2 * side + kind) * hidden
            weights = 0.5 * w_ref[0, :, start : start + hidden].astype(jnp.float32)
            group = lane_group(weights.shape, size)
            for part in range(parts):
                kept = jnp.where(group == part, weights, 0.0)
                at = ((side * parts + part) * 2 + kind) * hidden
                for a in range(parts):
                    moved = pltpu.roll(kept, ((a - part) % parts) * size, 1) if a != part else kept
                    wide_ref[a * hidden : (a + 1) * hidden, at : at + hidden] = moved.astype(jnp.bfloat16)


def spread_weights(w_in, layer, size):
    hidden = w_in.shape[1]
    parts = hidden // size
    shape = (parts * hidden, 4 * parts * hidden)
    return pl.pallas_call(
        functools.partial(spread_kernel, size),
        grid=(1,),
        in_specs=[pl.BlockSpec((1,) + w_in.shape[1:], lambda s: (layer, 0, 0))],
        out_specs=pl.BlockSpec(shape, lambda s: (0, 0)),
        out_shape=jax.ShapeDtypeStruct(shape, jnp.bfloat16),
        compiler_params=pltpu.CompilerParams(vmem_limit_bytes=16 * mebi),
        cost_estimate=pl.CostEstimate(flops=1 << 30, bytes_accessed=1 << 20, transcendentals=0),
        name="spread_weights",
    )(w_in)


def swap_matrix(half):
    shape = (half * half, half * half)
    to, of = lax.broadcasted_iota(jnp.int32, shape, 0), lax.broadcasted_iota(jnp.int32, shape, 1)
    same = jnp.logical_and(to // half == lax.rem(of, half), lax.rem(to, half) == of // half)
    return same.astype(jnp.float32).astype(jnp.bfloat16)


def swapped(values, swap_ref):
    half, _, lanes = values.shape
    moved = dot(swap_ref[...], values.reshape(half * half, lanes))
    return moved.astype(jnp.bfloat16).reshape(half, half, lanes)


def turn(taken, turned, swap_ref):
    half = 16
    for x in range(0, taken.shape[0], half):
        for y in range(0, taken.shape[1], half):
            turned[y : y + half, x : x + half] = swapped(taken[x : x + half, y : y + half], swap_ref)


def make_operand(side, taken, wide_ref, out_refs, laid, swap_ref):
    rows, size, hidden = taken.shape
    parts, bands, half = hidden // size, size, 16
    groups = rows // parts
    stacked = jnp.concatenate(
        [jnp.concatenate([taken[g * parts + a] for a in range(parts)], axis=1) for g in range(groups)], axis=0
    )
    for part in range(parts):
        at = (side * parts + part) * 2 * hidden
        made = dot(stacked, wide_ref[:, at : at + 2 * hidden])
        value = made[:, :hidden] * (1.0 + jnp.tanh(made[:, hidden:]))
        laid[side, :, part * size : (part + 1) * size, :] = value.astype(jnp.bfloat16).reshape(groups, size, hidden)
    blocks = [laid[side, g].T for g in range(groups)]
    starts = [sum(ref.shape[1] for ref in out_refs[:n]) for n in range(len(out_refs))]
    for first in range(0, bands, half):
        for row in range(0, rows, half):
            tiles = []
            for r in range(row, row + half):
                at = r % parts * bands + first
                tiles.append(blocks[r // parts][at : at + half])
            moved = swapped(jnp.stack(tiles), swap_ref)
            for start, ref in zip(starts, out_refs):
                low, high = max(start, first), min(start + ref.shape[1], first + half)
                if low < high:
                    ref[0, low - start : high - start, row : row + half] = moved[low - first : high - first]


def open_layer(layer, natural, left_refs, right_refs, wide, laid, turned, swap):
    turn(natural, turned, swap)
    for side, refs in ((0, left_refs), (1, right_refs)):
        make_operand(side, natural if side == layer % 2 else turned[...], wide, refs, laid, swap)


def norm_and_gate(values, row_alive, col_alive, w_ref, at, norm_ref, gate_ref):
    _, cols, channels = norm_ref.shape
    rows = values.shape[0] // cols
    normed = layer_norm(values)
    gate = sigmoid(dot(normed.astype(jnp.bfloat16), w_ref[0, :, -channels:]))
    gate_ref[0, pl.ds(at, rows)] = gate.reshape(rows, cols, channels)
    mask = row_alive[at : at + rows, None, :] * col_alive[None, :, :]
    norm_ref[pl.ds(at, rows)] = (normed.reshape(rows, cols, channels) * mask).astype(jnp.bfloat16)


def open_kernel(hidden, chunks, n_chan, n_sub, base, of, ids, blocks, pair_ref, chain_ref, w_ref, wide, *rest):
    gate_ref, *operand_refs, norm_ref, laid, turned, swap = rest[-(2 * chunks + 5) :]
    step = pl.program_id(0)
    _, rows, cols, channels = pair_ref.shape
    block = ids[0] * of + base + step

    @pl.when(step == 0)
    def _():
        swap[...] = swap_matrix(16)

    row_alive = alive_rows(chain_ref, (blocks[0, block] * n_chan + ids[1]) * rows, rows)
    col_alive = alive_rows(chain_ref, (blocks[1, block] * n_sub + ids[2]) * cols, cols)
    group = hidden // cols
    for at in range(0, rows, group):
        values = pair_ref[0, pl.ds(at, group)].reshape(group * cols, channels)
        norm_and_gate(values, row_alive, col_alive, w_ref, at, norm_ref, gate_ref)
    open_layer(0, norm_ref[...], operand_refs[:chunks], operand_refs[chunks:], wide, laid, turned, swap)


def operand_scratch(rows, size, hidden):
    parts = hidden // size
    return [
        pltpu.VMEM((2, rows // parts, parts * size, hidden), jnp.bfloat16),
        pltpu.VMEM((size, rows, hidden), jnp.bfloat16),
        pltpu.VMEM((256, 256), jnp.bfloat16),
    ]


def operand_outputs(slots, count, rows, hidden, bands):
    kept = [count if n == 0 else slots for n in range(len(bands))] * 2
    return [jax.ShapeDtypeStruct((k, b, rows, hidden), jnp.bfloat16) for k, b in zip(kept, bands * 2)]


def slot_specs(arrays, slots, base):
    def spec(array):
        offset = base if array.shape[0] == slots else 0
        return pl.BlockSpec((1,) + array.shape[1:], lambda s, *_: (s + offset, 0, 0, 0))

    return [spec(a) for a in arrays]


def fill(out_shape, earlier, slots, n_before):
    if earlier is None:
        return [], [], {}
    shared = [n for n, o in enumerate(out_shape) if o.shape[0] == slots]
    specs = [pl.BlockSpec(memory_space=pl.ANY)] * len(shared)
    return [earlier[n] for n in shared], specs, {n_before + k: n for k, n in enumerate(shared)}


def open_operands(ids, blocks, pair, chains, w_in, wide, hidden, bands, base, count, earlier):
    slots, rows, cols, channels = pair.shape
    out_shape = [jax.ShapeDtypeStruct(pair.shape, jnp.float32)] + operand_outputs(slots, count, rows, hidden, bands)
    more, more_specs, aliases = fill(out_shape, earlier, slots, 6)
    return pl.pallas_call(
        functools.partial(open_kernel, hidden, len(bands), lax.axis_size("chan"), lax.axis_size("sub"), base, slots),
        grid_spec=pltpu.PrefetchScalarGridSpec(
            num_scalar_prefetch=2,
            grid=(count,),
            in_specs=slot_specs([pair], slots, base)
            + [
                pl.BlockSpec(chains.shape, lambda s, *_: (0, 0)),
                pl.BlockSpec((1,) + w_in.shape[1:], lambda s, *_: (0, 0, 0)),
                pl.BlockSpec(wide.shape, lambda s, *_: (0, 0)),
            ]
            + more_specs,
            out_specs=slot_specs(out_shape, slots, base),
            scratch_shapes=[pltpu.VMEM((rows, cols, channels), jnp.bfloat16)] + operand_scratch(rows, cols, hidden),
        ),
        out_shape=out_shape,
        input_output_aliases=aliases,
        compiler_params=pltpu.CompilerParams(vmem_limit_bytes=28 * mebi),
        cost_estimate=pl.CostEstimate(flops=1 << 33, bytes_accessed=1 << 20, transcendentals=0),
        name="open_operands",
    )(ids, blocks, pair, chains, w_in, wide, *more)


def plan_kernel(n_blk, slots_dev, terms, capacity, ids, owners, slots, chosen, place, seen):
    for shift in range(n_blk):
        seen[shift] = 0
        target = lax.rem(ids[0] + shift, n_blk)
        for e in range(2 * (capacity + 1)):
            chosen[2 * shift * (capacity + 1) + e] = 0
        found = jnp.int32(0)
        for e in range(slots_dev * terms):
            block, term = target * slots_dev + e // terms, e % terms
            at = 2 * (shift * (capacity + 1) + jnp.minimum(found, capacity))
            chosen[at] = slots[term, 0, block]
            chosen[at + 1] = slots[term, 1, block]
            found = found + (owners[term, block] == ids[0]).astype(jnp.int32)
    for e in range(slots_dev * terms):
        owner = owners[e % terms, ids[0] * slots_dev + e // terms]
        count = seen[owner]
        seen[owner] = count + 1
        place[e] = lax.rem(ids[0] - owner + n_blk, n_blk) * capacity + count


def make_plan(ids, owners, slots, n_blk, slots_dev, terms, capacity):
    scalars = pl.BlockSpec(memory_space=pltpu.SMEM)
    return pl.pallas_call(
        functools.partial(plan_kernel, n_blk, slots_dev, terms, capacity),
        in_specs=[scalars] * 3,
        out_specs=[scalars] * 2,
        out_shape=[
            jax.ShapeDtypeStruct((2 * n_blk * (capacity + 1),), jnp.int32),
            jax.ShapeDtypeStruct((slots_dev * terms,), jnp.int32),
        ],
        scratch_shapes=[pltpu.SMEM((n_blk,), jnp.int32)],
        compiler_params=pltpu.CompilerParams(vmem_limit_bytes=mebi),
        name="make_plan",
    )(ids, owners, slots)


def banded_kernel(shifts, capacity, pieces, n_refs, size, ids, chosen, *rest):
    refs, rest = rest[:n_refs], rest[n_refs:]
    out_refs, (left_held, right_held, out_held, sems, out_sems) = rest[: len(shifts)], rest[len(shifts) :]
    halves, _, bands, rows, hidden = left_held.shape
    parts = hidden // size
    at_once = 2 if capacity % 2 == 0 else 1

    def copy(n, source):
        side, half, base, *_ = pieces[n]
        target = (left_held, right_held)[side].at[half, pl.ds(base, refs[source].shape[0])]
        return pltpu.make_async_copy(refs[source], target, sems.at[n])

    for n, (*_, on, off) in enumerate(pieces):
        if on == off:
            copy(n, on).start()
        else:

            @pl.when(ids[3] == 1)
            def _(n=n, on=on):
                copy(n, on).start()

            @pl.when(ids[3] == 0)
            def _(n=n, off=off):
                copy(n, off).start()

    for n, piece in enumerate(pieces):
        copy(n, piece[-1]).wait()

    def leave(n):
        return pltpu.make_async_copy(out_held.at[pl.ds(n * capacity, capacity)], out_refs[n], out_sems.at[n])

    for n, shift in enumerate(shifts):

        def one(turn, carry, n=n, shift=shift):
            group = lane_group((size, hidden), size)
            for term in [turn * at_once + t for t in range(at_once)]:
                at = 2 * (shift * (capacity + 1) + term)
                left_slot, right_slot = chosen[at], chosen[at + 1]
                for band in range(bands):
                    left = jnp.concatenate([left_held[h, left_slot, band] for h in range(halves)], axis=1)
                    apart = []
                    for h in range(halves):
                        right = right_held[h, right_slot, band]
                        apart += [jnp.where(group == part, right, jnp.zeros_like(right)) for part in range(parts)]
                    made = dot(left, jnp.concatenate(apart, axis=0))
                    out_held[n * capacity + term, band] = made.astype(jnp.bfloat16)
            return carry

        lax.fori_loop(0, capacity // at_once, one, 0)
        leave(n).start()
    for n in range(len(shifts)):
        leave(n).wait()


def banded_products(shifts, ids, chosen, operands, capacity, size):
    refs, pieces = [], []

    def index_of(array):
        for n, known in enumerate(refs):
            if known is array:
                return n
        refs.append(array)
        return len(refs) - 1

    slots = 0
    for both in operands:
        for side in range(2):
            for half, (on, off) in enumerate(both[side]):
                pieces.append((side, half, slots, index_of(on), index_of(off)))
        slots += both[0][0][0].shape[0]
    halves = len(operands[0][0])
    _, bands, rows, hidden = operands[0][0][0][0].shape
    count = len(shifts) * capacity
    anywhere = pl.BlockSpec(memory_space=pl.ANY)
    return pl.pallas_call(
        functools.partial(banded_kernel, shifts, capacity, tuple(pieces), len(refs), size),
        grid_spec=pltpu.PrefetchScalarGridSpec(
            num_scalar_prefetch=2,
            grid=(),
            in_specs=[anywhere] * len(refs),
            out_specs=[anywhere] * len(shifts),
            scratch_shapes=[
                pltpu.VMEM((halves, slots, bands, rows, hidden), jnp.bfloat16),
                pltpu.VMEM((halves, slots, bands, size, hidden), jnp.bfloat16),
                pltpu.VMEM((count, bands, rows, hidden), jnp.bfloat16),
                pltpu.SemaphoreType.DMA((len(pieces),)),
                pltpu.SemaphoreType.DMA((len(shifts),)),
            ],
        ),
        out_shape=[jax.ShapeDtypeStruct((capacity, bands, rows, hidden), jnp.bfloat16)] * len(shifts),
        compiler_params=pltpu.CompilerParams(vmem_limit_bytes=14 * mebi),
        cost_estimate=pl.CostEstimate(
            flops=2 * count * bands * rows * hidden * hidden * halves, bytes_accessed=1, transcendentals=0
        ),
        name="banded_products",
    )(ids, chosen, *refs)


def close_kernel(layer, last, n_parts, n_blk, n_chan, n_sub, base, of, terms, capacity, ids, blocks, place, *rest):
    chunks = n_parts // n_blk
    arrived, rest = rest[:n_parts], rest[n_parts:]
    cur_ref, gate_ref, w_out_ref = rest[:3]
    if last:
        out_ref, held, wide_out, sems, swap = rest[3:]
    else:
        chain_ref, w_ref, wide = rest[3:6]
        out_ref, next_gate_ref, *operand_refs, held, wide_out, sems, norm_ref, laid, turned, swap = rest[
            -(2 * chunks + 9) :
        ]
        left_refs, right_refs = operand_refs[:chunks], operand_refs[chunks:]
    step = pl.program_id(0)
    _, rows, cols, channels = cur_ref.shape
    _, bands, _, hidden = held.shape
    parts, size = hidden // bands, bands

    def arrival(n):
        at = sum(arrived[m * n_blk].shape[1] for m in range(n // n_blk))
        count = arrived[n].shape[1]
        target = held.at[pl.ds(n % n_blk * capacity, capacity), pl.ds(at, count)]
        return pltpu.make_async_copy(arrived[n], target, sems.at[n])

    @pl.when(step == 0)
    def _():
        for n in range(n_parts):
            arrival(n).start()
        wide_out[...] = jnp.zeros_like(wide_out)
        for part in range(parts):
            for a in range(parts):
                at = (part * parts + a) * bands
                wide_out[at : at + bands, a * channels : (a + 1) * channels] = w_out_ref[
                    0, part * bands : (part + 1) * bands, :
                ]
        swap[...] = swap_matrix(16)
        for n in range(n_parts):
            arrival(n).wait()

    if not last:
        block = ids[0] * of + base + step
        row_alive = alive_rows(chain_ref, (blocks[0, block] * n_chan + ids[1]) * rows, rows)
        col_alive = alive_rows(chain_ref, (blocks[1, block] * n_sub + ids[2]) * cols, cols)
    half = 16
    by_row = [[] for _ in range(rows)]
    for row in range(0, rows, half):
        for band in range(0, bands, half):
            taken = pl.ds(band, half), pl.ds(row, half)
            total = held[(place[(base + step) * terms], *taken)].astype(jnp.float32)
            for t in range(1, terms):
                total = total + held[(place[(base + step) * terms + t], *taken)].astype(jnp.float32)
            moved = swapped(total.astype(jnp.bfloat16), swap)
            for r in range(half):
                by_row[row + r].append(moved[r])
    groups = rows // parts
    pieces = []
    for g in range(groups):
        block = jnp.concatenate([x for a in range(parts) for x in by_row[g * parts + a]]).T
        pieces.append(jnp.concatenate([block[p * cols : (p + 1) * cols] for p in range(parts)], axis=1))
    mixture = jnp.concatenate(pieces)
    together = (lane_group((hidden, hidden), size) == lax.broadcasted_iota(jnp.int32, (hidden, hidden), 0) // size)
    together = together.astype(jnp.float32).astype(jnp.bfloat16)
    average = dot(mixture, jnp.concatenate([together] * parts)) * (1.0 / hidden)
    centred = [mixture[:, p * hidden : (p + 1) * hidden].astype(jnp.float32) - average for p in range(parts)]
    squares = sum(c * c for c in centred)
    high = squares.astype(jnp.bfloat16)
    low = (squares - high.astype(jnp.float32)).astype(jnp.bfloat16)
    variance = dot(jnp.concatenate([high, low], axis=1), jnp.concatenate([together] * 2)) * (1.0 / hidden)
    scale = lax.rsqrt(variance + norm_epsilon)
    normed = jnp.concatenate([(c * scale).astype(jnp.bfloat16) for c in centred], axis=1)
    update = dot(normed, wide_out[...])
    for g in range(groups):
        taken = pl.ds(g * parts, parts)
        change = jnp.concatenate(
            [update[g * cols : (g + 1) * cols, a * channels : (a + 1) * channels] for a in range(parts)]
        )
        gate = gate_ref[0, taken].reshape(parts * cols, channels)
        current = cur_ref[0, taken].astype(jnp.float32).reshape(parts * cols, channels)
        result = (current + gate * change).astype(jnp.bfloat16)
        out_ref[0, taken] = result.reshape(parts, cols, channels)
        if not last:
            norm_and_gate(result, row_alive, col_alive, w_ref, g * parts, norm_ref, next_gate_ref)
    if not last:
        open_layer(layer + 1, norm_ref[...], left_refs, right_refs, wide, laid, turned, swap)


def close_layer(
    layer, arrived, ids, blocks, place, current, gate, w_out, capacity, terms, chains, w_in, wide, last, bands, base, count, earlier
):
    n_blk = len(arrived[0])
    flat = [part for chunk in arrived for part in chunk]
    slots, rows, cols, channels = current.shape
    hidden = w_out.shape[1]

    def layer_spec(array, index):
        return pl.BlockSpec((1,) + array.shape[1:], lambda s, *_: (index, 0, 0))

    in_specs = [pl.BlockSpec(memory_space=pl.ANY)] * len(flat)
    in_specs += slot_specs([current, gate], slots, base) + [layer_spec(w_out, layer)]
    operands = [*flat, current, gate, w_out]
    out_shape = [jax.ShapeDtypeStruct(current.shape, jnp.bfloat16)]
    scratch = [
        pltpu.VMEM((n_blk * capacity, sum(bands[layer]), rows, hidden), jnp.bfloat16),
        pltpu.VMEM((hidden // cols * hidden, hidden // cols * channels), jnp.bfloat16),
        pltpu.SemaphoreType.DMA((len(flat),)),
    ]
    if not last:
        operands += [chains, w_in, wide]
        in_specs += [pl.BlockSpec(chains.shape, lambda s, *_: (0, 0)), layer_spec(w_in, layer + 1)]
        in_specs += [pl.BlockSpec(wide.shape, lambda s, *_: (0, 0))]
        out_shape += [jax.ShapeDtypeStruct(current.shape, jnp.float32)]
        out_shape += operand_outputs(slots, count, cols, hidden, bands[layer + 1])
        scratch += [pltpu.VMEM((rows, cols, channels), jnp.bfloat16)] + operand_scratch(cols, rows, hidden)
    else:
        scratch += [pltpu.VMEM((256, 256), jnp.bfloat16)]
    more, more_specs, aliases = fill(out_shape, earlier, slots, 3 + len(operands))
    return pl.pallas_call(
        functools.partial(
            close_kernel,
            *(layer, last, len(flat), n_blk, lax.axis_size("chan"), lax.axis_size("sub"), base, slots, terms, capacity),
        ),
        grid_spec=pltpu.PrefetchScalarGridSpec(
            num_scalar_prefetch=3,
            grid=(count,),
            in_specs=in_specs + more_specs,
            out_specs=slot_specs(out_shape, slots, base),
            scratch_shapes=scratch,
        ),
        out_shape=out_shape,
        input_output_aliases=aliases,
        compiler_params=pltpu.CompilerParams(vmem_limit_bytes=32 * mebi),
        cost_estimate=pl.CostEstimate(flops=1 << 33, bytes_accessed=1 << 20, transcendentals=0),
        name="close_layer",
    )(ids, blocks, place, *operands, *more)


def after(value, *others):
    return lax.optimization_barrier((value, *others))[0]


def exchange_bands_outgoing(left, right, over):
    both = ("chan", "sub")
    other = lax.ppermute(left, "sub", [(0, 1), (1, 0)])
    one = lax.ppermute(right, both, [(0, 2), (3, 1), (1, 0), (2, 3)])
    two = lax.ppermute(right, both, [(1, 2), (2, 1)])
    return [(other, left), (left, other)], [(one, one), (right, two)]


def exchange_bands_incoming(left, right, over):
    both = ("chan", "sub")
    one = lax.ppermute(left, both, [(1, 3), (2, 0), (0, 1), (3, 2)])
    other = lax.ppermute(right, "chan", [(0, 1), (1, 0)])
    two = lax.ppermute(after(one, over), both, [(0, 1), (3, 2)])
    return [(left, one), (one, two)], [(right, right), (other, other)]


def banded(pair, ids, blocks, owners, slot_of, chains, w_in, w_out, capacity, terms, n_blk):
    slots, rows, cols, channels = pair.shape
    hidden = w_out.shape[1]
    far = n_blk // 2
    shifts = [far] + [s for s in range(1, n_blk) if s != far] + [0]
    layers = w_in.shape[0]
    current = pair
    bands = [[8, 24], [12, 20]]
    chosen, place = make_plan(ids, owners, slot_of, n_blk, slots, terms, capacity)
    half = slots // 2
    halves = [(0, half), (half, slots - half)]
    for layer in range(layers):
        count = len(bands[layer])
        if layer == 0:
            calls, wide = [None], spread_weights(w_in, 0, cols)
            for base, size in halves:
                calls.append(open_operands(ids, blocks, pair, chains, w_in, wide, hidden, bands[0], base, size, calls[-1]))
            gate = calls[-1][0]
        operands = [call[-2 * count :] for call in calls[1:]]
        exchange = exchange_bands_incoming if layer % 2 else exchange_bands_outgoing
        arrived = []
        for chunk in range(count):
            if chunk == 0:
                exchanged = []
                over = operands[-1][count]
                for left, right in [(o[0], o[count]) for o in operands]:
                    if exchanged and layer % 2:
                        (_, (one, two)), (_, (other, _)) = exchanged[-1]
                        left, right = lax.optimization_barrier((left, right, one, other))[:2]
                        right = after(right, two)
                    elif exchanged:
                        ((other, _), _), ((one, _), (_, two)) = exchanged[-1]
                        left, right = lax.optimization_barrier((left, right, other, one, two))[:2]
                    exchanged.append(exchange(left, right, over))
            else:
                left, right = operands[-1][chunk], operands[-1][count + chunk]
                if layer % 2:
                    (_, (_, two)), (_, (other, _)) = exchanged[-1]
                    left, right = lax.optimization_barrier((left, right, two, other))[:2]
                else:
                    ((other, _), _), ((one, _), (_, two)) = exchanged[-1]
                    left = after(left, other)
                    right = after(right, one, two, chosen)
                exchanged = [exchange(left, right, arrived[-1][far])]
            made = banded_products(shifts, ids, chosen, exchanged, capacity, cols)
            parts = [None] * n_blk
            for shift, part in zip(shifts, made):
                if shift:
                    if arrived:
                        part = after(part, arrived[-1][shift])
                    part = lax.ppermute(part, "blk", [(p, (p + shift) % n_blk) for p in range(n_blk)])
                parts[shift] = part
            arrived.append(parts)
        last = layer == layers - 1
        calls = [None]
        if not last:
            wide = spread_weights(after(w_in, made[-1]), layer + 1, cols)
        for base, size in [(0, slots)] if last else halves:
            calls.append(
                close_layer(
                    *(layer, arrived, ids, blocks, place, current, gate, w_out, capacity, terms, chains, w_in, wide, last),
                    *(bands, base, size, calls[-1]),
                )
            )
        if last:
            return calls[-1][0]
        current, gate = calls[-1][:2]


def per_device(pair, block_list, term_owner, term_slots, chain_ids, w_in, w_out):
    n_blk = lax.axis_size("blk")
    n_chan = lax.axis_size("chan")
    n_sub = lax.axis_size("sub")
    position = lax.axis_index("blk")
    row_group = lax.axis_index("chan")
    col_group = lax.axis_index("sub")
    slots, rows, cols, channels = pair.shape
    hidden = w_out.shape[1]
    terms = term_owner.shape[1]
    capacity = max(2, -(-slots * terms // n_blk))
    fast = n_chan == 2 and n_sub == 2
    on_diagonal = (row_group == col_group).astype(jnp.int32)
    ids = jnp.stack([position, row_group, col_group, on_diagonal]).astype(jnp.int32)
    blocks = block_list.T
    owners = term_owner.T
    slot_of = jnp.transpose(term_slots, (1, 2, 0))
    chains = chain_ids.reshape(-1, 128)
    if fast and rows == cols == 32 and channels == hidden == 128:
        return banded(pair, ids, blocks, owners, slot_of, chains, w_in, w_out, capacity, terms, n_blk)
    shifts = [n_blk // 2] + [s for s in range(1, n_blk) if s != n_blk // 2] + [0]

    def all_products(lefts, right):
        parts = [None] * n_blk
        for shift in shifts:
            made = term_products(shift, ids, owners, slot_of, lefts, right, capacity, slots, terms)
            if shift:
                pairs = [(p, (p + shift) % n_blk) for p in range(n_blk)]
                made = lax.ppermute(made, "blk", pairs)
            parts[shift] = made
        return parts

    def at_home(layer, parts, current, gate, at, of, into=None):
        last = layer == w_in.shape[0] - 1
        return home(
            layer, parts, ids, blocks, owners, current, gate, w_out, capacity, terms, at, of, chains, w_in, last, into
        )

    gate, left, *rights = first_operands(ids, blocks, pair, chains, w_in, hidden, 2 if fast else 1)
    lefts, chunks = exchange_outgoing(left, rights, n_chan, n_sub)
    count = len(chunks)
    made = [all_products(lefts, right) for right in chunks]
    homes = [at_home(0, parts, pair, gate, at, count) for at, parts in enumerate(made)]
    lefts, chunks = exchange_incoming([h[2] for h in homes], [h[3] for h in homes], n_chan, n_sub)
    made = [all_products(lefts, right) for right in chunks]
    out = None
    for at, parts in enumerate(made):
        (out,) = at_home(1, parts, homes[at][0], homes[at][1], at, count, into=out)
    return out


def solution(mesh):
    in_specs = (
        P(("groups", "blk"), "chan", "sub", None),
        P("groups", None),
        P("groups", None),
        P("groups", None, None),
        P("groups"),
        P(),
        P(),
    )
    out_specs = P(("groups", "blk"), "chan", "sub", None)
    return jax.shard_map(
        per_device, mesh=mesh, in_specs=in_specs, out_specs=out_specs, check_vma=False
    )
```

```python
import functools

import jax
import jax.numpy as jnp
from jax import lax
from jax.experimental import pallas as pl
from jax.experimental.pallas import tpu as pltpu
from jax.sharding import PartitionSpec as P

norm_epsilon = 1e-05
mebi = 1024 * 1024
vmem_limit = 56 * mebi


def sigmoid(values):
    return 0.5 + 0.5 * jnp.tanh(0.5 * values)


def layer_norm(values):
    values = values.astype(jnp.float32)
    centred = values - jnp.mean(values, axis=-1, keepdims=True)
    variance = jnp.mean(centred * centred, axis=-1, keepdims=True)
    return centred * lax.rsqrt(variance + norm_epsilon)


def alive_rows(chain_ref, start, size):
    lanes = chain_ref.shape[1]
    line = chain_ref[pl.ds(start // lanes, 1), :] >= 0
    spot = lax.broadcasted_iota(jnp.int32, (size, lanes), 0) + lax.rem(start, lanes)
    pick = jnp.logical_and(lax.broadcasted_iota(jnp.int32, (size, lanes), 1) == spot, line)
    return dot(pick.astype(jnp.float32).astype(jnp.bfloat16), jnp.ones((lanes, lanes), jnp.bfloat16))


def dot(a, b):
    return jnp.dot(a, b, preferred_element_type=jnp.float32)


def gated_pair(projected, mask, hidden):
    left = mask * sigmoid(projected[:, hidden : 2 * hidden]) * projected[:, :hidden]
    right = mask * sigmoid(projected[:, 3 * hidden : 4 * hidden]) * projected[:, 2 * hidden : 3 * hidden]
    return left.astype(jnp.bfloat16), right.astype(jnp.bfloat16)


def first_kernel(hidden, row_parts, n_chan, n_sub, ids, blocks, pair_ref, chain_ref, w_ref, gate_ref, left_ref, *rest):
    right_refs, (norm_ref, turned_ref) = rest[:row_parts], rest[row_parts:]
    slots = pl.num_programs(0)
    _, rows, cols, channels = pair_ref.shape
    block = ids[0] * slots + pl.program_id(0)
    row_alive = alive_rows(chain_ref, (blocks[0, block] * n_chan + ids[1]) * rows, rows)
    col_alive = alive_rows(chain_ref, (blocks[1, block] * n_sub + ids[2]) * cols, cols)
    group = max(1, 256 // cols)
    for start in range(0, rows, group):
        at = pl.ds(start, group)
        normed = layer_norm(pair_ref[0, at].reshape(group * cols, channels))
        norm_ref[pl.ds(start * cols, group * cols), :] = normed
        gate = sigmoid(dot(normed.astype(jnp.bfloat16), w_ref[0, :, 4 * hidden :]))
        gate_ref[0, at] = gate.reshape(group, cols, channels)
    for col in range(cols):
        turned_ref[col] = norm_ref[pl.ds(col, rows, stride=cols), :].astype(jnp.bfloat16)
    step = max(1, 128 // rows)
    part = rows // row_parts
    for start in range(0, cols, step):
        taken = turned_ref[start : start + step].reshape(step * rows, channels)
        projected = dot(taken, w_ref[0, :, : 4 * hidden])
        mask = col_alive[start : start + step][:, None, :] * row_alive[None, :, :]
        left, right = gated_pair(projected, mask.reshape(step * rows, -1), hidden)
        left_ref[0, start : start + step] = left.reshape(step, rows, hidden)
        right = right.reshape(step, rows, hidden)
        for p, right_ref in enumerate(right_refs):
            right_ref[0, start : start + step] = right[:, p * part : (p + 1) * part]


def first_operands(ids, blocks, pair, chains, w_in, hidden, row_parts):
    slots, rows, cols, channels = pair.shape
    part = rows // row_parts
    operand = jax.ShapeDtypeStruct((slots, cols, rows, hidden), jnp.bfloat16)
    right = jax.ShapeDtypeStruct((slots, cols, part, hidden), jnp.bfloat16)
    return pl.pallas_call(
        functools.partial(first_kernel, hidden, row_parts, lax.axis_size("chan"), lax.axis_size("sub")),
        grid_spec=pltpu.PrefetchScalarGridSpec(
            num_scalar_prefetch=2,
            grid=(slots,),
            in_specs=[
                pl.BlockSpec((1, rows, cols, channels), lambda s, *_: (s, 0, 0, 0)),
                pl.BlockSpec(chains.shape, lambda s, *_: (0, 0)),
                pl.BlockSpec((1,) + w_in.shape[1:], lambda s, *_: (0, 0, 0)),
            ],
            out_specs=[
                pl.BlockSpec((1, rows, cols, channels), lambda s, *_: (s, 0, 0, 0)),
                pl.BlockSpec((1, cols, rows, hidden), lambda s, *_: (s, 0, 0, 0)),
            ]
            + [pl.BlockSpec((1, cols, part, hidden), lambda s, *_: (s, 0, 0, 0))] * row_parts,
            scratch_shapes=[
                pltpu.VMEM((rows * cols, channels), jnp.float32),
                pltpu.VMEM((cols, rows, channels), jnp.bfloat16),
            ],
        ),
        out_shape=[jax.ShapeDtypeStruct(pair.shape, jnp.float32), operand] + [right] * row_parts,
        compiler_params=pltpu.CompilerParams(vmem_limit_bytes=vmem_limit),
        name="first_operands",
    )(ids, blocks, pair, chains, w_in)


def product_kernel(shift, n_blk, slots_dev, terms, capacity, pieces, n_refs, ids, owners, slots, *rest):
    refs = rest[:n_refs]
    out_ref, left_held, right_held, right_wide, chosen, sems = rest[n_refs:]
    step = pl.program_id(0)
    turn = lax.rem(step, 2)
    _, depth, n_i, hidden = left_held.shape
    n_j = right_wide.shape[1]

    @pl.when(step == 0)
    def _():
        target = lax.rem(ids[0] + shift, n_blk)
        for e in range(2 * capacity):
            chosen[e] = 0

        def scan(e, count):
            block, term = target * slots_dev + e // terms, lax.rem(e, terms)
            here = jnp.logical_and(owners[term, block] == ids[0], count < capacity)

            @pl.when(here)
            def _():
                chosen[2 * count] = slots[term, 0, block]
                chosen[2 * count + 1] = slots[term, 1, block]

            return count + here.astype(jnp.int32)

        lax.fori_loop(0, slots_dev * terms, scan, jnp.int32(0))

    def copy(n, term, buffer, source):
        side, _, _, k0, depth_of, i0, size = pieces[n]
        held = (left_held, right_held)[side]
        return pltpu.make_async_copy(
            refs[source].at[chosen[2 * term + side]],
            held.at[buffer, pl.ds(k0, depth_of), pl.ds(i0, size), :],
            sems.at[buffer, n],
        )

    def start(term, buffer):
        for n, (_, on, off, *_) in enumerate(pieces):
            if on == off:
                copy(n, term, buffer, on).start()
            else:

                @pl.when(ids[3] == 1)
                def _(n=n, on=on):
                    copy(n, term, buffer, on).start()

                @pl.when(ids[3] == 0)
                def _(n=n, off=off):
                    copy(n, term, buffer, off).start()

    @pl.when(step == 0)
    def _():
        start(0, 0)

    @pl.when(step + 1 < capacity)
    def _():
        start(step + 1, 1 - turn)

    for n, piece in enumerate(pieces):
        copy(n, step, turn, piece[1]).wait()

    span = 8

    def widen(n, carry):
        at = pl.ds(n * span, span)
        right_wide[at] = right_held[turn, at].astype(jnp.float32)
        return carry

    lax.fori_loop(0, depth // span, widen, 0)

    group = min(8, n_j)
    unroll = 4
    for j0 in range(0, n_j, group):

        def body(n, sums):
            for u in range(unroll):
                k = n * unroll + u
                left = left_held[turn, k].astype(jnp.float32).reshape(n_i // 8, 8, hidden)
                sums = tuple(
                    total + left * right_wide[k, pl.ds(j0 + j, 8, stride=0), :][None]
                    for j, total in enumerate(sums)
                )
            return sums

        zero = jnp.zeros((n_i // 8, 8, hidden), jnp.float32)
        sums = lax.fori_loop(0, depth // unroll, body, (zero,) * group)
        for j, total in enumerate(sums):
            out_ref[0, j0 + j] = total.reshape(n_i, hidden).astype(jnp.bfloat16)


def term_products(shift, ids, owners, slots, lefts, rights, capacity, slots_dev, terms):
    n_blk = lax.axis_size("blk")
    refs, pieces = [], []

    def index_of(array):
        for n, known in enumerate(refs):
            if known is array:
                return n
        refs.append(array)
        return len(refs) - 1

    for side, operands in ((0, lefts), (1, rights)):
        for on, off, k0, i0 in operands:
            pieces.append((side, index_of(on), index_of(off), k0, on.shape[1], i0, on.shape[2]))
    hidden = lefts[0][0].shape[3]
    n_i = max(p[5] + p[6] for p in pieces if p[0] == 0)
    n_j = max(p[5] + p[6] for p in pieces if p[0] == 1)
    depth = max(p[3] + p[4] for p in pieces)
    return pl.pallas_call(
        functools.partial(
            product_kernel, shift, n_blk, slots_dev, terms, capacity, tuple(pieces), len(refs)
        ),
        grid_spec=pltpu.PrefetchScalarGridSpec(
            num_scalar_prefetch=3,
            grid=(capacity,),
            in_specs=[pl.BlockSpec(memory_space=pl.ANY)] * len(refs),
            out_specs=pl.BlockSpec((1, n_j, n_i, hidden), lambda t, *_: (t, 0, 0, 0)),
            scratch_shapes=[
                pltpu.VMEM((2, depth, n_i, hidden), jnp.bfloat16),
                pltpu.VMEM((2, depth, n_j, hidden), jnp.bfloat16),
                pltpu.VMEM((depth, n_j, hidden), jnp.float32),
                pltpu.SMEM((2 * capacity,), jnp.int32),
                pltpu.SemaphoreType.DMA((2, len(pieces))),
            ],
        ),
        out_shape=jax.ShapeDtypeStruct((capacity, n_j, n_i, hidden), jnp.bfloat16),
        compiler_params=pltpu.CompilerParams(vmem_limit_bytes=vmem_limit),
        cost_estimate=pl.CostEstimate(
            flops=2 * capacity * n_i * n_j * depth * hidden * 100,
            bytes_accessed=capacity * (depth * (n_i + n_j) + n_i * n_j) * hidden * 2,
            transcendentals=0,
        ),
        name="term_products",
    )(ids, owners, slots, *refs)


def home_kernel(last, hidden, n_blk, n_chan, n_sub, at, of, slots_dev, terms, capacity, ids, blocks, owners, *rest):
    parts, rest = rest[:n_blk], rest[n_blk:]
    scratch, rest = rest[-5:], rest[:-5]
    held, turned, place, seen, sems = scratch
    cur_ref, gate_ref, w_out_ref = rest[:3]
    if last:
        out_ref = rest[-1]
    else:
        chain_ref, w_ref, out_ref, next_gate_ref, left_ref, right_ref = rest[3:]
    step = pl.program_id(0)
    _, rows, cols, channels = cur_ref.shape

    def arrival(shift):
        return pltpu.make_async_copy(parts[shift], held.at[pl.ds(shift * capacity, capacity)], sems.at[shift])

    @pl.when(step == 0)
    def _():
        for shift in range(n_blk):
            arrival(shift).start()
            seen[shift] = 0

        def scan(e, carry):
            owner = owners[lax.rem(e, terms), ids[0] * slots_dev + e // terms]
            shift = lax.rem(ids[0] - owner + n_blk, n_blk)
            count = seen[owner]
            seen[owner] = count + 1
            place[e] = shift * capacity + count
            return carry

        lax.fori_loop(0, slots_dev * terms, scan, jnp.int32(0))
        for shift in range(n_blk):
            arrival(shift).wait()

    if not last:
        block = ids[0] * slots_dev + step
        row_alive = alive_rows(chain_ref, (blocks[0, block] * n_chan + ids[1]) * rows, rows)
        col_alive = alive_rows(chain_ref, ((blocks[1, block] * n_sub + ids[2]) * of + at) * cols, cols)
    span = max(1, 128 // rows)
    for start in range(0, cols, span):
        taken = pl.ds(start, span)
        total = held[place[step * terms], taken].astype(jnp.float32)
        for t in range(1, terms):
            total = total + held[place[step * terms + t], taken].astype(jnp.float32)
        rounded = total.astype(jnp.bfloat16).astype(jnp.float32)
        turned[pl.ds(start * rows, span * rows), :] = rounded.reshape(span * rows, hidden)
    group = min(rows, max(1, 256 // cols))
    for start in range(0, rows, group):
        taken = pl.ds(start, group)
        mixture = jnp.concatenate(
            [turned[pl.ds(row, cols, stride=rows), :].astype(jnp.bfloat16) for row in range(start, start + group)]
        )
        update = dot(layer_norm(mixture).astype(jnp.bfloat16), w_out_ref[0])
        current = cur_ref[0, taken].astype(jnp.float32).reshape(group * cols, channels)
        gate = gate_ref[0, taken].reshape(group * cols, channels)
        result = (current + gate * update).astype(jnp.bfloat16)
        out_ref[0, taken] = result.reshape(group, cols, channels)
        if not last:
            normed = layer_norm(result).astype(jnp.bfloat16)
            projected = dot(normed, w_ref[0])
            next_gate_ref[0, taken] = sigmoid(projected[:, 4 * hidden :]).reshape(group, cols, channels)
            mask = row_alive[start : start + group][:, None, :] * col_alive[None, :, :]
            left, right = gated_pair(projected, mask.reshape(group * cols, channels), hidden)
            left_ref[0, taken] = left.reshape(group, cols, hidden)
            right_ref[0, taken] = right.reshape(group, cols, hidden)


def home(layer, parts, ids, blocks, owners, current, gate, w_out, capacity, terms, at, of, chains, w_in, last, into=None):
    n_blk = len(parts)
    slots, rows, _, channels = current.shape
    hidden = w_out.shape[1]
    cols = parts[0].shape[1]
    chunk = (1, rows, cols, channels)

    def chunk_spec(array):
        whole = array.shape[2] != cols
        return pl.BlockSpec(chunk, lambda s, *_: (s, 0, at if whole else 0, 0))

    def layer_spec(array, index):
        return pl.BlockSpec((1,) + array.shape[1:], lambda s, *_: (index, 0, 0))

    in_specs = [pl.BlockSpec(memory_space=pl.ANY)] * n_blk + [
        chunk_spec(current),
        chunk_spec(gate),
        layer_spec(w_out, layer),
    ]
    operands = [*parts, current, gate, w_out]
    aliases = {}
    if last:
        if into is not None:
            aliases = {3 + len(operands): 0}
            operands.append(into)
            in_specs.append(pl.BlockSpec(memory_space=pl.ANY))
        out_shape = [jax.ShapeDtypeStruct((slots, rows, cols * of, channels), jnp.bfloat16)]
        out_specs = [pl.BlockSpec(chunk, lambda s, *_: (s, 0, at, 0))]
    else:
        operands += [chains, w_in]
        in_specs += [pl.BlockSpec(chains.shape, lambda s, *_: (0, 0)), layer_spec(w_in, layer + 1)]
        small = (slots, rows, cols, channels)
        out_shape = [jax.ShapeDtypeStruct(small, t) for t in (jnp.bfloat16, jnp.float32, jnp.bfloat16, jnp.bfloat16)]
        out_specs = [pl.BlockSpec(chunk, lambda s, *_: (s, 0, 0, 0))] * 4
    return pl.pallas_call(
        functools.partial(
            home_kernel, last, hidden, n_blk, lax.axis_size("chan"), lax.axis_size("sub"), at, of, slots, terms, capacity
        ),
        grid_spec=pltpu.PrefetchScalarGridSpec(
            num_scalar_prefetch=3,
            grid=(slots,),
            in_specs=in_specs,
            out_specs=out_specs,
            scratch_shapes=[
                pltpu.VMEM((n_blk * capacity, cols, rows, hidden), jnp.bfloat16),
                pltpu.VMEM((rows * cols, hidden), jnp.float32),
                pltpu.SMEM((slots * terms,), jnp.int32),
                pltpu.SMEM((n_blk,), jnp.int32),
                pltpu.SemaphoreType.DMA((n_blk,)),
            ],
        ),
        out_shape=out_shape,
        input_output_aliases=aliases,
        compiler_params=pltpu.CompilerParams(vmem_limit_bytes=vmem_limit),
        cost_estimate=pl.CostEstimate(
            flops=2 * slots * rows * cols * channels * 6 * channels * 10,
            bytes_accessed=slots * rows * cols * channels * 16,
            transcendentals=0,
        ),
        name="home",
    )(ids, blocks, owners, *operands)


def exchange_outgoing(left, rights, n_chan, n_sub):
    if n_chan == 2 and n_sub == 2:
        both = ("chan", "sub")
        other_left = lax.ppermute(left, "sub", [(0, 1), (1, 0)])
        lefts = [(other_left, left, 0, 0), (left, other_left, left.shape[1], 0)]
        chunks = []
        for right in rights:
            if chunks:
                (one, *_), (_, two, *_) = chunks[-1]
                right, *_ = lax.optimization_barrier((right, one, two))
            one = lax.ppermute(right, both, [(0, 2), (3, 1), (1, 0), (2, 3)])
            two = lax.ppermute(right, both, [(1, 2), (2, 1)])
            chunks.append([(one, one, 0, 0), (right, two, right.shape[1], 0)])
        return lefts, chunks
    left = lax.all_gather(left, "sub", axis=1, tiled=True)
    right = jnp.concatenate(rights, axis=2)
    right = lax.all_gather(right, "chan", axis=2, tiled=True)
    right = lax.all_to_all(right, "sub", split_axis=2, concat_axis=1, tiled=True)
    cols = right.shape[2] // 2
    chunks = [right[:, :, :cols], right[:, :, cols:]]
    return [(left, left, 0, 0)], [[(r, r, 0, 0)] for r in chunks]


def exchange_incoming(lefts, rights, n_chan, n_sub):
    if n_chan == 2 and n_sub == 2:
        both = ("chan", "sub")
        left_pieces, chunks = [], []
        at = 0
        for left, right in zip(lefts, rights):
            depth = left.shape[1]
            one = lax.ppermute(left, both, [(1, 3), (2, 0), (0, 1), (3, 2)])
            two = lax.ppermute(one, both, [(0, 1), (3, 2)])
            left_pieces += [(left, one, 0, at), (one, two, depth, at)]
            other = lax.ppermute(right, "chan", [(0, 1), (1, 0)])
            chunks.append([(right, right, 0, 0), (other, other, depth, 0)])
            at += left.shape[2]
        return left_pieces, chunks
    left = lax.all_gather(jnp.concatenate(lefts, axis=2), "chan", axis=1, tiled=True)
    left = lax.all_gather(left, "sub", axis=2, tiled=True)
    size = left.shape[2] // n_chan
    left = lax.dynamic_slice_in_dim(left, lax.axis_index("chan") * size, size, 2)
    gathered = [lax.all_gather(right, "chan", axis=1, tiled=True) for right in rights]
    return [(left, left, 0, 0)], [[(r, r, 0, 0)] for r in gathered]


def lane_group(shape, size):
    return lax.broadcasted_iota(jnp.int32, shape, 1) // size


def spread_kernel(size, w_ref, wide_ref):
    hidden = w_ref.shape[1]
    parts = hidden // size
    for side in range(2):
        for kind in range(2):
            start = (2 * side + kind) * hidden
            weights = 0.5 * w_ref[0, :, start : start + hidden].astype(jnp.float32)
            group = lane_group(weights.shape, size)
            for part in range(parts):
                kept = jnp.where(group == part, weights, 0.0)
                at = ((side * parts + part) * 2 + kind) * hidden
                for a in range(parts):
                    moved = pltpu.roll(kept, ((a - part) % parts) * size, 1) if a != part else kept
                    wide_ref[a * hidden : (a + 1) * hidden, at : at + hidden] = moved.astype(jnp.bfloat16)


def spread_weights(w_in, layer, size):
    hidden = w_in.shape[1]
    parts = hidden // size
    shape = (parts * hidden, 4 * parts * hidden)
    return pl.pallas_call(
        functools.partial(spread_kernel, size),
        grid=(1,),
        in_specs=[pl.BlockSpec((1,) + w_in.shape[1:], lambda s: (layer, 0, 0))],
        out_specs=pl.BlockSpec(shape, lambda s: (0, 0)),
        out_shape=jax.ShapeDtypeStruct(shape, jnp.bfloat16),
        compiler_params=pltpu.CompilerParams(vmem_limit_bytes=16 * mebi),
        cost_estimate=pl.CostEstimate(flops=1 << 30, bytes_accessed=1 << 20, transcendentals=0),
        name="spread_weights",
    )(w_in)


def swap_matrix(half):
    shape = (half * half, half * half)
    to, of = lax.broadcasted_iota(jnp.int32, shape, 0), lax.broadcasted_iota(jnp.int32, shape, 1)
    same = jnp.logical_and(to // half == lax.rem(of, half), lax.rem(to, half) == of // half)
    return same.astype(jnp.float32).astype(jnp.bfloat16)


def swapped(values, swap_ref):
    half, _, lanes = values.shape
    moved = dot(swap_ref[...], values.reshape(half * half, lanes))
    return moved.astype(jnp.bfloat16).reshape(half, half, lanes)


def turn(taken, turned, swap_ref):
    half = 16
    for x in range(0, taken.shape[0], half):
        for y in range(0, taken.shape[1], half):
            turned[y : y + half, x : x + half] = swapped(taken[x : x + half, y : y + half], swap_ref)


def make_operand(side, taken, wide_ref, out_refs, laid, swap_ref):
    rows, size, hidden = taken.shape
    parts, bands, half = hidden // size, size, 16
    groups = rows // parts
    stacked = jnp.concatenate(
        [jnp.concatenate([taken[g * parts + a] for a in range(parts)], axis=1) for g in range(groups)], axis=0
    )
    for part in range(parts):
        at = (side * parts + part) * 2 * hidden
        made = dot(stacked, wide_ref[:, at : at + 2 * hidden])
        value = made[:, :hidden] * (1.0 + jnp.tanh(made[:, hidden:]))
        laid[side, :, part * size : (part + 1) * size, :] = value.astype(jnp.bfloat16).reshape(groups, size, hidden)
    blocks = [laid[side, g].T for g in range(groups)]
    starts = [sum(ref.shape[1] for ref in out_refs[:n]) for n in range(len(out_refs))]
    for first in range(0, bands, half):
        for row in range(0, rows, half):
            tiles = []
            for r in range(row, row + half):
                at = r % parts * bands + first
                tiles.append(blocks[r // parts][at : at + half])
            moved = swapped(jnp.stack(tiles), swap_ref)
            for start, ref in zip(starts, out_refs):
                low, high = max(start, first), min(start + ref.shape[1], first + half)
                if low < high:
                    ref[0, low - start : high - start, row : row + half] = moved[low - first : high - first]


def open_layer(layer, natural, left_refs, right_refs, wide, laid, turned, swap):
    turn(natural, turned, swap)
    for side, refs in ((0, left_refs), (1, right_refs)):
        make_operand(side, natural if side == layer % 2 else turned[...], wide, refs, laid, swap)


def norm_and_gate(values, row_alive, col_alive, at, norm_ref, w_ref=None, gate_ref=None):
    _, cols, channels = norm_ref.shape
    rows = values.shape[0] // cols
    normed = layer_norm(values)
    if gate_ref is not None:
        gate = sigmoid(dot(normed.astype(jnp.bfloat16), w_ref[0, :, -channels:]))
        gate_ref[0, pl.ds(at, rows)] = gate.reshape(rows, cols, channels)
    mask = row_alive[at : at + rows, None, :] * col_alive[None, :, :]
    norm_ref[pl.ds(at, rows)] = (normed.reshape(rows, cols, channels) * mask).astype(jnp.bfloat16)


def open_kernel(hidden, chunks, n_chan, n_sub, base, of, ids, blocks, pair_ref, chain_ref, w_ref, wide, *rest):
    gate_ref, *operand_refs, norm_ref, laid, turned, swap = rest[-(2 * chunks + 5) :]
    step = pl.program_id(0)
    _, rows, cols, channels = pair_ref.shape
    block = ids[0] * of + base + step

    @pl.when(step == 0)
    def _():
        swap[...] = swap_matrix(16)

    row_alive = alive_rows(chain_ref, (blocks[0, block] * n_chan + ids[1]) * rows, rows)
    col_alive = alive_rows(chain_ref, (blocks[1, block] * n_sub + ids[2]) * cols, cols)
    group = hidden // cols
    for at in range(0, rows, group):
        values = pair_ref[0, pl.ds(at, group)].reshape(group * cols, channels)
        norm_and_gate(values, row_alive, col_alive, at, norm_ref, w_ref, gate_ref)
    open_layer(0, norm_ref[...], operand_refs[:chunks], operand_refs[chunks:], wide, laid, turned, swap)


def operand_scratch(rows, size, hidden):
    parts = hidden // size
    return [
        pltpu.VMEM((2, rows // parts, parts * size, hidden), jnp.bfloat16),
        pltpu.VMEM((size, rows, hidden), jnp.bfloat16),
        pltpu.VMEM((256, 256), jnp.bfloat16),
    ]


def operand_outputs(slots, count, rows, hidden, bands):
    kept = [count if n == 0 else slots for n in range(len(bands))] * 2
    return [jax.ShapeDtypeStruct((k, b, rows, hidden), jnp.bfloat16) for k, b in zip(kept, bands * 2)]


def slot_specs(arrays, slots, base):
    def spec(array):
        offset = base if array.shape[0] == slots else 0
        return pl.BlockSpec((1,) + array.shape[1:], lambda s, *_: (s + offset, 0, 0, 0))

    return [spec(a) for a in arrays]


def fill(out_shape, earlier, slots, n_before):
    if earlier is None:
        return [], [], {}
    shared = [n for n, o in enumerate(out_shape) if o.shape[0] == slots]
    specs = [pl.BlockSpec(memory_space=pl.ANY)] * len(shared)
    return [earlier[n] for n in shared], specs, {n_before + k: n for k, n in enumerate(shared)}


def open_operands(ids, blocks, pair, chains, w_in, wide, hidden, bands, base, count, earlier):
    slots, rows, cols, channels = pair.shape
    out_shape = [jax.ShapeDtypeStruct(pair.shape, jnp.float32)] + operand_outputs(slots, count, rows, hidden, bands)
    more, more_specs, aliases = fill(out_shape, earlier, slots, 6)
    return pl.pallas_call(
        functools.partial(open_kernel, hidden, len(bands), lax.axis_size("chan"), lax.axis_size("sub"), base, slots),
        grid_spec=pltpu.PrefetchScalarGridSpec(
            num_scalar_prefetch=2,
            grid=(count,),
            in_specs=slot_specs([pair], slots, base)
            + [
                pl.BlockSpec(chains.shape, lambda s, *_: (0, 0)),
                pl.BlockSpec((1,) + w_in.shape[1:], lambda s, *_: (0, 0, 0)),
                pl.BlockSpec(wide.shape, lambda s, *_: (0, 0)),
            ]
            + more_specs,
            out_specs=slot_specs(out_shape, slots, base),
            scratch_shapes=[pltpu.VMEM((rows, cols, channels), jnp.bfloat16)] + operand_scratch(rows, cols, hidden),
        ),
        out_shape=out_shape,
        input_output_aliases=aliases,
        compiler_params=pltpu.CompilerParams(vmem_limit_bytes=28 * mebi),
        cost_estimate=pl.CostEstimate(flops=1 << 33, bytes_accessed=1 << 20, transcendentals=0),
        name="open_operands",
    )(ids, blocks, pair, chains, w_in, wide, *more)


def far_kernel(layer, n_blk, far, n_chan, n_sub, of, bases, ids, blocks, mine, *rest):
    sources, (chain_ref, wide, left_ref, right_ref, norm_ref, laid, turned, swap) = rest[:-8], rest[-8:]
    step = pl.program_id(0)
    rows, cols, channels = norm_ref.shape
    holder = lax.rem(ids[0] - far + n_blk, n_blk)

    @pl.when(step == 0)
    def _():
        swap[...] = swap_matrix(16)

    group = channels // cols
    for side, out_ref in ((0, left_ref), (1, right_ref)):
        slot = mine[2 * step + side]
        refs = sources[side * len(bases) : (side + 1) * len(bases)]
        block = holder * of + slot
        row_alive = alive_rows(chain_ref, (blocks[0, block] * n_chan + ids[1]) * rows, rows)
        col_alive = alive_rows(chain_ref, (blocks[1, block] * n_sub + ids[2]) * cols, cols)
        for at in range(0, rows, group):
            values = refs[0][0, pl.ds(at, group)]
            for base, ref in zip(bases[1:], refs[1:]):
                values = jnp.where(slot >= base, ref[0, pl.ds(at, group)], values)
            norm_and_gate(values.reshape(group * cols, channels), row_alive, col_alive, at, norm_ref)
        if side == layer % 2:
            make_operand(side, norm_ref[...], wide, [out_ref], laid, swap)
        else:
            turn(norm_ref[...], turned, swap)
            make_operand(side, turned[...], wide, [out_ref], laid, swap)


def far_operands(layer, ids, blocks, mine, sources, chains, wide, far, capacity, of, hidden):
    n_blk = lax.axis_size("blk")
    _, rows, cols, channels = sources[0].shape
    bases = [sum(a.shape[0] for a in sources[:n]) for n in range(len(sources))]

    def source_spec(side, base, size):
        def place(t, ids, blocks, mine):
            return jnp.clip(mine[2 * t + side] - base, 0, size - 1), 0, 0, 0

        return pl.BlockSpec((1, rows, cols, channels), place)

    in_specs = [source_spec(side, b, a.shape[0]) for side in range(2) for b, a in zip(bases, sources)]
    in_specs += [pl.BlockSpec(chains.shape, lambda t, *_: (0, 0)), pl.BlockSpec(wide.shape, lambda t, *_: (0, 0))]
    shape = (capacity, hidden // (hidden // cols), rows, hidden)
    return pl.pallas_call(
        functools.partial(
            far_kernel, layer, n_blk, far, lax.axis_size("chan"), lax.axis_size("sub"), of, tuple(bases)
        ),
        grid_spec=pltpu.PrefetchScalarGridSpec(
            num_scalar_prefetch=3,
            grid=(capacity,),
            in_specs=in_specs,
            out_specs=[pl.BlockSpec((1,) + shape[1:], lambda t, *_: (t, 0, 0, 0))] * 2,
            scratch_shapes=[pltpu.VMEM((rows, cols, channels), jnp.bfloat16)] + operand_scratch(rows, cols, hidden),
        ),
        out_shape=[jax.ShapeDtypeStruct(shape, jnp.bfloat16)] * 2,
        compiler_params=pltpu.CompilerParams(vmem_limit_bytes=20 * mebi),
        cost_estimate=pl.CostEstimate(flops=1 << 33, bytes_accessed=1 << 20, transcendentals=0),
        name="far_operands",
    )(ids, blocks, mine, *sources, *sources, chains, wide)


def plan_kernel(n_blk, far, slots_dev, terms, capacity, ids, owners, slots, chosen, place, mine, seen):
    for shift in range(n_blk):
        seen[shift] = 0
        target = lax.rem(ids[0] + shift, n_blk)
        for e in range(2 * (capacity + 1)):
            chosen[2 * shift * (capacity + 1) + e] = 0
        found = jnp.int32(0)
        for e in range(slots_dev * terms):
            block, term = target * slots_dev + e // terms, e % terms
            at = 2 * (shift * (capacity + 1) + jnp.minimum(found, capacity))
            chosen[at] = slots[term, 0, block]
            chosen[at + 1] = slots[term, 1, block]
            found = found + (owners[term, block] == ids[0]).astype(jnp.int32)
    for e in range(slots_dev * terms):
        owner = owners[e % terms, ids[0] * slots_dev + e // terms]
        count = seen[owner]
        seen[owner] = count + 1
        place[e] = lax.rem(ids[0] - owner + n_blk, n_blk) * capacity + count
    for e in range(2 * (capacity + 1)):
        mine[e] = 0
    found = jnp.int32(0)
    for e in range(slots_dev * terms):
        block, term = ids[0] * slots_dev + e // terms, e % terms
        at = 2 * jnp.minimum(found, capacity)
        mine[at] = slots[term, 0, block]
        mine[at + 1] = slots[term, 1, block]
        found = found + (owners[term, block] == lax.rem(ids[0] - far + n_blk, n_blk)).astype(jnp.int32)


def make_plan(ids, owners, slots, n_blk, far, slots_dev, terms, capacity):
    scalars = pl.BlockSpec(memory_space=pltpu.SMEM)
    return pl.pallas_call(
        functools.partial(plan_kernel, n_blk, far, slots_dev, terms, capacity),
        in_specs=[scalars] * 3,
        out_specs=[scalars] * 3,
        out_shape=[
            jax.ShapeDtypeStruct((2 * n_blk * (capacity + 1),), jnp.int32),
            jax.ShapeDtypeStruct((slots_dev * terms,), jnp.int32),
            jax.ShapeDtypeStruct((2 * (capacity + 1),), jnp.int32),
        ],
        scratch_shapes=[pltpu.SMEM((n_blk,), jnp.int32)],
        compiler_params=pltpu.CompilerParams(vmem_limit_bytes=mebi),
        name="make_plan",
    )(ids, owners, slots)


def banded_kernel(shifts, capacity, pieces, n_refs, size, ids, chosen, *rest):
    refs, rest = rest[:n_refs], rest[n_refs:]
    out_refs, (left_held, right_held, out_held, sems, out_sems) = rest[: len(shifts)], rest[len(shifts) :]
    halves, _, bands, rows, hidden = left_held.shape
    parts = hidden // size
    at_once = 2 if capacity % 2 == 0 else 1

    def copy(n, source):
        side, half, base, *_ = pieces[n]
        target = (left_held, right_held)[side].at[half, pl.ds(base, refs[source].shape[0])]
        return pltpu.make_async_copy(refs[source], target, sems.at[n])

    for n, (*_, on, off) in enumerate(pieces):
        if on == off:
            copy(n, on).start()
        else:

            @pl.when(ids[3] == 1)
            def _(n=n, on=on):
                copy(n, on).start()

            @pl.when(ids[3] == 0)
            def _(n=n, off=off):
                copy(n, off).start()

    for n, piece in enumerate(pieces):
        copy(n, piece[-1]).wait()

    def leave(n):
        return pltpu.make_async_copy(out_held.at[pl.ds(n * capacity, capacity)], out_refs[n], out_sems.at[n])

    for n, shift in enumerate(shifts):

        def one(turn, carry, n=n, shift=shift):
            group = lane_group((size, hidden), size)
            for term in [turn * at_once + t for t in range(at_once)]:
                at = 2 * (shift * (capacity + 1) + term)
                left_slot, right_slot = chosen[at], chosen[at + 1]
                for band in range(bands):
                    left = jnp.concatenate([left_held[h, left_slot, band] for h in range(halves)], axis=1)
                    apart = []
                    for h in range(halves):
                        right = right_held[h, right_slot, band]
                        apart += [jnp.where(group == part, right, jnp.zeros_like(right)) for part in range(parts)]
                    made = dot(left, jnp.concatenate(apart, axis=0))
                    out_held[n * capacity + term, band] = made.astype(jnp.bfloat16)
            return carry

        lax.fori_loop(0, capacity // at_once, one, 0)
        leave(n).start()
    for n in range(len(shifts)):
        leave(n).wait()


def banded_products(shifts, ids, chosen, operands, capacity, size):
    refs, pieces = [], []

    def index_of(array):
        for n, known in enumerate(refs):
            if known is array:
                return n
        refs.append(array)
        return len(refs) - 1

    slots = 0
    for both in operands:
        for side in range(2):
            for half, (on, off) in enumerate(both[side]):
                pieces.append((side, half, slots, index_of(on), index_of(off)))
        slots += both[0][0][0].shape[0]
    halves = len(operands[0][0])
    _, bands, rows, hidden = operands[0][0][0][0].shape
    count = len(shifts) * capacity
    anywhere = pl.BlockSpec(memory_space=pl.ANY)
    return pl.pallas_call(
        functools.partial(banded_kernel, shifts, capacity, tuple(pieces), len(refs), size),
        grid_spec=pltpu.PrefetchScalarGridSpec(
            num_scalar_prefetch=2,
            grid=(),
            in_specs=[anywhere] * len(refs),
            out_specs=[anywhere] * len(shifts),
            scratch_shapes=[
                pltpu.VMEM((halves, slots, bands, rows, hidden), jnp.bfloat16),
                pltpu.VMEM((halves, slots, bands, size, hidden), jnp.bfloat16),
                pltpu.VMEM((count, bands, rows, hidden), jnp.bfloat16),
                pltpu.SemaphoreType.DMA((len(pieces),)),
                pltpu.SemaphoreType.DMA((len(shifts),)),
            ],
        ),
        out_shape=[jax.ShapeDtypeStruct((capacity, bands, rows, hidden), jnp.bfloat16)] * len(shifts),
        compiler_params=pltpu.CompilerParams(vmem_limit_bytes=14 * mebi),
        cost_estimate=pl.CostEstimate(
            flops=2 * count * bands * rows * hidden * hidden * halves, bytes_accessed=1, transcendentals=0
        ),
        name="banded_products",
    )(ids, chosen, *refs)


def close_kernel(layer, last, spots, chunks, n_chan, n_sub, base, of, terms, capacity, ids, blocks, place, *rest):
    n_parts = len(spots)
    arrived, rest = rest[:n_parts], rest[n_parts:]
    cur_ref, gate_ref, w_out_ref = rest[:3]
    if last:
        out_ref, held, wide_out, sems, swap = rest[3:]
    else:
        chain_ref, w_ref, wide = rest[3:6]
        out_ref, next_gate_ref, sent_ref, *operand_refs, held, wide_out, sems, norm_ref, laid, turned, swap = rest[
            -(2 * chunks + 10) :
        ]
        left_refs, right_refs = operand_refs[:chunks], operand_refs[chunks:]
    step = pl.program_id(0)
    _, rows, cols, channels = cur_ref.shape
    _, bands, _, hidden = held.shape
    parts, size = hidden // bands, bands

    def arrival(n):
        shift, at = spots[n]
        target = held.at[pl.ds(shift * capacity, capacity), pl.ds(at, arrived[n].shape[1])]
        return pltpu.make_async_copy(arrived[n], target, sems.at[n])

    @pl.when(step == 0)
    def _():
        for n in range(n_parts):
            arrival(n).start()
        wide_out[...] = jnp.zeros_like(wide_out)
        for part in range(parts):
            for a in range(parts):
                at = (part * parts + a) * bands
                wide_out[at : at + bands, a * channels : (a + 1) * channels] = w_out_ref[
                    0, part * bands : (part + 1) * bands, :
                ]
        swap[...] = swap_matrix(16)
        for n in range(n_parts):
            arrival(n).wait()

    if not last:
        block = ids[0] * of + base + step
        row_alive = alive_rows(chain_ref, (blocks[0, block] * n_chan + ids[1]) * rows, rows)
        col_alive = alive_rows(chain_ref, (blocks[1, block] * n_sub + ids[2]) * cols, cols)
    half = 16
    by_row = [[] for _ in range(rows)]
    for row in range(0, rows, half):
        for band in range(0, bands, half):
            taken = pl.ds(band, half), pl.ds(row, half)
            total = held[(place[(base + step) * terms], *taken)].astype(jnp.float32)
            for t in range(1, terms):
                total = total + held[(place[(base + step) * terms + t], *taken)].astype(jnp.float32)
            moved = swapped(total.astype(jnp.bfloat16), swap)
            for r in range(half):
                by_row[row + r].append(moved[r])
    groups = rows // parts
    pieces = []
    for g in range(groups):
        block = jnp.concatenate([x for a in range(parts) for x in by_row[g * parts + a]]).T
        pieces.append(jnp.concatenate([block[p * cols : (p + 1) * cols] for p in range(parts)], axis=1))
    mixture = jnp.concatenate(pieces)
    together = (lane_group((hidden, hidden), size) == lax.broadcasted_iota(jnp.int32, (hidden, hidden), 0) // size)
    together = together.astype(jnp.float32).astype(jnp.bfloat16)
    average = dot(mixture, jnp.concatenate([together] * parts)) * (1.0 / hidden)
    centred = [mixture[:, p * hidden : (p + 1) * hidden].astype(jnp.float32) - average for p in range(parts)]
    squares = sum(c * c for c in centred)
    high = squares.astype(jnp.bfloat16)
    low = (squares - high.astype(jnp.float32)).astype(jnp.bfloat16)
    variance = dot(jnp.concatenate([high, low], axis=1), jnp.concatenate([together] * 2)) * (1.0 / hidden)
    scale = lax.rsqrt(variance + norm_epsilon)
    normed = jnp.concatenate([(c * scale).astype(jnp.bfloat16) for c in centred], axis=1)
    update = dot(normed, wide_out[...])
    for g in range(groups):
        taken = pl.ds(g * parts, parts)
        change = jnp.concatenate(
            [update[g * cols : (g + 1) * cols, a * channels : (a + 1) * channels] for a in range(parts)]
        )
        gate = gate_ref[0, taken].reshape(parts * cols, channels)
        current = cur_ref[0, taken].astype(jnp.float32).reshape(parts * cols, channels)
        result = (current + gate * change).astype(jnp.bfloat16)
        out_ref[0, taken] = result.reshape(parts, cols, channels)
        if not last:
            sent_ref[0, taken] = result.reshape(parts, cols, channels)
            norm_and_gate(result, row_alive, col_alive, g * parts, norm_ref, w_ref, next_gate_ref)
    if not last:
        open_layer(layer + 1, norm_ref[...], left_refs, right_refs, wide, laid, turned, swap)


def close_layer(
    layer, arrived, ids, blocks, place, current, gate, w_out, capacity, terms, chains, w_in, wide, last, bands, base, count, earlier
):
    flat, spots = [part for part, *_ in arrived], tuple((shift, at) for _, shift, at in arrived)
    n_blk = lax.axis_size("blk")
    slots, rows, cols, channels = current.shape
    hidden = w_out.shape[1]

    def layer_spec(array, index):
        return pl.BlockSpec((1,) + array.shape[1:], lambda s, *_: (index, 0, 0))

    in_specs = [pl.BlockSpec(memory_space=pl.ANY)] * len(flat)
    in_specs += slot_specs([current, gate], slots, base) + [layer_spec(w_out, layer)]
    operands = [*flat, current, gate, w_out]
    out_shape = [jax.ShapeDtypeStruct(current.shape, jnp.bfloat16)]
    scratch = [
        pltpu.VMEM((n_blk * capacity, sum(bands[layer]), rows, hidden), jnp.bfloat16),
        pltpu.VMEM((hidden // cols * hidden, hidden // cols * channels), jnp.bfloat16),
        pltpu.SemaphoreType.DMA((len(flat),)),
    ]
    if not last:
        operands += [chains, w_in, wide]
        in_specs += [pl.BlockSpec(chains.shape, lambda s, *_: (0, 0)), layer_spec(w_in, layer + 1)]
        in_specs += [pl.BlockSpec(wide.shape, lambda s, *_: (0, 0))]
        out_shape += [jax.ShapeDtypeStruct(current.shape, jnp.float32)]
        out_shape += [jax.ShapeDtypeStruct((count,) + current.shape[1:], jnp.bfloat16)]
        out_shape += operand_outputs(slots, count, cols, hidden, bands[layer + 1])
        scratch += [pltpu.VMEM((rows, cols, channels), jnp.bfloat16)] + operand_scratch(cols, rows, hidden)
    else:
        scratch += [pltpu.VMEM((256, 256), jnp.bfloat16)]
    more, more_specs, aliases = fill(out_shape, earlier, slots, 3 + len(operands))
    return pl.pallas_call(
        functools.partial(
            close_kernel,
            *(layer, last, spots, 0 if last else len(bands[layer + 1]), lax.axis_size("chan"), lax.axis_size("sub")),
            *(base, slots, terms, capacity),
        ),
        grid_spec=pltpu.PrefetchScalarGridSpec(
            num_scalar_prefetch=3,
            grid=(count,),
            in_specs=in_specs + more_specs,
            out_specs=slot_specs(out_shape, slots, base),
            scratch_shapes=scratch,
        ),
        out_shape=out_shape,
        input_output_aliases=aliases,
        compiler_params=pltpu.CompilerParams(vmem_limit_bytes=32 * mebi),
        cost_estimate=pl.CostEstimate(flops=1 << 33, bytes_accessed=1 << 20, transcendentals=0),
        name="close_layer",
    )(ids, blocks, place, *operands, *more)


def after(value, *others):
    return lax.optimization_barrier((value, *others))[0]


def exchange_bands_outgoing(left, right, over):
    both = ("chan", "sub")
    other = lax.ppermute(left, "sub", [(0, 1), (1, 0)])
    one = lax.ppermute(right, both, [(0, 2), (3, 1), (1, 0), (2, 3)])
    two = lax.ppermute(right, both, [(1, 2), (2, 1)])
    return [(other, left), (left, other)], [(one, one), (right, two)]


def exchange_bands_incoming(left, right, over):
    both = ("chan", "sub")
    one = lax.ppermute(left, both, [(1, 3), (2, 0), (0, 1), (3, 2)])
    other = lax.ppermute(right, "chan", [(0, 1), (1, 0)])
    two = lax.ppermute(one if over is None else after(one, over), both, [(0, 1), (3, 2)])
    return [(left, one), (one, two)], [(right, right), (other, other)]


def banded(pair, ids, blocks, owners, slot_of, chains, w_in, w_out, capacity, terms, n_blk):
    slots, rows, cols, channels = pair.shape
    hidden = w_out.shape[1]
    far = n_blk // 2
    near = [s for s in range(1, n_blk) if s != far] + [0]
    layers = w_in.shape[0]
    current = pair
    bands = [[14, 18], [14, 18]]
    chosen, place, mine = make_plan(ids, owners, slot_of, n_blk, far, slots, terms, capacity)
    in_order = jnp.repeat(jnp.arange(capacity, dtype=jnp.int32), 2)
    half = slots // 2
    halves = [(0, half), (half, slots - half)]

    def over_blk(value, shift):
        return lax.ppermute(value, "blk", [(p, (p + shift) % n_blk) for p in range(n_blk)])

    for layer in range(layers):
        count = len(bands[layer])
        if layer == 0:
            raw = [over_blk(pair, far)]
            calls, wide = [None], spread_weights(w_in, 0, cols)
            for base, size in halves:
                calls.append(
                    open_operands(ids, blocks, pair, chains, w_in, wide, hidden, bands[0], base, size, calls[-1])
                )
            gate = calls[-1][0]
        else:
            raw = []
            for call in calls[1:]:
                raw.append(over_blk(after(call[2], *raw) if raw else call[2], far))
        operands = [call[-2 * count :] for call in calls[1:]]
        exchange = exchange_bands_incoming if layer % 2 else exchange_bands_outgoing
        arrived, by_shift = [], {}
        for chunk in range(count):
            if chunk == 0:
                exchanged = []
                over = operands[-1][count]
                for left, right in [(o[0], o[count]) for o in operands]:
                    if exchanged and layer % 2:
                        (_, (one, two)), (_, (other, _)) = exchanged[-1]
                        left, right = lax.optimization_barrier((left, right, one, other))[:2]
                        right = after(right, two)
                    elif exchanged:
                        ((other, _), _), ((one, _), (_, two)) = exchanged[-1]
                        left, right = lax.optimization_barrier((left, right, other, one, two))[:2]
                    exchanged.append(exchange(left, right, over))
            else:
                left, right = operands[-1][chunk], operands[-1][count + chunk]
                if layer % 2:
                    (_, (_, two)), (_, (other, _)) = exchanged[-1]
                    left, right = lax.optimization_barrier((left, right, two, other))[:2]
                else:
                    ((other, _), _), ((one, _), (_, two)) = exchanged[-1]
                    left = after(left, other)
                    right = after(right, one, two, chosen)
                exchanged = [exchange(left, right, by_shift[near[0]])]
                ids = after(ids, *by_shift.values())
            made = banded_products(near, ids, chosen, exchanged, capacity, cols)
            start = sum(bands[layer][:chunk])
            for shift, part in zip(near, made):
                if shift:
                    part = over_blk(after(part, by_shift.get(shift, raw[-1])), shift)
                    by_shift[shift] = part
                arrived.append((part, shift, start))
            if chunk == 0:
                sources = list(lax.optimization_barrier((*raw, made[-1]))[:-1])
                far_left, far_right = far_operands(
                    layer, ids, blocks, mine, sources, chains, wide, far, capacity, slots, hidden
                )
        far_exchanged = [exchange(far_left, far_right, made[-1])]
        (part,) = banded_products([0], ids, in_order, far_exchanged, capacity, cols)
        arrived.append((part, far, 0))
        last = layer == layers - 1
        calls = [None]
        if not last:
            wide = spread_weights(after(w_in, made[-1]), layer + 1, cols)
        for base, size in [(0, slots)] if last else halves:
            calls.append(
                close_layer(
                    *(layer, arrived, ids, blocks, place, current, gate, w_out, capacity, terms, chains, w_in, wide, last),
                    *(bands, base, size, calls[-1]),
                )
            )
        if last:
            return calls[-1][0]
        current, gate = calls[-1][:2]


def per_device(pair, block_list, term_owner, term_slots, chain_ids, w_in, w_out):
    n_blk = lax.axis_size("blk")
    n_chan = lax.axis_size("chan")
    n_sub = lax.axis_size("sub")
    position = lax.axis_index("blk")
    row_group = lax.axis_index("chan")
    col_group = lax.axis_index("sub")
    slots, rows, cols, channels = pair.shape
    hidden = w_out.shape[1]
    terms = term_owner.shape[1]
    capacity = max(2, -(-slots * terms // n_blk))
    fast = n_chan == 2 and n_sub == 2
    on_diagonal = (row_group == col_group).astype(jnp.int32)
    ids = jnp.stack([position, row_group, col_group, on_diagonal]).astype(jnp.int32)
    blocks = block_list.T
    owners = term_owner.T
    slot_of = jnp.transpose(term_slots, (1, 2, 0))
    chains = chain_ids.reshape(-1, 128)
    if fast and n_blk > 1 and rows == cols == 32 and channels == hidden == 128:
        return banded(pair, ids, blocks, owners, slot_of, chains, w_in, w_out, capacity, terms, n_blk)
    shifts = [n_blk // 2] + [s for s in range(1, n_blk) if s != n_blk // 2] + [0]

    def all_products(lefts, right):
        parts = [None] * n_blk
        for shift in shifts:
            made = term_products(shift, ids, owners, slot_of, lefts, right, capacity, slots, terms)
            if shift:
                pairs = [(p, (p + shift) % n_blk) for p in range(n_blk)]
                made = lax.ppermute(made, "blk", pairs)
            parts[shift] = made
        return parts

    def at_home(layer, parts, current, gate, at, of, into=None):
        last = layer == w_in.shape[0] - 1
        return home(
            layer, parts, ids, blocks, owners, current, gate, w_out, capacity, terms, at, of, chains, w_in, last, into
        )

    gate, left, *rights = first_operands(ids, blocks, pair, chains, w_in, hidden, 2 if fast else 1)
    lefts, chunks = exchange_outgoing(left, rights, n_chan, n_sub)
    count = len(chunks)
    made = [all_products(lefts, right) for right in chunks]
    homes = [at_home(0, parts, pair, gate, at, count) for at, parts in enumerate(made)]
    lefts, chunks = exchange_incoming([h[2] for h in homes], [h[3] for h in homes], n_chan, n_sub)
    made = [all_products(lefts, right) for right in chunks]
    out = None
    for at, parts in enumerate(made):
        (out,) = at_home(1, parts, homes[at][0], homes[at][1], at, count, into=out)
    return out


def solution(mesh):
    in_specs = (
        P(("groups", "blk"), "chan", "sub", None),
        P("groups", None),
        P("groups", None),
        P("groups", None, None),
        P("groups"),
        P(),
        P(),
    )
    out_specs = P(("groups", "blk"), "chan", "sub", None)
    return jax.shard_map(
        per_device, mesh=mesh, in_specs=in_specs, out_specs=out_specs, check_vma=False
    )
```

```python
import functools

import jax
import jax.numpy as jnp
from jax import lax
from jax.experimental import pallas as pl
from jax.experimental.pallas import tpu as pltpu
from jax.sharding import PartitionSpec as P

norm_epsilon = 1e-05
mebi = 1024 * 1024
vmem_limit = 56 * mebi


def sigmoid(values):
    return 0.5 + 0.5 * jnp.tanh(0.5 * values)


def layer_norm(values):
    values = values.astype(jnp.float32)
    centred = values - jnp.mean(values, axis=-1, keepdims=True)
    variance = jnp.mean(centred * centred, axis=-1, keepdims=True)
    return centred * lax.rsqrt(variance + norm_epsilon)


def alive_rows(chain_ref, start, size):
    lanes = chain_ref.shape[1]
    line = chain_ref[pl.ds(start // lanes, 1), :] >= 0
    spot = lax.broadcasted_iota(jnp.int32, (size, lanes), 0) + lax.rem(start, lanes)
    pick = jnp.logical_and(lax.broadcasted_iota(jnp.int32, (size, lanes), 1) == spot, line)
    return dot(pick.astype(jnp.float32).astype(jnp.bfloat16), jnp.ones((lanes, lanes), jnp.bfloat16))


def dot(a, b):
    return jnp.dot(a, b, preferred_element_type=jnp.float32)


def gated_pair(projected, mask, hidden):
    left = mask * sigmoid(projected[:, hidden : 2 * hidden]) * projected[:, :hidden]
    right = mask * sigmoid(projected[:, 3 * hidden : 4 * hidden]) * projected[:, 2 * hidden : 3 * hidden]
    return left.astype(jnp.bfloat16), right.astype(jnp.bfloat16)


def first_kernel(hidden, row_parts, n_chan, n_sub, ids, blocks, pair_ref, chain_ref, w_ref, gate_ref, left_ref, *rest):
    right_refs, (norm_ref, turned_ref) = rest[:row_parts], rest[row_parts:]
    slots = pl.num_programs(0)
    _, rows, cols, channels = pair_ref.shape
    block = ids[0] * slots + pl.program_id(0)
    row_alive = alive_rows(chain_ref, (blocks[0, block] * n_chan + ids[1]) * rows, rows)
    col_alive = alive_rows(chain_ref, (blocks[1, block] * n_sub + ids[2]) * cols, cols)
    group = max(1, 256 // cols)
    for start in range(0, rows, group):
        at = pl.ds(start, group)
        normed = layer_norm(pair_ref[0, at].reshape(group * cols, channels))
        norm_ref[pl.ds(start * cols, group * cols), :] = normed
        gate = sigmoid(dot(normed.astype(jnp.bfloat16), w_ref[0, :, 4 * hidden :]))
        gate_ref[0, at] = gate.reshape(group, cols, channels)
    for col in range(cols):
        turned_ref[col] = norm_ref[pl.ds(col, rows, stride=cols), :].astype(jnp.bfloat16)
    step = max(1, 128 // rows)
    part = rows // row_parts
    for start in range(0, cols, step):
        taken = turned_ref[start : start + step].reshape(step * rows, channels)
        projected = dot(taken, w_ref[0, :, : 4 * hidden])
        mask = col_alive[start : start + step][:, None, :] * row_alive[None, :, :]
        left, right = gated_pair(projected, mask.reshape(step * rows, -1), hidden)
        left_ref[0, start : start + step] = left.reshape(step, rows, hidden)
        right = right.reshape(step, rows, hidden)
        for p, right_ref in enumerate(right_refs):
            right_ref[0, start : start + step] = right[:, p * part : (p + 1) * part]


def first_operands(ids, blocks, pair, chains, w_in, hidden, row_parts):
    slots, rows, cols, channels = pair.shape
    part = rows // row_parts
    operand = jax.ShapeDtypeStruct((slots, cols, rows, hidden), jnp.bfloat16)
    right = jax.ShapeDtypeStruct((slots, cols, part, hidden), jnp.bfloat16)
    return pl.pallas_call(
        functools.partial(first_kernel, hidden, row_parts, lax.axis_size("chan"), lax.axis_size("sub")),
        grid_spec=pltpu.PrefetchScalarGridSpec(
            num_scalar_prefetch=2,
            grid=(slots,),
            in_specs=[
                pl.BlockSpec((1, rows, cols, channels), lambda s, *_: (s, 0, 0, 0)),
                pl.BlockSpec(chains.shape, lambda s, *_: (0, 0)),
                pl.BlockSpec((1,) + w_in.shape[1:], lambda s, *_: (0, 0, 0)),
            ],
            out_specs=[
                pl.BlockSpec((1, rows, cols, channels), lambda s, *_: (s, 0, 0, 0)),
                pl.BlockSpec((1, cols, rows, hidden), lambda s, *_: (s, 0, 0, 0)),
            ]
            + [pl.BlockSpec((1, cols, part, hidden), lambda s, *_: (s, 0, 0, 0))] * row_parts,
            scratch_shapes=[
                pltpu.VMEM((rows * cols, channels), jnp.float32),
                pltpu.VMEM((cols, rows, channels), jnp.bfloat16),
            ],
        ),
        out_shape=[jax.ShapeDtypeStruct(pair.shape, jnp.float32), operand] + [right] * row_parts,
        compiler_params=pltpu.CompilerParams(vmem_limit_bytes=vmem_limit),
        name="first_operands",
    )(ids, blocks, pair, chains, w_in)


def product_kernel(shift, n_blk, slots_dev, terms, capacity, pieces, n_refs, ids, owners, slots, *rest):
    refs = rest[:n_refs]
    out_ref, left_held, right_held, right_wide, chosen, sems = rest[n_refs:]
    step = pl.program_id(0)
    turn = lax.rem(step, 2)
    _, depth, n_i, hidden = left_held.shape
    n_j = right_wide.shape[1]

    @pl.when(step == 0)
    def _():
        target = lax.rem(ids[0] + shift, n_blk)
        for e in range(2 * capacity):
            chosen[e] = 0

        def scan(e, count):
            block, term = target * slots_dev + e // terms, lax.rem(e, terms)
            here = jnp.logical_and(owners[term, block] == ids[0], count < capacity)

            @pl.when(here)
            def _():
                chosen[2 * count] = slots[term, 0, block]
                chosen[2 * count + 1] = slots[term, 1, block]

            return count + here.astype(jnp.int32)

        lax.fori_loop(0, slots_dev * terms, scan, jnp.int32(0))

    def copy(n, term, buffer, source):
        side, _, _, k0, depth_of, i0, size = pieces[n]
        held = (left_held, right_held)[side]
        return pltpu.make_async_copy(
            refs[source].at[chosen[2 * term + side]],
            held.at[buffer, pl.ds(k0, depth_of), pl.ds(i0, size), :],
            sems.at[buffer, n],
        )

    def start(term, buffer):
        for n, (_, on, off, *_) in enumerate(pieces):
            if on == off:
                copy(n, term, buffer, on).start()
            else:

                @pl.when(ids[3] == 1)
                def _(n=n, on=on):
                    copy(n, term, buffer, on).start()

                @pl.when(ids[3] == 0)
                def _(n=n, off=off):
                    copy(n, term, buffer, off).start()

    @pl.when(step == 0)
    def _():
        start(0, 0)

    @pl.when(step + 1 < capacity)
    def _():
        start(step + 1, 1 - turn)

    for n, piece in enumerate(pieces):
        copy(n, step, turn, piece[1]).wait()

    span = 8

    def widen(n, carry):
        at = pl.ds(n * span, span)
        right_wide[at] = right_held[turn, at].astype(jnp.float32)
        return carry

    lax.fori_loop(0, depth // span, widen, 0)

    group = min(8, n_j)
    unroll = 4
    for j0 in range(0, n_j, group):

        def body(n, sums):
            for u in range(unroll):
                k = n * unroll + u
                left = left_held[turn, k].astype(jnp.float32).reshape(n_i // 8, 8, hidden)
                sums = tuple(
                    total + left * right_wide[k, pl.ds(j0 + j, 8, stride=0), :][None]
                    for j, total in enumerate(sums)
                )
            return sums

        zero = jnp.zeros((n_i // 8, 8, hidden), jnp.float32)
        sums = lax.fori_loop(0, depth // unroll, body, (zero,) * group)
        for j, total in enumerate(sums):
            out_ref[0, j0 + j] = total.reshape(n_i, hidden).astype(jnp.bfloat16)


def term_products(shift, ids, owners, slots, lefts, rights, capacity, slots_dev, terms):
    n_blk = lax.axis_size("blk")
    refs, pieces = [], []

    def index_of(array):
        for n, known in enumerate(refs):
            if known is array:
                return n
        refs.append(array)
        return len(refs) - 1

    for side, operands in ((0, lefts), (1, rights)):
        for on, off, k0, i0 in operands:
            pieces.append((side, index_of(on), index_of(off), k0, on.shape[1], i0, on.shape[2]))
    hidden = lefts[0][0].shape[3]
    n_i = max(p[5] + p[6] for p in pieces if p[0] == 0)
    n_j = max(p[5] + p[6] for p in pieces if p[0] == 1)
    depth = max(p[3] + p[4] for p in pieces)
    return pl.pallas_call(
        functools.partial(
            product_kernel, shift, n_blk, slots_dev, terms, capacity, tuple(pieces), len(refs)
        ),
        grid_spec=pltpu.PrefetchScalarGridSpec(
            num_scalar_prefetch=3,
            grid=(capacity,),
            in_specs=[pl.BlockSpec(memory_space=pl.ANY)] * len(refs),
            out_specs=pl.BlockSpec((1, n_j, n_i, hidden), lambda t, *_: (t, 0, 0, 0)),
            scratch_shapes=[
                pltpu.VMEM((2, depth, n_i, hidden), jnp.bfloat16),
                pltpu.VMEM((2, depth, n_j, hidden), jnp.bfloat16),
                pltpu.VMEM((depth, n_j, hidden), jnp.float32),
                pltpu.SMEM((2 * capacity,), jnp.int32),
                pltpu.SemaphoreType.DMA((2, len(pieces))),
            ],
        ),
        out_shape=jax.ShapeDtypeStruct((capacity, n_j, n_i, hidden), jnp.bfloat16),
        compiler_params=pltpu.CompilerParams(vmem_limit_bytes=vmem_limit),
        cost_estimate=pl.CostEstimate(
            flops=2 * capacity * n_i * n_j * depth * hidden * 100,
            bytes_accessed=capacity * (depth * (n_i + n_j) + n_i * n_j) * hidden * 2,
            transcendentals=0,
        ),
        name="term_products",
    )(ids, owners, slots, *refs)


def home_kernel(last, hidden, n_blk, n_chan, n_sub, at, of, slots_dev, terms, capacity, ids, blocks, owners, *rest):
    parts, rest = rest[:n_blk], rest[n_blk:]
    scratch, rest = rest[-5:], rest[:-5]
    held, turned, place, seen, sems = scratch
    cur_ref, gate_ref, w_out_ref = rest[:3]
    if last:
        out_ref = rest[-1]
    else:
        chain_ref, w_ref, out_ref, next_gate_ref, left_ref, right_ref = rest[3:]
    step = pl.program_id(0)
    _, rows, cols, channels = cur_ref.shape

    def arrival(shift):
        return pltpu.make_async_copy(parts[shift], held.at[pl.ds(shift * capacity, capacity)], sems.at[shift])

    @pl.when(step == 0)
    def _():
        for shift in range(n_blk):
            arrival(shift).start()
            seen[shift] = 0

        def scan(e, carry):
            owner = owners[lax.rem(e, terms), ids[0] * slots_dev + e // terms]
            shift = lax.rem(ids[0] - owner + n_blk, n_blk)
            count = seen[owner]
            seen[owner] = count + 1
            place[e] = shift * capacity + count
            return carry

        lax.fori_loop(0, slots_dev * terms, scan, jnp.int32(0))
        for shift in range(n_blk):
            arrival(shift).wait()

    if not last:
        block = ids[0] * slots_dev + step
        row_alive = alive_rows(chain_ref, (blocks[0, block] * n_chan + ids[1]) * rows, rows)
        col_alive = alive_rows(chain_ref, ((blocks[1, block] * n_sub + ids[2]) * of + at) * cols, cols)
    span = max(1, 128 // rows)
    for start in range(0, cols, span):
        taken = pl.ds(start, span)
        total = held[place[step * terms], taken].astype(jnp.float32)
        for t in range(1, terms):
            total = total + held[place[step * terms + t], taken].astype(jnp.float32)
        rounded = total.astype(jnp.bfloat16).astype(jnp.float32)
        turned[pl.ds(start * rows, span * rows), :] = rounded.reshape(span * rows, hidden)
    group = min(rows, max(1, 256 // cols))
    for start in range(0, rows, group):
        taken = pl.ds(start, group)
        mixture = jnp.concatenate(
            [turned[pl.ds(row, cols, stride=rows), :].astype(jnp.bfloat16) for row in range(start, start + group)]
        )
        update = dot(layer_norm(mixture).astype(jnp.bfloat16), w_out_ref[0])
        current = cur_ref[0, taken].astype(jnp.float32).reshape(group * cols, channels)
        gate = gate_ref[0, taken].reshape(group * cols, channels)
        result = (current + gate * update).astype(jnp.bfloat16)
        out_ref[0, taken] = result.reshape(group, cols, channels)
        if not last:
            normed = layer_norm(result).astype(jnp.bfloat16)
            projected = dot(normed, w_ref[0])
            next_gate_ref[0, taken] = sigmoid(projected[:, 4 * hidden :]).reshape(group, cols, channels)
            mask = row_alive[start : start + group][:, None, :] * col_alive[None, :, :]
            left, right = gated_pair(projected, mask.reshape(group * cols, channels), hidden)
            left_ref[0, taken] = left.reshape(group, cols, hidden)
            right_ref[0, taken] = right.reshape(group, cols, hidden)


def home(layer, parts, ids, blocks, owners, current, gate, w_out, capacity, terms, at, of, chains, w_in, last, into=None):
    n_blk = len(parts)
    slots, rows, _, channels = current.shape
    hidden = w_out.shape[1]
    cols = parts[0].shape[1]
    chunk = (1, rows, cols, channels)

    def chunk_spec(array):
        whole = array.shape[2] != cols
        return pl.BlockSpec(chunk, lambda s, *_: (s, 0, at if whole else 0, 0))

    def layer_spec(array, index):
        return pl.BlockSpec((1,) + array.shape[1:], lambda s, *_: (index, 0, 0))

    in_specs = [pl.BlockSpec(memory_space=pl.ANY)] * n_blk + [
        chunk_spec(current),
        chunk_spec(gate),
        layer_spec(w_out, layer),
    ]
    operands = [*parts, current, gate, w_out]
    aliases = {}
    if last:
        if into is not None:
            aliases = {3 + len(operands): 0}
            operands.append(into)
            in_specs.append(pl.BlockSpec(memory_space=pl.ANY))
        out_shape = [jax.ShapeDtypeStruct((slots, rows, cols * of, channels), jnp.bfloat16)]
        out_specs = [pl.BlockSpec(chunk, lambda s, *_: (s, 0, at, 0))]
    else:
        operands += [chains, w_in]
        in_specs += [pl.BlockSpec(chains.shape, lambda s, *_: (0, 0)), layer_spec(w_in, layer + 1)]
        small = (slots, rows, cols, channels)
        out_shape = [jax.ShapeDtypeStruct(small, t) for t in (jnp.bfloat16, jnp.float32, jnp.bfloat16, jnp.bfloat16)]
        out_specs = [pl.BlockSpec(chunk, lambda s, *_: (s, 0, 0, 0))] * 4
    return pl.pallas_call(
        functools.partial(
            home_kernel, last, hidden, n_blk, lax.axis_size("chan"), lax.axis_size("sub"), at, of, slots, terms, capacity
        ),
        grid_spec=pltpu.PrefetchScalarGridSpec(
            num_scalar_prefetch=3,
            grid=(slots,),
            in_specs=in_specs,
            out_specs=out_specs,
            scratch_shapes=[
                pltpu.VMEM((n_blk * capacity, cols, rows, hidden), jnp.bfloat16),
                pltpu.VMEM((rows * cols, hidden), jnp.float32),
                pltpu.SMEM((slots * terms,), jnp.int32),
                pltpu.SMEM((n_blk,), jnp.int32),
                pltpu.SemaphoreType.DMA((n_blk,)),
            ],
        ),
        out_shape=out_shape,
        input_output_aliases=aliases,
        compiler_params=pltpu.CompilerParams(vmem_limit_bytes=vmem_limit),
        cost_estimate=pl.CostEstimate(
            flops=2 * slots * rows * cols * channels * 6 * channels * 10,
            bytes_accessed=slots * rows * cols * channels * 16,
            transcendentals=0,
        ),
        name="home",
    )(ids, blocks, owners, *operands)


def exchange_outgoing(left, rights, n_chan, n_sub):
    if n_chan == 2 and n_sub == 2:
        both = ("chan", "sub")
        other_left = lax.ppermute(left, "sub", [(0, 1), (1, 0)])
        lefts = [(other_left, left, 0, 0), (left, other_left, left.shape[1], 0)]
        chunks = []
        for right in rights:
            if chunks:
                (one, *_), (_, two, *_) = chunks[-1]
                right, *_ = lax.optimization_barrier((right, one, two))
            one = lax.ppermute(right, both, [(0, 2), (3, 1), (1, 0), (2, 3)])
            two = lax.ppermute(right, both, [(1, 2), (2, 1)])
            chunks.append([(one, one, 0, 0), (right, two, right.shape[1], 0)])
        return lefts, chunks
    left = lax.all_gather(left, "sub", axis=1, tiled=True)
    right = jnp.concatenate(rights, axis=2)
    right = lax.all_gather(right, "chan", axis=2, tiled=True)
    right = lax.all_to_all(right, "sub", split_axis=2, concat_axis=1, tiled=True)
    cols = right.shape[2] // 2
    chunks = [right[:, :, :cols], right[:, :, cols:]]
    return [(left, left, 0, 0)], [[(r, r, 0, 0)] for r in chunks]


def exchange_incoming(lefts, rights, n_chan, n_sub):
    if n_chan == 2 and n_sub == 2:
        both = ("chan", "sub")
        left_pieces, chunks = [], []
        at = 0
        for left, right in zip(lefts, rights):
            depth = left.shape[1]
            one = lax.ppermute(left, both, [(1, 3), (2, 0), (0, 1), (3, 2)])
            two = lax.ppermute(one, both, [(0, 1), (3, 2)])
            left_pieces += [(left, one, 0, at), (one, two, depth, at)]
            other = lax.ppermute(right, "chan", [(0, 1), (1, 0)])
            chunks.append([(right, right, 0, 0), (other, other, depth, 0)])
            at += left.shape[2]
        return left_pieces, chunks
    left = lax.all_gather(jnp.concatenate(lefts, axis=2), "chan", axis=1, tiled=True)
    left = lax.all_gather(left, "sub", axis=2, tiled=True)
    size = left.shape[2] // n_chan
    left = lax.dynamic_slice_in_dim(left, lax.axis_index("chan") * size, size, 2)
    gathered = [lax.all_gather(right, "chan", axis=1, tiled=True) for right in rights]
    return [(left, left, 0, 0)], [[(r, r, 0, 0)] for r in gathered]


def lane_group(shape, size):
    return lax.broadcasted_iota(jnp.int32, shape, 1) // size


def spread_kernel(size, w_ref, wide_ref):
    hidden = w_ref.shape[1]
    parts = hidden // size
    for side in range(2):
        for kind in range(2):
            start = (2 * side + kind) * hidden
            weights = 0.5 * w_ref[0, :, start : start + hidden].astype(jnp.float32)
            group = lane_group(weights.shape, size)
            for part in range(parts):
                kept = jnp.where(group == part, weights, 0.0)
                at = ((side * parts + part) * 2 + kind) * hidden
                for a in range(parts):
                    moved = pltpu.roll(kept, ((a - part) % parts) * size, 1) if a != part else kept
                    wide_ref[a * hidden : (a + 1) * hidden, at : at + hidden] = moved.astype(jnp.bfloat16)


def spread_weights(w_in, layer, size):
    hidden = w_in.shape[1]
    parts = hidden // size
    shape = (parts * hidden, 4 * parts * hidden)
    return pl.pallas_call(
        functools.partial(spread_kernel, size),
        grid=(1,),
        in_specs=[pl.BlockSpec((1,) + w_in.shape[1:], lambda s: (layer, 0, 0))],
        out_specs=pl.BlockSpec(shape, lambda s: (0, 0)),
        out_shape=jax.ShapeDtypeStruct(shape, jnp.bfloat16),
        compiler_params=pltpu.CompilerParams(vmem_limit_bytes=16 * mebi),
        cost_estimate=pl.CostEstimate(flops=1 << 30, bytes_accessed=1 << 20, transcendentals=0),
        name="spread_weights",
    )(w_in)


def swap_matrix(half):
    shape = (half * half, half * half)
    to, of = lax.broadcasted_iota(jnp.int32, shape, 0), lax.broadcasted_iota(jnp.int32, shape, 1)
    same = jnp.logical_and(to // half == lax.rem(of, half), lax.rem(to, half) == of // half)
    return same.astype(jnp.float32).astype(jnp.bfloat16)


def swapped(values, swap_ref):
    half, _, lanes = values.shape
    moved = dot(swap_ref[...], values.reshape(half * half, lanes))
    return moved.astype(jnp.bfloat16).reshape(half, half, lanes)


def turn(taken, turned, swap_ref):
    half = 16
    for x in range(0, taken.shape[0], half):
        for y in range(0, taken.shape[1], half):
            turned[y : y + half, x : x + half] = swapped(taken[x : x + half, y : y + half], swap_ref)


def make_operand(side, taken, wide_ref, out_refs, laid, swap_ref):
    rows, size, hidden = taken.shape
    parts, bands, half = hidden // size, size, 16
    groups = rows // parts
    stacked = jnp.concatenate(
        [jnp.concatenate([taken[g * parts + a] for a in range(parts)], axis=1) for g in range(groups)], axis=0
    )
    for part in range(parts):
        at = (side * parts + part) * 2 * hidden
        made = dot(stacked, wide_ref[:, at : at + 2 * hidden])
        value = made[:, :hidden] * (1.0 + jnp.tanh(made[:, hidden:]))
        laid[side, :, part * size : (part + 1) * size, :] = value.astype(jnp.bfloat16).reshape(groups, size, hidden)
    blocks = [laid[side, g].T for g in range(groups)]
    starts = [sum(ref.shape[1] for ref in out_refs[:n]) for n in range(len(out_refs))]
    for first in range(0, bands, half):
        for row in range(0, rows, half):
            tiles = []
            for r in range(row, row + half):
                at = r % parts * bands + first
                tiles.append(blocks[r // parts][at : at + half])
            moved = swapped(jnp.stack(tiles), swap_ref)
            for start, ref in zip(starts, out_refs):
                low, high = max(start, first), min(start + ref.shape[1], first + half)
                if low < high:
                    ref[0, low - start : high - start, row : row + half] = moved[low - first : high - first]


def open_layer(layer, natural, left_refs, right_refs, wide, laid, turned, swap):
    turn(natural, turned, swap)
    for side, refs in ((0, left_refs), (1, right_refs)):
        make_operand(side, natural if side == layer % 2 else turned[...], wide, refs, laid, swap)


def norm_and_gate(values, row_alive, col_alive, at, norm_ref, w_ref=None, gate_ref=None):
    _, cols, channels = norm_ref.shape
    rows = values.shape[0] // cols
    normed = layer_norm(values)
    if gate_ref is not None:
        gate = sigmoid(dot(normed.astype(jnp.bfloat16), w_ref[0, :, -channels:]))
        gate_ref[0, pl.ds(at, rows)] = gate.reshape(rows, cols, channels)
    mask = row_alive[at : at + rows, None, :] * col_alive[None, :, :]
    norm_ref[pl.ds(at, rows)] = (normed.reshape(rows, cols, channels) * mask).astype(jnp.bfloat16)


def open_kernel(hidden, chunks, n_chan, n_sub, base, of, ids, blocks, pair_ref, chain_ref, w_ref, wide, *rest):
    gate_ref, *operand_refs, norm_ref, laid, turned, swap = rest[-(2 * chunks + 5) :]
    step = pl.program_id(0)
    _, rows, cols, channels = pair_ref.shape
    block = ids[0] * of + base + step

    @pl.when(step == 0)
    def _():
        swap[...] = swap_matrix(16)

    row_alive = alive_rows(chain_ref, (blocks[0, block] * n_chan + ids[1]) * rows, rows)
    col_alive = alive_rows(chain_ref, (blocks[1, block] * n_sub + ids[2]) * cols, cols)
    group = hidden // cols
    for at in range(0, rows, group):
        values = pair_ref[0, pl.ds(at, group)].reshape(group * cols, channels)
        norm_and_gate(values, row_alive, col_alive, at, norm_ref, w_ref, gate_ref)
    open_layer(0, norm_ref[...], operand_refs[:chunks], operand_refs[chunks:], wide, laid, turned, swap)


def operand_scratch(rows, size, hidden):
    parts = hidden // size
    return [
        pltpu.VMEM((2, rows // parts, parts * size, hidden), jnp.bfloat16),
        pltpu.VMEM((size, rows, hidden), jnp.bfloat16),
        pltpu.VMEM((256, 256), jnp.bfloat16),
    ]


def operand_outputs(slots, count, rows, hidden, bands):
    kept = [count if n == 0 else slots for n in range(len(bands))] * 2
    return [jax.ShapeDtypeStruct((k, b, rows, hidden), jnp.bfloat16) for k, b in zip(kept, bands * 2)]


def slot_specs(arrays, slots, base):
    def spec(array):
        offset = base if array.shape[0] == slots else 0
        return pl.BlockSpec((1,) + array.shape[1:], lambda s, *_: (s + offset, 0, 0, 0))

    return [spec(a) for a in arrays]


def fill(out_shape, earlier, slots, n_before):
    if earlier is None:
        return [], [], {}
    shared = [n for n, o in enumerate(out_shape) if o.shape[0] == slots]
    specs = [pl.BlockSpec(memory_space=pl.ANY)] * len(shared)
    return [earlier[n] for n in shared], specs, {n_before + k: n for k, n in enumerate(shared)}


def open_operands(ids, blocks, pair, chains, w_in, wide, hidden, bands, base, count, earlier):
    slots, rows, cols, channels = pair.shape
    out_shape = [jax.ShapeDtypeStruct(pair.shape, jnp.float32)] + operand_outputs(slots, count, rows, hidden, bands)
    more, more_specs, aliases = fill(out_shape, earlier, slots, 6)
    return pl.pallas_call(
        functools.partial(open_kernel, hidden, len(bands), lax.axis_size("chan"), lax.axis_size("sub"), base, slots),
        grid_spec=pltpu.PrefetchScalarGridSpec(
            num_scalar_prefetch=2,
            grid=(count,),
            in_specs=slot_specs([pair], slots, base)
            + [
                pl.BlockSpec(chains.shape, lambda s, *_: (0, 0)),
                pl.BlockSpec((1,) + w_in.shape[1:], lambda s, *_: (0, 0, 0)),
                pl.BlockSpec(wide.shape, lambda s, *_: (0, 0)),
            ]
            + more_specs,
            out_specs=slot_specs(out_shape, slots, base),
            scratch_shapes=[pltpu.VMEM((rows, cols, channels), jnp.bfloat16)] + operand_scratch(rows, cols, hidden),
        ),
        out_shape=out_shape,
        input_output_aliases=aliases,
        compiler_params=pltpu.CompilerParams(vmem_limit_bytes=18 * mebi),
        cost_estimate=pl.CostEstimate(flops=1 << 33, bytes_accessed=1 << 20, transcendentals=0),
        name="open_operands",
    )(ids, blocks, pair, chains, w_in, wide, *more)


def far_kernel(layer, n_blk, far, n_chan, n_sub, of, bases, ids, blocks, mine, *rest):
    sources, (chain_ref, wide, left_ref, right_ref, norm_ref, laid, turned, swap) = rest[:-8], rest[-8:]
    step = pl.program_id(0)
    rows, cols, channels = norm_ref.shape
    holder = lax.rem(ids[0] - far + n_blk, n_blk)

    @pl.when(step == 0)
    def _():
        swap[...] = swap_matrix(16)

    group = channels // cols
    for side, out_ref in ((0, left_ref), (1, right_ref)):
        slot = mine[2 * step + side]
        refs = sources[side * len(bases) : (side + 1) * len(bases)]
        block = holder * of + slot
        row_alive = alive_rows(chain_ref, (blocks[0, block] * n_chan + ids[1]) * rows, rows)
        col_alive = alive_rows(chain_ref, (blocks[1, block] * n_sub + ids[2]) * cols, cols)
        for at in range(0, rows, group):
            values = refs[0][0, pl.ds(at, group)]
            for base, ref in zip(bases[1:], refs[1:]):
                values = jnp.where(slot >= base, ref[0, pl.ds(at, group)], values)
            norm_and_gate(values.reshape(group * cols, channels), row_alive, col_alive, at, norm_ref)
        if side == layer % 2:
            make_operand(side, norm_ref[...], wide, [out_ref], laid, swap)
        else:
            turn(norm_ref[...], turned, swap)
            make_operand(side, turned[...], wide, [out_ref], laid, swap)


def far_operands(layer, ids, blocks, mine, sources, chains, wide, far, capacity, of, hidden):
    n_blk = lax.axis_size("blk")
    _, rows, cols, channels = sources[0].shape
    bases = [sum(a.shape[0] for a in sources[:n]) for n in range(len(sources))]

    def source_spec(side, base, size):
        def place(t, ids, blocks, mine):
            return jnp.clip(mine[2 * t + side] - base, 0, size - 1), 0, 0, 0

        return pl.BlockSpec((1, rows, cols, channels), place)

    in_specs = [source_spec(side, b, a.shape[0]) for side in range(2) for b, a in zip(bases, sources)]
    in_specs += [pl.BlockSpec(chains.shape, lambda t, *_: (0, 0)), pl.BlockSpec(wide.shape, lambda t, *_: (0, 0))]
    shape = (capacity, hidden // (hidden // cols), rows, hidden)
    return pl.pallas_call(
        functools.partial(
            far_kernel, layer, n_blk, far, lax.axis_size("chan"), lax.axis_size("sub"), of, tuple(bases)
        ),
        grid_spec=pltpu.PrefetchScalarGridSpec(
            num_scalar_prefetch=3,
            grid=(capacity,),
            in_specs=in_specs,
            out_specs=[pl.BlockSpec((1,) + shape[1:], lambda t, *_: (t, 0, 0, 0))] * 2,
            scratch_shapes=[pltpu.VMEM((rows, cols, channels), jnp.bfloat16)] + operand_scratch(rows, cols, hidden),
        ),
        out_shape=[jax.ShapeDtypeStruct(shape, jnp.bfloat16)] * 2,
        compiler_params=pltpu.CompilerParams(vmem_limit_bytes=14 * mebi),
        cost_estimate=pl.CostEstimate(flops=1 << 33, bytes_accessed=1 << 20, transcendentals=0),
        name="far_operands",
    )(ids, blocks, mine, *sources, *sources, chains, wide)


def plan_kernel(n_blk, far, slots_dev, terms, capacity, ids, owners, slots, chosen, place, mine, seen):
    for shift in range(n_blk):
        seen[shift] = 0
        target = lax.rem(ids[0] + shift, n_blk)
        for e in range(2 * (capacity + 1)):
            chosen[2 * shift * (capacity + 1) + e] = 0
        found = jnp.int32(0)
        for e in range(slots_dev * terms):
            block, term = target * slots_dev + e // terms, e % terms
            at = 2 * (shift * (capacity + 1) + jnp.minimum(found, capacity))
            chosen[at] = slots[term, 0, block]
            chosen[at + 1] = slots[term, 1, block]
            found = found + (owners[term, block] == ids[0]).astype(jnp.int32)
    for e in range(slots_dev * terms):
        owner = owners[e % terms, ids[0] * slots_dev + e // terms]
        count = seen[owner]
        seen[owner] = count + 1
        place[e] = lax.rem(ids[0] - owner + n_blk, n_blk) * capacity + count
    for e in range(2 * (capacity + 1)):
        mine[e] = 0
    found = jnp.int32(0)
    for e in range(slots_dev * terms):
        block, term = ids[0] * slots_dev + e // terms, e % terms
        at = 2 * jnp.minimum(found, capacity)
        mine[at] = slots[term, 0, block]
        mine[at + 1] = slots[term, 1, block]
        found = found + (owners[term, block] == lax.rem(ids[0] - far + n_blk, n_blk)).astype(jnp.int32)


def make_plan(ids, owners, slots, n_blk, far, slots_dev, terms, capacity):
    scalars = pl.BlockSpec(memory_space=pltpu.SMEM)
    return pl.pallas_call(
        functools.partial(plan_kernel, n_blk, far, slots_dev, terms, capacity),
        in_specs=[scalars] * 3,
        out_specs=[scalars] * 3,
        out_shape=[
            jax.ShapeDtypeStruct((2 * n_blk * (capacity + 1),), jnp.int32),
            jax.ShapeDtypeStruct((slots_dev * terms,), jnp.int32),
            jax.ShapeDtypeStruct((2 * (capacity + 1),), jnp.int32),
        ],
        scratch_shapes=[pltpu.SMEM((n_blk,), jnp.int32)],
        compiler_params=pltpu.CompilerParams(vmem_limit_bytes=mebi),
        name="make_plan",
    )(ids, owners, slots)


def banded_kernel(shifts, capacity, pieces, n_refs, size, ids, chosen, *rest):
    refs, rest = rest[:n_refs], rest[n_refs:]
    out_refs, (left_held, right_held, out_held, sems, out_sems) = rest[: len(shifts)], rest[len(shifts) :]
    halves, _, bands, rows, hidden = left_held.shape
    parts = hidden // size
    at_once = 2 if capacity % 2 == 0 else 1

    def copy(n, source):
        side, half, base, *_ = pieces[n]
        target = (left_held, right_held)[side].at[half, pl.ds(base, refs[source].shape[0])]
        return pltpu.make_async_copy(refs[source], target, sems.at[n])

    for n, (*_, on, off) in enumerate(pieces):
        if on == off:
            copy(n, on).start()
        else:

            @pl.when(ids[3] == 1)
            def _(n=n, on=on):
                copy(n, on).start()

            @pl.when(ids[3] == 0)
            def _(n=n, off=off):
                copy(n, off).start()

    for n, piece in enumerate(pieces):
        copy(n, piece[-1]).wait()

    def leave(n):
        return pltpu.make_async_copy(out_held.at[pl.ds(n * capacity, capacity)], out_refs[n], out_sems.at[n])

    for n, shift in enumerate(shifts):

        def one(turn, carry, n=n, shift=shift):
            group = lane_group((size, hidden), size)
            for term in [turn * at_once + t for t in range(at_once)]:
                at = 2 * (shift * (capacity + 1) + term)
                left_slot, right_slot = chosen[at], chosen[at + 1]
                for band in range(bands):
                    left = jnp.concatenate([left_held[h, left_slot, band] for h in range(halves)], axis=1)
                    apart = []
                    for h in range(halves):
                        right = right_held[h, right_slot, band]
                        apart += [jnp.where(group == part, right, jnp.zeros_like(right)) for part in range(parts)]
                    made = dot(left, jnp.concatenate(apart, axis=0))
                    out_held[n * capacity + term, band] = made.astype(jnp.bfloat16)
            return carry

        lax.fori_loop(0, capacity // at_once, one, 0)
        leave(n).start()
    for n in range(len(shifts)):
        leave(n).wait()


def banded_products(shifts, ids, chosen, operands, capacity, size):
    refs, pieces = [], []

    def index_of(array):
        for n, known in enumerate(refs):
            if known is array:
                return n
        refs.append(array)
        return len(refs) - 1

    slots = 0
    for both in operands:
        for side in range(2):
            for half, (on, off) in enumerate(both[side]):
                pieces.append((side, half, slots, index_of(on), index_of(off)))
        slots += both[0][0][0].shape[0]
    halves = len(operands[0][0])
    _, bands, rows, hidden = operands[0][0][0][0].shape
    count = len(shifts) * capacity
    anywhere = pl.BlockSpec(memory_space=pl.ANY)
    return pl.pallas_call(
        functools.partial(banded_kernel, shifts, capacity, tuple(pieces), len(refs), size),
        grid_spec=pltpu.PrefetchScalarGridSpec(
            num_scalar_prefetch=2,
            grid=(),
            in_specs=[anywhere] * len(refs),
            out_specs=[anywhere] * len(shifts),
            scratch_shapes=[
                pltpu.VMEM((halves, slots, bands, rows, hidden), jnp.bfloat16),
                pltpu.VMEM((halves, slots, bands, size, hidden), jnp.bfloat16),
                pltpu.VMEM((count, bands, rows, hidden), jnp.bfloat16),
                pltpu.SemaphoreType.DMA((len(pieces),)),
                pltpu.SemaphoreType.DMA((len(shifts),)),
            ],
        ),
        out_shape=[jax.ShapeDtypeStruct((capacity, bands, rows, hidden), jnp.bfloat16)] * len(shifts),
        compiler_params=pltpu.CompilerParams(vmem_limit_bytes=14 * mebi),
        cost_estimate=pl.CostEstimate(
            flops=2 * count * bands * rows * hidden * hidden * halves, bytes_accessed=1, transcendentals=0
        ),
        name="banded_products",
    )(ids, chosen, *refs)


def close_kernel(layer, last, spots, chunks, n_chan, n_sub, base, of, terms, capacity, ids, blocks, place, *rest):
    n_parts = len(spots)
    arrived, rest = rest[:n_parts], rest[n_parts:]
    cur_ref, gate_ref, w_out_ref = rest[:3]
    if last:
        out_ref, held, wide_out, sems, swap = rest[3:]
    else:
        chain_ref, w_ref, wide = rest[3:6]
        out_ref, next_gate_ref, sent_ref, *operand_refs, held, wide_out, sems, norm_ref, laid, turned, swap = rest[
            -(2 * chunks + 10) :
        ]
        left_refs, right_refs = operand_refs[:chunks], operand_refs[chunks:]
    step = pl.program_id(0)
    _, rows, cols, channels = cur_ref.shape
    _, bands, _, hidden = held.shape
    parts, size = hidden // bands, bands

    def arrival(n):
        shift, at = spots[n]
        target = held.at[pl.ds(shift * capacity, capacity), pl.ds(at, arrived[n].shape[1])]
        return pltpu.make_async_copy(arrived[n], target, sems.at[n])

    @pl.when(step == 0)
    def _():
        for n in range(n_parts):
            arrival(n).start()
        wide_out[...] = jnp.zeros_like(wide_out)
        for part in range(parts):
            for a in range(parts):
                at = (part * parts + a) * bands
                wide_out[at : at + bands, a * channels : (a + 1) * channels] = w_out_ref[
                    0, part * bands : (part + 1) * bands, :
                ]
        swap[...] = swap_matrix(16)
        for n in range(n_parts):
            arrival(n).wait()

    if not last:
        block = ids[0] * of + base + step
        row_alive = alive_rows(chain_ref, (blocks[0, block] * n_chan + ids[1]) * rows, rows)
        col_alive = alive_rows(chain_ref, (blocks[1, block] * n_sub + ids[2]) * cols, cols)
    half = 16
    by_row = [[] for _ in range(rows)]
    for row in range(0, rows, half):
        for band in range(0, bands, half):
            taken = pl.ds(band, half), pl.ds(row, half)
            total = held[(place[(base + step) * terms], *taken)].astype(jnp.float32)
            for t in range(1, terms):
                total = total + held[(place[(base + step) * terms + t], *taken)].astype(jnp.float32)
            moved = swapped(total.astype(jnp.bfloat16), swap)
            for r in range(half):
                by_row[row + r].append(moved[r])
    groups = rows // parts
    pieces = []
    for g in range(groups):
        block = jnp.concatenate([x for a in range(parts) for x in by_row[g * parts + a]]).T
        pieces.append(jnp.concatenate([block[p * cols : (p + 1) * cols] for p in range(parts)], axis=1))
    mixture = jnp.concatenate(pieces)
    together = (lane_group((hidden, hidden), size) == lax.broadcasted_iota(jnp.int32, (hidden, hidden), 0) // size)
    together = together.astype(jnp.float32).astype(jnp.bfloat16)
    average = dot(mixture, jnp.concatenate([together] * parts)) * (1.0 / hidden)
    centred = [mixture[:, p * hidden : (p + 1) * hidden].astype(jnp.float32) - average for p in range(parts)]
    squares = sum(c * c for c in centred)
    high = squares.astype(jnp.bfloat16)
    low = (squares - high.astype(jnp.float32)).astype(jnp.bfloat16)
    variance = dot(jnp.concatenate([high, low], axis=1), jnp.concatenate([together] * 2)) * (1.0 / hidden)
    scale = lax.rsqrt(variance + norm_epsilon)
    normed = jnp.concatenate([(c * scale).astype(jnp.bfloat16) for c in centred], axis=1)
    update = dot(normed, wide_out[...])
    for g in range(groups):
        taken = pl.ds(g * parts, parts)
        change = jnp.concatenate(
            [update[g * cols : (g + 1) * cols, a * channels : (a + 1) * channels] for a in range(parts)]
        )
        gate = gate_ref[0, taken].reshape(parts * cols, channels)
        current = cur_ref[0, taken].astype(jnp.float32).reshape(parts * cols, channels)
        result = (current + gate * change).astype(jnp.bfloat16)
        out_ref[0, taken] = result.reshape(parts, cols, channels)
        if not last:
            sent_ref[0, taken] = result.reshape(parts, cols, channels)
            norm_and_gate(result, row_alive, col_alive, g * parts, norm_ref, w_ref, next_gate_ref)
    if not last:
        open_layer(layer + 1, norm_ref[...], left_refs, right_refs, wide, laid, turned, swap)


def close_layer(
    layer, arrived, ids, blocks, place, current, gate, w_out, capacity, terms, chains, w_in, wide, last, bands, base, count, earlier
):
    flat, spots = [part for part, *_ in arrived], tuple((shift, at) for _, shift, at in arrived)
    n_blk = lax.axis_size("blk")
    slots, rows, cols, channels = current.shape
    hidden = w_out.shape[1]

    def layer_spec(array, index):
        return pl.BlockSpec((1,) + array.shape[1:], lambda s, *_: (index, 0, 0))

    in_specs = [pl.BlockSpec(memory_space=pl.ANY)] * len(flat)
    in_specs += slot_specs([current, gate], slots, base) + [layer_spec(w_out, layer)]
    operands = [*flat, current, gate, w_out]
    out_shape = [jax.ShapeDtypeStruct(current.shape, jnp.bfloat16)]
    scratch = [
        pltpu.VMEM((n_blk * capacity, sum(bands[layer]), rows, hidden), jnp.bfloat16),
        pltpu.VMEM((hidden // cols * hidden, hidden // cols * channels), jnp.bfloat16),
        pltpu.SemaphoreType.DMA((len(flat),)),
    ]
    if not last:
        operands += [chains, w_in, wide]
        in_specs += [pl.BlockSpec(chains.shape, lambda s, *_: (0, 0)), layer_spec(w_in, layer + 1)]
        in_specs += [pl.BlockSpec(wide.shape, lambda s, *_: (0, 0))]
        out_shape += [jax.ShapeDtypeStruct(current.shape, jnp.float32)]
        out_shape += [jax.ShapeDtypeStruct((count,) + current.shape[1:], jnp.bfloat16)]
        out_shape += operand_outputs(slots, count, cols, hidden, bands[layer + 1])
        scratch += [pltpu.VMEM((rows, cols, channels), jnp.bfloat16)] + operand_scratch(cols, rows, hidden)
    else:
        scratch += [pltpu.VMEM((256, 256), jnp.bfloat16)]
    more, more_specs, aliases = fill(out_shape, earlier, slots, 3 + len(operands))
    return pl.pallas_call(
        functools.partial(
            close_kernel,
            *(layer, last, spots, 0 if last else len(bands[layer + 1]), lax.axis_size("chan"), lax.axis_size("sub")),
            *(base, slots, terms, capacity),
        ),
        grid_spec=pltpu.PrefetchScalarGridSpec(
            num_scalar_prefetch=3,
            grid=(count,),
            in_specs=in_specs + more_specs,
            out_specs=slot_specs(out_shape, slots, base),
            scratch_shapes=scratch,
        ),
        out_shape=out_shape,
        input_output_aliases=aliases,
        compiler_params=pltpu.CompilerParams(vmem_limit_bytes=24 * mebi),
        cost_estimate=pl.CostEstimate(flops=1 << 33, bytes_accessed=1 << 20, transcendentals=0),
        name="close_layer",
    )(ids, blocks, place, *operands, *more)


def after(value, *others):
    return lax.optimization_barrier((value, *others))[0]


def exchange_bands_outgoing(left, right, over):
    both = ("chan", "sub")
    other = lax.ppermute(left, "sub", [(0, 1), (1, 0)])
    one = lax.ppermute(right, both, [(0, 2), (3, 1), (1, 0), (2, 3)])
    two = lax.ppermute(right, both, [(1, 2), (2, 1)])
    return [(other, left), (left, other)], [(one, one), (right, two)]


def exchange_bands_incoming(left, right, over):
    both = ("chan", "sub")
    one = lax.ppermute(left, both, [(1, 3), (2, 0), (0, 1), (3, 2)])
    other = lax.ppermute(right, "chan", [(0, 1), (1, 0)])
    two = lax.ppermute(one if over is None else after(one, over), both, [(0, 1), (3, 2)])
    return [(left, one), (one, two)], [(right, right), (other, other)]


def banded(pair, ids, blocks, owners, slot_of, chains, w_in, w_out, capacity, terms, n_blk):
    slots, rows, cols, channels = pair.shape
    hidden = w_out.shape[1]
    far = 1
    middle = n_blk // 2
    near = [s for s in (middle, *range(1, n_blk)) if s != far]
    near = [s for n, s in enumerate(near) if s not in near[:n]] + [0]
    layers = w_in.shape[0]
    current = pair
    bands = [[12, 20], [14, 18]]
    chosen, place, mine = make_plan(ids, owners, slot_of, n_blk, far, slots, terms, capacity)
    in_order = jnp.repeat(jnp.arange(capacity, dtype=jnp.int32), 2)
    half = slots // 2
    halves = [(0, half), (half, slots - half)]

    def over_blk(value, shift):
        return lax.ppermute(value, "blk", [(p, (p + shift) % n_blk) for p in range(n_blk)])

    for layer in range(layers):
        count = len(bands[layer])
        if layer == 0:
            raw = [over_blk(pair, far)]
            calls, wide = [None], spread_weights(w_in, 0, cols)
            for base, size in halves:
                calls.append(
                    open_operands(ids, blocks, pair, chains, w_in, wide, hidden, bands[0], base, size, calls[-1])
                )
            gate = calls[-1][0]
        else:
            raw = []
            for call in calls[1:]:
                raw.append(over_blk(after(call[2], *raw) if raw else call[2], far))
        operands = [call[-2 * count :] for call in calls[1:]]
        exchange = exchange_bands_incoming if layer % 2 else exchange_bands_outgoing
        arrived, by_shift = [], {}
        for chunk in range(count):
            if chunk == 0:
                exchanged = []
                over = operands[-1][count]
                for left, right in [(o[0], o[count]) for o in operands]:
                    if exchanged and layer % 2:
                        (_, (one, two)), (_, (other, _)) = exchanged[-1]
                        left, right = lax.optimization_barrier((left, right, one, other))[:2]
                        right = after(right, two)
                    elif exchanged:
                        ((other, _), _), ((one, _), (_, two)) = exchanged[-1]
                        left, right = lax.optimization_barrier((left, right, other, one, two))[:2]
                    exchanged.append(exchange(left, right, over))
            else:
                left, right = operands[-1][chunk], operands[-1][count + chunk]
                if layer % 2:
                    (_, (_, two)), (_, (other, _)) = exchanged[-1]
                    left, right = lax.optimization_barrier((left, right, two, other))[:2]
                else:
                    ((other, _), _), ((one, _), (_, two)) = exchanged[-1]
                    left = after(left, other)
                    right = after(right, one, two, chosen)
                exchanged = [exchange(left, right, list(by_shift.values())[-1] if by_shift else made[-1])]
                ids = after(ids, *by_shift.values())
            made = banded_products(near, ids, chosen, exchanged, capacity, cols)
            start = sum(bands[layer][:chunk])
            for shift, part in zip(near, made):
                if shift:
                    part = over_blk(after(part, by_shift.get(shift, raw[-1])), shift)
                    by_shift[shift] = part
                arrived.append((part, shift, start))
            if chunk == 0:
                sources = list(lax.optimization_barrier((*raw, made[-1]))[:-1])
                far_left, far_right = far_operands(
                    layer, ids, blocks, mine, sources, chains, wide, far, capacity, slots, hidden
                )
        far_exchanged = [exchange(far_left, far_right, made[-1])]
        (part,) = banded_products([0], ids, in_order, far_exchanged, capacity, cols)
        arrived.append((part, far, 0))
        last = layer == layers - 1
        calls = [None]
        if not last:
            wide = spread_weights(after(w_in, made[-1]), layer + 1, cols)
        for base, size in [(0, slots)] if last else halves:
            calls.append(
                close_layer(
                    *(layer, arrived, ids, blocks, place, current, gate, w_out, capacity, terms, chains, w_in, wide, last),
                    *(bands, base, size, calls[-1]),
                )
            )
        if last:
            return calls[-1][0]
        current, gate = calls[-1][:2]


def per_device(pair, block_list, term_owner, term_slots, chain_ids, w_in, w_out):
    n_blk = lax.axis_size("blk")
    n_chan = lax.axis_size("chan")
    n_sub = lax.axis_size("sub")
    position = lax.axis_index("blk")
    row_group = lax.axis_index("chan")
    col_group = lax.axis_index("sub")
    slots, rows, cols, channels = pair.shape
    hidden = w_out.shape[1]
    terms = term_owner.shape[1]
    capacity = max(2, -(-slots * terms // n_blk))
    fast = n_chan == 2 and n_sub == 2
    on_diagonal = (row_group == col_group).astype(jnp.int32)
    ids = jnp.stack([position, row_group, col_group, on_diagonal]).astype(jnp.int32)
    blocks = block_list.T
    owners = term_owner.T
    slot_of = jnp.transpose(term_slots, (1, 2, 0))
    chains = chain_ids.reshape(-1, 128)
    if fast and n_blk > 1 and rows == cols == 32 and channels == hidden == 128:
        return banded(pair, ids, blocks, owners, slot_of, chains, w_in, w_out, capacity, terms, n_blk)
    shifts = [n_blk // 2] + [s for s in range(1, n_blk) if s != n_blk // 2] + [0]

    def all_products(lefts, right):
        parts = [None] * n_blk
        for shift in shifts:
            made = term_products(shift, ids, owners, slot_of, lefts, right, capacity, slots, terms)
            if shift:
                pairs = [(p, (p + shift) % n_blk) for p in range(n_blk)]
                made = lax.ppermute(made, "blk", pairs)
            parts[shift] = made
        return parts

    def at_home(layer, parts, current, gate, at, of, into=None):
        last = layer == w_in.shape[0] - 1
        return home(
            layer, parts, ids, blocks, owners, current, gate, w_out, capacity, terms, at, of, chains, w_in, last, into
        )

    gate, left, *rights = first_operands(ids, blocks, pair, chains, w_in, hidden, 2 if fast else 1)
    lefts, chunks = exchange_outgoing(left, rights, n_chan, n_sub)
    count = len(chunks)
    made = [all_products(lefts, right) for right in chunks]
    homes = [at_home(0, parts, pair, gate, at, count) for at, parts in enumerate(made)]
    lefts, chunks = exchange_incoming([h[2] for h in homes], [h[3] for h in homes], n_chan, n_sub)
    made = [all_products(lefts, right) for right in chunks]
    out = None
    for at, parts in enumerate(made):
        (out,) = at_home(1, parts, homes[at][0], homes[at][1], at, count, into=out)
    return out


def solution(mesh):
    in_specs = (
        P(("groups", "blk"), "chan", "sub", None),
        P("groups", None),
        P("groups", None),
        P("groups", None, None),
        P("groups"),
        P(),
        P(),
    )
    out_specs = P(("groups", "blk"), "chan", "sub", None)
    return jax.shard_map(
        per_device, mesh=mesh, in_specs=in_specs, out_specs=out_specs, check_vma=False
    )
```

```python
import functools

import jax
import jax.numpy as jnp
from jax import lax
from jax.experimental import pallas as pl
from jax.experimental.pallas import tpu as pltpu
from jax.sharding import PartitionSpec as P

norm_epsilon = 1e-05
mebi = 1024 * 1024
vmem_limit = 56 * mebi


def sigmoid(values):
    return 0.5 + 0.5 * jnp.tanh(0.5 * values)


def layer_norm(values):
    values = values.astype(jnp.float32)
    centred = values - jnp.mean(values, axis=-1, keepdims=True)
    variance = jnp.mean(centred * centred, axis=-1, keepdims=True)
    return centred * lax.rsqrt(variance + norm_epsilon)


def alive_rows(chain_ref, start, size):
    lanes = chain_ref.shape[1]
    line = chain_ref[pl.ds(start // lanes, 1), :] >= 0
    spot = lax.broadcasted_iota(jnp.int32, (size, lanes), 0) + lax.rem(start, lanes)
    pick = jnp.logical_and(lax.broadcasted_iota(jnp.int32, (size, lanes), 1) == spot, line)
    return dot(pick.astype(jnp.float32).astype(jnp.bfloat16), jnp.ones((lanes, lanes), jnp.bfloat16))


def dot(a, b):
    return jnp.dot(a, b, preferred_element_type=jnp.float32)


def gated_pair(projected, mask, hidden):
    left = mask * sigmoid(projected[:, hidden : 2 * hidden]) * projected[:, :hidden]
    right = mask * sigmoid(projected[:, 3 * hidden : 4 * hidden]) * projected[:, 2 * hidden : 3 * hidden]
    return left.astype(jnp.bfloat16), right.astype(jnp.bfloat16)


def first_kernel(hidden, row_parts, n_chan, n_sub, ids, blocks, pair_ref, chain_ref, w_ref, gate_ref, left_ref, *rest):
    right_refs, (norm_ref, turned_ref) = rest[:row_parts], rest[row_parts:]
    slots = pl.num_programs(0)
    _, rows, cols, channels = pair_ref.shape
    block = ids[0] * slots + pl.program_id(0)
    row_alive = alive_rows(chain_ref, (blocks[0, block] * n_chan + ids[1]) * rows, rows)
    col_alive = alive_rows(chain_ref, (blocks[1, block] * n_sub + ids[2]) * cols, cols)
    group = max(1, 256 // cols)
    for start in range(0, rows, group):
        at = pl.ds(start, group)
        normed = layer_norm(pair_ref[0, at].reshape(group * cols, channels))
        norm_ref[pl.ds(start * cols, group * cols), :] = normed
        gate = sigmoid(dot(normed.astype(jnp.bfloat16), w_ref[0, :, 4 * hidden :]))
        gate_ref[0, at] = gate.reshape(group, cols, channels)
    for col in range(cols):
        turned_ref[col] = norm_ref[pl.ds(col, rows, stride=cols), :].astype(jnp.bfloat16)
    step = max(1, 128 // rows)
    part = rows // row_parts
    for start in range(0, cols, step):
        taken = turned_ref[start : start + step].reshape(step * rows, channels)
        projected = dot(taken, w_ref[0, :, : 4 * hidden])
        mask = col_alive[start : start + step][:, None, :] * row_alive[None, :, :]
        left, right = gated_pair(projected, mask.reshape(step * rows, -1), hidden)
        left_ref[0, start : start + step] = left.reshape(step, rows, hidden)
        right = right.reshape(step, rows, hidden)
        for p, right_ref in enumerate(right_refs):
            right_ref[0, start : start + step] = right[:, p * part : (p + 1) * part]


def first_operands(ids, blocks, pair, chains, w_in, hidden, row_parts):
    slots, rows, cols, channels = pair.shape
    part = rows // row_parts
    operand = jax.ShapeDtypeStruct((slots, cols, rows, hidden), jnp.bfloat16)
    right = jax.ShapeDtypeStruct((slots, cols, part, hidden), jnp.bfloat16)
    return pl.pallas_call(
        functools.partial(first_kernel, hidden, row_parts, lax.axis_size("chan"), lax.axis_size("sub")),
        grid_spec=pltpu.PrefetchScalarGridSpec(
            num_scalar_prefetch=2,
            grid=(slots,),
            in_specs=[
                pl.BlockSpec((1, rows, cols, channels), lambda s, *_: (s, 0, 0, 0)),
                pl.BlockSpec(chains.shape, lambda s, *_: (0, 0)),
                pl.BlockSpec((1,) + w_in.shape[1:], lambda s, *_: (0, 0, 0)),
            ],
            out_specs=[
                pl.BlockSpec((1, rows, cols, channels), lambda s, *_: (s, 0, 0, 0)),
                pl.BlockSpec((1, cols, rows, hidden), lambda s, *_: (s, 0, 0, 0)),
            ]
            + [pl.BlockSpec((1, cols, part, hidden), lambda s, *_: (s, 0, 0, 0))] * row_parts,
            scratch_shapes=[
                pltpu.VMEM((rows * cols, channels), jnp.float32),
                pltpu.VMEM((cols, rows, channels), jnp.bfloat16),
            ],
        ),
        out_shape=[jax.ShapeDtypeStruct(pair.shape, jnp.float32), operand] + [right] * row_parts,
        compiler_params=pltpu.CompilerParams(vmem_limit_bytes=vmem_limit),
        name="first_operands",
    )(ids, blocks, pair, chains, w_in)


def product_kernel(shift, n_blk, slots_dev, terms, capacity, pieces, n_refs, ids, owners, slots, *rest):
    refs = rest[:n_refs]
    out_ref, left_held, right_held, right_wide, chosen, sems = rest[n_refs:]
    step = pl.program_id(0)
    turn = lax.rem(step, 2)
    _, depth, n_i, hidden = left_held.shape
    n_j = right_wide.shape[1]

    @pl.when(step == 0)
    def _():
        target = lax.rem(ids[0] + shift, n_blk)
        for e in range(2 * capacity):
            chosen[e] = 0

        def scan(e, count):
            block, term = target * slots_dev + e // terms, lax.rem(e, terms)
            here = jnp.logical_and(owners[term, block] == ids[0], count < capacity)

            @pl.when(here)
            def _():
                chosen[2 * count] = slots[term, 0, block]
                chosen[2 * count + 1] = slots[term, 1, block]

            return count + here.astype(jnp.int32)

        lax.fori_loop(0, slots_dev * terms, scan, jnp.int32(0))

    def copy(n, term, buffer, source):
        side, _, _, k0, depth_of, i0, size = pieces[n]
        held = (left_held, right_held)[side]
        return pltpu.make_async_copy(
            refs[source].at[chosen[2 * term + side]],
            held.at[buffer, pl.ds(k0, depth_of), pl.ds(i0, size), :],
            sems.at[buffer, n],
        )

    def start(term, buffer):
        for n, (_, on, off, *_) in enumerate(pieces):
            if on == off:
                copy(n, term, buffer, on).start()
            else:

                @pl.when(ids[3] == 1)
                def _(n=n, on=on):
                    copy(n, term, buffer, on).start()

                @pl.when(ids[3] == 0)
                def _(n=n, off=off):
                    copy(n, term, buffer, off).start()

    @pl.when(step == 0)
    def _():
        start(0, 0)

    @pl.when(step + 1 < capacity)
    def _():
        start(step + 1, 1 - turn)

    for n, piece in enumerate(pieces):
        copy(n, step, turn, piece[1]).wait()

    span = 8

    def widen(n, carry):
        at = pl.ds(n * span, span)
        right_wide[at] = right_held[turn, at].astype(jnp.float32)
        return carry

    lax.fori_loop(0, depth // span, widen, 0)

    group = min(8, n_j)
    unroll = 4
    for j0 in range(0, n_j, group):

        def body(n, sums):
            for u in range(unroll):
                k = n * unroll + u
                left = left_held[turn, k].astype(jnp.float32).reshape(n_i // 8, 8, hidden)
                sums = tuple(
                    total + left * right_wide[k, pl.ds(j0 + j, 8, stride=0), :][None]
                    for j, total in enumerate(sums)
                )
            return sums

        zero = jnp.zeros((n_i // 8, 8, hidden), jnp.float32)
        sums = lax.fori_loop(0, depth // unroll, body, (zero,) * group)
        for j, total in enumerate(sums):
            out_ref[0, j0 + j] = total.reshape(n_i, hidden).astype(jnp.bfloat16)


def term_products(shift, ids, owners, slots, lefts, rights, capacity, slots_dev, terms):
    n_blk = lax.axis_size("blk")
    refs, pieces = [], []

    def index_of(array):
        for n, known in enumerate(refs):
            if known is array:
                return n
        refs.append(array)
        return len(refs) - 1

    for side, operands in ((0, lefts), (1, rights)):
        for on, off, k0, i0 in operands:
            pieces.append((side, index_of(on), index_of(off), k0, on.shape[1], i0, on.shape[2]))
    hidden = lefts[0][0].shape[3]
    n_i = max(p[5] + p[6] for p in pieces if p[0] == 0)
    n_j = max(p[5] + p[6] for p in pieces if p[0] == 1)
    depth = max(p[3] + p[4] for p in pieces)
    return pl.pallas_call(
        functools.partial(
            product_kernel, shift, n_blk, slots_dev, terms, capacity, tuple(pieces), len(refs)
        ),
        grid_spec=pltpu.PrefetchScalarGridSpec(
            num_scalar_prefetch=3,
            grid=(capacity,),
            in_specs=[pl.BlockSpec(memory_space=pl.ANY)] * len(refs),
            out_specs=pl.BlockSpec((1, n_j, n_i, hidden), lambda t, *_: (t, 0, 0, 0)),
            scratch_shapes=[
                pltpu.VMEM((2, depth, n_i, hidden), jnp.bfloat16),
                pltpu.VMEM((2, depth, n_j, hidden), jnp.bfloat16),
                pltpu.VMEM((depth, n_j, hidden), jnp.float32),
                pltpu.SMEM((2 * capacity,), jnp.int32),
                pltpu.SemaphoreType.DMA((2, len(pieces))),
            ],
        ),
        out_shape=jax.ShapeDtypeStruct((capacity, n_j, n_i, hidden), jnp.bfloat16),
        compiler_params=pltpu.CompilerParams(vmem_limit_bytes=vmem_limit),
        cost_estimate=pl.CostEstimate(
            flops=2 * capacity * n_i * n_j * depth * hidden * 100,
            bytes_accessed=capacity * (depth * (n_i + n_j) + n_i * n_j) * hidden * 2,
            transcendentals=0,
        ),
        name="term_products",
    )(ids, owners, slots, *refs)


def home_kernel(last, hidden, n_blk, n_chan, n_sub, at, of, slots_dev, terms, capacity, ids, blocks, owners, *rest):
    parts, rest = rest[:n_blk], rest[n_blk:]
    scratch, rest = rest[-5:], rest[:-5]
    held, turned, place, seen, sems = scratch
    cur_ref, gate_ref, w_out_ref = rest[:3]
    if last:
        out_ref = rest[-1]
    else:
        chain_ref, w_ref, out_ref, next_gate_ref, left_ref, right_ref = rest[3:]
    step = pl.program_id(0)
    _, rows, cols, channels = cur_ref.shape

    def arrival(shift):
        return pltpu.make_async_copy(parts[shift], held.at[pl.ds(shift * capacity, capacity)], sems.at[shift])

    @pl.when(step == 0)
    def _():
        for shift in range(n_blk):
            arrival(shift).start()
            seen[shift] = 0

        def scan(e, carry):
            owner = owners[lax.rem(e, terms), ids[0] * slots_dev + e // terms]
            shift = lax.rem(ids[0] - owner + n_blk, n_blk)
            count = seen[owner]
            seen[owner] = count + 1
            place[e] = shift * capacity + count
            return carry

        lax.fori_loop(0, slots_dev * terms, scan, jnp.int32(0))
        for shift in range(n_blk):
            arrival(shift).wait()

    if not last:
        block = ids[0] * slots_dev + step
        row_alive = alive_rows(chain_ref, (blocks[0, block] * n_chan + ids[1]) * rows, rows)
        col_alive = alive_rows(chain_ref, ((blocks[1, block] * n_sub + ids[2]) * of + at) * cols, cols)
    span = max(1, 128 // rows)
    for start in range(0, cols, span):
        taken = pl.ds(start, span)
        total = held[place[step * terms], taken].astype(jnp.float32)
        for t in range(1, terms):
            total = total + held[place[step * terms + t], taken].astype(jnp.float32)
        rounded = total.astype(jnp.bfloat16).astype(jnp.float32)
        turned[pl.ds(start * rows, span * rows), :] = rounded.reshape(span * rows, hidden)
    group = min(rows, max(1, 256 // cols))
    for start in range(0, rows, group):
        taken = pl.ds(start, group)
        mixture = jnp.concatenate(
            [turned[pl.ds(row, cols, stride=rows), :].astype(jnp.bfloat16) for row in range(start, start + group)]
        )
        update = dot(layer_norm(mixture).astype(jnp.bfloat16), w_out_ref[0])
        current = cur_ref[0, taken].astype(jnp.float32).reshape(group * cols, channels)
        gate = gate_ref[0, taken].reshape(group * cols, channels)
        result = (current + gate * update).astype(jnp.bfloat16)
        out_ref[0, taken] = result.reshape(group, cols, channels)
        if not last:
            normed = layer_norm(result).astype(jnp.bfloat16)
            projected = dot(normed, w_ref[0])
            next_gate_ref[0, taken] = sigmoid(projected[:, 4 * hidden :]).reshape(group, cols, channels)
            mask = row_alive[start : start + group][:, None, :] * col_alive[None, :, :]
            left, right = gated_pair(projected, mask.reshape(group * cols, channels), hidden)
            left_ref[0, taken] = left.reshape(group, cols, hidden)
            right_ref[0, taken] = right.reshape(group, cols, hidden)


def home(layer, parts, ids, blocks, owners, current, gate, w_out, capacity, terms, at, of, chains, w_in, last, into=None):
    n_blk = len(parts)
    slots, rows, _, channels = current.shape
    hidden = w_out.shape[1]
    cols = parts[0].shape[1]
    chunk = (1, rows, cols, channels)

    def chunk_spec(array):
        whole = array.shape[2] != cols
        return pl.BlockSpec(chunk, lambda s, *_: (s, 0, at if whole else 0, 0))

    def layer_spec(array, index):
        return pl.BlockSpec((1,) + array.shape[1:], lambda s, *_: (index, 0, 0))

    in_specs = [pl.BlockSpec(memory_space=pl.ANY)] * n_blk + [
        chunk_spec(current),
        chunk_spec(gate),
        layer_spec(w_out, layer),
    ]
    operands = [*parts, current, gate, w_out]
    aliases = {}
    if last:
        if into is not None:
            aliases = {3 + len(operands): 0}
            operands.append(into)
            in_specs.append(pl.BlockSpec(memory_space=pl.ANY))
        out_shape = [jax.ShapeDtypeStruct((slots, rows, cols * of, channels), jnp.bfloat16)]
        out_specs = [pl.BlockSpec(chunk, lambda s, *_: (s, 0, at, 0))]
    else:
        operands += [chains, w_in]
        in_specs += [pl.BlockSpec(chains.shape, lambda s, *_: (0, 0)), layer_spec(w_in, layer + 1)]
        small = (slots, rows, cols, channels)
        out_shape = [jax.ShapeDtypeStruct(small, t) for t in (jnp.bfloat16, jnp.float32, jnp.bfloat16, jnp.bfloat16)]
        out_specs = [pl.BlockSpec(chunk, lambda s, *_: (s, 0, 0, 0))] * 4
    return pl.pallas_call(
        functools.partial(
            home_kernel, last, hidden, n_blk, lax.axis_size("chan"), lax.axis_size("sub"), at, of, slots, terms, capacity
        ),
        grid_spec=pltpu.PrefetchScalarGridSpec(
            num_scalar_prefetch=3,
            grid=(slots,),
            in_specs=in_specs,
            out_specs=out_specs,
            scratch_shapes=[
                pltpu.VMEM((n_blk * capacity, cols, rows, hidden), jnp.bfloat16),
                pltpu.VMEM((rows * cols, hidden), jnp.float32),
                pltpu.SMEM((slots * terms,), jnp.int32),
                pltpu.SMEM((n_blk,), jnp.int32),
                pltpu.SemaphoreType.DMA((n_blk,)),
            ],
        ),
        out_shape=out_shape,
        input_output_aliases=aliases,
        compiler_params=pltpu.CompilerParams(vmem_limit_bytes=vmem_limit),
        cost_estimate=pl.CostEstimate(
            flops=2 * slots * rows * cols * channels * 6 * channels * 10,
            bytes_accessed=slots * rows * cols * channels * 16,
            transcendentals=0,
        ),
        name="home",
    )(ids, blocks, owners, *operands)


def exchange_outgoing(left, rights, n_chan, n_sub):
    if n_chan == 2 and n_sub == 2:
        both = ("chan", "sub")
        other_left = lax.ppermute(left, "sub", [(0, 1), (1, 0)])
        lefts = [(other_left, left, 0, 0), (left, other_left, left.shape[1], 0)]
        chunks = []
        for right in rights:
            if chunks:
                (one, *_), (_, two, *_) = chunks[-1]
                right, *_ = lax.optimization_barrier((right, one, two))
            one = lax.ppermute(right, both, [(0, 2), (3, 1), (1, 0), (2, 3)])
            two = lax.ppermute(right, both, [(1, 2), (2, 1)])
            chunks.append([(one, one, 0, 0), (right, two, right.shape[1], 0)])
        return lefts, chunks
    left = lax.all_gather(left, "sub", axis=1, tiled=True)
    right = jnp.concatenate(rights, axis=2)
    right = lax.all_gather(right, "chan", axis=2, tiled=True)
    right = lax.all_to_all(right, "sub", split_axis=2, concat_axis=1, tiled=True)
    cols = right.shape[2] // 2
    chunks = [right[:, :, :cols], right[:, :, cols:]]
    return [(left, left, 0, 0)], [[(r, r, 0, 0)] for r in chunks]


def exchange_incoming(lefts, rights, n_chan, n_sub):
    if n_chan == 2 and n_sub == 2:
        both = ("chan", "sub")
        left_pieces, chunks = [], []
        at = 0
        for left, right in zip(lefts, rights):
            depth = left.shape[1]
            one = lax.ppermute(left, both, [(1, 3), (2, 0), (0, 1), (3, 2)])
            two = lax.ppermute(one, both, [(0, 1), (3, 2)])
            left_pieces += [(left, one, 0, at), (one, two, depth, at)]
            other = lax.ppermute(right, "chan", [(0, 1), (1, 0)])
            chunks.append([(right, right, 0, 0), (other, other, depth, 0)])
            at += left.shape[2]
        return left_pieces, chunks
    left = lax.all_gather(jnp.concatenate(lefts, axis=2), "chan", axis=1, tiled=True)
    left = lax.all_gather(left, "sub", axis=2, tiled=True)
    size = left.shape[2] // n_chan
    left = lax.dynamic_slice_in_dim(left, lax.axis_index("chan") * size, size, 2)
    gathered = [lax.all_gather(right, "chan", axis=1, tiled=True) for right in rights]
    return [(left, left, 0, 0)], [[(r, r, 0, 0)] for r in gathered]


def lane_group(shape, size):
    return lax.broadcasted_iota(jnp.int32, shape, 1) // size


def spread_kernel(size, w_ref, wide_ref):
    hidden = w_ref.shape[1]
    parts = hidden // size
    for side in range(2):
        for kind in range(2):
            start = (2 * side + kind) * hidden
            weights = 0.5 * w_ref[0, :, start : start + hidden].astype(jnp.float32)
            group = lane_group(weights.shape, size)
            for part in range(parts):
                kept = jnp.where(group == part, weights, 0.0)
                at = ((side * parts + part) * 2 + kind) * hidden
                for a in range(parts):
                    moved = pltpu.roll(kept, ((a - part) % parts) * size, 1) if a != part else kept
                    wide_ref[a * hidden : (a + 1) * hidden, at : at + hidden] = moved.astype(jnp.bfloat16)


def spread_weights(w_in, layer, size):
    hidden = w_in.shape[1]
    parts = hidden // size
    shape = (parts * hidden, 4 * parts * hidden)
    return pl.pallas_call(
        functools.partial(spread_kernel, size),
        grid=(1,),
        in_specs=[pl.BlockSpec((1,) + w_in.shape[1:], lambda s: (layer, 0, 0))],
        out_specs=pl.BlockSpec(shape, lambda s: (0, 0)),
        out_shape=jax.ShapeDtypeStruct(shape, jnp.bfloat16),
        compiler_params=pltpu.CompilerParams(vmem_limit_bytes=16 * mebi),
        cost_estimate=pl.CostEstimate(flops=1 << 30, bytes_accessed=1 << 20, transcendentals=0),
        name="spread_weights",
    )(w_in)


def swap_matrix(half):
    shape = (half * half, half * half)
    to, of = lax.broadcasted_iota(jnp.int32, shape, 0), lax.broadcasted_iota(jnp.int32, shape, 1)
    same = jnp.logical_and(to // half == lax.rem(of, half), lax.rem(to, half) == of // half)
    return same.astype(jnp.float32).astype(jnp.bfloat16)


def swapped(values, swap_ref):
    half, _, lanes = values.shape
    moved = dot(swap_ref[...], values.reshape(half * half, lanes))
    return moved.astype(jnp.bfloat16).reshape(half, half, lanes)


def turn(taken, turned, swap_ref):
    half = 16
    for x in range(0, taken.shape[0], half):
        for y in range(0, taken.shape[1], half):
            turned[y : y + half, x : x + half] = swapped(taken[x : x + half, y : y + half], swap_ref)


def make_operand(side, taken, wide_ref, out_refs, laid, swap_ref):
    rows, size, hidden = taken.shape
    parts, bands, half = hidden // size, size, 16
    groups = rows // parts
    stacked = jnp.concatenate(
        [jnp.concatenate([taken[g * parts + a] for a in range(parts)], axis=1) for g in range(groups)], axis=0
    )
    for part in range(parts):
        at = (side * parts + part) * 2 * hidden
        made = dot(stacked, wide_ref[:, at : at + 2 * hidden])
        value = made[:, :hidden] * (1.0 + jnp.tanh(made[:, hidden:]))
        laid[side, :, part * size : (part + 1) * size, :] = value.astype(jnp.bfloat16).reshape(groups, size, hidden)
    blocks = [laid[side, g].T for g in range(groups)]
    starts = [sum(ref.shape[1] for ref in out_refs[:n]) for n in range(len(out_refs))]
    for first in range(0, bands, half):
        for row in range(0, rows, half):
            tiles = []
            for r in range(row, row + half):
                at = r % parts * bands + first
                tiles.append(blocks[r // parts][at : at + half])
            moved = swapped(jnp.stack(tiles), swap_ref)
            for start, ref in zip(starts, out_refs):
                low, high = max(start, first), min(start + ref.shape[1], first + half)
                if low < high:
                    ref[0, low - start : high - start, row : row + half] = moved[low - first : high - first]


def open_layer(layer, natural, left_refs, right_refs, wide, laid, turned, swap):
    turn(natural, turned, swap)
    for side, refs in ((0, left_refs), (1, right_refs)):
        make_operand(side, natural if side == layer % 2 else turned[...], wide, refs, laid, swap)


def norm_and_gate(values, row_alive, col_alive, at, norm_ref, w_ref=None, gate_ref=None):
    _, cols, channels = norm_ref.shape
    rows = values.shape[0] // cols
    normed = layer_norm(values)
    if gate_ref is not None:
        gate = sigmoid(dot(normed.astype(jnp.bfloat16), w_ref[0, :, -channels:]))
        gate_ref[0, pl.ds(at, rows)] = gate.reshape(rows, cols, channels)
    mask = row_alive[at : at + rows, None, :] * col_alive[None, :, :]
    norm_ref[pl.ds(at, rows)] = (normed.reshape(rows, cols, channels) * mask).astype(jnp.bfloat16)


def open_kernel(hidden, chunks, n_chan, n_sub, base, of, ids, blocks, pair_ref, chain_ref, w_ref, wide, *rest):
    gate_ref, *operand_refs, norm_ref, laid, turned, swap = rest[-(2 * chunks + 5) :]
    step = pl.program_id(0)
    _, rows, cols, channels = pair_ref.shape
    block = ids[0] * of + base + step

    @pl.when(step == 0)
    def _():
        swap[...] = swap_matrix(16)

    row_alive = alive_rows(chain_ref, (blocks[0, block] * n_chan + ids[1]) * rows, rows)
    col_alive = alive_rows(chain_ref, (blocks[1, block] * n_sub + ids[2]) * cols, cols)
    group = hidden // cols
    for at in range(0, rows, group):
        values = pair_ref[0, pl.ds(at, group)].reshape(group * cols, channels)
        norm_and_gate(values, row_alive, col_alive, at, norm_ref, w_ref, gate_ref)
    open_layer(0, norm_ref[...], operand_refs[:chunks], operand_refs[chunks:], wide, laid, turned, swap)


def operand_scratch(rows, size, hidden):
    parts = hidden // size
    return [
        pltpu.VMEM((2, rows // parts, parts * size, hidden), jnp.bfloat16),
        pltpu.VMEM((size, rows, hidden), jnp.bfloat16),
        pltpu.VMEM((256, 256), jnp.bfloat16),
    ]


def operand_outputs(slots, count, rows, hidden, bands):
    kept = [count if n == 0 else slots for n in range(len(bands))] * 2
    return [jax.ShapeDtypeStruct((k, b, rows, hidden), jnp.bfloat16) for k, b in zip(kept, bands * 2)]


def slot_specs(arrays, slots, base):
    def spec(array):
        offset = base if array.shape[0] == slots else 0
        return pl.BlockSpec((1,) + array.shape[1:], lambda s, *_: (s + offset, 0, 0, 0))

    return [spec(a) for a in arrays]


def fill(out_shape, earlier, slots, n_before):
    if earlier is None:
        return [], [], {}
    shared = [n for n, o in enumerate(out_shape) if o.shape[0] == slots]
    specs = [pl.BlockSpec(memory_space=pl.ANY)] * len(shared)
    return [earlier[n] for n in shared], specs, {n_before + k: n for k, n in enumerate(shared)}


def open_operands(ids, blocks, pair, chains, w_in, wide, hidden, bands, base, count, earlier):
    slots, rows, cols, channels = pair.shape
    out_shape = [jax.ShapeDtypeStruct(pair.shape, jnp.float32)] + operand_outputs(slots, count, rows, hidden, bands)
    more, more_specs, aliases = fill(out_shape, earlier, slots, 6)
    return pl.pallas_call(
        functools.partial(open_kernel, hidden, len(bands), lax.axis_size("chan"), lax.axis_size("sub"), base, slots),
        grid_spec=pltpu.PrefetchScalarGridSpec(
            num_scalar_prefetch=2,
            grid=(count,),
            in_specs=slot_specs([pair], slots, base)
            + [
                pl.BlockSpec(chains.shape, lambda s, *_: (0, 0)),
                pl.BlockSpec((1,) + w_in.shape[1:], lambda s, *_: (0, 0, 0)),
                pl.BlockSpec(wide.shape, lambda s, *_: (0, 0)),
            ]
            + more_specs,
            out_specs=slot_specs(out_shape, slots, base),
            scratch_shapes=[pltpu.VMEM((rows, cols, channels), jnp.bfloat16)] + operand_scratch(rows, cols, hidden),
        ),
        out_shape=out_shape,
        input_output_aliases=aliases,
        compiler_params=pltpu.CompilerParams(vmem_limit_bytes=18 * mebi),
        cost_estimate=pl.CostEstimate(flops=1 << 33, bytes_accessed=1 << 20, transcendentals=0),
        name="open_operands",
    )(ids, blocks, pair, chains, w_in, wide, *more)


def far_kernel(layer, n_blk, far, n_chan, n_sub, of, bases, ids, blocks, mine, *rest):
    sources, (chain_ref, wide, left_ref, right_ref, norm_ref, laid, turned, swap) = rest[:-8], rest[-8:]
    step = pl.program_id(0)
    rows, cols, channels = norm_ref.shape
    holder = lax.rem(ids[0] - far + n_blk, n_blk)

    @pl.when(step == 0)
    def _():
        swap[...] = swap_matrix(16)

    group = channels // cols
    for side, out_ref in ((0, left_ref), (1, right_ref)):
        slot = mine[2 * step + side]
        refs = sources[side * len(bases) : (side + 1) * len(bases)]
        block = holder * of + slot
        row_alive = alive_rows(chain_ref, (blocks[0, block] * n_chan + ids[1]) * rows, rows)
        col_alive = alive_rows(chain_ref, (blocks[1, block] * n_sub + ids[2]) * cols, cols)
        for at in range(0, rows, group):
            values = refs[0][0, pl.ds(at, group)]
            for base, ref in zip(bases[1:], refs[1:]):
                values = jnp.where(slot >= base, ref[0, pl.ds(at, group)], values)
            norm_and_gate(values.reshape(group * cols, channels), row_alive, col_alive, at, norm_ref)
        if side == layer % 2:
            make_operand(side, norm_ref[...], wide, [out_ref], laid, swap)
        else:
            turn(norm_ref[...], turned, swap)
            make_operand(side, turned[...], wide, [out_ref], laid, swap)


def far_operands(layer, ids, blocks, mine, sources, chains, wide, far, capacity, of, hidden):
    n_blk = lax.axis_size("blk")
    _, rows, cols, channels = sources[0].shape
    bases = [sum(a.shape[0] for a in sources[:n]) for n in range(len(sources))]

    def source_spec(side, base, size):
        def place(t, ids, blocks, mine):
            return jnp.clip(mine[2 * t + side] - base, 0, size - 1), 0, 0, 0

        return pl.BlockSpec((1, rows, cols, channels), place)

    in_specs = [source_spec(side, b, a.shape[0]) for side in range(2) for b, a in zip(bases, sources)]
    in_specs += [pl.BlockSpec(chains.shape, lambda t, *_: (0, 0)), pl.BlockSpec(wide.shape, lambda t, *_: (0, 0))]
    shape = (capacity, hidden // (hidden // cols), rows, hidden)
    return pl.pallas_call(
        functools.partial(
            far_kernel, layer, n_blk, far, lax.axis_size("chan"), lax.axis_size("sub"), of, tuple(bases)
        ),
        grid_spec=pltpu.PrefetchScalarGridSpec(
            num_scalar_prefetch=3,
            grid=(capacity,),
            in_specs=in_specs,
            out_specs=[pl.BlockSpec((1,) + shape[1:], lambda t, *_: (t, 0, 0, 0))] * 2,
            scratch_shapes=[pltpu.VMEM((rows, cols, channels), jnp.bfloat16)] + operand_scratch(rows, cols, hidden),
        ),
        out_shape=[jax.ShapeDtypeStruct(shape, jnp.bfloat16)] * 2,
        compiler_params=pltpu.CompilerParams(vmem_limit_bytes=14 * mebi),
        cost_estimate=pl.CostEstimate(flops=1 << 33, bytes_accessed=1 << 20, transcendentals=0),
        name="far_operands",
    )(ids, blocks, mine, *sources, *sources, chains, wide)


def plan_kernel(n_blk, far, slots_dev, terms, capacity, ids, owners, slots, chosen, place, mine, seen):
    for shift in range(n_blk):
        seen[shift] = 0
        target = lax.rem(ids[0] + shift, n_blk)
        for e in range(2 * (capacity + 1)):
            chosen[2 * shift * (capacity + 1) + e] = 0
        found = jnp.int32(0)
        for e in range(slots_dev * terms):
            block, term = target * slots_dev + e // terms, e % terms
            at = 2 * (shift * (capacity + 1) + jnp.minimum(found, capacity))
            chosen[at] = slots[term, 0, block]
            chosen[at + 1] = slots[term, 1, block]
            found = found + (owners[term, block] == ids[0]).astype(jnp.int32)
    for e in range(slots_dev * terms):
        owner = owners[e % terms, ids[0] * slots_dev + e // terms]
        count = seen[owner]
        seen[owner] = count + 1
        place[e] = lax.rem(ids[0] - owner + n_blk, n_blk) * capacity + count
    for e in range(2 * (capacity + 1)):
        mine[e] = 0
    found = jnp.int32(0)
    for e in range(slots_dev * terms):
        block, term = ids[0] * slots_dev + e // terms, e % terms
        at = 2 * jnp.minimum(found, capacity)
        mine[at] = slots[term, 0, block]
        mine[at + 1] = slots[term, 1, block]
        found = found + (owners[term, block] == lax.rem(ids[0] - far + n_blk, n_blk)).astype(jnp.int32)


def make_plan(ids, owners, slots, n_blk, far, slots_dev, terms, capacity):
    scalars = pl.BlockSpec(memory_space=pltpu.SMEM)
    return pl.pallas_call(
        functools.partial(plan_kernel, n_blk, far, slots_dev, terms, capacity),
        in_specs=[scalars] * 3,
        out_specs=[scalars] * 3,
        out_shape=[
            jax.ShapeDtypeStruct((2 * n_blk * (capacity + 1),), jnp.int32),
            jax.ShapeDtypeStruct((slots_dev * terms,), jnp.int32),
            jax.ShapeDtypeStruct((2 * (capacity + 1),), jnp.int32),
        ],
        scratch_shapes=[pltpu.SMEM((n_blk,), jnp.int32)],
        compiler_params=pltpu.CompilerParams(vmem_limit_bytes=mebi),
        name="make_plan",
    )(ids, owners, slots)


def banded_kernel(shifts, capacity, pieces, n_refs, size, ids, chosen, *rest):
    refs, rest = rest[:n_refs], rest[n_refs:]
    out_refs, (left_held, right_held, out_held, sems, out_sems) = rest[: len(shifts)], rest[len(shifts) :]
    halves, _, bands, rows, hidden = left_held.shape
    parts = hidden // size
    at_once = 2 if capacity % 2 == 0 else 1

    def copy(n, source):
        side, half, base, *_ = pieces[n]
        target = (left_held, right_held)[side].at[half, pl.ds(base, refs[source].shape[0])]
        return pltpu.make_async_copy(refs[source], target, sems.at[n])

    for n, (*_, on, off) in enumerate(pieces):
        if on == off:
            copy(n, on).start()
        else:

            @pl.when(ids[3] == 1)
            def _(n=n, on=on):
                copy(n, on).start()

            @pl.when(ids[3] == 0)
            def _(n=n, off=off):
                copy(n, off).start()

    for n, piece in enumerate(pieces):
        copy(n, piece[-1]).wait()

    def leave(n):
        return pltpu.make_async_copy(out_held.at[pl.ds(n * capacity, capacity)], out_refs[n], out_sems.at[n])

    for n, shift in enumerate(shifts):

        def one(turn, carry, n=n, shift=shift):
            group = lane_group((size, hidden), size)
            for term in [turn * at_once + t for t in range(at_once)]:
                at = 2 * (shift * (capacity + 1) + term)
                left_slot, right_slot = chosen[at], chosen[at + 1]
                for band in range(bands):
                    left = jnp.concatenate([left_held[h, left_slot, band] for h in range(halves)], axis=1)
                    apart = []
                    for h in range(halves):
                        right = right_held[h, right_slot, band]
                        apart += [jnp.where(group == part, right, jnp.zeros_like(right)) for part in range(parts)]
                    made = dot(left, jnp.concatenate(apart, axis=0))
                    out_held[n * capacity + term, band] = made.astype(jnp.bfloat16)
            return carry

        lax.fori_loop(0, capacity // at_once, one, 0)
        leave(n).start()
    for n in range(len(shifts)):
        leave(n).wait()


def banded_products(shifts, ids, chosen, operands, capacity, size):
    refs, pieces = [], []

    def index_of(array):
        for n, known in enumerate(refs):
            if known is array:
                return n
        refs.append(array)
        return len(refs) - 1

    slots = 0
    for both in operands:
        for side in range(2):
            for half, (on, off) in enumerate(both[side]):
                pieces.append((side, half, slots, index_of(on), index_of(off)))
        slots += both[0][0][0].shape[0]
    halves = len(operands[0][0])
    _, bands, rows, hidden = operands[0][0][0][0].shape
    count = len(shifts) * capacity
    anywhere = pl.BlockSpec(memory_space=pl.ANY)
    return pl.pallas_call(
        functools.partial(banded_kernel, shifts, capacity, tuple(pieces), len(refs), size),
        grid_spec=pltpu.PrefetchScalarGridSpec(
            num_scalar_prefetch=2,
            grid=(),
            in_specs=[anywhere] * len(refs),
            out_specs=[anywhere] * len(shifts),
            scratch_shapes=[
                pltpu.VMEM((halves, slots, bands, rows, hidden), jnp.bfloat16),
                pltpu.VMEM((halves, slots, bands, size, hidden), jnp.bfloat16),
                pltpu.VMEM((count, bands, rows, hidden), jnp.bfloat16),
                pltpu.SemaphoreType.DMA((len(pieces),)),
                pltpu.SemaphoreType.DMA((len(shifts),)),
            ],
        ),
        out_shape=[jax.ShapeDtypeStruct((capacity, bands, rows, hidden), jnp.bfloat16)] * len(shifts),
        compiler_params=pltpu.CompilerParams(vmem_limit_bytes=14 * mebi),
        cost_estimate=pl.CostEstimate(
            flops=2 * count * bands * rows * hidden * hidden * halves, bytes_accessed=1, transcendentals=0
        ),
        name="banded_products",
    )(ids, chosen, *refs)


def close_kernel(layer, last, spots, chunks, n_chan, n_sub, base, of, terms, capacity, ids, blocks, place, *rest):
    n_parts = len(spots)
    arrived, rest = rest[:n_parts], rest[n_parts:]
    cur_ref, gate_ref, w_out_ref = rest[:3]
    if last:
        out_ref, held, wide_out, sems, swap = rest[3:]
    else:
        chain_ref, w_ref, wide = rest[3:6]
        out_ref, next_gate_ref, sent_ref, *operand_refs, held, wide_out, sems, norm_ref, laid, turned, swap = rest[
            -(2 * chunks + 10) :
        ]
        left_refs, right_refs = operand_refs[:chunks], operand_refs[chunks:]
    step = pl.program_id(0)
    _, rows, cols, channels = cur_ref.shape
    _, bands, _, hidden = held.shape
    parts, size = hidden // bands, bands

    def arrival(n):
        shift, at = spots[n]
        target = held.at[pl.ds(shift * capacity, capacity), pl.ds(at, arrived[n].shape[1])]
        return pltpu.make_async_copy(arrived[n], target, sems.at[n])

    @pl.when(step == 0)
    def _():
        for n in range(n_parts):
            arrival(n).start()
        wide_out[...] = jnp.zeros_like(wide_out)
        for part in range(parts):
            for a in range(parts):
                at = (part * parts + a) * bands
                wide_out[at : at + bands, a * channels : (a + 1) * channels] = w_out_ref[
                    0, part * bands : (part + 1) * bands, :
                ]
        swap[...] = swap_matrix(16)
        for n in range(n_parts):
            arrival(n).wait()

    if not last:
        block = ids[0] * of + base + step
        row_alive = alive_rows(chain_ref, (blocks[0, block] * n_chan + ids[1]) * rows, rows)
        col_alive = alive_rows(chain_ref, (blocks[1, block] * n_sub + ids[2]) * cols, cols)
    half = 16
    by_row = [[] for _ in range(rows)]
    for row in range(0, rows, half):
        for band in range(0, bands, half):
            taken = pl.ds(band, half), pl.ds(row, half)
            total = held[(place[(base + step) * terms], *taken)].astype(jnp.float32)
            for t in range(1, terms):
                total = total + held[(place[(base + step) * terms + t], *taken)].astype(jnp.float32)
            moved = swapped(total.astype(jnp.bfloat16), swap)
            for r in range(half):
                by_row[row + r].append(moved[r])
    groups = rows // parts
    pieces = []
    for g in range(groups):
        block = jnp.concatenate([x for a in range(parts) for x in by_row[g * parts + a]]).T
        pieces.append(jnp.concatenate([block[p * cols : (p + 1) * cols] for p in range(parts)], axis=1))
    mixture = jnp.concatenate(pieces)
    together = (lane_group((hidden, hidden), size) == lax.broadcasted_iota(jnp.int32, (hidden, hidden), 0) // size)
    together = together.astype(jnp.float32).astype(jnp.bfloat16)
    average = dot(mixture, jnp.concatenate([together] * parts)) * (1.0 / hidden)
    centred = [mixture[:, p * hidden : (p + 1) * hidden].astype(jnp.float32) - average for p in range(parts)]
    squares = sum(c * c for c in centred)
    high = squares.astype(jnp.bfloat16)
    low = (squares - high.astype(jnp.float32)).astype(jnp.bfloat16)
    variance = dot(jnp.concatenate([high, low], axis=1), jnp.concatenate([together] * 2)) * (1.0 / hidden)
    scale = lax.rsqrt(variance + norm_epsilon)
    normed = jnp.concatenate([(c * scale).astype(jnp.bfloat16) for c in centred], axis=1)
    update = dot(normed, wide_out[...])
    for g in range(groups):
        taken = pl.ds(g * parts, parts)
        change = jnp.concatenate(
            [update[g * cols : (g + 1) * cols, a * channels : (a + 1) * channels] for a in range(parts)]
        )
        gate = gate_ref[0, taken].reshape(parts * cols, channels)
        current = cur_ref[0, taken].astype(jnp.float32).reshape(parts * cols, channels)
        result = (current + gate * change).astype(jnp.bfloat16)
        out_ref[0, taken] = result.reshape(parts, cols, channels)
        if not last:
            sent_ref[0, taken] = result.reshape(parts, cols, channels)
            norm_and_gate(result, row_alive, col_alive, g * parts, norm_ref, w_ref, next_gate_ref)
    if not last:
        open_layer(layer + 1, norm_ref[...], left_refs, right_refs, wide, laid, turned, swap)


def close_layer(
    layer, arrived, ids, blocks, place, current, gate, w_out, capacity, terms, chains, w_in, wide, last, bands, base, count, earlier
):
    flat, spots = [part for part, *_ in arrived], tuple((shift, at) for _, shift, at in arrived)
    n_blk = lax.axis_size("blk")
    slots, rows, cols, channels = current.shape
    hidden = w_out.shape[1]

    def layer_spec(array, index):
        return pl.BlockSpec((1,) + array.shape[1:], lambda s, *_: (index, 0, 0))

    in_specs = [pl.BlockSpec(memory_space=pl.ANY)] * len(flat)
    in_specs += slot_specs([current, gate], slots, base) + [layer_spec(w_out, layer)]
    operands = [*flat, current, gate, w_out]
    out_shape = [jax.ShapeDtypeStruct(current.shape, jnp.bfloat16)]
    scratch = [
        pltpu.VMEM((n_blk * capacity, sum(bands[layer]), rows, hidden), jnp.bfloat16),
        pltpu.VMEM((hidden // cols * hidden, hidden // cols * channels), jnp.bfloat16),
        pltpu.SemaphoreType.DMA((len(flat),)),
    ]
    if not last:
        operands += [chains, w_in, wide]
        in_specs += [pl.BlockSpec(chains.shape, lambda s, *_: (0, 0)), layer_spec(w_in, layer + 1)]
        in_specs += [pl.BlockSpec(wide.shape, lambda s, *_: (0, 0))]
        out_shape += [jax.ShapeDtypeStruct(current.shape, jnp.float32)]
        out_shape += [jax.ShapeDtypeStruct((count,) + current.shape[1:], jnp.bfloat16)]
        out_shape += operand_outputs(slots, count, cols, hidden, bands[layer + 1])
        scratch += [pltpu.VMEM((rows, cols, channels), jnp.bfloat16)] + operand_scratch(cols, rows, hidden)
    else:
        scratch += [pltpu.VMEM((256, 256), jnp.bfloat16)]
    more, more_specs, aliases = fill(out_shape, earlier, slots, 3 + len(operands))
    return pl.pallas_call(
        functools.partial(
            close_kernel,
            *(layer, last, spots, 0 if last else len(bands[layer + 1]), lax.axis_size("chan"), lax.axis_size("sub")),
            *(base, slots, terms, capacity),
        ),
        grid_spec=pltpu.PrefetchScalarGridSpec(
            num_scalar_prefetch=3,
            grid=(count,),
            in_specs=in_specs + more_specs,
            out_specs=slot_specs(out_shape, slots, base),
            scratch_shapes=scratch,
        ),
        out_shape=out_shape,
        input_output_aliases=aliases,
        compiler_params=pltpu.CompilerParams(vmem_limit_bytes=24 * mebi),
        cost_estimate=pl.CostEstimate(flops=1 << 33, bytes_accessed=1 << 20, transcendentals=0),
        name="close_layer",
    )(ids, blocks, place, *operands, *more)


def after(value, *others):
    return lax.optimization_barrier((value, *others))[0]


def exchange_bands_outgoing(left, right, over):
    both = ("chan", "sub")
    other = lax.ppermute(left, "sub", [(0, 1), (1, 0)])
    one = lax.ppermute(right, both, [(0, 2), (3, 1), (1, 0), (2, 3)])
    two = lax.ppermute(right, both, [(1, 2), (2, 1)])
    return [(other, left), (left, other)], [(one, one), (right, two)]


def exchange_bands_incoming(left, right, over):
    both = ("chan", "sub")
    one = lax.ppermute(left, both, [(1, 3), (2, 0), (0, 1), (3, 2)])
    other = lax.ppermute(right, "chan", [(0, 1), (1, 0)])
    two = lax.ppermute(after(one, other if over is None else over), both, [(0, 1), (3, 2)])
    return [(left, one), (one, two)], [(right, right), (other, other)]


def banded(pair, ids, blocks, owners, slot_of, chains, w_in, w_out, capacity, terms, n_blk):
    slots, rows, cols, channels = pair.shape
    hidden = w_out.shape[1]
    far = 1
    middle = n_blk // 2
    near = [s for s in (middle, *range(1, n_blk)) if s != far]
    near = [s for n, s in enumerate(near) if s not in near[:n]] + [0]
    layers = w_in.shape[0]
    current = pair
    bands = [[16, 16], [20, 12]]
    chosen, place, mine = make_plan(ids, owners, slot_of, n_blk, far, slots, terms, capacity)
    in_order = jnp.repeat(jnp.arange(capacity, dtype=jnp.int32), 2)
    half = slots // 2
    halves = [(0, half), (half, slots - half)]

    def over_blk(value, shift):
        return lax.ppermute(value, "blk", [(p, (p + shift) % n_blk) for p in range(n_blk)])

    for layer in range(layers):
        count = len(bands[layer])
        if layer == 0:
            raw = [over_blk(pair, far)]
            calls, wide = [None], spread_weights(w_in, 0, cols)
            for base, size in halves:
                calls.append(
                    open_operands(ids, blocks, pair, chains, w_in, wide, hidden, bands[0], base, size, calls[-1])
                )
            gate = calls[-1][0]
        else:
            raw = []
            for call in calls[1:]:
                raw.append(over_blk(after(call[2], *raw) if raw else call[2], far))
        operands = [call[-2 * count :] for call in calls[1:]]
        exchange = exchange_bands_incoming if layer % 2 else exchange_bands_outgoing
        arrived, by_shift = [], {}
        for chunk in range(count):
            if chunk == 0:
                exchanged = []
                over = operands[-1][count]
                for left, right in [(o[0], o[count]) for o in operands]:
                    if exchanged and layer % 2:
                        (_, (one, two)), (_, (other, _)) = exchanged[-1]
                        left, right = lax.optimization_barrier((left, right, one, other))[:2]
                        right = after(right, two)
                    elif exchanged:
                        ((other, _), _), ((one, _), (_, two)) = exchanged[-1]
                        left, right = lax.optimization_barrier((left, right, other, one, two))[:2]
                    exchanged.append(exchange(left, right, over))
            else:
                left, right = operands[-1][chunk], operands[-1][count + chunk]
                if layer % 2:
                    (_, (_, two)), (_, (other, _)) = exchanged[-1]
                    left, right = lax.optimization_barrier((left, right, two, other))[:2]
                else:
                    ((other, _), _), ((one, _), (_, two)) = exchanged[-1]
                    left = after(left, other)
                    right = after(right, one, two, made[-1])
                exchanged = [exchange(left, right, list(by_shift.values())[-1] if by_shift else made[-1])]
                ids = after(ids, *by_shift.values())
            made = banded_products(near, ids, chosen, exchanged, capacity, cols)
            start = sum(bands[layer][:chunk])
            for shift, part in zip(near, made):
                if shift:
                    part = over_blk(after(part, by_shift.get(shift, raw[-1])), shift)
                    by_shift[shift] = part
                arrived.append((part, shift, start))
            if chunk == 0:
                sources = list(lax.optimization_barrier((*raw, made[-1]))[:-1])
                far_left, far_right = far_operands(
                    layer, ids, blocks, mine, sources, chains, wide, far, capacity, slots, hidden
                )
        if layer % 2:
            far_left, far_right = lax.optimization_barrier((far_left, far_right, made[-1]))[:2]
        far_exchanged = [exchange(far_left, far_right, list(by_shift.values())[-1] if by_shift else made[-1])]
        (part,) = banded_products([0], ids, in_order, far_exchanged, capacity, cols)
        arrived.append((part, far, 0))
        last = layer == layers - 1
        calls = [None]
        if not last:
            wide = spread_weights(after(w_in, made[-1]), layer + 1, cols)
        for base, size in [(0, slots)] if last else halves:
            calls.append(
                close_layer(
                    *(layer, arrived, ids, blocks, place, current, gate, w_out, capacity, terms, chains, w_in, wide, last),
                    *(bands, base, size, calls[-1]),
                )
            )
        if last:
            return calls[-1][0]
        current, gate = calls[-1][:2]


def per_device(pair, block_list, term_owner, term_slots, chain_ids, w_in, w_out):
    n_blk = lax.axis_size("blk")
    n_chan = lax.axis_size("chan")
    n_sub = lax.axis_size("sub")
    position = lax.axis_index("blk")
    row_group = lax.axis_index("chan")
    col_group = lax.axis_index("sub")
    slots, rows, cols, channels = pair.shape
    hidden = w_out.shape[1]
    terms = term_owner.shape[1]
    capacity = max(2, -(-slots * terms // n_blk))
    fast = n_chan == 2 and n_sub == 2
    on_diagonal = (row_group == col_group).astype(jnp.int32)
    ids = jnp.stack([position, row_group, col_group, on_diagonal]).astype(jnp.int32)
    blocks = block_list.T
    owners = term_owner.T
    slot_of = jnp.transpose(term_slots, (1, 2, 0))
    chains = chain_ids.reshape(-1, 128)
    if fast and n_blk > 1 and rows == cols == 32 and channels == hidden == 128:
        return banded(pair, ids, blocks, owners, slot_of, chains, w_in, w_out, capacity, terms, n_blk)
    shifts = [n_blk // 2] + [s for s in range(1, n_blk) if s != n_blk // 2] + [0]

    def all_products(lefts, right):
        parts = [None] * n_blk
        for shift in shifts:
            made = term_products(shift, ids, owners, slot_of, lefts, right, capacity, slots, terms)
            if shift:
                pairs = [(p, (p + shift) % n_blk) for p in range(n_blk)]
                made = lax.ppermute(made, "blk", pairs)
            parts[shift] = made
        return parts

    def at_home(layer, parts, current, gate, at, of, into=None):
        last = layer == w_in.shape[0] - 1
        return home(
            layer, parts, ids, blocks, owners, current, gate, w_out, capacity, terms, at, of, chains, w_in, last, into
        )

    gate, left, *rights = first_operands(ids, blocks, pair, chains, w_in, hidden, 2 if fast else 1)
    lefts, chunks = exchange_outgoing(left, rights, n_chan, n_sub)
    count = len(chunks)
    made = [all_products(lefts, right) for right in chunks]
    homes = [at_home(0, parts, pair, gate, at, count) for at, parts in enumerate(made)]
    lefts, chunks = exchange_incoming([h[2] for h in homes], [h[3] for h in homes], n_chan, n_sub)
    made = [all_products(lefts, right) for right in chunks]
    out = None
    for at, parts in enumerate(made):
        (out,) = at_home(1, parts, homes[at][0], homes[at][1], at, count, into=out)
    return out


def solution(mesh):
    in_specs = (
        P(("groups", "blk"), "chan", "sub", None),
        P("groups", None),
        P("groups", None),
        P("groups", None, None),
        P("groups"),
        P(),
        P(),
    )
    out_specs = P(("groups", "blk"), "chan", "sub", None)
    return jax.shard_map(
        per_device, mesh=mesh, in_specs=in_specs, out_specs=out_specs, check_vma=False
    )
```

```python
import functools

import jax
import jax.numpy as jnp
from jax import lax
from jax.experimental import pallas as pl
from jax.experimental.pallas import tpu as pltpu
from jax.sharding import PartitionSpec as P

norm_epsilon = 1e-05
mebi = 1024 * 1024
vmem_limit = 56 * mebi


def sigmoid(values):
    return 0.5 + 0.5 * jnp.tanh(0.5 * values)


def layer_norm(values):
    values = values.astype(jnp.float32)
    centred = values - jnp.mean(values, axis=-1, keepdims=True)
    variance = jnp.mean(centred * centred, axis=-1, keepdims=True)
    return centred * lax.rsqrt(variance + norm_epsilon)


def alive_rows(chain_ref, start, size):
    lanes = chain_ref.shape[1]
    line = chain_ref[pl.ds(start // lanes, 1), :] >= 0
    spot = lax.broadcasted_iota(jnp.int32, (size, lanes), 0) + lax.rem(start, lanes)
    pick = jnp.logical_and(lax.broadcasted_iota(jnp.int32, (size, lanes), 1) == spot, line)
    return dot(pick.astype(jnp.float32).astype(jnp.bfloat16), jnp.ones((lanes, lanes), jnp.bfloat16))


def dot(a, b):
    return jnp.dot(a, b, preferred_element_type=jnp.float32)


def gated_pair(projected, mask, hidden):
    left = mask * sigmoid(projected[:, hidden : 2 * hidden]) * projected[:, :hidden]
    right = mask * sigmoid(projected[:, 3 * hidden : 4 * hidden]) * projected[:, 2 * hidden : 3 * hidden]
    return left.astype(jnp.bfloat16), right.astype(jnp.bfloat16)


def first_kernel(hidden, row_parts, n_chan, n_sub, ids, blocks, pair_ref, chain_ref, w_ref, gate_ref, left_ref, *rest):
    right_refs, (norm_ref, turned_ref) = rest[:row_parts], rest[row_parts:]
    slots = pl.num_programs(0)
    _, rows, cols, channels = pair_ref.shape
    block = ids[0] * slots + pl.program_id(0)
    row_alive = alive_rows(chain_ref, (blocks[0, block] * n_chan + ids[1]) * rows, rows)
    col_alive = alive_rows(chain_ref, (blocks[1, block] * n_sub + ids[2]) * cols, cols)
    group = max(1, 256 // cols)
    for start in range(0, rows, group):
        at = pl.ds(start, group)
        normed = layer_norm(pair_ref[0, at].reshape(group * cols, channels))
        norm_ref[pl.ds(start * cols, group * cols), :] = normed
        gate = sigmoid(dot(normed.astype(jnp.bfloat16), w_ref[0, :, 4 * hidden :]))
        gate_ref[0, at] = gate.reshape(group, cols, channels)
    for col in range(cols):
        turned_ref[col] = norm_ref[pl.ds(col, rows, stride=cols), :].astype(jnp.bfloat16)
    step = max(1, 128 // rows)
    part = rows // row_parts
    for start in range(0, cols, step):
        taken = turned_ref[start : start + step].reshape(step * rows, channels)
        projected = dot(taken, w_ref[0, :, : 4 * hidden])
        mask = col_alive[start : start + step][:, None, :] * row_alive[None, :, :]
        left, right = gated_pair(projected, mask.reshape(step * rows, -1), hidden)
        left_ref[0, start : start + step] = left.reshape(step, rows, hidden)
        right = right.reshape(step, rows, hidden)
        for p, right_ref in enumerate(right_refs):
            right_ref[0, start : start + step] = right[:, p * part : (p + 1) * part]


def first_operands(ids, blocks, pair, chains, w_in, hidden, row_parts):
    slots, rows, cols, channels = pair.shape
    part = rows // row_parts
    operand = jax.ShapeDtypeStruct((slots, cols, rows, hidden), jnp.bfloat16)
    right = jax.ShapeDtypeStruct((slots, cols, part, hidden), jnp.bfloat16)
    return pl.pallas_call(
        functools.partial(first_kernel, hidden, row_parts, lax.axis_size("chan"), lax.axis_size("sub")),
        grid_spec=pltpu.PrefetchScalarGridSpec(
            num_scalar_prefetch=2,
            grid=(slots,),
            in_specs=[
                pl.BlockSpec((1, rows, cols, channels), lambda s, *_: (s, 0, 0, 0)),
                pl.BlockSpec(chains.shape, lambda s, *_: (0, 0)),
                pl.BlockSpec((1,) + w_in.shape[1:], lambda s, *_: (0, 0, 0)),
            ],
            out_specs=[
                pl.BlockSpec((1, rows, cols, channels), lambda s, *_: (s, 0, 0, 0)),
                pl.BlockSpec((1, cols, rows, hidden), lambda s, *_: (s, 0, 0, 0)),
            ]
            + [pl.BlockSpec((1, cols, part, hidden), lambda s, *_: (s, 0, 0, 0))] * row_parts,
            scratch_shapes=[
                pltpu.VMEM((rows * cols, channels), jnp.float32),
                pltpu.VMEM((cols, rows, channels), jnp.bfloat16),
            ],
        ),
        out_shape=[jax.ShapeDtypeStruct(pair.shape, jnp.float32), operand] + [right] * row_parts,
        compiler_params=pltpu.CompilerParams(vmem_limit_bytes=vmem_limit),
        name="first_operands",
    )(ids, blocks, pair, chains, w_in)


def product_kernel(shift, n_blk, slots_dev, terms, capacity, pieces, n_refs, ids, owners, slots, *rest):
    refs = rest[:n_refs]
    out_ref, left_held, right_held, right_wide, chosen, sems = rest[n_refs:]
    step = pl.program_id(0)
    turn = lax.rem(step, 2)
    _, depth, n_i, hidden = left_held.shape
    n_j = right_wide.shape[1]

    @pl.when(step == 0)
    def _():
        target = lax.rem(ids[0] + shift, n_blk)
        for e in range(2 * capacity):
            chosen[e] = 0

        def scan(e, count):
            block, term = target * slots_dev + e // terms, lax.rem(e, terms)
            here = jnp.logical_and(owners[term, block] == ids[0], count < capacity)

            @pl.when(here)
            def _():
                chosen[2 * count] = slots[term, 0, block]
                chosen[2 * count + 1] = slots[term, 1, block]

            return count + here.astype(jnp.int32)

        lax.fori_loop(0, slots_dev * terms, scan, jnp.int32(0))

    def copy(n, term, buffer, source):
        side, _, _, k0, depth_of, i0, size = pieces[n]
        held = (left_held, right_held)[side]
        return pltpu.make_async_copy(
            refs[source].at[chosen[2 * term + side]],
            held.at[buffer, pl.ds(k0, depth_of), pl.ds(i0, size), :],
            sems.at[buffer, n],
        )

    def start(term, buffer):
        for n, (_, on, off, *_) in enumerate(pieces):
            if on == off:
                copy(n, term, buffer, on).start()
            else:

                @pl.when(ids[3] == 1)
                def _(n=n, on=on):
                    copy(n, term, buffer, on).start()

                @pl.when(ids[3] == 0)
                def _(n=n, off=off):
                    copy(n, term, buffer, off).start()

    @pl.when(step == 0)
    def _():
        start(0, 0)

    @pl.when(step + 1 < capacity)
    def _():
        start(step + 1, 1 - turn)

    for n, piece in enumerate(pieces):
        copy(n, step, turn, piece[1]).wait()

    span = 8

    def widen(n, carry):
        at = pl.ds(n * span, span)
        right_wide[at] = right_held[turn, at].astype(jnp.float32)
        return carry

    lax.fori_loop(0, depth // span, widen, 0)

    group = min(8, n_j)
    unroll = 4
    for j0 in range(0, n_j, group):

        def body(n, sums):
            for u in range(unroll):
                k = n * unroll + u
                left = left_held[turn, k].astype(jnp.float32).reshape(n_i // 8, 8, hidden)
                sums = tuple(
                    total + left * right_wide[k, pl.ds(j0 + j, 8, stride=0), :][None]
                    for j, total in enumerate(sums)
                )
            return sums

        zero = jnp.zeros((n_i // 8, 8, hidden), jnp.float32)
        sums = lax.fori_loop(0, depth // unroll, body, (zero,) * group)
        for j, total in enumerate(sums):
            out_ref[0, j0 + j] = total.reshape(n_i, hidden).astype(jnp.bfloat16)


def term_products(shift, ids, owners, slots, lefts, rights, capacity, slots_dev, terms):
    n_blk = lax.axis_size("blk")
    refs, pieces = [], []

    def index_of(array):
        for n, known in enumerate(refs):
            if known is array:
                return n
        refs.append(array)
        return len(refs) - 1

    for side, operands in ((0, lefts), (1, rights)):
        for on, off, k0, i0 in operands:
            pieces.append((side, index_of(on), index_of(off), k0, on.shape[1], i0, on.shape[2]))
    hidden = lefts[0][0].shape[3]
    n_i = max(p[5] + p[6] for p in pieces if p[0] == 0)
    n_j = max(p[5] + p[6] for p in pieces if p[0] == 1)
    depth = max(p[3] + p[4] for p in pieces)
    return pl.pallas_call(
        functools.partial(
            product_kernel, shift, n_blk, slots_dev, terms, capacity, tuple(pieces), len(refs)
        ),
        grid_spec=pltpu.PrefetchScalarGridSpec(
            num_scalar_prefetch=3,
            grid=(capacity,),
            in_specs=[pl.BlockSpec(memory_space=pl.ANY)] * len(refs),
            out_specs=pl.BlockSpec((1, n_j, n_i, hidden), lambda t, *_: (t, 0, 0, 0)),
            scratch_shapes=[
                pltpu.VMEM((2, depth, n_i, hidden), jnp.bfloat16),
                pltpu.VMEM((2, depth, n_j, hidden), jnp.bfloat16),
                pltpu.VMEM((depth, n_j, hidden), jnp.float32),
                pltpu.SMEM((2 * capacity,), jnp.int32),
                pltpu.SemaphoreType.DMA((2, len(pieces))),
            ],
        ),
        out_shape=jax.ShapeDtypeStruct((capacity, n_j, n_i, hidden), jnp.bfloat16),
        compiler_params=pltpu.CompilerParams(vmem_limit_bytes=vmem_limit),
        cost_estimate=pl.CostEstimate(
            flops=2 * capacity * n_i * n_j * depth * hidden * 100,
            bytes_accessed=capacity * (depth * (n_i + n_j) + n_i * n_j) * hidden * 2,
            transcendentals=0,
        ),
        name="term_products",
    )(ids, owners, slots, *refs)


def home_kernel(last, hidden, n_blk, n_chan, n_sub, at, of, slots_dev, terms, capacity, ids, blocks, owners, *rest):
    parts, rest = rest[:n_blk], rest[n_blk:]
    scratch, rest = rest[-5:], rest[:-5]
    held, turned, place, seen, sems = scratch
    cur_ref, gate_ref, w_out_ref = rest[:3]
    if last:
        out_ref = rest[-1]
    else:
        chain_ref, w_ref, out_ref, next_gate_ref, left_ref, right_ref = rest[3:]
    step = pl.program_id(0)
    _, rows, cols, channels = cur_ref.shape

    def arrival(shift):
        return pltpu.make_async_copy(parts[shift], held.at[pl.ds(shift * capacity, capacity)], sems.at[shift])

    @pl.when(step == 0)
    def _():
        for shift in range(n_blk):
            arrival(shift).start()
            seen[shift] = 0

        def scan(e, carry):
            owner = owners[lax.rem(e, terms), ids[0] * slots_dev + e // terms]
            shift = lax.rem(ids[0] - owner + n_blk, n_blk)
            count = seen[owner]
            seen[owner] = count + 1
            place[e] = shift * capacity + count
            return carry

        lax.fori_loop(0, slots_dev * terms, scan, jnp.int32(0))
        for shift in range(n_blk):
            arrival(shift).wait()

    if not last:
        block = ids[0] * slots_dev + step
        row_alive = alive_rows(chain_ref, (blocks[0, block] * n_chan + ids[1]) * rows, rows)
        col_alive = alive_rows(chain_ref, ((blocks[1, block] * n_sub + ids[2]) * of + at) * cols, cols)
    span = max(1, 128 // rows)
    for start in range(0, cols, span):
        taken = pl.ds(start, span)
        total = held[place[step * terms], taken].astype(jnp.float32)
        for t in range(1, terms):
            total = total + held[place[step * terms + t], taken].astype(jnp.float32)
        rounded = total.astype(jnp.bfloat16).astype(jnp.float32)
        turned[pl.ds(start * rows, span * rows), :] = rounded.reshape(span * rows, hidden)
    group = min(rows, max(1, 256 // cols))
    for start in range(0, rows, group):
        taken = pl.ds(start, group)
        mixture = jnp.concatenate(
            [turned[pl.ds(row, cols, stride=rows), :].astype(jnp.bfloat16) for row in range(start, start + group)]
        )
        update = dot(layer_norm(mixture).astype(jnp.bfloat16), w_out_ref[0])
        current = cur_ref[0, taken].astype(jnp.float32).reshape(group * cols, channels)
        gate = gate_ref[0, taken].reshape(group * cols, channels)
        result = (current + gate * update).astype(jnp.bfloat16)
        out_ref[0, taken] = result.reshape(group, cols, channels)
        if not last:
            normed = layer_norm(result).astype(jnp.bfloat16)
            projected = dot(normed, w_ref[0])
            next_gate_ref[0, taken] = sigmoid(projected[:, 4 * hidden :]).reshape(group, cols, channels)
            mask = row_alive[start : start + group][:, None, :] * col_alive[None, :, :]
            left, right = gated_pair(projected, mask.reshape(group * cols, channels), hidden)
            left_ref[0, taken] = left.reshape(group, cols, hidden)
            right_ref[0, taken] = right.reshape(group, cols, hidden)


def home(layer, parts, ids, blocks, owners, current, gate, w_out, capacity, terms, at, of, chains, w_in, last, into=None):
    n_blk = len(parts)
    slots, rows, _, channels = current.shape
    hidden = w_out.shape[1]
    cols = parts[0].shape[1]
    chunk = (1, rows, cols, channels)

    def chunk_spec(array):
        whole = array.shape[2] != cols
        return pl.BlockSpec(chunk, lambda s, *_: (s, 0, at if whole else 0, 0))

    def layer_spec(array, index):
        return pl.BlockSpec((1,) + array.shape[1:], lambda s, *_: (index, 0, 0))

    in_specs = [pl.BlockSpec(memory_space=pl.ANY)] * n_blk + [
        chunk_spec(current),
        chunk_spec(gate),
        layer_spec(w_out, layer),
    ]
    operands = [*parts, current, gate, w_out]
    aliases = {}
    if last:
        if into is not None:
            aliases = {3 + len(operands): 0}
            operands.append(into)
            in_specs.append(pl.BlockSpec(memory_space=pl.ANY))
        out_shape = [jax.ShapeDtypeStruct((slots, rows, cols * of, channels), jnp.bfloat16)]
        out_specs = [pl.BlockSpec(chunk, lambda s, *_: (s, 0, at, 0))]
    else:
        operands += [chains, w_in]
        in_specs += [pl.BlockSpec(chains.shape, lambda s, *_: (0, 0)), layer_spec(w_in, layer + 1)]
        small = (slots, rows, cols, channels)
        out_shape = [jax.ShapeDtypeStruct(small, t) for t in (jnp.bfloat16, jnp.float32, jnp.bfloat16, jnp.bfloat16)]
        out_specs = [pl.BlockSpec(chunk, lambda s, *_: (s, 0, 0, 0))] * 4
    return pl.pallas_call(
        functools.partial(
            home_kernel, last, hidden, n_blk, lax.axis_size("chan"), lax.axis_size("sub"), at, of, slots, terms, capacity
        ),
        grid_spec=pltpu.PrefetchScalarGridSpec(
            num_scalar_prefetch=3,
            grid=(slots,),
            in_specs=in_specs,
            out_specs=out_specs,
            scratch_shapes=[
                pltpu.VMEM((n_blk * capacity, cols, rows, hidden), jnp.bfloat16),
                pltpu.VMEM((rows * cols, hidden), jnp.float32),
                pltpu.SMEM((slots * terms,), jnp.int32),
                pltpu.SMEM((n_blk,), jnp.int32),
                pltpu.SemaphoreType.DMA((n_blk,)),
            ],
        ),
        out_shape=out_shape,
        input_output_aliases=aliases,
        compiler_params=pltpu.CompilerParams(vmem_limit_bytes=vmem_limit),
        cost_estimate=pl.CostEstimate(
            flops=2 * slots * rows * cols * channels * 6 * channels * 10,
            bytes_accessed=slots * rows * cols * channels * 16,
            transcendentals=0,
        ),
        name="home",
    )(ids, blocks, owners, *operands)


def exchange_outgoing(left, rights, n_chan, n_sub):
    if n_chan == 2 and n_sub == 2:
        both = ("chan", "sub")
        other_left = lax.ppermute(left, "sub", [(0, 1), (1, 0)])
        lefts = [(other_left, left, 0, 0), (left, other_left, left.shape[1], 0)]
        chunks = []
        for right in rights:
            if chunks:
                (one, *_), (_, two, *_) = chunks[-1]
                right, *_ = lax.optimization_barrier((right, one, two))
            one = lax.ppermute(right, both, [(0, 2), (3, 1), (1, 0), (2, 3)])
            two = lax.ppermute(right, both, [(1, 2), (2, 1)])
            chunks.append([(one, one, 0, 0), (right, two, right.shape[1], 0)])
        return lefts, chunks
    left = lax.all_gather(left, "sub", axis=1, tiled=True)
    right = jnp.concatenate(rights, axis=2)
    right = lax.all_gather(right, "chan", axis=2, tiled=True)
    right = lax.all_to_all(right, "sub", split_axis=2, concat_axis=1, tiled=True)
    cols = right.shape[2] // 2
    chunks = [right[:, :, :cols], right[:, :, cols:]]
    return [(left, left, 0, 0)], [[(r, r, 0, 0)] for r in chunks]


def exchange_incoming(lefts, rights, n_chan, n_sub):
    if n_chan == 2 and n_sub == 2:
        both = ("chan", "sub")
        left_pieces, chunks = [], []
        at = 0
        for left, right in zip(lefts, rights):
            depth = left.shape[1]
            one = lax.ppermute(left, both, [(1, 3), (2, 0), (0, 1), (3, 2)])
            two = lax.ppermute(one, both, [(0, 1), (3, 2)])
            left_pieces += [(left, one, 0, at), (one, two, depth, at)]
            other = lax.ppermute(right, "chan", [(0, 1), (1, 0)])
            chunks.append([(right, right, 0, 0), (other, other, depth, 0)])
            at += left.shape[2]
        return left_pieces, chunks
    left = lax.all_gather(jnp.concatenate(lefts, axis=2), "chan", axis=1, tiled=True)
    left = lax.all_gather(left, "sub", axis=2, tiled=True)
    size = left.shape[2] // n_chan
    left = lax.dynamic_slice_in_dim(left, lax.axis_index("chan") * size, size, 2)
    gathered = [lax.all_gather(right, "chan", axis=1, tiled=True) for right in rights]
    return [(left, left, 0, 0)], [[(r, r, 0, 0)] for r in gathered]


def lane_group(shape, size):
    return lax.broadcasted_iota(jnp.int32, shape, 1) // size


def spread_kernel(size, w_ref, wide_ref):
    hidden = w_ref.shape[1]
    parts = hidden // size
    for side in range(2):
        for kind in range(2):
            start = (2 * side + kind) * hidden
            weights = 0.5 * w_ref[0, :, start : start + hidden].astype(jnp.float32)
            group = lane_group(weights.shape, size)
            for part in range(parts):
                kept = jnp.where(group == part, weights, 0.0)
                at = ((side * parts + part) * 2 + kind) * hidden
                for a in range(parts):
                    moved = pltpu.roll(kept, ((a - part) % parts) * size, 1) if a != part else kept
                    wide_ref[a * hidden : (a + 1) * hidden, at : at + hidden] = moved.astype(jnp.bfloat16)


def spread_weights(w_in, layer, size):
    hidden = w_in.shape[1]
    parts = hidden // size
    shape = (parts * hidden, 4 * parts * hidden)
    return pl.pallas_call(
        functools.partial(spread_kernel, size),
        grid=(1,),
        in_specs=[pl.BlockSpec((1,) + w_in.shape[1:], lambda s: (layer, 0, 0))],
        out_specs=pl.BlockSpec(shape, lambda s: (0, 0)),
        out_shape=jax.ShapeDtypeStruct(shape, jnp.bfloat16),
        compiler_params=pltpu.CompilerParams(vmem_limit_bytes=16 * mebi),
        cost_estimate=pl.CostEstimate(flops=1 << 30, bytes_accessed=1 << 20, transcendentals=0),
        name="spread_weights",
    )(w_in)


def swap_matrix(half):
    shape = (half * half, half * half)
    to, of = lax.broadcasted_iota(jnp.int32, shape, 0), lax.broadcasted_iota(jnp.int32, shape, 1)
    same = jnp.logical_and(to // half == lax.rem(of, half), lax.rem(to, half) == of // half)
    return same.astype(jnp.float32).astype(jnp.bfloat16)


def swapped(values, swap_ref):
    half, _, lanes = values.shape
    moved = dot(swap_ref[...], values.reshape(half * half, lanes))
    return moved.astype(jnp.bfloat16).reshape(half, half, lanes)


def turn(taken, turned, swap_ref):
    half = 16
    for x in range(0, taken.shape[0], half):
        for y in range(0, taken.shape[1], half):
            turned[y : y + half, x : x + half] = swapped(taken[x : x + half, y : y + half], swap_ref)


def make_operand(side, taken, wide_ref, out_refs, laid, swap_ref):
    rows, size, hidden = taken.shape
    parts, bands, half = hidden // size, size, 16
    groups = rows // parts
    stacked = jnp.concatenate(
        [jnp.concatenate([taken[g * parts + a] for a in range(parts)], axis=1) for g in range(groups)], axis=0
    )
    for part in range(parts):
        at = (side * parts + part) * 2 * hidden
        made = dot(stacked, wide_ref[:, at : at + 2 * hidden])
        value = made[:, :hidden] * (1.0 + jnp.tanh(made[:, hidden:]))
        laid[side, :, part * size : (part + 1) * size, :] = value.astype(jnp.bfloat16).reshape(groups, size, hidden)
    blocks = [laid[side, g].T for g in range(groups)]
    starts = [sum(ref.shape[1] for ref in out_refs[:n]) for n in range(len(out_refs))]
    for first in range(0, bands, half):
        for row in range(0, rows, half):
            tiles = []
            for r in range(row, row + half):
                at = r % parts * bands + first
                tiles.append(blocks[r // parts][at : at + half])
            moved = swapped(jnp.stack(tiles), swap_ref)
            for start, ref in zip(starts, out_refs):
                low, high = max(start, first), min(start + ref.shape[1], first + half)
                if low < high:
                    ref[0, low - start : high - start, row : row + half] = moved[low - first : high - first]


def open_layer(layer, natural, left_refs, right_refs, wide, laid, turned, swap):
    turn(natural, turned, swap)
    for side, refs in ((0, left_refs), (1, right_refs)):
        make_operand(side, natural if side == layer % 2 else turned[...], wide, refs, laid, swap)


def norm_and_gate(values, row_alive, col_alive, at, norm_ref, w_ref=None, gate_ref=None):
    _, cols, channels = norm_ref.shape
    rows = values.shape[0] // cols
    normed = layer_norm(values)
    if gate_ref is not None:
        gate = sigmoid(dot(normed.astype(jnp.bfloat16), w_ref[0, :, -channels:]))
        gate_ref[0, pl.ds(at, rows)] = gate.reshape(rows, cols, channels)
    mask = row_alive[at : at + rows, None, :] * col_alive[None, :, :]
    norm_ref[pl.ds(at, rows)] = (normed.reshape(rows, cols, channels) * mask).astype(jnp.bfloat16)


def open_kernel(hidden, chunks, n_chan, n_sub, base, of, ids, blocks, pair_ref, chain_ref, w_ref, wide, *rest):
    gate_ref, *operand_refs, norm_ref, laid, turned, swap = rest[-(2 * chunks + 5) :]
    step = pl.program_id(0)
    _, rows, cols, channels = pair_ref.shape
    block = ids[0] * of + base + step

    @pl.when(step == 0)
    def _():
        swap[...] = swap_matrix(16)

    row_alive = alive_rows(chain_ref, (blocks[0, block] * n_chan + ids[1]) * rows, rows)
    col_alive = alive_rows(chain_ref, (blocks[1, block] * n_sub + ids[2]) * cols, cols)
    group = hidden // cols
    for at in range(0, rows, group):
        values = pair_ref[0, pl.ds(at, group)].reshape(group * cols, channels)
        norm_and_gate(values, row_alive, col_alive, at, norm_ref, w_ref, gate_ref)
    open_layer(0, norm_ref[...], operand_refs[:chunks], operand_refs[chunks:], wide, laid, turned, swap)


def operand_scratch(rows, size, hidden):
    parts = hidden // size
    return [
        pltpu.VMEM((2, rows // parts, parts * size, hidden), jnp.bfloat16),
        pltpu.VMEM((size, rows, hidden), jnp.bfloat16),
        pltpu.VMEM((256, 256), jnp.bfloat16),
    ]


def operand_outputs(slots, count, rows, hidden, bands):
    kept = [count if n == 0 else slots for n in range(len(bands))] * 2
    return [jax.ShapeDtypeStruct((k, b, rows, hidden), jnp.bfloat16) for k, b in zip(kept, bands * 2)]


def slot_specs(arrays, slots, base):
    def spec(array):
        offset = base if array.shape[0] == slots else 0
        return pl.BlockSpec((1,) + array.shape[1:], lambda s, *_: (s + offset, 0, 0, 0))

    return [spec(a) for a in arrays]


def fill(out_shape, earlier, slots, n_before):
    if earlier is None:
        return [], [], {}
    shared = [n for n, o in enumerate(out_shape) if o.shape[0] == slots]
    specs = [pl.BlockSpec(memory_space=pl.ANY)] * len(shared)
    return [earlier[n] for n in shared], specs, {n_before + k: n for k, n in enumerate(shared)}


def open_operands(ids, blocks, pair, chains, w_in, wide, hidden, bands, base, count, earlier):
    slots, rows, cols, channels = pair.shape
    out_shape = [jax.ShapeDtypeStruct(pair.shape, jnp.float32)] + operand_outputs(slots, count, rows, hidden, bands)
    more, more_specs, aliases = fill(out_shape, earlier, slots, 6)
    return pl.pallas_call(
        functools.partial(open_kernel, hidden, len(bands), lax.axis_size("chan"), lax.axis_size("sub"), base, slots),
        grid_spec=pltpu.PrefetchScalarGridSpec(
            num_scalar_prefetch=2,
            grid=(count,),
            in_specs=slot_specs([pair], slots, base)
            + [
                pl.BlockSpec(chains.shape, lambda s, *_: (0, 0)),
                pl.BlockSpec((1,) + w_in.shape[1:], lambda s, *_: (0, 0, 0)),
                pl.BlockSpec(wide.shape, lambda s, *_: (0, 0)),
            ]
            + more_specs,
            out_specs=slot_specs(out_shape, slots, base),
            scratch_shapes=[pltpu.VMEM((rows, cols, channels), jnp.bfloat16)] + operand_scratch(rows, cols, hidden),
        ),
        out_shape=out_shape,
        input_output_aliases=aliases,
        compiler_params=pltpu.CompilerParams(vmem_limit_bytes=18 * mebi),
        cost_estimate=pl.CostEstimate(flops=1 << 33, bytes_accessed=1 << 20, transcendentals=0),
        name="open_operands",
    )(ids, blocks, pair, chains, w_in, wide, *more)


def far_kernel(layer, n_blk, far, n_chan, n_sub, of, bases, ids, blocks, mine, *rest):
    sources, (chain_ref, wide, left_ref, right_ref, norm_ref, laid, turned, swap) = rest[:-8], rest[-8:]
    step = pl.program_id(0)
    rows, cols, channels = norm_ref.shape
    holder = lax.rem(ids[0] - far + n_blk, n_blk)

    @pl.when(step == 0)
    def _():
        swap[...] = swap_matrix(16)

    group = channels // cols
    for side, out_ref in ((0, left_ref), (1, right_ref)):
        slot = mine[2 * step + side]
        refs = sources[side * len(bases) : (side + 1) * len(bases)]
        block = holder * of + slot
        row_alive = alive_rows(chain_ref, (blocks[0, block] * n_chan + ids[1]) * rows, rows)
        col_alive = alive_rows(chain_ref, (blocks[1, block] * n_sub + ids[2]) * cols, cols)
        for at in range(0, rows, group):
            values = refs[0][0, pl.ds(at, group)]
            for base, ref in zip(bases[1:], refs[1:]):
                values = jnp.where(slot >= base, ref[0, pl.ds(at, group)], values)
            norm_and_gate(values.reshape(group * cols, channels), row_alive, col_alive, at, norm_ref)
        if side == layer % 2:
            make_operand(side, norm_ref[...], wide, [out_ref], laid, swap)
        else:
            turn(norm_ref[...], turned, swap)
            make_operand(side, turned[...], wide, [out_ref], laid, swap)


def far_operands(layer, ids, blocks, mine, sources, chains, wide, far, capacity, of, hidden):
    n_blk = lax.axis_size("blk")
    _, rows, cols, channels = sources[0].shape
    bases = [sum(a.shape[0] for a in sources[:n]) for n in range(len(sources))]

    def source_spec(side, base, size):
        def place(t, ids, blocks, mine):
            return jnp.clip(mine[2 * t + side] - base, 0, size - 1), 0, 0, 0

        return pl.BlockSpec((1, rows, cols, channels), place)

    in_specs = [source_spec(side, b, a.shape[0]) for side in range(2) for b, a in zip(bases, sources)]
    in_specs += [pl.BlockSpec(chains.shape, lambda t, *_: (0, 0)), pl.BlockSpec(wide.shape, lambda t, *_: (0, 0))]
    shape = (capacity, hidden // (hidden // cols), rows, hidden)
    return pl.pallas_call(
        functools.partial(
            far_kernel, layer, n_blk, far, lax.axis_size("chan"), lax.axis_size("sub"), of, tuple(bases)
        ),
        grid_spec=pltpu.PrefetchScalarGridSpec(
            num_scalar_prefetch=3,
            grid=(capacity,),
            in_specs=in_specs,
            out_specs=[pl.BlockSpec((1,) + shape[1:], lambda t, *_: (t, 0, 0, 0))] * 2,
            scratch_shapes=[pltpu.VMEM((rows, cols, channels), jnp.bfloat16)] + operand_scratch(rows, cols, hidden),
        ),
        out_shape=[jax.ShapeDtypeStruct(shape, jnp.bfloat16)] * 2,
        compiler_params=pltpu.CompilerParams(vmem_limit_bytes=14 * mebi),
        cost_estimate=pl.CostEstimate(flops=1 << 33, bytes_accessed=1 << 20, transcendentals=0),
        name="far_operands",
    )(ids, blocks, mine, *sources, *sources, chains, wide)


def plan_kernel(n_blk, far, slots_dev, terms, capacity, ids, owners, slots, chosen, place, mine, seen):
    for shift in range(n_blk):
        seen[shift] = 0
        target = lax.rem(ids[0] + shift, n_blk)
        for e in range(2 * (capacity + 1)):
            chosen[2 * shift * (capacity + 1) + e] = 0
        found = jnp.int32(0)
        for e in range(slots_dev * terms):
            block, term = target * slots_dev + e // terms, e % terms
            at = 2 * (shift * (capacity + 1) + jnp.minimum(found, capacity))
            chosen[at] = slots[term, 0, block]
            chosen[at + 1] = slots[term, 1, block]
            found = found + (owners[term, block] == ids[0]).astype(jnp.int32)
    for e in range(slots_dev * terms):
        owner = owners[e % terms, ids[0] * slots_dev + e // terms]
        count = seen[owner]
        seen[owner] = count + 1
        place[e] = lax.rem(ids[0] - owner + n_blk, n_blk) * capacity + count
    for e in range(2 * (capacity + 1)):
        mine[e] = 0
    found = jnp.int32(0)
    for e in range(slots_dev * terms):
        block, term = ids[0] * slots_dev + e // terms, e % terms
        at = 2 * jnp.minimum(found, capacity)
        mine[at] = slots[term, 0, block]
        mine[at + 1] = slots[term, 1, block]
        found = found + (owners[term, block] == lax.rem(ids[0] - far + n_blk, n_blk)).astype(jnp.int32)


def make_plan(ids, owners, slots, n_blk, far, slots_dev, terms, capacity):
    scalars = pl.BlockSpec(memory_space=pltpu.SMEM)
    return pl.pallas_call(
        functools.partial(plan_kernel, n_blk, far, slots_dev, terms, capacity),
        in_specs=[scalars] * 3,
        out_specs=[scalars] * 3,
        out_shape=[
            jax.ShapeDtypeStruct((2 * n_blk * (capacity + 1),), jnp.int32),
            jax.ShapeDtypeStruct((slots_dev * terms,), jnp.int32),
            jax.ShapeDtypeStruct((2 * (capacity + 1),), jnp.int32),
        ],
        scratch_shapes=[pltpu.SMEM((n_blk,), jnp.int32)],
        compiler_params=pltpu.CompilerParams(vmem_limit_bytes=mebi),
        name="make_plan",
    )(ids, owners, slots)


def banded_kernel(shifts, capacity, pieces, n_refs, size, ids, chosen, *rest):
    refs, rest = rest[:n_refs], rest[n_refs:]
    out_refs, (left_held, right_held, out_held, sems, out_sems) = rest[: len(shifts)], rest[len(shifts) :]
    halves, _, bands, rows, hidden = left_held.shape
    parts = hidden // size
    at_once = 2 if capacity % 2 == 0 else 1

    def copy(n, source):
        side, half, base, *_ = pieces[n]
        target = (left_held, right_held)[side].at[half, pl.ds(base, refs[source].shape[0])]
        return pltpu.make_async_copy(refs[source], target, sems.at[n])

    for n, (*_, on, off) in enumerate(pieces):
        if on == off:
            copy(n, on).start()
        else:

            @pl.when(ids[3] == 1)
            def _(n=n, on=on):
                copy(n, on).start()

            @pl.when(ids[3] == 0)
            def _(n=n, off=off):
                copy(n, off).start()

    for n, piece in enumerate(pieces):
        copy(n, piece[-1]).wait()

    def leave(n):
        return pltpu.make_async_copy(out_held.at[pl.ds(n * capacity, capacity)], out_refs[n], out_sems.at[n])

    for n, shift in enumerate(shifts):

        def one(turn, carry, n=n, shift=shift):
            group = lane_group((size, hidden), size)
            for term in [turn * at_once + t for t in range(at_once)]:
                at = 2 * (shift * (capacity + 1) + term)
                left_slot, right_slot = chosen[at], chosen[at + 1]
                for band in range(bands):
                    left = jnp.concatenate([left_held[h, left_slot, band] for h in range(halves)], axis=1)
                    apart = []
                    for h in range(halves):
                        right = right_held[h, right_slot, band]
                        apart += [jnp.where(group == part, right, jnp.zeros_like(right)) for part in range(parts)]
                    made = dot(left, jnp.concatenate(apart, axis=0))
                    out_held[n * capacity + term, band] = made.astype(jnp.bfloat16)
            return carry

        lax.fori_loop(0, capacity // at_once, one, 0)
        leave(n).start()
    for n in range(len(shifts)):
        leave(n).wait()


def banded_products(shifts, ids, chosen, operands, capacity, size):
    refs, pieces = [], []

    def index_of(array):
        for n, known in enumerate(refs):
            if known is array:
                return n
        refs.append(array)
        return len(refs) - 1

    slots = 0
    for both in operands:
        for side in range(2):
            for half, (on, off) in enumerate(both[side]):
                pieces.append((side, half, slots, index_of(on), index_of(off)))
        slots += both[0][0][0].shape[0]
    halves = len(operands[0][0])
    _, bands, rows, hidden = operands[0][0][0][0].shape
    count = len(shifts) * capacity
    anywhere = pl.BlockSpec(memory_space=pl.ANY)
    return pl.pallas_call(
        functools.partial(banded_kernel, shifts, capacity, tuple(pieces), len(refs), size),
        grid_spec=pltpu.PrefetchScalarGridSpec(
            num_scalar_prefetch=2,
            grid=(),
            in_specs=[anywhere] * len(refs),
            out_specs=[anywhere] * len(shifts),
            scratch_shapes=[
                pltpu.VMEM((halves, slots, bands, rows, hidden), jnp.bfloat16),
                pltpu.VMEM((halves, slots, bands, size, hidden), jnp.bfloat16),
                pltpu.VMEM((count, bands, rows, hidden), jnp.bfloat16),
                pltpu.SemaphoreType.DMA((len(pieces),)),
                pltpu.SemaphoreType.DMA((len(shifts),)),
            ],
        ),
        out_shape=[jax.ShapeDtypeStruct((capacity, bands, rows, hidden), jnp.bfloat16)] * len(shifts),
        compiler_params=pltpu.CompilerParams(vmem_limit_bytes=14 * mebi),
        cost_estimate=pl.CostEstimate(
            flops=2 * count * bands * rows * hidden * hidden * halves, bytes_accessed=1, transcendentals=0
        ),
        name="banded_products",
    )(ids, chosen, *refs)


def close_kernel(layer, last, spots, chunks, n_chan, n_sub, base, of, terms, capacity, ids, blocks, place, *rest):
    n_parts = len(spots)
    arrived, rest = rest[:n_parts], rest[n_parts:]
    cur_ref, gate_ref, w_out_ref = rest[:3]
    if last:
        out_ref, held, wide_out, sems, swap = rest[3:]
    else:
        chain_ref, w_ref, wide = rest[3:6]
        out_ref, next_gate_ref, sent_ref, *operand_refs, held, wide_out, sems, norm_ref, laid, turned, swap = rest[
            -(2 * chunks + 10) :
        ]
        left_refs, right_refs = operand_refs[:chunks], operand_refs[chunks:]
    step = pl.program_id(0)
    _, rows, cols, channels = cur_ref.shape
    _, bands, _, hidden = held.shape
    parts, size = hidden // bands, bands

    def arrival(n):
        shift, at = spots[n]
        target = held.at[pl.ds(shift * capacity, capacity), pl.ds(at, arrived[n].shape[1])]
        return pltpu.make_async_copy(arrived[n], target, sems.at[n])

    @pl.when(step == 0)
    def _():
        for n in range(n_parts):
            arrival(n).start()
        wide_out[...] = jnp.zeros_like(wide_out)
        for part in range(parts):
            for a in range(parts):
                at = (part * parts + a) * bands
                wide_out[at : at + bands, a * channels : (a + 1) * channels] = w_out_ref[
                    0, part * bands : (part + 1) * bands, :
                ]
        swap[...] = swap_matrix(16)
        for n in range(n_parts):
            arrival(n).wait()

    if not last:
        block = ids[0] * of + base + step
        row_alive = alive_rows(chain_ref, (blocks[0, block] * n_chan + ids[1]) * rows, rows)
        col_alive = alive_rows(chain_ref, (blocks[1, block] * n_sub + ids[2]) * cols, cols)
    half = 16
    by_row = [[] for _ in range(rows)]
    for row in range(0, rows, half):
        for band in range(0, bands, half):
            taken = pl.ds(band, half), pl.ds(row, half)
            total = held[(place[(base + step) * terms], *taken)].astype(jnp.float32)
            for t in range(1, terms):
                total = total + held[(place[(base + step) * terms + t], *taken)].astype(jnp.float32)
            moved = swapped(total.astype(jnp.bfloat16), swap)
            for r in range(half):
                by_row[row + r].append(moved[r])
    groups = rows // parts
    pieces = []
    for g in range(groups):
        block = jnp.concatenate([x for a in range(parts) for x in by_row[g * parts + a]]).T
        pieces.append(jnp.concatenate([block[p * cols : (p + 1) * cols] for p in range(parts)], axis=1))
    mixture = jnp.concatenate(pieces)
    together = (lane_group((hidden, hidden), size) == lax.broadcasted_iota(jnp.int32, (hidden, hidden), 0) // size)
    together = together.astype(jnp.float32).astype(jnp.bfloat16)
    average = dot(mixture, jnp.concatenate([together] * parts)) * (1.0 / hidden)
    centred = [mixture[:, p * hidden : (p + 1) * hidden].astype(jnp.float32) - average for p in range(parts)]
    squares = sum(c * c for c in centred)
    high = squares.astype(jnp.bfloat16)
    low = (squares - high.astype(jnp.float32)).astype(jnp.bfloat16)
    variance = dot(jnp.concatenate([high, low], axis=1), jnp.concatenate([together] * 2)) * (1.0 / hidden)
    scale = lax.rsqrt(variance + norm_epsilon)
    normed = jnp.concatenate([(c * scale).astype(jnp.bfloat16) for c in centred], axis=1)
    update = dot(normed, wide_out[...])
    for g in range(groups):
        taken = pl.ds(g * parts, parts)
        change = jnp.concatenate(
            [update[g * cols : (g + 1) * cols, a * channels : (a + 1) * channels] for a in range(parts)]
        )
        gate = gate_ref[0, taken].reshape(parts * cols, channels)
        current = cur_ref[0, taken].astype(jnp.float32).reshape(parts * cols, channels)
        result = (current + gate * change).astype(jnp.bfloat16)
        out_ref[0, taken] = result.reshape(parts, cols, channels)
        if not last:
            sent_ref[0, taken] = result.reshape(parts, cols, channels)
            norm_and_gate(result, row_alive, col_alive, g * parts, norm_ref, w_ref, next_gate_ref)
    if not last:
        open_layer(layer + 1, norm_ref[...], left_refs, right_refs, wide, laid, turned, swap)


def close_layer(
    layer, arrived, ids, blocks, place, current, gate, w_out, capacity, terms, chains, w_in, wide, last, bands, base, count, earlier
):
    flat, spots = [part for part, *_ in arrived], tuple((shift, at) for _, shift, at in arrived)
    n_blk = lax.axis_size("blk")
    slots, rows, cols, channels = current.shape
    hidden = w_out.shape[1]

    def layer_spec(array, index):
        return pl.BlockSpec((1,) + array.shape[1:], lambda s, *_: (index, 0, 0))

    in_specs = [pl.BlockSpec(memory_space=pl.ANY)] * len(flat)
    in_specs += slot_specs([current, gate], slots, base) + [layer_spec(w_out, layer)]
    operands = [*flat, current, gate, w_out]
    out_shape = [jax.ShapeDtypeStruct(current.shape, jnp.bfloat16)]
    scratch = [
        pltpu.VMEM((n_blk * capacity, sum(bands[layer]), rows, hidden), jnp.bfloat16),
        pltpu.VMEM((hidden // cols * hidden, hidden // cols * channels), jnp.bfloat16),
        pltpu.SemaphoreType.DMA((len(flat),)),
    ]
    if not last:
        operands += [chains, w_in, wide]
        in_specs += [pl.BlockSpec(chains.shape, lambda s, *_: (0, 0)), layer_spec(w_in, layer + 1)]
        in_specs += [pl.BlockSpec(wide.shape, lambda s, *_: (0, 0))]
        out_shape += [jax.ShapeDtypeStruct(current.shape, jnp.float32)]
        out_shape += [jax.ShapeDtypeStruct((count,) + current.shape[1:], jnp.bfloat16)]
        out_shape += operand_outputs(slots, count, cols, hidden, bands[layer + 1])
        scratch += [pltpu.VMEM((rows, cols, channels), jnp.bfloat16)] + operand_scratch(cols, rows, hidden)
    else:
        scratch += [pltpu.VMEM((256, 256), jnp.bfloat16)]
    more, more_specs, aliases = fill(out_shape, earlier, slots, 3 + len(operands))
    return pl.pallas_call(
        functools.partial(
            close_kernel,
            *(layer, last, spots, 0 if last else len(bands[layer + 1]), lax.axis_size("chan"), lax.axis_size("sub")),
            *(base, slots, terms, capacity),
        ),
        grid_spec=pltpu.PrefetchScalarGridSpec(
            num_scalar_prefetch=3,
            grid=(count,),
            in_specs=in_specs + more_specs,
            out_specs=slot_specs(out_shape, slots, base),
            scratch_shapes=scratch,
        ),
        out_shape=out_shape,
        input_output_aliases=aliases,
        compiler_params=pltpu.CompilerParams(vmem_limit_bytes=24 * mebi),
        cost_estimate=pl.CostEstimate(flops=1 << 33, bytes_accessed=1 << 20, transcendentals=0),
        name="close_layer",
    )(ids, blocks, place, *operands, *more)


def after(value, *others):
    return lax.optimization_barrier((value, *others))[0]


def exchange_bands_outgoing(left, right, over):
    both = ("chan", "sub")
    other = lax.ppermute(left, "sub", [(0, 1), (1, 0)])
    one = lax.ppermute(right, both, [(0, 2), (3, 1), (1, 0), (2, 3)])
    two = lax.ppermute(right, both, [(1, 2), (2, 1)])
    return [(other, left), (left, other)], [(one, one), (right, two)]


def exchange_bands_incoming(left, right, over):
    both = ("chan", "sub")
    one = lax.ppermute(left, both, [(1, 3), (2, 0), (0, 1), (3, 2)])
    other = lax.ppermute(right, "chan", [(0, 1), (1, 0)])
    two = lax.ppermute(after(one, other if over is None else over), both, [(0, 1), (3, 2)])
    return [(left, one), (one, two)], [(right, right), (other, other)]


def banded(pair, ids, blocks, owners, slot_of, chains, w_in, w_out, capacity, terms, n_blk):
    slots, rows, cols, channels = pair.shape
    hidden = w_out.shape[1]
    far = 1
    middle = n_blk // 2
    near = [s for s in (middle, *range(1, n_blk)) if s != far]
    near = [s for n, s in enumerate(near) if s not in near[:n]] + [0]
    layers = w_in.shape[0]
    current = pair
    bands = [[16, 16], [20, 12]]
    chosen, place, mine = make_plan(ids, owners, slot_of, n_blk, far, slots, terms, capacity)
    in_order = jnp.repeat(jnp.arange(capacity, dtype=jnp.int32), 2)
    half = slots // 2
    halves = [(0, half), (half, slots - half)]

    def over_blk(value, shift):
        return lax.ppermute(value, "blk", [(p, (p + shift) % n_blk) for p in range(n_blk)])

    for layer in range(layers):
        count = len(bands[layer])
        if layer == 0:
            raw = [over_blk(pair, far)]
            calls, wide = [None], spread_weights(w_in, 0, cols)
            for base, size in halves:
                calls.append(
                    open_operands(ids, blocks, pair, chains, w_in, wide, hidden, bands[0], base, size, calls[-1])
                )
            gate = calls[-1][0]
        else:
            raw = []
            for call in calls[1:]:
                raw.append(over_blk(after(call[2], *raw) if raw else call[2], far))
        operands = [call[-2 * count :] for call in calls[1:]]
        exchange = exchange_bands_incoming if layer % 2 else exchange_bands_outgoing
        arrived, by_shift = [], {}
        for chunk in range(count):
            if chunk == 0:
                exchanged = []
                over = operands[-1][count]
                for left, right in [(o[0], o[count]) for o in operands]:
                    if exchanged and layer % 2:
                        (_, (one, two)), (_, (other, _)) = exchanged[-1]
                        left, right = lax.optimization_barrier((left, right, one, other))[:2]
                        right = after(right, two)
                    elif exchanged:
                        ((other, _), _), ((one, _), (_, two)) = exchanged[-1]
                        left, right = lax.optimization_barrier((left, right, other, one, two))[:2]
                    exchanged.append(exchange(left, right, over))
            else:
                left, right = operands[-1][chunk], operands[-1][count + chunk]
                if layer % 2:
                    (_, (_, two)), (_, (other, _)) = exchanged[-1]
                    left, right = lax.optimization_barrier((left, right, two, other))[:2]
                else:
                    ((other, _), _), ((one, _), (_, two)) = exchanged[-1]
                    left = after(left, other)
                    right = after(right, one, two, made[-1])
                exchanged = [exchange(left, right, made[-1])]
                ids = after(ids, *by_shift.values())
            made = banded_products(near, ids, chosen, exchanged, capacity, cols)
            start = sum(bands[layer][:chunk])
            for shift, part in zip(near, made):
                if shift:
                    part = over_blk(after(part, by_shift.get(shift, raw[-1])), shift)
                    by_shift[shift] = part
                arrived.append((part, shift, start))
            if chunk == 0:
                sources = list(lax.optimization_barrier((*raw, made[-1]))[:-1])
                far_left, far_right = far_operands(
                    layer, ids, blocks, mine, sources, chains, wide, far, capacity, slots, hidden
                )
        far_exchanged = [exchange(far_left, far_right, list(by_shift.values())[-1] if by_shift else made[-1])]
        (part,) = banded_products([0], ids, in_order, far_exchanged, capacity, cols)
        arrived.append((part, far, 0))
        last = layer == layers - 1
        calls = [None]
        if not last:
            wide = spread_weights(after(w_in, made[-1]), layer + 1, cols)
        for base, size in [(0, slots)] if last else halves:
            calls.append(
                close_layer(
                    *(layer, arrived, ids, blocks, place, current, gate, w_out, capacity, terms, chains, w_in, wide, last),
                    *(bands, base, size, calls[-1]),
                )
            )
        if last:
            return calls[-1][0]
        current, gate = calls[-1][:2]


def per_device(pair, block_list, term_owner, term_slots, chain_ids, w_in, w_out):
    n_blk = lax.axis_size("blk")
    n_chan = lax.axis_size("chan")
    n_sub = lax.axis_size("sub")
    position = lax.axis_index("blk")
    row_group = lax.axis_index("chan")
    col_group = lax.axis_index("sub")
    slots, rows, cols, channels = pair.shape
    hidden = w_out.shape[1]
    terms = term_owner.shape[1]
    capacity = max(2, -(-slots * terms // n_blk))
    fast = n_chan == 2 and n_sub == 2
    on_diagonal = (row_group == col_group).astype(jnp.int32)
    ids = jnp.stack([position, row_group, col_group, on_diagonal]).astype(jnp.int32)
    blocks = block_list.T
    owners = term_owner.T
    slot_of = jnp.transpose(term_slots, (1, 2, 0))
    chains = chain_ids.reshape(-1, 128)
    if fast and n_blk > 1 and rows == cols == 32 and channels == hidden == 128:
        return banded(pair, ids, blocks, owners, slot_of, chains, w_in, w_out, capacity, terms, n_blk)
    shifts = [n_blk // 2] + [s for s in range(1, n_blk) if s != n_blk // 2] + [0]

    def all_products(lefts, right):
        parts = [None] * n_blk
        for shift in shifts:
            made = term_products(shift, ids, owners, slot_of, lefts, right, capacity, slots, terms)
            if shift:
                pairs = [(p, (p + shift) % n_blk) for p in range(n_blk)]
                made = lax.ppermute(made, "blk", pairs)
            parts[shift] = made
        return parts

    def at_home(layer, parts, current, gate, at, of, into=None):
        last = layer == w_in.shape[0] - 1
        return home(
            layer, parts, ids, blocks, owners, current, gate, w_out, capacity, terms, at, of, chains, w_in, last, into
        )

    gate, left, *rights = first_operands(ids, blocks, pair, chains, w_in, hidden, 2 if fast else 1)
    lefts, chunks = exchange_outgoing(left, rights, n_chan, n_sub)
    count = len(chunks)
    made = [all_products(lefts, right) for right in chunks]
    homes = [at_home(0, parts, pair, gate, at, count) for at, parts in enumerate(made)]
    lefts, chunks = exchange_incoming([h[2] for h in homes], [h[3] for h in homes], n_chan, n_sub)
    made = [all_products(lefts, right) for right in chunks]
    out = None
    for at, parts in enumerate(made):
        (out,) = at_home(1, parts, homes[at][0], homes[at][1], at, count, into=out)
    return out


def solution(mesh):
    in_specs = (
        P(("groups", "blk"), "chan", "sub", None),
        P("groups", None),
        P("groups", None),
        P("groups", None, None),
        P("groups"),
        P(),
        P(),
    )
    out_specs = P(("groups", "blk"), "chan", "sub", None)
    return jax.shard_map(
        per_device, mesh=mesh, in_specs=in_specs, out_specs=out_specs, check_vma=False
    )
```

```python
import functools

import jax
import jax.numpy as jnp
from jax import lax
from jax.experimental import pallas as pl
from jax.experimental.pallas import tpu as pltpu
from jax.sharding import PartitionSpec as P

norm_epsilon = 1e-05
mebi = 1024 * 1024
vmem_limit = 56 * mebi


def sigmoid(values):
    return 0.5 + 0.5 * jnp.tanh(0.5 * values)


def layer_norm(values):
    values = values.astype(jnp.float32)
    centred = values - jnp.mean(values, axis=-1, keepdims=True)
    variance = jnp.mean(centred * centred, axis=-1, keepdims=True)
    return centred * lax.rsqrt(variance + norm_epsilon)


def alive_rows(chain_ref, start, size):
    lanes = chain_ref.shape[1]
    line = chain_ref[pl.ds(start // lanes, 1), :] >= 0
    spot = lax.broadcasted_iota(jnp.int32, (size, lanes), 0) + lax.rem(start, lanes)
    pick = jnp.logical_and(lax.broadcasted_iota(jnp.int32, (size, lanes), 1) == spot, line)
    return dot(pick.astype(jnp.float32).astype(jnp.bfloat16), jnp.ones((lanes, lanes), jnp.bfloat16))


def dot(a, b):
    return jnp.dot(a, b, preferred_element_type=jnp.float32)


def gated_pair(projected, mask, hidden):
    left = mask * sigmoid(projected[:, hidden : 2 * hidden]) * projected[:, :hidden]
    right = mask * sigmoid(projected[:, 3 * hidden : 4 * hidden]) * projected[:, 2 * hidden : 3 * hidden]
    return left.astype(jnp.bfloat16), right.astype(jnp.bfloat16)


def first_kernel(hidden, row_parts, n_chan, n_sub, ids, blocks, pair_ref, chain_ref, w_ref, gate_ref, left_ref, *rest):
    right_refs, (norm_ref, turned_ref) = rest[:row_parts], rest[row_parts:]
    slots = pl.num_programs(0)
    _, rows, cols, channels = pair_ref.shape
    block = ids[0] * slots + pl.program_id(0)
    row_alive = alive_rows(chain_ref, (blocks[0, block] * n_chan + ids[1]) * rows, rows)
    col_alive = alive_rows(chain_ref, (blocks[1, block] * n_sub + ids[2]) * cols, cols)
    group = max(1, 256 // cols)
    for start in range(0, rows, group):
        at = pl.ds(start, group)
        normed = layer_norm(pair_ref[0, at].reshape(group * cols, channels))
        norm_ref[pl.ds(start * cols, group * cols), :] = normed
        gate = sigmoid(dot(normed.astype(jnp.bfloat16), w_ref[0, :, 4 * hidden :]))
        gate_ref[0, at] = gate.reshape(group, cols, channels)
    for col in range(cols):
        turned_ref[col] = norm_ref[pl.ds(col, rows, stride=cols), :].astype(jnp.bfloat16)
    step = max(1, 128 // rows)
    part = rows // row_parts
    for start in range(0, cols, step):
        taken = turned_ref[start : start + step].reshape(step * rows, channels)
        projected = dot(taken, w_ref[0, :, : 4 * hidden])
        mask = col_alive[start : start + step][:, None, :] * row_alive[None, :, :]
        left, right = gated_pair(projected, mask.reshape(step * rows, -1), hidden)
        left_ref[0, start : start + step] = left.reshape(step, rows, hidden)
        right = right.reshape(step, rows, hidden)
        for p, right_ref in enumerate(right_refs):
            right_ref[0, start : start + step] = right[:, p * part : (p + 1) * part]


def first_operands(ids, blocks, pair, chains, w_in, hidden, row_parts):
    slots, rows, cols, channels = pair.shape
    part = rows // row_parts
    operand = jax.ShapeDtypeStruct((slots, cols, rows, hidden), jnp.bfloat16)
    right = jax.ShapeDtypeStruct((slots, cols, part, hidden), jnp.bfloat16)
    return pl.pallas_call(
        functools.partial(first_kernel, hidden, row_parts, lax.axis_size("chan"), lax.axis_size("sub")),
        grid_spec=pltpu.PrefetchScalarGridSpec(
            num_scalar_prefetch=2,
            grid=(slots,),
            in_specs=[
                pl.BlockSpec((1, rows, cols, channels), lambda s, *_: (s, 0, 0, 0)),
                pl.BlockSpec(chains.shape, lambda s, *_: (0, 0)),
                pl.BlockSpec((1,) + w_in.shape[1:], lambda s, *_: (0, 0, 0)),
            ],
            out_specs=[
                pl.BlockSpec((1, rows, cols, channels), lambda s, *_: (s, 0, 0, 0)),
                pl.BlockSpec((1, cols, rows, hidden), lambda s, *_: (s, 0, 0, 0)),
            ]
            + [pl.BlockSpec((1, cols, part, hidden), lambda s, *_: (s, 0, 0, 0))] * row_parts,
            scratch_shapes=[
                pltpu.VMEM((rows * cols, channels), jnp.float32),
                pltpu.VMEM((cols, rows, channels), jnp.bfloat16),
            ],
        ),
        out_shape=[jax.ShapeDtypeStruct(pair.shape, jnp.float32), operand] + [right] * row_parts,
        compiler_params=pltpu.CompilerParams(vmem_limit_bytes=vmem_limit),
        name="first_operands",
    )(ids, blocks, pair, chains, w_in)


def product_kernel(shift, n_blk, slots_dev, terms, capacity, pieces, n_refs, ids, owners, slots, *rest):
    refs = rest[:n_refs]
    out_ref, left_held, right_held, right_wide, chosen, sems = rest[n_refs:]
    step = pl.program_id(0)
    turn = lax.rem(step, 2)
    _, depth, n_i, hidden = left_held.shape
    n_j = right_wide.shape[1]

    @pl.when(step == 0)
    def _():
        target = lax.rem(ids[0] + shift, n_blk)
        for e in range(2 * capacity):
            chosen[e] = 0

        def scan(e, count):
            block, term = target * slots_dev + e // terms, lax.rem(e, terms)
            here = jnp.logical_and(owners[term, block] == ids[0], count < capacity)

            @pl.when(here)
            def _():
                chosen[2 * count] = slots[term, 0, block]
                chosen[2 * count + 1] = slots[term, 1, block]

            return count + here.astype(jnp.int32)

        lax.fori_loop(0, slots_dev * terms, scan, jnp.int32(0))

    def copy(n, term, buffer, source):
        side, _, _, k0, depth_of, i0, size = pieces[n]
        held = (left_held, right_held)[side]
        return pltpu.make_async_copy(
            refs[source].at[chosen[2 * term + side]],
            held.at[buffer, pl.ds(k0, depth_of), pl.ds(i0, size), :],
            sems.at[buffer, n],
        )

    def start(term, buffer):
        for n, (_, on, off, *_) in enumerate(pieces):
            if on == off:
                copy(n, term, buffer, on).start()
            else:

                @pl.when(ids[3] == 1)
                def _(n=n, on=on):
                    copy(n, term, buffer, on).start()

                @pl.when(ids[3] == 0)
                def _(n=n, off=off):
                    copy(n, term, buffer, off).start()

    @pl.when(step == 0)
    def _():
        start(0, 0)

    @pl.when(step + 1 < capacity)
    def _():
        start(step + 1, 1 - turn)

    for n, piece in enumerate(pieces):
        copy(n, step, turn, piece[1]).wait()

    span = 8

    def widen(n, carry):
        at = pl.ds(n * span, span)
        right_wide[at] = right_held[turn, at].astype(jnp.float32)
        return carry

    lax.fori_loop(0, depth // span, widen, 0)

    group = min(8, n_j)
    unroll = 4
    for j0 in range(0, n_j, group):

        def body(n, sums):
            for u in range(unroll):
                k = n * unroll + u
                left = left_held[turn, k].astype(jnp.float32).reshape(n_i // 8, 8, hidden)
                sums = tuple(
                    total + left * right_wide[k, pl.ds(j0 + j, 8, stride=0), :][None]
                    for j, total in enumerate(sums)
                )
            return sums

        zero = jnp.zeros((n_i // 8, 8, hidden), jnp.float32)
        sums = lax.fori_loop(0, depth // unroll, body, (zero,) * group)
        for j, total in enumerate(sums):
            out_ref[0, j0 + j] = total.reshape(n_i, hidden).astype(jnp.bfloat16)


def term_products(shift, ids, owners, slots, lefts, rights, capacity, slots_dev, terms):
    n_blk = lax.axis_size("blk")
    refs, pieces = [], []

    def index_of(array):
        for n, known in enumerate(refs):
            if known is array:
                return n
        refs.append(array)
        return len(refs) - 1

    for side, operands in ((0, lefts), (1, rights)):
        for on, off, k0, i0 in operands:
            pieces.append((side, index_of(on), index_of(off), k0, on.shape[1], i0, on.shape[2]))
    hidden = lefts[0][0].shape[3]
    n_i = max(p[5] + p[6] for p in pieces if p[0] == 0)
    n_j = max(p[5] + p[6] for p in pieces if p[0] == 1)
    depth = max(p[3] + p[4] for p in pieces)
    return pl.pallas_call(
        functools.partial(
            product_kernel, shift, n_blk, slots_dev, terms, capacity, tuple(pieces), len(refs)
        ),
        grid_spec=pltpu.PrefetchScalarGridSpec(
            num_scalar_prefetch=3,
            grid=(capacity,),
            in_specs=[pl.BlockSpec(memory_space=pl.ANY)] * len(refs),
            out_specs=pl.BlockSpec((1, n_j, n_i, hidden), lambda t, *_: (t, 0, 0, 0)),
            scratch_shapes=[
                pltpu.VMEM((2, depth, n_i, hidden), jnp.bfloat16),
                pltpu.VMEM((2, depth, n_j, hidden), jnp.bfloat16),
                pltpu.VMEM((depth, n_j, hidden), jnp.float32),
                pltpu.SMEM((2 * capacity,), jnp.int32),
                pltpu.SemaphoreType.DMA((2, len(pieces))),
            ],
        ),
        out_shape=jax.ShapeDtypeStruct((capacity, n_j, n_i, hidden), jnp.bfloat16),
        compiler_params=pltpu.CompilerParams(vmem_limit_bytes=vmem_limit),
        cost_estimate=pl.CostEstimate(
            flops=2 * capacity * n_i * n_j * depth * hidden * 100,
            bytes_accessed=capacity * (depth * (n_i + n_j) + n_i * n_j) * hidden * 2,
            transcendentals=0,
        ),
        name="term_products",
    )(ids, owners, slots, *refs)


def home_kernel(last, hidden, n_blk, n_chan, n_sub, at, of, slots_dev, terms, capacity, ids, blocks, owners, *rest):
    parts, rest = rest[:n_blk], rest[n_blk:]
    scratch, rest = rest[-5:], rest[:-5]
    held, turned, place, seen, sems = scratch
    cur_ref, gate_ref, w_out_ref = rest[:3]
    if last:
        out_ref = rest[-1]
    else:
        chain_ref, w_ref, out_ref, next_gate_ref, left_ref, right_ref = rest[3:]
    step = pl.program_id(0)
    _, rows, cols, channels = cur_ref.shape

    def arrival(shift):
        return pltpu.make_async_copy(parts[shift], held.at[pl.ds(shift * capacity, capacity)], sems.at[shift])

    @pl.when(step == 0)
    def _():
        for shift in range(n_blk):
            arrival(shift).start()
            seen[shift] = 0

        def scan(e, carry):
            owner = owners[lax.rem(e, terms), ids[0] * slots_dev + e // terms]
            shift = lax.rem(ids[0] - owner + n_blk, n_blk)
            count = seen[owner]
            seen[owner] = count + 1
            place[e] = shift * capacity + count
            return carry

        lax.fori_loop(0, slots_dev * terms, scan, jnp.int32(0))
        for shift in range(n_blk):
            arrival(shift).wait()

    if not last:
        block = ids[0] * slots_dev + step
        row_alive = alive_rows(chain_ref, (blocks[0, block] * n_chan + ids[1]) * rows, rows)
        col_alive = alive_rows(chain_ref, ((blocks[1, block] * n_sub + ids[2]) * of + at) * cols, cols)
    span = max(1, 128 // rows)
    for start in range(0, cols, span):
        taken = pl.ds(start, span)
        total = held[place[step * terms], taken].astype(jnp.float32)
        for t in range(1, terms):
            total = total + held[place[step * terms + t], taken].astype(jnp.float32)
        rounded = total.astype(jnp.bfloat16).astype(jnp.float32)
        turned[pl.ds(start * rows, span * rows), :] = rounded.reshape(span * rows, hidden)
    group = min(rows, max(1, 256 // cols))
    for start in range(0, rows, group):
        taken = pl.ds(start, group)
        mixture = jnp.concatenate(
            [turned[pl.ds(row, cols, stride=rows), :].astype(jnp.bfloat16) for row in range(start, start + group)]
        )
        update = dot(layer_norm(mixture).astype(jnp.bfloat16), w_out_ref[0])
        current = cur_ref[0, taken].astype(jnp.float32).reshape(group * cols, channels)
        gate = gate_ref[0, taken].reshape(group * cols, channels)
        result = (current + gate * update).astype(jnp.bfloat16)
        out_ref[0, taken] = result.reshape(group, cols, channels)
        if not last:
            normed = layer_norm(result).astype(jnp.bfloat16)
            projected = dot(normed, w_ref[0])
            next_gate_ref[0, taken] = sigmoid(projected[:, 4 * hidden :]).reshape(group, cols, channels)
            mask = row_alive[start : start + group][:, None, :] * col_alive[None, :, :]
            left, right = gated_pair(projected, mask.reshape(group * cols, channels), hidden)
            left_ref[0, taken] = left.reshape(group, cols, hidden)
            right_ref[0, taken] = right.reshape(group, cols, hidden)


def home(layer, parts, ids, blocks, owners, current, gate, w_out, capacity, terms, at, of, chains, w_in, last, into=None):
    n_blk = len(parts)
    slots, rows, _, channels = current.shape
    hidden = w_out.shape[1]
    cols = parts[0].shape[1]
    chunk = (1, rows, cols, channels)

    def chunk_spec(array):
        whole = array.shape[2] != cols
        return pl.BlockSpec(chunk, lambda s, *_: (s, 0, at if whole else 0, 0))

    def layer_spec(array, index):
        return pl.BlockSpec((1,) + array.shape[1:], lambda s, *_: (index, 0, 0))

    in_specs = [pl.BlockSpec(memory_space=pl.ANY)] * n_blk + [
        chunk_spec(current),
        chunk_spec(gate),
        layer_spec(w_out, layer),
    ]
    operands = [*parts, current, gate, w_out]
    aliases = {}
    if last:
        if into is not None:
            aliases = {3 + len(operands): 0}
            operands.append(into)
            in_specs.append(pl.BlockSpec(memory_space=pl.ANY))
        out_shape = [jax.ShapeDtypeStruct((slots, rows, cols * of, channels), jnp.bfloat16)]
        out_specs = [pl.BlockSpec(chunk, lambda s, *_: (s, 0, at, 0))]
    else:
        operands += [chains, w_in]
        in_specs += [pl.BlockSpec(chains.shape, lambda s, *_: (0, 0)), layer_spec(w_in, layer + 1)]
        small = (slots, rows, cols, channels)
        out_shape = [jax.ShapeDtypeStruct(small, t) for t in (jnp.bfloat16, jnp.float32, jnp.bfloat16, jnp.bfloat16)]
        out_specs = [pl.BlockSpec(chunk, lambda s, *_: (s, 0, 0, 0))] * 4
    return pl.pallas_call(
        functools.partial(
            home_kernel, last, hidden, n_blk, lax.axis_size("chan"), lax.axis_size("sub"), at, of, slots, terms, capacity
        ),
        grid_spec=pltpu.PrefetchScalarGridSpec(
            num_scalar_prefetch=3,
            grid=(slots,),
            in_specs=in_specs,
            out_specs=out_specs,
            scratch_shapes=[
                pltpu.VMEM((n_blk * capacity, cols, rows, hidden), jnp.bfloat16),
                pltpu.VMEM((rows * cols, hidden), jnp.float32),
                pltpu.SMEM((slots * terms,), jnp.int32),
                pltpu.SMEM((n_blk,), jnp.int32),
                pltpu.SemaphoreType.DMA((n_blk,)),
            ],
        ),
        out_shape=out_shape,
        input_output_aliases=aliases,
        compiler_params=pltpu.CompilerParams(vmem_limit_bytes=vmem_limit),
        cost_estimate=pl.CostEstimate(
            flops=2 * slots * rows * cols * channels * 6 * channels * 10,
            bytes_accessed=slots * rows * cols * channels * 16,
            transcendentals=0,
        ),
        name="home",
    )(ids, blocks, owners, *operands)


def exchange_outgoing(left, rights, n_chan, n_sub):
    if n_chan == 2 and n_sub == 2:
        both = ("chan", "sub")
        other_left = lax.ppermute(left, "sub", [(0, 1), (1, 0)])
        lefts = [(other_left, left, 0, 0), (left, other_left, left.shape[1], 0)]
        chunks = []
        for right in rights:
            if chunks:
                (one, *_), (_, two, *_) = chunks[-1]
                right, *_ = lax.optimization_barrier((right, one, two))
            one = lax.ppermute(right, both, [(0, 2), (3, 1), (1, 0), (2, 3)])
            two = lax.ppermute(right, both, [(1, 2), (2, 1)])
            chunks.append([(one, one, 0, 0), (right, two, right.shape[1], 0)])
        return lefts, chunks
    left = lax.all_gather(left, "sub", axis=1, tiled=True)
    right = jnp.concatenate(rights, axis=2)
    right = lax.all_gather(right, "chan", axis=2, tiled=True)
    right = lax.all_to_all(right, "sub", split_axis=2, concat_axis=1, tiled=True)
    cols = right.shape[2] // 2
    chunks = [right[:, :, :cols], right[:, :, cols:]]
    return [(left, left, 0, 0)], [[(r, r, 0, 0)] for r in chunks]


def exchange_incoming(lefts, rights, n_chan, n_sub):
    if n_chan == 2 and n_sub == 2:
        both = ("chan", "sub")
        left_pieces, chunks = [], []
        at = 0
        for left, right in zip(lefts, rights):
            depth = left.shape[1]
            one = lax.ppermute(left, both, [(1, 3), (2, 0), (0, 1), (3, 2)])
            two = lax.ppermute(one, both, [(0, 1), (3, 2)])
            left_pieces += [(left, one, 0, at), (one, two, depth, at)]
            other = lax.ppermute(right, "chan", [(0, 1), (1, 0)])
            chunks.append([(right, right, 0, 0), (other, other, depth, 0)])
            at += left.shape[2]
        return left_pieces, chunks
    left = lax.all_gather(jnp.concatenate(lefts, axis=2), "chan", axis=1, tiled=True)
    left = lax.all_gather(left, "sub", axis=2, tiled=True)
    size = left.shape[2] // n_chan
    left = lax.dynamic_slice_in_dim(left, lax.axis_index("chan") * size, size, 2)
    gathered = [lax.all_gather(right, "chan", axis=1, tiled=True) for right in rights]
    return [(left, left, 0, 0)], [[(r, r, 0, 0)] for r in gathered]


def lane_group(shape, size):
    return lax.broadcasted_iota(jnp.int32, shape, 1) // size


def spread_kernel(size, w_ref, wide_ref):
    hidden = w_ref.shape[1]
    parts = hidden // size
    for side in range(2):
        for kind in range(2):
            start = (2 * side + kind) * hidden
            weights = 0.5 * w_ref[0, :, start : start + hidden].astype(jnp.float32)
            group = lane_group(weights.shape, size)
            for part in range(parts):
                kept = jnp.where(group == part, weights, 0.0)
                at = ((side * parts + part) * 2 + kind) * hidden
                for a in range(parts):
                    moved = pltpu.roll(kept, ((a - part) % parts) * size, 1) if a != part else kept
                    wide_ref[a * hidden : (a + 1) * hidden, at : at + hidden] = moved.astype(jnp.bfloat16)


def spread_weights(w_in, layer, size):
    hidden = w_in.shape[1]
    parts = hidden // size
    shape = (parts * hidden, 4 * parts * hidden)
    return pl.pallas_call(
        functools.partial(spread_kernel, size),
        grid=(1,),
        in_specs=[pl.BlockSpec((1,) + w_in.shape[1:], lambda s: (layer, 0, 0))],
        out_specs=pl.BlockSpec(shape, lambda s: (0, 0)),
        out_shape=jax.ShapeDtypeStruct(shape, jnp.bfloat16),
        compiler_params=pltpu.CompilerParams(vmem_limit_bytes=16 * mebi),
        cost_estimate=pl.CostEstimate(flops=1 << 30, bytes_accessed=1 << 20, transcendentals=0),
        name="spread_weights",
    )(w_in)


def swap_matrix(half):
    shape = (half * half, half * half)
    to, of = lax.broadcasted_iota(jnp.int32, shape, 0), lax.broadcasted_iota(jnp.int32, shape, 1)
    same = jnp.logical_and(to // half == lax.rem(of, half), lax.rem(to, half) == of // half)
    return same.astype(jnp.float32).astype(jnp.bfloat16)


def swapped(values, swap_ref):
    half, _, lanes = values.shape
    moved = dot(swap_ref[...], values.reshape(half * half, lanes))
    return moved.astype(jnp.bfloat16).reshape(half, half, lanes)


def turn(taken, turned, swap_ref):
    half = 16
    for x in range(0, taken.shape[0], half):
        for y in range(0, taken.shape[1], half):
            turned[y : y + half, x : x + half] = swapped(taken[x : x + half, y : y + half], swap_ref)


def make_operand(side, taken, wide_ref, out_refs, laid, swap_ref):
    rows, size, hidden = taken.shape
    parts, bands, half = hidden // size, size, 16
    groups = rows // parts
    stacked = jnp.concatenate(
        [jnp.concatenate([taken[g * parts + a] for a in range(parts)], axis=1) for g in range(groups)], axis=0
    )
    for part in range(parts):
        at = (side * parts + part) * 2 * hidden
        made = dot(stacked, wide_ref[:, at : at + 2 * hidden])
        value = made[:, :hidden] * (1.0 + jnp.tanh(made[:, hidden:]))
        laid[side, :, part * size : (part + 1) * size, :] = value.astype(jnp.bfloat16).reshape(groups, size, hidden)
    blocks = [laid[side, g].T for g in range(groups)]
    starts = [sum(ref.shape[1] for ref in out_refs[:n]) for n in range(len(out_refs))]
    for first in range(0, bands, half):
        for row in range(0, rows, half):
            tiles = []
            for r in range(row, row + half):
                at = r % parts * bands + first
                tiles.append(blocks[r // parts][at : at + half])
            moved = swapped(jnp.stack(tiles), swap_ref)
            for start, ref in zip(starts, out_refs):
                low, high = max(start, first), min(start + ref.shape[1], first + half)
                if low < high:
                    ref[0, low - start : high - start, row : row + half] = moved[low - first : high - first]


def open_layer(layer, natural, left_refs, right_refs, wide, laid, turned, swap):
    turn(natural, turned, swap)
    for side, refs in ((0, left_refs), (1, right_refs)):
        make_operand(side, natural if side == layer % 2 else turned[...], wide, refs, laid, swap)


def norm_and_gate(values, row_alive, col_alive, at, norm_ref, w_ref=None, gate_ref=None):
    _, cols, channels = norm_ref.shape
    rows = values.shape[0] // cols
    normed = layer_norm(values)
    if gate_ref is not None:
        gate = sigmoid(dot(normed.astype(jnp.bfloat16), w_ref[0, :, -channels:]))
        gate_ref[0, pl.ds(at, rows)] = gate.reshape(rows, cols, channels)
    mask = row_alive[at : at + rows, None, :] * col_alive[None, :, :]
    norm_ref[pl.ds(at, rows)] = (normed.reshape(rows, cols, channels) * mask).astype(jnp.bfloat16)


def open_kernel(hidden, chunks, n_chan, n_sub, base, of, ids, blocks, pair_ref, chain_ref, w_ref, wide, *rest):
    gate_ref, *operand_refs, norm_ref, laid, turned, swap = rest[-(2 * chunks + 5) :]
    step = pl.program_id(0)
    _, rows, cols, channels = pair_ref.shape
    block = ids[0] * of + base + step

    @pl.when(step == 0)
    def _():
        swap[...] = swap_matrix(16)

    row_alive = alive_rows(chain_ref, (blocks[0, block] * n_chan + ids[1]) * rows, rows)
    col_alive = alive_rows(chain_ref, (blocks[1, block] * n_sub + ids[2]) * cols, cols)
    group = hidden // cols
    for at in range(0, rows, group):
        values = pair_ref[0, pl.ds(at, group)].reshape(group * cols, channels)
        norm_and_gate(values, row_alive, col_alive, at, norm_ref, w_ref, gate_ref)
    open_layer(0, norm_ref[...], operand_refs[:chunks], operand_refs[chunks:], wide, laid, turned, swap)


def operand_scratch(rows, size, hidden):
    parts = hidden // size
    return [
        pltpu.VMEM((2, rows // parts, parts * size, hidden), jnp.bfloat16),
        pltpu.VMEM((size, rows, hidden), jnp.bfloat16),
        pltpu.VMEM((256, 256), jnp.bfloat16),
    ]


def operand_outputs(slots, count, rows, hidden, bands):
    kept = [count if n == 0 else slots for n in range(len(bands))] * 2
    return [jax.ShapeDtypeStruct((k, b, rows, hidden), jnp.bfloat16) for k, b in zip(kept, bands * 2)]


def slot_specs(arrays, slots, base):
    def spec(array):
        offset = base if array.shape[0] == slots else 0
        return pl.BlockSpec((1,) + array.shape[1:], lambda s, *_: (s + offset, 0, 0, 0))

    return [spec(a) for a in arrays]


def fill(out_shape, earlier, slots, n_before):
    if earlier is None:
        return [], [], {}
    shared = [n for n, o in enumerate(out_shape) if o.shape[0] == slots]
    specs = [pl.BlockSpec(memory_space=pl.ANY)] * len(shared)
    return [earlier[n] for n in shared], specs, {n_before + k: n for k, n in enumerate(shared)}


def open_operands(ids, blocks, pair, chains, w_in, wide, hidden, bands, base, count, earlier):
    slots, rows, cols, channels = pair.shape
    out_shape = [jax.ShapeDtypeStruct(pair.shape, jnp.float32)] + operand_outputs(slots, count, rows, hidden, bands)
    more, more_specs, aliases = fill(out_shape, earlier, slots, 6)
    return pl.pallas_call(
        functools.partial(open_kernel, hidden, len(bands), lax.axis_size("chan"), lax.axis_size("sub"), base, slots),
        grid_spec=pltpu.PrefetchScalarGridSpec(
            num_scalar_prefetch=2,
            grid=(count,),
            in_specs=slot_specs([pair], slots, base)
            + [
                pl.BlockSpec(chains.shape, lambda s, *_: (0, 0)),
                pl.BlockSpec((1,) + w_in.shape[1:], lambda s, *_: (0, 0, 0)),
                pl.BlockSpec(wide.shape, lambda s, *_: (0, 0)),
            ]
            + more_specs,
            out_specs=slot_specs(out_shape, slots, base),
            scratch_shapes=[pltpu.VMEM((rows, cols, channels), jnp.bfloat16)] + operand_scratch(rows, cols, hidden),
        ),
        out_shape=out_shape,
        input_output_aliases=aliases,
        compiler_params=pltpu.CompilerParams(vmem_limit_bytes=18 * mebi),
        cost_estimate=pl.CostEstimate(flops=1 << 33, bytes_accessed=1 << 20, transcendentals=0),
        name="open_operands",
    )(ids, blocks, pair, chains, w_in, wide, *more)


def far_kernel(layer, n_blk, far, n_chan, n_sub, of, bases, ids, blocks, mine, *rest):
    sources, (chain_ref, wide, left_ref, right_ref, norm_ref, laid, turned, swap) = rest[:-8], rest[-8:]
    step = pl.program_id(0)
    rows, cols, channels = norm_ref.shape
    holder = lax.rem(ids[0] - far + n_blk, n_blk)

    @pl.when(step == 0)
    def _():
        swap[...] = swap_matrix(16)

    group = channels // cols
    for side, out_ref in ((0, left_ref), (1, right_ref)):
        slot = mine[2 * step + side]
        refs = sources[side * len(bases) : (side + 1) * len(bases)]
        block = holder * of + slot
        row_alive = alive_rows(chain_ref, (blocks[0, block] * n_chan + ids[1]) * rows, rows)
        col_alive = alive_rows(chain_ref, (blocks[1, block] * n_sub + ids[2]) * cols, cols)
        for at in range(0, rows, group):
            values = refs[0][0, pl.ds(at, group)]
            for base, ref in zip(bases[1:], refs[1:]):
                values = jnp.where(slot >= base, ref[0, pl.ds(at, group)], values)
            norm_and_gate(values.reshape(group * cols, channels), row_alive, col_alive, at, norm_ref)
        if side == layer % 2:
            make_operand(side, norm_ref[...], wide, [out_ref], laid, swap)
        else:
            turn(norm_ref[...], turned, swap)
            make_operand(side, turned[...], wide, [out_ref], laid, swap)


def far_operands(layer, ids, blocks, mine, sources, chains, wide, far, capacity, of, hidden):
    n_blk = lax.axis_size("blk")
    _, rows, cols, channels = sources[0].shape
    bases = [sum(a.shape[0] for a in sources[:n]) for n in range(len(sources))]

    def source_spec(side, base, size):
        def place(t, ids, blocks, mine):
            return jnp.clip(mine[2 * t + side] - base, 0, size - 1), 0, 0, 0

        return pl.BlockSpec((1, rows, cols, channels), place)

    in_specs = [source_spec(side, b, a.shape[0]) for side in range(2) for b, a in zip(bases, sources)]
    in_specs += [pl.BlockSpec(chains.shape, lambda t, *_: (0, 0)), pl.BlockSpec(wide.shape, lambda t, *_: (0, 0))]
    shape = (capacity, hidden // (hidden // cols), rows, hidden)
    return pl.pallas_call(
        functools.partial(
            far_kernel, layer, n_blk, far, lax.axis_size("chan"), lax.axis_size("sub"), of, tuple(bases)
        ),
        grid_spec=pltpu.PrefetchScalarGridSpec(
            num_scalar_prefetch=3,
            grid=(capacity,),
            in_specs=in_specs,
            out_specs=[pl.BlockSpec((1,) + shape[1:], lambda t, *_: (t, 0, 0, 0))] * 2,
            scratch_shapes=[pltpu.VMEM((rows, cols, channels), jnp.bfloat16)] + operand_scratch(rows, cols, hidden),
        ),
        out_shape=[jax.ShapeDtypeStruct(shape, jnp.bfloat16)] * 2,
        compiler_params=pltpu.CompilerParams(vmem_limit_bytes=14 * mebi),
        cost_estimate=pl.CostEstimate(flops=1 << 33, bytes_accessed=1 << 20, transcendentals=0),
        name="far_operands",
    )(ids, blocks, mine, *sources, *sources, chains, wide)


def plan_kernel(n_blk, far, slots_dev, terms, capacity, ids, owners, slots, chosen, place, mine, seen):
    for shift in range(n_blk):
        seen[shift] = 0
        target = lax.rem(ids[0] + shift, n_blk)
        for e in range(2 * (capacity + 1)):
            chosen[2 * shift * (capacity + 1) + e] = 0
        found = jnp.int32(0)
        for e in range(slots_dev * terms):
            block, term = target * slots_dev + e // terms, e % terms
            at = 2 * (shift * (capacity + 1) + jnp.minimum(found, capacity))
            chosen[at] = slots[term, 0, block]
            chosen[at + 1] = slots[term, 1, block]
            found = found + (owners[term, block] == ids[0]).astype(jnp.int32)
    for e in range(slots_dev * terms):
        owner = owners[e % terms, ids[0] * slots_dev + e // terms]
        count = seen[owner]
        seen[owner] = count + 1
        place[e] = lax.rem(ids[0] - owner + n_blk, n_blk) * capacity + count
    for e in range(2 * (capacity + 1)):
        mine[e] = 0
    found = jnp.int32(0)
    for e in range(slots_dev * terms):
        block, term = ids[0] * slots_dev + e // terms, e % terms
        at = 2 * jnp.minimum(found, capacity)
        mine[at] = slots[term, 0, block]
        mine[at + 1] = slots[term, 1, block]
        found = found + (owners[term, block] == lax.rem(ids[0] - far + n_blk, n_blk)).astype(jnp.int32)


def make_plan(ids, owners, slots, n_blk, far, slots_dev, terms, capacity):
    scalars = pl.BlockSpec(memory_space=pltpu.SMEM)
    return pl.pallas_call(
        functools.partial(plan_kernel, n_blk, far, slots_dev, terms, capacity),
        in_specs=[scalars] * 3,
        out_specs=[scalars] * 3,
        out_shape=[
            jax.ShapeDtypeStruct((2 * n_blk * (capacity + 1),), jnp.int32),
            jax.ShapeDtypeStruct((slots_dev * terms,), jnp.int32),
            jax.ShapeDtypeStruct((2 * (capacity + 1),), jnp.int32),
        ],
        scratch_shapes=[pltpu.SMEM((n_blk,), jnp.int32)],
        compiler_params=pltpu.CompilerParams(vmem_limit_bytes=mebi),
        name="make_plan",
    )(ids, owners, slots)


def banded_kernel(shifts, capacity, pieces, n_refs, size, ids, chosen, *rest):
    refs, rest = rest[:n_refs], rest[n_refs:]
    out_refs, (left_held, right_held, out_held, sems, out_sems) = rest[: len(shifts)], rest[len(shifts) :]
    halves, _, bands, rows, hidden = left_held.shape
    parts = hidden // size
    at_once = 2 if capacity % 2 == 0 else 1

    def copy(n, source):
        side, half, base, *_ = pieces[n]
        target = (left_held, right_held)[side].at[half, pl.ds(base, refs[source].shape[0])]
        return pltpu.make_async_copy(refs[source], target, sems.at[n])

    for n, (*_, on, off) in enumerate(pieces):
        if on == off:
            copy(n, on).start()
        else:

            @pl.when(ids[3] == 1)
            def _(n=n, on=on):
                copy(n, on).start()

            @pl.when(ids[3] == 0)
            def _(n=n, off=off):
                copy(n, off).start()

    for n, piece in enumerate(pieces):
        copy(n, piece[-1]).wait()

    def leave(n):
        return pltpu.make_async_copy(out_held.at[pl.ds(n * capacity, capacity)], out_refs[n], out_sems.at[n])

    for n, shift in enumerate(shifts):

        def one(turn, carry, n=n, shift=shift):
            group = lane_group((size, hidden), size)
            for term in [turn * at_once + t for t in range(at_once)]:
                at = 2 * (shift * (capacity + 1) + term)
                left_slot, right_slot = chosen[at], chosen[at + 1]
                for band in range(bands):
                    left = jnp.concatenate([left_held[h, left_slot, band] for h in range(halves)], axis=1)
                    apart = []
                    for h in range(halves):
                        right = right_held[h, right_slot, band]
                        apart += [jnp.where(group == part, right, jnp.zeros_like(right)) for part in range(parts)]
                    made = dot(left, jnp.concatenate(apart, axis=0))
                    out_held[n * capacity + term, band] = made.astype(jnp.bfloat16)
            return carry

        lax.fori_loop(0, capacity // at_once, one, 0)
        leave(n).start()
    for n in range(len(shifts)):
        leave(n).wait()


def banded_products(shifts, ids, chosen, operands, capacity, size):
    refs, pieces = [], []

    def index_of(array):
        for n, known in enumerate(refs):
            if known is array:
                return n
        refs.append(array)
        return len(refs) - 1

    slots = 0
    for both in operands:
        for side in range(2):
            for half, (on, off) in enumerate(both[side]):
                pieces.append((side, half, slots, index_of(on), index_of(off)))
        slots += both[0][0][0].shape[0]
    halves = len(operands[0][0])
    _, bands, rows, hidden = operands[0][0][0][0].shape
    count = len(shifts) * capacity
    anywhere = pl.BlockSpec(memory_space=pl.ANY)
    return pl.pallas_call(
        functools.partial(banded_kernel, shifts, capacity, tuple(pieces), len(refs), size),
        grid_spec=pltpu.PrefetchScalarGridSpec(
            num_scalar_prefetch=2,
            grid=(),
            in_specs=[anywhere] * len(refs),
            out_specs=[anywhere] * len(shifts),
            scratch_shapes=[
                pltpu.VMEM((halves, slots, bands, rows, hidden), jnp.bfloat16),
                pltpu.VMEM((halves, slots, bands, size, hidden), jnp.bfloat16),
                pltpu.VMEM((count, bands, rows, hidden), jnp.bfloat16),
                pltpu.SemaphoreType.DMA((len(pieces),)),
                pltpu.SemaphoreType.DMA((len(shifts),)),
            ],
        ),
        out_shape=[jax.ShapeDtypeStruct((capacity, bands, rows, hidden), jnp.bfloat16)] * len(shifts),
        compiler_params=pltpu.CompilerParams(vmem_limit_bytes=14 * mebi),
        cost_estimate=pl.CostEstimate(
            flops=2 * count * bands * rows * hidden * hidden * halves, bytes_accessed=1, transcendentals=0
        ),
        name="banded_products",
    )(ids, chosen, *refs)


def close_kernel(layer, last, spots, chunks, n_chan, n_sub, base, of, terms, capacity, ids, blocks, place, *rest):
    n_parts = len(spots)
    arrived, rest = rest[:n_parts], rest[n_parts:]
    cur_ref, gate_ref, w_out_ref = rest[:3]
    if last:
        out_ref, held, wide_out, sems, swap = rest[3:]
    else:
        chain_ref, w_ref, wide = rest[3:6]
        out_ref, next_gate_ref, sent_ref, *operand_refs, held, wide_out, sems, norm_ref, laid, turned, swap = rest[
            -(2 * chunks + 10) :
        ]
        left_refs, right_refs = operand_refs[:chunks], operand_refs[chunks:]
    step = pl.program_id(0)
    _, rows, cols, channels = cur_ref.shape
    _, bands, _, hidden = held.shape
    parts, size = hidden // bands, bands

    def arrival(n):
        shift, at = spots[n]
        target = held.at[pl.ds(shift * capacity, capacity), pl.ds(at, arrived[n].shape[1])]
        return pltpu.make_async_copy(arrived[n], target, sems.at[n])

    @pl.when(step == 0)
    def _():
        for n in range(n_parts):
            arrival(n).start()
        wide_out[...] = jnp.zeros_like(wide_out)
        for part in range(parts):
            for a in range(parts):
                at = (part * parts + a) * bands
                wide_out[at : at + bands, a * channels : (a + 1) * channels] = w_out_ref[
                    0, part * bands : (part + 1) * bands, :
                ]
        swap[...] = swap_matrix(16)
        for n in range(n_parts):
            arrival(n).wait()

    if not last:
        block = ids[0] * of + base + step
        row_alive = alive_rows(chain_ref, (blocks[0, block] * n_chan + ids[1]) * rows, rows)
        col_alive = alive_rows(chain_ref, (blocks[1, block] * n_sub + ids[2]) * cols, cols)
    half = 16
    by_row = [[] for _ in range(rows)]
    for row in range(0, rows, half):
        for band in range(0, bands, half):
            taken = pl.ds(band, half), pl.ds(row, half)
            total = held[(place[(base + step) * terms], *taken)].astype(jnp.float32)
            for t in range(1, terms):
                total = total + held[(place[(base + step) * terms + t], *taken)].astype(jnp.float32)
            moved = swapped(total.astype(jnp.bfloat16), swap)
            for r in range(half):
                by_row[row + r].append(moved[r])
    groups = rows // parts
    pieces = []
    for g in range(groups):
        block = jnp.concatenate([x for a in range(parts) for x in by_row[g * parts + a]]).T
        pieces.append(jnp.concatenate([block[p * cols : (p + 1) * cols] for p in range(parts)], axis=1))
    mixture = jnp.concatenate(pieces)
    together = (lane_group((hidden, hidden), size) == lax.broadcasted_iota(jnp.int32, (hidden, hidden), 0) // size)
    together = together.astype(jnp.float32).astype(jnp.bfloat16)
    average = dot(mixture, jnp.concatenate([together] * parts)) * (1.0 / hidden)
    centred = [mixture[:, p * hidden : (p + 1) * hidden].astype(jnp.float32) - average for p in range(parts)]
    squares = sum(c * c for c in centred)
    high = squares.astype(jnp.bfloat16)
    low = (squares - high.astype(jnp.float32)).astype(jnp.bfloat16)
    variance = dot(jnp.concatenate([high, low], axis=1), jnp.concatenate([together] * 2)) * (1.0 / hidden)
    scale = lax.rsqrt(variance + norm_epsilon)
    normed = jnp.concatenate([(c * scale).astype(jnp.bfloat16) for c in centred], axis=1)
    update = dot(normed, wide_out[...])
    for g in range(groups):
        taken = pl.ds(g * parts, parts)
        change = jnp.concatenate(
            [update[g * cols : (g + 1) * cols, a * channels : (a + 1) * channels] for a in range(parts)]
        )
        gate = gate_ref[0, taken].reshape(parts * cols, channels)
        current = cur_ref[0, taken].astype(jnp.float32).reshape(parts * cols, channels)
        result = (current + gate * change).astype(jnp.bfloat16)
        out_ref[0, taken] = result.reshape(parts, cols, channels)
        if not last:
            sent_ref[0, taken] = result.reshape(parts, cols, channels)
            norm_and_gate(result, row_alive, col_alive, g * parts, norm_ref, w_ref, next_gate_ref)
    if not last:
        open_layer(layer + 1, norm_ref[...], left_refs, right_refs, wide, laid, turned, swap)


def close_layer(
    layer, arrived, ids, blocks, place, current, gate, w_out, capacity, terms, chains, w_in, wide, last, bands, base, count, earlier
):
    flat, spots = [part for part, *_ in arrived], tuple((shift, at) for _, shift, at in arrived)
    n_blk = lax.axis_size("blk")
    slots, rows, cols, channels = current.shape
    hidden = w_out.shape[1]

    def layer_spec(array, index):
        return pl.BlockSpec((1,) + array.shape[1:], lambda s, *_: (index, 0, 0))

    in_specs = [pl.BlockSpec(memory_space=pl.ANY)] * len(flat)
    in_specs += slot_specs([current, gate], slots, base) + [layer_spec(w_out, layer)]
    operands = [*flat, current, gate, w_out]
    out_shape = [jax.ShapeDtypeStruct(current.shape, jnp.bfloat16)]
    scratch = [
        pltpu.VMEM((n_blk * capacity, sum(bands[layer]), rows, hidden), jnp.bfloat16),
        pltpu.VMEM((hidden // cols * hidden, hidden // cols * channels), jnp.bfloat16),
        pltpu.SemaphoreType.DMA((len(flat),)),
    ]
    if not last:
        operands += [chains, w_in, wide]
        in_specs += [pl.BlockSpec(chains.shape, lambda s, *_: (0, 0)), layer_spec(w_in, layer + 1)]
        in_specs += [pl.BlockSpec(wide.shape, lambda s, *_: (0, 0))]
        out_shape += [jax.ShapeDtypeStruct(current.shape, jnp.float32)]
        out_shape += [jax.ShapeDtypeStruct((count,) + current.shape[1:], jnp.bfloat16)]
        out_shape += operand_outputs(slots, count, cols, hidden, bands[layer + 1])
        scratch += [pltpu.VMEM((rows, cols, channels), jnp.bfloat16)] + operand_scratch(cols, rows, hidden)
    else:
        scratch += [pltpu.VMEM((256, 256), jnp.bfloat16)]
    more, more_specs, aliases = fill(out_shape, earlier, slots, 3 + len(operands))
    return pl.pallas_call(
        functools.partial(
            close_kernel,
            *(layer, last, spots, 0 if last else len(bands[layer + 1]), lax.axis_size("chan"), lax.axis_size("sub")),
            *(base, slots, terms, capacity),
        ),
        grid_spec=pltpu.PrefetchScalarGridSpec(
            num_scalar_prefetch=3,
            grid=(count,),
            in_specs=in_specs + more_specs,
            out_specs=slot_specs(out_shape, slots, base),
            scratch_shapes=scratch,
        ),
        out_shape=out_shape,
        input_output_aliases=aliases,
        compiler_params=pltpu.CompilerParams(vmem_limit_bytes=24 * mebi),
        cost_estimate=pl.CostEstimate(flops=1 << 33, bytes_accessed=1 << 20, transcendentals=0),
        name="close_layer",
    )(ids, blocks, place, *operands, *more)


def after(value, *others):
    return lax.optimization_barrier((value, *others))[0]


def exchange_bands_outgoing(left, right, over):
    both = ("chan", "sub")
    other = lax.ppermute(left, "sub", [(0, 1), (1, 0)])
    one = lax.ppermute(right, both, [(0, 2), (3, 1), (1, 0), (2, 3)])
    two = lax.ppermute(right, both, [(1, 2), (2, 1)])
    return [(other, left), (left, other)], [(one, one), (right, two)]


def exchange_bands_incoming(left, right, over):
    both = ("chan", "sub")
    one = lax.ppermute(left, both, [(1, 3), (2, 0), (0, 1), (3, 2)])
    other = lax.ppermute(right, "chan", [(0, 1), (1, 0)])
    two = lax.ppermute(after(one, other if over is None else over), both, [(0, 1), (3, 2)])
    return [(left, one), (one, two)], [(right, right), (other, other)]


def banded(pair, ids, blocks, owners, slot_of, chains, w_in, w_out, capacity, terms, n_blk):
    slots, rows, cols, channels = pair.shape
    hidden = w_out.shape[1]
    far = 1
    middle = n_blk // 2
    near = [s for s in (middle, *range(1, n_blk)) if s != far]
    near = [s for n, s in enumerate(near) if s not in near[:n]] + [0]
    layers = w_in.shape[0]
    current = pair
    bands = [[16, 16], [20, 12]]
    chosen, place, mine = make_plan(ids, owners, slot_of, n_blk, far, slots, terms, capacity)
    in_order = jnp.repeat(jnp.arange(capacity, dtype=jnp.int32), 2)
    half = slots // 2
    halves = [(0, half), (half, slots - half)]

    def over_blk(value, shift):
        return lax.ppermute(value, "blk", [(p, (p + shift) % n_blk) for p in range(n_blk)])

    for layer in range(layers):
        count = len(bands[layer])
        if layer == 0:
            raw = [over_blk(pair, far)]
            calls, wide = [None], spread_weights(w_in, 0, cols)
            for base, size in halves:
                calls.append(
                    open_operands(ids, blocks, pair, chains, w_in, wide, hidden, bands[0], base, size, calls[-1])
                )
            gate = calls[-1][0]
        else:
            raw = []
            for call in calls[1:]:
                raw.append(over_blk(after(call[2], *raw) if raw else call[2], far))
        operands = [call[-2 * count :] for call in calls[1:]]
        exchange = exchange_bands_incoming if layer % 2 else exchange_bands_outgoing
        arrived, by_shift = [], {}
        for chunk in range(count):
            if chunk == 0:
                exchanged = []
                over = operands[-1][count]
                for left, right in [(o[0], o[count]) for o in operands]:
                    if exchanged and layer % 2:
                        (_, (one, two)), (_, (other, _)) = exchanged[-1]
                        left, right = lax.optimization_barrier((left, right, one, other))[:2]
                        right = after(right, two)
                    elif exchanged:
                        ((other, _), _), ((one, _), (_, two)) = exchanged[-1]
                        left, right = lax.optimization_barrier((left, right, other, one, two))[:2]
                    exchanged.append(exchange(left, right, over))
            else:
                left, right = operands[-1][chunk], operands[-1][count + chunk]
                if layer % 2:
                    (_, (_, two)), (_, (other, _)) = exchanged[-1]
                    left, right = lax.optimization_barrier((left, right, two, other))[:2]
                else:
                    ((other, _), _), ((one, _), (_, two)) = exchanged[-1]
                    left = after(left, other)
                    right = after(right, one, two, made[-1])
                exchanged = [exchange(left, right, list(by_shift.values())[-1] if by_shift else made[-1])]
                ids = after(ids, *by_shift.values())
            made = banded_products(near, ids, chosen, exchanged, capacity, cols)
            start = sum(bands[layer][:chunk])
            for shift, part in zip(near, made):
                if shift:
                    part = over_blk(after(part, by_shift.get(shift, raw[-1])), shift)
                    by_shift[shift] = part
                arrived.append((part, shift, start))
            if chunk == 0:
                sources = list(lax.optimization_barrier((*raw, made[-1]))[:-1])
                far_left, far_right = far_operands(
                    layer, ids, blocks, mine, sources, chains, wide, far, capacity, slots, hidden
                )
        far_exchanged = [exchange(far_left, far_right, list(by_shift.values())[-1] if by_shift else made[-1])]
        (part,) = banded_products([0], ids, in_order, far_exchanged, capacity, cols)
        arrived.append((part, far, 0))
        last = layer == layers - 1
        calls = [None]
        if not last:
            wide = spread_weights(after(w_in, made[-1]), layer + 1, cols)
        for base, size in [(0, slots)] if last else halves:
            calls.append(
                close_layer(
                    *(layer, arrived, ids, blocks, place, current, gate, w_out, capacity, terms, chains, w_in, wide, last),
                    *(bands, base, size, calls[-1]),
                )
            )
        if last:
            return calls[-1][0]
        current, gate = calls[-1][:2]


def per_device(pair, block_list, term_owner, term_slots, chain_ids, w_in, w_out):
    n_blk = lax.axis_size("blk")
    n_chan = lax.axis_size("chan")
    n_sub = lax.axis_size("sub")
    position = lax.axis_index("blk")
    row_group = lax.axis_index("chan")
    col_group = lax.axis_index("sub")
    slots, rows, cols, channels = pair.shape
    hidden = w_out.shape[1]
    terms = term_owner.shape[1]
    capacity = max(2, -(-slots * terms // n_blk))
    fast = n_chan == 2 and n_sub == 2
    on_diagonal = (row_group == col_group).astype(jnp.int32)
    ids = jnp.stack([position, row_group, col_group, on_diagonal]).astype(jnp.int32)
    blocks = block_list.T
    owners = term_owner.T
    slot_of = jnp.transpose(term_slots, (1, 2, 0))
    chains = chain_ids.reshape(-1, 128)
    if fast and n_blk > 1 and rows == cols == 32 and channels == hidden == 128:
        return banded(pair, ids, blocks, owners, slot_of, chains, w_in, w_out, capacity, terms, n_blk)
    shifts = [n_blk // 2] + [s for s in range(1, n_blk) if s != n_blk // 2] + [0]

    def all_products(lefts, right):
        parts = [None] * n_blk
        for shift in shifts:
            made = term_products(shift, ids, owners, slot_of, lefts, right, capacity, slots, terms)
            if shift:
                pairs = [(p, (p + shift) % n_blk) for p in range(n_blk)]
                made = lax.ppermute(made, "blk", pairs)
            parts[shift] = made
        return parts

    def at_home(layer, parts, current, gate, at, of, into=None):
        last = layer == w_in.shape[0] - 1
        return home(
            layer, parts, ids, blocks, owners, current, gate, w_out, capacity, terms, at, of, chains, w_in, last, into
        )

    gate, left, *rights = first_operands(ids, blocks, pair, chains, w_in, hidden, 2 if fast else 1)
    lefts, chunks = exchange_outgoing(left, rights, n_chan, n_sub)
    count = len(chunks)
    made = [all_products(lefts, right) for right in chunks]
    homes = [at_home(0, parts, pair, gate, at, count) for at, parts in enumerate(made)]
    lefts, chunks = exchange_incoming([h[2] for h in homes], [h[3] for h in homes], n_chan, n_sub)
    made = [all_products(lefts, right) for right in chunks]
    out = None
    for at, parts in enumerate(made):
        (out,) = at_home(1, parts, homes[at][0], homes[at][1], at, count, into=out)
    return out


def solution(mesh):
    in_specs = (
        P(("groups", "blk"), "chan", "sub", None),
        P("groups", None),
        P("groups", None),
        P("groups", None, None),
        P("groups"),
        P(),
        P(),
    )
    out_specs = P(("groups", "blk"), "chan", "sub", None)
    return jax.shard_map(
        per_device, mesh=mesh, in_specs=in_specs, out_specs=out_specs, check_vma=False
    )
```

```python
import functools

import jax
import jax.numpy as jnp
from jax import lax
from jax.experimental import pallas as pl
from jax.experimental.pallas import tpu as pltpu
from jax.sharding import PartitionSpec as P

norm_epsilon = 1e-05
mebi = 1024 * 1024
vmem_limit = 56 * mebi


def sigmoid(values):
    return 0.5 + 0.5 * jnp.tanh(0.5 * values)


def layer_norm(values):
    values = values.astype(jnp.float32)
    centred = values - jnp.mean(values, axis=-1, keepdims=True)
    variance = jnp.mean(centred * centred, axis=-1, keepdims=True)
    return centred * lax.rsqrt(variance + norm_epsilon)


def alive_rows(chain_ref, start, size):
    lanes = chain_ref.shape[1]
    line = chain_ref[pl.ds(start // lanes, 1), :] >= 0
    spot = lax.broadcasted_iota(jnp.int32, (size, lanes), 0) + lax.rem(start, lanes)
    pick = jnp.logical_and(lax.broadcasted_iota(jnp.int32, (size, lanes), 1) == spot, line)
    return dot(pick.astype(jnp.float32).astype(jnp.bfloat16), jnp.ones((lanes, lanes), jnp.bfloat16))


def dot(a, b):
    return jnp.dot(a, b, preferred_element_type=jnp.float32)


def gated_pair(projected, mask, hidden):
    left = mask * sigmoid(projected[:, hidden : 2 * hidden]) * projected[:, :hidden]
    right = mask * sigmoid(projected[:, 3 * hidden : 4 * hidden]) * projected[:, 2 * hidden : 3 * hidden]
    return left.astype(jnp.bfloat16), right.astype(jnp.bfloat16)


def first_kernel(hidden, row_parts, n_chan, n_sub, ids, blocks, pair_ref, chain_ref, w_ref, gate_ref, left_ref, *rest):
    right_refs, (norm_ref, turned_ref) = rest[:row_parts], rest[row_parts:]
    slots = pl.num_programs(0)
    _, rows, cols, channels = pair_ref.shape
    block = ids[0] * slots + pl.program_id(0)
    row_alive = alive_rows(chain_ref, (blocks[0, block] * n_chan + ids[1]) * rows, rows)
    col_alive = alive_rows(chain_ref, (blocks[1, block] * n_sub + ids[2]) * cols, cols)
    group = max(1, 256 // cols)
    for start in range(0, rows, group):
        at = pl.ds(start, group)
        normed = layer_norm(pair_ref[0, at].reshape(group * cols, channels))
        norm_ref[pl.ds(start * cols, group * cols), :] = normed
        gate = sigmoid(dot(normed.astype(jnp.bfloat16), w_ref[0, :, 4 * hidden :]))
        gate_ref[0, at] = gate.reshape(group, cols, channels)
    for col in range(cols):
        turned_ref[col] = norm_ref[pl.ds(col, rows, stride=cols), :].astype(jnp.bfloat16)
    step = max(1, 128 // rows)
    part = rows // row_parts
    for start in range(0, cols, step):
        taken = turned_ref[start : start + step].reshape(step * rows, channels)
        projected = dot(taken, w_ref[0, :, : 4 * hidden])
        mask = col_alive[start : start + step][:, None, :] * row_alive[None, :, :]
        left, right = gated_pair(projected, mask.reshape(step * rows, -1), hidden)
        left_ref[0, start : start + step] = left.reshape(step, rows, hidden)
        right = right.reshape(step, rows, hidden)
        for p, right_ref in enumerate(right_refs):
            right_ref[0, start : start + step] = right[:, p * part : (p + 1) * part]


def first_operands(ids, blocks, pair, chains, w_in, hidden, row_parts):
    slots, rows, cols, channels = pair.shape
    part = rows // row_parts
    operand = jax.ShapeDtypeStruct((slots, cols, rows, hidden), jnp.bfloat16)
    right = jax.ShapeDtypeStruct((slots, cols, part, hidden), jnp.bfloat16)
    return pl.pallas_call(
        functools.partial(first_kernel, hidden, row_parts, lax.axis_size("chan"), lax.axis_size("sub")),
        grid_spec=pltpu.PrefetchScalarGridSpec(
            num_scalar_prefetch=2,
            grid=(slots,),
            in_specs=[
                pl.BlockSpec((1, rows, cols, channels), lambda s, *_: (s, 0, 0, 0)),
                pl.BlockSpec(chains.shape, lambda s, *_: (0, 0)),
                pl.BlockSpec((1,) + w_in.shape[1:], lambda s, *_: (0, 0, 0)),
            ],
            out_specs=[
                pl.BlockSpec((1, rows, cols, channels), lambda s, *_: (s, 0, 0, 0)),
                pl.BlockSpec((1, cols, rows, hidden), lambda s, *_: (s, 0, 0, 0)),
            ]
            + [pl.BlockSpec((1, cols, part, hidden), lambda s, *_: (s, 0, 0, 0))] * row_parts,
            scratch_shapes=[
                pltpu.VMEM((rows * cols, channels), jnp.float32),
                pltpu.VMEM((cols, rows, channels), jnp.bfloat16),
            ],
        ),
        out_shape=[jax.ShapeDtypeStruct(pair.shape, jnp.float32), operand] + [right] * row_parts,
        compiler_params=pltpu.CompilerParams(vmem_limit_bytes=vmem_limit),
        name="first_operands",
    )(ids, blocks, pair, chains, w_in)


def product_kernel(shift, n_blk, slots_dev, terms, capacity, pieces, n_refs, ids, owners, slots, *rest):
    refs = rest[:n_refs]
    out_ref, left_held, right_held, right_wide, chosen, sems = rest[n_refs:]
    step = pl.program_id(0)
    turn = lax.rem(step, 2)
    _, depth, n_i, hidden = left_held.shape
    n_j = right_wide.shape[1]

    @pl.when(step == 0)
    def _():
        target = lax.rem(ids[0] + shift, n_blk)
        for e in range(2 * capacity):
            chosen[e] = 0

        def scan(e, count):
            block, term = target * slots_dev + e // terms, lax.rem(e, terms)
            here = jnp.logical_and(owners[term, block] == ids[0], count < capacity)

            @pl.when(here)
            def _():
                chosen[2 * count] = slots[term, 0, block]
                chosen[2 * count + 1] = slots[term, 1, block]

            return count + here.astype(jnp.int32)

        lax.fori_loop(0, slots_dev * terms, scan, jnp.int32(0))

    def copy(n, term, buffer, source):
        side, _, _, k0, depth_of, i0, size = pieces[n]
        held = (left_held, right_held)[side]
        return pltpu.make_async_copy(
            refs[source].at[chosen[2 * term + side]],
            held.at[buffer, pl.ds(k0, depth_of), pl.ds(i0, size), :],
            sems.at[buffer, n],
        )

    def start(term, buffer):
        for n, (_, on, off, *_) in enumerate(pieces):
            if on == off:
                copy(n, term, buffer, on).start()
            else:

                @pl.when(ids[3] == 1)
                def _(n=n, on=on):
                    copy(n, term, buffer, on).start()

                @pl.when(ids[3] == 0)
                def _(n=n, off=off):
                    copy(n, term, buffer, off).start()

    @pl.when(step == 0)
    def _():
        start(0, 0)

    @pl.when(step + 1 < capacity)
    def _():
        start(step + 1, 1 - turn)

    for n, piece in enumerate(pieces):
        copy(n, step, turn, piece[1]).wait()

    span = 8

    def widen(n, carry):
        at = pl.ds(n * span, span)
        right_wide[at] = right_held[turn, at].astype(jnp.float32)
        return carry

    lax.fori_loop(0, depth // span, widen, 0)

    group = min(8, n_j)
    unroll = 4
    for j0 in range(0, n_j, group):

        def body(n, sums):
            for u in range(unroll):
                k = n * unroll + u
                left = left_held[turn, k].astype(jnp.float32).reshape(n_i // 8, 8, hidden)
                sums = tuple(
                    total + left * right_wide[k, pl.ds(j0 + j, 8, stride=0), :][None]
                    for j, total in enumerate(sums)
                )
            return sums

        zero = jnp.zeros((n_i // 8, 8, hidden), jnp.float32)
        sums = lax.fori_loop(0, depth // unroll, body, (zero,) * group)
        for j, total in enumerate(sums):
            out_ref[0, j0 + j] = total.reshape(n_i, hidden).astype(jnp.bfloat16)


def term_products(shift, ids, owners, slots, lefts, rights, capacity, slots_dev, terms):
    n_blk = lax.axis_size("blk")
    refs, pieces = [], []

    def index_of(array):
        for n, known in enumerate(refs):
            if known is array:
                return n
        refs.append(array)
        return len(refs) - 1

    for side, operands in ((0, lefts), (1, rights)):
        for on, off, k0, i0 in operands:
            pieces.append((side, index_of(on), index_of(off), k0, on.shape[1], i0, on.shape[2]))
    hidden = lefts[0][0].shape[3]
    n_i = max(p[5] + p[6] for p in pieces if p[0] == 0)
    n_j = max(p[5] + p[6] for p in pieces if p[0] == 1)
    depth = max(p[3] + p[4] for p in pieces)
    return pl.pallas_call(
        functools.partial(
            product_kernel, shift, n_blk, slots_dev, terms, capacity, tuple(pieces), len(refs)
        ),
        grid_spec=pltpu.PrefetchScalarGridSpec(
            num_scalar_prefetch=3,
            grid=(capacity,),
            in_specs=[pl.BlockSpec(memory_space=pl.ANY)] * len(refs),
            out_specs=pl.BlockSpec((1, n_j, n_i, hidden), lambda t, *_: (t, 0, 0, 0)),
            scratch_shapes=[
                pltpu.VMEM((2, depth, n_i, hidden), jnp.bfloat16),
                pltpu.VMEM((2, depth, n_j, hidden), jnp.bfloat16),
                pltpu.VMEM((depth, n_j, hidden), jnp.float32),
                pltpu.SMEM((2 * capacity,), jnp.int32),
                pltpu.SemaphoreType.DMA((2, len(pieces))),
            ],
        ),
        out_shape=jax.ShapeDtypeStruct((capacity, n_j, n_i, hidden), jnp.bfloat16),
        compiler_params=pltpu.CompilerParams(vmem_limit_bytes=vmem_limit),
        cost_estimate=pl.CostEstimate(
            flops=2 * capacity * n_i * n_j * depth * hidden * 100,
            bytes_accessed=capacity * (depth * (n_i + n_j) + n_i * n_j) * hidden * 2,
            transcendentals=0,
        ),
        name="term_products",
    )(ids, owners, slots, *refs)


def home_kernel(last, hidden, n_blk, n_chan, n_sub, at, of, slots_dev, terms, capacity, ids, blocks, owners, *rest):
    parts, rest = rest[:n_blk], rest[n_blk:]
    scratch, rest = rest[-5:], rest[:-5]
    held, turned, place, seen, sems = scratch
    cur_ref, gate_ref, w_out_ref = rest[:3]
    if last:
        out_ref = rest[-1]
    else:
        chain_ref, w_ref, out_ref, next_gate_ref, left_ref, right_ref = rest[3:]
    step = pl.program_id(0)
    _, rows, cols, channels = cur_ref.shape

    def arrival(shift):
        return pltpu.make_async_copy(parts[shift], held.at[pl.ds(shift * capacity, capacity)], sems.at[shift])

    @pl.when(step == 0)
    def _():
        for shift in range(n_blk):
            arrival(shift).start()
            seen[shift] = 0

        def scan(e, carry):
            owner = owners[lax.rem(e, terms), ids[0] * slots_dev + e // terms]
            shift = lax.rem(ids[0] - owner + n_blk, n_blk)
            count = seen[owner]
            seen[owner] = count + 1
            place[e] = shift * capacity + count
            return carry

        lax.fori_loop(0, slots_dev * terms, scan, jnp.int32(0))
        for shift in range(n_blk):
            arrival(shift).wait()

    if not last:
        block = ids[0] * slots_dev + step
        row_alive = alive_rows(chain_ref, (blocks[0, block] * n_chan + ids[1]) * rows, rows)
        col_alive = alive_rows(chain_ref, ((blocks[1, block] * n_sub + ids[2]) * of + at) * cols, cols)
    span = max(1, 128 // rows)
    for start in range(0, cols, span):
        taken = pl.ds(start, span)
        total = held[place[step * terms], taken].astype(jnp.float32)
        for t in range(1, terms):
            total = total + held[place[step * terms + t], taken].astype(jnp.float32)
        rounded = total.astype(jnp.bfloat16).astype(jnp.float32)
        turned[pl.ds(start * rows, span * rows), :] = rounded.reshape(span * rows, hidden)
    group = min(rows, max(1, 256 // cols))
    for start in range(0, rows, group):
        taken = pl.ds(start, group)
        mixture = jnp.concatenate(
            [turned[pl.ds(row, cols, stride=rows), :].astype(jnp.bfloat16) for row in range(start, start + group)]
        )
        update = dot(layer_norm(mixture).astype(jnp.bfloat16), w_out_ref[0])
        current = cur_ref[0, taken].astype(jnp.float32).reshape(group * cols, channels)
        gate = gate_ref[0, taken].reshape(group * cols, channels)
        result = (current + gate * update).astype(jnp.bfloat16)
        out_ref[0, taken] = result.reshape(group, cols, channels)
        if not last:
            normed = layer_norm(result).astype(jnp.bfloat16)
            projected = dot(normed, w_ref[0])
            next_gate_ref[0, taken] = sigmoid(projected[:, 4 * hidden :]).reshape(group, cols, channels)
            mask = row_alive[start : start + group][:, None, :] * col_alive[None, :, :]
            left, right = gated_pair(projected, mask.reshape(group * cols, channels), hidden)
            left_ref[0, taken] = left.reshape(group, cols, hidden)
            right_ref[0, taken] = right.reshape(group, cols, hidden)


def home(layer, parts, ids, blocks, owners, current, gate, w_out, capacity, terms, at, of, chains, w_in, last, into=None):
    n_blk = len(parts)
    slots, rows, _, channels = current.shape
    hidden = w_out.shape[1]
    cols = parts[0].shape[1]
    chunk = (1, rows, cols, channels)

    def chunk_spec(array):
        whole = array.shape[2] != cols
        return pl.BlockSpec(chunk, lambda s, *_: (s, 0, at if whole else 0, 0))

    def layer_spec(array, index):
        return pl.BlockSpec((1,) + array.shape[1:], lambda s, *_: (index, 0, 0))

    in_specs = [pl.BlockSpec(memory_space=pl.ANY)] * n_blk + [
        chunk_spec(current),
        chunk_spec(gate),
        layer_spec(w_out, layer),
    ]
    operands = [*parts, current, gate, w_out]
    aliases = {}
    if last:
        if into is not None:
            aliases = {3 + len(operands): 0}
            operands.append(into)
            in_specs.append(pl.BlockSpec(memory_space=pl.ANY))
        out_shape = [jax.ShapeDtypeStruct((slots, rows, cols * of, channels), jnp.bfloat16)]
        out_specs = [pl.BlockSpec(chunk, lambda s, *_: (s, 0, at, 0))]
    else:
        operands += [chains, w_in]
        in_specs += [pl.BlockSpec(chains.shape, lambda s, *_: (0, 0)), layer_spec(w_in, layer + 1)]
        small = (slots, rows, cols, channels)
        out_shape = [jax.ShapeDtypeStruct(small, t) for t in (jnp.bfloat16, jnp.float32, jnp.bfloat16, jnp.bfloat16)]
        out_specs = [pl.BlockSpec(chunk, lambda s, *_: (s, 0, 0, 0))] * 4
    return pl.pallas_call(
        functools.partial(
            home_kernel, last, hidden, n_blk, lax.axis_size("chan"), lax.axis_size("sub"), at, of, slots, terms, capacity
        ),
        grid_spec=pltpu.PrefetchScalarGridSpec(
            num_scalar_prefetch=3,
            grid=(slots,),
            in_specs=in_specs,
            out_specs=out_specs,
            scratch_shapes=[
                pltpu.VMEM((n_blk * capacity, cols, rows, hidden), jnp.bfloat16),
                pltpu.VMEM((rows * cols, hidden), jnp.float32),
                pltpu.SMEM((slots * terms,), jnp.int32),
                pltpu.SMEM((n_blk,), jnp.int32),
                pltpu.SemaphoreType.DMA((n_blk,)),
            ],
        ),
        out_shape=out_shape,
        input_output_aliases=aliases,
        compiler_params=pltpu.CompilerParams(vmem_limit_bytes=vmem_limit),
        cost_estimate=pl.CostEstimate(
            flops=2 * slots * rows * cols * channels * 6 * channels * 10,
            bytes_accessed=slots * rows * cols * channels * 16,
            transcendentals=0,
        ),
        name="home",
    )(ids, blocks, owners, *operands)


def exchange_outgoing(left, rights, n_chan, n_sub):
    if n_chan == 2 and n_sub == 2:
        both = ("chan", "sub")
        other_left = lax.ppermute(left, "sub", [(0, 1), (1, 0)])
        lefts = [(other_left, left, 0, 0), (left, other_left, left.shape[1], 0)]
        chunks = []
        for right in rights:
            if chunks:
                (one, *_), (_, two, *_) = chunks[-1]
                right, *_ = lax.optimization_barrier((right, one, two))
            one = lax.ppermute(right, both, [(0, 2), (3, 1), (1, 0), (2, 3)])
            two = lax.ppermute(right, both, [(1, 2), (2, 1)])
            chunks.append([(one, one, 0, 0), (right, two, right.shape[1], 0)])
        return lefts, chunks
    left = lax.all_gather(left, "sub", axis=1, tiled=True)
    right = jnp.concatenate(rights, axis=2)
    right = lax.all_gather(right, "chan", axis=2, tiled=True)
    right = lax.all_to_all(right, "sub", split_axis=2, concat_axis=1, tiled=True)
    cols = right.shape[2] // 2
    chunks = [right[:, :, :cols], right[:, :, cols:]]
    return [(left, left, 0, 0)], [[(r, r, 0, 0)] for r in chunks]


def exchange_incoming(lefts, rights, n_chan, n_sub):
    if n_chan == 2 and n_sub == 2:
        both = ("chan", "sub")
        left_pieces, chunks = [], []
        at = 0
        for left, right in zip(lefts, rights):
            depth = left.shape[1]
            one = lax.ppermute(left, both, [(1, 3), (2, 0), (0, 1), (3, 2)])
            two = lax.ppermute(one, both, [(0, 1), (3, 2)])
            left_pieces += [(left, one, 0, at), (one, two, depth, at)]
            other = lax.ppermute(right, "chan", [(0, 1), (1, 0)])
            chunks.append([(right, right, 0, 0), (other, other, depth, 0)])
            at += left.shape[2]
        return left_pieces, chunks
    left = lax.all_gather(jnp.concatenate(lefts, axis=2), "chan", axis=1, tiled=True)
    left = lax.all_gather(left, "sub", axis=2, tiled=True)
    size = left.shape[2] // n_chan
    left = lax.dynamic_slice_in_dim(left, lax.axis_index("chan") * size, size, 2)
    gathered = [lax.all_gather(right, "chan", axis=1, tiled=True) for right in rights]
    return [(left, left, 0, 0)], [[(r, r, 0, 0)] for r in gathered]


def lane_group(shape, size):
    return lax.broadcasted_iota(jnp.int32, shape, 1) // size


def spread_kernel(size, w_ref, wide_ref):
    hidden = w_ref.shape[1]
    parts = hidden // size
    for side in range(2):
        for kind in range(2):
            start = (2 * side + kind) * hidden
            weights = 0.5 * w_ref[0, :, start : start + hidden].astype(jnp.float32)
            group = lane_group(weights.shape, size)
            for part in range(parts):
                kept = jnp.where(group == part, weights, 0.0)
                at = ((side * parts + part) * 2 + kind) * hidden
                for a in range(parts):
                    moved = pltpu.roll(kept, ((a - part) % parts) * size, 1) if a != part else kept
                    wide_ref[a * hidden : (a + 1) * hidden, at : at + hidden] = moved.astype(jnp.bfloat16)


def spread_weights(w_in, layer, size):
    hidden = w_in.shape[1]
    parts = hidden // size
    shape = (parts * hidden, 4 * parts * hidden)
    return pl.pallas_call(
        functools.partial(spread_kernel, size),
        grid=(1,),
        in_specs=[pl.BlockSpec((1,) + w_in.shape[1:], lambda s: (layer, 0, 0))],
        out_specs=pl.BlockSpec(shape, lambda s: (0, 0)),
        out_shape=jax.ShapeDtypeStruct(shape, jnp.bfloat16),
        compiler_params=pltpu.CompilerParams(vmem_limit_bytes=16 * mebi),
        cost_estimate=pl.CostEstimate(flops=1 << 30, bytes_accessed=1 << 20, transcendentals=0),
        name="spread_weights",
    )(w_in)


def swap_matrix(half):
    shape = (half * half, half * half)
    to, of = lax.broadcasted_iota(jnp.int32, shape, 0), lax.broadcasted_iota(jnp.int32, shape, 1)
    same = jnp.logical_and(to // half == lax.rem(of, half), lax.rem(to, half) == of // half)
    return same.astype(jnp.float32).astype(jnp.bfloat16)


def swapped(values, swap_ref):
    half, _, lanes = values.shape
    moved = dot(swap_ref[...], values.reshape(half * half, lanes))
    return moved.astype(jnp.bfloat16).reshape(half, half, lanes)


def turn(taken, turned, swap_ref):
    half = 16
    for x in range(0, taken.shape[0], half):
        for y in range(0, taken.shape[1], half):
            turned[y : y + half, x : x + half] = swapped(taken[x : x + half, y : y + half], swap_ref)


def make_operand(side, taken, wide_ref, out_refs, laid, swap_ref):
    rows, size, hidden = taken.shape
    parts, bands, half = hidden // size, size, 16
    groups = rows // parts
    stacked = jnp.concatenate(
        [jnp.concatenate([taken[g * parts + a] for a in range(parts)], axis=1) for g in range(groups)], axis=0
    )
    for part in range(parts):
        at = (side * parts + part) * 2 * hidden
        made = dot(stacked, wide_ref[:, at : at + 2 * hidden])
        value = made[:, :hidden] * (1.0 + jnp.tanh(made[:, hidden:]))
        laid[side, :, part * size : (part + 1) * size, :] = value.astype(jnp.bfloat16).reshape(groups, size, hidden)
    blocks = [laid[side, g].T for g in range(groups)]
    starts = [sum(ref.shape[1] for ref in out_refs[:n]) for n in range(len(out_refs))]
    for first in range(0, bands, half):
        for row in range(0, rows, half):
            tiles = []
            for r in range(row, row + half):
                at = r % parts * bands + first
                tiles.append(blocks[r // parts][at : at + half])
            moved = swapped(jnp.stack(tiles), swap_ref)
            for start, ref in zip(starts, out_refs):
                low, high = max(start, first), min(start + ref.shape[1], first + half)
                if low < high:
                    ref[0, low - start : high - start, row : row + half] = moved[low - first : high - first]


def open_layer(layer, natural, left_refs, right_refs, wide, laid, turned, swap):
    turn(natural, turned, swap)
    for side, refs in ((0, left_refs), (1, right_refs)):
        make_operand(side, natural if side == layer % 2 else turned[...], wide, refs, laid, swap)


def norm_and_gate(values, row_alive, col_alive, at, norm_ref, w_ref=None, gate_ref=None):
    _, cols, channels = norm_ref.shape
    rows = values.shape[0] // cols
    normed = layer_norm(values)
    if gate_ref is not None:
        gate = sigmoid(dot(normed.astype(jnp.bfloat16), w_ref[0, :, -channels:]))
        gate_ref[0, pl.ds(at, rows)] = gate.reshape(rows, cols, channels)
    mask = row_alive[at : at + rows, None, :] * col_alive[None, :, :]
    norm_ref[pl.ds(at, rows)] = (normed.reshape(rows, cols, channels) * mask).astype(jnp.bfloat16)


def open_kernel(hidden, chunks, n_chan, n_sub, base, of, ids, blocks, pair_ref, chain_ref, w_ref, wide, *rest):
    gate_ref, *operand_refs, norm_ref, laid, turned, swap = rest[-(2 * chunks + 5) :]
    step = pl.program_id(0)
    _, rows, cols, channels = pair_ref.shape
    block = ids[0] * of + base + step

    @pl.when(step == 0)
    def _():
        swap[...] = swap_matrix(16)

    row_alive = alive_rows(chain_ref, (blocks[0, block] * n_chan + ids[1]) * rows, rows)
    col_alive = alive_rows(chain_ref, (blocks[1, block] * n_sub + ids[2]) * cols, cols)
    group = hidden // cols
    for at in range(0, rows, group):
        values = pair_ref[0, pl.ds(at, group)].reshape(group * cols, channels)
        norm_and_gate(values, row_alive, col_alive, at, norm_ref, w_ref, gate_ref)
    open_layer(0, norm_ref[...], operand_refs[:chunks], operand_refs[chunks:], wide, laid, turned, swap)


def operand_scratch(rows, size, hidden):
    parts = hidden // size
    return [
        pltpu.VMEM((2, rows // parts, parts * size, hidden), jnp.bfloat16),
        pltpu.VMEM((size, rows, hidden), jnp.bfloat16),
        pltpu.VMEM((256, 256), jnp.bfloat16),
    ]


def operand_outputs(slots, count, rows, hidden, bands):
    kept = [count if n == 0 else slots for n in range(len(bands))] * 2
    return [jax.ShapeDtypeStruct((k, b, rows, hidden), jnp.bfloat16) for k, b in zip(kept, bands * 2)]


def slot_specs(arrays, slots, base):
    def spec(array):
        offset = base if array.shape[0] == slots else 0
        return pl.BlockSpec((1,) + array.shape[1:], lambda s, *_: (s + offset, 0, 0, 0))

    return [spec(a) for a in arrays]


def fill(out_shape, earlier, slots, n_before):
    if earlier is None:
        return [], [], {}
    shared = [n for n, o in enumerate(out_shape) if o.shape[0] == slots]
    specs = [pl.BlockSpec(memory_space=pl.ANY)] * len(shared)
    return [earlier[n] for n in shared], specs, {n_before + k: n for k, n in enumerate(shared)}


def open_operands(ids, blocks, pair, chains, w_in, wide, hidden, bands, base, count, earlier):
    slots, rows, cols, channels = pair.shape
    out_shape = [jax.ShapeDtypeStruct(pair.shape, jnp.float32)] + operand_outputs(slots, count, rows, hidden, bands)
    more, more_specs, aliases = fill(out_shape, earlier, slots, 6)
    return pl.pallas_call(
        functools.partial(open_kernel, hidden, len(bands), lax.axis_size("chan"), lax.axis_size("sub"), base, slots),
        grid_spec=pltpu.PrefetchScalarGridSpec(
            num_scalar_prefetch=2,
            grid=(count,),
            in_specs=slot_specs([pair], slots, base)
            + [
                pl.BlockSpec(chains.shape, lambda s, *_: (0, 0)),
                pl.BlockSpec((1,) + w_in.shape[1:], lambda s, *_: (0, 0, 0)),
                pl.BlockSpec(wide.shape, lambda s, *_: (0, 0)),
            ]
            + more_specs,
            out_specs=slot_specs(out_shape, slots, base),
            scratch_shapes=[pltpu.VMEM((rows, cols, channels), jnp.bfloat16)] + operand_scratch(rows, cols, hidden),
        ),
        out_shape=out_shape,
        input_output_aliases=aliases,
        compiler_params=pltpu.CompilerParams(vmem_limit_bytes=18 * mebi),
        cost_estimate=pl.CostEstimate(flops=1 << 33, bytes_accessed=1 << 20, transcendentals=0),
        name="open_operands",
    )(ids, blocks, pair, chains, w_in, wide, *more)


def far_kernel(layer, n_blk, far, n_chan, n_sub, of, bases, ids, blocks, mine, *rest):
    sources, (chain_ref, wide, left_ref, right_ref, norm_ref, laid, turned, swap) = rest[:-8], rest[-8:]
    step = pl.program_id(0)
    rows, cols, channels = norm_ref.shape
    holder = lax.rem(ids[0] - far + n_blk, n_blk)

    @pl.when(step == 0)
    def _():
        swap[...] = swap_matrix(16)

    group = channels // cols
    for side, out_ref in ((0, left_ref), (1, right_ref)):
        slot = mine[2 * step + side]
        refs = sources[side * len(bases) : (side + 1) * len(bases)]
        block = holder * of + slot
        row_alive = alive_rows(chain_ref, (blocks[0, block] * n_chan + ids[1]) * rows, rows)
        col_alive = alive_rows(chain_ref, (blocks[1, block] * n_sub + ids[2]) * cols, cols)
        for at in range(0, rows, group):
            values = refs[0][0, pl.ds(at, group)]
            for base, ref in zip(bases[1:], refs[1:]):
                values = jnp.where(slot >= base, ref[0, pl.ds(at, group)], values)
            norm_and_gate(values.reshape(group * cols, channels), row_alive, col_alive, at, norm_ref)
        if side == layer % 2:
            make_operand(side, norm_ref[...], wide, [out_ref], laid, swap)
        else:
            turn(norm_ref[...], turned, swap)
            make_operand(side, turned[...], wide, [out_ref], laid, swap)


def far_operands(layer, ids, blocks, mine, sources, chains, wide, far, capacity, of, hidden):
    n_blk = lax.axis_size("blk")
    _, rows, cols, channels = sources[0].shape
    bases = [sum(a.shape[0] for a in sources[:n]) for n in range(len(sources))]

    def source_spec(side, base, size):
        def place(t, ids, blocks, mine):
            return jnp.clip(mine[2 * t + side] - base, 0, size - 1), 0, 0, 0

        return pl.BlockSpec((1, rows, cols, channels), place)

    in_specs = [source_spec(side, b, a.shape[0]) for side in range(2) for b, a in zip(bases, sources)]
    in_specs += [pl.BlockSpec(chains.shape, lambda t, *_: (0, 0)), pl.BlockSpec(wide.shape, lambda t, *_: (0, 0))]
    shape = (capacity, hidden // (hidden // cols), rows, hidden)
    return pl.pallas_call(
        functools.partial(
            far_kernel, layer, n_blk, far, lax.axis_size("chan"), lax.axis_size("sub"), of, tuple(bases)
        ),
        grid_spec=pltpu.PrefetchScalarGridSpec(
            num_scalar_prefetch=3,
            grid=(capacity,),
            in_specs=in_specs,
            out_specs=[pl.BlockSpec((1,) + shape[1:], lambda t, *_: (t, 0, 0, 0))] * 2,
            scratch_shapes=[pltpu.VMEM((rows, cols, channels), jnp.bfloat16)] + operand_scratch(rows, cols, hidden),
        ),
        out_shape=[jax.ShapeDtypeStruct(shape, jnp.bfloat16)] * 2,
        compiler_params=pltpu.CompilerParams(vmem_limit_bytes=14 * mebi),
        cost_estimate=pl.CostEstimate(flops=1 << 33, bytes_accessed=1 << 20, transcendentals=0),
        name="far_operands",
    )(ids, blocks, mine, *sources, *sources, chains, wide)


def plan_kernel(n_blk, far, slots_dev, terms, capacity, ids, owners, slots, chosen, place, mine, seen):
    for shift in range(n_blk):
        seen[shift] = 0
        target = lax.rem(ids[0] + shift, n_blk)
        for e in range(2 * (capacity + 1)):
            chosen[2 * shift * (capacity + 1) + e] = 0
        found = jnp.int32(0)
        for e in range(slots_dev * terms):
            block, term = target * slots_dev + e // terms, e % terms
            at = 2 * (shift * (capacity + 1) + jnp.minimum(found, capacity))
            chosen[at] = slots[term, 0, block]
            chosen[at + 1] = slots[term, 1, block]
            found = found + (owners[term, block] == ids[0]).astype(jnp.int32)
    for e in range(slots_dev * terms):
        owner = owners[e % terms, ids[0] * slots_dev + e // terms]
        count = seen[owner]
        seen[owner] = count + 1
        place[e] = lax.rem(ids[0] - owner + n_blk, n_blk) * capacity + count
    for e in range(2 * (capacity + 1)):
        mine[e] = 0
    found = jnp.int32(0)
    for e in range(slots_dev * terms):
        block, term = ids[0] * slots_dev + e // terms, e % terms
        at = 2 * jnp.minimum(found, capacity)
        mine[at] = slots[term, 0, block]
        mine[at + 1] = slots[term, 1, block]
        found = found + (owners[term, block] == lax.rem(ids[0] - far + n_blk, n_blk)).astype(jnp.int32)


def make_plan(ids, owners, slots, n_blk, far, slots_dev, terms, capacity):
    scalars = pl.BlockSpec(memory_space=pltpu.SMEM)
    return pl.pallas_call(
        functools.partial(plan_kernel, n_blk, far, slots_dev, terms, capacity),
        in_specs=[scalars] * 3,
        out_specs=[scalars] * 3,
        out_shape=[
            jax.ShapeDtypeStruct((2 * n_blk * (capacity + 1),), jnp.int32),
            jax.ShapeDtypeStruct((slots_dev * terms,), jnp.int32),
            jax.ShapeDtypeStruct((2 * (capacity + 1),), jnp.int32),
        ],
        scratch_shapes=[pltpu.SMEM((n_blk,), jnp.int32)],
        compiler_params=pltpu.CompilerParams(vmem_limit_bytes=mebi),
        name="make_plan",
    )(ids, owners, slots)


def banded_kernel(shifts, capacity, pieces, n_refs, size, ids, chosen, *rest):
    refs, rest = rest[:n_refs], rest[n_refs:]
    out_refs, (left_held, right_held, out_held, sems, out_sems) = rest[: len(shifts)], rest[len(shifts) :]
    halves, _, bands, rows, hidden = left_held.shape
    parts = hidden // size
    at_once = 2 if capacity % 2 == 0 else 1

    def copy(n, source):
        side, half, base, *_ = pieces[n]
        target = (left_held, right_held)[side].at[half, pl.ds(base, refs[source].shape[0])]
        return pltpu.make_async_copy(refs[source], target, sems.at[n])

    for n, (*_, on, off) in enumerate(pieces):
        if on == off:
            copy(n, on).start()
        else:

            @pl.when(ids[3] == 1)
            def _(n=n, on=on):
                copy(n, on).start()

            @pl.when(ids[3] == 0)
            def _(n=n, off=off):
                copy(n, off).start()

    for n, piece in enumerate(pieces):
        copy(n, piece[-1]).wait()

    def leave(n):
        return pltpu.make_async_copy(out_held.at[pl.ds(n * capacity, capacity)], out_refs[n], out_sems.at[n])

    for n, shift in enumerate(shifts):

        def one(turn, carry, n=n, shift=shift):
            group = lane_group((size, hidden), size)
            for term in [turn * at_once + t for t in range(at_once)]:
                at = 2 * (shift * (capacity + 1) + term)
                left_slot, right_slot = chosen[at], chosen[at + 1]
                for band in range(bands):
                    left = jnp.concatenate([left_held[h, left_slot, band] for h in range(halves)], axis=1)
                    apart = []
                    for h in range(halves):
                        right = right_held[h, right_slot, band]
                        apart += [jnp.where(group == part, right, jnp.zeros_like(right)) for part in range(parts)]
                    made = dot(left, jnp.concatenate(apart, axis=0))
                    out_held[n * capacity + term, band] = made.astype(jnp.bfloat16)
            return carry

        lax.fori_loop(0, capacity // at_once, one, 0)
        leave(n).start()
    for n in range(len(shifts)):
        leave(n).wait()


def banded_products(shifts, ids, chosen, operands, capacity, size):
    refs, pieces = [], []

    def index_of(array):
        for n, known in enumerate(refs):
            if known is array:
                return n
        refs.append(array)
        return len(refs) - 1

    slots = 0
    for both in operands:
        for side in range(2):
            for half, (on, off) in enumerate(both[side]):
                pieces.append((side, half, slots, index_of(on), index_of(off)))
        slots += both[0][0][0].shape[0]
    halves = len(operands[0][0])
    _, bands, rows, hidden = operands[0][0][0][0].shape
    count = len(shifts) * capacity
    anywhere = pl.BlockSpec(memory_space=pl.ANY)
    return pl.pallas_call(
        functools.partial(banded_kernel, shifts, capacity, tuple(pieces), len(refs), size),
        grid_spec=pltpu.PrefetchScalarGridSpec(
            num_scalar_prefetch=2,
            grid=(),
            in_specs=[anywhere] * len(refs),
            out_specs=[anywhere] * len(shifts),
            scratch_shapes=[
                pltpu.VMEM((halves, slots, bands, rows, hidden), jnp.bfloat16),
                pltpu.VMEM((halves, slots, bands, size, hidden), jnp.bfloat16),
                pltpu.VMEM((count, bands, rows, hidden), jnp.bfloat16),
                pltpu.SemaphoreType.DMA((len(pieces),)),
                pltpu.SemaphoreType.DMA((len(shifts),)),
            ],
        ),
        out_shape=[jax.ShapeDtypeStruct((capacity, bands, rows, hidden), jnp.bfloat16)] * len(shifts),
        compiler_params=pltpu.CompilerParams(vmem_limit_bytes=14 * mebi),
        cost_estimate=pl.CostEstimate(
            flops=2 * count * bands * rows * hidden * hidden * halves, bytes_accessed=1, transcendentals=0
        ),
        name="banded_products",
    )(ids, chosen, *refs)


def close_kernel(layer, last, spots, chunks, n_chan, n_sub, base, of, terms, capacity, ids, blocks, place, *rest):
    n_parts = len(spots)
    arrived, rest = rest[:n_parts], rest[n_parts:]
    cur_ref, gate_ref, w_out_ref = rest[:3]
    if last:
        out_ref, held, wide_out, sems, swap = rest[3:]
    else:
        chain_ref, w_ref, wide = rest[3:6]
        out_ref, next_gate_ref, sent_ref, *operand_refs, held, wide_out, sems, norm_ref, laid, turned, swap = rest[
            -(2 * chunks + 10) :
        ]
        left_refs, right_refs = operand_refs[:chunks], operand_refs[chunks:]
    step = pl.program_id(0)
    _, rows, cols, channels = cur_ref.shape
    _, bands, _, hidden = held.shape
    parts, size = hidden // bands, bands

    def arrival(n):
        shift, at = spots[n]
        target = held.at[pl.ds(shift * capacity, capacity), pl.ds(at, arrived[n].shape[1])]
        return pltpu.make_async_copy(arrived[n], target, sems.at[n])

    @pl.when(step == 0)
    def _():
        for n in range(n_parts):
            arrival(n).start()
        wide_out[...] = jnp.zeros_like(wide_out)
        for part in range(parts):
            for a in range(parts):
                at = (part * parts + a) * bands
                wide_out[at : at + bands, a * channels : (a + 1) * channels] = w_out_ref[
                    0, part * bands : (part + 1) * bands, :
                ]
        swap[...] = swap_matrix(16)
        for n in range(n_parts):
            arrival(n).wait()

    if not last:
        block = ids[0] * of + base + step
        row_alive = alive_rows(chain_ref, (blocks[0, block] * n_chan + ids[1]) * rows, rows)
        col_alive = alive_rows(chain_ref, (blocks[1, block] * n_sub + ids[2]) * cols, cols)
    half = 16
    by_row = [[] for _ in range(rows)]
    for row in range(0, rows, half):
        for band in range(0, bands, half):
            taken = pl.ds(band, half), pl.ds(row, half)
            each = [held[(place[(base + step) * terms + t], *taken)] for t in range(terms)]
            each = jnp.concatenate([x.reshape(half * half, hidden) for x in each])
            total = dot(jnp.concatenate([swap[...]] * terms, axis=1), each)
            moved = total.astype(jnp.bfloat16).reshape(half, half, hidden)
            for r in range(half):
                by_row[row + r].append(moved[r])
    groups = rows // parts
    pieces = []
    for g in range(groups):
        block = jnp.concatenate([x for a in range(parts) for x in by_row[g * parts + a]]).T
        pieces.append(jnp.concatenate([block[p * cols : (p + 1) * cols] for p in range(parts)], axis=1))
    mixture = jnp.concatenate(pieces)
    together = (lane_group((hidden, hidden), size) == lax.broadcasted_iota(jnp.int32, (hidden, hidden), 0) // size)
    together = together.astype(jnp.float32).astype(jnp.bfloat16)
    average = dot(mixture, jnp.concatenate([together] * parts)) * (1.0 / hidden)
    centred = [mixture[:, p * hidden : (p + 1) * hidden].astype(jnp.float32) - average for p in range(parts)]
    squares = sum(c * c for c in centred)
    high = squares.astype(jnp.bfloat16)
    low = (squares - high.astype(jnp.float32)).astype(jnp.bfloat16)
    variance = dot(jnp.concatenate([high, low], axis=1), jnp.concatenate([together] * 2)) * (1.0 / hidden)
    scale = lax.rsqrt(variance + norm_epsilon)
    normed = jnp.concatenate([(c * scale).astype(jnp.bfloat16) for c in centred], axis=1)
    update = dot(normed, wide_out[...])
    for g in range(groups):
        taken = pl.ds(g * parts, parts)
        change = jnp.concatenate(
            [update[g * cols : (g + 1) * cols, a * channels : (a + 1) * channels] for a in range(parts)]
        )
        gate = gate_ref[0, taken].reshape(parts * cols, channels)
        current = cur_ref[0, taken].astype(jnp.float32).reshape(parts * cols, channels)
        result = (current + gate * change).astype(jnp.bfloat16)
        out_ref[0, taken] = result.reshape(parts, cols, channels)
        if not last:
            sent_ref[0, taken] = result.reshape(parts, cols, channels)
            norm_and_gate(result, row_alive, col_alive, g * parts, norm_ref, w_ref, next_gate_ref)
    if not last:
        open_layer(layer + 1, norm_ref[...], left_refs, right_refs, wide, laid, turned, swap)


def close_layer(
    layer, arrived, ids, blocks, place, current, gate, w_out, capacity, terms, chains, w_in, wide, last, bands, base, count, earlier
):
    flat, spots = [part for part, *_ in arrived], tuple((shift, at) for _, shift, at in arrived)
    n_blk = lax.axis_size("blk")
    slots, rows, cols, channels = current.shape
    hidden = w_out.shape[1]

    def layer_spec(array, index):
        return pl.BlockSpec((1,) + array.shape[1:], lambda s, *_: (index, 0, 0))

    in_specs = [pl.BlockSpec(memory_space=pl.ANY)] * len(flat)
    in_specs += slot_specs([current, gate], slots, base) + [layer_spec(w_out, layer)]
    operands = [*flat, current, gate, w_out]
    out_shape = [jax.ShapeDtypeStruct(current.shape, jnp.bfloat16)]
    scratch = [
        pltpu.VMEM((n_blk * capacity, sum(bands[layer]), rows, hidden), jnp.bfloat16),
        pltpu.VMEM((hidden // cols * hidden, hidden // cols * channels), jnp.bfloat16),
        pltpu.SemaphoreType.DMA((len(flat),)),
    ]
    if not last:
        operands += [chains, w_in, wide]
        in_specs += [pl.BlockSpec(chains.shape, lambda s, *_: (0, 0)), layer_spec(w_in, layer + 1)]
        in_specs += [pl.BlockSpec(wide.shape, lambda s, *_: (0, 0))]
        out_shape += [jax.ShapeDtypeStruct(current.shape, jnp.float32)]
        out_shape += [jax.ShapeDtypeStruct((count,) + current.shape[1:], jnp.bfloat16)]
        out_shape += operand_outputs(slots, count, cols, hidden, bands[layer + 1])
        scratch += [pltpu.VMEM((rows, cols, channels), jnp.bfloat16)] + operand_scratch(cols, rows, hidden)
    else:
        scratch += [pltpu.VMEM((256, 256), jnp.bfloat16)]
    more, more_specs, aliases = fill(out_shape, earlier, slots, 3 + len(operands))
    return pl.pallas_call(
        functools.partial(
            close_kernel,
            *(layer, last, spots, 0 if last else len(bands[layer + 1]), lax.axis_size("chan"), lax.axis_size("sub")),
            *(base, slots, terms, capacity),
        ),
        grid_spec=pltpu.PrefetchScalarGridSpec(
            num_scalar_prefetch=3,
            grid=(count,),
            in_specs=in_specs + more_specs,
            out_specs=slot_specs(out_shape, slots, base),
            scratch_shapes=scratch,
        ),
        out_shape=out_shape,
        input_output_aliases=aliases,
        compiler_params=pltpu.CompilerParams(vmem_limit_bytes=24 * mebi),
        cost_estimate=pl.CostEstimate(flops=1 << 33, bytes_accessed=1 << 20, transcendentals=0),
        name="close_layer",
    )(ids, blocks, place, *operands, *more)


def after(value, *others):
    return lax.optimization_barrier((value, *others))[0]


def exchange_bands_outgoing(left, right, over):
    both = ("chan", "sub")
    other = lax.ppermute(left, "sub", [(0, 1), (1, 0)])
    one = lax.ppermute(right, both, [(0, 2), (3, 1), (1, 0), (2, 3)])
    two = lax.ppermute(right, both, [(1, 2), (2, 1)])
    return [(other, left), (left, other)], [(one, one), (right, two)]


def exchange_bands_incoming(left, right, over):
    both = ("chan", "sub")
    one = lax.ppermute(left, both, [(1, 3), (2, 0), (0, 1), (3, 2)])
    other = lax.ppermute(right, "chan", [(0, 1), (1, 0)])
    two = lax.ppermute(after(one, other if over is None else over), both, [(0, 1), (3, 2)])
    return [(left, one), (one, two)], [(right, right), (other, other)]


def banded(pair, ids, blocks, owners, slot_of, chains, w_in, w_out, capacity, terms, n_blk):
    slots, rows, cols, channels = pair.shape
    hidden = w_out.shape[1]
    far = 1
    middle = n_blk // 2
    near = [s for s in (middle, *range(1, n_blk)) if s != far]
    near = [s for n, s in enumerate(near) if s not in near[:n]] + [0]
    layers = w_in.shape[0]
    current = pair
    bands = [[16, 16], [18, 14]]
    chosen, place, mine = make_plan(ids, owners, slot_of, n_blk, far, slots, terms, capacity)
    in_order = jnp.repeat(jnp.arange(capacity, dtype=jnp.int32), 2)
    half = slots // 2
    halves = [(0, half), (half, slots - half)]

    def over_blk(value, shift):
        return lax.ppermute(value, "blk", [(p, (p + shift) % n_blk) for p in range(n_blk)])

    for layer in range(layers):
        count = len(bands[layer])
        if layer == 0:
            raw = [over_blk(pair, far)]
            calls, wide = [None], spread_weights(w_in, 0, cols)
            for base, size in halves:
                calls.append(
                    open_operands(ids, blocks, pair, chains, w_in, wide, hidden, bands[0], base, size, calls[-1])
                )
            gate = calls[-1][0]
        else:
            raw = []
            for call in calls[1:]:
                raw.append(over_blk(after(call[2], *raw) if raw else call[2], far))
        operands = [call[-2 * count :] for call in calls[1:]]
        exchange = exchange_bands_incoming if layer % 2 else exchange_bands_outgoing
        arrived, by_shift = [], {}
        for chunk in range(count):
            if chunk == 0:
                exchanged = []
                over = operands[-1][count]
                for left, right in [(o[0], o[count]) for o in operands]:
                    if exchanged and layer % 2:
                        (_, (one, two)), (_, (other, _)) = exchanged[-1]
                        left, right = lax.optimization_barrier((left, right, one, other))[:2]
                        right = after(right, two)
                    elif exchanged:
                        ((other, _), _), ((one, _), (_, two)) = exchanged[-1]
                        left, right = lax.optimization_barrier((left, right, other, one, two))[:2]
                    exchanged.append(exchange(left, right, over))
            else:
                left, right = operands[-1][chunk], operands[-1][count + chunk]
                if layer % 2:
                    (_, (_, two)), (_, (other, _)) = exchanged[-1]
                    left, right = lax.optimization_barrier((left, right, two, other))[:2]
                else:
                    ((other, _), _), ((one, _), (_, two)) = exchanged[-1]
                    left = after(left, other)
                    right = after(right, one, two, made[-1])
                exchanged = [exchange(left, right, list(by_shift.values())[-1] if by_shift else made[-1])]
                ids = after(ids, *by_shift.values())
            made = banded_products(near, ids, chosen, exchanged, capacity, cols)
            start = sum(bands[layer][:chunk])
            for shift, part in zip(near, made):
                if shift:
                    part = over_blk(after(part, by_shift.get(shift, raw[-1])), shift)
                    by_shift[shift] = part
                arrived.append((part, shift, start))
            if chunk == 0:
                sources = list(lax.optimization_barrier((*raw, made[-1]))[:-1])
                far_left, far_right = far_operands(
                    layer, ids, blocks, mine, sources, chains, wide, far, capacity, slots, hidden
                )
        far_exchanged = [exchange(far_left, far_right, made[-1])]
        (part,) = banded_products([0], ids, in_order, far_exchanged, capacity, cols)
        arrived.append((part, far, 0))
        last = layer == layers - 1
        calls = [None]
        if not last:
            wide = spread_weights(after(w_in, made[-1]), layer + 1, cols)
        for base, size in [(0, slots)] if last else halves:
            calls.append(
                close_layer(
                    *(layer, arrived, ids, blocks, place, current, gate, w_out, capacity, terms, chains, w_in, wide, last),
                    *(bands, base, size, calls[-1]),
                )
            )
        if last:
            return calls[-1][0]
        current, gate = calls[-1][:2]


def per_device(pair, block_list, term_owner, term_slots, chain_ids, w_in, w_out):
    n_blk = lax.axis_size("blk")
    n_chan = lax.axis_size("chan")
    n_sub = lax.axis_size("sub")
    position = lax.axis_index("blk")
    row_group = lax.axis_index("chan")
    col_group = lax.axis_index("sub")
    slots, rows, cols, channels = pair.shape
    hidden = w_out.shape[1]
    terms = term_owner.shape[1]
    capacity = max(2, -(-slots * terms // n_blk))
    fast = n_chan == 2 and n_sub == 2
    on_diagonal = (row_group == col_group).astype(jnp.int32)
    ids = jnp.stack([position, row_group, col_group, on_diagonal]).astype(jnp.int32)
    blocks = block_list.T
    owners = term_owner.T
    slot_of = jnp.transpose(term_slots, (1, 2, 0))
    chains = chain_ids.reshape(-1, 128)
    if fast and n_blk > 1 and rows == cols == 32 and channels == hidden == 128:
        return banded(pair, ids, blocks, owners, slot_of, chains, w_in, w_out, capacity, terms, n_blk)
    shifts = [n_blk // 2] + [s for s in range(1, n_blk) if s != n_blk // 2] + [0]

    def all_products(lefts, right):
        parts = [None] * n_blk
        for shift in shifts:
            made = term_products(shift, ids, owners, slot_of, lefts, right, capacity, slots, terms)
            if shift:
                pairs = [(p, (p + shift) % n_blk) for p in range(n_blk)]
                made = lax.ppermute(made, "blk", pairs)
            parts[shift] = made
        return parts

    def at_home(layer, parts, current, gate, at, of, into=None):
        last = layer == w_in.shape[0] - 1
        return home(
            layer, parts, ids, blocks, owners, current, gate, w_out, capacity, terms, at, of, chains, w_in, last, into
        )

    gate, left, *rights = first_operands(ids, blocks, pair, chains, w_in, hidden, 2 if fast else 1)
    lefts, chunks = exchange_outgoing(left, rights, n_chan, n_sub)
    count = len(chunks)
    made = [all_products(lefts, right) for right in chunks]
    homes = [at_home(0, parts, pair, gate, at, count) for at, parts in enumerate(made)]
    lefts, chunks = exchange_incoming([h[2] for h in homes], [h[3] for h in homes], n_chan, n_sub)
    made = [all_products(lefts, right) for right in chunks]
    out = None
    for at, parts in enumerate(made):
        (out,) = at_home(1, parts, homes[at][0], homes[at][1], at, count, into=out)
    return out


def solution(mesh):
    in_specs = (
        P(("groups", "blk"), "chan", "sub", None),
        P("groups", None),
        P("groups", None),
        P("groups", None, None),
        P("groups"),
        P(),
        P(),
    )
    out_specs = P(("groups", "blk"), "chan", "sub", None)
    return jax.shard_map(
        per_device, mesh=mesh, in_specs=in_specs, out_specs=out_specs, check_vma=False
    )
```

```python
import functools

import jax
import jax.numpy as jnp
from jax import lax
from jax.experimental import pallas as pl
from jax.experimental.pallas import tpu as pltpu
from jax.sharding import PartitionSpec as P

norm_epsilon = 1e-05
mebi = 1024 * 1024
vmem_limit = 56 * mebi


def sigmoid(values):
    return 0.5 + 0.5 * jnp.tanh(0.5 * values)


def layer_norm(values):
    values = values.astype(jnp.float32)
    centred = values - jnp.mean(values, axis=-1, keepdims=True)
    variance = jnp.mean(centred * centred, axis=-1, keepdims=True)
    return centred * lax.rsqrt(variance + norm_epsilon)


def alive_rows(chain_ref, start, size):
    lanes = chain_ref.shape[1]
    line = chain_ref[pl.ds(start // lanes, 1), :] >= 0
    spot = lax.broadcasted_iota(jnp.int32, (size, lanes), 0) + lax.rem(start, lanes)
    pick = jnp.logical_and(lax.broadcasted_iota(jnp.int32, (size, lanes), 1) == spot, line)
    return dot(pick.astype(jnp.float32).astype(jnp.bfloat16), jnp.ones((lanes, lanes), jnp.bfloat16))


def dot(a, b):
    return jnp.dot(a, b, preferred_element_type=jnp.float32)


def gated_pair(projected, mask, hidden):
    left = mask * sigmoid(projected[:, hidden : 2 * hidden]) * projected[:, :hidden]
    right = mask * sigmoid(projected[:, 3 * hidden : 4 * hidden]) * projected[:, 2 * hidden : 3 * hidden]
    return left.astype(jnp.bfloat16), right.astype(jnp.bfloat16)


def first_kernel(hidden, row_parts, n_chan, n_sub, ids, blocks, pair_ref, chain_ref, w_ref, gate_ref, left_ref, *rest):
    right_refs, (norm_ref, turned_ref) = rest[:row_parts], rest[row_parts:]
    slots = pl.num_programs(0)
    _, rows, cols, channels = pair_ref.shape
    block = ids[0] * slots + pl.program_id(0)
    row_alive = alive_rows(chain_ref, (blocks[0, block] * n_chan + ids[1]) * rows, rows)
    col_alive = alive_rows(chain_ref, (blocks[1, block] * n_sub + ids[2]) * cols, cols)
    group = max(1, 256 // cols)
    for start in range(0, rows, group):
        at = pl.ds(start, group)
        normed = layer_norm(pair_ref[0, at].reshape(group * cols, channels))
        norm_ref[pl.ds(start * cols, group * cols), :] = normed
        gate = sigmoid(dot(normed.astype(jnp.bfloat16), w_ref[0, :, 4 * hidden :]))
        gate_ref[0, at] = gate.reshape(group, cols, channels)
    for col in range(cols):
        turned_ref[col] = norm_ref[pl.ds(col, rows, stride=cols), :].astype(jnp.bfloat16)
    step = max(1, 128 // rows)
    part = rows // row_parts
    for start in range(0, cols, step):
        taken = turned_ref[start : start + step].reshape(step * rows, channels)
        projected = dot(taken, w_ref[0, :, : 4 * hidden])
        mask = col_alive[start : start + step][:, None, :] * row_alive[None, :, :]
        left, right = gated_pair(projected, mask.reshape(step * rows, -1), hidden)
        left_ref[0, start : start + step] = left.reshape(step, rows, hidden)
        right = right.reshape(step, rows, hidden)
        for p, right_ref in enumerate(right_refs):
            right_ref[0, start : start + step] = right[:, p * part : (p + 1) * part]


def first_operands(ids, blocks, pair, chains, w_in, hidden, row_parts):
    slots, rows, cols, channels = pair.shape
    part = rows // row_parts
    operand = jax.ShapeDtypeStruct((slots, cols, rows, hidden), jnp.bfloat16)
    right = jax.ShapeDtypeStruct((slots, cols, part, hidden), jnp.bfloat16)
    return pl.pallas_call(
        functools.partial(first_kernel, hidden, row_parts, lax.axis_size("chan"), lax.axis_size("sub")),
        grid_spec=pltpu.PrefetchScalarGridSpec(
            num_scalar_prefetch=2,
            grid=(slots,),
            in_specs=[
                pl.BlockSpec((1, rows, cols, channels), lambda s, *_: (s, 0, 0, 0)),
                pl.BlockSpec(chains.shape, lambda s, *_: (0, 0)),
                pl.BlockSpec((1,) + w_in.shape[1:], lambda s, *_: (0, 0, 0)),
            ],
            out_specs=[
                pl.BlockSpec((1, rows, cols, channels), lambda s, *_: (s, 0, 0, 0)),
                pl.BlockSpec((1, cols, rows, hidden), lambda s, *_: (s, 0, 0, 0)),
            ]
            + [pl.BlockSpec((1, cols, part, hidden), lambda s, *_: (s, 0, 0, 0))] * row_parts,
            scratch_shapes=[
                pltpu.VMEM((rows * cols, channels), jnp.float32),
                pltpu.VMEM((cols, rows, channels), jnp.bfloat16),
            ],
        ),
        out_shape=[jax.ShapeDtypeStruct(pair.shape, jnp.float32), operand] + [right] * row_parts,
        compiler_params=pltpu.CompilerParams(vmem_limit_bytes=vmem_limit),
        name="first_operands",
    )(ids, blocks, pair, chains, w_in)


def product_kernel(shift, n_blk, slots_dev, terms, capacity, pieces, n_refs, ids, owners, slots, *rest):
    refs = rest[:n_refs]
    out_ref, left_held, right_held, right_wide, chosen, sems = rest[n_refs:]
    step = pl.program_id(0)
    turn = lax.rem(step, 2)
    _, depth, n_i, hidden = left_held.shape
    n_j = right_wide.shape[1]

    @pl.when(step == 0)
    def _():
        target = lax.rem(ids[0] + shift, n_blk)
        for e in range(2 * capacity):
            chosen[e] = 0

        def scan(e, count):
            block, term = target * slots_dev + e // terms, lax.rem(e, terms)
            here = jnp.logical_and(owners[term, block] == ids[0], count < capacity)

            @pl.when(here)
            def _():
                chosen[2 * count] = slots[term, 0, block]
                chosen[2 * count + 1] = slots[term, 1, block]

            return count + here.astype(jnp.int32)

        lax.fori_loop(0, slots_dev * terms, scan, jnp.int32(0))

    def copy(n, term, buffer, source):
        side, _, _, k0, depth_of, i0, size = pieces[n]
        held = (left_held, right_held)[side]
        return pltpu.make_async_copy(
            refs[source].at[chosen[2 * term + side]],
            held.at[buffer, pl.ds(k0, depth_of), pl.ds(i0, size), :],
            sems.at[buffer, n],
        )

    def start(term, buffer):
        for n, (_, on, off, *_) in enumerate(pieces):
            if on == off:
                copy(n, term, buffer, on).start()
            else:

                @pl.when(ids[3] == 1)
                def _(n=n, on=on):
                    copy(n, term, buffer, on).start()

                @pl.when(ids[3] == 0)
                def _(n=n, off=off):
                    copy(n, term, buffer, off).start()

    @pl.when(step == 0)
    def _():
        start(0, 0)

    @pl.when(step + 1 < capacity)
    def _():
        start(step + 1, 1 - turn)

    for n, piece in enumerate(pieces):
        copy(n, step, turn, piece[1]).wait()

    span = 8

    def widen(n, carry):
        at = pl.ds(n * span, span)
        right_wide[at] = right_held[turn, at].astype(jnp.float32)
        return carry

    lax.fori_loop(0, depth // span, widen, 0)

    group = min(8, n_j)
    unroll = 4
    for j0 in range(0, n_j, group):

        def body(n, sums):
            for u in range(unroll):
                k = n * unroll + u
                left = left_held[turn, k].astype(jnp.float32).reshape(n_i // 8, 8, hidden)
                sums = tuple(
                    total + left * right_wide[k, pl.ds(j0 + j, 8, stride=0), :][None]
                    for j, total in enumerate(sums)
                )
            return sums

        zero = jnp.zeros((n_i // 8, 8, hidden), jnp.float32)
        sums = lax.fori_loop(0, depth // unroll, body, (zero,) * group)
        for j, total in enumerate(sums):
            out_ref[0, j0 + j] = total.reshape(n_i, hidden).astype(jnp.bfloat16)


def term_products(shift, ids, owners, slots, lefts, rights, capacity, slots_dev, terms):
    n_blk = lax.axis_size("blk")
    refs, pieces = [], []

    def index_of(array):
        for n, known in enumerate(refs):
            if known is array:
                return n
        refs.append(array)
        return len(refs) - 1

    for side, operands in ((0, lefts), (1, rights)):
        for on, off, k0, i0 in operands:
            pieces.append((side, index_of(on), index_of(off), k0, on.shape[1], i0, on.shape[2]))
    hidden = lefts[0][0].shape[3]
    n_i = max(p[5] + p[6] for p in pieces if p[0] == 0)
    n_j = max(p[5] + p[6] for p in pieces if p[0] == 1)
    depth = max(p[3] + p[4] for p in pieces)
    return pl.pallas_call(
        functools.partial(
            product_kernel, shift, n_blk, slots_dev, terms, capacity, tuple(pieces), len(refs)
        ),
        grid_spec=pltpu.PrefetchScalarGridSpec(
            num_scalar_prefetch=3,
            grid=(capacity,),
            in_specs=[pl.BlockSpec(memory_space=pl.ANY)] * len(refs),
            out_specs=pl.BlockSpec((1, n_j, n_i, hidden), lambda t, *_: (t, 0, 0, 0)),
            scratch_shapes=[
                pltpu.VMEM((2, depth, n_i, hidden), jnp.bfloat16),
                pltpu.VMEM((2, depth, n_j, hidden), jnp.bfloat16),
                pltpu.VMEM((depth, n_j, hidden), jnp.float32),
                pltpu.SMEM((2 * capacity,), jnp.int32),
                pltpu.SemaphoreType.DMA((2, len(pieces))),
            ],
        ),
        out_shape=jax.ShapeDtypeStruct((capacity, n_j, n_i, hidden), jnp.bfloat16),
        compiler_params=pltpu.CompilerParams(vmem_limit_bytes=vmem_limit),
        cost_estimate=pl.CostEstimate(
            flops=2 * capacity * n_i * n_j * depth * hidden * 100,
            bytes_accessed=capacity * (depth * (n_i + n_j) + n_i * n_j) * hidden * 2,
            transcendentals=0,
        ),
        name="term_products",
    )(ids, owners, slots, *refs)


def home_kernel(last, hidden, n_blk, n_chan, n_sub, at, of, slots_dev, terms, capacity, ids, blocks, owners, *rest):
    parts, rest = rest[:n_blk], rest[n_blk:]
    scratch, rest = rest[-5:], rest[:-5]
    held, turned, place, seen, sems = scratch
    cur_ref, gate_ref, w_out_ref = rest[:3]
    if last:
        out_ref = rest[-1]
    else:
        chain_ref, w_ref, out_ref, next_gate_ref, left_ref, right_ref = rest[3:]
    step = pl.program_id(0)
    _, rows, cols, channels = cur_ref.shape

    def arrival(shift):
        return pltpu.make_async_copy(parts[shift], held.at[pl.ds(shift * capacity, capacity)], sems.at[shift])

    @pl.when(step == 0)
    def _():
        for shift in range(n_blk):
            arrival(shift).start()
            seen[shift] = 0

        def scan(e, carry):
            owner = owners[lax.rem(e, terms), ids[0] * slots_dev + e // terms]
            shift = lax.rem(ids[0] - owner + n_blk, n_blk)
            count = seen[owner]
            seen[owner] = count + 1
            place[e] = shift * capacity + count
            return carry

        lax.fori_loop(0, slots_dev * terms, scan, jnp.int32(0))
        for shift in range(n_blk):
            arrival(shift).wait()

    if not last:
        block = ids[0] * slots_dev + step
        row_alive = alive_rows(chain_ref, (blocks[0, block] * n_chan + ids[1]) * rows, rows)
        col_alive = alive_rows(chain_ref, ((blocks[1, block] * n_sub + ids[2]) * of + at) * cols, cols)
    span = max(1, 128 // rows)
    for start in range(0, cols, span):
        taken = pl.ds(start, span)
        total = held[place[step * terms], taken].astype(jnp.float32)
        for t in range(1, terms):
            total = total + held[place[step * terms + t], taken].astype(jnp.float32)
        rounded = total.astype(jnp.bfloat16).astype(jnp.float32)
        turned[pl.ds(start * rows, span * rows), :] = rounded.reshape(span * rows, hidden)
    group = min(rows, max(1, 256 // cols))
    for start in range(0, rows, group):
        taken = pl.ds(start, group)
        mixture = jnp.concatenate(
            [turned[pl.ds(row, cols, stride=rows), :].astype(jnp.bfloat16) for row in range(start, start + group)]
        )
        update = dot(layer_norm(mixture).astype(jnp.bfloat16), w_out_ref[0])
        current = cur_ref[0, taken].astype(jnp.float32).reshape(group * cols, channels)
        gate = gate_ref[0, taken].reshape(group * cols, channels)
        result = (current + gate * update).astype(jnp.bfloat16)
        out_ref[0, taken] = result.reshape(group, cols, channels)
        if not last:
            normed = layer_norm(result).astype(jnp.bfloat16)
            projected = dot(normed, w_ref[0])
            next_gate_ref[0, taken] = sigmoid(projected[:, 4 * hidden :]).reshape(group, cols, channels)
            mask = row_alive[start : start + group][:, None, :] * col_alive[None, :, :]
            left, right = gated_pair(projected, mask.reshape(group * cols, channels), hidden)
            left_ref[0, taken] = left.reshape(group, cols, hidden)
            right_ref[0, taken] = right.reshape(group, cols, hidden)


def home(layer, parts, ids, blocks, owners, current, gate, w_out, capacity, terms, at, of, chains, w_in, last, into=None):
    n_blk = len(parts)
    slots, rows, _, channels = current.shape
    hidden = w_out.shape[1]
    cols = parts[0].shape[1]
    chunk = (1, rows, cols, channels)

    def chunk_spec(array):
        whole = array.shape[2] != cols
        return pl.BlockSpec(chunk, lambda s, *_: (s, 0, at if whole else 0, 0))

    def layer_spec(array, index):
        return pl.BlockSpec((1,) + array.shape[1:], lambda s, *_: (index, 0, 0))

    in_specs = [pl.BlockSpec(memory_space=pl.ANY)] * n_blk + [
        chunk_spec(current),
        chunk_spec(gate),
        layer_spec(w_out, layer),
    ]
    operands = [*parts, current, gate, w_out]
    aliases = {}
    if last:
        if into is not None:
            aliases = {3 + len(operands): 0}
            operands.append(into)
            in_specs.append(pl.BlockSpec(memory_space=pl.ANY))
        out_shape = [jax.ShapeDtypeStruct((slots, rows, cols * of, channels), jnp.bfloat16)]
        out_specs = [pl.BlockSpec(chunk, lambda s, *_: (s, 0, at, 0))]
    else:
        operands += [chains, w_in]
        in_specs += [pl.BlockSpec(chains.shape, lambda s, *_: (0, 0)), layer_spec(w_in, layer + 1)]
        small = (slots, rows, cols, channels)
        out_shape = [jax.ShapeDtypeStruct(small, t) for t in (jnp.bfloat16, jnp.float32, jnp.bfloat16, jnp.bfloat16)]
        out_specs = [pl.BlockSpec(chunk, lambda s, *_: (s, 0, 0, 0))] * 4
    return pl.pallas_call(
        functools.partial(
            home_kernel, last, hidden, n_blk, lax.axis_size("chan"), lax.axis_size("sub"), at, of, slots, terms, capacity
        ),
        grid_spec=pltpu.PrefetchScalarGridSpec(
            num_scalar_prefetch=3,
            grid=(slots,),
            in_specs=in_specs,
            out_specs=out_specs,
            scratch_shapes=[
                pltpu.VMEM((n_blk * capacity, cols, rows, hidden), jnp.bfloat16),
                pltpu.VMEM((rows * cols, hidden), jnp.float32),
                pltpu.SMEM((slots * terms,), jnp.int32),
                pltpu.SMEM((n_blk,), jnp.int32),
                pltpu.SemaphoreType.DMA((n_blk,)),
            ],
        ),
        out_shape=out_shape,
        input_output_aliases=aliases,
        compiler_params=pltpu.CompilerParams(vmem_limit_bytes=vmem_limit),
        cost_estimate=pl.CostEstimate(
            flops=2 * slots * rows * cols * channels * 6 * channels * 10,
            bytes_accessed=slots * rows * cols * channels * 16,
            transcendentals=0,
        ),
        name="home",
    )(ids, blocks, owners, *operands)


def exchange_outgoing(left, rights, n_chan, n_sub):
    if n_chan == 2 and n_sub == 2:
        both = ("chan", "sub")
        other_left = lax.ppermute(left, "sub", [(0, 1), (1, 0)])
        lefts = [(other_left, left, 0, 0), (left, other_left, left.shape[1], 0)]
        chunks = []
        for right in rights:
            if chunks:
                (one, *_), (_, two, *_) = chunks[-1]
                right, *_ = lax.optimization_barrier((right, one, two))
            one = lax.ppermute(right, both, [(0, 2), (3, 1), (1, 0), (2, 3)])
            two = lax.ppermute(right, both, [(1, 2), (2, 1)])
            chunks.append([(one, one, 0, 0), (right, two, right.shape[1], 0)])
        return lefts, chunks
    left = lax.all_gather(left, "sub", axis=1, tiled=True)
    right = jnp.concatenate(rights, axis=2)
    right = lax.all_gather(right, "chan", axis=2, tiled=True)
    right = lax.all_to_all(right, "sub", split_axis=2, concat_axis=1, tiled=True)
    cols = right.shape[2] // 2
    chunks = [right[:, :, :cols], right[:, :, cols:]]
    return [(left, left, 0, 0)], [[(r, r, 0, 0)] for r in chunks]


def exchange_incoming(lefts, rights, n_chan, n_sub):
    if n_chan == 2 and n_sub == 2:
        both = ("chan", "sub")
        left_pieces, chunks = [], []
        at = 0
        for left, right in zip(lefts, rights):
            depth = left.shape[1]
            one = lax.ppermute(left, both, [(1, 3), (2, 0), (0, 1), (3, 2)])
            two = lax.ppermute(one, both, [(0, 1), (3, 2)])
            left_pieces += [(left, one, 0, at), (one, two, depth, at)]
            other = lax.ppermute(right, "chan", [(0, 1), (1, 0)])
            chunks.append([(right, right, 0, 0), (other, other, depth, 0)])
            at += left.shape[2]
        return left_pieces, chunks
    left = lax.all_gather(jnp.concatenate(lefts, axis=2), "chan", axis=1, tiled=True)
    left = lax.all_gather(left, "sub", axis=2, tiled=True)
    size = left.shape[2] // n_chan
    left = lax.dynamic_slice_in_dim(left, lax.axis_index("chan") * size, size, 2)
    gathered = [lax.all_gather(right, "chan", axis=1, tiled=True) for right in rights]
    return [(left, left, 0, 0)], [[(r, r, 0, 0)] for r in gathered]


def lane_group(shape, size):
    return lax.broadcasted_iota(jnp.int32, shape, 1) // size


def spread_kernel(size, w_ref, wide_ref):
    hidden = w_ref.shape[1]
    parts = hidden // size
    for side in range(2):
        for kind in range(2):
            start = (2 * side + kind) * hidden
            weights = 0.5 * w_ref[0, :, start : start + hidden].astype(jnp.float32)
            group = lane_group(weights.shape, size)
            for part in range(parts):
                kept = jnp.where(group == part, weights, 0.0)
                at = ((side * parts + part) * 2 + kind) * hidden
                for a in range(parts):
                    moved = pltpu.roll(kept, ((a - part) % parts) * size, 1) if a != part else kept
                    wide_ref[a * hidden : (a + 1) * hidden, at : at + hidden] = moved.astype(jnp.bfloat16)


def spread_weights(w_in, layer, size):
    hidden = w_in.shape[1]
    parts = hidden // size
    shape = (parts * hidden, 4 * parts * hidden)
    return pl.pallas_call(
        functools.partial(spread_kernel, size),
        grid=(1,),
        in_specs=[pl.BlockSpec((1,) + w_in.shape[1:], lambda s: (layer, 0, 0))],
        out_specs=pl.BlockSpec(shape, lambda s: (0, 0)),
        out_shape=jax.ShapeDtypeStruct(shape, jnp.bfloat16),
        compiler_params=pltpu.CompilerParams(vmem_limit_bytes=10 * mebi),
        cost_estimate=pl.CostEstimate(flops=1 << 30, bytes_accessed=1 << 20, transcendentals=0),
        name="spread_weights",
    )(w_in)


def swap_matrix(half):
    shape = (half * half, half * half)
    to, of = lax.broadcasted_iota(jnp.int32, shape, 0), lax.broadcasted_iota(jnp.int32, shape, 1)
    same = jnp.logical_and(to // half == lax.rem(of, half), lax.rem(to, half) == of // half)
    return same.astype(jnp.float32).astype(jnp.bfloat16)


def swapped(values, swap_ref):
    half, _, lanes = values.shape
    moved = dot(swap_ref[...], values.reshape(half * half, lanes))
    return moved.astype(jnp.bfloat16).reshape(half, half, lanes)


def turn(taken, turned, swap_ref):
    half = 16
    for x in range(0, taken.shape[0], half):
        for y in range(0, taken.shape[1], half):
            turned[y : y + half, x : x + half] = swapped(taken[x : x + half, y : y + half], swap_ref)


def make_operand(side, taken, wide_ref, out_refs, laid, swap_ref):
    rows, size, hidden = taken.shape
    parts, bands, half = hidden // size, size, 16
    groups = rows // parts
    stacked = jnp.concatenate(
        [jnp.concatenate([taken[g * parts + a] for a in range(parts)], axis=1) for g in range(groups)], axis=0
    )
    for part in range(parts):
        at = (side * parts + part) * 2 * hidden
        made = dot(stacked, wide_ref[:, at : at + 2 * hidden])
        value = made[:, :hidden] * (1.0 + jnp.tanh(made[:, hidden:]))
        laid[side, :, part * size : (part + 1) * size, :] = value.astype(jnp.bfloat16).reshape(groups, size, hidden)
    blocks = [laid[side, g].T for g in range(groups)]
    starts = [sum(ref.shape[1] for ref in out_refs[:n]) for n in range(len(out_refs))]
    for first in range(0, bands, half):
        for row in range(0, rows, half):
            tiles = []
            for r in range(row, row + half):
                at = r % parts * bands + first
                tiles.append(blocks[r // parts][at : at + half])
            moved = swapped(jnp.stack(tiles), swap_ref)
            for start, ref in zip(starts, out_refs):
                low, high = max(start, first), min(start + ref.shape[1], first + half)
                if low < high:
                    ref[0, low - start : high - start, row : row + half] = moved[low - first : high - first]


def open_layer(layer, natural, left_refs, right_refs, wide, laid, turned, swap):
    turn(natural, turned, swap)
    for side, refs in ((0, left_refs), (1, right_refs)):
        make_operand(side, natural if side == layer % 2 else turned[...], wide, refs, laid, swap)


def norm_and_gate(values, row_alive, col_alive, at, norm_ref, w_ref=None, gate_ref=None):
    _, cols, channels = norm_ref.shape
    rows = values.shape[0] // cols
    normed = layer_norm(values)
    if gate_ref is not None:
        gate = sigmoid(dot(normed.astype(jnp.bfloat16), w_ref[0, :, -channels:]))
        gate_ref[0, pl.ds(at, rows)] = gate.reshape(rows, cols, channels)
    mask = row_alive[at : at + rows, None, :] * col_alive[None, :, :]
    norm_ref[pl.ds(at, rows)] = (normed.reshape(rows, cols, channels) * mask).astype(jnp.bfloat16)


def open_kernel(hidden, chunks, n_chan, n_sub, base, of, ids, blocks, pair_ref, chain_ref, w_ref, wide, *rest):
    gate_ref, *operand_refs, norm_ref, laid, turned, swap = rest[-(2 * chunks + 5) :]
    step = pl.program_id(0)
    _, rows, cols, channels = pair_ref.shape
    block = ids[0] * of + base + step

    @pl.when(step == 0)
    def _():
        swap[...] = swap_matrix(16)

    row_alive = alive_rows(chain_ref, (blocks[0, block] * n_chan + ids[1]) * rows, rows)
    col_alive = alive_rows(chain_ref, (blocks[1, block] * n_sub + ids[2]) * cols, cols)
    group = hidden // cols
    for at in range(0, rows, group):
        values = pair_ref[0, pl.ds(at, group)].reshape(group * cols, channels)
        norm_and_gate(values, row_alive, col_alive, at, norm_ref, w_ref, gate_ref)
    open_layer(0, norm_ref[...], operand_refs[:chunks], operand_refs[chunks:], wide, laid, turned, swap)


def operand_scratch(rows, size, hidden):
    parts = hidden // size
    return [
        pltpu.VMEM((2, rows // parts, parts * size, hidden), jnp.bfloat16),
        pltpu.VMEM((size, rows, hidden), jnp.bfloat16),
        pltpu.VMEM((256, 256), jnp.bfloat16),
    ]


def operand_outputs(slots, count, rows, hidden, bands):
    kept = [count if n == 0 else slots for n in range(len(bands))] * 2
    return [jax.ShapeDtypeStruct((k, b, rows, hidden), jnp.bfloat16) for k, b in zip(kept, bands * 2)]


def slot_specs(arrays, slots, base):
    def spec(array):
        offset = base if array.shape[0] == slots else 0
        return pl.BlockSpec((1,) + array.shape[1:], lambda s, *_: (s + offset, 0, 0, 0))

    return [spec(a) for a in arrays]


def fill(out_shape, earlier, slots, n_before):
    if earlier is None:
        return [], [], {}
    shared = [n for n, o in enumerate(out_shape) if o.shape[0] == slots]
    specs = [pl.BlockSpec(memory_space=pl.ANY)] * len(shared)
    return [earlier[n] for n in shared], specs, {n_before + k: n for k, n in enumerate(shared)}


def open_operands(ids, blocks, pair, chains, w_in, wide, hidden, bands, base, count, earlier):
    slots, rows, cols, channels = pair.shape
    out_shape = [jax.ShapeDtypeStruct(pair.shape, jnp.float32)] + operand_outputs(slots, count, rows, hidden, bands)
    more, more_specs, aliases = fill(out_shape, earlier, slots, 6)
    return pl.pallas_call(
        functools.partial(open_kernel, hidden, len(bands), lax.axis_size("chan"), lax.axis_size("sub"), base, slots),
        grid_spec=pltpu.PrefetchScalarGridSpec(
            num_scalar_prefetch=2,
            grid=(count,),
            in_specs=slot_specs([pair], slots, base)
            + [
                pl.BlockSpec(chains.shape, lambda s, *_: (0, 0)),
                pl.BlockSpec((1,) + w_in.shape[1:], lambda s, *_: (0, 0, 0)),
                pl.BlockSpec(wide.shape, lambda s, *_: (0, 0)),
            ]
            + more_specs,
            out_specs=slot_specs(out_shape, slots, base),
            scratch_shapes=[pltpu.VMEM((rows, cols, channels), jnp.bfloat16)] + operand_scratch(rows, cols, hidden),
        ),
        out_shape=out_shape,
        input_output_aliases=aliases,
        compiler_params=pltpu.CompilerParams(vmem_limit_bytes=18 * mebi),
        cost_estimate=pl.CostEstimate(flops=1 << 33, bytes_accessed=1 << 20, transcendentals=0),
        name="open_operands",
    )(ids, blocks, pair, chains, w_in, wide, *more)


def far_kernel(layer, n_blk, far, n_chan, n_sub, of, bases, ids, blocks, mine, *rest):
    sources, (chain_ref, wide, left_ref, right_ref, norm_ref, laid, turned, swap) = rest[:-8], rest[-8:]
    step = pl.program_id(0)
    rows, cols, channels = norm_ref.shape
    holder = lax.rem(ids[0] - far + n_blk, n_blk)

    @pl.when(step == 0)
    def _():
        swap[...] = swap_matrix(16)

    group = channels // cols
    for side, out_ref in ((0, left_ref), (1, right_ref)):
        slot = mine[2 * step + side]
        refs = sources[side * len(bases) : (side + 1) * len(bases)]
        block = holder * of + slot
        row_alive = alive_rows(chain_ref, (blocks[0, block] * n_chan + ids[1]) * rows, rows)
        col_alive = alive_rows(chain_ref, (blocks[1, block] * n_sub + ids[2]) * cols, cols)
        for at in range(0, rows, group):
            values = refs[0][0, pl.ds(at, group)]
            for base, ref in zip(bases[1:], refs[1:]):
                values = jnp.where(slot >= base, ref[0, pl.ds(at, group)], values)
            norm_and_gate(values.reshape(group * cols, channels), row_alive, col_alive, at, norm_ref)
        if side == layer % 2:
            make_operand(side, norm_ref[...], wide, [out_ref], laid, swap)
        else:
            turn(norm_ref[...], turned, swap)
            make_operand(side, turned[...], wide, [out_ref], laid, swap)


def far_operands(layer, ids, blocks, mine, sources, chains, wide, far, capacity, of, hidden):
    n_blk = lax.axis_size("blk")
    _, rows, cols, channels = sources[0].shape
    bases = [sum(a.shape[0] for a in sources[:n]) for n in range(len(sources))]

    def source_spec(side, base, size):
        def place(t, ids, blocks, mine):
            return jnp.clip(mine[2 * t + side] - base, 0, size - 1), 0, 0, 0

        return pl.BlockSpec((1, rows, cols, channels), place)

    in_specs = [source_spec(side, b, a.shape[0]) for side in range(2) for b, a in zip(bases, sources)]
    in_specs += [pl.BlockSpec(chains.shape, lambda t, *_: (0, 0)), pl.BlockSpec(wide.shape, lambda t, *_: (0, 0))]
    shape = (capacity, hidden // (hidden // cols), rows, hidden)
    return pl.pallas_call(
        functools.partial(
            far_kernel, layer, n_blk, far, lax.axis_size("chan"), lax.axis_size("sub"), of, tuple(bases)
        ),
        grid_spec=pltpu.PrefetchScalarGridSpec(
            num_scalar_prefetch=3,
            grid=(capacity,),
            in_specs=in_specs,
            out_specs=[pl.BlockSpec((1,) + shape[1:], lambda t, *_: (t, 0, 0, 0))] * 2,
            scratch_shapes=[pltpu.VMEM((rows, cols, channels), jnp.bfloat16)] + operand_scratch(rows, cols, hidden),
        ),
        out_shape=[jax.ShapeDtypeStruct(shape, jnp.bfloat16)] * 2,
        compiler_params=pltpu.CompilerParams(vmem_limit_bytes=14 * mebi),
        cost_estimate=pl.CostEstimate(flops=1 << 33, bytes_accessed=1 << 20, transcendentals=0),
        name="far_operands",
    )(ids, blocks, mine, *sources, *sources, chains, wide)


def plan_kernel(n_blk, far, slots_dev, terms, capacity, ids, owners, slots, chosen, place, mine, seen):
    for shift in range(n_blk):
        seen[shift] = 0
        target = lax.rem(ids[0] + shift, n_blk)
        for e in range(2 * (capacity + 1)):
            chosen[2 * shift * (capacity + 1) + e] = 0
        found = jnp.int32(0)
        for e in range(slots_dev * terms):
            block, term = target * slots_dev + e // terms, e % terms
            at = 2 * (shift * (capacity + 1) + jnp.minimum(found, capacity))
            chosen[at] = slots[term, 0, block]
            chosen[at + 1] = slots[term, 1, block]
            found = found + (owners[term, block] == ids[0]).astype(jnp.int32)
    for e in range(slots_dev * terms):
        owner = owners[e % terms, ids[0] * slots_dev + e // terms]
        count = seen[owner]
        seen[owner] = count + 1
        place[e] = lax.rem(ids[0] - owner + n_blk, n_blk) * capacity + count
    for e in range(2 * (capacity + 1)):
        mine[e] = 0
    found = jnp.int32(0)
    for e in range(slots_dev * terms):
        block, term = ids[0] * slots_dev + e // terms, e % terms
        at = 2 * jnp.minimum(found, capacity)
        mine[at] = slots[term, 0, block]
        mine[at + 1] = slots[term, 1, block]
        found = found + (owners[term, block] == lax.rem(ids[0] - far + n_blk, n_blk)).astype(jnp.int32)


def make_plan(ids, owners, slots, n_blk, far, slots_dev, terms, capacity):
    scalars = pl.BlockSpec(memory_space=pltpu.SMEM)
    return pl.pallas_call(
        functools.partial(plan_kernel, n_blk, far, slots_dev, terms, capacity),
        in_specs=[scalars] * 3,
        out_specs=[scalars] * 3,
        out_shape=[
            jax.ShapeDtypeStruct((2 * n_blk * (capacity + 1),), jnp.int32),
            jax.ShapeDtypeStruct((slots_dev * terms,), jnp.int32),
            jax.ShapeDtypeStruct((2 * (capacity + 1),), jnp.int32),
        ],
        scratch_shapes=[pltpu.SMEM((n_blk,), jnp.int32)],
        compiler_params=pltpu.CompilerParams(vmem_limit_bytes=mebi),
        name="make_plan",
    )(ids, owners, slots)


def banded_kernel(shifts, capacity, pieces, n_refs, size, ids, chosen, *rest):
    refs, rest = rest[:n_refs], rest[n_refs:]
    out_refs, (left_held, right_held, out_held, sems, out_sems) = rest[: len(shifts)], rest[len(shifts) :]
    halves, _, bands, rows, hidden = left_held.shape
    parts = hidden // size
    at_once = 2 if capacity % 2 == 0 else 1

    def copy(n, source):
        side, half, base, *_ = pieces[n]
        target = (left_held, right_held)[side].at[half, pl.ds(base, refs[source].shape[0])]
        return pltpu.make_async_copy(refs[source], target, sems.at[n])

    for n, (*_, on, off) in enumerate(pieces):
        if on == off:
            copy(n, on).start()
        else:

            @pl.when(ids[3] == 1)
            def _(n=n, on=on):
                copy(n, on).start()

            @pl.when(ids[3] == 0)
            def _(n=n, off=off):
                copy(n, off).start()

    for n, piece in enumerate(pieces):
        copy(n, piece[-1]).wait()

    def leave(n):
        return pltpu.make_async_copy(out_held.at[pl.ds(n * capacity, capacity)], out_refs[n], out_sems.at[n])

    for n, shift in enumerate(shifts):

        def one(turn, carry, n=n, shift=shift):
            group = lane_group((size, hidden), size)
            for term in [turn * at_once + t for t in range(at_once)]:
                at = 2 * (shift * (capacity + 1) + term)
                left_slot, right_slot = chosen[at], chosen[at + 1]
                for band in range(bands):
                    left = jnp.concatenate([left_held[h, left_slot, band] for h in range(halves)], axis=1)
                    apart = []
                    for h in range(halves):
                        right = right_held[h, right_slot, band]
                        apart += [jnp.where(group == part, right, jnp.zeros_like(right)) for part in range(parts)]
                    made = dot(left, jnp.concatenate(apart, axis=0))
                    out_held[n * capacity + term, band] = made.astype(jnp.bfloat16)
            return carry

        lax.fori_loop(0, capacity // at_once, one, 0)
        leave(n).start()
    for n in range(len(shifts)):
        leave(n).wait()


def banded_products(shifts, ids, chosen, operands, capacity, size):
    refs, pieces = [], []

    def index_of(array):
        for n, known in enumerate(refs):
            if known is array:
                return n
        refs.append(array)
        return len(refs) - 1

    slots = 0
    for both in operands:
        for side in range(2):
            for half, (on, off) in enumerate(both[side]):
                pieces.append((side, half, slots, index_of(on), index_of(off)))
        slots += both[0][0][0].shape[0]
    halves = len(operands[0][0])
    _, bands, rows, hidden = operands[0][0][0][0].shape
    count = len(shifts) * capacity
    anywhere = pl.BlockSpec(memory_space=pl.ANY)
    return pl.pallas_call(
        functools.partial(banded_kernel, shifts, capacity, tuple(pieces), len(refs), size),
        grid_spec=pltpu.PrefetchScalarGridSpec(
            num_scalar_prefetch=2,
            grid=(),
            in_specs=[anywhere] * len(refs),
            out_specs=[anywhere] * len(shifts),
            scratch_shapes=[
                pltpu.VMEM((halves, slots, bands, rows, hidden), jnp.bfloat16),
                pltpu.VMEM((halves, slots, bands, size, hidden), jnp.bfloat16),
                pltpu.VMEM((count, bands, rows, hidden), jnp.bfloat16),
                pltpu.SemaphoreType.DMA((len(pieces),)),
                pltpu.SemaphoreType.DMA((len(shifts),)),
            ],
        ),
        out_shape=[jax.ShapeDtypeStruct((capacity, bands, rows, hidden), jnp.bfloat16)] * len(shifts),
        compiler_params=pltpu.CompilerParams(vmem_limit_bytes=10 * mebi),
        cost_estimate=pl.CostEstimate(
            flops=2 * count * bands * rows * hidden * hidden * halves, bytes_accessed=1, transcendentals=0
        ),
        name="banded_products",
    )(ids, chosen, *refs)


def close_kernel(layer, last, spots, chunks, n_chan, n_sub, base, of, terms, capacity, ids, blocks, place, *rest):
    n_parts = len(spots)
    arrived, rest = rest[:n_parts], rest[n_parts:]
    cur_ref, gate_ref, w_out_ref = rest[:3]
    if last:
        out_ref, held, wide_out, sems, swap = rest[3:]
    else:
        chain_ref, w_ref, wide = rest[3:6]
        out_ref, next_gate_ref, sent_ref, *operand_refs, held, wide_out, sems, norm_ref, laid, turned, swap = rest[
            -(2 * chunks + 10) :
        ]
        left_refs, right_refs = operand_refs[:chunks], operand_refs[chunks:]
    step = pl.program_id(0)
    _, rows, cols, channels = cur_ref.shape
    _, bands, _, hidden = held.shape
    parts, size = hidden // bands, bands

    def arrival(n):
        shift, at = spots[n]
        target = held.at[pl.ds(shift * capacity, capacity), pl.ds(at, arrived[n].shape[1])]
        return pltpu.make_async_copy(arrived[n], target, sems.at[n])

    @pl.when(step == 0)
    def _():
        for n in range(n_parts):
            arrival(n).start()
        wide_out[...] = jnp.zeros_like(wide_out)
        for part in range(parts):
            for a in range(parts):
                at = (part * parts + a) * bands
                wide_out[at : at + bands, a * channels : (a + 1) * channels] = w_out_ref[
                    0, part * bands : (part + 1) * bands, :
                ]
        swap[...] = swap_matrix(16)
        for n in range(n_parts):
            arrival(n).wait()

    if not last:
        block = ids[0] * of + base + step
        row_alive = alive_rows(chain_ref, (blocks[0, block] * n_chan + ids[1]) * rows, rows)
        col_alive = alive_rows(chain_ref, (blocks[1, block] * n_sub + ids[2]) * cols, cols)
    half = 16
    by_row = [[] for _ in range(rows)]
    for row in range(0, rows, half):
        for band in range(0, bands, half):
            taken = pl.ds(band, half), pl.ds(row, half)
            total = held[(place[(base + step) * terms], *taken)].astype(jnp.float32)
            for t in range(1, terms):
                total = total + held[(place[(base + step) * terms + t], *taken)].astype(jnp.float32)
            moved = swapped(total.astype(jnp.bfloat16), swap)
            for r in range(half):
                by_row[row + r].append(moved[r])
    groups = rows // parts
    pieces = []
    for g in range(groups):
        block = jnp.concatenate([x for a in range(parts) for x in by_row[g * parts + a]]).T
        pieces.append(jnp.concatenate([block[p * cols : (p + 1) * cols] for p in range(parts)], axis=1))
    mixture = jnp.concatenate(pieces)
    together = (lane_group((hidden, hidden), size) == lax.broadcasted_iota(jnp.int32, (hidden, hidden), 0) // size)
    together = together.astype(jnp.float32).astype(jnp.bfloat16)
    average = dot(mixture, jnp.concatenate([together] * parts)) * (1.0 / hidden)
    centred = [mixture[:, p * hidden : (p + 1) * hidden].astype(jnp.float32) - average for p in range(parts)]
    squares = sum(c * c for c in centred)
    high = squares.astype(jnp.bfloat16)
    low = (squares - high.astype(jnp.float32)).astype(jnp.bfloat16)
    variance = dot(jnp.concatenate([high, low], axis=1), jnp.concatenate([together] * 2)) * (1.0 / hidden)
    scale = lax.rsqrt(variance + norm_epsilon)
    normed = jnp.concatenate([(c * scale).astype(jnp.bfloat16) for c in centred], axis=1)
    update = dot(normed, wide_out[...])
    for g in range(groups):
        taken = pl.ds(g * parts, parts)
        change = jnp.concatenate(
            [update[g * cols : (g + 1) * cols, a * channels : (a + 1) * channels] for a in range(parts)]
        )
        gate = gate_ref[0, taken].reshape(parts * cols, channels)
        current = cur_ref[0, taken].astype(jnp.float32).reshape(parts * cols, channels)
        result = (current + gate * change).astype(jnp.bfloat16)
        out_ref[0, taken] = result.reshape(parts, cols, channels)
        if not last:
            sent_ref[0, taken] = result.reshape(parts, cols, channels)
            norm_and_gate(result, row_alive, col_alive, g * parts, norm_ref, w_ref, next_gate_ref)
    if not last:
        open_layer(layer + 1, norm_ref[...], left_refs, right_refs, wide, laid, turned, swap)


def close_layer(
    layer, arrived, ids, blocks, place, current, gate, w_out, capacity, terms, chains, w_in, wide, last, bands, base, count, earlier
):
    flat, spots = [part for part, *_ in arrived], tuple((shift, at) for _, shift, at in arrived)
    n_blk = lax.axis_size("blk")
    slots, rows, cols, channels = current.shape
    hidden = w_out.shape[1]

    def layer_spec(array, index):
        return pl.BlockSpec((1,) + array.shape[1:], lambda s, *_: (index, 0, 0))

    in_specs = [pl.BlockSpec(memory_space=pl.ANY)] * len(flat)
    in_specs += slot_specs([current, gate], slots, base) + [layer_spec(w_out, layer)]
    operands = [*flat, current, gate, w_out]
    out_shape = [jax.ShapeDtypeStruct(current.shape, jnp.bfloat16)]
    scratch = [
        pltpu.VMEM((n_blk * capacity, sum(bands[layer]), rows, hidden), jnp.bfloat16),
        pltpu.VMEM((hidden // cols * hidden, hidden // cols * channels), jnp.bfloat16),
        pltpu.SemaphoreType.DMA((len(flat),)),
    ]
    if not last:
        operands += [chains, w_in, wide]
        in_specs += [pl.BlockSpec(chains.shape, lambda s, *_: (0, 0)), layer_spec(w_in, layer + 1)]
        in_specs += [pl.BlockSpec(wide.shape, lambda s, *_: (0, 0))]
        out_shape += [jax.ShapeDtypeStruct(current.shape, jnp.float32)]
        out_shape += [jax.ShapeDtypeStruct((count,) + current.shape[1:], jnp.bfloat16)]
        out_shape += operand_outputs(slots, count, cols, hidden, bands[layer + 1])
        scratch += [pltpu.VMEM((rows, cols, channels), jnp.bfloat16)] + operand_scratch(cols, rows, hidden)
    else:
        scratch += [pltpu.VMEM((256, 256), jnp.bfloat16)]
    more, more_specs, aliases = fill(out_shape, earlier, slots, 3 + len(operands))
    return pl.pallas_call(
        functools.partial(
            close_kernel,
            *(layer, last, spots, 0 if last else len(bands[layer + 1]), lax.axis_size("chan"), lax.axis_size("sub")),
            *(base, slots, terms, capacity),
        ),
        grid_spec=pltpu.PrefetchScalarGridSpec(
            num_scalar_prefetch=3,
            grid=(count,),
            in_specs=in_specs + more_specs,
            out_specs=slot_specs(out_shape, slots, base),
            scratch_shapes=scratch,
        ),
        out_shape=out_shape,
        input_output_aliases=aliases,
        compiler_params=pltpu.CompilerParams(vmem_limit_bytes=24 * mebi),
        cost_estimate=pl.CostEstimate(flops=1 << 33, bytes_accessed=1 << 20, transcendentals=0),
        name="close_layer",
    )(ids, blocks, place, *operands, *more)


def after(value, *others):
    return lax.optimization_barrier((value, *others))[0]


def exchange_bands_outgoing(left, right, over):
    both = ("chan", "sub")
    other = lax.ppermute(left, "sub", [(0, 1), (1, 0)])
    one = lax.ppermute(right, both, [(0, 2), (3, 1), (1, 0), (2, 3)])
    two = lax.ppermute(right, both, [(1, 2), (2, 1)])
    return [(other, left), (left, other)], [(one, one), (right, two)]


def exchange_bands_incoming(left, right, over):
    both = ("chan", "sub")
    one = lax.ppermute(left, both, [(1, 3), (2, 0), (0, 1), (3, 2)])
    other = lax.ppermute(right, "chan", [(0, 1), (1, 0)])
    two = lax.ppermute(after(one, other if over is None else over), both, [(0, 1), (3, 2)])
    return [(left, one), (one, two)], [(right, right), (other, other)]


def banded(pair, ids, blocks, owners, slot_of, chains, w_in, w_out, capacity, terms, n_blk):
    slots, rows, cols, channels = pair.shape
    hidden = w_out.shape[1]
    far = 1
    middle = n_blk // 2
    near = [s for s in (middle, *range(1, n_blk)) if s != far]
    near = [s for n, s in enumerate(near) if s not in near[:n]] + [0]
    layers = w_in.shape[0]
    current = pair
    bands = [[14, 18], [20, 12]]
    chosen, place, mine = make_plan(ids, owners, slot_of, n_blk, far, slots, terms, capacity)
    in_order = jnp.repeat(jnp.arange(capacity, dtype=jnp.int32), 2)
    half = slots // 2
    halves = [(0, half), (half, slots - half)]

    def over_blk(value, shift):
        return lax.ppermute(value, "blk", [(p, (p + shift) % n_blk) for p in range(n_blk)])

    for layer in range(layers):
        count = len(bands[layer])
        if layer == 0:
            raw = [over_blk(pair, far)]
            calls, wide = [None], spread_weights(w_in, 0, cols)
            for base, size in halves:
                calls.append(
                    open_operands(ids, blocks, pair, chains, w_in, wide, hidden, bands[0], base, size, calls[-1])
                )
            gate = calls[-1][0]
        else:
            raw = []
            for call in calls[1:]:
                raw.append(over_blk(after(call[2], *raw) if raw else call[2], far))
        operands = [call[-2 * count :] for call in calls[1:]]
        exchange = exchange_bands_incoming if layer % 2 else exchange_bands_outgoing
        arrived, by_shift = [], {}
        for chunk in range(count):
            if chunk == 0:
                exchanged = []
                over = operands[-1][count]
                for left, right in [(o[0], o[count]) for o in operands]:
                    if exchanged and layer % 2:
                        (_, (one, two)), (_, (other, _)) = exchanged[-1]
                        left, right = lax.optimization_barrier((left, right, one, other))[:2]
                        right = after(right, two)
                    elif exchanged:
                        ((other, _), _), ((one, _), (_, two)) = exchanged[-1]
                        left, right = lax.optimization_barrier((left, right, other, one, two))[:2]
                    exchanged.append(exchange(left, right, over))
            else:
                left, right = operands[-1][chunk], operands[-1][count + chunk]
                if layer % 2:
                    (_, (_, two)), (_, (other, _)) = exchanged[-1]
                    left, right = lax.optimization_barrier((left, right, two, other))[:2]
                else:
                    ((other, _), _), ((one, _), (_, two)) = exchanged[-1]
                    left = after(left, other)
                    right = after(right, one, two, made[-1])
                exchanged = [exchange(left, right, list(by_shift.values())[-1] if by_shift else made[-1])]
                ids = after(ids, *by_shift.values())
            made = banded_products(near, ids, chosen, exchanged, capacity, cols)
            start = sum(bands[layer][:chunk])
            for shift, part in zip(near, made):
                if shift:
                    part = over_blk(after(part, by_shift.get(shift, raw[-1])), shift)
                    by_shift[shift] = part
                arrived.append((part, shift, start))
            if chunk == 0:
                sources = list(lax.optimization_barrier((*raw, made[-1]))[:-1])
                far_left, far_right = far_operands(
                    layer, ids, blocks, mine, sources, chains, wide, far, capacity, slots, hidden
                )
        far_exchanged = [exchange(far_left, far_right, list(by_shift.values())[-1] if by_shift else made[-1])]
        (part,) = banded_products([0], ids, in_order, far_exchanged, capacity, cols)
        arrived.append((part, far, 0))
        last = layer == layers - 1
        calls = [None]
        if not last:
            wide = spread_weights(after(w_in, made[-1]), layer + 1, cols)
        for base, size in [(0, slots)] if last else halves:
            calls.append(
                close_layer(
                    *(layer, arrived, ids, blocks, place, current, gate, w_out, capacity, terms, chains, w_in, wide, last),
                    *(bands, base, size, calls[-1]),
                )
            )
        if last:
            return calls[-1][0]
        current, gate = calls[-1][:2]


def per_device(pair, block_list, term_owner, term_slots, chain_ids, w_in, w_out):
    n_blk = lax.axis_size("blk")
    n_chan = lax.axis_size("chan")
    n_sub = lax.axis_size("sub")
    position = lax.axis_index("blk")
    row_group = lax.axis_index("chan")
    col_group = lax.axis_index("sub")
    slots, rows, cols, channels = pair.shape
    hidden = w_out.shape[1]
    terms = term_owner.shape[1]
    capacity = max(2, -(-slots * terms // n_blk))
    fast = n_chan == 2 and n_sub == 2
    on_diagonal = (row_group == col_group).astype(jnp.int32)
    ids = jnp.stack([position, row_group, col_group, on_diagonal]).astype(jnp.int32)
    blocks = block_list.T
    owners = term_owner.T
    slot_of = jnp.transpose(term_slots, (1, 2, 0))
    chains = chain_ids.reshape(-1, 128)
    if fast and n_blk > 1 and rows == cols == 32 and channels == hidden == 128:
        return banded(pair, ids, blocks, owners, slot_of, chains, w_in, w_out, capacity, terms, n_blk)
    shifts = [n_blk // 2] + [s for s in range(1, n_blk) if s != n_blk // 2] + [0]

    def all_products(lefts, right):
        parts = [None] * n_blk
        for shift in shifts:
            made = term_products(shift, ids, owners, slot_of, lefts, right, capacity, slots, terms)
            if shift:
                pairs = [(p, (p + shift) % n_blk) for p in range(n_blk)]
                made = lax.ppermute(made, "blk", pairs)
            parts[shift] = made
        return parts

    def at_home(layer, parts, current, gate, at, of, into=None):
        last = layer == w_in.shape[0] - 1
        return home(
            layer, parts, ids, blocks, owners, current, gate, w_out, capacity, terms, at, of, chains, w_in, last, into
        )

    gate, left, *rights = first_operands(ids, blocks, pair, chains, w_in, hidden, 2 if fast else 1)
    lefts, chunks = exchange_outgoing(left, rights, n_chan, n_sub)
    count = len(chunks)
    made = [all_products(lefts, right) for right in chunks]
    homes = [at_home(0, parts, pair, gate, at, count) for at, parts in enumerate(made)]
    lefts, chunks = exchange_incoming([h[2] for h in homes], [h[3] for h in homes], n_chan, n_sub)
    made = [all_products(lefts, right) for right in chunks]
    out = None
    for at, parts in enumerate(made):
        (out,) = at_home(1, parts, homes[at][0], homes[at][1], at, count, into=out)
    return out


def solution(mesh):
    in_specs = (
        P(("groups", "blk"), "chan", "sub", None),
        P("groups", None),
        P("groups", None),
        P("groups", None, None),
        P("groups"),
        P(),
        P(),
    )
    out_specs = P(("groups", "blk"), "chan", "sub", None)
    return jax.shard_map(
        per_device, mesh=mesh, in_specs=in_specs, out_specs=out_specs, check_vma=False
    )
```

```python
import functools

import jax
import jax.numpy as jnp
from jax import lax
from jax.experimental import pallas as pl
from jax.experimental.pallas import tpu as pltpu
from jax.sharding import PartitionSpec as P

norm_epsilon = 1e-05
mebi = 1024 * 1024
vmem_limit = 56 * mebi


def sigmoid(values):
    return 0.5 + 0.5 * jnp.tanh(0.5 * values)


def layer_norm(values):
    values = values.astype(jnp.float32)
    centred = values - jnp.mean(values, axis=-1, keepdims=True)
    variance = jnp.mean(centred * centred, axis=-1, keepdims=True)
    return centred * lax.rsqrt(variance + norm_epsilon)


def alive_rows(chain_ref, start, size):
    lanes = chain_ref.shape[1]
    line = chain_ref[pl.ds(start // lanes, 1), :] >= 0
    spot = lax.broadcasted_iota(jnp.int32, (size, lanes), 0) + lax.rem(start, lanes)
    pick = jnp.logical_and(lax.broadcasted_iota(jnp.int32, (size, lanes), 1) == spot, line)
    return dot(pick.astype(jnp.float32).astype(jnp.bfloat16), jnp.ones((lanes, lanes), jnp.bfloat16))


def dot(a, b):
    return jnp.dot(a, b, preferred_element_type=jnp.float32)


def gated_pair(projected, mask, hidden):
    left = mask * sigmoid(projected[:, hidden : 2 * hidden]) * projected[:, :hidden]
    right = mask * sigmoid(projected[:, 3 * hidden : 4 * hidden]) * projected[:, 2 * hidden : 3 * hidden]
    return left.astype(jnp.bfloat16), right.astype(jnp.bfloat16)


def first_kernel(hidden, row_parts, n_chan, n_sub, ids, blocks, pair_ref, chain_ref, w_ref, gate_ref, left_ref, *rest):
    right_refs, (norm_ref, turned_ref) = rest[:row_parts], rest[row_parts:]
    slots = pl.num_programs(0)
    _, rows, cols, channels = pair_ref.shape
    block = ids[0] * slots + pl.program_id(0)
    row_alive = alive_rows(chain_ref, (blocks[0, block] * n_chan + ids[1]) * rows, rows)
    col_alive = alive_rows(chain_ref, (blocks[1, block] * n_sub + ids[2]) * cols, cols)
    group = max(1, 256 // cols)
    for start in range(0, rows, group):
        at = pl.ds(start, group)
        normed = layer_norm(pair_ref[0, at].reshape(group * cols, channels))
        norm_ref[pl.ds(start * cols, group * cols), :] = normed
        gate = sigmoid(dot(normed.astype(jnp.bfloat16), w_ref[0, :, 4 * hidden :]))
        gate_ref[0, at] = gate.reshape(group, cols, channels)
    for col in range(cols):
        turned_ref[col] = norm_ref[pl.ds(col, rows, stride=cols), :].astype(jnp.bfloat16)
    step = max(1, 128 // rows)
    part = rows // row_parts
    for start in range(0, cols, step):
        taken = turned_ref[start : start + step].reshape(step * rows, channels)
        projected = dot(taken, w_ref[0, :, : 4 * hidden])
        mask = col_alive[start : start + step][:, None, :] * row_alive[None, :, :]
        left, right = gated_pair(projected, mask.reshape(step * rows, -1), hidden)
        left_ref[0, start : start + step] = left.reshape(step, rows, hidden)
        right = right.reshape(step, rows, hidden)
        for p, right_ref in enumerate(right_refs):
            right_ref[0, start : start + step] = right[:, p * part : (p + 1) * part]


def first_operands(ids, blocks, pair, chains, w_in, hidden, row_parts):
    slots, rows, cols, channels = pair.shape
    part = rows // row_parts
    operand = jax.ShapeDtypeStruct((slots, cols, rows, hidden), jnp.bfloat16)
    right = jax.ShapeDtypeStruct((slots, cols, part, hidden), jnp.bfloat16)
    return pl.pallas_call(
        functools.partial(first_kernel, hidden, row_parts, lax.axis_size("chan"), lax.axis_size("sub")),
        grid_spec=pltpu.PrefetchScalarGridSpec(
            num_scalar_prefetch=2,
            grid=(slots,),
            in_specs=[
                pl.BlockSpec((1, rows, cols, channels), lambda s, *_: (s, 0, 0, 0)),
                pl.BlockSpec(chains.shape, lambda s, *_: (0, 0)),
                pl.BlockSpec((1,) + w_in.shape[1:], lambda s, *_: (0, 0, 0)),
            ],
            out_specs=[
                pl.BlockSpec((1, rows, cols, channels), lambda s, *_: (s, 0, 0, 0)),
                pl.BlockSpec((1, cols, rows, hidden), lambda s, *_: (s, 0, 0, 0)),
            ]
            + [pl.BlockSpec((1, cols, part, hidden), lambda s, *_: (s, 0, 0, 0))] * row_parts,
            scratch_shapes=[
                pltpu.VMEM((rows * cols, channels), jnp.float32),
                pltpu.VMEM((cols, rows, channels), jnp.bfloat16),
            ],
        ),
        out_shape=[jax.ShapeDtypeStruct(pair.shape, jnp.float32), operand] + [right] * row_parts,
        compiler_params=pltpu.CompilerParams(vmem_limit_bytes=vmem_limit),
        name="first_operands",
    )(ids, blocks, pair, chains, w_in)


def product_kernel(shift, n_blk, slots_dev, terms, capacity, pieces, n_refs, ids, owners, slots, *rest):
    refs = rest[:n_refs]
    out_ref, left_held, right_held, right_wide, chosen, sems = rest[n_refs:]
    step = pl.program_id(0)
    turn = lax.rem(step, 2)
    _, depth, n_i, hidden = left_held.shape
    n_j = right_wide.shape[1]

    @pl.when(step == 0)
    def _():
        target = lax.rem(ids[0] + shift, n_blk)
        for e in range(2 * capacity):
            chosen[e] = 0

        def scan(e, count):
            block, term = target * slots_dev + e // terms, lax.rem(e, terms)
            here = jnp.logical_and(owners[term, block] == ids[0], count < capacity)

            @pl.when(here)
            def _():
                chosen[2 * count] = slots[term, 0, block]
                chosen[2 * count + 1] = slots[term, 1, block]

            return count + here.astype(jnp.int32)

        lax.fori_loop(0, slots_dev * terms, scan, jnp.int32(0))

    def copy(n, term, buffer, source):
        side, _, _, k0, depth_of, i0, size = pieces[n]
        held = (left_held, right_held)[side]
        return pltpu.make_async_copy(
            refs[source].at[chosen[2 * term + side]],
            held.at[buffer, pl.ds(k0, depth_of), pl.ds(i0, size), :],
            sems.at[buffer, n],
        )

    def start(term, buffer):
        for n, (_, on, off, *_) in enumerate(pieces):
            if on == off:
                copy(n, term, buffer, on).start()
            else:

                @pl.when(ids[3] == 1)
                def _(n=n, on=on):
                    copy(n, term, buffer, on).start()

                @pl.when(ids[3] == 0)
                def _(n=n, off=off):
                    copy(n, term, buffer, off).start()

    @pl.when(step == 0)
    def _():
        start(0, 0)

    @pl.when(step + 1 < capacity)
    def _():
        start(step + 1, 1 - turn)

    for n, piece in enumerate(pieces):
        copy(n, step, turn, piece[1]).wait()

    span = 8

    def widen(n, carry):
        at = pl.ds(n * span, span)
        right_wide[at] = right_held[turn, at].astype(jnp.float32)
        return carry

    lax.fori_loop(0, depth // span, widen, 0)

    group = min(8, n_j)
    unroll = 4
    for j0 in range(0, n_j, group):

        def body(n, sums):
            for u in range(unroll):
                k = n * unroll + u
                left = left_held[turn, k].astype(jnp.float32).reshape(n_i // 8, 8, hidden)
                sums = tuple(
                    total + left * right_wide[k, pl.ds(j0 + j, 8, stride=0), :][None]
                    for j, total in enumerate(sums)
                )
            return sums

        zero = jnp.zeros((n_i // 8, 8, hidden), jnp.float32)
        sums = lax.fori_loop(0, depth // unroll, body, (zero,) * group)
        for j, total in enumerate(sums):
            out_ref[0, j0 + j] = total.reshape(n_i, hidden).astype(jnp.bfloat16)


def term_products(shift, ids, owners, slots, lefts, rights, capacity, slots_dev, terms):
    n_blk = lax.axis_size("blk")
    refs, pieces = [], []

    def index_of(array):
        for n, known in enumerate(refs):
            if known is array:
                return n
        refs.append(array)
        return len(refs) - 1

    for side, operands in ((0, lefts), (1, rights)):
        for on, off, k0, i0 in operands:
            pieces.append((side, index_of(on), index_of(off), k0, on.shape[1], i0, on.shape[2]))
    hidden = lefts[0][0].shape[3]
    n_i = max(p[5] + p[6] for p in pieces if p[0] == 0)
    n_j = max(p[5] + p[6] for p in pieces if p[0] == 1)
    depth = max(p[3] + p[4] for p in pieces)
    return pl.pallas_call(
        functools.partial(
            product_kernel, shift, n_blk, slots_dev, terms, capacity, tuple(pieces), len(refs)
        ),
        grid_spec=pltpu.PrefetchScalarGridSpec(
            num_scalar_prefetch=3,
            grid=(capacity,),
            in_specs=[pl.BlockSpec(memory_space=pl.ANY)] * len(refs),
            out_specs=pl.BlockSpec((1, n_j, n_i, hidden), lambda t, *_: (t, 0, 0, 0)),
            scratch_shapes=[
                pltpu.VMEM((2, depth, n_i, hidden), jnp.bfloat16),
                pltpu.VMEM((2, depth, n_j, hidden), jnp.bfloat16),
                pltpu.VMEM((depth, n_j, hidden), jnp.float32),
                pltpu.SMEM((2 * capacity,), jnp.int32),
                pltpu.SemaphoreType.DMA((2, len(pieces))),
            ],
        ),
        out_shape=jax.ShapeDtypeStruct((capacity, n_j, n_i, hidden), jnp.bfloat16),
        compiler_params=pltpu.CompilerParams(vmem_limit_bytes=vmem_limit),
        cost_estimate=pl.CostEstimate(
            flops=2 * capacity * n_i * n_j * depth * hidden * 100,
            bytes_accessed=capacity * (depth * (n_i + n_j) + n_i * n_j) * hidden * 2,
            transcendentals=0,
        ),
        name="term_products",
    )(ids, owners, slots, *refs)


def home_kernel(last, hidden, n_blk, n_chan, n_sub, at, of, slots_dev, terms, capacity, ids, blocks, owners, *rest):
    parts, rest = rest[:n_blk], rest[n_blk:]
    scratch, rest = rest[-5:], rest[:-5]
    held, turned, place, seen, sems = scratch
    cur_ref, gate_ref, w_out_ref = rest[:3]
    if last:
        out_ref = rest[-1]
    else:
        chain_ref, w_ref, out_ref, next_gate_ref, left_ref, right_ref = rest[3:]
    step = pl.program_id(0)
    _, rows, cols, channels = cur_ref.shape

    def arrival(shift):
        return pltpu.make_async_copy(parts[shift], held.at[pl.ds(shift * capacity, capacity)], sems.at[shift])

    @pl.when(step == 0)
    def _():
        for shift in range(n_blk):
            arrival(shift).start()
            seen[shift] = 0

        def scan(e, carry):
            owner = owners[lax.rem(e, terms), ids[0] * slots_dev + e // terms]
            shift = lax.rem(ids[0] - owner + n_blk, n_blk)
            count = seen[owner]
            seen[owner] = count + 1
            place[e] = shift * capacity + count
            return carry

        lax.fori_loop(0, slots_dev * terms, scan, jnp.int32(0))
        for shift in range(n_blk):
            arrival(shift).wait()

    if not last:
        block = ids[0] * slots_dev + step
        row_alive = alive_rows(chain_ref, (blocks[0, block] * n_chan + ids[1]) * rows, rows)
        col_alive = alive_rows(chain_ref, ((blocks[1, block] * n_sub + ids[2]) * of + at) * cols, cols)
    span = max(1, 128 // rows)
    for start in range(0, cols, span):
        taken = pl.ds(start, span)
        total = held[place[step * terms], taken].astype(jnp.float32)
        for t in range(1, terms):
            total = total + held[place[step * terms + t], taken].astype(jnp.float32)
        rounded = total.astype(jnp.bfloat16).astype(jnp.float32)
        turned[pl.ds(start * rows, span * rows), :] = rounded.reshape(span * rows, hidden)
    group = min(rows, max(1, 256 // cols))
    for start in range(0, rows, group):
        taken = pl.ds(start, group)
        mixture = jnp.concatenate(
            [turned[pl.ds(row, cols, stride=rows), :].astype(jnp.bfloat16) for row in range(start, start + group)]
        )
        update = dot(layer_norm(mixture).astype(jnp.bfloat16), w_out_ref[0])
        current = cur_ref[0, taken].astype(jnp.float32).reshape(group * cols, channels)
        gate = gate_ref[0, taken].reshape(group * cols, channels)
        result = (current + gate * update).astype(jnp.bfloat16)
        out_ref[0, taken] = result.reshape(group, cols, channels)
        if not last:
            normed = layer_norm(result).astype(jnp.bfloat16)
            projected = dot(normed, w_ref[0])
            next_gate_ref[0, taken] = sigmoid(projected[:, 4 * hidden :]).reshape(group, cols, channels)
            mask = row_alive[start : start + group][:, None, :] * col_alive[None, :, :]
            left, right = gated_pair(projected, mask.reshape(group * cols, channels), hidden)
            left_ref[0, taken] = left.reshape(group, cols, hidden)
            right_ref[0, taken] = right.reshape(group, cols, hidden)


def home(layer, parts, ids, blocks, owners, current, gate, w_out, capacity, terms, at, of, chains, w_in, last, into=None):
    n_blk = len(parts)
    slots, rows, _, channels = current.shape
    hidden = w_out.shape[1]
    cols = parts[0].shape[1]
    chunk = (1, rows, cols, channels)

    def chunk_spec(array):
        whole = array.shape[2] != cols
        return pl.BlockSpec(chunk, lambda s, *_: (s, 0, at if whole else 0, 0))

    def layer_spec(array, index):
        return pl.BlockSpec((1,) + array.shape[1:], lambda s, *_: (index, 0, 0))

    in_specs = [pl.BlockSpec(memory_space=pl.ANY)] * n_blk + [
        chunk_spec(current),
        chunk_spec(gate),
        layer_spec(w_out, layer),
    ]
    operands = [*parts, current, gate, w_out]
    aliases = {}
    if last:
        if into is not None:
            aliases = {3 + len(operands): 0}
            operands.append(into)
            in_specs.append(pl.BlockSpec(memory_space=pl.ANY))
        out_shape = [jax.ShapeDtypeStruct((slots, rows, cols * of, channels), jnp.bfloat16)]
        out_specs = [pl.BlockSpec(chunk, lambda s, *_: (s, 0, at, 0))]
    else:
        operands += [chains, w_in]
        in_specs += [pl.BlockSpec(chains.shape, lambda s, *_: (0, 0)), layer_spec(w_in, layer + 1)]
        small = (slots, rows, cols, channels)
        out_shape = [jax.ShapeDtypeStruct(small, t) for t in (jnp.bfloat16, jnp.float32, jnp.bfloat16, jnp.bfloat16)]
        out_specs = [pl.BlockSpec(chunk, lambda s, *_: (s, 0, 0, 0))] * 4
    return pl.pallas_call(
        functools.partial(
            home_kernel, last, hidden, n_blk, lax.axis_size("chan"), lax.axis_size("sub"), at, of, slots, terms, capacity
        ),
        grid_spec=pltpu.PrefetchScalarGridSpec(
            num_scalar_prefetch=3,
            grid=(slots,),
            in_specs=in_specs,
            out_specs=out_specs,
            scratch_shapes=[
                pltpu.VMEM((n_blk * capacity, cols, rows, hidden), jnp.bfloat16),
                pltpu.VMEM((rows * cols, hidden), jnp.float32),
                pltpu.SMEM((slots * terms,), jnp.int32),
                pltpu.SMEM((n_blk,), jnp.int32),
                pltpu.SemaphoreType.DMA((n_blk,)),
            ],
        ),
        out_shape=out_shape,
        input_output_aliases=aliases,
        compiler_params=pltpu.CompilerParams(vmem_limit_bytes=vmem_limit),
        cost_estimate=pl.CostEstimate(
            flops=2 * slots * rows * cols * channels * 6 * channels * 10,
            bytes_accessed=slots * rows * cols * channels * 16,
            transcendentals=0,
        ),
        name="home",
    )(ids, blocks, owners, *operands)


def exchange_outgoing(left, rights, n_chan, n_sub):
    if n_chan == 2 and n_sub == 2:
        both = ("chan", "sub")
        other_left = lax.ppermute(left, "sub", [(0, 1), (1, 0)])
        lefts = [(other_left, left, 0, 0), (left, other_left, left.shape[1], 0)]
        chunks = []
        for right in rights:
            if chunks:
                (one, *_), (_, two, *_) = chunks[-1]
                right, *_ = lax.optimization_barrier((right, one, two))
            one = lax.ppermute(right, both, [(0, 2), (3, 1), (1, 0), (2, 3)])
            two = lax.ppermute(right, both, [(1, 2), (2, 1)])
            chunks.append([(one, one, 0, 0), (right, two, right.shape[1], 0)])
        return lefts, chunks
    left = lax.all_gather(left, "sub", axis=1, tiled=True)
    right = jnp.concatenate(rights, axis=2)
    right = lax.all_gather(right, "chan", axis=2, tiled=True)
    right = lax.all_to_all(right, "sub", split_axis=2, concat_axis=1, tiled=True)
    cols = right.shape[2] // 2
    chunks = [right[:, :, :cols], right[:, :, cols:]]
    return [(left, left, 0, 0)], [[(r, r, 0, 0)] for r in chunks]


def exchange_incoming(lefts, rights, n_chan, n_sub):
    if n_chan == 2 and n_sub == 2:
        both = ("chan", "sub")
        left_pieces, chunks = [], []
        at = 0
        for left, right in zip(lefts, rights):
            depth = left.shape[1]
            one = lax.ppermute(left, both, [(1, 3), (2, 0), (0, 1), (3, 2)])
            two = lax.ppermute(one, both, [(0, 1), (3, 2)])
            left_pieces += [(left, one, 0, at), (one, two, depth, at)]
            other = lax.ppermute(right, "chan", [(0, 1), (1, 0)])
            chunks.append([(right, right, 0, 0), (other, other, depth, 0)])
            at += left.shape[2]
        return left_pieces, chunks
    left = lax.all_gather(jnp.concatenate(lefts, axis=2), "chan", axis=1, tiled=True)
    left = lax.all_gather(left, "sub", axis=2, tiled=True)
    size = left.shape[2] // n_chan
    left = lax.dynamic_slice_in_dim(left, lax.axis_index("chan") * size, size, 2)
    gathered = [lax.all_gather(right, "chan", axis=1, tiled=True) for right in rights]
    return [(left, left, 0, 0)], [[(r, r, 0, 0)] for r in gathered]


def lane_group(shape, size):
    return lax.broadcasted_iota(jnp.int32, shape, 1) // size


def spread_kernel(size, w_ref, wide_ref):
    hidden = w_ref.shape[1]
    parts = hidden // size
    for side in range(2):
        for kind in range(2):
            start = (2 * side + kind) * hidden
            weights = 0.5 * w_ref[0, :, start : start + hidden].astype(jnp.float32)
            group = lane_group(weights.shape, size)
            for part in range(parts):
                kept = jnp.where(group == part, weights, 0.0)
                at = ((side * parts + part) * 2 + kind) * hidden
                for a in range(parts):
                    moved = pltpu.roll(kept, ((a - part) % parts) * size, 1) if a != part else kept
                    wide_ref[a * hidden : (a + 1) * hidden, at : at + hidden] = moved.astype(jnp.bfloat16)


def spread_weights(w_in, layer, size):
    hidden = w_in.shape[1]
    parts = hidden // size
    shape = (parts * hidden, 4 * parts * hidden)
    return pl.pallas_call(
        functools.partial(spread_kernel, size),
        grid=(1,),
        in_specs=[pl.BlockSpec((1,) + w_in.shape[1:], lambda s: (layer, 0, 0))],
        out_specs=pl.BlockSpec(shape, lambda s: (0, 0)),
        out_shape=jax.ShapeDtypeStruct(shape, jnp.bfloat16),
        compiler_params=pltpu.CompilerParams(vmem_limit_bytes=16 * mebi),
        cost_estimate=pl.CostEstimate(flops=1 << 30, bytes_accessed=1 << 20, transcendentals=0),
        name="spread_weights",
    )(w_in)


def swap_matrix(half):
    shape = (half * half, half * half)
    to, of = lax.broadcasted_iota(jnp.int32, shape, 0), lax.broadcasted_iota(jnp.int32, shape, 1)
    same = jnp.logical_and(to // half == lax.rem(of, half), lax.rem(to, half) == of // half)
    return same.astype(jnp.float32).astype(jnp.bfloat16)


def swapped(values, swap_ref):
    half, _, lanes = values.shape
    moved = dot(swap_ref[...], values.reshape(half * half, lanes))
    return moved.astype(jnp.bfloat16).reshape(half, half, lanes)


def turn(taken, turned, swap_ref):
    half = 16
    for x in range(0, taken.shape[0], half):
        for y in range(0, taken.shape[1], half):
            turned[y : y + half, x : x + half] = swapped(taken[x : x + half, y : y + half], swap_ref)


def make_operand(side, taken, wide_ref, out_refs, laid, swap_ref):
    rows, size, hidden = taken.shape
    parts, bands, half = hidden // size, size, 16
    groups = rows // parts
    stacked = jnp.concatenate(
        [jnp.concatenate([taken[g * parts + a] for a in range(parts)], axis=1) for g in range(groups)], axis=0
    )
    for part in range(parts):
        at = (side * parts + part) * 2 * hidden
        made = dot(stacked, wide_ref[:, at : at + 2 * hidden])
        value = made[:, :hidden] * (1.0 + jnp.tanh(made[:, hidden:]))
        laid[side, :, part * size : (part + 1) * size, :] = value.astype(jnp.bfloat16).reshape(groups, size, hidden)
    blocks = [laid[side, g].T for g in range(groups)]
    starts = [sum(ref.shape[1] for ref in out_refs[:n]) for n in range(len(out_refs))]
    for first in range(0, bands, half):
        for row in range(0, rows, half):
            tiles = []
            for r in range(row, row + half):
                at = r % parts * bands + first
                tiles.append(blocks[r // parts][at : at + half])
            moved = swapped(jnp.stack(tiles), swap_ref)
            for start, ref in zip(starts, out_refs):
                low, high = max(start, first), min(start + ref.shape[1], first + half)
                if low < high:
                    ref[0, low - start : high - start, row : row + half] = moved[low - first : high - first]


def open_layer(layer, natural, left_refs, right_refs, wide, laid, turned, swap):
    turn(natural, turned, swap)
    for side, refs in ((0, left_refs), (1, right_refs)):
        make_operand(side, natural if side == layer % 2 else turned[...], wide, refs, laid, swap)


def norm_and_gate(values, row_alive, col_alive, at, norm_ref, w_ref=None, gate_ref=None):
    _, cols, channels = norm_ref.shape
    rows = values.shape[0] // cols
    normed = layer_norm(values)
    if gate_ref is not None:
        gate = sigmoid(dot(normed.astype(jnp.bfloat16), w_ref[0, :, -channels:]))
        gate_ref[0, pl.ds(at, rows)] = gate.reshape(rows, cols, channels).astype(gate_ref.dtype)
    mask = row_alive[at : at + rows, None, :] * col_alive[None, :, :]
    norm_ref[pl.ds(at, rows)] = (normed.reshape(rows, cols, channels) * mask).astype(jnp.bfloat16)


def open_kernel(hidden, chunks, n_chan, n_sub, base, of, ids, blocks, pair_ref, chain_ref, w_ref, wide, *rest):
    gate_ref, *operand_refs, norm_ref, laid, turned, swap = rest[-(2 * chunks + 5) :]
    step = pl.program_id(0)
    _, rows, cols, channels = pair_ref.shape
    block = ids[0] * of + base + step

    @pl.when(step == 0)
    def _():
        swap[...] = swap_matrix(16)

    row_alive = alive_rows(chain_ref, (blocks[0, block] * n_chan + ids[1]) * rows, rows)
    col_alive = alive_rows(chain_ref, (blocks[1, block] * n_sub + ids[2]) * cols, cols)
    group = hidden // cols
    for at in range(0, rows, group):
        values = pair_ref[0, pl.ds(at, group)].reshape(group * cols, channels)
        norm_and_gate(values, row_alive, col_alive, at, norm_ref, w_ref, gate_ref)
    open_layer(0, norm_ref[...], operand_refs[:chunks], operand_refs[chunks:], wide, laid, turned, swap)


def operand_scratch(rows, size, hidden):
    parts = hidden // size
    return [
        pltpu.VMEM((2, rows // parts, parts * size, hidden), jnp.bfloat16),
        pltpu.VMEM((size, rows, hidden), jnp.bfloat16),
        pltpu.VMEM((256, 256), jnp.bfloat16),
    ]


def operand_outputs(slots, count, rows, hidden, bands):
    kept = [count if n == 0 else slots for n in range(len(bands))] * 2
    return [jax.ShapeDtypeStruct((k, b, rows, hidden), jnp.bfloat16) for k, b in zip(kept, bands * 2)]


def slot_specs(arrays, slots, base):
    def spec(array):
        offset = base if array.shape[0] == slots else 0
        return pl.BlockSpec((1,) + array.shape[1:], lambda s, *_: (s + offset, 0, 0, 0))

    return [spec(a) for a in arrays]


def fill(out_shape, earlier, slots, n_before):
    if earlier is None:
        return [], [], {}
    shared = [n for n, o in enumerate(out_shape) if o.shape[0] == slots]
    specs = [pl.BlockSpec(memory_space=pl.ANY)] * len(shared)
    return [earlier[n] for n in shared], specs, {n_before + k: n for k, n in enumerate(shared)}


def open_operands(ids, blocks, pair, chains, w_in, wide, hidden, bands, base, count, earlier):
    slots, rows, cols, channels = pair.shape
    out_shape = [jax.ShapeDtypeStruct(pair.shape, jnp.bfloat16)] + operand_outputs(slots, count, rows, hidden, bands)
    more, more_specs, aliases = fill(out_shape, earlier, slots, 6)
    return pl.pallas_call(
        functools.partial(open_kernel, hidden, len(bands), lax.axis_size("chan"), lax.axis_size("sub"), base, slots),
        grid_spec=pltpu.PrefetchScalarGridSpec(
            num_scalar_prefetch=2,
            grid=(count,),
            in_specs=slot_specs([pair], slots, base)
            + [
                pl.BlockSpec(chains.shape, lambda s, *_: (0, 0)),
                pl.BlockSpec((1,) + w_in.shape[1:], lambda s, *_: (0, 0, 0)),
                pl.BlockSpec(wide.shape, lambda s, *_: (0, 0)),
            ]
            + more_specs,
            out_specs=slot_specs(out_shape, slots, base),
            scratch_shapes=[pltpu.VMEM((rows, cols, channels), jnp.bfloat16)] + operand_scratch(rows, cols, hidden),
        ),
        out_shape=out_shape,
        input_output_aliases=aliases,
        compiler_params=pltpu.CompilerParams(vmem_limit_bytes=18 * mebi),
        cost_estimate=pl.CostEstimate(flops=1 << 33, bytes_accessed=1 << 20, transcendentals=0),
        name="open_operands",
    )(ids, blocks, pair, chains, w_in, wide, *more)


def far_kernel(layer, n_blk, far, n_chan, n_sub, of, bases, ids, blocks, mine, *rest):
    sources, (chain_ref, wide, left_ref, right_ref, norm_ref, laid, turned, swap) = rest[:-8], rest[-8:]
    step = pl.program_id(0)
    rows, cols, channels = norm_ref.shape
    holder = lax.rem(ids[0] - far + n_blk, n_blk)

    @pl.when(step == 0)
    def _():
        swap[...] = swap_matrix(16)

    group = channels // cols
    for side, out_ref in ((0, left_ref), (1, right_ref)):
        slot = mine[2 * step + side]
        refs = sources[side * len(bases) : (side + 1) * len(bases)]
        block = holder * of + slot
        row_alive = alive_rows(chain_ref, (blocks[0, block] * n_chan + ids[1]) * rows, rows)
        col_alive = alive_rows(chain_ref, (blocks[1, block] * n_sub + ids[2]) * cols, cols)
        for at in range(0, rows, group):
            values = refs[0][0, pl.ds(at, group)]
            for base, ref in zip(bases[1:], refs[1:]):
                values = jnp.where(slot >= base, ref[0, pl.ds(at, group)], values)
            norm_and_gate(values.reshape(group * cols, channels), row_alive, col_alive, at, norm_ref)
        if side == layer % 2:
            make_operand(side, norm_ref[...], wide, [out_ref], laid, swap)
        else:
            turn(norm_ref[...], turned, swap)
            make_operand(side, turned[...], wide, [out_ref], laid, swap)


def far_operands(layer, ids, blocks, mine, sources, chains, wide, far, capacity, of, hidden):
    n_blk = lax.axis_size("blk")
    _, rows, cols, channels = sources[0].shape
    bases = [sum(a.shape[0] for a in sources[:n]) for n in range(len(sources))]

    def source_spec(side, base, size):
        def place(t, ids, blocks, mine):
            return jnp.clip(mine[2 * t + side] - base, 0, size - 1), 0, 0, 0

        return pl.BlockSpec((1, rows, cols, channels), place)

    in_specs = [source_spec(side, b, a.shape[0]) for side in range(2) for b, a in zip(bases, sources)]
    in_specs += [pl.BlockSpec(chains.shape, lambda t, *_: (0, 0)), pl.BlockSpec(wide.shape, lambda t, *_: (0, 0))]
    shape = (capacity, hidden // (hidden // cols), rows, hidden)
    return pl.pallas_call(
        functools.partial(
            far_kernel, layer, n_blk, far, lax.axis_size("chan"), lax.axis_size("sub"), of, tuple(bases)
        ),
        grid_spec=pltpu.PrefetchScalarGridSpec(
            num_scalar_prefetch=3,
            grid=(capacity,),
            in_specs=in_specs,
            out_specs=[pl.BlockSpec((1,) + shape[1:], lambda t, *_: (t, 0, 0, 0))] * 2,
            scratch_shapes=[pltpu.VMEM((rows, cols, channels), jnp.bfloat16)] + operand_scratch(rows, cols, hidden),
        ),
        out_shape=[jax.ShapeDtypeStruct(shape, jnp.bfloat16)] * 2,
        compiler_params=pltpu.CompilerParams(vmem_limit_bytes=14 * mebi),
        cost_estimate=pl.CostEstimate(flops=1 << 33, bytes_accessed=1 << 20, transcendentals=0),
        name="far_operands",
    )(ids, blocks, mine, *sources, *sources, chains, wide)


def plan_kernel(n_blk, far, slots_dev, terms, capacity, ids, owners, slots, chosen, place, mine, seen):
    for shift in range(n_blk):
        seen[shift] = 0
        target = lax.rem(ids[0] + shift, n_blk)
        for e in range(2 * (capacity + 1)):
            chosen[2 * shift * (capacity + 1) + e] = 0
        found = jnp.int32(0)
        for e in range(slots_dev * terms):
            block, term = target * slots_dev + e // terms, e % terms
            at = 2 * (shift * (capacity + 1) + jnp.minimum(found, capacity))
            chosen[at] = slots[term, 0, block]
            chosen[at + 1] = slots[term, 1, block]
            found = found + (owners[term, block] == ids[0]).astype(jnp.int32)
    for e in range(slots_dev * terms):
        owner = owners[e % terms, ids[0] * slots_dev + e // terms]
        count = seen[owner]
        seen[owner] = count + 1
        place[e] = lax.rem(ids[0] - owner + n_blk, n_blk) * capacity + count
    for e in range(2 * (capacity + 1)):
        mine[e] = 0
    found = jnp.int32(0)
    for e in range(slots_dev * terms):
        block, term = ids[0] * slots_dev + e // terms, e % terms
        at = 2 * jnp.minimum(found, capacity)
        mine[at] = slots[term, 0, block]
        mine[at + 1] = slots[term, 1, block]
        found = found + (owners[term, block] == lax.rem(ids[0] - far + n_blk, n_blk)).astype(jnp.int32)


def make_plan(ids, owners, slots, n_blk, far, slots_dev, terms, capacity):
    scalars = pl.BlockSpec(memory_space=pltpu.SMEM)
    return pl.pallas_call(
        functools.partial(plan_kernel, n_blk, far, slots_dev, terms, capacity),
        in_specs=[scalars] * 3,
        out_specs=[scalars] * 3,
        out_shape=[
            jax.ShapeDtypeStruct((2 * n_blk * (capacity + 1),), jnp.int32),
            jax.ShapeDtypeStruct((slots_dev * terms,), jnp.int32),
            jax.ShapeDtypeStruct((2 * (capacity + 1),), jnp.int32),
        ],
        scratch_shapes=[pltpu.SMEM((n_blk,), jnp.int32)],
        compiler_params=pltpu.CompilerParams(vmem_limit_bytes=mebi),
        name="make_plan",
    )(ids, owners, slots)


def banded_kernel(shifts, capacity, pieces, n_refs, size, ids, chosen, *rest):
    refs, rest = rest[:n_refs], rest[n_refs:]
    out_refs, (left_held, right_held, out_held, sems, out_sems) = rest[: len(shifts)], rest[len(shifts) :]
    halves, _, bands, rows, hidden = left_held.shape
    parts = hidden // size
    at_once = 2 if capacity % 2 == 0 else 1

    def copy(n, source):
        side, half, base, *_ = pieces[n]
        target = (left_held, right_held)[side].at[half, pl.ds(base, refs[source].shape[0])]
        return pltpu.make_async_copy(refs[source], target, sems.at[n])

    for n, (*_, on, off) in enumerate(pieces):
        if on == off:
            copy(n, on).start()
        else:

            @pl.when(ids[3] == 1)
            def _(n=n, on=on):
                copy(n, on).start()

            @pl.when(ids[3] == 0)
            def _(n=n, off=off):
                copy(n, off).start()

    for n, piece in enumerate(pieces):
        copy(n, piece[-1]).wait()

    def leave(n):
        return pltpu.make_async_copy(out_held.at[pl.ds(n * capacity, capacity)], out_refs[n], out_sems.at[n])

    for n, shift in enumerate(shifts):

        def one(turn, carry, n=n, shift=shift):
            group = lane_group((size, hidden), size)
            for term in [turn * at_once + t for t in range(at_once)]:
                at = 2 * (shift * (capacity + 1) + term)
                left_slot, right_slot = chosen[at], chosen[at + 1]
                for band in range(bands):
                    left = jnp.concatenate([left_held[h, left_slot, band] for h in range(halves)], axis=1)
                    apart = []
                    for h in range(halves):
                        right = right_held[h, right_slot, band]
                        apart += [jnp.where(group == part, right, jnp.zeros_like(right)) for part in range(parts)]
                    made = dot(left, jnp.concatenate(apart, axis=0))
                    out_held[n * capacity + term, band] = made.astype(jnp.bfloat16)
            return carry

        lax.fori_loop(0, capacity // at_once, one, 0)
        leave(n).start()
    for n in range(len(shifts)):
        leave(n).wait()


def banded_products(shifts, ids, chosen, operands, capacity, size):
    refs, pieces = [], []

    def index_of(array):
        for n, known in enumerate(refs):
            if known is array:
                return n
        refs.append(array)
        return len(refs) - 1

    slots = 0
    for both in operands:
        for side in range(2):
            for half, (on, off) in enumerate(both[side]):
                pieces.append((side, half, slots, index_of(on), index_of(off)))
        slots += both[0][0][0].shape[0]
    halves = len(operands[0][0])
    _, bands, rows, hidden = operands[0][0][0][0].shape
    count = len(shifts) * capacity
    anywhere = pl.BlockSpec(memory_space=pl.ANY)
    return pl.pallas_call(
        functools.partial(banded_kernel, shifts, capacity, tuple(pieces), len(refs), size),
        grid_spec=pltpu.PrefetchScalarGridSpec(
            num_scalar_prefetch=2,
            grid=(),
            in_specs=[anywhere] * len(refs),
            out_specs=[anywhere] * len(shifts),
            scratch_shapes=[
                pltpu.VMEM((halves, slots, bands, rows, hidden), jnp.bfloat16),
                pltpu.VMEM((halves, slots, bands, size, hidden), jnp.bfloat16),
                pltpu.VMEM((count, bands, rows, hidden), jnp.bfloat16),
                pltpu.SemaphoreType.DMA((len(pieces),)),
                pltpu.SemaphoreType.DMA((len(shifts),)),
            ],
        ),
        out_shape=[jax.ShapeDtypeStruct((capacity, bands, rows, hidden), jnp.bfloat16)] * len(shifts),
        compiler_params=pltpu.CompilerParams(vmem_limit_bytes=14 * mebi),
        cost_estimate=pl.CostEstimate(
            flops=2 * count * bands * rows * hidden * hidden * halves, bytes_accessed=1, transcendentals=0
        ),
        name="banded_products",
    )(ids, chosen, *refs)


def close_kernel(layer, last, spots, chunks, n_chan, n_sub, base, of, terms, capacity, ids, blocks, place, *rest):
    n_parts = len(spots)
    arrived, rest = rest[:n_parts], rest[n_parts:]
    cur_ref, gate_ref, w_out_ref = rest[:3]
    if last:
        out_ref, held, wide_out, sems, swap = rest[3:]
    else:
        chain_ref, w_ref, wide = rest[3:6]
        out_ref, next_gate_ref, sent_ref, *operand_refs, held, wide_out, sems, norm_ref, laid, turned, swap = rest[
            -(2 * chunks + 10) :
        ]
        left_refs, right_refs = operand_refs[:chunks], operand_refs[chunks:]
    step = pl.program_id(0)
    _, rows, cols, channels = cur_ref.shape
    _, bands, _, hidden = held.shape
    parts, size = hidden // bands, bands

    def arrival(n):
        shift, at = spots[n]
        target = held.at[pl.ds(shift * capacity, capacity), pl.ds(at, arrived[n].shape[1])]
        return pltpu.make_async_copy(arrived[n], target, sems.at[n])

    @pl.when(step == 0)
    def _():
        for n in range(n_parts):
            arrival(n).start()
        wide_out[...] = jnp.zeros_like(wide_out)
        for part in range(parts):
            for a in range(parts):
                at = (part * parts + a) * bands
                wide_out[at : at + bands, a * channels : (a + 1) * channels] = w_out_ref[
                    0, part * bands : (part + 1) * bands, :
                ]
        swap[...] = swap_matrix(16)
        for n in range(n_parts):
            arrival(n).wait()

    if not last:
        block = ids[0] * of + base + step
        row_alive = alive_rows(chain_ref, (blocks[0, block] * n_chan + ids[1]) * rows, rows)
        col_alive = alive_rows(chain_ref, (blocks[1, block] * n_sub + ids[2]) * cols, cols)
    half = 16
    by_row = [[] for _ in range(rows)]
    for row in range(0, rows, half):
        for band in range(0, bands, half):
            taken = pl.ds(band, half), pl.ds(row, half)
            total = held[(place[(base + step) * terms], *taken)].astype(jnp.float32)
            for t in range(1, terms):
                total = total + held[(place[(base + step) * terms + t], *taken)].astype(jnp.float32)
            moved = swapped(total.astype(jnp.bfloat16), swap)
            for r in range(half):
                by_row[row + r].append(moved[r])
    groups = rows // parts
    pieces = []
    for g in range(groups):
        block = jnp.concatenate([x for a in range(parts) for x in by_row[g * parts + a]]).T
        pieces.append(jnp.concatenate([block[p * cols : (p + 1) * cols] for p in range(parts)], axis=1))
    mixture = jnp.concatenate(pieces)
    together = (lane_group((hidden, hidden), size) == lax.broadcasted_iota(jnp.int32, (hidden, hidden), 0) // size)
    together = together.astype(jnp.float32).astype(jnp.bfloat16)
    average = dot(mixture, jnp.concatenate([together] * parts)) * (1.0 / hidden)
    centred = [mixture[:, p * hidden : (p + 1) * hidden].astype(jnp.float32) - average for p in range(parts)]
    squares = sum(c * c for c in centred)
    high = squares.astype(jnp.bfloat16)
    low = (squares - high.astype(jnp.float32)).astype(jnp.bfloat16)
    variance = dot(jnp.concatenate([high, low], axis=1), jnp.concatenate([together] * 2)) * (1.0 / hidden)
    scale = lax.rsqrt(variance + norm_epsilon)
    normed = jnp.concatenate([(c * scale).astype(jnp.bfloat16) for c in centred], axis=1)
    update = dot(normed, wide_out[...])
    for g in range(groups):
        taken = pl.ds(g * parts, parts)
        change = jnp.concatenate(
            [update[g * cols : (g + 1) * cols, a * channels : (a + 1) * channels] for a in range(parts)]
        )
        gate = gate_ref[0, taken].astype(jnp.float32).reshape(parts * cols, channels)
        current = cur_ref[0, taken].astype(jnp.float32).reshape(parts * cols, channels)
        result = (current + gate * change).astype(jnp.bfloat16)
        out_ref[0, taken] = result.reshape(parts, cols, channels)
        if not last:
            sent_ref[0, taken] = result.reshape(parts, cols, channels)
            norm_and_gate(result, row_alive, col_alive, g * parts, norm_ref, w_ref, next_gate_ref)
    if not last:
        open_layer(layer + 1, norm_ref[...], left_refs, right_refs, wide, laid, turned, swap)


def close_layer(
    layer, arrived, ids, blocks, place, current, gate, w_out, capacity, terms, chains, w_in, wide, last, bands, base, count, earlier
):
    flat, spots = [part for part, *_ in arrived], tuple((shift, at) for _, shift, at in arrived)
    n_blk = lax.axis_size("blk")
    slots, rows, cols, channels = current.shape
    hidden = w_out.shape[1]

    def layer_spec(array, index):
        return pl.BlockSpec((1,) + array.shape[1:], lambda s, *_: (index, 0, 0))

    in_specs = [pl.BlockSpec(memory_space=pl.ANY)] * len(flat)
    in_specs += slot_specs([current, gate], slots, base) + [layer_spec(w_out, layer)]
    operands = [*flat, current, gate, w_out]
    out_shape = [jax.ShapeDtypeStruct(current.shape, jnp.bfloat16)]
    scratch = [
        pltpu.VMEM((n_blk * capacity, sum(bands[layer]), rows, hidden), jnp.bfloat16),
        pltpu.VMEM((hidden // cols * hidden, hidden // cols * channels), jnp.bfloat16),
        pltpu.SemaphoreType.DMA((len(flat),)),
    ]
    if not last:
        operands += [chains, w_in, wide]
        in_specs += [pl.BlockSpec(chains.shape, lambda s, *_: (0, 0)), layer_spec(w_in, layer + 1)]
        in_specs += [pl.BlockSpec(wide.shape, lambda s, *_: (0, 0))]
        out_shape += [jax.ShapeDtypeStruct(current.shape, jnp.bfloat16)]
        out_shape += [jax.ShapeDtypeStruct((count,) + current.shape[1:], jnp.bfloat16)]
        out_shape += operand_outputs(slots, count, cols, hidden, bands[layer + 1])
        scratch += [pltpu.VMEM((rows, cols, channels), jnp.bfloat16)] + operand_scratch(cols, rows, hidden)
    else:
        scratch += [pltpu.VMEM((256, 256), jnp.bfloat16)]
    more, more_specs, aliases = fill(out_shape, earlier, slots, 3 + len(operands))
    return pl.pallas_call(
        functools.partial(
            close_kernel,
            *(layer, last, spots, 0 if last else len(bands[layer + 1]), lax.axis_size("chan"), lax.axis_size("sub")),
            *(base, slots, terms, capacity),
        ),
        grid_spec=pltpu.PrefetchScalarGridSpec(
            num_scalar_prefetch=3,
            grid=(count,),
            in_specs=in_specs + more_specs,
            out_specs=slot_specs(out_shape, slots, base),
            scratch_shapes=scratch,
        ),
        out_shape=out_shape,
        input_output_aliases=aliases,
        compiler_params=pltpu.CompilerParams(vmem_limit_bytes=24 * mebi),
        cost_estimate=pl.CostEstimate(flops=1 << 33, bytes_accessed=1 << 20, transcendentals=0),
        name="close_layer",
    )(ids, blocks, place, *operands, *more)


def after(value, *others):
    return lax.optimization_barrier((value, *others))[0]


def exchange_bands_outgoing(left, right, over):
    both = ("chan", "sub")
    other = lax.ppermute(left, "sub", [(0, 1), (1, 0)])
    one = lax.ppermute(right, both, [(0, 2), (3, 1), (1, 0), (2, 3)])
    two = lax.ppermute(right, both, [(1, 2), (2, 1)])
    return [(other, left), (left, other)], [(one, one), (right, two)]


def exchange_bands_incoming(left, right, over):
    both = ("chan", "sub")
    one = lax.ppermute(left, both, [(1, 3), (2, 0), (0, 1), (3, 2)])
    other = lax.ppermute(right, "chan", [(0, 1), (1, 0)])
    two = lax.ppermute(after(one, other if over is None else over), both, [(0, 1), (3, 2)])
    return [(left, one), (one, two)], [(right, right), (other, other)]


def banded(pair, ids, blocks, owners, slot_of, chains, w_in, w_out, capacity, terms, n_blk):
    slots, rows, cols, channels = pair.shape
    hidden = w_out.shape[1]
    far = 1
    middle = n_blk // 2
    near = [s for s in (middle, *range(1, n_blk)) if s != far]
    near = [s for n, s in enumerate(near) if s not in near[:n]] + [0]
    layers = w_in.shape[0]
    current = pair
    bands = [[16, 16], [20, 12]]
    chosen, place, mine = make_plan(ids, owners, slot_of, n_blk, far, slots, terms, capacity)
    in_order = jnp.repeat(jnp.arange(capacity, dtype=jnp.int32), 2)
    half = slots // 2
    halves = [(0, half), (half, slots - half)]

    def over_blk(value, shift):
        return lax.ppermute(value, "blk", [(p, (p + shift) % n_blk) for p in range(n_blk)])

    for layer in range(layers):
        count = len(bands[layer])
        if layer == 0:
            raw = [over_blk(pair, far)]
            calls, wide = [None], spread_weights(w_in, 0, cols)
            for base, size in halves:
                calls.append(
                    open_operands(ids, blocks, pair, chains, w_in, wide, hidden, bands[0], base, size, calls[-1])
                )
            gate = calls[-1][0]
        else:
            raw = []
            for call in calls[1:]:
                raw.append(over_blk(after(call[2], *raw) if raw else call[2], far))
        operands = [call[-2 * count :] for call in calls[1:]]
        exchange = exchange_bands_incoming if layer % 2 else exchange_bands_outgoing
        arrived, by_shift = [], {}
        for chunk in range(count):
            if chunk == 0:
                exchanged = []
                over = operands[-1][count]
                for left, right in [(o[0], o[count]) for o in operands]:
                    if exchanged and layer % 2:
                        (_, (one, two)), (_, (other, _)) = exchanged[-1]
                        left, right = lax.optimization_barrier((left, right, one, other))[:2]
                        right = after(right, two)
                    elif exchanged:
                        ((other, _), _), ((one, _), (_, two)) = exchanged[-1]
                        left, right = lax.optimization_barrier((left, right, other, one, two))[:2]
                    exchanged.append(exchange(left, right, over))
            else:
                left, right = operands[-1][chunk], operands[-1][count + chunk]
                if layer % 2:
                    (_, (_, two)), (_, (other, _)) = exchanged[-1]
                    left, right = lax.optimization_barrier((left, right, two, other))[:2]
                else:
                    ((other, _), _), ((one, _), (_, two)) = exchanged[-1]
                    left = after(left, other)
                    right = after(right, one, two, made[-1])
                exchanged = [exchange(left, right, list(by_shift.values())[-1] if by_shift else made[-1])]
                ids = after(ids, *by_shift.values())
            made = banded_products(near, ids, chosen, exchanged, capacity, cols)
            start = sum(bands[layer][:chunk])
            for shift, part in zip(near, made):
                if shift:
                    part = over_blk(after(part, by_shift.get(shift, raw[-1])), shift)
                    by_shift[shift] = part
                arrived.append((part, shift, start))
            if chunk == 0:
                sources = list(lax.optimization_barrier((*raw, made[-1]))[:-1])
                far_left, far_right = far_operands(
                    layer, ids, blocks, mine, sources, chains, wide, far, capacity, slots, hidden
                )
        far_exchanged = [exchange(far_left, far_right, list(by_shift.values())[-1] if by_shift else made[-1])]
        (part,) = banded_products([0], ids, in_order, far_exchanged, capacity, cols)
        arrived.append((part, far, 0))
        last = layer == layers - 1
        calls = [None]
        if not last:
            wide = spread_weights(after(w_in, made[-1]), layer + 1, cols)
        for base, size in [(0, slots)] if last else halves:
            calls.append(
                close_layer(
                    *(layer, arrived, ids, blocks, place, current, gate, w_out, capacity, terms, chains, w_in, wide, last),
                    *(bands, base, size, calls[-1]),
                )
            )
        if last:
            return calls[-1][0]
        current, gate = calls[-1][:2]


def per_device(pair, block_list, term_owner, term_slots, chain_ids, w_in, w_out):
    n_blk = lax.axis_size("blk")
    n_chan = lax.axis_size("chan")
    n_sub = lax.axis_size("sub")
    position = lax.axis_index("blk")
    row_group = lax.axis_index("chan")
    col_group = lax.axis_index("sub")
    slots, rows, cols, channels = pair.shape
    hidden = w_out.shape[1]
    terms = term_owner.shape[1]
    capacity = max(2, -(-slots * terms // n_blk))
    fast = n_chan == 2 and n_sub == 2
    on_diagonal = (row_group == col_group).astype(jnp.int32)
    ids = jnp.stack([position, row_group, col_group, on_diagonal]).astype(jnp.int32)
    blocks = block_list.T
    owners = term_owner.T
    slot_of = jnp.transpose(term_slots, (1, 2, 0))
    chains = chain_ids.reshape(-1, 128)
    if fast and n_blk > 1 and rows == cols == 32 and channels == hidden == 128:
        return banded(pair, ids, blocks, owners, slot_of, chains, w_in, w_out, capacity, terms, n_blk)
    shifts = [n_blk // 2] + [s for s in range(1, n_blk) if s != n_blk // 2] + [0]

    def all_products(lefts, right):
        parts = [None] * n_blk
        for shift in shifts:
            made = term_products(shift, ids, owners, slot_of, lefts, right, capacity, slots, terms)
            if shift:
                pairs = [(p, (p + shift) % n_blk) for p in range(n_blk)]
                made = lax.ppermute(made, "blk", pairs)
            parts[shift] = made
        return parts

    def at_home(layer, parts, current, gate, at, of, into=None):
        last = layer == w_in.shape[0] - 1
        return home(
            layer, parts, ids, blocks, owners, current, gate, w_out, capacity, terms, at, of, chains, w_in, last, into
        )

    gate, left, *rights = first_operands(ids, blocks, pair, chains, w_in, hidden, 2 if fast else 1)
    lefts, chunks = exchange_outgoing(left, rights, n_chan, n_sub)
    count = len(chunks)
    made = [all_products(lefts, right) for right in chunks]
    homes = [at_home(0, parts, pair, gate, at, count) for at, parts in enumerate(made)]
    lefts, chunks = exchange_incoming([h[2] for h in homes], [h[3] for h in homes], n_chan, n_sub)
    made = [all_products(lefts, right) for right in chunks]
    out = None
    for at, parts in enumerate(made):
        (out,) = at_home(1, parts, homes[at][0], homes[at][1], at, count, into=out)
    return out


def solution(mesh):
    in_specs = (
        P(("groups", "blk"), "chan", "sub", None),
        P("groups", None),
        P("groups", None),
        P("groups", None, None),
        P("groups"),
        P(),
        P(),
    )
    out_specs = P(("groups", "blk"), "chan", "sub", None)
    return jax.shard_map(
        per_device, mesh=mesh, in_specs=in_specs, out_specs=out_specs, check_vma=False
    )
```
